32 devices in a mesh: seq: 8 (over z, x), dp: 4 (over y, core).
Axes of the slice: x: 2, y: 2, z: 4, core: 2. Of those that a mesh axis runs over, the one named last changes fastest.
Arguments:
- tokens: bfloat16 [4, 1024, 2048], P('dp', 'seq'), may hold values from -6 to 6
- out_grad: bfloat16 [4, 1024, 2048], P('dp', 'seq'), may hold values from -6 to 6
- span_order: int32 [16], replicated, may hold values from 0 to 15, each once
- doc_starts: int32 [4, 8], P('dp'), may hold values from 0 to 1023, as said below
- w_query: bfloat16 [2048, 2048], P(('seq', 'dp')), may hold values from -0.125 to 0.125
- w_key: bfloat16 [2048, 1024], P(('seq', 'dp')), may hold values from -0.125 to 0.125
- w_value: bfloat16 [2048, 1024], P(('seq', 'dp')), may hold values from -0.125 to 0.125
- w_output: bfloat16 [2048, 2048], P(('seq', 'dp')), may hold values from -2 to 2
- attn_gain: float32 [2048], P(('seq', 'dp')), may hold values from 0.5 to 1.5
- query_gain: float32 [128], replicated, may hold values from 0.5 to 1.5
- key_gain: float32 [128], replicated, may hold values from 0.5 to 1.5
- w_gate: bfloat16 [2048, 6144], P(('seq', 'dp')), may hold values from -0.125 to 0.125
- w_up: bfloat16 [2048, 6144], P(('seq', 'dp')), may hold values from -0.125 to 0.125
- w_down: bfloat16 [2048, 6144], P(('seq', 'dp')), may hold values from -0.078125 to 0.078125
- mlp_gain: float32 [2048], P(('seq', 'dp')), may hold values from 0.5 to 1.5
Outputs:
- block_out: bfloat16 [4, 1024, 2048], P('dp', 'seq')
- tokens_grad: float32 [4, 1024, 2048], P('dp', 'seq')
- w_query_grad: float32 [2048, 2048], P(('seq', 'dp'))
- w_key_grad: float32 [2048, 1024], P(('seq', 'dp'))
- w_value_grad: float32 [2048, 1024], P(('seq', 'dp'))
- w_output_grad: float32 [2048, 2048], P(('seq', 'dp'))
- attn_gain_grad: float32 [2048], P(('seq', 'dp'))
- query_gain_grad: float32 [128], replicated
- key_gain_grad: float32 [128], replicated
- w_gate_grad: float32 [2048, 6144], P(('seq', 'dp'))
- w_up_grad: float32 [2048, 6144], P(('seq', 'dp'))
- w_down_grad: float32 [2048, 6144], P(('seq', 'dp'))
- mlp_gain_grad: float32 [2048], P(('seq', 'dp'))
The draws below stay inside these ranges and needn't reach their ends.
Inputs may be any that keep to these rules, and one draw needn't show every extreme that they name: `span_order`: each span number appears once. `doc_starts`: in each row the offsets never fall and the first is 0; document j covers positions from offset j up to offset j + 1, the last up to 1024, so a document may be empty. Among the 1 sequence of each index of dp, one drawn from the seed has its second offset below 64 and all later ones above 960.
All inputs are finite; a program needn't handle non-finite values.
Results may differ from the reference program's by a relative error of at most 0.035.
Values may be sent and summed in bfloat16 or wider, within the bound.
A program may use at most 640 MiB of HBM per device.

```python
import math
import jax
import jax.numpy as jnp
from jax import lax

D = 2048
H = 16
KVH = 8
HD = 128
FF = 6144
SPAN = 64
SEQ_DEV = 1
DOCS = 8
SPANS = 16
LEN = 1024
BATCH = 4


def draw_doc_starts(key, part):
    key = jax.random.fold_in(key, 7)
    first, second, third, fourth = jax.random.split(key, 4)
    inner = jax.random.randint(first, (BATCH, DOCS - 1), 1, LEN, dtype=jnp.int32)
    inner = jnp.sort(inner, axis=1)
    starts = jnp.concatenate([jnp.zeros((BATCH, 1), jnp.int32), inner], axis=1)
    early = jax.random.randint(third, (BATCH, 1), 1, SPAN, dtype=jnp.int32)
    late = jax.random.randint(fourth, (BATCH, DOCS - 2), LEN - SPAN + 1, LEN, dtype=jnp.int32)
    late = jnp.sort(late, axis=1)
    spanning = jnp.concatenate([jnp.zeros((BATCH, 1), jnp.int32), early, late], axis=1)
    chosen = jax.random.randint(second, (BATCH // SEQ_DEV, 1), 0, SEQ_DEV, dtype=jnp.int32)
    member = (jnp.arange(BATCH, dtype=jnp.int32) % SEQ_DEV).reshape(BATCH // SEQ_DEV, SEQ_DEV)
    single = (member == chosen).reshape(BATCH, 1)
    return jnp.where(single, spanning, starts)


def level_of(key, shape, cuts, low, top_value):
    level = 1.0
    for axis_at, shards_of in cuts:
        draws = jax.random.uniform(jax.random.fold_in(jax.random.fold_in(key, 6), axis_at), (shards_of,), jnp.float32, low / len(cuts), top_value / len(cuts))
        level = level * jnp.repeat(jnp.exp(draws), shape[axis_at] // shards_of).reshape((-1,) + (1,) * (len(shape) - 1 - axis_at))
    return level


def noise(stream_key, shape, deviation, bound, shards=(), held_as=jnp.bfloat16):
    drawn = jax.random.normal(stream_key, shape, jnp.float32) * deviation
    if len(shards) > 0:
        drawn = level_of(stream_key, shape, shards, -0.22, 0.18) * drawn
    return jnp.clip(drawn, min=-bound, max=bound).astype(held_as)


def setup_inputs(seed: int = 0) -> dict:
    streams_of = jax.random.split(jax.random.key(seed), 16)
    return {
        "tokens": noise(streams_of[0], (BATCH, LEN, D), 1.0, 6.0, ((0, 4), (1, 8))),
        "out_grad": noise(streams_of[1], (BATCH, LEN, D), 1.0, 6.0, ((0, 4), (1, 8))),
        "span_order": jax.random.permutation(streams_of[2], SPANS).astype(jnp.int32),
        "doc_starts": draw_doc_starts(jax.random.fold_in(streams_of[15], 71), 0),
        "w_query": noise(streams_of[4], (D, H * HD), D ** -0.5, 0.125, ((0, 32),)),
        "w_key": noise(streams_of[5], (D, KVH * HD), D ** -0.5, 0.125, ((0, 32),)),
        "w_value": noise(streams_of[6], (D, KVH * HD), D ** -0.5, 0.125, ((0, 32),)),
        "w_output": noise(streams_of[7], (D, H * HD), (max(H * HD // 256, 1)) ** -0.5, 2.0, ((0, 32),)),
        "attn_gain": jnp.clip(1.0 + 0.1 * jax.random.normal(streams_of[8], (D,), jnp.float32), 0.5, 1.5),
        "query_gain": jnp.clip(1.0 + 0.1 * jax.random.normal(streams_of[9], (HD,), jnp.float32), 0.5, 1.5),
        "key_gain": jnp.clip(1.0 + 0.1 * jax.random.normal(streams_of[10], (HD,), jnp.float32), 0.5, 1.5),
        "w_gate": noise(streams_of[11], (D, FF), D ** -0.5, 0.125, ((0, 32),)),
        "w_up": noise(streams_of[12], (D, FF), D ** -0.5, 0.125, ((0, 32),)),
        "w_down": noise(streams_of[13], (D, FF), FF ** -0.5, 0.078125, ((0, 32),)),
        "mlp_gain": jnp.clip(1.0 + 0.1 * jax.random.normal(streams_of[14], (D,), jnp.float32), 0.5, 1.5),
    }


EPS = 1e-06
NEG = -1e+30
HIGH = lax.Precision.HIGHEST

@jax.custom_vjp
def low(v):
    return lax.optimization_barrier(v.astype(jnp.bfloat16)).astype(jnp.float32)

@jax.custom_vjp
def low_back(v):
    return v

def low_keep(v):
    return (low(v), None)

def low_pass(kept, grad):
    return (grad,)

def back_keep(v):
    return (v, None)

def back_low(kept, grad):
    return (low(grad),)
low.defvjp(low_keep, low_pass)
low_back.defvjp(back_keep, back_low)

def normed(v, gain):
    return v * lax.rsqrt(lax.optimization_barrier(jnp.mean(v * v, -1, keepdims=True)) + EPS) * gain

def rotary(pos, width):
    half = width // 2
    freqs = jnp.exp(jnp.arange(half, dtype=jnp.float32) * (-2.0 / width * math.log(1000000.0)))
    angle = pos.astype(jnp.float32)[:, None] * freqs[None, :]
    return (jnp.cos(angle)[:, None, :], jnp.sin(angle)[:, None, :])

def rotate(v, cosv, sinv):
    half = v.shape[-1] // 2
    first, second = (v[..., :half], v[..., half:])
    return jnp.concatenate([first * cosv - second * sinv, second * cosv + first * sinv], -1)

def positions(span_order):
    rows = jnp.arange(LEN, dtype=jnp.int32)
    return span_order[rows // SPAN] * SPAN + rows % SPAN

def documents(starts, pos):
    return lax.optimization_barrier(jnp.sum((starts[None, :] <= pos[:, None]).astype(jnp.int32), -1))

def matmul(left, right):
    return jnp.dot(left, right, precision=HIGH, preferred_element_type=jnp.float32)

def attend(query, key, value, pos, doc):
    block = min(512, LEN)
    share = H // KVH
    scale = 1.0 / math.sqrt(HD)
    grouped = query.reshape(LEN // block, block, KVH, share, HD)
    pos_blocks = pos.reshape(LEN // block, block)
    doc_blocks = doc.reshape(LEN // block, block)

    def one_block(items):
        rows, pos_rows, doc_rows = items
        score = jnp.einsum('qgjd,kgd->gjqk', rows, key, precision=HIGH) * scale
        score = low_back(score)
        visible = (doc_rows[:, None] == doc[None, :]) & (pos[None, :] <= pos_rows[:, None])
        score = jnp.where(visible[None, None], score, NEG)
        prob = low(jax.nn.softmax(score, axis=-1))
        return jnp.einsum('gjqk,kgd->qgjd', prob, value, precision=HIGH)
    out = lax.map(jax.checkpoint(one_block), (grouped, pos_blocks, doc_blocks))
    return out.reshape(LEN, H * HD)

def layer(xs, w_query, w_key, w_value, w_output, attn_gain, query_gain, key_gain, w_gate, w_up, w_down, mlp_gain, pos, doc, cosv, sinv):
    first = low(normed(xs, attn_gain))
    query = low_back(matmul(first, w_query)).reshape(LEN, H, HD)
    key = low_back(matmul(first, w_key)).reshape(LEN, KVH, HD)
    value = low(low_back(matmul(first, w_value))).reshape(LEN, KVH, HD)
    query = low(rotate(normed(query, query_gain), cosv, sinv))
    key = low(rotate(normed(key, key_gain), cosv, sinv))
    mixed = low(low_back(attend(query, key, value, pos, doc)))
    resid = xs + low_back(matmul(mixed, w_output.T))
    second = low(normed(resid, mlp_gain))
    gate = low_back(matmul(second, w_gate))
    upper = low_back(matmul(second, w_up))
    hidden = low(jax.nn.silu(gate) * upper)
    return resid + matmul(hidden, w_down.T)

def reference(tokens, out_grad, span_order, doc_starts, w_query, w_key, w_value, w_output, attn_gain, query_gain, key_gain, w_gate, w_up, w_down, mlp_gain):
    pos = positions(span_order)
    cosv, sinv = rotary(pos, HD)
    weights = tuple((w.astype(jnp.float32) for w in (w_query, w_key, w_value, w_output, attn_gain, query_gain, key_gain, w_gate, w_up, w_down, mlp_gain)))

    def one_sequence(totals, items):
        xs, grads_in, starts = items
        doc = documents(starts, pos)

        def forward(xv, *params):
            return layer(xv, *params, pos, doc, cosv, sinv)
        result, pull = jax.vjp(forward, xs.astype(jnp.float32), *weights)
        back = pull(grads_in.astype(jnp.float32))
        totals = tuple((a + b for a, b in zip(totals, back[1:])))
        return (totals, (result.astype(jnp.bfloat16), back[0]))
    zeros = tuple((jnp.zeros(w.shape, jnp.float32) for w in weights))
    totals, (outputs, input_grads) = lax.scan(one_sequence, zeros, (tokens, out_grad, doc_starts))
    return (outputs, input_grads, totals[0], totals[1], totals[2], totals[3], totals[4], totals[5], totals[6], totals[7], totals[8], totals[9], totals[10])
```

```python
import math

import jax
import jax.numpy as jnp
from jax import lax
from jax.sharding import PartitionSpec as P

EPS = 1e-06
NEG = -1e30


def normed(v, gain):
    scale_inv = lax.rsqrt(jnp.mean(v * v, -1, keepdims=True) + EPS)
    return (v * scale_inv * gain, scale_inv)


def norm_back(v, scale_inv, gain, grad):
    scaled = grad * gain
    inner = jnp.mean(scaled * v, -1, keepdims=True)
    dv = scale_inv * scaled - v * scale_inv * scale_inv * scale_inv * inner
    dgain = jnp.sum((grad * v * scale_inv).reshape(-1, v.shape[-1]), 0)
    return (dv, dgain)


def rotary(pos, width):
    half = width // 2
    freqs = jnp.exp(jnp.arange(half, dtype=jnp.float32) * (-2.0 / width * math.log(1000000.0)))
    angle = pos.astype(jnp.float32)[:, None] * freqs[None, :]
    return (jnp.cos(angle)[:, None, :], jnp.sin(angle)[:, None, :])


def rotate(v, cosv, sinv):
    half = v.shape[-1] // 2
    first, second = (v[..., :half], v[..., half:])
    return jnp.concatenate([first * cosv - second * sinv, second * cosv + first * sinv], -1)


def rotate_back(grad, cosv, sinv):
    half = grad.shape[-1] // 2
    first, second = (grad[..., :half], grad[..., half:])
    return jnp.concatenate([first * cosv + second * sinv, second * cosv - first * sinv], -1)


def place(order, begin, count, span):
    rows = begin + jnp.arange(count, dtype=jnp.int32)
    slots = rows // span
    picked = slots[:, None] == jnp.arange(order.shape[0], dtype=jnp.int32)[None, :]
    return jnp.sum(jnp.where(picked, order[None, :], 0), -1) * span + rows % span


def doc_of(starts, pos):
    return jnp.sum((starts[:, None, :] <= pos[None, :, None]).astype(jnp.int32), -1)


def gathered_body(
    tokens,
    out_grad,
    span_order,
    doc_starts,
    w_query,
    w_key,
    w_value,
    w_output,
    attn_gain,
    query_gain,
    key_gain,
    w_gate,
    w_up,
    w_down,
    mlp_gain,
):
    seqs, local, width = tokens.shape
    span = local // 2
    head_size = query_gain.shape[0]
    kv_heads = w_key.shape[1] // head_size
    heads = w_query.shape[1] // head_size
    share = heads // kv_heads
    kv_width = kv_heads * head_size
    ff_width = w_gate.shape[1]
    scale = 1.0 / math.sqrt(head_size)
    total_rows = seqs * local
    own_rows = width // lax.axis_size(("seq", "dp"))
    qpos = place(span_order, lax.axis_index("seq") * local, local, span)
    qdoc = doc_of(doc_starts, qpos)
    cosv, sinv = rotary(qpos, head_size)

    def gather_attn():
        return (
            lax.all_gather(w_query, ("seq", "dp"), axis=0, tiled=True),
            lax.all_gather(w_key, ("seq", "dp"), axis=0, tiled=True),
            lax.all_gather(w_value, ("seq", "dp"), axis=0, tiled=True),
            lax.all_gather(w_output, ("seq", "dp"), axis=0, tiled=True),
            lax.all_gather(
                attn_gain.astype(jnp.bfloat16), ("seq", "dp"), axis=0, tiled=True
            ).astype(attn_gain.dtype),
        )

    def gather_mlp():
        return (
            lax.all_gather(w_gate, ("seq", "dp"), axis=0, tiled=True),
            lax.all_gather(w_up, ("seq", "dp"), axis=0, tiled=True),
            lax.all_gather(w_down, ("seq", "dp"), axis=0, tiled=True),
            lax.all_gather(mlp_gain.astype(jnp.bfloat16), ("seq", "dp"), axis=0, tiled=True).astype(
                mlp_gain.dtype
            ),
        )

    x_rows = tokens.astype(jnp.float32).reshape(total_rows, width)
    wq_all, wk_all, wv_all, wo_all, ga_all = gather_attn()
    first_norm, first_inv = normed(x_rows, ga_all)
    first_in = first_norm.astype(jnp.bfloat16)
    q_raw = jnp.dot(first_in, wq_all, preferred_element_type=jnp.float32).reshape(
        seqs, local, heads, head_size
    )
    k_raw = jnp.dot(first_in, wk_all, preferred_element_type=jnp.float32).reshape(
        seqs, local, kv_heads, head_size
    )
    v_low = (
        jnp.dot(first_in, wv_all, preferred_element_type=jnp.float32)
        .astype(jnp.bfloat16)
        .reshape(seqs, local, kv_heads, head_size)
    )
    q_normed, q_inv = normed(q_raw, query_gain)
    k_normed, k_inv = normed(k_raw, key_gain)
    q_low = rotate(q_normed, cosv, sinv).astype(jnp.bfloat16)
    k_low = rotate(k_normed, cosv, sinv).astype(jnp.bfloat16)
    q_group = q_low.reshape(seqs, local, kv_heads, share, head_size)

    def scores(piece_key, start):
        count = piece_key.shape[1]
        kpos = place(span_order, start, count, span)
        kdoc = doc_of(doc_starts, kpos)
        visible = (qdoc[:, :, None] == kdoc[:, None, :]) & (
            kpos[None, None, :] <= qpos[None, :, None]
        )
        raw = (
            jnp.einsum("sqgjd,skgd->sgjqk", q_group, piece_key, preferred_element_type=jnp.float32)
            * scale
        )
        return (raw, visible[:, None, None])

    start_top = jnp.full((seqs, kv_heads, share, local), NEG, jnp.float32)
    piece = (
        lax.all_gather(k_low, "seq", axis=1, tiled=True),
        lax.all_gather(v_low, "seq", axis=1, tiled=True),
    )
    top = start_top
    raw, visible = scores(piece[0], jnp.int32(0))
    raw = jnp.where(visible, raw, NEG)
    new_top = jnp.maximum(top, jnp.max(raw, -1))
    weights = jnp.where(visible, jnp.exp(raw - new_top[..., None]), 0.0)
    total = jnp.sum(weights, -1)
    summed = jnp.einsum(
        "sgjqk,skgd->sgjqd",
        weights.astype(jnp.bfloat16),
        piece[1],
        preferred_element_type=jnp.float32,
    )
    top, total, summed = (new_top, total, summed)
    log_total = top + jnp.log(total)
    attn_vals = summed / total[..., None]
    out_low = (
        jnp.transpose(attn_vals, (0, 3, 1, 2, 4))
        .reshape(total_rows, heads * head_size)
        .astype(jnp.bfloat16)
    )
    resid = x_rows + jnp.einsum("nh,dh->nd", out_low, wo_all, preferred_element_type=jnp.float32)
    wg_all, wu_all, wd_all, gm_all = gather_mlp()
    second_norm, second_inv = normed(resid, gm_all)
    second_in = second_norm.astype(jnp.bfloat16)
    gate = jnp.dot(second_in, wg_all, preferred_element_type=jnp.float32)
    upper = jnp.dot(second_in, wu_all, preferred_element_type=jnp.float32)
    sigma = jax.nn.sigmoid(gate)
    act = gate * sigma
    hidden = (act * upper).astype(jnp.bfloat16)
    result = resid + jnp.einsum("nf,df->nd", hidden, wd_all, preferred_element_type=jnp.float32)
    block_out = result.astype(jnp.bfloat16).reshape(seqs, local, width)
    grad_low = out_grad.reshape(total_rows, width)
    wg_all, wu_all, wd_all, gm_all = gather_mlp()
    dmid = jnp.einsum("nd,df->nf", grad_low, wd_all, preferred_element_type=jnp.float32)
    dgate = (dmid * upper * sigma * (1.0 + gate * (1.0 - sigma))).astype(jnp.bfloat16)
    dupper = (dmid * act).astype(jnp.bfloat16)
    left = second_in
    outer = grad_low
    mlp_sums = lax.psum_scatter(
        jnp.concatenate(
            [
                jnp.einsum("nd,nf->df", left, dgate, preferred_element_type=jnp.float32),
                jnp.einsum("nd,nf->df", left, dupper, preferred_element_type=jnp.float32),
                jnp.einsum("nd,nf->df", outer, hidden, preferred_element_type=jnp.float32),
            ],
            1,
        ),
        ("seq", "dp"),
        scatter_dimension=0,
        tiled=True,
    )
    dsecond = jnp.einsum(
        "nf,df->nd", dgate, wg_all, preferred_element_type=jnp.float32
    ) + jnp.einsum("nf,df->nd", dupper, wu_all, preferred_element_type=jnp.float32)
    dresid_norm, dgm = norm_back(resid, second_inv, gm_all, dsecond)
    dresid = grad_low.astype(jnp.float32) + dresid_norm
    dresid_low = dresid.astype(jnp.bfloat16)
    wq_all, wk_all, wv_all, wo_all, ga_all = gather_attn()
    dout_low = jnp.einsum(
        "nd,dh->nh", dresid_low, wo_all, preferred_element_type=jnp.float32
    ).astype(jnp.bfloat16)
    dout_group = dout_low.reshape(seqs, local, kv_heads, share, head_size)
    delta = jnp.sum(jnp.transpose(dout_group.astype(jnp.float32), (0, 2, 3, 1, 4)) * attn_vals, -1)
    piece = (
        lax.all_gather(k_low, "seq", axis=1, tiled=True),
        lax.all_gather(v_low, "seq", axis=1, tiled=True),
    )
    count = piece[0].shape[1]
    raw, visible = scores(piece[0], jnp.int32(0))
    prob = jnp.where(visible, jnp.exp(raw - log_total[..., None]), 0.0)
    dprob = jnp.einsum(
        "sqgjd,skgd->sgjqk", dout_group, piece[1], preferred_element_type=jnp.float32
    )
    dscore = (prob * (dprob - delta[..., None])).astype(jnp.bfloat16)
    dq_sum = jnp.einsum("sgjqk,skgd->sqgjd", dscore, piece[0], preferred_element_type=jnp.float32)
    dk_part = (
        jnp.einsum("sgjqk,sqgjd->skgd", dscore, q_group, preferred_element_type=jnp.float32) * scale
    )
    dv_part = jnp.einsum(
        "sgjqk,sqgjd->skgd",
        prob.astype(jnp.bfloat16),
        dout_group,
        preferred_element_type=jnp.float32,
    )
    joined = jnp.concatenate(
        [dk_part.reshape(seqs, count, kv_width), dv_part.reshape(seqs, count, kv_width)], -1
    )
    buffer = joined
    dq_sum, buffer = (dq_sum, buffer)
    key_sums = lax.psum_scatter(
        buffer.astype(jnp.bfloat16), "seq", scatter_dimension=1, tiled=True
    ).astype(jnp.float32)
    dq_rot = (dq_sum * scale).reshape(seqs, local, heads, head_size)
    dq_raw, dgq = norm_back(q_raw, q_inv, query_gain, rotate_back(dq_rot, cosv, sinv))
    dk_rot = key_sums[..., :kv_width].reshape(seqs, local, kv_heads, head_size)
    dk_raw, dgk = norm_back(k_raw, k_inv, key_gain, rotate_back(dk_rot, cosv, sinv))
    dq_low = dq_raw.reshape(total_rows, heads * head_size).astype(jnp.bfloat16)
    dk_low = dk_raw.reshape(total_rows, kv_width).astype(jnp.bfloat16)
    dv_low = key_sums[..., kv_width:].reshape(total_rows, kv_width).astype(jnp.bfloat16)
    left = first_in
    outer = dresid_low
    attn_sums = lax.psum_scatter(
        jnp.concatenate(
            [
                jnp.einsum("nd,nh->dh", left, dq_low, preferred_element_type=jnp.float32),
                jnp.einsum("nd,nh->dh", left, dk_low, preferred_element_type=jnp.float32),
                jnp.einsum("nd,nh->dh", left, dv_low, preferred_element_type=jnp.float32),
                jnp.einsum("nd,nh->dh", outer, out_low, preferred_element_type=jnp.float32),
            ],
            1,
        ),
        ("seq", "dp"),
        scatter_dimension=0,
        tiled=True,
    )
    dfirst = jnp.einsum("nh,dh->nd", dq_low, wq_all, preferred_element_type=jnp.float32)
    dfirst = dfirst + jnp.einsum("nh,dh->nd", dk_low, wk_all, preferred_element_type=jnp.float32)
    dfirst = dfirst + jnp.einsum("nh,dh->nd", dv_low, wv_all, preferred_element_type=jnp.float32)
    dx_norm, dga = norm_back(x_rows, first_inv, ga_all, dfirst)
    tokens_grad = (dresid + dx_norm).reshape(seqs, local, width)
    dga_all, dgm_all, dgq_all, dgk_all = lax.psum((dga, dgm, dgq, dgk), ("seq", "dp"))
    offset = lax.axis_index(("seq", "dp")) * own_rows
    attn_gain_grad = lax.dynamic_slice_in_dim(dga_all, offset, own_rows, 0)
    mlp_gain_grad = lax.dynamic_slice_in_dim(dgm_all, offset, own_rows, 0)
    q_cols = heads * head_size
    w_query_grad = attn_sums[:, :q_cols]
    w_key_grad = attn_sums[:, q_cols : q_cols + kv_width]
    w_value_grad = attn_sums[:, q_cols + kv_width : q_cols + 2 * kv_width]
    w_output_grad = attn_sums[:, q_cols + 2 * kv_width :]
    w_gate_grad = mlp_sums[:, :ff_width]
    w_up_grad = mlp_sums[:, ff_width : 2 * ff_width]
    w_down_grad = mlp_sums[:, 2 * ff_width :]
    return (
        block_out,
        tokens_grad,
        w_query_grad,
        w_key_grad,
        w_value_grad,
        w_output_grad,
        attn_gain_grad,
        dgq_all,
        dgk_all,
        w_gate_grad,
        w_up_grad,
        w_down_grad,
        mlp_gain_grad,
    )


def columns_body(
    tokens,
    out_grad,
    span_order,
    doc_starts,
    w_query,
    w_key,
    w_value,
    w_output,
    attn_gain,
    query_gain,
    key_gain,
    w_gate,
    w_up,
    w_down,
    mlp_gain,
):
    ranks = lax.axis_size("seq")
    copies = lax.axis_size("dp")
    _, local, width = tokens.shape
    rows = local * ranks
    span = rows // span_order.shape[0]
    head_size = query_gain.shape[0]
    kv_heads = w_key.shape[1] // head_size // ranks
    heads = w_query.shape[1] // head_size // ranks
    share = heads // kv_heads
    scale = 1.0 / math.sqrt(head_size)
    q_cols, kv_cols = heads * head_size, kv_heads * head_size
    o_cols = w_output.shape[1] // ranks
    ff = w_gate.shape[1] // ranks
    own = width // (ranks * copies)
    low = jnp.bfloat16

    def by_rank(weight):
        return weight.reshape(own, ranks, -1)

    def spread(parts):
        block = jnp.transpose(jnp.concatenate(parts, -1), (1, 0, 2))
        block = lax.all_to_all(block, "seq", 0, 0, tiled=True)
        block = lax.all_gather(block, "dp", axis=1, tiled=True)
        return block.reshape(width, -1)

    def collect(grad):
        block = grad.reshape(ranks, copies * own, -1)
        block = lax.psum_scatter(block, "dp", scatter_dimension=1, tiled=True)
        return lax.all_to_all(block, "seq", 0, 0, tiled=True).astype(jnp.float32)

    gain_rows = attn_gain[:, None]
    mlp_rows = mlp_gain[:, None]
    attn_block = spread(
        [
            by_rank((w_query * gain_rows).astype(low)),
            by_rank((w_key * gain_rows).astype(low)),
            by_rank((w_value * gain_rows).astype(low)),
            by_rank(w_output),
        ]
    )
    wqkv = attn_block[:, : q_cols + 2 * kv_cols]
    wo = attn_block[:, q_cols + 2 * kv_cols :]
    x_all = lax.all_gather(tokens[0], "seq", axis=0, tiled=True)
    mlp_block = spread(
        [by_rank((w_gate * mlp_rows).astype(low)), by_rank((w_up * mlp_rows).astype(low)), by_rank(w_down)]
    )
    wgu = mlp_block[:, : 2 * ff]
    wd = mlp_block[:, 2 * ff :]
    dy_all = lax.all_gather(out_grad[0], "seq", axis=0, tiled=True)

    pos = place(span_order, 0, rows, span)
    doc = doc_of(doc_starts, pos)[0]
    cosv, sinv = rotary(pos, head_size)
    visible = (doc[:, None] == doc[None, :]) & (pos[None, :] <= pos[:, None])

    def scaled(v):
        inv = lax.rsqrt(jnp.mean(v * v, -1, keepdims=True) + EPS)
        return v * inv, inv

    def scaled_back(v, inv, grad):
        dv = inv * grad - v * inv * inv * inv * jnp.mean(grad * v, -1, keepdims=True)
        return dv, jnp.sum(grad * v * inv, 0)

    first_in = scaled(x_all.astype(jnp.float32))[0].astype(low)
    qkv = jnp.dot(first_in, wqkv, preferred_element_type=jnp.float32)
    q_raw = qkv[:, :q_cols].reshape(rows, heads, head_size)
    k_raw = qkv[:, q_cols : q_cols + kv_cols].reshape(rows, kv_heads, head_size)
    v_low = qkv[:, q_cols + kv_cols :].astype(low).reshape(rows, kv_heads, head_size)
    q_normed, q_inv = normed(q_raw, query_gain)
    k_normed, k_inv = normed(k_raw, key_gain)
    q_low = rotate(q_normed, cosv, sinv).astype(low).reshape(rows, kv_heads, share, head_size)
    k_low = rotate(k_normed, cosv, sinv).astype(low)
    raw = jnp.einsum("qgjd,kgd->gjqk", q_low, k_low, preferred_element_type=jnp.float32) * scale
    raw = jnp.where(visible, raw, NEG)
    top = jnp.max(raw, -1, keepdims=True)
    prob = jnp.where(visible, jnp.exp(raw - top), 0.0)
    prob = prob / jnp.sum(prob, -1, keepdims=True)
    prob_low = prob.astype(low)
    attn_vals = jnp.einsum("gjqk,kgd->qgjd", prob_low, v_low, preferred_element_type=jnp.float32)
    out_low = attn_vals.astype(low).reshape(rows, o_cols)
    part = jnp.einsum("nh,dh->nd", out_low, wo, preferred_element_type=jnp.float32).astype(low)
    summed = lax.psum_scatter(part, "seq", scatter_dimension=0, tiled=True)
    x_rows = tokens[0].astype(jnp.float32)
    resid = x_rows + summed.astype(jnp.float32)
    second_norm, second_inv = scaled(resid)
    second_in = lax.all_gather(second_norm.astype(low), "seq", axis=0, tiled=True)
    gate_up = jnp.dot(second_in, wgu, preferred_element_type=jnp.float32)
    gate, upper = gate_up[:, :ff], gate_up[:, ff:]
    sigma = jax.nn.sigmoid(gate)
    act = gate * sigma
    hidden = (act * upper).astype(low)
    part = jnp.einsum("nf,df->nd", hidden, wd, preferred_element_type=jnp.float32).astype(low)
    summed = lax.psum_scatter(part, "seq", scatter_dimension=0, tiled=True)
    block_out = (resid + summed.astype(jnp.float32)).astype(low)[None]

    dmid = jnp.dot(dy_all, wd, preferred_element_type=jnp.float32)
    dgate = (dmid * upper * sigma * (1.0 + gate * (1.0 - sigma))).astype(low)
    dupper = (dmid * act).astype(low)
    dgu = jnp.concatenate([dgate, dupper], -1)
    part = jnp.einsum("nf,df->nd", dgu, wgu, preferred_element_type=jnp.float32).astype(low)
    dsecond = lax.psum_scatter(part, "seq", scatter_dimension=0, tiled=True).astype(jnp.float32)
    gu_grad = jnp.einsum("nd,nf->df", second_in, dgu, preferred_element_type=jnp.float32)
    down_grad = jnp.einsum("nd,nf->df", dy_all, hidden, preferred_element_type=jnp.float32)
    mlp_sums = collect(jnp.concatenate([gu_grad.astype(low), down_grad.astype(low)], -1))
    dresid_norm, dgm = scaled_back(resid, second_inv, dsecond)
    dresid = out_grad[0].astype(jnp.float32) + dresid_norm
    dresid_all = lax.all_gather(dresid.astype(low), "seq", axis=0, tiled=True)
    dout_low = jnp.dot(dresid_all, wo, preferred_element_type=jnp.float32).astype(low)
    wo_grad = jnp.einsum("nd,nh->dh", dresid_all, out_low, preferred_element_type=jnp.float32)
    dout = dout_low.reshape(rows, kv_heads, share, head_size)
    delta = jnp.transpose(jnp.sum(dout.astype(jnp.float32) * attn_vals, -1), (1, 2, 0))
    dprob = jnp.einsum("qgjd,kgd->gjqk", dout, v_low, preferred_element_type=jnp.float32)
    dscore = (prob * (dprob - delta[..., None])).astype(low)
    dq_rot = jnp.einsum("gjqk,kgd->qgjd", dscore, k_low, preferred_element_type=jnp.float32) * scale
    dk_rot = jnp.einsum("gjqk,qgjd->kgd", dscore, q_low, preferred_element_type=jnp.float32) * scale
    dv = jnp.einsum("gjqk,qgjd->kgd", prob_low, dout, preferred_element_type=jnp.float32)
    dq_rot = dq_rot.reshape(rows, heads, head_size)
    dq_raw, dgq = norm_back(q_raw, q_inv, query_gain, rotate_back(dq_rot, cosv, sinv))
    dk_raw, dgk = norm_back(k_raw, k_inv, key_gain, rotate_back(dk_rot, cosv, sinv))
    dqkv = jnp.concatenate(
        [dq_raw.reshape(rows, -1), dk_raw.reshape(rows, -1), dv.reshape(rows, -1)], -1
    ).astype(low)
    part = jnp.einsum("nh,dh->nd", dqkv, wqkv, preferred_element_type=jnp.float32).astype(low)
    dfirst = lax.psum_scatter(part, "seq", scatter_dimension=0, tiled=True).astype(jnp.float32)
    qkv_grad = jnp.einsum("nd,nh->dh", first_in, dqkv, preferred_element_type=jnp.float32)
    first_inv = scaled(x_rows)[1]
    dx_norm, dga = scaled_back(x_rows, first_inv, dfirst)
    tokens_grad = (dresid + dx_norm)[None]
    small = jnp.concatenate(
        [
            dga[:, None],
            dgm[:, None],
            jnp.tile(dgq.reshape(-1, own).T, (ranks * copies, 1)),
            jnp.tile(dgk.reshape(-1, own).T, (ranks * copies, 1)),
        ],
        -1,
    )
    small = jnp.pad(small, ((0, 0), (0, head_size - small.shape[1])))
    attn_sums = collect(jnp.concatenate([qkv_grad.astype(low), wo_grad.astype(low), small.astype(low)], -1))
    gains = jnp.sum(attn_sums[..., q_cols + 2 * kv_cols + o_cols :], 0)
    pieces = head_size // own

    def wide(part):
        return jnp.transpose(part, (1, 0, 2)).reshape(own, -1)

    return (
        block_out,
        tokens_grad,
        wide(attn_sums[..., :q_cols]) * gain_rows,
        wide(attn_sums[..., q_cols : q_cols + kv_cols]) * gain_rows,
        wide(attn_sums[..., q_cols + kv_cols : q_cols + 2 * kv_cols]) * gain_rows,
        wide(attn_sums[..., q_cols + 2 * kv_cols : q_cols + 2 * kv_cols + o_cols]),
        gains[:, 0] / attn_gain,
        gains[:, 2 : 2 + pieces].T.reshape(-1),
        gains[:, 2 + pieces : 2 + 2 * pieces].T.reshape(-1),
        wide(mlp_sums[..., :ff]) * mlp_rows,
        wide(mlp_sums[..., ff : 2 * ff]) * mlp_rows,
        wide(mlp_sums[..., 2 * ff :]),
        gains[:, 1] / mlp_gain,
    )


def body(*args):
    tokens, w_key, query_gain = args[0], args[5], args[9]
    groups = w_key.shape[1] // query_gain.shape[0]
    if tokens.shape[0] == 1 and groups % lax.axis_size("seq") == 0:
        return columns_body(*args)
    return gathered_body(*args)


def solution(mesh):
    return jax.shard_map(
        body,
        mesh=mesh,
        in_specs=(
            P("dp", "seq", None),
            P("dp", "seq", None),
            P(),
            P("dp", None),
            P(("seq", "dp"), None),
            P(("seq", "dp"), None),
            P(("seq", "dp"), None),
            P(("seq", "dp"), None),
            P(("seq", "dp")),
            P(),
            P(),
            P(("seq", "dp"), None),
            P(("seq", "dp"), None),
            P(("seq", "dp"), None),
            P(("seq", "dp")),
        ),
        out_specs=(
            P("dp", "seq", None),
            P("dp", "seq", None),
            P(("seq", "dp"), None),
            P(("seq", "dp"), None),
            P(("seq", "dp"), None),
            P(("seq", "dp"), None),
            P(("seq", "dp")),
            P(),
            P(),
            P(("seq", "dp"), None),
            P(("seq", "dp"), None),
            P(("seq", "dp"), None),
            P(("seq", "dp")),
        ),
        check_vma=False,
    )
```

```python
import functools
import math

import jax
import jax.numpy as jnp
from jax import lax
from jax.experimental import pallas as pl
from jax.experimental.pallas import tpu as pltpu
from jax.sharding import PartitionSpec as P

EPS = 1e-06
NEG = -1e30


def normed(v, gain):
    scale_inv = lax.rsqrt(jnp.mean(v * v, -1, keepdims=True) + EPS)
    return (v * scale_inv * gain, scale_inv)


def norm_back(v, scale_inv, gain, grad):
    scaled = grad * gain
    inner = jnp.mean(scaled * v, -1, keepdims=True)
    dv = scale_inv * scaled - v * scale_inv * scale_inv * scale_inv * inner
    dgain = jnp.sum((grad * v * scale_inv).reshape(-1, v.shape[-1]), 0)
    return (dv, dgain)


def rotary(pos, width):
    half = width // 2
    freqs = jnp.exp(jnp.arange(half, dtype=jnp.float32) * (-2.0 / width * math.log(1000000.0)))
    angle = pos.astype(jnp.float32)[:, None] * freqs[None, :]
    return (jnp.cos(angle)[:, None, :], jnp.sin(angle)[:, None, :])


def rotate(v, cosv, sinv):
    half = v.shape[-1] // 2
    first, second = (v[..., :half], v[..., half:])
    return jnp.concatenate([first * cosv - second * sinv, second * cosv + first * sinv], -1)


def rotate_back(grad, cosv, sinv):
    half = grad.shape[-1] // 2
    first, second = (grad[..., :half], grad[..., half:])
    return jnp.concatenate([first * cosv + second * sinv, second * cosv - first * sinv], -1)


def place(order, begin, count, span):
    rows = begin + jnp.arange(count, dtype=jnp.int32)
    slots = rows // span
    picked = slots[:, None] == jnp.arange(order.shape[0], dtype=jnp.int32)[None, :]
    return jnp.sum(jnp.where(picked, order[None, :], 0), -1) * span + rows % span


def doc_of(starts, pos):
    return jnp.sum((starts[:, None, :] <= pos[None, :, None]).astype(jnp.int32), -1)


def gathered_body(
    tokens,
    out_grad,
    span_order,
    doc_starts,
    w_query,
    w_key,
    w_value,
    w_output,
    attn_gain,
    query_gain,
    key_gain,
    w_gate,
    w_up,
    w_down,
    mlp_gain,
):
    seqs, local, width = tokens.shape
    span = local // 2
    head_size = query_gain.shape[0]
    kv_heads = w_key.shape[1] // head_size
    heads = w_query.shape[1] // head_size
    share = heads // kv_heads
    kv_width = kv_heads * head_size
    ff_width = w_gate.shape[1]
    scale = 1.0 / math.sqrt(head_size)
    total_rows = seqs * local
    own_rows = width // lax.axis_size(("seq", "dp"))
    qpos = place(span_order, lax.axis_index("seq") * local, local, span)
    qdoc = doc_of(doc_starts, qpos)
    cosv, sinv = rotary(qpos, head_size)

    def gather_attn():
        return (
            lax.all_gather(w_query, ("seq", "dp"), axis=0, tiled=True),
            lax.all_gather(w_key, ("seq", "dp"), axis=0, tiled=True),
            lax.all_gather(w_value, ("seq", "dp"), axis=0, tiled=True),
            lax.all_gather(w_output, ("seq", "dp"), axis=0, tiled=True),
            lax.all_gather(
                attn_gain.astype(jnp.bfloat16), ("seq", "dp"), axis=0, tiled=True
            ).astype(attn_gain.dtype),
        )

    def gather_mlp():
        return (
            lax.all_gather(w_gate, ("seq", "dp"), axis=0, tiled=True),
            lax.all_gather(w_up, ("seq", "dp"), axis=0, tiled=True),
            lax.all_gather(w_down, ("seq", "dp"), axis=0, tiled=True),
            lax.all_gather(mlp_gain.astype(jnp.bfloat16), ("seq", "dp"), axis=0, tiled=True).astype(
                mlp_gain.dtype
            ),
        )

    x_rows = tokens.astype(jnp.float32).reshape(total_rows, width)
    wq_all, wk_all, wv_all, wo_all, ga_all = gather_attn()
    first_norm, first_inv = normed(x_rows, ga_all)
    first_in = first_norm.astype(jnp.bfloat16)
    q_raw = jnp.dot(first_in, wq_all, preferred_element_type=jnp.float32).reshape(
        seqs, local, heads, head_size
    )
    k_raw = jnp.dot(first_in, wk_all, preferred_element_type=jnp.float32).reshape(
        seqs, local, kv_heads, head_size
    )
    v_low = (
        jnp.dot(first_in, wv_all, preferred_element_type=jnp.float32)
        .astype(jnp.bfloat16)
        .reshape(seqs, local, kv_heads, head_size)
    )
    q_normed, q_inv = normed(q_raw, query_gain)
    k_normed, k_inv = normed(k_raw, key_gain)
    q_low = rotate(q_normed, cosv, sinv).astype(jnp.bfloat16)
    k_low = rotate(k_normed, cosv, sinv).astype(jnp.bfloat16)
    q_group = q_low.reshape(seqs, local, kv_heads, share, head_size)

    def scores(piece_key, start):
        count = piece_key.shape[1]
        kpos = place(span_order, start, count, span)
        kdoc = doc_of(doc_starts, kpos)
        visible = (qdoc[:, :, None] == kdoc[:, None, :]) & (
            kpos[None, None, :] <= qpos[None, :, None]
        )
        raw = (
            jnp.einsum("sqgjd,skgd->sgjqk", q_group, piece_key, preferred_element_type=jnp.float32)
            * scale
        )
        return (raw, visible[:, None, None])

    start_top = jnp.full((seqs, kv_heads, share, local), NEG, jnp.float32)
    piece = (
        lax.all_gather(k_low, "seq", axis=1, tiled=True),
        lax.all_gather(v_low, "seq", axis=1, tiled=True),
    )
    top = start_top
    raw, visible = scores(piece[0], jnp.int32(0))
    raw = jnp.where(visible, raw, NEG)
    new_top = jnp.maximum(top, jnp.max(raw, -1))
    weights = jnp.where(visible, jnp.exp(raw - new_top[..., None]), 0.0)
    total = jnp.sum(weights, -1)
    summed = jnp.einsum(
        "sgjqk,skgd->sgjqd",
        weights.astype(jnp.bfloat16),
        piece[1],
        preferred_element_type=jnp.float32,
    )
    top, total, summed = (new_top, total, summed)
    log_total = top + jnp.log(total)
    attn_vals = summed / total[..., None]
    out_low = (
        jnp.transpose(attn_vals, (0, 3, 1, 2, 4))
        .reshape(total_rows, heads * head_size)
        .astype(jnp.bfloat16)
    )
    resid = x_rows + jnp.einsum("nh,dh->nd", out_low, wo_all, preferred_element_type=jnp.float32)
    wg_all, wu_all, wd_all, gm_all = gather_mlp()
    second_norm, second_inv = normed(resid, gm_all)
    second_in = second_norm.astype(jnp.bfloat16)
    gate = jnp.dot(second_in, wg_all, preferred_element_type=jnp.float32)
    upper = jnp.dot(second_in, wu_all, preferred_element_type=jnp.float32)
    sigma = jax.nn.sigmoid(gate)
    act = gate * sigma
    hidden = (act * upper).astype(jnp.bfloat16)
    result = resid + jnp.einsum("nf,df->nd", hidden, wd_all, preferred_element_type=jnp.float32)
    block_out = result.astype(jnp.bfloat16).reshape(seqs, local, width)
    grad_low = out_grad.reshape(total_rows, width)
    wg_all, wu_all, wd_all, gm_all = gather_mlp()
    dmid = jnp.einsum("nd,df->nf", grad_low, wd_all, preferred_element_type=jnp.float32)
    dgate = (dmid * upper * sigma * (1.0 + gate * (1.0 - sigma))).astype(jnp.bfloat16)
    dupper = (dmid * act).astype(jnp.bfloat16)
    left = second_in
    outer = grad_low
    mlp_sums = lax.psum_scatter(
        jnp.concatenate(
            [
                jnp.einsum("nd,nf->df", left, dgate, preferred_element_type=jnp.float32),
                jnp.einsum("nd,nf->df", left, dupper, preferred_element_type=jnp.float32),
                jnp.einsum("nd,nf->df", outer, hidden, preferred_element_type=jnp.float32),
            ],
            1,
        ),
        ("seq", "dp"),
        scatter_dimension=0,
        tiled=True,
    )
    dsecond = jnp.einsum(
        "nf,df->nd", dgate, wg_all, preferred_element_type=jnp.float32
    ) + jnp.einsum("nf,df->nd", dupper, wu_all, preferred_element_type=jnp.float32)
    dresid_norm, dgm = norm_back(resid, second_inv, gm_all, dsecond)
    dresid = grad_low.astype(jnp.float32) + dresid_norm
    dresid_low = dresid.astype(jnp.bfloat16)
    wq_all, wk_all, wv_all, wo_all, ga_all = gather_attn()
    dout_low = jnp.einsum(
        "nd,dh->nh", dresid_low, wo_all, preferred_element_type=jnp.float32
    ).astype(jnp.bfloat16)
    dout_group = dout_low.reshape(seqs, local, kv_heads, share, head_size)
    delta = jnp.sum(jnp.transpose(dout_group.astype(jnp.float32), (0, 2, 3, 1, 4)) * attn_vals, -1)
    piece = (
        lax.all_gather(k_low, "seq", axis=1, tiled=True),
        lax.all_gather(v_low, "seq", axis=1, tiled=True),
    )
    count = piece[0].shape[1]
    raw, visible = scores(piece[0], jnp.int32(0))
    prob = jnp.where(visible, jnp.exp(raw - log_total[..., None]), 0.0)
    dprob = jnp.einsum(
        "sqgjd,skgd->sgjqk", dout_group, piece[1], preferred_element_type=jnp.float32
    )
    dscore = (prob * (dprob - delta[..., None])).astype(jnp.bfloat16)
    dq_sum = jnp.einsum("sgjqk,skgd->sqgjd", dscore, piece[0], preferred_element_type=jnp.float32)
    dk_part = (
        jnp.einsum("sgjqk,sqgjd->skgd", dscore, q_group, preferred_element_type=jnp.float32) * scale
    )
    dv_part = jnp.einsum(
        "sgjqk,sqgjd->skgd",
        prob.astype(jnp.bfloat16),
        dout_group,
        preferred_element_type=jnp.float32,
    )
    joined = jnp.concatenate(
        [dk_part.reshape(seqs, count, kv_width), dv_part.reshape(seqs, count, kv_width)], -1
    )
    buffer = joined
    dq_sum, buffer = (dq_sum, buffer)
    key_sums = lax.psum_scatter(
        buffer.astype(jnp.bfloat16), "seq", scatter_dimension=1, tiled=True
    ).astype(jnp.float32)
    dq_rot = (dq_sum * scale).reshape(seqs, local, heads, head_size)
    dq_raw, dgq = norm_back(q_raw, q_inv, query_gain, rotate_back(dq_rot, cosv, sinv))
    dk_rot = key_sums[..., :kv_width].reshape(seqs, local, kv_heads, head_size)
    dk_raw, dgk = norm_back(k_raw, k_inv, key_gain, rotate_back(dk_rot, cosv, sinv))
    dq_low = dq_raw.reshape(total_rows, heads * head_size).astype(jnp.bfloat16)
    dk_low = dk_raw.reshape(total_rows, kv_width).astype(jnp.bfloat16)
    dv_low = key_sums[..., kv_width:].reshape(total_rows, kv_width).astype(jnp.bfloat16)
    left = first_in
    outer = dresid_low
    attn_sums = lax.psum_scatter(
        jnp.concatenate(
            [
                jnp.einsum("nd,nh->dh", left, dq_low, preferred_element_type=jnp.float32),
                jnp.einsum("nd,nh->dh", left, dk_low, preferred_element_type=jnp.float32),
                jnp.einsum("nd,nh->dh", left, dv_low, preferred_element_type=jnp.float32),
                jnp.einsum("nd,nh->dh", outer, out_low, preferred_element_type=jnp.float32),
            ],
            1,
        ),
        ("seq", "dp"),
        scatter_dimension=0,
        tiled=True,
    )
    dfirst = jnp.einsum("nh,dh->nd", dq_low, wq_all, preferred_element_type=jnp.float32)
    dfirst = dfirst + jnp.einsum("nh,dh->nd", dk_low, wk_all, preferred_element_type=jnp.float32)
    dfirst = dfirst + jnp.einsum("nh,dh->nd", dv_low, wv_all, preferred_element_type=jnp.float32)
    dx_norm, dga = norm_back(x_rows, first_inv, ga_all, dfirst)
    tokens_grad = (dresid + dx_norm).reshape(seqs, local, width)
    dga_all, dgm_all, dgq_all, dgk_all = lax.psum((dga, dgm, dgq, dgk), ("seq", "dp"))
    offset = lax.axis_index(("seq", "dp")) * own_rows
    attn_gain_grad = lax.dynamic_slice_in_dim(dga_all, offset, own_rows, 0)
    mlp_gain_grad = lax.dynamic_slice_in_dim(dgm_all, offset, own_rows, 0)
    q_cols = heads * head_size
    w_query_grad = attn_sums[:, :q_cols]
    w_key_grad = attn_sums[:, q_cols : q_cols + kv_width]
    w_value_grad = attn_sums[:, q_cols + kv_width : q_cols + 2 * kv_width]
    w_output_grad = attn_sums[:, q_cols + 2 * kv_width :]
    w_gate_grad = mlp_sums[:, :ff_width]
    w_up_grad = mlp_sums[:, ff_width : 2 * ff_width]
    w_down_grad = mlp_sums[:, 2 * ff_width :]
    return (
        block_out,
        tokens_grad,
        w_query_grad,
        w_key_grad,
        w_value_grad,
        w_output_grad,
        attn_gain_grad,
        dgq_all,
        dgk_all,
        w_gate_grad,
        w_up_grad,
        w_down_grad,
        mlp_gain_grad,
    )


LOW = jnp.bfloat16
MESH = pl.DeviceIdType.MESH
LIMIT = 60 * 2**20


def ring_order(ranks):
    half = ranks // 2
    order = [0]
    for step in range(1, half):
        order += [step, ranks - step]
    return order + [half]


def ring_place(seq, ranks):
    z, x = lax.div(seq, 2), lax.rem(seq, 2)
    return z + x * (ranks - 1 - 2 * z)


def ring_seq(place, ranks):
    half = ranks // 2
    x, z = lax.div(place, half), lax.rem(place, half)
    return 2 * (z + x * (half - 1 - 2 * z)) + x


def neighbours(ranks):
    seq, dp = lax.axis_index("seq"), lax.axis_index("dp")
    at = ring_place(seq, ranks)
    right = ring_seq(lax.rem(at + 1, ranks), ranks)
    left = ring_seq(lax.rem(at + ranks - 1, ranks), ranks)
    return (right, dp), (left, dp)


def greet(devices):
    barrier = pltpu.get_barrier_semaphore()
    for device in devices:
        pl.semaphore_signal(barrier, inc=1, device_id=device, device_id_type=MESH)
    pl.semaphore_wait(barrier, len(devices))


def push(src, dst, send, recv, device):
    return pltpu.make_async_remote_copy(
        src_ref=src, dst_ref=dst, send_sem=send, recv_sem=recv, device_id=device, device_id_type=MESH
    )


def dot_nn(left, right):
    return jnp.dot(left, right, preferred_element_type=jnp.float32)


def dot_nt(left, right):
    return lax.dot_general(left, right, (((1,), (1,)), ((), ())), preferred_element_type=jnp.float32)


def dot_tn(left, right):
    return lax.dot_general(left, right, (((0,), (0,)), ((), ())), preferred_element_type=jnp.float32)


class RingGather:
    def __init__(self, buf, local, ranks, send, recv, right, left):
        self.buf, self.local, self.half = buf, local, ranks // 2
        self.send, self.recv, self.right, self.left = send, recv, right, left
        self.row = {rel: at * local for at, rel in enumerate(ring_order(ranks))}
        self.ranks = ranks

    def copies(self, step):
        last = step == self.half
        rows = self.local // 2 if last else self.local
        skip = self.local // 2 if last else 0
        pairs = (
            ((self.ranks - step + 1) % self.ranks, self.ranks - step, 0, self.right),
            (step - 1, step, skip, self.left),
        )
        return [
            push(
                self.buf.at[pl.ds(self.row[src] + begin, rows)],
                self.buf.at[pl.ds(self.row[dst] + begin, rows)],
                self.send.at[way, step - 1],
                self.recv.at[way, step - 1],
                device,
            )
            for way, (src, dst, begin, device) in enumerate(pairs)
        ]

    def start(self, step):
        for copy in self.copies(step):
            copy.start()

    def arrive(self, step):
        for copy in self.copies(step):
            copy.wait_recv()

    def finish(self):
        for step in range(1, self.half + 1):
            for copy in self.copies(step):
                copy.wait_send()

    def rows(self, step):
        if step == 0:
            return 0, self.local
        if step == self.half:
            return self.row[self.half], self.local
        return self.row[step], 2 * self.local


class RingSum:
    def __init__(self, part, term, out_buf, in_buf, local, ranks, send, recv, right, left):
        self.part, self.term, self.out_buf, self.in_buf = part, term, out_buf, in_buf
        self.local, self.ranks, self.half = local, ranks, ranks // 2
        self.send, self.recv, self.right, self.left = send, recv, right, left
        self.row = {rel: at * local for at, rel in enumerate(ring_order(ranks))}

    def copies(self, step):
        rows = self.local // 2 if step == 1 else self.local
        skip = self.local // 2 if step == 1 else 0
        return [
            push(
                self.out_buf.at[way, step - 1, pl.ds(begin, rows)],
                self.in_buf.at[way, step - 1, pl.ds(begin, rows)],
                self.send.at[way, step - 1],
                self.recv.at[way, step - 1],
                device,
            )
            for way, begin, device in ((0, 0, self.right), (1, skip, self.left))
        ]

    def compute(self, step):
        if step == 1:
            self.part(self.row[self.half], self.local)
        elif step <= self.half:
            self.part(self.row[self.half + 1 - step], 2 * self.local)
        else:
            self.part(0, self.local)

    def launch(self, step):
        local, skip = self.local, self.local // 2
        if step == 1:
            self.out_buf[0, 0, :skip] = self.term[:skip].astype(LOW)
            self.out_buf[1, 0, skip:] = self.term[skip:local].astype(LOW)
        else:
            for copy in self.copies(step - 1):
                copy.wait_recv()
            for way in range(2):
                for begin, with_sum in ((0, step > 2 or way == 0), (skip, step > 2 or way == 1)):
                    value = self.term[pl.ds(way * local + begin, skip)]
                    if with_sum:
                        value = value + self.in_buf[way, step - 2, pl.ds(begin, skip)].astype(jnp.float32)
                    self.out_buf[way, step - 1, pl.ds(begin, skip)] = value.astype(LOW)
        for copy in self.copies(step):
            copy.start()

    def last(self, begin, count):
        rows = pl.ds(begin, count)
        value = self.term[rows] + self.in_buf[0, self.half - 1, rows].astype(jnp.float32)
        return value + self.in_buf[1, self.half - 1, rows].astype(jnp.float32)

    def arrive_last(self):
        for copy in self.copies(self.half):
            copy.wait_recv()

    def finish(self):
        for step in range(1, self.half + 1):
            for copy in self.copies(step):
                copy.wait_send()


def ring_sems(ranks):
    return [pltpu.SemaphoreType.DMA((2, ranks // 2)), pltpu.SemaphoreType.DMA((2, ranks // 2))]


def sum_bufs(local, ranks, width):
    shape = (2, ranks // 2, local, width)
    return [pltpu.VMEM((2 * local, width), jnp.float32), pltpu.VMEM(shape, LOW), pltpu.VMEM(shape, LOW)]


def turn(v):
    return pltpu.roll(v, v.shape[-1] // 2, v.ndim - 1)


def rows_scaled(v):
    inv = lax.rsqrt(jnp.mean(v * v, -1, keepdims=True) + EPS)
    return v * inv, inv


def rows_scaled_back(v, inv, grad):
    return inv * grad - v * (inv * inv * inv * jnp.mean(grad * v, -1, keepdims=True))


class Spread:
    def __init__(self, rows, block, ranks, own, sems):
        self.rows, self.block, self.ranks, self.own = rows, block, ranks, own
        self.send, self.recv, self.hop_send, self.hop_recv, self.here = sems
        self.seq, self.dp = lax.axis_index("seq"), lax.axis_index("dp")
        y, core = lax.div(self.dp, 2), lax.rem(self.dp, 2)
        self.beside, self.sibling = (1 - y) * 2 + core, y * 2 + 1 - core

    def at(self, dp):
        return pl.ds(pl.multiple_of(dp * self.own, self.own), self.own)

    def exchange(self):
        for step in range(1, self.ranks):
            peer = lax.rem(self.seq + step, self.ranks)
            yield push(
                self.rows.at[peer],
                self.block.at[self.seq, self.at(self.dp)],
                self.send.at[step],
                self.recv.at[step],
                (peer, self.dp),
            )

    def keep(self):
        return pltpu.make_async_copy(
            self.rows.at[self.seq], self.block.at[self.seq, self.at(self.dp)], self.here
        )

    def hop(self, number):
        dp = self.beside if number == 2 else self.dp
        part = self.block.at[:, self.at(dp)]
        to = self.beside if number == 0 else self.sibling
        return push(part, part, self.hop_send.at[number], self.hop_recv.at[number], (self.seq, to))

    def start(self):
        self.keep().start()
        for copy in self.exchange():
            copy.start()

    def arrive(self):
        self.keep().wait()
        for copy in self.exchange():
            copy.wait_recv()

    def finish(self):
        for copy in self.exchange():
            copy.wait_send()
        for number in range(3):
            self.hop(number).wait_send()


def spread_sems(ranks):
    return [
        pltpu.SemaphoreType.DMA((ranks,)),
        pltpu.SemaphoreType.DMA((ranks,)),
        pltpu.SemaphoreType.DMA((3,)),
        pltpu.SemaphoreType.DMA((3,)),
        pltpu.SemaphoreType.DMA,
    ]


def enter_kernel(ranks, tokens, attn_rows, mlp_rows, first_in, qkv, attn_block, mlp_block, held, *sems):
    local, width = tokens.shape
    own = attn_rows.shape[1]
    cols = qkv.shape[1]
    seq, dp = lax.axis_index("seq"), lax.axis_index("dp")
    right, left = neighbours(ranks)
    attn = Spread(attn_rows, attn_block, ranks, own, sems[2:7])
    mlp = Spread(mlp_rows, mlp_block, ranks, own, sems[7:12])
    peers = [(lax.rem(seq + step, ranks), dp) for step in range(1, ranks)]
    greet(peers + [(seq, attn.beside), (seq, attn.sibling)])
    ring = RingGather(held, local, ranks, sems[0], sems[1], right, left)
    attn.start()
    held[:local] = tokens[...]
    ring.start(1)
    mlp.start()

    def scale_rows(begin, count):
        def some(at, _):
            rows = pl.ds(pl.multiple_of(begin + at * 32, 32), 32)
            first_in[rows] = rows_scaled(held[rows].astype(jnp.float32))[0].astype(LOW)
            return 0

        lax.fori_loop(0, count // 32, some, 0)

    def project(begin, count):
        rows = pl.ds(begin, count)
        weight = attn_block[:, :, :cols].reshape(width, cols)
        qkv[rows] = dot_nn(first_in[rows], weight)

    scale_rows(*ring.rows(0))
    attn.arrive()
    attn.hop(0).start()
    ring.arrive(1)
    ring.start(2)
    scale_rows(*ring.rows(1))
    attn.hop(0).wait_recv()
    attn.hop(1).start()
    attn.hop(2).start()
    ring.arrive(2)
    ring.start(3)
    scale_rows(*ring.rows(2))
    attn.hop(1).wait_recv()
    attn.hop(2).wait_recv()
    for step in range(3):
        project(*ring.rows(step))
    for step in range(3, ranks // 2 + 1):
        ring.arrive(step)
        if step < ranks // 2:
            ring.start(step + 1)
        scale_rows(*ring.rows(step))
        project(*ring.rows(step))
    mlp.arrive()
    mlp.hop(0).start()
    mlp.hop(1).start()
    mlp.hop(0).wait_recv()
    mlp.hop(2).start()
    mlp.hop(1).wait_recv()
    mlp.hop(2).wait_recv()
    ring.finish()
    attn.finish()
    mlp.finish()


def attend_kernel(
    ranks, kv_heads, out_grad, tokens, qkv, attn_block, cosv, sinv, pos, begins, pos_row, query_gain, key_gain,
    dy_all, q_low, k_low, v_low, prob, out_low, resid, second, term, out_buf, in_buf, *sems,
):
    local, width = tokens.shape
    rows = local * ranks
    size = cosv.shape[1]
    heads = q_low.shape[0]
    share = heads // kv_heads
    scale = 1.0 / math.sqrt(size)
    right, left = neighbours(ranks)
    greet([right, left])
    ring = RingGather(dy_all, local, ranks, sems[0], sems[1], right, left)
    dy_all[:local] = out_grad[...]
    ring.start(1)
    tile = rows // (ranks // 2)

    def rotated(at, rows_at, gain):
        v = rows_scaled(qkv[rows_at, at * size : (at + 1) * size])[0] * gain[...]
        return (v * cosv[rows_at] + turn(v) * sinv[rows_at]).astype(LOW)

    for piece in range(ranks // 2):
        rows_at = pl.ds(piece * tile, tile)
        for head in range(heads):
            q_low[head, rows_at] = rotated(head, rows_at, query_gain)
        for group in range(kv_heads):
            k_low[group, rows_at] = rotated(heads + group, rows_at, key_gain)
            at = (heads + kv_heads + group) * size
            v_low[group, rows_at] = qkv[rows_at, at : at + size].astype(LOW)
    for piece in range(ranks // 2):
        if piece > 0:
            ring.arrive(piece)
            ring.start(piece + 1)
        rows_at = pl.ds(piece * tile, tile)
        seen = (pos_row[...] <= pos[rows_at]) & (pos_row[...] >= begins[rows_at])
        for head in range(heads):
            raw = dot_nt(q_low[head, rows_at], k_low[head // share]) * scale
            raw = jnp.where(seen, raw, NEG)
            weight = jnp.exp(raw - jnp.max(raw, -1, keepdims=True))
            weight = (weight * (1.0 / jnp.sum(weight, -1, keepdims=True))).astype(LOW)
            prob[head, rows_at] = weight
            value = dot_nn(weight, v_low[head // share])
            out_low[rows_at, head * size : (head + 1) * size] = value.astype(LOW)
    first_col = (heads + 2 * kv_heads) * size
    deep = attn_block.shape[1]

    def part(begin, count):
        def some(at, _):
            value = dot_nt(out_low[pl.ds(begin, count)], attn_block[at, :, first_col:])
            term[:count, pl.ds(pl.multiple_of(at * deep, deep), deep)] = value
            return 0

        lax.fori_loop(0, ranks, some, 0)

    total = RingSum(part, term, out_buf, in_buf, local, ranks, sems[2], sems[3], right, left)
    for step in range(1, ranks // 2 + 1):
        total.compute(step)
        total.launch(step)
    total.compute(ranks // 2 + 1)
    ring.arrive(ranks // 2)
    total.arrive_last()

    def some(at, _):
        begin = pl.multiple_of(at * 32, 32)
        rows_at = pl.ds(begin, 32)
        value = tokens[rows_at].astype(jnp.float32) + total.last(begin, 32)
        resid[rows_at] = value
        second[rows_at] = rows_scaled(value)[0].astype(LOW)
        return 0

    lax.fori_loop(0, local // 32, some, 0)
    ring.finish()
    total.finish()


def mlp_kernel(
    ranks, second, resid, out_grad, dy_all, mlp_block, block_out, dresid, dresid_low, gain_grad, grads,
    held, weights, hidden, dgu, term, out_buf, in_buf, y_term, y_out, y_in, here, *sems,
):
    local, width = second.shape
    ff = hidden.shape[1]
    deep = weights.shape[1]
    half = ranks // 2
    right, left = neighbours(ranks)
    load = pltpu.make_async_copy(mlp_block, weights, here)
    load.start()
    greet([right, left])
    ring = RingGather(held, local, ranks, sems[0], sems[1], right, left)
    held[:local] = second[...]
    ring.start(1)
    load.wait()
    wide = 256

    def middle(begin, count):
        rows = pl.ds(begin, count)

        def some(at, _):
            first = pl.multiple_of(at * wide, wide)
            gate = dot_nn(held[rows], weights[:, :, pl.ds(first, wide)].reshape(width, wide))
            upper = dot_nn(held[rows], weights[:, :, pl.ds(ff + first, wide)].reshape(width, wide))
            dmid = dot_nn(dy_all[rows], weights[:, :, pl.ds(2 * ff + first, wide)].reshape(width, wide))
            sigma = 1.0 / (1.0 + jnp.exp(-gate))
            act = gate * sigma
            hidden[rows, pl.ds(first, wide)] = (act * upper).astype(LOW)
            slope = sigma * (1.0 + gate * (1.0 - sigma))
            dgu[rows, pl.ds(first, wide)] = (dmid * upper * slope).astype(LOW)
            dgu[rows, pl.ds(ff + first, wide)] = (dmid * act).astype(LOW)
            return 0

        lax.fori_loop(0, ff // wide, some, 0)

    middle(*ring.rows(0))
    for step in range(1, half + 1):
        ring.arrive(step)
        if step < half:
            ring.start(step + 1)
        middle(*ring.rows(step))

    def back_part(begin, count):
        def some(at, _):
            value = dot_nt(dgu[pl.ds(begin, count)], weights[at, :, : 2 * ff])
            term[:count, pl.ds(pl.multiple_of(at * deep, deep), deep)] = value
            return 0

        lax.fori_loop(0, ranks, some, 0)

    def out_part(begin, count):
        def some(at, _):
            value = dot_nt(hidden[pl.ds(begin, count)], weights[at, :, 2 * ff :])
            y_term[:count, pl.ds(pl.multiple_of(at * deep, deep), deep)] = value
            return 0

        lax.fori_loop(0, ranks, some, 0)

    def weight_grads(first, count):
        def some(at, _):
            cols = pl.ds(pl.multiple_of(at * deep, deep), deep)
            grads[at, :, : 2 * ff] = dot_tn(held[:, cols], dgu[...]).astype(LOW)
            grads[at, :, 2 * ff :] = dot_tn(dy_all[:, cols], hidden[...]).astype(LOW)
            return 0

        lax.fori_loop(first, first + count, some, 0)

    back = RingSum(back_part, term, out_buf, in_buf, local, ranks, sems[2], sems[3], right, left)
    out = RingSum(out_part, y_term, y_out, y_in, local, ranks, sems[4], sems[5], right, left)
    for step in range(1, half + 1):
        back.compute(step)
        back.launch(step)
        out.compute(step)
        out.launch(step)
        weight_grads((step - 1) * ranks // half, ranks // half)
    back.compute(half + 1)
    out.compute(half + 1)
    back.arrive_last()
    gain_grad[...] = jnp.zeros_like(gain_grad)

    def finish_back(at, _):
        begin = pl.multiple_of(at * 32, 32)
        rows = pl.ds(begin, 32)
        value = resid[rows]
        normal, inv = rows_scaled(value)
        grad = back.last(begin, 32)
        full = out_grad[rows].astype(jnp.float32) + rows_scaled_back(value, inv, grad)
        dresid[rows] = full
        dresid_low[rows] = full.astype(LOW)
        gain_grad[...] += jnp.sum(grad * normal, 0, keepdims=True)
        return 0

    lax.fori_loop(0, local // 32, finish_back, 0)
    out.arrive_last()

    def finish_out(at, _):
        begin = pl.multiple_of(at * 32, 32)
        rows = pl.ds(begin, 32)
        block_out[rows] = (resid[rows] + out.last(begin, 32)).astype(LOW)
        return 0

    lax.fori_loop(0, local // 32, finish_out, 0)
    ring.finish()
    back.finish()
    out.finish()


def back_kernel(
    ranks, kv_heads, tokens, dresid, dresid_low, first_in, attn_block, qkv, cosv, sinv, query_gain, key_gain,
    q_low, k_low, v_low, prob, out_low,
    tokens_grad, gain_grad, query_gain_grad, key_gain_grad, grads,
    held, dout, dk, dv, dqkv, term, out_buf, in_buf, *sems,
):
    local, width = tokens.shape
    rows = local * ranks
    half = ranks // 2
    size = cosv.shape[1]
    heads = q_low.shape[0]
    share = heads // kv_heads
    scale = 1.0 / math.sqrt(size)
    cols = (heads + 2 * kv_heads) * size
    deep = attn_block.shape[1]
    o_cols = heads * size
    right, left = neighbours(ranks)
    greet([right, left])
    ring = RingGather(held, local, ranks, sems[0], sems[1], right, left)
    held[:local] = dresid_low[...]
    ring.start(1)

    def project(begin, count):
        at = pl.ds(begin, count)
        dout[at] = dot_nn(held[at], attn_block[:, :, cols:].reshape(width, o_cols)).astype(LOW)

    project(*ring.rows(0))
    for step in range(1, half + 1):
        ring.arrive(step)
        if step < half:
            ring.start(step + 1)
        project(*ring.rows(step))
    tile = rows // half
    query_gain_grad[...] = jnp.zeros_like(query_gain_grad)
    key_gain_grad[...] = jnp.zeros_like(key_gain_grad)

    def unrotated(grad, column, rows_at, gain, gain_grad_ref):
        grad = grad * cosv[rows_at] - turn(grad) * sinv[rows_at]
        value = qkv[rows_at, column * size : (column + 1) * size]
        normal, inv = rows_scaled(value)
        gain_grad_ref[...] += jnp.sum(grad * normal, 0, keepdims=True)
        back = rows_scaled_back(value, inv, grad * gain[...])
        dqkv[rows_at, column * size : (column + 1) * size] = back.astype(LOW)

    for head in range(heads):
        group = head // share

        def one(piece, _):
            rows_at = pl.ds(pl.multiple_of(piece * tile, tile), tile)
            weight = prob[head, rows_at]
            grad = dout[rows_at, head * size : (head + 1) * size]
            dprob = dot_nt(grad, v_low[group])
            full = weight.astype(jnp.float32)
            delta = jnp.sum(full * dprob, -1, keepdims=True)
            dscore = (full * (dprob - delta)).astype(LOW)
            dq = dot_nn(dscore, k_low[group]) * scale
            dk_add = dot_tn(dscore, q_low[head, rows_at]) * scale
            dv_add = dot_tn(weight, grad)
            dk[group] += dk_add
            dv[group] += dv_add
            unrotated(dq, head, rows_at, query_gain, query_gain_grad)
            return 0

        if head % share == 0:
            dk[group] = jnp.zeros_like(dk[group])
            dv[group] = jnp.zeros_like(dv[group])
        lax.fori_loop(0, half, one, 0)
    for group in range(kv_heads):
        def one_key(piece, _):
            rows_at = pl.ds(pl.multiple_of(piece * tile, tile), tile)
            unrotated(dk[group, rows_at], heads + group, rows_at, key_gain, key_gain_grad)
            at = (heads + kv_heads + group) * size
            dqkv[rows_at, at : at + size] = dv[group, rows_at].astype(LOW)
            return 0

        lax.fori_loop(0, half, one_key, 0)

    def part(begin, count):
        def some(at, _):
            value = dot_nt(dqkv[pl.ds(begin, count)], attn_block[at, :, :cols])
            term[:count, pl.ds(pl.multiple_of(at * deep, deep), deep)] = value
            return 0

        lax.fori_loop(0, ranks, some, 0)

    def weight_grads(first, count):
        def some(at, _):
            some_cols = pl.ds(pl.multiple_of(at * deep, deep), deep)
            grads[at, :, :cols] = dot_tn(first_in[:, some_cols], dqkv[...]).astype(LOW)
            grads[at, :, cols:] = dot_tn(held[:, some_cols], out_low[...]).astype(LOW)
            return 0

        lax.fori_loop(first, first + count, some, 0)

    total = RingSum(part, term, out_buf, in_buf, local, ranks, sems[2], sems[3], right, left)
    for step in range(1, half + 1):
        total.compute(step)
        total.launch(step)
        weight_grads((step - 1) * ranks // half, ranks // half)
    total.compute(half + 1)
    total.arrive_last()
    gain_grad[...] = jnp.zeros_like(gain_grad)

    def last(at, _):
        begin = pl.multiple_of(at * 32, 32)
        rows_at = pl.ds(begin, 32)
        value = tokens[rows_at].astype(jnp.float32)
        normal, inv = rows_scaled(value)
        grad = total.last(begin, 32)
        tokens_grad[rows_at] = dresid[rows_at] + rows_scaled_back(value, inv, grad)
        gain_grad[...] += jnp.sum(grad * normal, 0, keepdims=True)
        return 0

    lax.fori_loop(0, local // 32, last, 0)
    ring.finish()
    total.finish()


class Collect:
    def __init__(self, grads, from_core, to_y, from_y, to_all, from_all, ranks, own, cols, sems):
        self.grads, self.from_core, self.to_y, self.from_y = grads, from_core, to_y, from_y
        self.to_all, self.from_all = to_all, from_all
        self.ranks, self.own, self.cols = ranks, own, cols
        self.hop_send, self.hop_recv, self.send, self.recv, self.here = sems
        self.seq, self.dp = lax.axis_index("seq"), lax.axis_index("dp")
        self.y, self.core = lax.div(self.dp, 2), lax.rem(self.dp, 2)
        self.beside, self.sibling = (1 - self.y) * 2 + self.core, self.y * 2 + 1 - self.core

    def at(self, y, core):
        return pl.ds(pl.multiple_of((y * 2 + core) * self.own, self.own), self.own)

    def hop(self, number):
        cols = self.cols
        if number == 2:
            src, dst, to = self.to_y.at[:, :, cols], self.from_y.at[:, :, cols], self.beside
        else:
            rows = self.at(1 - self.y if number == 0 else self.y, 1 - self.core)
            src, dst, to = self.grads.at[:, rows, cols], self.from_core.at[number, :, :, cols], self.sibling
        return push(src, dst, self.hop_send.at[number], self.hop_recv.at[number], (self.seq, to))

    def exchange(self):
        for step in range(1, self.ranks):
            peer = lax.rem(self.seq + step, self.ranks)
            yield push(
                self.to_all.at[peer, :, self.cols],
                self.from_all.at[self.seq, :, self.cols],
                self.send.at[step],
                self.recv.at[step],
                (peer, self.dp),
            )

    def keep(self):
        return pltpu.make_async_copy(
            self.to_all.at[self.seq, :, self.cols], self.from_all.at[self.seq, :, self.cols], self.here
        )

    def first(self):
        self.hop(0).start()
        self.hop(1).start()

    def second(self):
        self.hop(0).wait_recv()
        rows = self.at(1 - self.y, self.core)

        def some(at, _):
            value = self.grads[at, rows, self.cols].astype(jnp.float32)
            value = value + self.from_core[0, at, :, self.cols].astype(jnp.float32)
            self.to_y[at, :, self.cols] = value.astype(LOW)
            return 0

        lax.fori_loop(0, self.ranks, some, 0)
        self.hop(2).start()

    def third(self):
        self.hop(1).wait_recv()
        self.hop(2).wait_recv()
        rows = self.at(self.y, self.core)

        def some(at, _):
            value = self.grads[at, rows, self.cols].astype(jnp.float32)
            value = value + self.from_core[1, at, :, self.cols].astype(jnp.float32)
            value = value + self.from_y[at, :, self.cols].astype(jnp.float32)
            self.to_all[at, :, self.cols] = value.astype(LOW)
            return 0

        lax.fori_loop(0, self.ranks, some, 0)
        self.keep().start()
        for copy in self.exchange():
            copy.start()

    def finish(self):
        self.keep().wait()
        for copy in self.exchange():
            copy.wait_recv()
        for copy in self.exchange():
            copy.wait_send()
        for number in range(3):
            self.hop(number).wait_send()


def collect_sems(ranks):
    return [
        pltpu.SemaphoreType.DMA((3,)),
        pltpu.SemaphoreType.DMA((3,)),
        pltpu.SemaphoreType.DMA((ranks,)),
        pltpu.SemaphoreType.DMA((ranks,)),
        pltpu.SemaphoreType.DMA,
    ]


def collect_bufs(ranks, own, cols):
    return [
        pltpu.VMEM((2, ranks, own, cols), LOW),
        pltpu.VMEM((ranks, own, cols), LOW),
        pltpu.VMEM((ranks, own, cols), LOW),
        pltpu.VMEM((ranks, own, cols), LOW),
    ]


def collect_kernel(ranks, own, cuts, count, *refs):
    grads, outs = refs[:count], refs[count : 2 * count]
    bufs = refs[2 * count : 6 * count]
    sems = refs[6 * count :]
    seq, dp = lax.axis_index("seq"), lax.axis_index("dp")
    pieces = []
    for number in range(count):
        from_core, to_y, from_y, to_all = bufs[4 * number : 4 * number + 4]
        for begin, size in cuts[number]:
            some = sems[5 * len(pieces) : 5 * len(pieces) + 5]
            pieces.append(
                Collect(
                    grads[number], from_core, to_y, from_y, to_all, outs[number], ranks, own,
                    pl.ds(begin, size), some,
                )
            )
    peers = [(lax.rem(seq + step, ranks), dp) for step in range(1, ranks)]
    greet(peers + [(seq, pieces[0].beside), (seq, pieces[0].sibling)])
    for piece in pieces:
        piece.first()
    for piece in pieces:
        piece.second()
    for piece in pieces:
        piece.third()
    for piece in pieces:
        piece.finish()


VM = pl.BlockSpec(memory_space=pltpu.VMEM)
ANY = pl.BlockSpec(memory_space=pl.ANY)


def call(kernel, number, ins, outs, scratch, operands):
    return pl.pallas_call(
        kernel,
        out_shape=[jax.ShapeDtypeStruct(shape, dtype) for shape, dtype, _ in outs],
        in_specs=ins,
        out_specs=[spec for _, _, spec in outs],
        scratch_shapes=scratch,
        compiler_params=pltpu.CompilerParams(
            collective_id=number, has_side_effects=True, vmem_limit_bytes=LIMIT
        ),
    )(*operands)


def columns_body(
    tokens,
    out_grad,
    span_order,
    doc_starts,
    w_query,
    w_key,
    w_value,
    w_output,
    attn_gain,
    query_gain,
    key_gain,
    w_gate,
    w_up,
    w_down,
    mlp_gain,
):
    ranks = lax.axis_size("seq")
    copies = lax.axis_size("dp")
    _, local, width = tokens.shape
    rows = local * ranks
    span = rows // span_order.shape[0]
    size = query_gain.shape[0]
    kv_heads = w_key.shape[1] // size // ranks
    heads = w_query.shape[1] // size // ranks
    q_cols, kv_cols = heads * size, kv_heads * size
    qkv_cols = q_cols + 2 * kv_cols
    a_cols = qkv_cols + q_cols
    ff = w_gate.shape[1] // ranks
    own = width // (ranks * copies)
    deep = own * copies
    f32 = jnp.float32

    def by_rank(parts):
        block = jnp.concatenate([part.reshape(own, ranks, -1) for part in parts], -1)
        return jnp.transpose(block, (1, 0, 2))

    gain_rows = attn_gain[:, None]
    mlp_rows = mlp_gain[:, None]
    attn_parts = [(w * gain_rows).astype(LOW) for w in (w_query, w_key, w_value)] + [w_output]
    mlp_parts = [(w * mlp_rows).astype(LOW) for w in (w_gate, w_up)] + [w_down]
    first_in, qkv, attn_block, mlp_block = call(
        functools.partial(enter_kernel, ranks),
        1,
        [VM, ANY, ANY],
        [
            ((rows, width), LOW, VM),
            ((rows, qkv_cols), f32, VM),
            ((ranks, deep, a_cols), LOW, VM),
            ((ranks, deep, 3 * ff), LOW, ANY),
        ],
        [pltpu.VMEM((rows, width), LOW)] + ring_sems(ranks) + spread_sems(ranks) + spread_sems(ranks),
        (tokens[0], by_rank(attn_parts), by_rank(mlp_parts)),
    )
    at = ring_place(lax.axis_index("seq"), ranks)
    order = jnp.array(ring_order(ranks), jnp.int32)
    blocks = ring_seq(lax.rem(at + order, ranks), ranks)
    row_ids = (blocks[:, None] * local + jnp.arange(local, dtype=jnp.int32)[None, :]).reshape(-1)
    picked = (row_ids // span)[:, None] == jnp.arange(span_order.shape[0], dtype=jnp.int32)[None, :]
    pos = jnp.sum(jnp.where(picked, span_order[None, :], 0), -1) * span + row_ids % span
    begins = jnp.max(jnp.where(doc_starts <= pos[:, None], doc_starts, 0), -1)
    cosv, sinv = rotary(pos, size)
    cosv = jnp.concatenate([cosv[:, 0], cosv[:, 0]], -1)
    sinv = jnp.concatenate([-sinv[:, 0], sinv[:, 0]], -1)
    q_gain, k_gain = query_gain[None], key_gain[None]
    dy_all, q_low, k_low, v_low, prob, out_low, resid, second = call(
        functools.partial(attend_kernel, ranks, kv_heads),
        2,
        [VM] * 11,
        [
            ((rows, width), LOW, VM),
            ((heads, rows, size), LOW, VM),
            ((kv_heads, rows, size), LOW, VM),
            ((kv_heads, rows, size), LOW, VM),
            ((heads, rows, rows), LOW, VM),
            ((rows, q_cols), LOW, VM),
            ((local, width), f32, VM),
            ((local, width), LOW, VM),
        ],
        sum_bufs(local, ranks, width) + ring_sems(ranks) + ring_sems(ranks),
        (
            out_grad[0], tokens[0], qkv, attn_block, cosv, sinv, pos[:, None], begins[:, None], pos[None], q_gain,
            k_gain,
        ),
    )
    block_out, dresid, dresid_low, dgm, mlp_grads = call(
        functools.partial(mlp_kernel, ranks),
        3,
        [VM, VM, VM, VM, ANY],
        [
            ((local, width), LOW, VM),
            ((local, width), f32, VM),
            ((local, width), LOW, VM),
            ((1, width), f32, VM),
            ((ranks, deep, 3 * ff), LOW, VM),
        ],
        [
            pltpu.VMEM((rows, width), LOW),
            pltpu.VMEM((ranks, deep, 3 * ff), LOW),
            pltpu.VMEM((rows, ff), LOW),
            pltpu.VMEM((rows, 2 * ff), LOW),
        ]
        + sum_bufs(local, ranks, width)
        + sum_bufs(local, ranks, width)
        + [pltpu.SemaphoreType.DMA]
        + ring_sems(ranks) * 3,
        (second, resid, out_grad[0], dy_all, mlp_block),
    )
    tokens_grad, dga, dgq, dgk, attn_grads = call(
        functools.partial(back_kernel, ranks, kv_heads),
        4,
        [VM] * 15,
        [
            ((local, width), f32, VM),
            ((1, width), f32, VM),
            ((1, size), f32, VM),
            ((1, size), f32, VM),
            ((ranks, deep, a_cols), LOW, VM),
        ],
        [
            pltpu.VMEM((rows, width), LOW),
            pltpu.VMEM((rows, q_cols), LOW),
            pltpu.VMEM((kv_heads, rows, size), f32),
            pltpu.VMEM((kv_heads, rows, size), f32),
            pltpu.VMEM((rows, qkv_cols), LOW),
        ]
        + sum_bufs(local, ranks, width)
        + ring_sems(ranks) * 2,
        (
            tokens[0], dresid, dresid_low, first_in, attn_block, qkv, cosv, sinv, q_gain, k_gain, q_low, k_low,
            v_low, prob, out_low,
        ),
    )
    pieces = size // own
    small = jnp.concatenate(
        [
            dga.T,
            dgm.T,
            jnp.tile(dgq.reshape(-1, own).T, (ranks * copies, 1)),
            jnp.tile(dgk.reshape(-1, own).T, (ranks * copies, 1)),
        ],
        -1,
    )
    small = jnp.pad(small, ((0, 0), (0, size - small.shape[1]))).astype(LOW).reshape(ranks, deep, size)
    cuts = [[(0, ff), (ff, ff), (2 * ff, ff)], [(0, a_cols)], [(0, size)]]
    shapes = (3 * ff, a_cols, size)
    count = sum(len(cut) for cut in cuts)
    mlp_sums, attn_sums, gains = call(
        functools.partial(collect_kernel, ranks, own, cuts, len(cuts)),
        5,
        [VM] * len(cuts),
        [((ranks, own, cols), LOW, VM) for cols in shapes],
        sum([collect_bufs(ranks, own, cols) for cols in shapes], []) + collect_sems(ranks) * count,
        (mlp_grads, attn_grads, small),
    )
    gains = jnp.sum(gains.astype(f32), 0)

    def wide(part):
        return jnp.transpose(part, (1, 0, 2)).reshape(own, -1).astype(f32)

    return (
        block_out[None],
        tokens_grad[None],
        wide(attn_sums[..., :q_cols]) * gain_rows,
        wide(attn_sums[..., q_cols : q_cols + kv_cols]) * gain_rows,
        wide(attn_sums[..., q_cols + kv_cols : qkv_cols]) * gain_rows,
        wide(attn_sums[..., qkv_cols:]),
        gains[:, 0] / attn_gain,
        gains[:, 2 : 2 + pieces].T.reshape(-1),
        gains[:, 2 + pieces : 2 + 2 * pieces].T.reshape(-1),
        wide(mlp_sums[..., :ff]) * mlp_rows,
        wide(mlp_sums[..., ff : 2 * ff]) * mlp_rows,
        wide(mlp_sums[..., 2 * ff :]),
        gains[:, 1] / mlp_gain,
    )


def body(*args):
    tokens, w_key, query_gain = args[0], args[5], args[9]
    groups = w_key.shape[1] // query_gain.shape[0]
    ranks = lax.axis_size("seq")
    if tokens.shape[0] == 1 and ranks % 2 == 0 and groups % ranks == 0 and lax.axis_size("dp") == 4:
        return columns_body(*args)
    return gathered_body(*args)


def solution(mesh):
    return jax.shard_map(
        body,
        mesh=mesh,
        in_specs=(
            P("dp", "seq", None),
            P("dp", "seq", None),
            P(),
            P("dp", None),
            P(("seq", "dp"), None),
            P(("seq", "dp"), None),
            P(("seq", "dp"), None),
            P(("seq", "dp"), None),
            P(("seq", "dp")),
            P(),
            P(),
            P(("seq", "dp"), None),
            P(("seq", "dp"), None),
            P(("seq", "dp"), None),
            P(("seq", "dp")),
        ),
        out_specs=(
            P("dp", "seq", None),
            P("dp", "seq", None),
            P(("seq", "dp"), None),
            P(("seq", "dp"), None),
            P(("seq", "dp"), None),
            P(("seq", "dp"), None),
            P(("seq", "dp")),
            P(),
            P(),
            P(("seq", "dp"), None),
            P(("seq", "dp"), None),
            P(("seq", "dp"), None),
            P(("seq", "dp")),
        ),
        check_vma=False,
    )
```

```python
import functools
import math

import jax
import jax.numpy as jnp
from jax import lax
from jax.experimental import pallas as pl
from jax.experimental.pallas import tpu as pltpu
from jax.sharding import PartitionSpec as P

EPS = 1e-06
NEG = -1e30


def normed(v, gain):
    scale_inv = lax.rsqrt(jnp.mean(v * v, -1, keepdims=True) + EPS)
    return (v * scale_inv * gain, scale_inv)


def norm_back(v, scale_inv, gain, grad):
    scaled = grad * gain
    inner = jnp.mean(scaled * v, -1, keepdims=True)
    dv = scale_inv * scaled - v * scale_inv * scale_inv * scale_inv * inner
    dgain = jnp.sum((grad * v * scale_inv).reshape(-1, v.shape[-1]), 0)
    return (dv, dgain)


def rotary(pos, width):
    half = width // 2
    freqs = jnp.exp(jnp.arange(half, dtype=jnp.float32) * (-2.0 / width * math.log(1000000.0)))
    angle = pos.astype(jnp.float32)[:, None] * freqs[None, :]
    return (jnp.cos(angle)[:, None, :], jnp.sin(angle)[:, None, :])


def rotate(v, cosv, sinv):
    half = v.shape[-1] // 2
    first, second = (v[..., :half], v[..., half:])
    return jnp.concatenate([first * cosv - second * sinv, second * cosv + first * sinv], -1)


def rotate_back(grad, cosv, sinv):
    half = grad.shape[-1] // 2
    first, second = (grad[..., :half], grad[..., half:])
    return jnp.concatenate([first * cosv + second * sinv, second * cosv - first * sinv], -1)


def place(order, begin, count, span):
    rows = begin + jnp.arange(count, dtype=jnp.int32)
    slots = rows // span
    picked = slots[:, None] == jnp.arange(order.shape[0], dtype=jnp.int32)[None, :]
    return jnp.sum(jnp.where(picked, order[None, :], 0), -1) * span + rows % span


def doc_of(starts, pos):
    return jnp.sum((starts[:, None, :] <= pos[None, :, None]).astype(jnp.int32), -1)


def gathered_body(
    tokens,
    out_grad,
    span_order,
    doc_starts,
    w_query,
    w_key,
    w_value,
    w_output,
    attn_gain,
    query_gain,
    key_gain,
    w_gate,
    w_up,
    w_down,
    mlp_gain,
):
    seqs, local, width = tokens.shape
    span = local // 2
    head_size = query_gain.shape[0]
    kv_heads = w_key.shape[1] // head_size
    heads = w_query.shape[1] // head_size
    share = heads // kv_heads
    kv_width = kv_heads * head_size
    ff_width = w_gate.shape[1]
    scale = 1.0 / math.sqrt(head_size)
    total_rows = seqs * local
    own_rows = width // lax.axis_size(("seq", "dp"))
    qpos = place(span_order, lax.axis_index("seq") * local, local, span)
    qdoc = doc_of(doc_starts, qpos)
    cosv, sinv = rotary(qpos, head_size)

    def gather_attn():
        return (
            lax.all_gather(w_query, ("seq", "dp"), axis=0, tiled=True),
            lax.all_gather(w_key, ("seq", "dp"), axis=0, tiled=True),
            lax.all_gather(w_value, ("seq", "dp"), axis=0, tiled=True),
            lax.all_gather(w_output, ("seq", "dp"), axis=0, tiled=True),
            lax.all_gather(
                attn_gain.astype(jnp.bfloat16), ("seq", "dp"), axis=0, tiled=True
            ).astype(attn_gain.dtype),
        )

    def gather_mlp():
        return (
            lax.all_gather(w_gate, ("seq", "dp"), axis=0, tiled=True),
            lax.all_gather(w_up, ("seq", "dp"), axis=0, tiled=True),
            lax.all_gather(w_down, ("seq", "dp"), axis=0, tiled=True),
            lax.all_gather(mlp_gain.astype(jnp.bfloat16), ("seq", "dp"), axis=0, tiled=True).astype(
                mlp_gain.dtype
            ),
        )

    x_rows = tokens.astype(jnp.float32).reshape(total_rows, width)
    wq_all, wk_all, wv_all, wo_all, ga_all = gather_attn()
    first_norm, first_inv = normed(x_rows, ga_all)
    first_in = first_norm.astype(jnp.bfloat16)
    q_raw = jnp.dot(first_in, wq_all, preferred_element_type=jnp.float32).reshape(
        seqs, local, heads, head_size
    )
    k_raw = jnp.dot(first_in, wk_all, preferred_element_type=jnp.float32).reshape(
        seqs, local, kv_heads, head_size
    )
    v_low = (
        jnp.dot(first_in, wv_all, preferred_element_type=jnp.float32)
        .astype(jnp.bfloat16)
        .reshape(seqs, local, kv_heads, head_size)
    )
    q_normed, q_inv = normed(q_raw, query_gain)
    k_normed, k_inv = normed(k_raw, key_gain)
    q_low = rotate(q_normed, cosv, sinv).astype(jnp.bfloat16)
    k_low = rotate(k_normed, cosv, sinv).astype(jnp.bfloat16)
    q_group = q_low.reshape(seqs, local, kv_heads, share, head_size)

    def scores(piece_key, start):
        count = piece_key.shape[1]
        kpos = place(span_order, start, count, span)
        kdoc = doc_of(doc_starts, kpos)
        visible = (qdoc[:, :, None] == kdoc[:, None, :]) & (
            kpos[None, None, :] <= qpos[None, :, None]
        )
        raw = (
            jnp.einsum("sqgjd,skgd->sgjqk", q_group, piece_key, preferred_element_type=jnp.float32)
            * scale
        )
        return (raw, visible[:, None, None])

    start_top = jnp.full((seqs, kv_heads, share, local), NEG, jnp.float32)
    piece = (
        lax.all_gather(k_low, "seq", axis=1, tiled=True),
        lax.all_gather(v_low, "seq", axis=1, tiled=True),
    )
    top = start_top
    raw, visible = scores(piece[0], jnp.int32(0))
    raw = jnp.where(visible, raw, NEG)
    new_top = jnp.maximum(top, jnp.max(raw, -1))
    weights = jnp.where(visible, jnp.exp(raw - new_top[..., None]), 0.0)
    total = jnp.sum(weights, -1)
    summed = jnp.einsum(
        "sgjqk,skgd->sgjqd",
        weights.astype(jnp.bfloat16),
        piece[1],
        preferred_element_type=jnp.float32,
    )
    top, total, summed = (new_top, total, summed)
    log_total = top + jnp.log(total)
    attn_vals = summed / total[..., None]
    out_low = (
        jnp.transpose(attn_vals, (0, 3, 1, 2, 4))
        .reshape(total_rows, heads * head_size)
        .astype(jnp.bfloat16)
    )
    resid = x_rows + jnp.einsum("nh,dh->nd", out_low, wo_all, preferred_element_type=jnp.float32)
    wg_all, wu_all, wd_all, gm_all = gather_mlp()
    second_norm, second_inv = normed(resid, gm_all)
    second_in = second_norm.astype(jnp.bfloat16)
    gate = jnp.dot(second_in, wg_all, preferred_element_type=jnp.float32)
    upper = jnp.dot(second_in, wu_all, preferred_element_type=jnp.float32)
    sigma = jax.nn.sigmoid(gate)
    act = gate * sigma
    hidden = (act * upper).astype(jnp.bfloat16)
    result = resid + jnp.einsum("nf,df->nd", hidden, wd_all, preferred_element_type=jnp.float32)
    block_out = result.astype(jnp.bfloat16).reshape(seqs, local, width)
    grad_low = out_grad.reshape(total_rows, width)
    wg_all, wu_all, wd_all, gm_all = gather_mlp()
    dmid = jnp.einsum("nd,df->nf", grad_low, wd_all, preferred_element_type=jnp.float32)
    dgate = (dmid * upper * sigma * (1.0 + gate * (1.0 - sigma))).astype(jnp.bfloat16)
    dupper = (dmid * act).astype(jnp.bfloat16)
    left = second_in
    outer = grad_low
    mlp_sums = lax.psum_scatter(
        jnp.concatenate(
            [
                jnp.einsum("nd,nf->df", left, dgate, preferred_element_type=jnp.float32),
                jnp.einsum("nd,nf->df", left, dupper, preferred_element_type=jnp.float32),
                jnp.einsum("nd,nf->df", outer, hidden, preferred_element_type=jnp.float32),
            ],
            1,
        ),
        ("seq", "dp"),
        scatter_dimension=0,
        tiled=True,
    )
    dsecond = jnp.einsum(
        "nf,df->nd", dgate, wg_all, preferred_element_type=jnp.float32
    ) + jnp.einsum("nf,df->nd", dupper, wu_all, preferred_element_type=jnp.float32)
    dresid_norm, dgm = norm_back(resid, second_inv, gm_all, dsecond)
    dresid = grad_low.astype(jnp.float32) + dresid_norm
    dresid_low = dresid.astype(jnp.bfloat16)
    wq_all, wk_all, wv_all, wo_all, ga_all = gather_attn()
    dout_low = jnp.einsum(
        "nd,dh->nh", dresid_low, wo_all, preferred_element_type=jnp.float32
    ).astype(jnp.bfloat16)
    dout_group = dout_low.reshape(seqs, local, kv_heads, share, head_size)
    delta = jnp.sum(jnp.transpose(dout_group.astype(jnp.float32), (0, 2, 3, 1, 4)) * attn_vals, -1)
    piece = (
        lax.all_gather(k_low, "seq", axis=1, tiled=True),
        lax.all_gather(v_low, "seq", axis=1, tiled=True),
    )
    count = piece[0].shape[1]
    raw, visible = scores(piece[0], jnp.int32(0))
    prob = jnp.where(visible, jnp.exp(raw - log_total[..., None]), 0.0)
    dprob = jnp.einsum(
        "sqgjd,skgd->sgjqk", dout_group, piece[1], preferred_element_type=jnp.float32
    )
    dscore = (prob * (dprob - delta[..., None])).astype(jnp.bfloat16)
    dq_sum = jnp.einsum("sgjqk,skgd->sqgjd", dscore, piece[0], preferred_element_type=jnp.float32)
    dk_part = (
        jnp.einsum("sgjqk,sqgjd->skgd", dscore, q_group, preferred_element_type=jnp.float32) * scale
    )
    dv_part = jnp.einsum(
        "sgjqk,sqgjd->skgd",
        prob.astype(jnp.bfloat16),
        dout_group,
        preferred_element_type=jnp.float32,
    )
    joined = jnp.concatenate(
        [dk_part.reshape(seqs, count, kv_width), dv_part.reshape(seqs, count, kv_width)], -1
    )
    buffer = joined
    dq_sum, buffer = (dq_sum, buffer)
    key_sums = lax.psum_scatter(
        buffer.astype(jnp.bfloat16), "seq", scatter_dimension=1, tiled=True
    ).astype(jnp.float32)
    dq_rot = (dq_sum * scale).reshape(seqs, local, heads, head_size)
    dq_raw, dgq = norm_back(q_raw, q_inv, query_gain, rotate_back(dq_rot, cosv, sinv))
    dk_rot = key_sums[..., :kv_width].reshape(seqs, local, kv_heads, head_size)
    dk_raw, dgk = norm_back(k_raw, k_inv, key_gain, rotate_back(dk_rot, cosv, sinv))
    dq_low = dq_raw.reshape(total_rows, heads * head_size).astype(jnp.bfloat16)
    dk_low = dk_raw.reshape(total_rows, kv_width).astype(jnp.bfloat16)
    dv_low = key_sums[..., kv_width:].reshape(total_rows, kv_width).astype(jnp.bfloat16)
    left = first_in
    outer = dresid_low
    attn_sums = lax.psum_scatter(
        jnp.concatenate(
            [
                jnp.einsum("nd,nh->dh", left, dq_low, preferred_element_type=jnp.float32),
                jnp.einsum("nd,nh->dh", left, dk_low, preferred_element_type=jnp.float32),
                jnp.einsum("nd,nh->dh", left, dv_low, preferred_element_type=jnp.float32),
                jnp.einsum("nd,nh->dh", outer, out_low, preferred_element_type=jnp.float32),
            ],
            1,
        ),
        ("seq", "dp"),
        scatter_dimension=0,
        tiled=True,
    )
    dfirst = jnp.einsum("nh,dh->nd", dq_low, wq_all, preferred_element_type=jnp.float32)
    dfirst = dfirst + jnp.einsum("nh,dh->nd", dk_low, wk_all, preferred_element_type=jnp.float32)
    dfirst = dfirst + jnp.einsum("nh,dh->nd", dv_low, wv_all, preferred_element_type=jnp.float32)
    dx_norm, dga = norm_back(x_rows, first_inv, ga_all, dfirst)
    tokens_grad = (dresid + dx_norm).reshape(seqs, local, width)
    dga_all, dgm_all, dgq_all, dgk_all = lax.psum((dga, dgm, dgq, dgk), ("seq", "dp"))
    offset = lax.axis_index(("seq", "dp")) * own_rows
    attn_gain_grad = lax.dynamic_slice_in_dim(dga_all, offset, own_rows, 0)
    mlp_gain_grad = lax.dynamic_slice_in_dim(dgm_all, offset, own_rows, 0)
    q_cols = heads * head_size
    w_query_grad = attn_sums[:, :q_cols]
    w_key_grad = attn_sums[:, q_cols : q_cols + kv_width]
    w_value_grad = attn_sums[:, q_cols + kv_width : q_cols + 2 * kv_width]
    w_output_grad = attn_sums[:, q_cols + 2 * kv_width :]
    w_gate_grad = mlp_sums[:, :ff_width]
    w_up_grad = mlp_sums[:, ff_width : 2 * ff_width]
    w_down_grad = mlp_sums[:, 2 * ff_width :]
    return (
        block_out,
        tokens_grad,
        w_query_grad,
        w_key_grad,
        w_value_grad,
        w_output_grad,
        attn_gain_grad,
        dgq_all,
        dgk_all,
        w_gate_grad,
        w_up_grad,
        w_down_grad,
        mlp_gain_grad,
    )


LOW = jnp.bfloat16
MESH = pl.DeviceIdType.MESH
LIMIT = 60 * 2**20


def ring_order(ranks):
    half = ranks // 2
    order = [0]
    for step in range(1, half):
        order += [step, ranks - step]
    return order + [half]


def ring_place(seq, ranks):
    z, x = lax.div(seq, 2), lax.rem(seq, 2)
    return z + x * (ranks - 1 - 2 * z)


def ring_seq(place, ranks):
    half = ranks // 2
    x, z = lax.div(place, half), lax.rem(place, half)
    return 2 * (z + x * (half - 1 - 2 * z)) + x


def neighbours(ranks):
    seq, dp = lax.axis_index("seq"), lax.axis_index("dp")
    at = ring_place(seq, ranks)
    right = ring_seq(lax.rem(at + 1, ranks), ranks)
    left = ring_seq(lax.rem(at + ranks - 1, ranks), ranks)
    return (right, dp), (left, dp)


def greet(devices):
    barrier = pltpu.get_barrier_semaphore()
    for device in devices:
        pl.semaphore_signal(barrier, inc=1, device_id=device, device_id_type=MESH)
    pl.semaphore_wait(barrier, len(devices))


def push(src, dst, send, recv, device):
    return pltpu.make_async_remote_copy(
        src_ref=src, dst_ref=dst, send_sem=send, recv_sem=recv, device_id=device, device_id_type=MESH
    )


def dot_nn(left, right):
    return jnp.dot(left, right, preferred_element_type=jnp.float32)


def dot_nt(left, right):
    return lax.dot_general(left, right, (((1,), (1,)), ((), ())), preferred_element_type=jnp.float32)


def dot_tn(left, right):
    return lax.dot_general(left, right, (((0,), (0,)), ((), ())), preferred_element_type=jnp.float32)


class RingGather:
    def __init__(self, buf, local, ranks, send, recv, right, left):
        self.buf, self.local, self.half = buf, local, ranks // 2
        self.send, self.recv, self.right, self.left = send, recv, right, left
        self.row = {rel: at * local for at, rel in enumerate(ring_order(ranks))}
        self.ranks = ranks

    def copies(self, step):
        last = step == self.half
        rows = self.local // 2 if last else self.local
        skip = self.local // 2 if last else 0
        pairs = (
            ((self.ranks - step + 1) % self.ranks, self.ranks - step, 0, self.right),
            (step - 1, step, skip, self.left),
        )
        return [
            push(
                self.buf.at[pl.ds(self.row[src] + begin, rows)],
                self.buf.at[pl.ds(self.row[dst] + begin, rows)],
                self.send.at[way, step - 1],
                self.recv.at[way, step - 1],
                device,
            )
            for way, (src, dst, begin, device) in enumerate(pairs)
        ]

    def start(self, step):
        for copy in self.copies(step):
            copy.start()

    def arrive(self, step):
        for copy in self.copies(step):
            copy.wait_recv()

    def finish(self):
        for step in range(1, self.half + 1):
            for copy in self.copies(step):
                copy.wait_send()

    def rows(self, step):
        if step == 0:
            return 0, self.local
        if step == self.half:
            return self.row[self.half], self.local
        return self.row[step], 2 * self.local


class RingSum:
    def __init__(self, part, term, out_buf, in_buf, local, ranks, send, recv, right, left):
        self.part, self.term, self.out_buf, self.in_buf = part, term, out_buf, in_buf
        self.local, self.ranks, self.half = local, ranks, ranks // 2
        self.send, self.recv, self.right, self.left = send, recv, right, left
        self.row = {rel: at * local for at, rel in enumerate(ring_order(ranks))}

    def copies(self, step):
        rows = self.local // 2 if step == 1 else self.local
        skip = self.local // 2 if step == 1 else 0
        return [
            push(
                self.out_buf.at[way, (step - 1) % 2, pl.ds(begin, rows)],
                self.in_buf.at[way, step - 1, pl.ds(begin, rows)],
                self.send.at[way, step - 1],
                self.recv.at[way, step - 1],
                device,
            )
            for way, begin, device in ((0, 0, self.right), (1, skip, self.left))
        ]

    def compute(self, step):
        if step == 1:
            self.part(self.row[self.half], self.local)
        elif step <= self.half:
            self.part(self.row[self.half + 1 - step], 2 * self.local)
        else:
            self.part(0, self.local)

    def launch(self, step):
        local, skip = self.local, self.local // 2
        if step > 2:
            for copy in self.copies(step - 2):
                copy.wait_send()
        if step == 1:
            self.out_buf[0, 0, :skip] = self.term[:skip].astype(LOW)
            self.out_buf[1, 0, skip:] = self.term[skip:local].astype(LOW)
        else:
            for copy in self.copies(step - 1):
                copy.wait_recv()
            for way in range(2):
                for begin, with_sum in ((0, step > 2 or way == 0), (skip, step > 2 or way == 1)):
                    value = self.term[pl.ds(way * local + begin, skip)]
                    if with_sum:
                        value = value + self.in_buf[way, step - 2, pl.ds(begin, skip)].astype(jnp.float32)
                    self.out_buf[way, (step - 1) % 2, pl.ds(begin, skip)] = value.astype(LOW)
        for copy in self.copies(step):
            copy.start()

    def last(self, begin, count):
        rows = pl.ds(begin, count)
        value = self.term[rows] + self.in_buf[0, self.half - 1, rows].astype(jnp.float32)
        return value + self.in_buf[1, self.half - 1, rows].astype(jnp.float32)

    def arrive_last(self):
        for copy in self.copies(self.half):
            copy.wait_recv()

    def finish(self):
        for step in range(max(1, self.half - 1), self.half + 1):
            for copy in self.copies(step):
                copy.wait_send()


def ring_sems(ranks):
    return [pltpu.SemaphoreType.DMA((2, ranks // 2)), pltpu.SemaphoreType.DMA((2, ranks // 2))]


def sum_bufs(local, ranks, width):
    return [
        pltpu.VMEM((2 * local, width), jnp.float32),
        pltpu.VMEM((2, 2, local, width), LOW),
        pltpu.VMEM((2, ranks // 2, local, width), LOW),
    ]


def turn(v):
    return pltpu.roll(v, v.shape[-1] // 2, v.ndim - 1)


def rows_scaled(v):
    inv = lax.rsqrt(jnp.mean(v * v, -1, keepdims=True) + EPS)
    return v * inv, inv


def rows_scaled_back(v, inv, grad):
    return inv * grad - v * (inv * inv * inv * jnp.mean(grad * v, -1, keepdims=True))


class Spread:
    def __init__(self, rows, block, ranks, own, cols, sems):
        self.rows, self.block, self.ranks, self.own, self.cols = rows, block, ranks, own, cols
        self.send, self.recv, self.hop_send, self.hop_recv, self.here = sems
        self.seq, self.dp = lax.axis_index("seq"), lax.axis_index("dp")
        y, core = lax.div(self.dp, 2), lax.rem(self.dp, 2)
        self.beside, self.sibling = (1 - y) * 2 + core, y * 2 + 1 - core

    def at(self, dp):
        return pl.ds(pl.multiple_of(dp * self.own, self.own), self.own)

    def exchange(self):
        for step in range(1, self.ranks):
            peer = lax.rem(self.seq + step, self.ranks)
            yield push(
                self.rows.at[peer, :, self.cols],
                self.block.at[self.seq, self.at(self.dp), self.cols],
                self.send.at[step],
                self.recv.at[step],
                (peer, self.dp),
            )

    def keep(self):
        return pltpu.make_async_copy(
            self.rows.at[self.seq, :, self.cols],
            self.block.at[self.seq, self.at(self.dp), self.cols],
            self.here,
        )

    def hop(self, number):
        dp = self.beside if number == 2 else self.dp
        part = self.block.at[:, self.at(dp), self.cols]
        to = self.beside if number == 0 else self.sibling
        return push(part, part, self.hop_send.at[number], self.hop_recv.at[number], (self.seq, to))

    def start(self):
        self.keep().start()
        for copy in self.exchange():
            copy.start()

    def arrive(self):
        self.keep().wait()
        for copy in self.exchange():
            copy.wait_recv()

    def finish(self):
        for copy in self.exchange():
            copy.wait_send()
        for number in range(3):
            self.hop(number).wait_send()


def spread_sems(ranks):
    return [
        pltpu.SemaphoreType.DMA((ranks,)),
        pltpu.SemaphoreType.DMA((ranks,)),
        pltpu.SemaphoreType.DMA((3,)),
        pltpu.SemaphoreType.DMA((3,)),
        pltpu.SemaphoreType.DMA,
    ]


class Reduce:
    def __init__(self, grads, from_core, from_y, total, own, first, count, cols, sems):
        self.grads, self.from_core, self.from_y, self.total = grads, from_core, from_y, total
        self.own, self.begin, self.count, self.cols = own, first, count, cols
        self.send, self.recv = sems
        self.seq, dp = lax.axis_index("seq"), lax.axis_index("dp")
        self.y, self.core = lax.div(dp, 2), lax.rem(dp, 2)
        self.beside, self.sibling = (1 - self.y) * 2 + self.core, self.y * 2 + 1 - self.core

    def at(self, y, core):
        return pl.ds(pl.multiple_of((y * 2 + core) * self.own, self.own), self.own)

    def hop(self, number):
        some, cols = pl.ds(self.begin, self.count), self.cols
        if number == 2:
            src, dst, to = self.from_core.at[0, some, :, cols], self.from_y.at[some, :, cols], self.beside
        else:
            rows = self.at(1 - self.y if number == 0 else self.y, 1 - self.core)
            src, dst, to = self.grads.at[some, rows, cols], self.from_core.at[number, some, :, cols], self.sibling
        return push(src, dst, self.send.at[number], self.recv.at[number], (self.seq, to))

    def first(self):
        self.hop(0).start()
        self.hop(1).start()

    def second(self):
        self.hop(0).wait_recv()
        rows = self.at(1 - self.y, self.core)

        def some(at, _):
            value = self.grads[at, rows, self.cols].astype(jnp.float32)
            value = value + self.from_core[0, at, :, self.cols].astype(jnp.float32)
            self.from_core[0, at, :, self.cols] = value.astype(LOW)
            return 0

        lax.fori_loop(self.begin, self.begin + self.count, some, 0)
        self.hop(2).start()

    def third(self):
        self.hop(1).wait_recv()
        self.hop(2).wait_recv()
        rows = self.at(self.y, self.core)

        def some(at, _):
            value = self.grads[at, rows, self.cols].astype(jnp.float32)
            value = value + self.from_core[1, at, :, self.cols].astype(jnp.float32)
            value = value + self.from_y[at, :, self.cols].astype(jnp.float32)
            self.total[at, :, self.cols] = value.astype(LOW)
            return 0

        lax.fori_loop(self.begin, self.begin + self.count, some, 0)

    def finish(self):
        for number in range(3):
            self.hop(number).wait_send()


def reduce_sems():
    return [pltpu.SemaphoreType.DMA((3,)), pltpu.SemaphoreType.DMA((3,))]


def reduce_bufs(ranks, own, cols):
    return [pltpu.VMEM((2, ranks, own, cols), LOW), pltpu.VMEM((ranks, own, cols), LOW)]


class Deliver:
    def __init__(self, rows, out, cols, ranks, sems):
        self.rows, self.out, self.cols, self.ranks = rows, out, cols, ranks
        self.send, self.recv, self.here = sems
        self.seq, self.dp = lax.axis_index("seq"), lax.axis_index("dp")

    def exchange(self):
        for step in range(1, self.ranks):
            peer = lax.rem(self.seq + step, self.ranks)
            yield push(
                self.rows.at[peer, :, self.cols],
                self.out.at[self.seq, :, self.cols],
                self.send.at[step],
                self.recv.at[step],
                (peer, self.dp),
            )

    def keep(self):
        return pltpu.make_async_copy(
            self.rows.at[self.seq, :, self.cols], self.out.at[self.seq, :, self.cols], self.here
        )

    def start(self):
        self.keep().start()
        for copy in self.exchange():
            copy.start()

    def finish(self):
        self.keep().wait()
        for copy in self.exchange():
            copy.wait_recv()
        for copy in self.exchange():
            copy.wait_send()


def deliver_sems(ranks):
    return [pltpu.SemaphoreType.DMA((ranks,)), pltpu.SemaphoreType.DMA((ranks,)), pltpu.SemaphoreType.DMA]


def enter_kernel(ranks, tokens, attn_rows, first_in, qkv, attn_block, held, *sems):
    local, width = tokens.shape
    own = attn_rows.shape[1]
    cols = qkv.shape[1]
    seq, dp = lax.axis_index("seq"), lax.axis_index("dp")
    right, left = neighbours(ranks)
    attn = Spread(attn_rows, attn_block, ranks, own, pl.ds(0, attn_rows.shape[2]), sems[2:7])
    peers = [(lax.rem(seq + step, ranks), dp) for step in range(1, ranks)]
    greet(peers + [(seq, attn.beside), (seq, attn.sibling)])
    ring = RingGather(held, local, ranks, sems[0], sems[1], right, left)
    attn.start()
    held[:local] = tokens[...]
    ring.start(1)

    def scale_rows(begin, count):
        def some(at, _):
            rows = pl.ds(pl.multiple_of(begin + at * 32, 32), 32)
            first_in[rows] = rows_scaled(held[rows].astype(jnp.float32))[0].astype(LOW)
            return 0

        lax.fori_loop(0, count // 32, some, 0)

    def project(begin, count):
        rows = pl.ds(begin, count)
        weight = attn_block[:, :, :cols].reshape(width, cols)
        qkv[rows] = dot_nn(first_in[rows], weight)

    scale_rows(*ring.rows(0))
    attn.arrive()
    attn.hop(0).start()
    ring.arrive(1)
    ring.start(2)
    scale_rows(*ring.rows(1))
    attn.hop(0).wait_recv()
    attn.hop(1).start()
    attn.hop(2).start()
    ring.arrive(2)
    ring.start(3)
    scale_rows(*ring.rows(2))
    attn.hop(1).wait_recv()
    attn.hop(2).wait_recv()
    for step in range(3):
        project(*ring.rows(step))
    for step in range(3, ranks // 2 + 1):
        ring.arrive(step)
        if step < ranks // 2:
            ring.start(step + 1)
        scale_rows(*ring.rows(step))
        project(*ring.rows(step))
    ring.finish()
    attn.finish()


def attend_kernel(
    ranks, kv_heads, out_grad, tokens, qkv, attn_block, cosv, sinv, pos, begins, pos_row, query_gain, key_gain,
    mlp_rows, dy_all, q_low, k_low, v_low, prob, out_low, resid, second, mlp_block, term, out_buf, in_buf, *sems,
):
    local, width = tokens.shape
    rows = local * ranks
    size = cosv.shape[1]
    heads = q_low.shape[0]
    share = heads // kv_heads
    scale = 1.0 / math.sqrt(size)
    right, left = neighbours(ranks)
    seq, dp = lax.axis_index("seq"), lax.axis_index("dp")
    own = mlp_rows.shape[1]
    third = mlp_rows.shape[2] // 3
    mlp = [
        Spread(mlp_rows, mlp_block, ranks, own, pl.ds(at * third, third), sems[4 + 5 * at : 9 + 5 * at])
        for at in range(3)
    ]
    peers = [(lax.rem(seq + step, ranks), dp) for step in range(1, ranks)]
    greet(peers + [(seq, mlp[0].beside), (seq, mlp[0].sibling)])
    ring = RingGather(dy_all, local, ranks, sems[0], sems[1], right, left)
    dy_all[:local] = out_grad[...]
    ring.start(1)
    for piece in mlp:
        piece.start()
    tile = rows // (ranks // 2)

    def rotated(at, rows_at, gain):
        v = rows_scaled(qkv[rows_at, at * size : (at + 1) * size])[0] * gain[...]
        return (v * cosv[rows_at] + turn(v) * sinv[rows_at]).astype(LOW)

    for piece in range(ranks // 2):
        rows_at = pl.ds(piece * tile, tile)
        for head in range(heads):
            q_low[head, rows_at] = rotated(head, rows_at, query_gain)
        for group in range(kv_heads):
            k_low[group, rows_at] = rotated(heads + group, rows_at, key_gain)
            at = (heads + kv_heads + group) * size
            v_low[group, rows_at] = qkv[rows_at, at : at + size].astype(LOW)
    for piece in range(ranks // 2):
        if piece > 0:
            ring.arrive(piece)
            ring.start(piece + 1)
        rows_at = pl.ds(piece * tile, tile)
        seen = (pos_row[...] <= pos[rows_at]) & (pos_row[...] >= begins[rows_at])
        for head in range(heads):
            raw = dot_nt(q_low[head, rows_at], k_low[head // share]) * scale
            raw = jnp.where(seen, raw, NEG)
            weight = jnp.exp(raw - jnp.max(raw, -1, keepdims=True))
            weight = (weight * (1.0 / jnp.sum(weight, -1, keepdims=True))).astype(LOW)
            prob[head, rows_at] = weight
            value = dot_nn(weight, v_low[head // share])
            out_low[rows_at, head * size : (head + 1) * size] = value.astype(LOW)
        if piece > 0:
            mlp[piece - 1].arrive()
            mlp[piece - 1].hop(0).start()
            mlp[piece - 1].hop(1).start()
    first_col = (heads + 2 * kv_heads) * size
    deep = attn_block.shape[1]

    def part(begin, count):
        def some(at, _):
            value = dot_nt(out_low[pl.ds(begin, count)], attn_block[at, :, first_col:])
            term[:count, pl.ds(pl.multiple_of(at * deep, deep), deep)] = value
            return 0

        lax.fori_loop(0, ranks, some, 0)

    total = RingSum(part, term, out_buf, in_buf, local, ranks, sems[2], sems[3], right, left)
    for step in range(1, ranks // 2 + 1):
        total.compute(step)
        total.launch(step)
        if 1 < step < 5:
            mlp[step - 2].hop(0).wait_recv()
            mlp[step - 2].hop(2).start()
    total.compute(ranks // 2 + 1)
    ring.arrive(ranks // 2)
    total.arrive_last()

    def some(at, _):
        begin = pl.multiple_of(at * 32, 32)
        rows_at = pl.ds(begin, 32)
        value = tokens[rows_at].astype(jnp.float32) + total.last(begin, 32)
        resid[rows_at] = value
        second[rows_at] = rows_scaled(value)[0].astype(LOW)
        return 0

    lax.fori_loop(0, local // 32, some, 0)
    ring.finish()
    total.finish()
    for piece in mlp:
        piece.hop(1).wait_recv()
        piece.hop(2).wait_recv()
        piece.finish()


def mlp_kernel(
    ranks, second, resid, out_grad, dy_all, mlp_block, block_out, dresid, dresid_low, gain_grad, own_grads,
    grads, from_core, from_y, held, weights, hidden, dgu, term, out_buf, in_buf, y_out, y_in, here, *sems,
):
    local, width = second.shape
    ff = hidden.shape[1]
    deep = weights.shape[1]
    half = ranks // 2
    right, left = neighbours(ranks)
    load = pltpu.make_async_copy(mlp_block, weights, here)
    load.start()
    seq, dp = lax.axis_index("seq"), lax.axis_index("dp")
    own = own_grads.shape[1]
    pieces = [
        Reduce(
            grads, from_core, from_y, own_grads, own, at * ranks // 4, ranks // 4, pl.ds(0, 3 * ff),
            sems[6 + 2 * at : 8 + 2 * at],
        )
        for at in range(4)
    ]
    greet([right, left, (seq, pieces[0].beside), (seq, pieces[0].sibling)])
    ring = RingGather(held, local, ranks, sems[0], sems[1], right, left)
    held[:local] = second[...]
    ring.start(1)
    load.wait()
    wide = 256

    def middle(begin, count):
        rows = pl.ds(begin, count)

        def some(at, _):
            first = pl.multiple_of(at * wide, wide)
            gate = dot_nn(held[rows], weights[:, :, pl.ds(first, wide)].reshape(width, wide))
            upper = dot_nn(held[rows], weights[:, :, pl.ds(ff + first, wide)].reshape(width, wide))
            dmid = dot_nn(dy_all[rows], weights[:, :, pl.ds(2 * ff + first, wide)].reshape(width, wide))
            sigma = 1.0 / (1.0 + jnp.exp(-gate))
            act = gate * sigma
            hidden[rows, pl.ds(first, wide)] = (act * upper).astype(LOW)
            slope = sigma * (1.0 + gate * (1.0 - sigma))
            dgu[rows, pl.ds(first, wide)] = (dmid * upper * slope).astype(LOW)
            dgu[rows, pl.ds(ff + first, wide)] = (dmid * act).astype(LOW)
            return 0

        lax.fori_loop(0, ff // wide, some, 0)

    middle(*ring.rows(0))
    for step in range(1, half + 1):
        ring.arrive(step)
        if step < half:
            ring.start(step + 1)
        middle(*ring.rows(step))

    def back_part(begin, count):
        def some(at, _):
            value = dot_nt(dgu[pl.ds(begin, count)], weights[at, :, : 2 * ff])
            term[:count, pl.ds(pl.multiple_of(at * deep, deep), deep)] = value
            return 0

        lax.fori_loop(0, ranks, some, 0)

    def out_part(begin, count):
        def some(at, _):
            value = dot_nt(hidden[pl.ds(begin, count)], weights[at, :, 2 * ff :])
            term[:count, pl.ds(pl.multiple_of(at * deep, deep), deep)] = value
            return 0

        lax.fori_loop(0, ranks, some, 0)

    def weight_grads(first, count):
        def some(at, _):
            cols = pl.ds(pl.multiple_of(at * deep, deep), deep)
            grads[at, :, : 2 * ff] = dot_tn(held[:, cols], dgu[...]).astype(LOW)
            grads[at, :, 2 * ff :] = dot_tn(dy_all[:, cols], hidden[...]).astype(LOW)
            return 0

        lax.fori_loop(first, first + count, some, 0)

    back = RingSum(back_part, term, out_buf, in_buf, local, ranks, sems[2], sems[3], right, left)
    out = RingSum(out_part, term, y_out, y_in, local, ranks, sems[4], sems[5], right, left)
    for step in range(1, half + 1):
        back.compute(step)
        back.launch(step)
        out.compute(step)
        out.launch(step)
        if step < 3:
            for piece in pieces[2 * step - 2 : 2 * step]:
                weight_grads(piece.begin, piece.count)
                piece.first()
        if 1 < step < 4:
            for piece in pieces[2 * step - 4 : 2 * step - 2]:
                piece.second()
        if step > 2:
            for piece in pieces[2 * step - 6 : 2 * step - 4]:
                piece.third()
    back.compute(half + 1)
    back.arrive_last()
    gain_grad[...] = jnp.zeros_like(gain_grad)

    def finish_back(at, _):
        begin = pl.multiple_of(at * 32, 32)
        rows = pl.ds(begin, 32)
        value = resid[rows]
        normal, inv = rows_scaled(value)
        grad = back.last(begin, 32)
        full = out_grad[rows].astype(jnp.float32) + rows_scaled_back(value, inv, grad)
        dresid[rows] = full
        dresid_low[rows] = full.astype(LOW)
        gain_grad[...] += jnp.sum(grad * normal, 0, keepdims=True)
        return 0

    lax.fori_loop(0, local // 32, finish_back, 0)
    out.compute(half + 1)
    out.arrive_last()

    def finish_out(at, _):
        begin = pl.multiple_of(at * 32, 32)
        rows = pl.ds(begin, 32)
        block_out[rows] = (resid[rows] + out.last(begin, 32)).astype(LOW)
        return 0

    lax.fori_loop(0, local // 32, finish_out, 0)
    ring.finish()
    back.finish()
    out.finish()
    for piece in pieces:
        piece.finish()


def back_kernel(
    ranks, kv_heads, tokens, dresid, dresid_low, first_in, attn_block, qkv, cosv, sinv, query_gain, key_gain,
    q_low, k_low, v_low, prob, out_low, mlp_gain_part, mlp_own,
    tokens_grad, gains, mlp_sums, attn_sums,
    grads, from_core, from_y, own_grads, gain_grad, query_gain_grad, key_gain_grad,
    tiles, tiles_in, tile_sums, tile_sums_in, held, dout, dk, dv, dqkv, term, out_buf, in_buf, *sems,
):
    local, width = tokens.shape
    rows = local * ranks
    half = ranks // 2
    size = cosv.shape[1]
    heads = q_low.shape[0]
    share = heads // kv_heads
    scale = 1.0 / math.sqrt(size)
    cols = (heads + 2 * kv_heads) * size
    deep = attn_block.shape[1]
    o_cols = heads * size
    right, left = neighbours(ranks)
    seq, dp = lax.axis_index("seq"), lax.axis_index("dp")
    own = mlp_own.shape[1]
    copies = tiles.shape[1]
    all_cols = grads.shape[2]
    out_piece = Reduce(
        grads, from_core, from_y, own_grads, own, 0, ranks, pl.ds(cols, all_cols - cols), sems[4:6]
    )
    qkv_piece = Reduce(grads, from_core, from_y, own_grads, own, 0, ranks, pl.ds(0, cols), sems[6:8])
    mlp_way = Deliver(mlp_own, mlp_sums, pl.ds(0, mlp_own.shape[2]), ranks, sems[8:11])
    out_way = Deliver(own_grads, attn_sums, pl.ds(cols, all_cols - cols), ranks, sems[11:14])
    qkv_way = Deliver(own_grads, attn_sums, pl.ds(0, cols), ranks, sems[14:17])
    peers = [(lax.rem(seq + step, ranks), dp) for step in range(1, ranks)]
    greet(peers + [(seq, lax.rem(dp + step, copies)) for step in range(1, copies)])
    ring = RingGather(held, local, ranks, sems[0], sems[1], right, left)
    held[:local] = dresid_low[...]
    ring.start(1)

    def project(begin, count):
        at = pl.ds(begin, count)
        dout[at] = dot_nn(held[at], attn_block[:, :, cols:].reshape(width, o_cols)).astype(LOW)

    project(*ring.rows(0))
    for step in range(1, half + 1):
        ring.arrive(step)
        if step < half:
            ring.start(step + 1)
        project(*ring.rows(step))
    mlp_way.start()

    def out_grads(at, _):
        some_cols = pl.ds(pl.multiple_of(at * deep, deep), deep)
        grads[at, :, cols:] = dot_tn(held[:, some_cols], out_low[...]).astype(LOW)
        return 0

    lax.fori_loop(0, ranks, out_grads, 0)
    out_piece.first()
    tile = rows // half
    query_gain_grad[...] = jnp.zeros_like(query_gain_grad)
    key_gain_grad[...] = jnp.zeros_like(key_gain_grad)

    def unrotated(grad, column, rows_at, gain, gain_grad_ref):
        grad = grad * cosv[rows_at] - turn(grad) * sinv[rows_at]
        value = qkv[rows_at, column * size : (column + 1) * size]
        normal, inv = rows_scaled(value)
        gain_grad_ref[...] += jnp.sum(grad * normal, 0, keepdims=True)
        back = rows_scaled_back(value, inv, grad * gain[...])
        dqkv[rows_at, column * size : (column + 1) * size] = back.astype(LOW)

    for head in range(heads):
        group = head // share

        def one(piece, _):
            rows_at = pl.ds(pl.multiple_of(piece * tile, tile), tile)
            weight = prob[head, rows_at]
            grad = dout[rows_at, head * size : (head + 1) * size]
            dprob = dot_nt(grad, v_low[group])
            full = weight.astype(jnp.float32)
            delta = jnp.sum(full * dprob, -1, keepdims=True)
            dscore = (full * (dprob - delta)).astype(LOW)
            dq = dot_nn(dscore, k_low[group]) * scale
            dk_add = dot_tn(dscore, q_low[head, rows_at]) * scale
            dv_add = dot_tn(weight, grad)
            dk[group] += dk_add
            dv[group] += dv_add
            unrotated(dq, head, rows_at, query_gain, query_gain_grad)
            return 0

        if head % share == 0:
            dk[group] = jnp.zeros_like(dk[group])
            dv[group] = jnp.zeros_like(dv[group])
        lax.fori_loop(0, half, one, 0)
        if head == 0:
            out_piece.second()
    for group in range(kv_heads):
        def one_key(piece, _):
            rows_at = pl.ds(pl.multiple_of(piece * tile, tile), tile)
            unrotated(dk[group, rows_at], heads + group, rows_at, key_gain, key_gain_grad)
            at = (heads + kv_heads + group) * size
            dqkv[rows_at, at : at + size] = dv[group, rows_at].astype(LOW)
            return 0

        lax.fori_loop(0, half, one_key, 0)

    def part(begin, count):
        def some(at, _):
            value = dot_nt(dqkv[pl.ds(begin, count)], attn_block[at, :, :cols])
            term[:count, pl.ds(pl.multiple_of(at * deep, deep), deep)] = value
            return 0

        lax.fori_loop(0, ranks, some, 0)

    def qkv_grads(at, _):
        some_cols = pl.ds(pl.multiple_of(at * deep, deep), deep)
        grads[at, :, :cols] = dot_tn(first_in[:, some_cols], dqkv[...]).astype(LOW)
        return 0

    total = RingSum(part, term, out_buf, in_buf, local, ranks, sems[2], sems[3], right, left)
    for step in range(1, half + 1):
        total.compute(step)
        total.launch(step)
        if step == 1:
            lax.fori_loop(0, ranks, qkv_grads, 0)
            qkv_piece.first()
            out_piece.third()
            out_way.start()
        if step == 2:
            qkv_piece.second()
        if step == half:
            qkv_piece.third()
            qkv_way.start()
    total.compute(half + 1)
    total.arrive_last()
    gain_grad[...] = jnp.zeros_like(gain_grad)

    def last(at, _):
        begin = pl.multiple_of(at * 32, 32)
        rows_at = pl.ds(begin, 32)
        value = tokens[rows_at].astype(jnp.float32)
        normal, inv = rows_scaled(value)
        grad = total.last(begin, 32)
        tokens_grad[rows_at] = dresid[rows_at] + rows_scaled_back(value, inv, grad)
        gain_grad[...] += jnp.sum(grad * normal, 0, keepdims=True)
        return 0

    lax.fori_loop(0, local // 32, last, 0)
    lane = lax.broadcasted_iota(jnp.int32, (1, size), 1)
    per_row = size // own
    for number in range(ranks * copies):
        at = number // per_row
        first = gain_grad[:, at * size : (at + 1) * size]
        second = mlp_gain_part[:, at * size : (at + 1) * size]
        shift = number % per_row * own
        first = pltpu.roll(first, (size - shift) % size, 1) if shift else first
        second = pltpu.roll(second, (size + own - shift) % size, 1) if shift != own else second
        tile_at = tiles.at[number // copies, number % copies]
        tile_at[0:1] = jnp.where(lane < own, first, second)
        tile_at[1:2] = query_gain_grad[...]
        tile_at[2:3] = key_gain_grad[...]
        tile_at[3:] = jnp.zeros((tiles.shape[2] - 3, size), jnp.float32)

    def to_ranks(step):
        peer = lax.rem(seq + step, ranks)
        return push(tiles.at[peer], tiles_in.at[seq], sems[17].at[step], sems[18].at[step], (peer, dp))

    def to_copies(step):
        peer = lax.rem(dp + step, copies)
        return push(
            tile_sums.at[peer], tile_sums_in.at[dp], sems[19].at[step], sems[20].at[step], (seq, peer)
        )

    for step in range(1, ranks):
        to_ranks(step).start()
    tiles_in[seq] = tiles[seq]
    for step in range(1, ranks):
        to_ranks(step).wait_recv()
    tile_sums[...] = jnp.sum(tiles_in[...], 0)
    for step in range(1, copies):
        to_copies(step).start()
    tile_sums_in[dp] = tile_sums[dp]
    for step in range(1, copies):
        to_copies(step).wait_recv()
    gains[...] = jnp.sum(tile_sums_in[...], 0)
    for step in range(1, ranks):
        to_ranks(step).wait_send()
    for step in range(1, copies):
        to_copies(step).wait_send()
    ring.finish()
    total.finish()
    out_piece.finish()
    qkv_piece.finish()
    mlp_way.finish()
    out_way.finish()
    qkv_way.finish()


VM = pl.BlockSpec(memory_space=pltpu.VMEM)
ANY = pl.BlockSpec(memory_space=pl.ANY)


def call(kernel, number, ins, outs, scratch, operands):
    return pl.pallas_call(
        kernel,
        out_shape=[jax.ShapeDtypeStruct(shape, dtype) for shape, dtype, _ in outs],
        in_specs=ins,
        out_specs=[spec for _, _, spec in outs],
        scratch_shapes=scratch,
        compiler_params=pltpu.CompilerParams(
            collective_id=number, has_side_effects=True, vmem_limit_bytes=LIMIT
        ),
    )(*operands)


def columns_body(
    tokens,
    out_grad,
    span_order,
    doc_starts,
    w_query,
    w_key,
    w_value,
    w_output,
    attn_gain,
    query_gain,
    key_gain,
    w_gate,
    w_up,
    w_down,
    mlp_gain,
):
    ranks = lax.axis_size("seq")
    copies = lax.axis_size("dp")
    _, local, width = tokens.shape
    rows = local * ranks
    span = rows // span_order.shape[0]
    size = query_gain.shape[0]
    kv_heads = w_key.shape[1] // size // ranks
    heads = w_query.shape[1] // size // ranks
    q_cols, kv_cols = heads * size, kv_heads * size
    qkv_cols = q_cols + 2 * kv_cols
    a_cols = qkv_cols + q_cols
    ff = w_gate.shape[1] // ranks
    own = width // (ranks * copies)
    deep = own * copies
    f32 = jnp.float32

    def by_rank(parts):
        block = jnp.concatenate([part.reshape(own, ranks, -1) for part in parts], -1)
        return jnp.transpose(block, (1, 0, 2))

    gain_rows = attn_gain[:, None]
    mlp_rows = mlp_gain[:, None]
    attn_parts = [(w * gain_rows).astype(LOW) for w in (w_query, w_key, w_value)] + [w_output]
    mlp_parts = [(w * mlp_rows).astype(LOW) for w in (w_gate, w_up)] + [w_down]
    first_in, qkv, attn_block = call(
        functools.partial(enter_kernel, ranks),
        1,
        [VM, ANY],
        [
            ((rows, width), LOW, VM),
            ((rows, qkv_cols), f32, VM),
            ((ranks, deep, a_cols), LOW, VM),
        ],
        [pltpu.VMEM((rows, width), LOW)] + ring_sems(ranks) + spread_sems(ranks),
        (tokens[0], by_rank(attn_parts)),
    )
    at = ring_place(lax.axis_index("seq"), ranks)
    order = jnp.array(ring_order(ranks), jnp.int32)
    blocks = ring_seq(lax.rem(at + order, ranks), ranks)
    row_ids = (blocks[:, None] * local + jnp.arange(local, dtype=jnp.int32)[None, :]).reshape(-1)
    picked = (row_ids // span)[:, None] == jnp.arange(span_order.shape[0], dtype=jnp.int32)[None, :]
    pos = jnp.sum(jnp.where(picked, span_order[None, :], 0), -1) * span + row_ids % span
    begins = jnp.max(jnp.where(doc_starts <= pos[:, None], doc_starts, 0), -1)
    cosv, sinv = rotary(pos, size)
    cosv = jnp.concatenate([cosv[:, 0], cosv[:, 0]], -1)
    sinv = jnp.concatenate([-sinv[:, 0], sinv[:, 0]], -1)
    q_gain, k_gain = query_gain[None], key_gain[None]
    dy_all, q_low, k_low, v_low, prob, out_low, resid, second, mlp_block = call(
        functools.partial(attend_kernel, ranks, kv_heads),
        2,
        [VM] * 11 + [ANY],
        [
            ((rows, width), LOW, VM),
            ((heads, rows, size), LOW, VM),
            ((kv_heads, rows, size), LOW, VM),
            ((kv_heads, rows, size), LOW, VM),
            ((heads, rows, rows), LOW, VM),
            ((rows, q_cols), LOW, VM),
            ((local, width), f32, VM),
            ((local, width), LOW, VM),
            ((ranks, deep, 3 * ff), LOW, ANY),
        ],
        sum_bufs(local, ranks, width) + ring_sems(ranks) * 2 + spread_sems(ranks) * 3,
        (
            out_grad[0], tokens[0], qkv, attn_block, cosv, sinv, pos[:, None], begins[:, None], pos[None], q_gain,
            k_gain, by_rank(mlp_parts),
        ),
    )
    block_out, dresid, dresid_low, dgm, mlp_own = call(
        functools.partial(mlp_kernel, ranks),
        3,
        [VM, VM, VM, VM, ANY],
        [
            ((local, width), LOW, VM),
            ((local, width), f32, VM),
            ((local, width), LOW, VM),
            ((1, width), f32, VM),
            ((ranks, own, 3 * ff), LOW, VM),
        ],
        [pltpu.VMEM((ranks, deep, 3 * ff), LOW)]
        + reduce_bufs(ranks, own, 3 * ff)
        + [
            pltpu.VMEM((rows, width), LOW),
            pltpu.VMEM((ranks, deep, 3 * ff), LOW),
            pltpu.VMEM((rows, ff), LOW),
            pltpu.VMEM((rows, 2 * ff), LOW),
        ]
        + sum_bufs(local, ranks, width)
        + sum_bufs(local, ranks, width)[1:]
        + [pltpu.SemaphoreType.DMA]
        + ring_sems(ranks) * 3
        + reduce_sems() * 4,
        (second, resid, out_grad[0], dy_all, mlp_block),
    )
    tokens_grad, gains, mlp_sums, attn_sums = call(
        functools.partial(back_kernel, ranks, kv_heads),
        4,
        [VM] * 16 + [ANY],
        [
            ((local, width), f32, VM),
            ((8, size), f32, VM),
            ((ranks, own, 3 * ff), LOW, ANY),
            ((ranks, own, a_cols), LOW, VM),
        ],
        [pltpu.VMEM((ranks, deep, a_cols), LOW)]
        + reduce_bufs(ranks, own, a_cols)
        + [
            pltpu.VMEM((ranks, own, a_cols), LOW),
            pltpu.VMEM((1, width), f32),
            pltpu.VMEM((1, size), f32),
            pltpu.VMEM((1, size), f32),
            pltpu.VMEM((ranks, copies, 8, size), f32),
            pltpu.VMEM((ranks, copies, 8, size), f32),
            pltpu.VMEM((copies, 8, size), f32),
            pltpu.VMEM((copies, 8, size), f32),
            pltpu.VMEM((rows, width), LOW),
            pltpu.VMEM((rows, q_cols), LOW),
            pltpu.VMEM((kv_heads, rows, size), f32),
            pltpu.VMEM((kv_heads, rows, size), f32),
            pltpu.VMEM((rows, qkv_cols), LOW),
        ]
        + sum_bufs(local, ranks, width)
        + ring_sems(ranks) * 2
        + reduce_sems() * 2
        + deliver_sems(ranks) * 3
        + [pltpu.SemaphoreType.DMA((ranks,))] * 2
        + [pltpu.SemaphoreType.DMA((copies,))] * 2,
        (
            tokens[0], dresid, dresid_low, first_in, attn_block, qkv, cosv, sinv, q_gain, k_gain, q_low, k_low,
            v_low, prob, out_low, dgm, mlp_own,
        ),
    )

    def wide(part):
        return jnp.transpose(part, (1, 0, 2)).reshape(own, -1).astype(f32)

    return (
        block_out[None],
        tokens_grad[None],
        wide(attn_sums[..., :q_cols]) * gain_rows,
        wide(attn_sums[..., q_cols : q_cols + kv_cols]) * gain_rows,
        wide(attn_sums[..., q_cols + kv_cols : qkv_cols]) * gain_rows,
        wide(attn_sums[..., qkv_cols:]),
        gains[0, :own] / attn_gain,
        gains[1],
        gains[2],
        wide(mlp_sums[..., :ff]) * mlp_rows,
        wide(mlp_sums[..., ff : 2 * ff]) * mlp_rows,
        wide(mlp_sums[..., 2 * ff :]),
        gains[0, own : 2 * own] / mlp_gain,
    )


def body(*args):
    tokens, w_key, query_gain = args[0], args[5], args[9]
    groups = w_key.shape[1] // query_gain.shape[0]
    ranks = lax.axis_size("seq")
    if tokens.shape[0] == 1 and ranks % 2 == 0 and groups % ranks == 0 and lax.axis_size("dp") == 4:
        return columns_body(*args)
    return gathered_body(*args)


def solution(mesh):
    return jax.shard_map(
        body,
        mesh=mesh,
        in_specs=(
            P("dp", "seq", None),
            P("dp", "seq", None),
            P(),
            P("dp", None),
            P(("seq", "dp"), None),
            P(("seq", "dp"), None),
            P(("seq", "dp"), None),
            P(("seq", "dp"), None),
            P(("seq", "dp")),
            P(),
            P(),
            P(("seq", "dp"), None),
            P(("seq", "dp"), None),
            P(("seq", "dp"), None),
            P(("seq", "dp")),
        ),
        out_specs=(
            P("dp", "seq", None),
            P("dp", "seq", None),
            P(("seq", "dp"), None),
            P(("seq", "dp"), None),
            P(("seq", "dp"), None),
            P(("seq", "dp"), None),
            P(("seq", "dp")),
            P(),
            P(),
            P(("seq", "dp"), None),
            P(("seq", "dp"), None),
            P(("seq", "dp"), None),
            P(("seq", "dp")),
        ),
        check_vma=False,
    )
```

```python
import functools
import math

import jax
import jax.numpy as jnp
import numpy as np
from jax import lax
from jax.experimental import pallas as pl
from jax.experimental.pallas import tpu as pltpu
from jax.sharding import PartitionSpec as P

EPS = 1e-06
NEG = -1e30


def normed(v, gain):
    scale_inv = lax.rsqrt(jnp.mean(v * v, -1, keepdims=True) + EPS)
    return (v * scale_inv * gain, scale_inv)


def norm_back(v, scale_inv, gain, grad):
    scaled = grad * gain
    inner = jnp.mean(scaled * v, -1, keepdims=True)
    dv = scale_inv * scaled - v * scale_inv * scale_inv * scale_inv * inner
    dgain = jnp.sum((grad * v * scale_inv).reshape(-1, v.shape[-1]), 0)
    return (dv, dgain)


def rotary(pos, width):
    half = width // 2
    freqs = jnp.exp(jnp.arange(half, dtype=jnp.float32) * (-2.0 / width * math.log(1000000.0)))
    angle = pos.astype(jnp.float32)[:, None] * freqs[None, :]
    return (jnp.cos(angle)[:, None, :], jnp.sin(angle)[:, None, :])


def rotate(v, cosv, sinv):
    half = v.shape[-1] // 2
    first, second = (v[..., :half], v[..., half:])
    return jnp.concatenate([first * cosv - second * sinv, second * cosv + first * sinv], -1)


def rotate_back(grad, cosv, sinv):
    half = grad.shape[-1] // 2
    first, second = (grad[..., :half], grad[..., half:])
    return jnp.concatenate([first * cosv + second * sinv, second * cosv - first * sinv], -1)


def place(order, begin, count, span):
    rows = begin + jnp.arange(count, dtype=jnp.int32)
    slots = rows // span
    picked = slots[:, None] == jnp.arange(order.shape[0], dtype=jnp.int32)[None, :]
    return jnp.sum(jnp.where(picked, order[None, :], 0), -1) * span + rows % span


def doc_of(starts, pos):
    return jnp.sum((starts[:, None, :] <= pos[None, :, None]).astype(jnp.int32), -1)


def gathered_body(
    tokens,
    out_grad,
    span_order,
    doc_starts,
    w_query,
    w_key,
    w_value,
    w_output,
    attn_gain,
    query_gain,
    key_gain,
    w_gate,
    w_up,
    w_down,
    mlp_gain,
):
    seqs, local, width = tokens.shape
    span = local // 2
    head_size = query_gain.shape[0]
    kv_heads = w_key.shape[1] // head_size
    heads = w_query.shape[1] // head_size
    share = heads // kv_heads
    kv_width = kv_heads * head_size
    ff_width = w_gate.shape[1]
    scale = 1.0 / math.sqrt(head_size)
    total_rows = seqs * local
    own_rows = width // lax.axis_size(("seq", "dp"))
    qpos = place(span_order, lax.axis_index("seq") * local, local, span)
    qdoc = doc_of(doc_starts, qpos)
    cosv, sinv = rotary(qpos, head_size)

    def gather_attn():
        return (
            lax.all_gather(w_query, ("seq", "dp"), axis=0, tiled=True),
            lax.all_gather(w_key, ("seq", "dp"), axis=0, tiled=True),
            lax.all_gather(w_value, ("seq", "dp"), axis=0, tiled=True),
            lax.all_gather(w_output, ("seq", "dp"), axis=0, tiled=True),
            lax.all_gather(
                attn_gain.astype(jnp.bfloat16), ("seq", "dp"), axis=0, tiled=True
            ).astype(attn_gain.dtype),
        )

    def gather_mlp():
        return (
            lax.all_gather(w_gate, ("seq", "dp"), axis=0, tiled=True),
            lax.all_gather(w_up, ("seq", "dp"), axis=0, tiled=True),
            lax.all_gather(w_down, ("seq", "dp"), axis=0, tiled=True),
            lax.all_gather(mlp_gain.astype(jnp.bfloat16), ("seq", "dp"), axis=0, tiled=True).astype(
                mlp_gain.dtype
            ),
        )

    x_rows = tokens.astype(jnp.float32).reshape(total_rows, width)
    wq_all, wk_all, wv_all, wo_all, ga_all = gather_attn()
    first_norm, first_inv = normed(x_rows, ga_all)
    first_in = first_norm.astype(jnp.bfloat16)
    q_raw = jnp.dot(first_in, wq_all, preferred_element_type=jnp.float32).reshape(
        seqs, local, heads, head_size
    )
    k_raw = jnp.dot(first_in, wk_all, preferred_element_type=jnp.float32).reshape(
        seqs, local, kv_heads, head_size
    )
    v_low = (
        jnp.dot(first_in, wv_all, preferred_element_type=jnp.float32)
        .astype(jnp.bfloat16)
        .reshape(seqs, local, kv_heads, head_size)
    )
    q_normed, q_inv = normed(q_raw, query_gain)
    k_normed, k_inv = normed(k_raw, key_gain)
    q_low = rotate(q_normed, cosv, sinv).astype(jnp.bfloat16)
    k_low = rotate(k_normed, cosv, sinv).astype(jnp.bfloat16)
    q_group = q_low.reshape(seqs, local, kv_heads, share, head_size)

    def scores(piece_key, start):
        count = piece_key.shape[1]
        kpos = place(span_order, start, count, span)
        kdoc = doc_of(doc_starts, kpos)
        visible = (qdoc[:, :, None] == kdoc[:, None, :]) & (
            kpos[None, None, :] <= qpos[None, :, None]
        )
        raw = (
            jnp.einsum("sqgjd,skgd->sgjqk", q_group, piece_key, preferred_element_type=jnp.float32)
            * scale
        )
        return (raw, visible[:, None, None])

    start_top = jnp.full((seqs, kv_heads, share, local), NEG, jnp.float32)
    piece = (
        lax.all_gather(k_low, "seq", axis=1, tiled=True),
        lax.all_gather(v_low, "seq", axis=1, tiled=True),
    )
    top = start_top
    raw, visible = scores(piece[0], jnp.int32(0))
    raw = jnp.where(visible, raw, NEG)
    new_top = jnp.maximum(top, jnp.max(raw, -1))
    weights = jnp.where(visible, jnp.exp(raw - new_top[..., None]), 0.0)
    total = jnp.sum(weights, -1)
    summed = jnp.einsum(
        "sgjqk,skgd->sgjqd",
        weights.astype(jnp.bfloat16),
        piece[1],
        preferred_element_type=jnp.float32,
    )
    top, total, summed = (new_top, total, summed)
    log_total = top + jnp.log(total)
    attn_vals = summed / total[..., None]
    out_low = (
        jnp.transpose(attn_vals, (0, 3, 1, 2, 4))
        .reshape(total_rows, heads * head_size)
        .astype(jnp.bfloat16)
    )
    resid = x_rows + jnp.einsum("nh,dh->nd", out_low, wo_all, preferred_element_type=jnp.float32)
    wg_all, wu_all, wd_all, gm_all = gather_mlp()
    second_norm, second_inv = normed(resid, gm_all)
    second_in = second_norm.astype(jnp.bfloat16)
    gate = jnp.dot(second_in, wg_all, preferred_element_type=jnp.float32)
    upper = jnp.dot(second_in, wu_all, preferred_element_type=jnp.float32)
    sigma = jax.nn.sigmoid(gate)
    act = gate * sigma
    hidden = (act * upper).astype(jnp.bfloat16)
    result = resid + jnp.einsum("nf,df->nd", hidden, wd_all, preferred_element_type=jnp.float32)
    block_out = result.astype(jnp.bfloat16).reshape(seqs, local, width)
    grad_low = out_grad.reshape(total_rows, width)
    wg_all, wu_all, wd_all, gm_all = gather_mlp()
    dmid = jnp.einsum("nd,df->nf", grad_low, wd_all, preferred_element_type=jnp.float32)
    dgate = (dmid * upper * sigma * (1.0 + gate * (1.0 - sigma))).astype(jnp.bfloat16)
    dupper = (dmid * act).astype(jnp.bfloat16)
    left = second_in
    outer = grad_low
    mlp_sums = lax.psum_scatter(
        jnp.concatenate(
            [
                jnp.einsum("nd,nf->df", left, dgate, preferred_element_type=jnp.float32),
                jnp.einsum("nd,nf->df", left, dupper, preferred_element_type=jnp.float32),
                jnp.einsum("nd,nf->df", outer, hidden, preferred_element_type=jnp.float32),
            ],
            1,
        ),
        ("seq", "dp"),
        scatter_dimension=0,
        tiled=True,
    )
    dsecond = jnp.einsum(
        "nf,df->nd", dgate, wg_all, preferred_element_type=jnp.float32
    ) + jnp.einsum("nf,df->nd", dupper, wu_all, preferred_element_type=jnp.float32)
    dresid_norm, dgm = norm_back(resid, second_inv, gm_all, dsecond)
    dresid = grad_low.astype(jnp.float32) + dresid_norm
    dresid_low = dresid.astype(jnp.bfloat16)
    wq_all, wk_all, wv_all, wo_all, ga_all = gather_attn()
    dout_low = jnp.einsum(
        "nd,dh->nh", dresid_low, wo_all, preferred_element_type=jnp.float32
    ).astype(jnp.bfloat16)
    dout_group = dout_low.reshape(seqs, local, kv_heads, share, head_size)
    delta = jnp.sum(jnp.transpose(dout_group.astype(jnp.float32), (0, 2, 3, 1, 4)) * attn_vals, -1)
    piece = (
        lax.all_gather(k_low, "seq", axis=1, tiled=True),
        lax.all_gather(v_low, "seq", axis=1, tiled=True),
    )
    count = piece[0].shape[1]
    raw, visible = scores(piece[0], jnp.int32(0))
    prob = jnp.where(visible, jnp.exp(raw - log_total[..., None]), 0.0)
    dprob = jnp.einsum(
        "sqgjd,skgd->sgjqk", dout_group, piece[1], preferred_element_type=jnp.float32
    )
    dscore = (prob * (dprob - delta[..., None])).astype(jnp.bfloat16)
    dq_sum = jnp.einsum("sgjqk,skgd->sqgjd", dscore, piece[0], preferred_element_type=jnp.float32)
    dk_part = (
        jnp.einsum("sgjqk,sqgjd->skgd", dscore, q_group, preferred_element_type=jnp.float32) * scale
    )
    dv_part = jnp.einsum(
        "sgjqk,sqgjd->skgd",
        prob.astype(jnp.bfloat16),
        dout_group,
        preferred_element_type=jnp.float32,
    )
    joined = jnp.concatenate(
        [dk_part.reshape(seqs, count, kv_width), dv_part.reshape(seqs, count, kv_width)], -1
    )
    buffer = joined
    dq_sum, buffer = (dq_sum, buffer)
    key_sums = lax.psum_scatter(
        buffer.astype(jnp.bfloat16), "seq", scatter_dimension=1, tiled=True
    ).astype(jnp.float32)
    dq_rot = (dq_sum * scale).reshape(seqs, local, heads, head_size)
    dq_raw, dgq = norm_back(q_raw, q_inv, query_gain, rotate_back(dq_rot, cosv, sinv))
    dk_rot = key_sums[..., :kv_width].reshape(seqs, local, kv_heads, head_size)
    dk_raw, dgk = norm_back(k_raw, k_inv, key_gain, rotate_back(dk_rot, cosv, sinv))
    dq_low = dq_raw.reshape(total_rows, heads * head_size).astype(jnp.bfloat16)
    dk_low = dk_raw.reshape(total_rows, kv_width).astype(jnp.bfloat16)
    dv_low = key_sums[..., kv_width:].reshape(total_rows, kv_width).astype(jnp.bfloat16)
    left = first_in
    outer = dresid_low
    attn_sums = lax.psum_scatter(
        jnp.concatenate(
            [
                jnp.einsum("nd,nh->dh", left, dq_low, preferred_element_type=jnp.float32),
                jnp.einsum("nd,nh->dh", left, dk_low, preferred_element_type=jnp.float32),
                jnp.einsum("nd,nh->dh", left, dv_low, preferred_element_type=jnp.float32),
                jnp.einsum("nd,nh->dh", outer, out_low, preferred_element_type=jnp.float32),
            ],
            1,
        ),
        ("seq", "dp"),
        scatter_dimension=0,
        tiled=True,
    )
    dfirst = jnp.einsum("nh,dh->nd", dq_low, wq_all, preferred_element_type=jnp.float32)
    dfirst = dfirst + jnp.einsum("nh,dh->nd", dk_low, wk_all, preferred_element_type=jnp.float32)
    dfirst = dfirst + jnp.einsum("nh,dh->nd", dv_low, wv_all, preferred_element_type=jnp.float32)
    dx_norm, dga = norm_back(x_rows, first_inv, ga_all, dfirst)
    tokens_grad = (dresid + dx_norm).reshape(seqs, local, width)
    dga_all, dgm_all, dgq_all, dgk_all = lax.psum((dga, dgm, dgq, dgk), ("seq", "dp"))
    offset = lax.axis_index(("seq", "dp")) * own_rows
    attn_gain_grad = lax.dynamic_slice_in_dim(dga_all, offset, own_rows, 0)
    mlp_gain_grad = lax.dynamic_slice_in_dim(dgm_all, offset, own_rows, 0)
    q_cols = heads * head_size
    w_query_grad = attn_sums[:, :q_cols]
    w_key_grad = attn_sums[:, q_cols : q_cols + kv_width]
    w_value_grad = attn_sums[:, q_cols + kv_width : q_cols + 2 * kv_width]
    w_output_grad = attn_sums[:, q_cols + 2 * kv_width :]
    w_gate_grad = mlp_sums[:, :ff_width]
    w_up_grad = mlp_sums[:, ff_width : 2 * ff_width]
    w_down_grad = mlp_sums[:, 2 * ff_width :]
    return (
        block_out,
        tokens_grad,
        w_query_grad,
        w_key_grad,
        w_value_grad,
        w_output_grad,
        attn_gain_grad,
        dgq_all,
        dgk_all,
        w_gate_grad,
        w_up_grad,
        w_down_grad,
        mlp_gain_grad,
    )


LOW = jnp.bfloat16
MESH = pl.DeviceIdType.MESH
LIMIT = 60 * 2**20


def ring_order(ranks):
    half = ranks // 2
    order = [0]
    for step in range(1, half):
        order += [step, ranks - step]
    return order + [half]


def ring_place(seq, ranks):
    z, x = lax.div(seq, 2), lax.rem(seq, 2)
    return z + x * (ranks - 1 - 2 * z)


def ring_seq(place, ranks):
    half = ranks // 2
    x, z = lax.div(place, half), lax.rem(place, half)
    return 2 * (z + x * (half - 1 - 2 * z)) + x


def neighbours(ranks):
    seq, dp = lax.axis_index("seq"), lax.axis_index("dp")
    at = ring_place(seq, ranks)
    right = ring_seq(lax.rem(at + 1, ranks), ranks)
    left = ring_seq(lax.rem(at + ranks - 1, ranks), ranks)
    return (right, dp), (left, dp)


def knock(devices):
    barrier = pltpu.get_barrier_semaphore()
    for device in devices:
        pl.semaphore_signal(barrier, inc=1, device_id=device, device_id_type=MESH)


def answered(devices):
    pl.semaphore_wait(pltpu.get_barrier_semaphore(), len(devices))


def move(src, dst, sem):
    copy = pltpu.make_async_copy(src, dst, sem)
    copy.start()
    return copy


def push(src, dst, send, recv, device):
    return pltpu.make_async_remote_copy(
        src_ref=src, dst_ref=dst, send_sem=send, recv_sem=recv, device_id=device, device_id_type=MESH
    )


def dot_nn(left, right):
    return jnp.dot(left, right, preferred_element_type=jnp.float32)


def dot_nt(left, right):
    return lax.dot_general(left, right, (((1,), (1,)), ((), ())), preferred_element_type=jnp.float32)


def dot_tn(left, right):
    return lax.dot_general(left, right, (((0,), (0,)), ((), ())), preferred_element_type=jnp.float32)


class RingGather:
    def __init__(self, buf, local, ranks, send, recv, right, left):
        self.buf, self.local, self.half = buf, local, ranks // 2
        self.send, self.recv, self.right, self.left = send, recv, right, left
        self.row = {rel: at * local for at, rel in enumerate(ring_order(ranks))}
        self.ranks = ranks

    def copies(self, step):
        last = step == self.half
        rows = self.local // 2 if last else self.local
        skip = self.local // 2 if last else 0
        pairs = (
            ((self.ranks - step + 1) % self.ranks, self.ranks - step, 0, self.right),
            (step - 1, step, skip, self.left),
        )
        return [
            push(
                self.buf.at[pl.ds(self.row[src] + begin, rows)],
                self.buf.at[pl.ds(self.row[dst] + begin, rows)],
                self.send.at[way, step - 1],
                self.recv.at[way, step - 1],
                device,
            )
            for way, (src, dst, begin, device) in enumerate(pairs)
        ]

    def start(self, step):
        for copy in self.copies(step):
            copy.start()

    def arrive(self, step):
        for copy in self.copies(step):
            copy.wait_recv()

    def finish(self):
        for step in range(1, self.half + 1):
            for copy in self.copies(step):
                copy.wait_send()

    def rows(self, step):
        if step == 0:
            return 0, self.local
        if step == self.half:
            return self.row[self.half], self.local
        return self.row[step], 2 * self.local


class RingSum:
    def __init__(self, part, term, out_buf, in_buf, local, ranks, send, recv, right, left):
        self.part, self.term, self.out_buf, self.in_buf = part, term, out_buf, in_buf
        self.local, self.ranks, self.half = local, ranks, ranks // 2
        self.send, self.recv, self.right, self.left = send, recv, right, left
        self.row = {rel: at * local for at, rel in enumerate(ring_order(ranks))}

    def copies(self, step):
        rows = self.local // 2 if step == 1 else self.local
        skip = self.local // 2 if step == 1 else 0
        return [
            push(
                self.out_buf.at[way, (step - 1) % 2, pl.ds(begin, rows)],
                self.in_buf.at[way, step - 1, pl.ds(begin, rows)],
                self.send.at[way, step - 1],
                self.recv.at[way, step - 1],
                device,
            )
            for way, begin, device in ((0, 0, self.right), (1, skip, self.left))
        ]

    def compute(self, step):
        if step == 1:
            self.part(self.row[self.half], self.local)
        elif step <= self.half:
            self.part(self.row[self.half + 1 - step], 2 * self.local)
        else:
            self.part(0, self.local)

    def launch(self, step):
        local, skip = self.local, self.local // 2
        if step > 2:
            for copy in self.copies(step - 2):
                copy.wait_send()
        if step == 1:
            self.out_buf[0, 0, :skip] = self.term[:skip].astype(LOW)
            self.out_buf[1, 0, skip:] = self.term[skip:local].astype(LOW)
        else:
            for copy in self.copies(step - 1):
                copy.wait_recv()
            for way in range(2):
                for begin, with_sum in ((0, step > 2 or way == 0), (skip, step > 2 or way == 1)):
                    value = self.term[pl.ds(way * local + begin, skip)]
                    if with_sum:
                        value = value + self.in_buf[way, step - 2, pl.ds(begin, skip)].astype(jnp.float32)
                    self.out_buf[way, (step - 1) % 2, pl.ds(begin, skip)] = value.astype(LOW)
        for copy in self.copies(step):
            copy.start()

    def last(self, begin, count):
        rows = pl.ds(begin, count)
        value = self.term[rows] + self.in_buf[0, self.half - 1, rows].astype(jnp.float32)
        return value + self.in_buf[1, self.half - 1, rows].astype(jnp.float32)

    def arrive_last(self):
        for copy in self.copies(self.half):
            copy.wait_recv()

    def finish(self):
        for step in range(max(1, self.half - 1), self.half + 1):
            for copy in self.copies(step):
                copy.wait_send()


def ring_sems(ranks):
    return [pltpu.SemaphoreType.DMA((2, ranks // 2)), pltpu.SemaphoreType.DMA((2, ranks // 2))]


def sum_bufs(local, ranks, width):
    return [
        pltpu.VMEM((2 * local, width), jnp.float32),
        pltpu.VMEM((2, 2, local, width), LOW),
        pltpu.VMEM((2, ranks // 2, local, width), LOW),
    ]


def turn(v):
    return pltpu.roll(v, v.shape[-1] // 2, v.ndim - 1)


def rows_scaled(v):
    inv = lax.rsqrt(jnp.mean(v * v, -1, keepdims=True) + EPS)
    return v * inv, inv


def rows_scaled_back(v, inv, grad):
    return inv * grad - v * (inv * inv * inv * jnp.mean(grad * v, -1, keepdims=True))


class Spread:
    def __init__(self, rows, block, ranks, own, cols, sems):
        self.rows, self.block, self.ranks, self.own, self.cols = rows, block, ranks, own, cols
        self.send, self.recv, self.hop_send, self.hop_recv, self.here = sems
        self.seq, self.dp = lax.axis_index("seq"), lax.axis_index("dp")
        y, core = lax.div(self.dp, 2), lax.rem(self.dp, 2)
        self.beside, self.sibling = (1 - y) * 2 + core, y * 2 + 1 - core

    def at(self, dp):
        return pl.ds(pl.multiple_of(dp * self.own, self.own), self.own)

    def exchange(self):
        for step in range(1, self.ranks):
            peer = lax.rem(self.seq + step, self.ranks)
            yield push(
                self.rows.at[peer, :, self.cols],
                self.block.at[self.seq, self.at(self.dp), self.cols],
                self.send.at[step],
                self.recv.at[step],
                (peer, self.dp),
            )

    def keep(self):
        return pltpu.make_async_copy(
            self.rows.at[self.seq, :, self.cols],
            self.block.at[self.seq, self.at(self.dp), self.cols],
            self.here,
        )

    def hop(self, number):
        dp = self.beside if number == 2 else self.dp
        part = self.block.at[:, self.at(dp), self.cols]
        to = self.beside if number == 0 else self.sibling
        return push(part, part, self.hop_send.at[number], self.hop_recv.at[number], (self.seq, to))

    def start(self):
        self.keep().start()
        for copy in self.exchange():
            copy.start()

    def arrive(self):
        self.keep().wait()
        for copy in self.exchange():
            copy.wait_recv()

    def finish(self):
        for copy in self.exchange():
            copy.wait_send()
        for number in range(3):
            self.hop(number).wait_send()


def spread_sems(ranks):
    return [
        pltpu.SemaphoreType.DMA((ranks,)),
        pltpu.SemaphoreType.DMA((ranks,)),
        pltpu.SemaphoreType.DMA((3,)),
        pltpu.SemaphoreType.DMA((3,)),
        pltpu.SemaphoreType.DMA,
    ]


class Reduce:
    def __init__(self, grads, from_core, from_y, total, own, first, count, cols, sems):
        self.grads, self.from_core, self.from_y, self.total = grads, from_core, from_y, total
        self.own, self.begin, self.count, self.cols = own, first, count, cols
        self.send, self.recv = sems
        self.seq, dp = lax.axis_index("seq"), lax.axis_index("dp")
        self.y, self.core = lax.div(dp, 2), lax.rem(dp, 2)
        self.beside, self.sibling = (1 - self.y) * 2 + self.core, self.y * 2 + 1 - self.core

    def at(self, y, core):
        return pl.ds(pl.multiple_of((y * 2 + core) * self.own, self.own), self.own)

    def hop(self, number):
        some, cols = pl.ds(self.begin, self.count), self.cols
        if number == 2:
            src, dst, to = self.from_core.at[0, some, :, cols], self.from_y.at[some, :, cols], self.beside
        else:
            rows = self.at(1 - self.y if number == 0 else self.y, 1 - self.core)
            src, dst, to = self.grads.at[some, rows, cols], self.from_core.at[number, some, :, cols], self.sibling
        return push(src, dst, self.send.at[number], self.recv.at[number], (self.seq, to))

    def first(self):
        self.hop(0).start()
        self.hop(1).start()

    def second(self):
        self.hop(0).wait_recv()
        rows = self.at(1 - self.y, self.core)

        def some(at, _):
            value = self.grads[at, rows, self.cols].astype(jnp.float32)
            value = value + self.from_core[0, at, :, self.cols].astype(jnp.float32)
            self.from_core[0, at, :, self.cols] = value.astype(LOW)
            return 0

        lax.fori_loop(self.begin, self.begin + self.count, some, 0)
        self.hop(2).start()

    def third(self):
        self.hop(1).wait_recv()
        self.hop(2).wait_recv()
        rows = self.at(self.y, self.core)

        def some(at, _):
            value = self.grads[at, rows, self.cols].astype(jnp.float32)
            value = value + self.from_core[1, at, :, self.cols].astype(jnp.float32)
            value = value + self.from_y[at, :, self.cols].astype(jnp.float32)
            self.total[at, :, self.cols] = value.astype(LOW)
            return 0

        lax.fori_loop(self.begin, self.begin + self.count, some, 0)

    def finish(self):
        for number in range(3):
            self.hop(number).wait_send()


def reduce_sems():
    return [pltpu.SemaphoreType.DMA((3,)), pltpu.SemaphoreType.DMA((3,))]


def reduce_bufs(ranks, own, cols):
    return [pltpu.VMEM((2, ranks, own, cols), LOW), pltpu.VMEM((ranks, own, cols), LOW)]


class Deliver:
    def __init__(self, rows, out, cols, ranks, sems):
        self.rows, self.out, self.cols, self.ranks = rows, out, cols, ranks
        self.send, self.recv, self.here = sems
        self.seq, self.dp = lax.axis_index("seq"), lax.axis_index("dp")

    def exchange(self):
        for step in range(1, self.ranks):
            peer = lax.rem(self.seq + step, self.ranks)
            yield push(
                self.rows.at[peer, :, self.cols],
                self.out.at[self.seq, :, self.cols],
                self.send.at[step],
                self.recv.at[step],
                (peer, self.dp),
            )

    def keep(self):
        return pltpu.make_async_copy(
            self.rows.at[self.seq, :, self.cols], self.out.at[self.seq, :, self.cols], self.here
        )

    def start(self):
        self.keep().start()
        for copy in self.exchange():
            copy.start()

    def finish(self):
        self.keep().wait()
        for copy in self.exchange():
            copy.wait_recv()
        for copy in self.exchange():
            copy.wait_send()


def deliver_sems(ranks):
    return [pltpu.SemaphoreType.DMA((ranks,)), pltpu.SemaphoreType.DMA((ranks,)), pltpu.SemaphoreType.DMA]


def enter_kernel(
    ranks, order, starts, tokens, freqs, attn_gain, mlp_gain, w_query, w_key, w_value, w_output, w_gate, w_up, w_down,
    first_in, qkv, attn_block, mlp_rows, cosv, sinv, pos, begins, pos_row,
    held, normal, kept, block, a_rows, m_rows, gate, up, down, *sems,
):
    local, width = tokens.shape
    own = w_query.shape[0]
    size = freqs.shape[1]
    cols = qkv.shape[1]
    half = ranks // 2
    local_sems = sems[7]
    seq, dp = lax.axis_index("seq"), lax.axis_index("dp")
    right, left = neighbours(ranks)
    attn = Spread(a_rows, block, ranks, own, pl.ds(0, a_rows.shape[2]), sems[2:7])
    peers = [(lax.rem(seq + step, ranks), dp) for step in range(1, ranks)]
    peers += [(seq, attn.beside), (seq, attn.sibling)]
    knock(peers)
    loads = [
        move(src, dst, local_sems.at[at])
        for at, (src, dst) in enumerate(((w_gate, gate), (w_up, up), (w_down, down)))
    ]
    held[:local] = tokens[...]

    def column(row):
        same = lax.broadcasted_iota(jnp.int32, (own, own), 0) == lax.broadcasted_iota(jnp.int32, (own, own), 1)
        return jnp.sum(jnp.where(same, row, 0.0), 1, keepdims=True)

    def lay(target, first, weight, gain):
        each = weight.shape[1] // ranks
        for rank in range(ranks):
            part = weight[:, rank * each : (rank + 1) * each]
            if gain is not None:
                part = (part.astype(jnp.float32) * gain).astype(LOW)
            target[rank, :, first : first + each] = part
        return first + each

    gain = column(attn_gain[...])
    at = 0
    for weight in (w_query, w_key, w_value):
        at = lay(a_rows, at, weight, gain)
    lay(a_rows, at, w_output, None)
    answered(peers)
    ring = RingGather(held, local, ranks, sems[0], sems[1], right, left)
    ring.start(1)
    attn.start()
    stores = []

    def scale_rows(begin, count):
        def some(at, _):
            rows = pl.ds(pl.multiple_of(begin + at * 32, 32), 32)
            normal[rows] = rows_scaled(held[rows].astype(jnp.float32))[0].astype(LOW)
            return 0

        lax.fori_loop(0, count // 32, some, 0)
        rows = pl.ds(begin, count)
        stores.append(move(normal.at[rows], first_in.at[rows], local_sems.at[len(stores)]))

    def project(begin, count):
        rows = pl.ds(begin, count)
        weight = block[:, :, :cols].reshape(width, cols)
        kept[rows] = dot_nn(normal[rows], weight)
        stores.append(move(kept.at[rows], qkv.at[rows], local_sems.at[len(stores)]))

    for load in loads:
        load.wait()
    gain = column(mlp_gain[...])
    each = gate.shape[1] // ranks
    lay(m_rows, 0, gate, gain)
    lay(m_rows, each, up, gain)
    lay(m_rows, 2 * each, down, None)
    stores.append(move(m_rows, mlp_rows, local_sems.at[len(stores)]))
    scale_rows(*ring.rows(0))
    ring.arrive(1)
    ring.start(2)
    scale_rows(*ring.rows(1))
    attn.arrive()
    attn.hop(0).start()
    attn.hop(1).start()
    spans = order.shape[0]
    span = local * ranks // spans
    place = ring_place(seq, ranks)
    for at, rel in enumerate(ring_order(ranks)):
        rows = pl.ds(at * local, local)
        owner = ring_seq(lax.rem(place + rel, ranks), ranks)
        ids = owner * local + lax.broadcasted_iota(jnp.int32, (1, local), 1)
        where = jnp.zeros_like(ids)
        for slot in range(spans):
            inside = (ids >= slot * span) & (ids < (slot + 1) * span)
            where = where + jnp.where(inside, ids + (order[slot] - slot) * span, 0)
        first = jnp.zeros_like(ids)
        for doc in range(starts.shape[1]):
            first = jnp.maximum(first, jnp.where(starts[0, doc] <= where, starts[0, doc], 0))
        pos_row[:, rows] = where
        across = jnp.broadcast_to(where, (local, local)).T
        pos[rows] = across[:, :1]
        begins[rows] = jnp.broadcast_to(first, (local, local)).T[:, :1]
        angle = across[:, :1].astype(jnp.float32) * freqs[...]
        lane = lax.broadcasted_iota(jnp.int32, (local, size), 1)
        cosv[rows] = jnp.cos(angle)
        sine = jnp.sin(angle)
        sinv[rows] = jnp.where(lane < size // 2, -sine, sine)
    ring.arrive(2)
    ring.start(3)
    scale_rows(*ring.rows(2))
    attn.hop(0).wait_recv()
    attn.hop(2).start()
    for step in range(3, half):
        ring.arrive(step)
        ring.start(step + 1)
        scale_rows(*ring.rows(step))
    attn.hop(1).wait_recv()
    attn.hop(2).wait_recv()
    stores.append(move(block, attn_block, local_sems.at[len(stores)]))
    for step in range(half):
        project(*ring.rows(step))
    ring.arrive(half)
    scale_rows(*ring.rows(half))
    project(*ring.rows(half))
    ring.finish()
    attn.finish()
    for store in stores:
        store.wait()


def attend_kernel(
    ranks, kv_heads, out_grad, tokens, qkv, cosv, sinv, pos, begins, pos_row, query_gain, key_gain, attn_block,
    mlp_rows, q_low, k_low, v_low, out_low, resid, second, dy_all, prob, mlp_block,
    dys, probs, w_output, term, out_buf, in_buf, *sems,
):
    local, width = tokens.shape
    rows = local * ranks
    size = cosv.shape[1]
    heads = q_low.shape[0]
    share = heads // kv_heads
    half = ranks // 2
    scale = 1.0 / math.sqrt(size)
    first_col = (heads + 2 * kv_heads) * size
    deep = attn_block.shape[1]
    right, left = neighbours(ranks)
    seq, dp = lax.axis_index("seq"), lax.axis_index("dp")
    own = mlp_rows.shape[1]
    third = mlp_rows.shape[2] // 3
    mlp = [
        Spread(mlp_rows, mlp_block, ranks, own, pl.ds(at * third, third), sems[4 + 5 * at : 9 + 5 * at])
        for at in range(3)
    ]
    local_sems = sems[19]
    peers = [(lax.rem(seq + step, ranks), dp) for step in range(1, ranks)]
    peers += [(seq, mlp[0].beside), (seq, mlp[0].sibling)]
    knock(peers)
    load = move(attn_block.at[:, :, pl.ds(first_col, heads * size)], w_output, local_sems.at[0])
    dys[:local] = out_grad[...]
    answered(peers)
    ring = RingGather(dys, local, ranks, sems[0], sems[1], right, left)
    for piece in mlp:
        piece.start()
    ring.start(1)
    tile = rows // half
    stores = []

    def rotated(at, rows_at, gain):
        v = rows_scaled(qkv[rows_at, at * size : (at + 1) * size])[0] * gain[...]
        return (v * cosv[rows_at] + turn(v) * sinv[rows_at]).astype(LOW)

    for piece in range(half):
        rows_at = pl.ds(piece * tile, tile)
        for head in range(heads):
            q_low[head, rows_at] = rotated(head, rows_at, query_gain)
        for group in range(kv_heads):
            k_low[group, rows_at] = rotated(heads + group, rows_at, key_gain)
            at = (heads + kv_heads + group) * size
            v_low[group, rows_at] = qkv[rows_at, at : at + size].astype(LOW)

    def forward(piece):
        mlp[piece].arrive()
        mlp[piece].hop(0).start()
        mlp[piece].hop(1).start()

    for piece in range(half):
        rows_at = pl.ds(piece * tile, tile)
        seen = (pos_row[...] <= pos[rows_at]) & (pos_row[...] >= begins[rows_at])
        for head in range(heads):
            raw = dot_nt(q_low[head, rows_at], k_low[head // share]) * scale
            raw = jnp.where(seen, raw, NEG)
            weight = jnp.exp(raw - jnp.max(raw, -1, keepdims=True))
            weight = (weight * (1.0 / jnp.sum(weight, -1, keepdims=True))).astype(LOW)
            probs[head, rows_at] = weight
            value = dot_nn(weight, v_low[head // share])
            out_low[rows_at, head * size : (head + 1) * size] = value.astype(LOW)
            stores.append(move(probs.at[head, rows_at], prob.at[head, rows_at], local_sems.at[1 + len(stores)]))
        if piece == 1:
            ring.arrive(1)
            ring.start(2)
        if piece >= 2:
            forward(piece - 2)
        if piece == half - 1:
            ring.arrive(2)
            ring.start(3)
    load.wait()

    def part(begin, count):
        def some(at, _):
            value = dot_nt(out_low[pl.ds(begin, count)], w_output[at])
            term[:count, pl.ds(pl.multiple_of(at * deep, deep), deep)] = value
            return 0

        lax.fori_loop(0, ranks, some, 0)

    total = RingSum(part, term, out_buf, in_buf, local, ranks, sems[2], sems[3], right, left)
    for step in range(1, half + 1):
        total.compute(step)
        total.launch(step)
        if step == 1:
            forward(2)
        if step == 2:
            for later in range(3, half):
                ring.arrive(later)
                ring.start(later + 1)
            mlp[0].hop(0).wait_recv()
            mlp[0].hop(2).start()
        if step == 3:
            mlp[1].hop(0).wait_recv()
            mlp[1].hop(2).start()
    total.compute(half + 1)
    ring.arrive(half)
    stores.append(move(dys, dy_all, local_sems.at[1 + len(stores)]))
    mlp[2].hop(0).wait_recv()
    mlp[2].hop(2).start()
    total.arrive_last()

    def some(at, _):
        begin = pl.multiple_of(at * 32, 32)
        rows_at = pl.ds(begin, 32)
        value = tokens[rows_at].astype(jnp.float32) + total.last(begin, 32)
        resid[rows_at] = value
        second[rows_at] = rows_scaled(value)[0].astype(LOW)
        return 0

    lax.fori_loop(0, local // 32, some, 0)
    ring.finish()
    total.finish()
    for piece in mlp:
        piece.hop(1).wait_recv()
        piece.hop(2).wait_recv()
        piece.finish()
    for store in stores:
        store.wait()


def mlp_kernel(
    ranks, second, out_grad, rest, dys, mlp_block, block_out, dresid, dresid_low, gain_grad, own_grads,
    grads, from_core, from_y, held, weights, hidden, dgu, resid, dy_all,
    term, out_buf, in_buf, y_out, y_in, here, *sems,
):
    local, width = second.shape
    ff = hidden.shape[1]
    deep = weights.shape[1]
    half = ranks // 2
    right, left = neighbours(ranks)
    loads = [
        move(src, dst, here.at[at])
        for at, (src, dst) in enumerate(((mlp_block, weights), (dys, dy_all), (rest, resid)))
    ]
    seq, dp = lax.axis_index("seq"), lax.axis_index("dp")
    own = own_grads.shape[1]
    pieces = [
        Reduce(
            grads, from_core, from_y, own_grads, own, at * ranks // 4, ranks // 4, pl.ds(0, 3 * ff),
            sems[6 + 2 * at : 8 + 2 * at],
        )
        for at in range(4)
    ]
    peers = [right, left, (seq, pieces[0].beside), (seq, pieces[0].sibling)]
    knock(peers)
    held[:local] = second[...]
    answered(peers)
    ring = RingGather(held, local, ranks, sems[0], sems[1], right, left)
    ring.start(1)
    loads[0].wait()
    loads[1].wait()
    wide = 256

    def middle(begin, count):
        rows = pl.ds(begin, count)

        def some(at, _):
            first = pl.multiple_of(at * wide, wide)
            gate = dot_nn(held[rows], weights[:, :, pl.ds(first, wide)].reshape(width, wide))
            upper = dot_nn(held[rows], weights[:, :, pl.ds(ff + first, wide)].reshape(width, wide))
            dmid = dot_nn(dy_all[rows], weights[:, :, pl.ds(2 * ff + first, wide)].reshape(width, wide))
            sigma = 1.0 / (1.0 + jnp.exp(-gate))
            act = gate * sigma
            hidden[rows, pl.ds(first, wide)] = (act * upper).astype(LOW)
            slope = sigma * (1.0 + gate * (1.0 - sigma))
            dgu[rows, pl.ds(first, wide)] = (dmid * upper * slope).astype(LOW)
            dgu[rows, pl.ds(ff + first, wide)] = (dmid * act).astype(LOW)
            return 0

        lax.fori_loop(0, ff // wide, some, 0)

    middle(*ring.rows(0))
    for step in range(1, half + 1):
        ring.arrive(step)
        if step < half:
            ring.start(step + 1)
        middle(*ring.rows(step))

    def back_part(begin, count):
        def some(at, _):
            value = dot_nt(dgu[pl.ds(begin, count)], weights[at, :, : 2 * ff])
            term[:count, pl.ds(pl.multiple_of(at * deep, deep), deep)] = value
            return 0

        lax.fori_loop(0, ranks, some, 0)

    def out_part(begin, count):
        def some(at, _):
            value = dot_nt(hidden[pl.ds(begin, count)], weights[at, :, 2 * ff :])
            term[:count, pl.ds(pl.multiple_of(at * deep, deep), deep)] = value
            return 0

        lax.fori_loop(0, ranks, some, 0)

    def weight_grads(first, count):
        def some(at, _):
            cols = pl.ds(pl.multiple_of(at * deep, deep), deep)
            grads[at, :, : 2 * ff] = dot_tn(held[:, cols], dgu[...]).astype(LOW)
            grads[at, :, 2 * ff :] = dot_tn(dy_all[:, cols], hidden[...]).astype(LOW)
            return 0

        lax.fori_loop(first, first + count, some, 0)

    back = RingSum(back_part, term, out_buf, in_buf, local, ranks, sems[2], sems[3], right, left)
    out = RingSum(out_part, term, y_out, y_in, local, ranks, sems[4], sems[5], right, left)
    for step in range(1, half + 1):
        back.compute(step)
        back.launch(step)
        out.compute(step)
        out.launch(step)
        if step < 3:
            for piece in pieces[2 * step - 2 : 2 * step]:
                weight_grads(piece.begin, piece.count)
                piece.first()
        if 1 < step < 4:
            for piece in pieces[2 * step - 4 : 2 * step - 2]:
                piece.second()
        if step > 2:
            for piece in pieces[2 * step - 6 : 2 * step - 4]:
                piece.third()
    back.compute(half + 1)
    loads[2].wait()
    back.arrive_last()
    gain_grad[...] = jnp.zeros_like(gain_grad)

    def finish_back(at, _):
        begin = pl.multiple_of(at * 32, 32)
        rows = pl.ds(begin, 32)
        value = resid[rows]
        normal, inv = rows_scaled(value)
        grad = back.last(begin, 32)
        full = out_grad[rows].astype(jnp.float32) + rows_scaled_back(value, inv, grad)
        dresid[rows] = full
        dresid_low[rows] = full.astype(LOW)
        gain_grad[...] += jnp.sum(grad * normal, 0, keepdims=True)
        return 0

    lax.fori_loop(0, local // 32, finish_back, 0)
    out.compute(half + 1)
    out.arrive_last()

    def finish_out(at, _):
        begin = pl.multiple_of(at * 32, 32)
        rows = pl.ds(begin, 32)
        block_out[rows] = (resid[rows] + out.last(begin, 32)).astype(LOW)
        return 0

    lax.fori_loop(0, local // 32, finish_out, 0)
    ring.finish()
    back.finish()
    out.finish()
    for piece in pieces:
        piece.finish()


def back_kernel(
    ranks, kv_heads, tokens, dresid_low, query_gain, key_gain, mlp_gain_part, out_low_in, first_in_in, block_in,
    qkv_in, cos_in, sin_in, q_in, k_in, v_in, prob_in, dresid_in, mlp_own,
    tokens_grad, gains, mlp_sums, attn_sums,
    grads, from_core, from_y, own_grads, gain_grad, query_gain_grad, key_gain_grad,
    tiles, tiles_in, tile_sums, tile_sums_in, held, dout, dk, dv, dqkv,
    out_low, first_in, attn_block, qkv, cosv, sinv, q_low, k_low, v_low, prob, dresid, term, out_buf, in_buf, *sems,
):
    local, width = tokens.shape
    rows = local * ranks
    half = ranks // 2
    size = cosv.shape[1]
    heads = q_low.shape[0]
    share = heads // kv_heads
    scale = 1.0 / math.sqrt(size)
    cols = (heads + 2 * kv_heads) * size
    deep = attn_block.shape[1]
    o_cols = heads * size
    right, left = neighbours(ranks)
    seq, dp = lax.axis_index("seq"), lax.axis_index("dp")
    own = mlp_own.shape[1]
    copies = tiles.shape[1]
    all_cols = grads.shape[2]
    out_piece = Reduce(
        grads, from_core, from_y, own_grads, own, 0, ranks, pl.ds(cols, all_cols - cols), sems[4:6]
    )
    qkv_piece = Reduce(grads, from_core, from_y, own_grads, own, 0, ranks, pl.ds(0, cols), sems[6:8])
    mlp_way = Deliver(mlp_own, mlp_sums, pl.ds(0, mlp_own.shape[2]), ranks, sems[8:11])
    out_way = Deliver(own_grads, attn_sums, pl.ds(cols, all_cols - cols), ranks, sems[11:14])
    qkv_way = Deliver(own_grads, attn_sums, pl.ds(0, cols), ranks, sems[14:17])
    peers = [(lax.rem(seq + step, ranks), dp) for step in range(1, ranks)]
    peers += [(seq, lax.rem(dp + step, copies)) for step in range(1, copies)]
    knock(peers)
    local_sems = sems[21]
    loads = {}
    for at, (name, src, dst) in enumerate(
        (
            ("block", block_in, attn_block), ("out", out_low_in, out_low), ("v", v_in, v_low),
            ("prob", prob_in, prob), ("k", k_in, k_low), ("q", q_in, q_low), ("cos", cos_in, cosv),
            ("sin", sin_in, sinv), ("qkv", qkv_in, qkv), ("first", first_in_in, first_in),
            ("dresid", dresid_in, dresid),
        )
    ):
        loads[name] = move(src, dst, local_sems.at[at])
    held[:local] = dresid_low[...]
    answered(peers)
    ring = RingGather(held, local, ranks, sems[0], sems[1], right, left)
    ring.start(1)
    loads["block"].wait()

    def project(begin, count):
        at = pl.ds(begin, count)
        dout[at] = dot_nn(held[at], attn_block[:, :, cols:].reshape(width, o_cols)).astype(LOW)

    project(*ring.rows(0))
    for step in range(1, half + 1):
        ring.arrive(step)
        if step < half:
            ring.start(step + 1)
        if step == half - 1:
            mlp_way.start()
        project(*ring.rows(step))
    loads["out"].wait()

    def out_grads(at, _):
        some_cols = pl.ds(pl.multiple_of(at * deep, deep), deep)
        grads[at, :, cols:] = dot_tn(held[:, some_cols], out_low[...]).astype(LOW)
        return 0

    lax.fori_loop(0, ranks, out_grads, 0)
    out_piece.first()
    for name in ("v", "prob", "k", "q", "cos", "sin", "qkv"):
        loads[name].wait()
    tile = rows // half
    query_gain_grad[...] = jnp.zeros_like(query_gain_grad)
    key_gain_grad[...] = jnp.zeros_like(key_gain_grad)

    def unrotated(grad, column, rows_at, gain, gain_grad_ref):
        grad = grad * cosv[rows_at] - turn(grad) * sinv[rows_at]
        value = qkv[rows_at, column * size : (column + 1) * size]
        normal, inv = rows_scaled(value)
        gain_grad_ref[...] += jnp.sum(grad * normal, 0, keepdims=True)
        back = rows_scaled_back(value, inv, grad * gain[...])
        dqkv[rows_at, column * size : (column + 1) * size] = back.astype(LOW)

    for head in range(heads):
        group = head // share

        def one(piece, _):
            rows_at = pl.ds(pl.multiple_of(piece * tile, tile), tile)
            weight = prob[head, rows_at]
            grad = dout[rows_at, head * size : (head + 1) * size]
            dprob = dot_nt(grad, v_low[group])
            full = weight.astype(jnp.float32)
            delta = jnp.sum(full * dprob, -1, keepdims=True)
            dscore = (full * (dprob - delta)).astype(LOW)
            dq = dot_nn(dscore, k_low[group]) * scale
            dk_add = dot_tn(dscore, q_low[head, rows_at]) * scale
            dv_add = dot_tn(weight, grad)
            dk[group] += dk_add
            dv[group] += dv_add
            unrotated(dq, head, rows_at, query_gain, query_gain_grad)
            return 0

        if head % share == 0:
            dk[group] = jnp.zeros_like(dk[group])
            dv[group] = jnp.zeros_like(dv[group])
        lax.fori_loop(0, half, one, 0)
        if head == 0:
            out_piece.second()
    for group in range(kv_heads):
        def one_key(piece, _):
            rows_at = pl.ds(pl.multiple_of(piece * tile, tile), tile)
            unrotated(dk[group, rows_at], heads + group, rows_at, key_gain, key_gain_grad)
            at = (heads + kv_heads + group) * size
            dqkv[rows_at, at : at + size] = dv[group, rows_at].astype(LOW)
            return 0

        lax.fori_loop(0, half, one_key, 0)

    def part(begin, count):
        def some(at, _):
            value = dot_nt(dqkv[pl.ds(begin, count)], attn_block[at, :, :cols])
            term[:count, pl.ds(pl.multiple_of(at * deep, deep), deep)] = value
            return 0

        lax.fori_loop(0, ranks, some, 0)

    def qkv_grads(at, _):
        some_cols = pl.ds(pl.multiple_of(at * deep, deep), deep)
        grads[at, :, :cols] = dot_tn(first_in[:, some_cols], dqkv[...]).astype(LOW)
        return 0

    total = RingSum(part, term, out_buf, in_buf, local, ranks, sems[2], sems[3], right, left)
    for step in range(1, half + 1):
        total.compute(step)
        total.launch(step)
        if step == 1:
            loads["first"].wait()
            lax.fori_loop(0, ranks, qkv_grads, 0)
            qkv_piece.first()
            out_piece.third()
            out_way.start()
        if step == 2:
            qkv_piece.second()
        if step == half - 1:
            qkv_piece.third()
            qkv_way.start()
    total.compute(half + 1)
    loads["dresid"].wait()
    total.arrive_last()
    gain_grad[...] = jnp.zeros_like(gain_grad)

    def last(at, _):
        begin = pl.multiple_of(at * 32, 32)
        rows_at = pl.ds(begin, 32)
        value = tokens[rows_at].astype(jnp.float32)
        normal, inv = rows_scaled(value)
        grad = total.last(begin, 32)
        tokens_grad[rows_at] = dresid[rows_at] + rows_scaled_back(value, inv, grad)
        gain_grad[...] += jnp.sum(grad * normal, 0, keepdims=True)
        return 0

    lax.fori_loop(0, local // 32, last, 0)
    lane = lax.broadcasted_iota(jnp.int32, (1, size), 1)
    per_row = size // own
    for number in range(ranks * copies):
        at = number // per_row
        first = gain_grad[:, at * size : (at + 1) * size]
        second = mlp_gain_part[:, at * size : (at + 1) * size]
        shift = number % per_row * own
        first = pltpu.roll(first, (size - shift) % size, 1) if shift else first
        second = pltpu.roll(second, (size + own - shift) % size, 1) if shift != own else second
        tile_at = tiles.at[number // copies, number % copies]
        tile_at[0:1] = jnp.where(lane < own, first, second)
        tile_at[1:2] = query_gain_grad[...]
        tile_at[2:3] = key_gain_grad[...]
        tile_at[3:] = jnp.zeros((tiles.shape[2] - 3, size), jnp.float32)

    def to_ranks(step):
        peer = lax.rem(seq + step, ranks)
        return push(tiles.at[peer], tiles_in.at[seq], sems[17].at[step], sems[18].at[step], (peer, dp))

    def to_copies(step):
        peer = lax.rem(dp + step, copies)
        return push(
            tile_sums.at[peer], tile_sums_in.at[dp], sems[19].at[step], sems[20].at[step], (seq, peer)
        )

    for step in range(1, ranks):
        to_ranks(step).start()
    tiles_in[seq] = tiles[seq]
    for step in range(1, ranks):
        to_ranks(step).wait_recv()
    tile_sums[...] = jnp.sum(tiles_in[...], 0)
    for step in range(1, copies):
        to_copies(step).start()
    tile_sums_in[dp] = tile_sums[dp]
    for step in range(1, copies):
        to_copies(step).wait_recv()
    gains[...] = jnp.sum(tile_sums_in[...], 0)
    for step in range(1, ranks):
        to_ranks(step).wait_send()
    for step in range(1, copies):
        to_copies(step).wait_send()
    ring.finish()
    total.finish()
    out_piece.finish()
    qkv_piece.finish()
    mlp_way.finish()
    out_way.finish()
    qkv_way.finish()


def leave_kernel(attn_sums, mlp_sums, gains, attn_gain, mlp_gain, *outs):
    own = attn_gain.shape[1]
    same = lax.broadcasted_iota(jnp.int32, (own, own), 0) == lax.broadcasted_iota(jnp.int32, (own, own), 1)

    def column(row):
        return jnp.sum(jnp.where(same, row, 0.0), 1, keepdims=True)

    first, second = column(attn_gain[...]), column(mlp_gain[...])
    for sums, parts in ((attn_sums, zip(outs[:4], (first, first, first, None))), (mlp_sums, zip(outs[4:7], (second, second, None)))):
        at = 0
        for out, gain in parts:
            value = sums[0, :, at : at + out.shape[1]].astype(jnp.float32)
            out[...] = value if gain is None else value * gain
            at += out.shape[1]
    outs[7][...] = gains[0:1, :own] / attn_gain[...]
    outs[8][...] = gains[0:1, own : 2 * own] / mlp_gain[...]


VM = pl.BlockSpec(memory_space=pltpu.VMEM)
SM = pl.BlockSpec(memory_space=pltpu.SMEM)
ANY = pl.BlockSpec(memory_space=pl.ANY)


def call(kernel, number, ins, outs, scratch, operands):
    return pl.pallas_call(
        kernel,
        out_shape=[jax.ShapeDtypeStruct(shape, dtype) for shape, dtype, _ in outs],
        in_specs=ins,
        out_specs=[spec for _, _, spec in outs],
        scratch_shapes=scratch,
        compiler_params=pltpu.CompilerParams(
            collective_id=number, has_side_effects=True, vmem_limit_bytes=LIMIT
        ),
    )(*operands)


def columns_body(
    tokens,
    out_grad,
    span_order,
    doc_starts,
    w_query,
    w_key,
    w_value,
    w_output,
    attn_gain,
    query_gain,
    key_gain,
    w_gate,
    w_up,
    w_down,
    mlp_gain,
):
    ranks = lax.axis_size("seq")
    copies = lax.axis_size("dp")
    _, local, width = tokens.shape
    rows = local * ranks
    size = query_gain.shape[0]
    kv_heads = w_key.shape[1] // size // ranks
    heads = w_query.shape[1] // size // ranks
    q_cols, kv_cols = heads * size, kv_heads * size
    qkv_cols = q_cols + 2 * kv_cols
    a_cols = qkv_cols + q_cols
    ff = w_gate.shape[1] // ranks
    own = width // (ranks * copies)
    deep = own * copies
    half = ranks // 2
    f32, i32 = jnp.float32, jnp.int32
    exponents = np.arange(size) % (size // 2) * (-2.0 / size * math.log(1000000.0))
    freqs = jnp.asarray(np.exp(exponents)[None], f32)
    first_in, qkv, attn_block, mlp_rows, cosv, sinv, pos, begins, pos_row = call(
        functools.partial(enter_kernel, ranks),
        1,
        [SM, SM] + [VM] * 8 + [ANY] * 3,
        [
            ((rows, width), LOW, ANY),
            ((rows, qkv_cols), f32, ANY),
            ((ranks, deep, a_cols), LOW, ANY),
            ((ranks, own, 3 * ff), LOW, ANY),
            ((rows, size), f32, VM),
            ((rows, size), f32, VM),
            ((rows, 1), i32, VM),
            ((rows, 1), i32, VM),
            ((1, rows), i32, VM),
        ],
        [
            pltpu.VMEM((rows, width), LOW),
            pltpu.VMEM((rows, width), LOW),
            pltpu.VMEM((rows, qkv_cols), f32),
            pltpu.VMEM((ranks, deep, a_cols), LOW),
            pltpu.VMEM((ranks, own, a_cols), LOW),
            pltpu.VMEM((ranks, own, 3 * ff), LOW),
        ]
        + [pltpu.VMEM((own, ff * ranks), LOW)] * 3
        + ring_sems(ranks)
        + spread_sems(ranks)
        + [pltpu.SemaphoreType.DMA((2 * half + 6,))],
        (
            span_order, doc_starts, tokens[0], freqs, attn_gain[None], mlp_gain[None], w_query, w_key, w_value,
            w_output, w_gate, w_up, w_down,
        ),
    )
    q_gain, k_gain = query_gain[None], key_gain[None]
    q_low, k_low, v_low, out_low, resid, second, dy_all, prob, mlp_block = call(
        functools.partial(attend_kernel, ranks, kv_heads),
        2,
        [VM] * 10 + [ANY] * 2,
        [
            ((heads, rows, size), LOW, VM),
            ((kv_heads, rows, size), LOW, VM),
            ((kv_heads, rows, size), LOW, VM),
            ((rows, q_cols), LOW, VM),
            ((local, width), f32, VM),
            ((local, width), LOW, VM),
            ((rows, width), LOW, ANY),
            ((heads, rows, rows), LOW, ANY),
            ((ranks, deep, 3 * ff), LOW, ANY),
        ],
        [
            pltpu.VMEM((rows, width), LOW),
            pltpu.VMEM((heads, rows, rows), LOW),
            pltpu.VMEM((ranks, deep, q_cols), LOW),
        ]
        + sum_bufs(local, ranks, width)
        + ring_sems(ranks) * 2
        + spread_sems(ranks) * 3
        + [pltpu.SemaphoreType.DMA((heads * half + 2,))],
        (
            out_grad[0], tokens[0], qkv, cosv, sinv, pos, begins, pos_row, q_gain, k_gain, attn_block, mlp_rows,
        ),
    )
    block_out, dresid, dresid_low, dgm, mlp_own = call(
        functools.partial(mlp_kernel, ranks),
        3,
        [VM, VM, ANY, ANY, ANY],
        [
            ((local, width), LOW, VM),
            ((local, width), f32, VM),
            ((local, width), LOW, VM),
            ((1, width), f32, VM),
            ((ranks, own, 3 * ff), LOW, VM),
        ],
        [pltpu.VMEM((ranks, deep, 3 * ff), LOW)]
        + reduce_bufs(ranks, own, 3 * ff)
        + [
            pltpu.VMEM((rows, width), LOW),
            pltpu.VMEM((ranks, deep, 3 * ff), LOW),
            pltpu.VMEM((rows, ff), LOW),
            pltpu.VMEM((rows, 2 * ff), LOW),
            pltpu.VMEM((local, width), f32),
            pltpu.VMEM((rows, width), LOW),
        ]
        + sum_bufs(local, ranks, width)
        + sum_bufs(local, ranks, width)[1:]
        + [pltpu.SemaphoreType.DMA((3,))]
        + ring_sems(ranks) * 3
        + reduce_sems() * 4,
        (second, out_grad[0], resid, dy_all, mlp_block),
    )
    tokens_grad, gains, mlp_sums, attn_sums = call(
        functools.partial(back_kernel, ranks, kv_heads),
        4,
        [VM] * 5 + [ANY] * 12,
        [
            ((local, width), f32, VM),
            ((8, size), f32, VM),
            ((ranks, own, 3 * ff), LOW, ANY),
            ((ranks, own, a_cols), LOW, VM),
        ],
        [pltpu.VMEM((ranks, deep, a_cols), LOW)]
        + reduce_bufs(ranks, own, a_cols)
        + [
            pltpu.VMEM((ranks, own, a_cols), LOW),
            pltpu.VMEM((1, width), f32),
            pltpu.VMEM((1, size), f32),
            pltpu.VMEM((1, size), f32),
            pltpu.VMEM((ranks, copies, 8, size), f32),
            pltpu.VMEM((ranks, copies, 8, size), f32),
            pltpu.VMEM((copies, 8, size), f32),
            pltpu.VMEM((copies, 8, size), f32),
            pltpu.VMEM((rows, width), LOW),
            pltpu.VMEM((rows, q_cols), LOW),
            pltpu.VMEM((kv_heads, rows, size), f32),
            pltpu.VMEM((kv_heads, rows, size), f32),
            pltpu.VMEM((rows, qkv_cols), LOW),
            pltpu.VMEM((rows, q_cols), LOW),
            pltpu.VMEM((rows, width), LOW),
            pltpu.VMEM((ranks, deep, a_cols), LOW),
            pltpu.VMEM((rows, qkv_cols), f32),
            pltpu.VMEM((rows, size), f32),
            pltpu.VMEM((rows, size), f32),
            pltpu.VMEM((heads, rows, size), LOW),
            pltpu.VMEM((kv_heads, rows, size), LOW),
            pltpu.VMEM((kv_heads, rows, size), LOW),
            pltpu.VMEM((heads, rows, rows), LOW),
            pltpu.VMEM((local, width), f32),
        ]
        + sum_bufs(local, ranks, width)
        + ring_sems(ranks) * 2
        + reduce_sems() * 2
        + deliver_sems(ranks) * 3
        + [pltpu.SemaphoreType.DMA((ranks,))] * 2
        + [pltpu.SemaphoreType.DMA((copies,))] * 2
        + [pltpu.SemaphoreType.DMA((11,))],
        (
            tokens[0], dresid_low, q_gain, k_gain, dgm, out_low, first_in, attn_block, qkv, cosv, sinv, q_low, k_low,
            v_low, prob, dresid, mlp_own,
        ),
    )
    whole = pl.BlockSpec((1, own), lambda at: (0, 0))
    each = (q_cols, kv_cols, kv_cols, q_cols, ff, ff, ff)
    *grads, dga, dgm = pl.pallas_call(
        leave_kernel,
        grid=(ranks,),
        out_shape=[jax.ShapeDtypeStruct((own, cols * ranks), f32) for cols in each]
        + [jax.ShapeDtypeStruct((1, own), f32)] * 2,
        in_specs=[
            pl.BlockSpec((1, own, a_cols), lambda at: (at, 0, 0)),
            pl.BlockSpec((1, own, 3 * ff), lambda at: (at, 0, 0)),
            pl.BlockSpec((8, size), lambda at: (0, 0)),
            whole,
            whole,
        ],
        out_specs=[pl.BlockSpec((own, cols), lambda at: (0, at)) for cols in each] + [whole, whole],
    )(attn_sums, mlp_sums, gains, attn_gain[None], mlp_gain[None])
    return (
        block_out[None], tokens_grad[None], *grads[:4], dga[0], gains[1], gains[2], *grads[4:], dgm[0],
    )


def body(*args):
    tokens, w_key, query_gain = args[0], args[5], args[9]
    groups = w_key.shape[1] // query_gain.shape[0]
    ranks = lax.axis_size("seq")
    if tokens.shape[0] == 1 and ranks % 2 == 0 and groups % ranks == 0 and lax.axis_size("dp") == 4:
        return columns_body(*args)
    return gathered_body(*args)


def solution(mesh):
    return jax.shard_map(
        body,
        mesh=mesh,
        in_specs=(
            P("dp", "seq", None),
            P("dp", "seq", None),
            P(),
            P("dp", None),
            P(("seq", "dp"), None),
            P(("seq", "dp"), None),
            P(("seq", "dp"), None),
            P(("seq", "dp"), None),
            P(("seq", "dp")),
            P(),
            P(),
            P(("seq", "dp"), None),
            P(("seq", "dp"), None),
            P(("seq", "dp"), None),
            P(("seq", "dp")),
        ),
        out_specs=(
            P("dp", "seq", None),
            P("dp", "seq", None),
            P(("seq", "dp"), None),
            P(("seq", "dp"), None),
            P(("seq", "dp"), None),
            P(("seq", "dp"), None),
            P(("seq", "dp")),
            P(),
            P(),
            P(("seq", "dp"), None),
            P(("seq", "dp"), None),
            P(("seq", "dp"), None),
            P(("seq", "dp")),
        ),
        check_vma=False,
    )
```

```python
import functools
import math

import jax
import jax.numpy as jnp
import numpy as np
from jax import lax
from jax.experimental import pallas as pl
from jax.experimental.pallas import tpu as pltpu
from jax.sharding import PartitionSpec as P

EPS = 1e-06
NEG = -1e30


def normed(v, gain):
    scale_inv = lax.rsqrt(jnp.mean(v * v, -1, keepdims=True) + EPS)
    return (v * scale_inv * gain, scale_inv)


def norm_back(v, scale_inv, gain, grad):
    scaled = grad * gain
    inner = jnp.mean(scaled * v, -1, keepdims=True)
    dv = scale_inv * scaled - v * scale_inv * scale_inv * scale_inv * inner
    dgain = jnp.sum((grad * v * scale_inv).reshape(-1, v.shape[-1]), 0)
    return (dv, dgain)


def rotary(pos, width):
    half = width // 2
    freqs = jnp.exp(jnp.arange(half, dtype=jnp.float32) * (-2.0 / width * math.log(1000000.0)))
    angle = pos.astype(jnp.float32)[:, None] * freqs[None, :]
    return (jnp.cos(angle)[:, None, :], jnp.sin(angle)[:, None, :])


def rotate(v, cosv, sinv):
    half = v.shape[-1] // 2
    first, second = (v[..., :half], v[..., half:])
    return jnp.concatenate([first * cosv - second * sinv, second * cosv + first * sinv], -1)


def rotate_back(grad, cosv, sinv):
    half = grad.shape[-1] // 2
    first, second = (grad[..., :half], grad[..., half:])
    return jnp.concatenate([first * cosv + second * sinv, second * cosv - first * sinv], -1)


def place(order, begin, count, span):
    rows = begin + jnp.arange(count, dtype=jnp.int32)
    slots = rows // span
    picked = slots[:, None] == jnp.arange(order.shape[0], dtype=jnp.int32)[None, :]
    return jnp.sum(jnp.where(picked, order[None, :], 0), -1) * span + rows % span


def doc_of(starts, pos):
    return jnp.sum((starts[:, None, :] <= pos[None, :, None]).astype(jnp.int32), -1)


def gathered_body(
    tokens,
    out_grad,
    span_order,
    doc_starts,
    w_query,
    w_key,
    w_value,
    w_output,
    attn_gain,
    query_gain,
    key_gain,
    w_gate,
    w_up,
    w_down,
    mlp_gain,
):
    seqs, local, width = tokens.shape
    span = local // 2
    head_size = query_gain.shape[0]
    kv_heads = w_key.shape[1] // head_size
    heads = w_query.shape[1] // head_size
    share = heads // kv_heads
    kv_width = kv_heads * head_size
    ff_width = w_gate.shape[1]
    scale = 1.0 / math.sqrt(head_size)
    total_rows = seqs * local
    own_rows = width // lax.axis_size(("seq", "dp"))
    qpos = place(span_order, lax.axis_index("seq") * local, local, span)
    qdoc = doc_of(doc_starts, qpos)
    cosv, sinv = rotary(qpos, head_size)

    def gather_attn():
        return (
            lax.all_gather(w_query, ("seq", "dp"), axis=0, tiled=True),
            lax.all_gather(w_key, ("seq", "dp"), axis=0, tiled=True),
            lax.all_gather(w_value, ("seq", "dp"), axis=0, tiled=True),
            lax.all_gather(w_output, ("seq", "dp"), axis=0, tiled=True),
            lax.all_gather(
                attn_gain.astype(jnp.bfloat16), ("seq", "dp"), axis=0, tiled=True
            ).astype(attn_gain.dtype),
        )

    def gather_mlp():
        return (
            lax.all_gather(w_gate, ("seq", "dp"), axis=0, tiled=True),
            lax.all_gather(w_up, ("seq", "dp"), axis=0, tiled=True),
            lax.all_gather(w_down, ("seq", "dp"), axis=0, tiled=True),
            lax.all_gather(mlp_gain.astype(jnp.bfloat16), ("seq", "dp"), axis=0, tiled=True).astype(
                mlp_gain.dtype
            ),
        )

    x_rows = tokens.astype(jnp.float32).reshape(total_rows, width)
    wq_all, wk_all, wv_all, wo_all, ga_all = gather_attn()
    first_norm, first_inv = normed(x_rows, ga_all)
    first_in = first_norm.astype(jnp.bfloat16)
    q_raw = jnp.dot(first_in, wq_all, preferred_element_type=jnp.float32).reshape(
        seqs, local, heads, head_size
    )
    k_raw = jnp.dot(first_in, wk_all, preferred_element_type=jnp.float32).reshape(
        seqs, local, kv_heads, head_size
    )
    v_low = (
        jnp.dot(first_in, wv_all, preferred_element_type=jnp.float32)
        .astype(jnp.bfloat16)
        .reshape(seqs, local, kv_heads, head_size)
    )
    q_normed, q_inv = normed(q_raw, query_gain)
    k_normed, k_inv = normed(k_raw, key_gain)
    q_low = rotate(q_normed, cosv, sinv).astype(jnp.bfloat16)
    k_low = rotate(k_normed, cosv, sinv).astype(jnp.bfloat16)
    q_group = q_low.reshape(seqs, local, kv_heads, share, head_size)

    def scores(piece_key, start):
        count = piece_key.shape[1]
        kpos = place(span_order, start, count, span)
        kdoc = doc_of(doc_starts, kpos)
        visible = (qdoc[:, :, None] == kdoc[:, None, :]) & (
            kpos[None, None, :] <= qpos[None, :, None]
        )
        raw = (
            jnp.einsum("sqgjd,skgd->sgjqk", q_group, piece_key, preferred_element_type=jnp.float32)
            * scale
        )
        return (raw, visible[:, None, None])

    start_top = jnp.full((seqs, kv_heads, share, local), NEG, jnp.float32)
    piece = (
        lax.all_gather(k_low, "seq", axis=1, tiled=True),
        lax.all_gather(v_low, "seq", axis=1, tiled=True),
    )
    top = start_top
    raw, visible = scores(piece[0], jnp.int32(0))
    raw = jnp.where(visible, raw, NEG)
    new_top = jnp.maximum(top, jnp.max(raw, -1))
    weights = jnp.where(visible, jnp.exp(raw - new_top[..., None]), 0.0)
    total = jnp.sum(weights, -1)
    summed = jnp.einsum(
        "sgjqk,skgd->sgjqd",
        weights.astype(jnp.bfloat16),
        piece[1],
        preferred_element_type=jnp.float32,
    )
    top, total, summed = (new_top, total, summed)
    log_total = top + jnp.log(total)
    attn_vals = summed / total[..., None]
    out_low = (
        jnp.transpose(attn_vals, (0, 3, 1, 2, 4))
        .reshape(total_rows, heads * head_size)
        .astype(jnp.bfloat16)
    )
    resid = x_rows + jnp.einsum("nh,dh->nd", out_low, wo_all, preferred_element_type=jnp.float32)
    wg_all, wu_all, wd_all, gm_all = gather_mlp()
    second_norm, second_inv = normed(resid, gm_all)
    second_in = second_norm.astype(jnp.bfloat16)
    gate = jnp.dot(second_in, wg_all, preferred_element_type=jnp.float32)
    upper = jnp.dot(second_in, wu_all, preferred_element_type=jnp.float32)
    sigma = jax.nn.sigmoid(gate)
    act = gate * sigma
    hidden = (act * upper).astype(jnp.bfloat16)
    result = resid + jnp.einsum("nf,df->nd", hidden, wd_all, preferred_element_type=jnp.float32)
    block_out = result.astype(jnp.bfloat16).reshape(seqs, local, width)
    grad_low = out_grad.reshape(total_rows, width)
    wg_all, wu_all, wd_all, gm_all = gather_mlp()
    dmid = jnp.einsum("nd,df->nf", grad_low, wd_all, preferred_element_type=jnp.float32)
    dgate = (dmid * upper * sigma * (1.0 + gate * (1.0 - sigma))).astype(jnp.bfloat16)
    dupper = (dmid * act).astype(jnp.bfloat16)
    left = second_in
    outer = grad_low
    mlp_sums = lax.psum_scatter(
        jnp.concatenate(
            [
                jnp.einsum("nd,nf->df", left, dgate, preferred_element_type=jnp.float32),
                jnp.einsum("nd,nf->df", left, dupper, preferred_element_type=jnp.float32),
                jnp.einsum("nd,nf->df", outer, hidden, preferred_element_type=jnp.float32),
            ],
            1,
        ),
        ("seq", "dp"),
        scatter_dimension=0,
        tiled=True,
    )
    dsecond = jnp.einsum(
        "nf,df->nd", dgate, wg_all, preferred_element_type=jnp.float32
    ) + jnp.einsum("nf,df->nd", dupper, wu_all, preferred_element_type=jnp.float32)
    dresid_norm, dgm = norm_back(resid, second_inv, gm_all, dsecond)
    dresid = grad_low.astype(jnp.float32) + dresid_norm
    dresid_low = dresid.astype(jnp.bfloat16)
    wq_all, wk_all, wv_all, wo_all, ga_all = gather_attn()
    dout_low = jnp.einsum(
        "nd,dh->nh", dresid_low, wo_all, preferred_element_type=jnp.float32
    ).astype(jnp.bfloat16)
    dout_group = dout_low.reshape(seqs, local, kv_heads, share, head_size)
    delta = jnp.sum(jnp.transpose(dout_group.astype(jnp.float32), (0, 2, 3, 1, 4)) * attn_vals, -1)
    piece = (
        lax.all_gather(k_low, "seq", axis=1, tiled=True),
        lax.all_gather(v_low, "seq", axis=1, tiled=True),
    )
    count = piece[0].shape[1]
    raw, visible = scores(piece[0], jnp.int32(0))
    prob = jnp.where(visible, jnp.exp(raw - log_total[..., None]), 0.0)
    dprob = jnp.einsum(
        "sqgjd,skgd->sgjqk", dout_group, piece[1], preferred_element_type=jnp.float32
    )
    dscore = (prob * (dprob - delta[..., None])).astype(jnp.bfloat16)
    dq_sum = jnp.einsum("sgjqk,skgd->sqgjd", dscore, piece[0], preferred_element_type=jnp.float32)
    dk_part = (
        jnp.einsum("sgjqk,sqgjd->skgd", dscore, q_group, preferred_element_type=jnp.float32) * scale
    )
    dv_part = jnp.einsum(
        "sgjqk,sqgjd->skgd",
        prob.astype(jnp.bfloat16),
        dout_group,
        preferred_element_type=jnp.float32,
    )
    joined = jnp.concatenate(
        [dk_part.reshape(seqs, count, kv_width), dv_part.reshape(seqs, count, kv_width)], -1
    )
    buffer = joined
    dq_sum, buffer = (dq_sum, buffer)
    key_sums = lax.psum_scatter(
        buffer.astype(jnp.bfloat16), "seq", scatter_dimension=1, tiled=True
    ).astype(jnp.float32)
    dq_rot = (dq_sum * scale).reshape(seqs, local, heads, head_size)
    dq_raw, dgq = norm_back(q_raw, q_inv, query_gain, rotate_back(dq_rot, cosv, sinv))
    dk_rot = key_sums[..., :kv_width].reshape(seqs, local, kv_heads, head_size)
    dk_raw, dgk = norm_back(k_raw, k_inv, key_gain, rotate_back(dk_rot, cosv, sinv))
    dq_low = dq_raw.reshape(total_rows, heads * head_size).astype(jnp.bfloat16)
    dk_low = dk_raw.reshape(total_rows, kv_width).astype(jnp.bfloat16)
    dv_low = key_sums[..., kv_width:].reshape(total_rows, kv_width).astype(jnp.bfloat16)
    left = first_in
    outer = dresid_low
    attn_sums = lax.psum_scatter(
        jnp.concatenate(
            [
                jnp.einsum("nd,nh->dh", left, dq_low, preferred_element_type=jnp.float32),
                jnp.einsum("nd,nh->dh", left, dk_low, preferred_element_type=jnp.float32),
                jnp.einsum("nd,nh->dh", left, dv_low, preferred_element_type=jnp.float32),
                jnp.einsum("nd,nh->dh", outer, out_low, preferred_element_type=jnp.float32),
            ],
            1,
        ),
        ("seq", "dp"),
        scatter_dimension=0,
        tiled=True,
    )
    dfirst = jnp.einsum("nh,dh->nd", dq_low, wq_all, preferred_element_type=jnp.float32)
    dfirst = dfirst + jnp.einsum("nh,dh->nd", dk_low, wk_all, preferred_element_type=jnp.float32)
    dfirst = dfirst + jnp.einsum("nh,dh->nd", dv_low, wv_all, preferred_element_type=jnp.float32)
    dx_norm, dga = norm_back(x_rows, first_inv, ga_all, dfirst)
    tokens_grad = (dresid + dx_norm).reshape(seqs, local, width)
    dga_all, dgm_all, dgq_all, dgk_all = lax.psum((dga, dgm, dgq, dgk), ("seq", "dp"))
    offset = lax.axis_index(("seq", "dp")) * own_rows
    attn_gain_grad = lax.dynamic_slice_in_dim(dga_all, offset, own_rows, 0)
    mlp_gain_grad = lax.dynamic_slice_in_dim(dgm_all, offset, own_rows, 0)
    q_cols = heads * head_size
    w_query_grad = attn_sums[:, :q_cols]
    w_key_grad = attn_sums[:, q_cols : q_cols + kv_width]
    w_value_grad = attn_sums[:, q_cols + kv_width : q_cols + 2 * kv_width]
    w_output_grad = attn_sums[:, q_cols + 2 * kv_width :]
    w_gate_grad = mlp_sums[:, :ff_width]
    w_up_grad = mlp_sums[:, ff_width : 2 * ff_width]
    w_down_grad = mlp_sums[:, 2 * ff_width :]
    return (
        block_out,
        tokens_grad,
        w_query_grad,
        w_key_grad,
        w_value_grad,
        w_output_grad,
        attn_gain_grad,
        dgq_all,
        dgk_all,
        w_gate_grad,
        w_up_grad,
        w_down_grad,
        mlp_gain_grad,
    )


LOW = jnp.bfloat16
MESH = pl.DeviceIdType.MESH
LIMIT = 60 * 2**20


def ring_order(ranks):
    half = ranks // 2
    order = [0]
    for step in range(1, half):
        order += [step, ranks - step]
    return order + [half]


def ring_place(seq, ranks):
    z, x = lax.div(seq, 2), lax.rem(seq, 2)
    return z + x * (ranks - 1 - 2 * z)


def ring_seq(place, ranks):
    half = ranks // 2
    x, z = lax.div(place, half), lax.rem(place, half)
    return 2 * (z + x * (half - 1 - 2 * z)) + x


def neighbours(ranks):
    seq, dp = lax.axis_index("seq"), lax.axis_index("dp")
    at = ring_place(seq, ranks)
    right = ring_seq(lax.rem(at + 1, ranks), ranks)
    left = ring_seq(lax.rem(at + ranks - 1, ranks), ranks)
    return (right, dp), (left, dp)


def knock(devices):
    barrier = pltpu.get_barrier_semaphore()
    for device in devices:
        pl.semaphore_signal(barrier, inc=1, device_id=device, device_id_type=MESH)


def answered(devices):
    pl.semaphore_wait(pltpu.get_barrier_semaphore(), len(devices))


def move(src, dst, sem):
    copy = pltpu.make_async_copy(src, dst, sem)
    copy.start()
    return copy


def push(src, dst, send, recv, device):
    return pltpu.make_async_remote_copy(
        src_ref=src, dst_ref=dst, send_sem=send, recv_sem=recv, device_id=device, device_id_type=MESH
    )


def dot_nn(left, right):
    return jnp.dot(left, right, preferred_element_type=jnp.float32)


def dot_nt(left, right):
    return lax.dot_general(left, right, (((1,), (1,)), ((), ())), preferred_element_type=jnp.float32)


def dot_tn(left, right):
    return lax.dot_general(left, right, (((0,), (0,)), ((), ())), preferred_element_type=jnp.float32)


class RingGather:
    def __init__(self, buf, local, ranks, send, recv, right, left):
        self.buf, self.local, self.half = buf, local, ranks // 2
        self.send, self.recv, self.right, self.left = send, recv, right, left
        self.row = {rel: at * local for at, rel in enumerate(ring_order(ranks))}
        self.ranks = ranks

    def copies(self, step):
        last = step == self.half
        rows = self.local // 2 if last else self.local
        skip = self.local // 2 if last else 0
        pairs = (
            ((self.ranks - step + 1) % self.ranks, self.ranks - step, 0, self.right),
            (step - 1, step, skip, self.left),
        )
        return [
            push(
                self.buf.at[pl.ds(self.row[src] + begin, rows)],
                self.buf.at[pl.ds(self.row[dst] + begin, rows)],
                self.send.at[way, step - 1],
                self.recv.at[way, step - 1],
                device,
            )
            for way, (src, dst, begin, device) in enumerate(pairs)
        ]

    def start(self, step):
        for copy in self.copies(step):
            copy.start()

    def arrive(self, step):
        for copy in self.copies(step):
            copy.wait_recv()

    def finish(self):
        for step in range(1, self.half + 1):
            for copy in self.copies(step):
                copy.wait_send()

    def rows(self, step):
        if step == 0:
            return 0, self.local
        if step == self.half:
            return self.row[self.half], self.local
        return self.row[step], 2 * self.local


class RingSum:
    def __init__(self, part, term, out_buf, in_buf, local, ranks, send, recv, right, left):
        self.part, self.term, self.out_buf, self.in_buf = part, term, out_buf, in_buf
        self.local, self.ranks, self.half = local, ranks, ranks // 2
        self.send, self.recv, self.right, self.left = send, recv, right, left
        self.row = {rel: at * local for at, rel in enumerate(ring_order(ranks))}

    def copies(self, step):
        rows = self.local // 2 if step == 1 else self.local
        skip = self.local // 2 if step == 1 else 0
        return [
            push(
                self.out_buf.at[way, (step - 1) % 2, pl.ds(begin, rows)],
                self.in_buf.at[way, step - 1, pl.ds(begin, rows)],
                self.send.at[way, step - 1],
                self.recv.at[way, step - 1],
                device,
            )
            for way, begin, device in ((0, 0, self.right), (1, skip, self.left))
        ]

    def compute(self, step):
        if step == 1:
            self.part(self.row[self.half], self.local)
        elif step <= self.half:
            self.part(self.row[self.half + 1 - step], 2 * self.local)
        else:
            self.part(0, self.local)

    def launch(self, step):
        local, skip = self.local, self.local // 2
        if step > 2:
            for copy in self.copies(step - 2):
                copy.wait_send()
        if step == 1:
            self.out_buf[0, 0, :skip] = self.term[:skip].astype(LOW)
            self.out_buf[1, 0, skip:] = self.term[skip:local].astype(LOW)
        else:
            for copy in self.copies(step - 1):
                copy.wait_recv()
            for way in range(2):
                for begin, with_sum in ((0, step > 2 or way == 0), (skip, step > 2 or way == 1)):
                    value = self.term[pl.ds(way * local + begin, skip)]
                    if with_sum:
                        value = value + self.in_buf[way, step - 2, pl.ds(begin, skip)].astype(jnp.float32)
                    self.out_buf[way, (step - 1) % 2, pl.ds(begin, skip)] = value.astype(LOW)
        for copy in self.copies(step):
            copy.start()

    def last(self, begin, count):
        rows = pl.ds(begin, count)
        value = self.term[rows] + self.in_buf[0, self.half - 1, rows].astype(jnp.float32)
        return value + self.in_buf[1, self.half - 1, rows].astype(jnp.float32)

    def arrive_last(self):
        for copy in self.copies(self.half):
            copy.wait_recv()

    def finish(self):
        for step in range(max(1, self.half - 1), self.half + 1):
            for copy in self.copies(step):
                copy.wait_send()


def ring_sems(ranks):
    return [pltpu.SemaphoreType.DMA((2, ranks // 2)), pltpu.SemaphoreType.DMA((2, ranks // 2))]


def sum_bufs(local, ranks, width):
    return [
        pltpu.VMEM((2 * local, width), jnp.float32),
        pltpu.VMEM((2, 2, local, width), LOW),
        pltpu.VMEM((2, ranks // 2, local, width), LOW),
    ]


def turn(v):
    return pltpu.roll(v, v.shape[-1] // 2, v.ndim - 1)


def rows_scaled(v):
    inv = lax.rsqrt(jnp.mean(v * v, -1, keepdims=True) + EPS)
    return v * inv, inv


def rows_scaled_back(v, inv, grad):
    return inv * grad - v * (inv * inv * inv * jnp.mean(grad * v, -1, keepdims=True))


class Spread:
    def __init__(self, rows, block, ranks, own, cols, sems):
        self.rows, self.block, self.ranks, self.own, self.cols = rows, block, ranks, own, cols
        self.send, self.recv, self.hop_send, self.hop_recv, self.here = sems
        self.seq, self.dp = lax.axis_index("seq"), lax.axis_index("dp")
        y, core = lax.div(self.dp, 2), lax.rem(self.dp, 2)
        self.beside, self.sibling = (1 - y) * 2 + core, y * 2 + 1 - core

    def at(self, dp):
        return pl.ds(pl.multiple_of(dp * self.own, self.own), self.own)

    def exchange(self):
        for step in range(1, self.ranks):
            peer = lax.rem(self.seq + step, self.ranks)
            yield push(
                self.rows.at[peer, :, self.cols],
                self.block.at[self.seq, self.at(self.dp), self.cols],
                self.send.at[step],
                self.recv.at[step],
                (peer, self.dp),
            )

    def keep(self):
        return pltpu.make_async_copy(
            self.rows.at[self.seq, :, self.cols],
            self.block.at[self.seq, self.at(self.dp), self.cols],
            self.here,
        )

    def hop(self, number):
        dp = self.beside if number == 2 else self.dp
        part = self.block.at[:, self.at(dp), self.cols]
        to = self.beside if number == 0 else self.sibling
        return push(part, part, self.hop_send.at[number], self.hop_recv.at[number], (self.seq, to))

    def start(self):
        self.keep().start()
        for copy in self.exchange():
            copy.start()

    def arrive(self):
        self.keep().wait()
        for copy in self.exchange():
            copy.wait_recv()

    def finish(self):
        for copy in self.exchange():
            copy.wait_send()
        for number in range(3):
            self.hop(number).wait_send()


def spread_sems(ranks):
    return [
        pltpu.SemaphoreType.DMA((ranks,)),
        pltpu.SemaphoreType.DMA((ranks,)),
        pltpu.SemaphoreType.DMA((3,)),
        pltpu.SemaphoreType.DMA((3,)),
        pltpu.SemaphoreType.DMA,
    ]


class WholeGather:
    def __init__(self, block, ranks, own, sems):
        self.block, self.ranks, self.half, self.own = block, ranks, ranks // 2, own
        self.send, self.recv, self.y_send, self.y_recv, self.core_send, self.core_recv = sems
        self.seq, self.dp = lax.axis_index("seq"), lax.axis_index("dp")
        self.right, self.left = neighbours(ranks)
        self.place = ring_place(self.seq, ranks)
        y, core = lax.div(self.dp, 2), lax.rem(self.dp, 2)
        self.beside, self.sibling = (1 - y) * 2 + core, y * 2 + 1 - core

    def at(self, rel, dp, begin, count):
        seq = ring_seq(lax.rem(self.place + rel + self.ranks, self.ranks), self.ranks)
        return self.block.at[seq, pl.ds(pl.multiple_of(dp * self.own + begin, count), count)]

    def copies(self, step):
        last = step == self.half
        rows = self.own // 2 if last else self.own
        skip = self.own // 2 if last else 0
        given = []
        for way, rel, begin, device in ((0, 1 - step, 0, self.right), (1, step - 1, skip, self.left)):
            part = self.at(rel, self.dp, begin, rows)
            given.append(push(part, part, self.send.at[way, step - 1], self.recv.at[way, step - 1], device))
        return given

    def start(self, step):
        for copy in self.copies(step):
            copy.start()

    def hops(self, step):
        for at, rel in enumerate(ring_order(self.ranks)):
            if min(rel, self.ranks - rel) == step:
                part = self.at(rel, self.dp, 0, self.own)
                yield push(part, part, self.y_send.at[at], self.y_recv.at[at], (self.seq, self.beside))
                yield push(part, part, self.core_send.at[at], self.core_recv.at[at], (self.seq, self.sibling))

    def arrive(self, step):
        for copy in self.copies(step):
            copy.wait_recv()

    def forward(self, step):
        for copy in self.hops(step):
            copy.start()

    def cross(self):
        part = self.block.at[:, pl.ds(pl.multiple_of(self.beside * self.own, self.own), self.own)]
        at = self.ranks
        return push(part, part, self.core_send.at[at], self.core_recv.at[at], (self.seq, self.sibling))

    def complete(self):
        for step in range(self.half + 1):
            for copy in self.hops(step):
                copy.wait_recv()
        self.cross().start()
        self.cross().wait_recv()

    def finish(self):
        for step in range(1, self.half + 1):
            for copy in self.copies(step):
                copy.wait_send()
        for step in range(self.half + 1):
            for copy in self.hops(step):
                copy.wait_send()
        self.cross().wait_send()


def whole_sems(ranks):
    return (
        ring_sems(ranks)
        + [pltpu.SemaphoreType.DMA((ranks,))] * 2
        + [pltpu.SemaphoreType.DMA((ranks + 1,))] * 2
    )


class Reduce:
    def __init__(self, grads, from_core, from_y, total, own, first, count, cols, sems):
        self.grads, self.from_core, self.from_y, self.total = grads, from_core, from_y, total
        self.own, self.begin, self.count, self.cols = own, first, count, cols
        self.send, self.recv = sems
        self.seq, dp = lax.axis_index("seq"), lax.axis_index("dp")
        self.y, self.core = lax.div(dp, 2), lax.rem(dp, 2)
        self.beside, self.sibling = (1 - self.y) * 2 + self.core, self.y * 2 + 1 - self.core

    def at(self, y, core):
        return pl.ds(pl.multiple_of((y * 2 + core) * self.own, self.own), self.own)

    def hop(self, number):
        some, cols = pl.ds(self.begin, self.count), self.cols
        if number == 2:
            src, dst, to = self.from_core.at[0, some, :, cols], self.from_y.at[some, :, cols], self.beside
        else:
            rows = self.at(1 - self.y if number == 0 else self.y, 1 - self.core)
            src, dst, to = self.grads.at[some, rows, cols], self.from_core.at[number, some, :, cols], self.sibling
        return push(src, dst, self.send.at[number], self.recv.at[number], (self.seq, to))

    def first(self):
        self.hop(0).start()
        self.hop(1).start()

    def second(self):
        self.hop(0).wait_recv()
        rows = self.at(1 - self.y, self.core)

        def some(at, _):
            value = self.grads[at, rows, self.cols].astype(jnp.float32)
            value = value + self.from_core[0, at, :, self.cols].astype(jnp.float32)
            self.from_core[0, at, :, self.cols] = value.astype(LOW)
            return 0

        lax.fori_loop(self.begin, self.begin + self.count, some, 0)
        self.hop(2).start()

    def third(self):
        self.hop(1).wait_recv()
        self.hop(2).wait_recv()
        rows = self.at(self.y, self.core)

        def some(at, _):
            value = self.grads[at, rows, self.cols].astype(jnp.float32)
            value = value + self.from_core[1, at, :, self.cols].astype(jnp.float32)
            value = value + self.from_y[at, :, self.cols].astype(jnp.float32)
            self.total[at, :, self.cols] = value.astype(LOW)
            return 0

        lax.fori_loop(self.begin, self.begin + self.count, some, 0)

    def finish(self):
        for number in range(3):
            self.hop(number).wait_send()


def reduce_sems():
    return [pltpu.SemaphoreType.DMA((3,)), pltpu.SemaphoreType.DMA((3,))]


def reduce_bufs(ranks, own, cols):
    return [pltpu.VMEM((2, ranks, own, cols), LOW), pltpu.VMEM((ranks, own, cols), LOW)]


class Deliver:
    def __init__(self, rows, out, cols, ranks, sems):
        self.rows, self.out, self.cols, self.ranks = rows, out, cols, ranks
        self.send, self.recv, self.here = sems
        self.seq, self.dp = lax.axis_index("seq"), lax.axis_index("dp")

    def exchange(self):
        for step in range(1, self.ranks):
            peer = lax.rem(self.seq + step, self.ranks)
            yield push(
                self.rows.at[peer, :, self.cols],
                self.out.at[self.seq, :, self.cols],
                self.send.at[step],
                self.recv.at[step],
                (peer, self.dp),
            )

    def keep(self):
        return pltpu.make_async_copy(
            self.rows.at[self.seq, :, self.cols], self.out.at[self.seq, :, self.cols], self.here
        )

    def start(self):
        self.keep().start()
        for copy in self.exchange():
            copy.start()

    def finish(self):
        self.keep().wait()
        for copy in self.exchange():
            copy.wait_recv()
        for copy in self.exchange():
            copy.wait_send()


def deliver_sems(ranks):
    return [pltpu.SemaphoreType.DMA((ranks,)), pltpu.SemaphoreType.DMA((ranks,)), pltpu.SemaphoreType.DMA]


def enter_kernel(
    ranks, order, starts, tokens, freqs, attn_gain, mlp_gain, w_query, w_key, w_value, w_gate, w_up, w_down,
    first_in, qkv, attn_block, mlp_rows, cosv, sinv, pos, begins, pos_row,
    held, normal, kept, block, a_rows, m_rows, gate, up, down, *sems,
):
    local, width = tokens.shape
    own = w_query.shape[0]
    size = freqs.shape[1]
    cols = qkv.shape[1]
    half = ranks // 2
    local_sems = sems[7]
    seq, dp = lax.axis_index("seq"), lax.axis_index("dp")
    right, left = neighbours(ranks)
    attn = Spread(a_rows, block, ranks, own, pl.ds(0, a_rows.shape[2]), sems[2:7])
    peers = [(lax.rem(seq + step, ranks), dp) for step in range(1, ranks)]
    peers += [(seq, attn.beside), (seq, attn.sibling)]
    knock(peers)
    loads = [
        move(src, dst, local_sems.at[at])
        for at, (src, dst) in enumerate(((w_gate, gate), (w_up, up), (w_down, down)))
    ]
    held[:local] = tokens[...]

    def column(row):
        same = lax.broadcasted_iota(jnp.int32, (own, own), 0) == lax.broadcasted_iota(jnp.int32, (own, own), 1)
        return jnp.sum(jnp.where(same, row, 0.0), 1, keepdims=True)

    def lay(target, first, weight, gain):
        each = weight.shape[1] // ranks
        for rank in range(ranks):
            part = weight[:, rank * each : (rank + 1) * each]
            if gain is not None:
                part = (part.astype(jnp.float32) * gain).astype(LOW)
            target[rank, :, first : first + each] = part
        return first + each

    gain = column(attn_gain[...])
    at = 0
    for weight in (w_query, w_key, w_value):
        at = lay(a_rows, at, weight, gain)
    answered(peers)
    ring = RingGather(held, local, ranks, sems[0], sems[1], right, left)
    ring.start(1)
    attn.start()
    stores = []

    def scale_rows(begin, count):
        def some(at, _):
            rows = pl.ds(pl.multiple_of(begin + at * 32, 32), 32)
            normal[rows] = rows_scaled(held[rows].astype(jnp.float32))[0].astype(LOW)
            return 0

        lax.fori_loop(0, count // 32, some, 0)
        rows = pl.ds(begin, count)
        stores.append(move(normal.at[rows], first_in.at[rows], local_sems.at[len(stores)]))

    def project(begin, count):
        rows = pl.ds(begin, count)
        weight = block[...].reshape(width, cols)
        kept[rows] = dot_nn(normal[rows], weight)
        stores.append(move(kept.at[rows], qkv.at[rows], local_sems.at[len(stores)]))

    for load in loads:
        load.wait()
    gain = column(mlp_gain[...])
    each = gate.shape[1] // ranks
    lay(m_rows, 0, gate, gain)
    lay(m_rows, each, up, gain)
    lay(m_rows, 2 * each, down, None)
    stores.append(move(m_rows, mlp_rows, local_sems.at[len(stores)]))
    scale_rows(*ring.rows(0))
    ring.arrive(1)
    ring.start(2)
    scale_rows(*ring.rows(1))
    attn.arrive()
    attn.hop(0).start()
    attn.hop(1).start()
    spans = order.shape[0]
    span = local * ranks // spans
    place = ring_place(seq, ranks)
    for at, rel in enumerate(ring_order(ranks)):
        rows = pl.ds(at * local, local)
        owner = ring_seq(lax.rem(place + rel, ranks), ranks)
        ids = owner * local + lax.broadcasted_iota(jnp.int32, (1, local), 1)
        where = jnp.zeros_like(ids)
        for slot in range(spans):
            inside = (ids >= slot * span) & (ids < (slot + 1) * span)
            where = where + jnp.where(inside, ids + (order[slot] - slot) * span, 0)
        first = jnp.zeros_like(ids)
        for doc in range(starts.shape[1]):
            first = jnp.maximum(first, jnp.where(starts[0, doc] <= where, starts[0, doc], 0))
        pos_row[:, rows] = where
        across = jnp.broadcast_to(where, (local, local)).T
        pos[rows] = across[:, :1]
        begins[rows] = jnp.broadcast_to(first, (local, local)).T[:, :1]
        angle = across[:, :1].astype(jnp.float32) * freqs[...]
        lane = lax.broadcasted_iota(jnp.int32, (local, size), 1)
        cosv[rows] = jnp.cos(angle)
        sine = jnp.sin(angle)
        sinv[rows] = jnp.where(lane < size // 2, -sine, sine)
    ring.arrive(2)
    ring.start(3)
    scale_rows(*ring.rows(2))
    attn.hop(0).wait_recv()
    attn.hop(2).start()
    for step in range(3, half):
        ring.arrive(step)
        ring.start(step + 1)
        scale_rows(*ring.rows(step))
    attn.hop(1).wait_recv()
    attn.hop(2).wait_recv()
    stores.append(move(block, attn_block, local_sems.at[len(stores)]))
    for step in range(half):
        project(*ring.rows(step))
    ring.arrive(half)
    scale_rows(*ring.rows(half))
    project(*ring.rows(half))
    ring.finish()
    attn.finish()
    for store in stores:
        store.wait()


def attend_kernel(
    ranks, kv_heads, out_grad, tokens, qkv, cosv, sinv, pos, begins, pos_row, query_gain, key_gain, out_rows,
    mlp_rows, q_low, k_low, v_low, own_out, resid, second, dy_all, prob, mlp_block, w_output,
    dys, probs, out_low, whole, *sems,
):
    local, width = tokens.shape
    rows = local * ranks
    size = cosv.shape[1]
    heads = q_low.shape[0]
    share = heads // kv_heads
    half = ranks // 2
    scale = 1.0 / math.sqrt(size)
    o_cols = heads * size
    deep = whole.shape[1]
    right, left = neighbours(ranks)
    seq, dp = lax.axis_index("seq"), lax.axis_index("dp")
    own = mlp_rows.shape[1]
    third = mlp_rows.shape[2] // 3
    mlp = [
        Spread(mlp_rows, mlp_block, ranks, own, pl.ds(at * third, third), sems[8 + 5 * at : 13 + 5 * at])
        for at in range(3)
    ]
    local_sems = sems[23]
    out_send, out_recv = sems[24:]
    peers = [(lax.rem(seq + step, ranks), dp) for step in range(1, ranks)]
    peers += [(seq, mlp[0].beside), (seq, mlp[0].sibling)]
    knock(peers)
    dys[:local] = out_grad[...]
    whole[seq, pl.ds(pl.multiple_of(dp * own, own), own)] = out_rows[...]
    answered(peers)
    ring = RingGather(dys, local, ranks, sems[0], sems[1], right, left)
    outs = WholeGather(whole, ranks, own, sems[2:8])
    outs.start(1)
    outs.forward(0)
    for piece in mlp:
        piece.start()
    ring.start(1)
    tile = rows // half
    stores = []

    def rotated(at, rows_at, gain):
        v = rows_scaled(qkv[rows_at, at * size : (at + 1) * size])[0] * gain[...]
        return (v * cosv[rows_at] + turn(v) * sinv[rows_at]).astype(LOW)

    for piece in range(half):
        rows_at = pl.ds(piece * tile, tile)
        for head in range(heads):
            q_low[head, rows_at] = rotated(head, rows_at, query_gain)
        for group in range(kv_heads):
            k_low[group, rows_at] = rotated(heads + group, rows_at, key_gain)
            at = (heads + kv_heads + group) * size
            v_low[group, rows_at] = qkv[rows_at, at : at + size].astype(LOW)

    def forward(piece):
        mlp[piece].arrive()
        mlp[piece].hop(0).start()
        mlp[piece].hop(1).start()

    for piece in range(half):
        rows_at = pl.ds(piece * tile, tile)
        seen = (pos_row[...] <= pos[rows_at]) & (pos_row[...] >= begins[rows_at])
        for head in range(heads):
            raw = dot_nt(q_low[head, rows_at], k_low[head // share]) * scale
            raw = jnp.where(seen, raw, NEG)
            weight = jnp.exp(raw - jnp.max(raw, -1, keepdims=True))
            weight = (weight * (1.0 / jnp.sum(weight, -1, keepdims=True))).astype(LOW)
            probs[head, rows_at] = weight
            value = dot_nn(weight, v_low[head // share])
            out_low[rows_at, head * size : (head + 1) * size] = value.astype(LOW)
            stores.append(move(probs.at[head, rows_at], prob.at[head, rows_at], local_sems.at[len(stores)]))
        outs.arrive(piece + 1)
        if piece + 1 < half:
            outs.start(piece + 2)
        outs.forward(piece + 1)
        if piece == 1:
            ring.arrive(1)
            ring.start(2)
        if piece >= 2:
            forward(piece - 2)

    place = ring_place(seq, ranks)

    def exchange(rel):
        to = ring_seq(lax.rem(place + rel, ranks), ranks)
        return push(
            out_low.at[pl.ds(ring.row[rel], local)],
            own_out.at[:, pl.ds(pl.multiple_of(seq * o_cols, o_cols), o_cols)],
            out_send.at[rel],
            out_recv.at[rel],
            (to, dp),
        )

    for rel in range(1, ranks):
        exchange(rel).start()
    own_out[:, pl.ds(pl.multiple_of(seq * o_cols, o_cols), o_cols)] = out_low[:local]
    ring.arrive(2)
    ring.start(3)
    outs.complete()
    stores.append(move(whole, w_output, local_sems.at[len(stores)]))
    for rel in range(1, ranks):
        exchange(rel).wait_recv()

    def project(at, _):
        cols = pl.ds(pl.multiple_of(at * deep, deep), deep)
        resid[:, cols] = tokens[:, cols].astype(jnp.float32) + dot_nt(own_out[...], whole[at])
        return 0

    lax.fori_loop(0, ranks, project, 0)

    def some(at, _):
        begin = pl.multiple_of(at * 32, 32)
        rows_at = pl.ds(begin, 32)
        second[rows_at] = rows_scaled(resid[rows_at])[0].astype(LOW)
        return 0

    lax.fori_loop(0, local // 32, some, 0)
    forward(2)
    for later in range(3, half):
        ring.arrive(later)
        ring.start(later + 1)
    for piece in mlp:
        piece.hop(0).wait_recv()
        piece.hop(2).start()
    ring.arrive(half)
    stores.append(move(dys, dy_all, local_sems.at[len(stores)]))
    ring.finish()
    outs.finish()
    for rel in range(1, ranks):
        exchange(rel).wait_send()
    for piece in mlp:
        piece.hop(1).wait_recv()
        piece.hop(2).wait_recv()
        piece.finish()
    for store in stores:
        store.wait()


def mlp_kernel(
    ranks, second, out_grad, rest, dys, mlp_block, block_out, dresid, dresid_low, gain_grad, own_grads,
    grads, from_core, from_y, held, weights, hidden, dgu, resid, dy_all,
    term, out_buf, in_buf, y_out, y_in, here, *sems,
):
    local, width = second.shape
    ff = hidden.shape[1]
    deep = weights.shape[1]
    half = ranks // 2
    right, left = neighbours(ranks)
    loads = [
        move(src, dst, here.at[at])
        for at, (src, dst) in enumerate(((mlp_block, weights), (dys, dy_all), (rest, resid)))
    ]
    seq, dp = lax.axis_index("seq"), lax.axis_index("dp")
    own = own_grads.shape[1]
    pieces = [
        Reduce(
            grads, from_core, from_y, own_grads, own, at * ranks // 4, ranks // 4, pl.ds(0, 3 * ff),
            sems[6 + 2 * at : 8 + 2 * at],
        )
        for at in range(4)
    ]
    peers = [right, left, (seq, pieces[0].beside), (seq, pieces[0].sibling)]
    knock(peers)
    held[:local] = second[...]
    answered(peers)
    ring = RingGather(held, local, ranks, sems[0], sems[1], right, left)
    ring.start(1)
    loads[0].wait()
    loads[1].wait()
    wide = 256

    def middle(begin, count):
        rows = pl.ds(begin, count)

        def some(at, _):
            first = pl.multiple_of(at * wide, wide)
            gate = dot_nn(held[rows], weights[:, :, pl.ds(first, wide)].reshape(width, wide))
            upper = dot_nn(held[rows], weights[:, :, pl.ds(ff + first, wide)].reshape(width, wide))
            dmid = dot_nn(dy_all[rows], weights[:, :, pl.ds(2 * ff + first, wide)].reshape(width, wide))
            sigma = 1.0 / (1.0 + jnp.exp(-gate))
            act = gate * sigma
            hidden[rows, pl.ds(first, wide)] = (act * upper).astype(LOW)
            slope = sigma * (1.0 + gate * (1.0 - sigma))
            dgu[rows, pl.ds(first, wide)] = (dmid * upper * slope).astype(LOW)
            dgu[rows, pl.ds(ff + first, wide)] = (dmid * act).astype(LOW)
            return 0

        lax.fori_loop(0, ff // wide, some, 0)

    middle(*ring.rows(0))
    for step in range(1, half + 1):
        ring.arrive(step)
        if step < half:
            ring.start(step + 1)
        middle(*ring.rows(step))

    def back_part(begin, count):
        def some(at, _):
            value = dot_nt(dgu[pl.ds(begin, count)], weights[at, :, : 2 * ff])
            term[:count, pl.ds(pl.multiple_of(at * deep, deep), deep)] = value
            return 0

        lax.fori_loop(0, ranks, some, 0)

    def out_part(begin, count):
        def some(at, _):
            value = dot_nt(hidden[pl.ds(begin, count)], weights[at, :, 2 * ff :])
            term[:count, pl.ds(pl.multiple_of(at * deep, deep), deep)] = value
            return 0

        lax.fori_loop(0, ranks, some, 0)

    def weight_grads(first, count):
        def some(at, _):
            cols = pl.ds(pl.multiple_of(at * deep, deep), deep)
            grads[at, :, : 2 * ff] = dot_tn(held[:, cols], dgu[...]).astype(LOW)
            grads[at, :, 2 * ff :] = dot_tn(dy_all[:, cols], hidden[...]).astype(LOW)
            return 0

        lax.fori_loop(first, first + count, some, 0)

    back = RingSum(back_part, term, out_buf, in_buf, local, ranks, sems[2], sems[3], right, left)
    out = RingSum(out_part, term, y_out, y_in, local, ranks, sems[4], sems[5], right, left)
    for step in range(1, half + 1):
        back.compute(step)
        back.launch(step)
        out.compute(step)
        out.launch(step)
        if step < 3:
            for piece in pieces[2 * step - 2 : 2 * step]:
                weight_grads(piece.begin, piece.count)
                piece.first()
        if 1 < step < 4:
            for piece in pieces[2 * step - 4 : 2 * step - 2]:
                piece.second()
        if step > 2:
            for piece in pieces[2 * step - 6 : 2 * step - 4]:
                piece.third()
    back.compute(half + 1)
    loads[2].wait()
    back.arrive_last()
    gain_grad[...] = jnp.zeros_like(gain_grad)

    def finish_back(at, _):
        begin = pl.multiple_of(at * 32, 32)
        rows = pl.ds(begin, 32)
        value = resid[rows]
        normal, inv = rows_scaled(value)
        grad = back.last(begin, 32)
        full = out_grad[rows].astype(jnp.float32) + rows_scaled_back(value, inv, grad)
        dresid[rows] = full
        dresid_low[rows] = full.astype(LOW)
        gain_grad[...] += jnp.sum(grad * normal, 0, keepdims=True)
        return 0

    lax.fori_loop(0, local // 32, finish_back, 0)
    out.compute(half + 1)
    out.arrive_last()

    def finish_out(at, _):
        begin = pl.multiple_of(at * 32, 32)
        rows = pl.ds(begin, 32)
        block_out[rows] = (resid[rows] + out.last(begin, 32)).astype(LOW)
        return 0

    lax.fori_loop(0, local // 32, finish_out, 0)
    ring.finish()
    back.finish()
    out.finish()
    for piece in pieces:
        piece.finish()


def back_kernel(
    ranks, kv_heads, tokens, dresid_low, query_gain, key_gain, mlp_gain_part, own_out, first_in_in, block_in,
    qkv_in, cos_in, sin_in, q_in, k_in, v_in, prob_in, dresid_in, mlp_own, w_output,
    tokens_grad, gains, w_output_grad, mlp_sums, attn_sums,
    grads, from_core, from_y, own_grads, o_grads, o_core, o_y, o_own, gain_grad, query_gain_grad, key_gain_grad,
    tiles, tiles_in, tile_sums, tile_sums_in, dob, dout, dk, dv, dqkv,
    first_in, attn_block, qkv, cosv, sinv, q_low, k_low, v_low, prob, dresid, term, out_buf, in_buf,
    o_term, o_out, o_in, *sems,
):
    local, width = tokens.shape
    rows = local * ranks
    half = ranks // 2
    size = cosv.shape[1]
    heads = q_low.shape[0]
    share = heads // kv_heads
    scale = 1.0 / math.sqrt(size)
    cols = (heads + 2 * kv_heads) * size
    deep = attn_block.shape[1]
    o_cols = heads * size
    right, left = neighbours(ranks)
    seq, dp = lax.axis_index("seq"), lax.axis_index("dp")
    place = ring_place(seq, ranks)
    own = mlp_own.shape[1]
    copies = tiles.shape[1]
    third = mlp_own.shape[2] // 3
    dob_send, dob_recv = sems[0:2]
    qkv_piece = Reduce(grads, from_core, from_y, own_grads, own, 0, ranks, pl.ds(0, cols), sems[4:6])
    out_piece = Reduce(o_grads, o_core, o_y, o_own, own, 0, ranks, pl.ds(0, width), sems[6:8])
    mlp_ways = [
        Deliver(mlp_own, mlp_sums, pl.ds(at * third, third), ranks, sems[8 + 3 * at : 11 + 3 * at])
        for at in range(3)
    ]
    qkv_way = Deliver(own_grads, attn_sums, pl.ds(0, cols), ranks, sems[24:27])
    peers = [(lax.rem(seq + step, ranks), dp) for step in range(1, ranks)]
    peers += [(seq, lax.rem(dp + step, copies)) for step in range(1, copies)]
    knock(peers)
    local_sems = sems[21]
    loads = {}
    for at, (name, src, dst) in enumerate(
        (
            ("w_output", w_output, o_grads), ("v", v_in, v_low), ("prob", prob_in, prob), ("k", k_in, k_low),
            ("q", q_in, q_low), ("cos", cos_in, cosv), ("sin", sin_in, sinv), ("qkv", qkv_in, qkv),
            ("block", block_in, attn_block), ("first", first_in_in, first_in), ("dresid", dresid_in, dresid),
        )
    ):
        loads[name] = move(src, dst, local_sems.at[at])
    answered(peers)
    mlp_ways[0].start()
    row = {rel: at * local for at, rel in enumerate(ring_order(ranks))}
    loads["w_output"].wait()

    def columns_of(rank):
        return pl.ds(pl.multiple_of(rank * o_cols, o_cols), o_cols)

    def owner(rel):
        return ring_seq(lax.rem(place + ranks - rel, ranks), ranks)

    def exchange(rel):
        to = owner(rel)
        return push(
            dob.at[:, columns_of(to)], dout.at[pl.ds(row[rel], local)], dob_send.at[rel], dob_recv.at[rel], (to, dp)
        )

    def project(rel):
        some = columns_of(owner(rel))
        dob[:, some] = dot_nn(dresid_low[...], o_grads[:, :, some].reshape(width, o_cols)).astype(LOW)

    for rel in range(1, ranks):
        project(rel)
        exchange(rel).start()
    project(0)
    dout[:local] = dob[:, columns_of(seq)]
    for way in mlp_ways[1:]:
        way.start()

    def out_grads(at, _):
        some_cols = pl.ds(pl.multiple_of(at * deep, deep), deep)
        o_grads[at] = dot_tn(dresid_low[:, some_cols], own_out[...]).astype(LOW)
        return 0

    lax.fori_loop(0, ranks, out_grads, 0)
    out_piece.first()
    for rel in range(1, ranks):
        exchange(rel).wait_recv()
    for name in ("v", "prob", "k", "q", "cos", "sin", "qkv"):
        loads[name].wait()
    tile = rows // half
    query_gain_grad[...] = jnp.zeros_like(query_gain_grad)
    key_gain_grad[...] = jnp.zeros_like(key_gain_grad)

    def unrotated(grad, column, rows_at, gain, gain_grad_ref):
        grad = grad * cosv[rows_at] - turn(grad) * sinv[rows_at]
        value = qkv[rows_at, column * size : (column + 1) * size]
        normal, inv = rows_scaled(value)
        gain_grad_ref[...] += jnp.sum(grad * normal, 0, keepdims=True)
        back = rows_scaled_back(value, inv, grad * gain[...])
        dqkv[rows_at, column * size : (column + 1) * size] = back.astype(LOW)

    for head in range(heads):
        group = head // share

        def one(piece, _):
            rows_at = pl.ds(pl.multiple_of(piece * tile, tile), tile)
            weight = prob[head, rows_at]
            grad = dout[rows_at, head * size : (head + 1) * size]
            dprob = dot_nt(grad, v_low[group])
            full = weight.astype(jnp.float32)
            delta = jnp.sum(full * dprob, -1, keepdims=True)
            dscore = (full * (dprob - delta)).astype(LOW)
            dq = dot_nn(dscore, k_low[group]) * scale
            dk_add = dot_tn(dscore, q_low[head, rows_at]) * scale
            dv_add = dot_tn(weight, grad)
            dk[group] += dk_add
            dv[group] += dv_add
            unrotated(dq, head, rows_at, query_gain, query_gain_grad)
            return 0

        if head % share == 0:
            dk[group] = jnp.zeros_like(dk[group])
            dv[group] = jnp.zeros_like(dv[group])
        lax.fori_loop(0, half, one, 0)
        if head == 0:
            out_piece.second()
    for group in range(kv_heads):
        def one_key(piece, _):
            rows_at = pl.ds(pl.multiple_of(piece * tile, tile), tile)
            unrotated(dk[group, rows_at], heads + group, rows_at, key_gain, key_gain_grad)
            at = (heads + kv_heads + group) * size
            dqkv[rows_at, at : at + size] = dv[group, rows_at].astype(LOW)
            return 0

        lax.fori_loop(0, half, one_key, 0)

    def part(begin, count):
        def some(at, _):
            value = dot_nt(dqkv[pl.ds(begin, count)], attn_block[at, :, :cols])
            term[:count, pl.ds(pl.multiple_of(at * deep, deep), deep)] = value
            return 0

        lax.fori_loop(0, ranks, some, 0)

    def qkv_grads(at, _):
        some_cols = pl.ds(pl.multiple_of(at * deep, deep), deep)
        grads[at, :, :cols] = dot_tn(first_in[:, some_cols], dqkv[...]).astype(LOW)
        return 0

    def out_part(begin, count):
        for at in range(begin // own, (begin + count) // own):
            to = ring_seq(lax.rem(place + ring_order(ranks)[at], ranks), ranks)
            o_term[at * own - begin : (at + 1) * own - begin] = o_own[to].astype(jnp.float32)

    total = RingSum(part, term, out_buf, in_buf, local, ranks, sems[2], sems[3], right, left)
    loads["block"].wait()
    out_total = RingSum(out_part, o_term, o_out, o_in, own, ranks, sems[22], sems[23], right, left)
    for step in range(1, half + 1):
        total.compute(step)
        total.launch(step)
        if step == 1:
            loads["first"].wait()
            lax.fori_loop(0, ranks, qkv_grads, 0)
            qkv_piece.first()
            out_piece.third()
        if step == 2:
            qkv_piece.second()
        if step == half - 1:
            qkv_piece.third()
            qkv_way.start()
        out_total.compute(step)
        out_total.launch(step)
    total.compute(half + 1)
    loads["dresid"].wait()
    total.arrive_last()
    gain_grad[...] = jnp.zeros_like(gain_grad)

    def last(at, _):
        begin = pl.multiple_of(at * 32, 32)
        rows_at = pl.ds(begin, 32)
        value = tokens[rows_at].astype(jnp.float32)
        normal, inv = rows_scaled(value)
        grad = total.last(begin, 32)
        tokens_grad[rows_at] = dresid[rows_at] + rows_scaled_back(value, inv, grad)
        gain_grad[...] += jnp.sum(grad * normal, 0, keepdims=True)
        return 0

    lax.fori_loop(0, local // 32, last, 0)
    out_total.compute(half + 1)
    out_total.arrive_last()
    w_output_grad[...] = out_total.last(0, own)
    lane = lax.broadcasted_iota(jnp.int32, (1, size), 1)
    per_row = size // own
    for number in range(ranks * copies):
        at = number // per_row
        first = gain_grad[:, at * size : (at + 1) * size]
        second = mlp_gain_part[:, at * size : (at + 1) * size]
        shift = number % per_row * own
        first = pltpu.roll(first, (size - shift) % size, 1) if shift else first
        second = pltpu.roll(second, (size + own - shift) % size, 1) if shift != own else second
        tile_at = tiles.at[number // copies, number % copies]
        tile_at[0:1] = jnp.where(lane < own, first, second)
        tile_at[1:2] = query_gain_grad[...]
        tile_at[2:3] = key_gain_grad[...]
        tile_at[3:] = jnp.zeros((tiles.shape[2] - 3, size), jnp.float32)

    def to_ranks(step):
        peer = lax.rem(seq + step, ranks)
        return push(tiles.at[peer], tiles_in.at[seq], sems[17].at[step], sems[18].at[step], (peer, dp))

    def to_copies(step):
        peer = lax.rem(dp + step, copies)
        return push(
            tile_sums.at[peer], tile_sums_in.at[dp], sems[19].at[step], sems[20].at[step], (seq, peer)
        )

    for step in range(1, ranks):
        to_ranks(step).start()
    tiles_in[seq] = tiles[seq]
    for step in range(1, ranks):
        to_ranks(step).wait_recv()
    tile_sums[...] = jnp.sum(tiles_in[...], 0)
    for step in range(1, copies):
        to_copies(step).start()
    tile_sums_in[dp] = tile_sums[dp]
    for step in range(1, copies):
        to_copies(step).wait_recv()
    gains[...] = jnp.sum(tile_sums_in[...], 0)
    for step in range(1, ranks):
        to_ranks(step).wait_send()
    for step in range(1, copies):
        to_copies(step).wait_send()
    total.finish()
    out_total.finish()
    out_piece.finish()
    qkv_piece.finish()
    for rel in range(1, ranks):
        exchange(rel).wait_send()
    for way in mlp_ways:
        way.finish()
    qkv_way.finish()


def leave_kernel(attn_sums, mlp_sums, gains, attn_gain, mlp_gain, *outs):
    own = attn_gain.shape[1]
    same = lax.broadcasted_iota(jnp.int32, (own, own), 0) == lax.broadcasted_iota(jnp.int32, (own, own), 1)

    def column(row):
        return jnp.sum(jnp.where(same, row, 0.0), 1, keepdims=True)

    first, second = column(attn_gain[...]), column(mlp_gain[...])
    for sums, parts in ((attn_sums, zip(outs[:3], (first, first, first))), (mlp_sums, zip(outs[3:6], (second, second, None)))):
        at = 0
        for out, gain in parts:
            value = sums[0, :, at : at + out.shape[1]].astype(jnp.float32)
            out[...] = value if gain is None else value * gain
            at += out.shape[1]
    outs[6][...] = gains[0:1, :own] / attn_gain[...]
    outs[7][...] = gains[0:1, own : 2 * own] / mlp_gain[...]


VM = pl.BlockSpec(memory_space=pltpu.VMEM)
SM = pl.BlockSpec(memory_space=pltpu.SMEM)
ANY = pl.BlockSpec(memory_space=pl.ANY)


def call(kernel, number, ins, outs, scratch, operands):
    return pl.pallas_call(
        kernel,
        out_shape=[jax.ShapeDtypeStruct(shape, dtype) for shape, dtype, _ in outs],
        in_specs=ins,
        out_specs=[spec for _, _, spec in outs],
        scratch_shapes=scratch,
        compiler_params=pltpu.CompilerParams(
            collective_id=number, has_side_effects=True, vmem_limit_bytes=LIMIT
        ),
    )(*operands)


def columns_body(
    tokens,
    out_grad,
    span_order,
    doc_starts,
    w_query,
    w_key,
    w_value,
    w_output,
    attn_gain,
    query_gain,
    key_gain,
    w_gate,
    w_up,
    w_down,
    mlp_gain,
):
    ranks = lax.axis_size("seq")
    copies = lax.axis_size("dp")
    _, local, width = tokens.shape
    rows = local * ranks
    size = query_gain.shape[0]
    kv_heads = w_key.shape[1] // size // ranks
    heads = w_query.shape[1] // size // ranks
    q_cols, kv_cols = heads * size, kv_heads * size
    qkv_cols = q_cols + 2 * kv_cols
    ff = w_gate.shape[1] // ranks
    own = width // (ranks * copies)
    deep = own * copies
    half = ranks // 2
    f32, i32 = jnp.float32, jnp.int32
    exponents = np.arange(size) % (size // 2) * (-2.0 / size * math.log(1000000.0))
    freqs = jnp.asarray(np.exp(exponents)[None], f32)
    first_in, qkv, attn_block, mlp_rows, cosv, sinv, pos, begins, pos_row = call(
        functools.partial(enter_kernel, ranks),
        1,
        [SM, SM] + [VM] * 7 + [ANY] * 3,
        [
            ((rows, width), LOW, ANY),
            ((rows, qkv_cols), f32, ANY),
            ((ranks, deep, qkv_cols), LOW, ANY),
            ((ranks, own, 3 * ff), LOW, ANY),
            ((rows, size), f32, VM),
            ((rows, size), f32, VM),
            ((rows, 1), i32, VM),
            ((rows, 1), i32, VM),
            ((1, rows), i32, VM),
        ],
        [
            pltpu.VMEM((rows, width), LOW),
            pltpu.VMEM((rows, width), LOW),
            pltpu.VMEM((rows, qkv_cols), f32),
            pltpu.VMEM((ranks, deep, qkv_cols), LOW),
            pltpu.VMEM((ranks, own, qkv_cols), LOW),
            pltpu.VMEM((ranks, own, 3 * ff), LOW),
        ]
        + [pltpu.VMEM((own, ff * ranks), LOW)] * 3
        + ring_sems(ranks)
        + spread_sems(ranks)
        + [pltpu.SemaphoreType.DMA((2 * half + 6,))],
        (
            span_order, doc_starts, tokens[0], freqs, attn_gain[None], mlp_gain[None], w_query, w_key, w_value,
            w_gate, w_up, w_down,
        ),
    )
    q_gain, k_gain = query_gain[None], key_gain[None]
    q_low, k_low, v_low, own_out, resid, second, dy_all, prob, mlp_block, wo_all = call(
        functools.partial(attend_kernel, ranks, kv_heads),
        2,
        [VM] * 11 + [ANY],
        [
            ((heads, rows, size), LOW, VM),
            ((kv_heads, rows, size), LOW, VM),
            ((kv_heads, rows, size), LOW, VM),
            ((local, q_cols * ranks), LOW, VM),
            ((local, width), f32, VM),
            ((local, width), LOW, VM),
            ((rows, width), LOW, ANY),
            ((heads, rows, rows), LOW, ANY),
            ((ranks, deep, 3 * ff), LOW, ANY),
            ((ranks, deep, q_cols * ranks), LOW, ANY),
        ],
        [
            pltpu.VMEM((rows, width), LOW),
            pltpu.VMEM((heads, rows, rows), LOW),
            pltpu.VMEM((rows, q_cols), LOW),
            pltpu.VMEM((ranks, deep, q_cols * ranks), LOW),
        ]
        + ring_sems(ranks)
        + whole_sems(ranks)
        + spread_sems(ranks) * 3
        + [pltpu.SemaphoreType.DMA((heads * half + 2,))]
        + [pltpu.SemaphoreType.DMA((ranks,))] * 2,
        (
            out_grad[0], tokens[0], qkv, cosv, sinv, pos, begins, pos_row, q_gain, k_gain, w_output, mlp_rows,
        ),
    )
    block_out, dresid, dresid_low, dgm, mlp_own = call(
        functools.partial(mlp_kernel, ranks),
        3,
        [VM, VM, ANY, ANY, ANY],
        [
            ((local, width), LOW, VM),
            ((local, width), f32, VM),
            ((local, width), LOW, VM),
            ((1, width), f32, VM),
            ((ranks, own, 3 * ff), LOW, VM),
        ],
        [pltpu.VMEM((ranks, deep, 3 * ff), LOW)]
        + reduce_bufs(ranks, own, 3 * ff)
        + [
            pltpu.VMEM((rows, width), LOW),
            pltpu.VMEM((ranks, deep, 3 * ff), LOW),
            pltpu.VMEM((rows, ff), LOW),
            pltpu.VMEM((rows, 2 * ff), LOW),
            pltpu.VMEM((local, width), f32),
            pltpu.VMEM((rows, width), LOW),
        ]
        + sum_bufs(local, ranks, width)
        + sum_bufs(local, ranks, width)[1:]
        + [pltpu.SemaphoreType.DMA((3,))]
        + ring_sems(ranks) * 3
        + reduce_sems() * 4,
        (second, out_grad[0], resid, dy_all, mlp_block),
    )
    tokens_grad, gains, wo_grad, mlp_sums, attn_sums = call(
        functools.partial(back_kernel, ranks, kv_heads),
        4,
        [VM] * 6 + [ANY] * 12,
        [
            ((local, width), f32, VM),
            ((8, size), f32, VM),
            ((own, q_cols * ranks), f32, VM),
            ((ranks, own, 3 * ff), LOW, ANY),
            ((ranks, own, qkv_cols), LOW, VM),
        ],
        [pltpu.VMEM((ranks, deep, qkv_cols), LOW)]
        + reduce_bufs(ranks, own, qkv_cols)
        + [pltpu.VMEM((ranks, own, qkv_cols), LOW), pltpu.VMEM((ranks, deep, q_cols * ranks), LOW)]
        + reduce_bufs(ranks, own, q_cols * ranks)
        + [
            pltpu.VMEM((ranks, own, q_cols * ranks), LOW),
            pltpu.VMEM((1, width), f32),
            pltpu.VMEM((1, size), f32),
            pltpu.VMEM((1, size), f32),
            pltpu.VMEM((ranks, copies, 8, size), f32),
            pltpu.VMEM((ranks, copies, 8, size), f32),
            pltpu.VMEM((copies, 8, size), f32),
            pltpu.VMEM((copies, 8, size), f32),
            pltpu.VMEM((local, q_cols * ranks), LOW),
            pltpu.VMEM((rows, q_cols), LOW),
            pltpu.VMEM((kv_heads, rows, size), f32),
            pltpu.VMEM((kv_heads, rows, size), f32),
            pltpu.VMEM((rows, qkv_cols), LOW),
            pltpu.VMEM((rows, width), LOW),
            pltpu.VMEM((ranks, deep, qkv_cols), LOW),
            pltpu.VMEM((rows, qkv_cols), f32),
            pltpu.VMEM((rows, size), f32),
            pltpu.VMEM((rows, size), f32),
            pltpu.VMEM((heads, rows, size), LOW),
            pltpu.VMEM((kv_heads, rows, size), LOW),
            pltpu.VMEM((kv_heads, rows, size), LOW),
            pltpu.VMEM((heads, rows, rows), LOW),
            pltpu.VMEM((local, width), f32),
        ]
        + sum_bufs(local, ranks, width)
        + sum_bufs(own, ranks, q_cols * ranks)
        + [pltpu.SemaphoreType.DMA((ranks,))] * 2
        + ring_sems(ranks)
        + reduce_sems() * 2
        + deliver_sems(ranks) * 3
        + [pltpu.SemaphoreType.DMA((ranks,))] * 2
        + [pltpu.SemaphoreType.DMA((copies,))] * 2
        + [pltpu.SemaphoreType.DMA((11,))]
        + ring_sems(ranks)
        + deliver_sems(ranks),
        (
            tokens[0], dresid_low, q_gain, k_gain, dgm, own_out, first_in, attn_block, qkv, cosv, sinv, q_low, k_low,
            v_low, prob, dresid, mlp_own, wo_all,
        ),
    )
    whole = pl.BlockSpec((1, own), lambda at: (0, 0))
    each = (q_cols, kv_cols, kv_cols, ff, ff, ff)
    *grads, dga, dgm = pl.pallas_call(
        leave_kernel,
        grid=(ranks,),
        out_shape=[jax.ShapeDtypeStruct((own, cols * ranks), f32) for cols in each]
        + [jax.ShapeDtypeStruct((1, own), f32)] * 2,
        in_specs=[
            pl.BlockSpec((1, own, qkv_cols), lambda at: (at, 0, 0)),
            pl.BlockSpec((1, own, 3 * ff), lambda at: (at, 0, 0)),
            pl.BlockSpec((8, size), lambda at: (0, 0)),
            whole,
            whole,
        ],
        out_specs=[pl.BlockSpec((own, cols), lambda at: (0, at)) for cols in each] + [whole, whole],
    )(attn_sums, mlp_sums, gains, attn_gain[None], mlp_gain[None])
    return (
        block_out[None], tokens_grad[None], *grads[:3], wo_grad, dga[0], gains[1], gains[2], *grads[3:], dgm[0],
    )


def body(*args):
    tokens, w_key, query_gain = args[0], args[5], args[9]
    groups = w_key.shape[1] // query_gain.shape[0]
    ranks = lax.axis_size("seq")
    if tokens.shape[0] == 1 and ranks % 2 == 0 and groups % ranks == 0 and lax.axis_size("dp") == 4:
        return columns_body(*args)
    return gathered_body(*args)


def solution(mesh):
    return jax.shard_map(
        body,
        mesh=mesh,
        in_specs=(
            P("dp", "seq", None),
            P("dp", "seq", None),
            P(),
            P("dp", None),
            P(("seq", "dp"), None),
            P(("seq", "dp"), None),
            P(("seq", "dp"), None),
            P(("seq", "dp"), None),
            P(("seq", "dp")),
            P(),
            P(),
            P(("seq", "dp"), None),
            P(("seq", "dp"), None),
            P(("seq", "dp"), None),
            P(("seq", "dp")),
        ),
        out_specs=(
            P("dp", "seq", None),
            P("dp", "seq", None),
            P(("seq", "dp"), None),
            P(("seq", "dp"), None),
            P(("seq", "dp"), None),
            P(("seq", "dp"), None),
            P(("seq", "dp")),
            P(),
            P(),
            P(("seq", "dp"), None),
            P(("seq", "dp"), None),
            P(("seq", "dp"), None),
            P(("seq", "dp")),
        ),
        check_vma=False,
    )
```

```python
import functools
import math

import jax
import jax.numpy as jnp
import numpy as np
from jax import lax
from jax.experimental import pallas as pl
from jax.experimental.pallas import tpu as pltpu
from jax.sharding import PartitionSpec as P

EPS = 1e-06
NEG = -1e30


def normed(v, gain):
    scale_inv = lax.rsqrt(jnp.mean(v * v, -1, keepdims=True) + EPS)
    return (v * scale_inv * gain, scale_inv)


def norm_back(v, scale_inv, gain, grad):
    scaled = grad * gain
    inner = jnp.mean(scaled * v, -1, keepdims=True)
    dv = scale_inv * scaled - v * scale_inv * scale_inv * scale_inv * inner
    dgain = jnp.sum((grad * v * scale_inv).reshape(-1, v.shape[-1]), 0)
    return (dv, dgain)


def rotary(pos, width):
    half = width // 2
    freqs = jnp.exp(jnp.arange(half, dtype=jnp.float32) * (-2.0 / width * math.log(1000000.0)))
    angle = pos.astype(jnp.float32)[:, None] * freqs[None, :]
    return (jnp.cos(angle)[:, None, :], jnp.sin(angle)[:, None, :])


def rotate(v, cosv, sinv):
    half = v.shape[-1] // 2
    first, second = (v[..., :half], v[..., half:])
    return jnp.concatenate([first * cosv - second * sinv, second * cosv + first * sinv], -1)


def rotate_back(grad, cosv, sinv):
    half = grad.shape[-1] // 2
    first, second = (grad[..., :half], grad[..., half:])
    return jnp.concatenate([first * cosv + second * sinv, second * cosv - first * sinv], -1)


def place(order, begin, count, span):
    rows = begin + jnp.arange(count, dtype=jnp.int32)
    slots = rows // span
    picked = slots[:, None] == jnp.arange(order.shape[0], dtype=jnp.int32)[None, :]
    return jnp.sum(jnp.where(picked, order[None, :], 0), -1) * span + rows % span


def doc_of(starts, pos):
    return jnp.sum((starts[:, None, :] <= pos[None, :, None]).astype(jnp.int32), -1)


def gathered_body(
    tokens,
    out_grad,
    span_order,
    doc_starts,
    w_query,
    w_key,
    w_value,
    w_output,
    attn_gain,
    query_gain,
    key_gain,
    w_gate,
    w_up,
    w_down,
    mlp_gain,
):
    seqs, local, width = tokens.shape
    span = local // 2
    head_size = query_gain.shape[0]
    kv_heads = w_key.shape[1] // head_size
    heads = w_query.shape[1] // head_size
    share = heads // kv_heads
    kv_width = kv_heads * head_size
    ff_width = w_gate.shape[1]
    scale = 1.0 / math.sqrt(head_size)
    total_rows = seqs * local
    own_rows = width // lax.axis_size(("seq", "dp"))
    qpos = place(span_order, lax.axis_index("seq") * local, local, span)
    qdoc = doc_of(doc_starts, qpos)
    cosv, sinv = rotary(qpos, head_size)

    def gather_attn():
        return (
            lax.all_gather(w_query, ("seq", "dp"), axis=0, tiled=True),
            lax.all_gather(w_key, ("seq", "dp"), axis=0, tiled=True),
            lax.all_gather(w_value, ("seq", "dp"), axis=0, tiled=True),
            lax.all_gather(w_output, ("seq", "dp"), axis=0, tiled=True),
            lax.all_gather(
                attn_gain.astype(jnp.bfloat16), ("seq", "dp"), axis=0, tiled=True
            ).astype(attn_gain.dtype),
        )

    def gather_mlp():
        return (
            lax.all_gather(w_gate, ("seq", "dp"), axis=0, tiled=True),
            lax.all_gather(w_up, ("seq", "dp"), axis=0, tiled=True),
            lax.all_gather(w_down, ("seq", "dp"), axis=0, tiled=True),
            lax.all_gather(mlp_gain.astype(jnp.bfloat16), ("seq", "dp"), axis=0, tiled=True).astype(
                mlp_gain.dtype
            ),
        )

    x_rows = tokens.astype(jnp.float32).reshape(total_rows, width)
    wq_all, wk_all, wv_all, wo_all, ga_all = gather_attn()
    first_norm, first_inv = normed(x_rows, ga_all)
    first_in = first_norm.astype(jnp.bfloat16)
    q_raw = jnp.dot(first_in, wq_all, preferred_element_type=jnp.float32).reshape(
        seqs, local, heads, head_size
    )
    k_raw = jnp.dot(first_in, wk_all, preferred_element_type=jnp.float32).reshape(
        seqs, local, kv_heads, head_size
    )
    v_low = (
        jnp.dot(first_in, wv_all, preferred_element_type=jnp.float32)
        .astype(jnp.bfloat16)
        .reshape(seqs, local, kv_heads, head_size)
    )
    q_normed, q_inv = normed(q_raw, query_gain)
    k_normed, k_inv = normed(k_raw, key_gain)
    q_low = rotate(q_normed, cosv, sinv).astype(jnp.bfloat16)
    k_low = rotate(k_normed, cosv, sinv).astype(jnp.bfloat16)
    q_group = q_low.reshape(seqs, local, kv_heads, share, head_size)

    def scores(piece_key, start):
        count = piece_key.shape[1]
        kpos = place(span_order, start, count, span)
        kdoc = doc_of(doc_starts, kpos)
        visible = (qdoc[:, :, None] == kdoc[:, None, :]) & (
            kpos[None, None, :] <= qpos[None, :, None]
        )
        raw = (
            jnp.einsum("sqgjd,skgd->sgjqk", q_group, piece_key, preferred_element_type=jnp.float32)
            * scale
        )
        return (raw, visible[:, None, None])

    start_top = jnp.full((seqs, kv_heads, share, local), NEG, jnp.float32)
    piece = (
        lax.all_gather(k_low, "seq", axis=1, tiled=True),
        lax.all_gather(v_low, "seq", axis=1, tiled=True),
    )
    top = start_top
    raw, visible = scores(piece[0], jnp.int32(0))
    raw = jnp.where(visible, raw, NEG)
    new_top = jnp.maximum(top, jnp.max(raw, -1))
    weights = jnp.where(visible, jnp.exp(raw - new_top[..., None]), 0.0)
    total = jnp.sum(weights, -1)
    summed = jnp.einsum(
        "sgjqk,skgd->sgjqd",
        weights.astype(jnp.bfloat16),
        piece[1],
        preferred_element_type=jnp.float32,
    )
    top, total, summed = (new_top, total, summed)
    log_total = top + jnp.log(total)
    attn_vals = summed / total[..., None]
    out_low = (
        jnp.transpose(attn_vals, (0, 3, 1, 2, 4))
        .reshape(total_rows, heads * head_size)
        .astype(jnp.bfloat16)
    )
    resid = x_rows + jnp.einsum("nh,dh->nd", out_low, wo_all, preferred_element_type=jnp.float32)
    wg_all, wu_all, wd_all, gm_all = gather_mlp()
    second_norm, second_inv = normed(resid, gm_all)
    second_in = second_norm.astype(jnp.bfloat16)
    gate = jnp.dot(second_in, wg_all, preferred_element_type=jnp.float32)
    upper = jnp.dot(second_in, wu_all, preferred_element_type=jnp.float32)
    sigma = jax.nn.sigmoid(gate)
    act = gate * sigma
    hidden = (act * upper).astype(jnp.bfloat16)
    result = resid + jnp.einsum("nf,df->nd", hidden, wd_all, preferred_element_type=jnp.float32)
    block_out = result.astype(jnp.bfloat16).reshape(seqs, local, width)
    grad_low = out_grad.reshape(total_rows, width)
    wg_all, wu_all, wd_all, gm_all = gather_mlp()
    dmid = jnp.einsum("nd,df->nf", grad_low, wd_all, preferred_element_type=jnp.float32)
    dgate = (dmid * upper * sigma * (1.0 + gate * (1.0 - sigma))).astype(jnp.bfloat16)
    dupper = (dmid * act).astype(jnp.bfloat16)
    left = second_in
    outer = grad_low
    mlp_sums = lax.psum_scatter(
        jnp.concatenate(
            [
                jnp.einsum("nd,nf->df", left, dgate, preferred_element_type=jnp.float32),
                jnp.einsum("nd,nf->df", left, dupper, preferred_element_type=jnp.float32),
                jnp.einsum("nd,nf->df", outer, hidden, preferred_element_type=jnp.float32),
            ],
            1,
        ),
        ("seq", "dp"),
        scatter_dimension=0,
        tiled=True,
    )
    dsecond = jnp.einsum(
        "nf,df->nd", dgate, wg_all, preferred_element_type=jnp.float32
    ) + jnp.einsum("nf,df->nd", dupper, wu_all, preferred_element_type=jnp.float32)
    dresid_norm, dgm = norm_back(resid, second_inv, gm_all, dsecond)
    dresid = grad_low.astype(jnp.float32) + dresid_norm
    dresid_low = dresid.astype(jnp.bfloat16)
    wq_all, wk_all, wv_all, wo_all, ga_all = gather_attn()
    dout_low = jnp.einsum(
        "nd,dh->nh", dresid_low, wo_all, preferred_element_type=jnp.float32
    ).astype(jnp.bfloat16)
    dout_group = dout_low.reshape(seqs, local, kv_heads, share, head_size)
    delta = jnp.sum(jnp.transpose(dout_group.astype(jnp.float32), (0, 2, 3, 1, 4)) * attn_vals, -1)
    piece = (
        lax.all_gather(k_low, "seq", axis=1, tiled=True),
        lax.all_gather(v_low, "seq", axis=1, tiled=True),
    )
    count = piece[0].shape[1]
    raw, visible = scores(piece[0], jnp.int32(0))
    prob = jnp.where(visible, jnp.exp(raw - log_total[..., None]), 0.0)
    dprob = jnp.einsum(
        "sqgjd,skgd->sgjqk", dout_group, piece[1], preferred_element_type=jnp.float32
    )
    dscore = (prob * (dprob - delta[..., None])).astype(jnp.bfloat16)
    dq_sum = jnp.einsum("sgjqk,skgd->sqgjd", dscore, piece[0], preferred_element_type=jnp.float32)
    dk_part = (
        jnp.einsum("sgjqk,sqgjd->skgd", dscore, q_group, preferred_element_type=jnp.float32) * scale
    )
    dv_part = jnp.einsum(
        "sgjqk,sqgjd->skgd",
        prob.astype(jnp.bfloat16),
        dout_group,
        preferred_element_type=jnp.float32,
    )
    joined = jnp.concatenate(
        [dk_part.reshape(seqs, count, kv_width), dv_part.reshape(seqs, count, kv_width)], -1
    )
    buffer = joined
    dq_sum, buffer = (dq_sum, buffer)
    key_sums = lax.psum_scatter(
        buffer.astype(jnp.bfloat16), "seq", scatter_dimension=1, tiled=True
    ).astype(jnp.float32)
    dq_rot = (dq_sum * scale).reshape(seqs, local, heads, head_size)
    dq_raw, dgq = norm_back(q_raw, q_inv, query_gain, rotate_back(dq_rot, cosv, sinv))
    dk_rot = key_sums[..., :kv_width].reshape(seqs, local, kv_heads, head_size)
    dk_raw, dgk = norm_back(k_raw, k_inv, key_gain, rotate_back(dk_rot, cosv, sinv))
    dq_low = dq_raw.reshape(total_rows, heads * head_size).astype(jnp.bfloat16)
    dk_low = dk_raw.reshape(total_rows, kv_width).astype(jnp.bfloat16)
    dv_low = key_sums[..., kv_width:].reshape(total_rows, kv_width).astype(jnp.bfloat16)
    left = first_in
    outer = dresid_low
    attn_sums = lax.psum_scatter(
        jnp.concatenate(
            [
                jnp.einsum("nd,nh->dh", left, dq_low, preferred_element_type=jnp.float32),
                jnp.einsum("nd,nh->dh", left, dk_low, preferred_element_type=jnp.float32),
                jnp.einsum("nd,nh->dh", left, dv_low, preferred_element_type=jnp.float32),
                jnp.einsum("nd,nh->dh", outer, out_low, preferred_element_type=jnp.float32),
            ],
            1,
        ),
        ("seq", "dp"),
        scatter_dimension=0,
        tiled=True,
    )
    dfirst = jnp.einsum("nh,dh->nd", dq_low, wq_all, preferred_element_type=jnp.float32)
    dfirst = dfirst + jnp.einsum("nh,dh->nd", dk_low, wk_all, preferred_element_type=jnp.float32)
    dfirst = dfirst + jnp.einsum("nh,dh->nd", dv_low, wv_all, preferred_element_type=jnp.float32)
    dx_norm, dga = norm_back(x_rows, first_inv, ga_all, dfirst)
    tokens_grad = (dresid + dx_norm).reshape(seqs, local, width)
    dga_all, dgm_all, dgq_all, dgk_all = lax.psum((dga, dgm, dgq, dgk), ("seq", "dp"))
    offset = lax.axis_index(("seq", "dp")) * own_rows
    attn_gain_grad = lax.dynamic_slice_in_dim(dga_all, offset, own_rows, 0)
    mlp_gain_grad = lax.dynamic_slice_in_dim(dgm_all, offset, own_rows, 0)
    q_cols = heads * head_size
    w_query_grad = attn_sums[:, :q_cols]
    w_key_grad = attn_sums[:, q_cols : q_cols + kv_width]
    w_value_grad = attn_sums[:, q_cols + kv_width : q_cols + 2 * kv_width]
    w_output_grad = attn_sums[:, q_cols + 2 * kv_width :]
    w_gate_grad = mlp_sums[:, :ff_width]
    w_up_grad = mlp_sums[:, ff_width : 2 * ff_width]
    w_down_grad = mlp_sums[:, 2 * ff_width :]
    return (
        block_out,
        tokens_grad,
        w_query_grad,
        w_key_grad,
        w_value_grad,
        w_output_grad,
        attn_gain_grad,
        dgq_all,
        dgk_all,
        w_gate_grad,
        w_up_grad,
        w_down_grad,
        mlp_gain_grad,
    )


LOW = jnp.bfloat16
MESH = pl.DeviceIdType.MESH
LIMIT = 60 * 2**20


def ring_order(ranks):
    half = ranks // 2
    order = [0]
    for step in range(1, half):
        order += [step, ranks - step]
    return order + [half]


def ring_place(seq, ranks):
    z, x = lax.div(seq, 2), lax.rem(seq, 2)
    return z + x * (ranks - 1 - 2 * z)


def ring_seq(place, ranks):
    half = ranks // 2
    x, z = lax.div(place, half), lax.rem(place, half)
    return 2 * (z + x * (half - 1 - 2 * z)) + x


def neighbours(ranks):
    seq, dp = lax.axis_index("seq"), lax.axis_index("dp")
    at = ring_place(seq, ranks)
    right = ring_seq(lax.rem(at + 1, ranks), ranks)
    left = ring_seq(lax.rem(at + ranks - 1, ranks), ranks)
    return (right, dp), (left, dp)


def knock(devices):
    barrier = pltpu.get_barrier_semaphore()
    for device in devices:
        pl.semaphore_signal(barrier, inc=1, device_id=device, device_id_type=MESH)


def answered(devices):
    pl.semaphore_wait(pltpu.get_barrier_semaphore(), len(devices))


def move(src, dst, sem):
    copy = pltpu.make_async_copy(src, dst, sem)
    copy.start()
    return copy


def push(src, dst, send, recv, device):
    return pltpu.make_async_remote_copy(
        src_ref=src, dst_ref=dst, send_sem=send, recv_sem=recv, device_id=device, device_id_type=MESH
    )


def dot_nn(left, right):
    return jnp.dot(left, right, preferred_element_type=jnp.float32)


def dot_nt(left, right):
    return lax.dot_general(left, right, (((1,), (1,)), ((), ())), preferred_element_type=jnp.float32)


def dot_tn(left, right):
    return lax.dot_general(left, right, (((0,), (0,)), ((), ())), preferred_element_type=jnp.float32)


def block_row(rel, local, ranks):
    place = ring_place(lax.axis_index("seq"), ranks)
    return pl.multiple_of(ring_seq(lax.rem(place + rel, ranks), ranks) * local, local)


def block_rows(ref, rels, local, ranks):
    blocks = [ref[pl.ds(block_row(rel, local, ranks), local)] for rel in rels]
    return blocks[0] if len(blocks) == 1 else jnp.concatenate(blocks, 0)


def rels_of(step, ranks):
    return [rel for rel in ring_order(ranks) if min(rel, ranks - rel) == step]


class RingGather:
    def __init__(self, buf, local, ranks, send, recv, right, left, row, fixed=False):
        self.buf, self.local, self.half = buf, local, ranks // 2
        self.send, self.recv, self.right, self.left = send, recv, right, left
        self.ranks, self.row, self.fixed = ranks, row, fixed

    def copies(self, step):
        last = step == self.half
        rows = self.local // 2 if last else self.local
        skip = self.local // 2 if last else 0
        ranks, row = self.ranks, self.row
        behind, ahead = (ranks - step + 1) % ranks, step - 1
        if self.fixed:
            to_right, to_left = row(ranks - step), row(step)
        else:
            to_right, to_left = row(behind), row(ahead)
        pairs = ((behind, 0, to_right, self.right), (ahead, skip, to_left + skip, self.left))
        return [
            push(
                self.buf.at[pl.ds(self.row(src) + begin, rows)],
                self.buf.at[pl.ds(there, rows)],
                self.send.at[way, step - 1],
                self.recv.at[way, step - 1],
                device,
            )
            for way, (src, begin, there, device) in enumerate(pairs)
        ]

    def start(self, step):
        for copy in self.copies(step):
            copy.start()

    def arrive(self, step):
        for copy in self.copies(step):
            copy.wait_recv()

    def finish(self):
        for step in range(1, self.half + 1):
            for copy in self.copies(step):
                copy.wait_send()


class RingSum:
    def __init__(self, part, term, out_buf, in_buf, local, ranks, send, recv, right, left):
        self.part, self.term, self.out_buf, self.in_buf = part, term, out_buf, in_buf
        self.local, self.ranks, self.half = local, ranks, ranks // 2
        self.send, self.recv, self.right, self.left = send, recv, right, left

    def copies(self, step):
        rows = self.local // 2 if step == 1 else self.local
        skip = self.local // 2 if step == 1 else 0
        return [
            push(
                self.out_buf.at[way, (step - 1) % 2, pl.ds(begin, rows)],
                self.in_buf.at[way, step - 1, pl.ds(begin, rows)],
                self.send.at[way, step - 1],
                self.recv.at[way, step - 1],
                device,
            )
            for way, begin, device in ((0, 0, self.right), (1, skip, self.left))
        ]

    def compute(self, step):
        if step == 1:
            self.part([self.half])
        elif step <= self.half:
            self.part(rels_of(self.half + 1 - step, self.ranks))
        else:
            self.part([0])

    def launch(self, step):
        local, skip = self.local, self.local // 2
        if step > 2:
            for copy in self.copies(step - 2):
                copy.wait_send()
        if step == 1:
            self.out_buf[0, 0, :skip] = self.term[:skip].astype(LOW)
            self.out_buf[1, 0, skip:] = self.term[skip:local].astype(LOW)
        else:
            for copy in self.copies(step - 1):
                copy.wait_recv()
            for way in range(2):
                for begin, with_sum in ((0, step > 2 or way == 0), (skip, step > 2 or way == 1)):
                    value = self.term[pl.ds(way * local + begin, skip)]
                    if with_sum:
                        value = value + self.in_buf[way, step - 2, pl.ds(begin, skip)].astype(jnp.float32)
                    self.out_buf[way, (step - 1) % 2, pl.ds(begin, skip)] = value.astype(LOW)
        for copy in self.copies(step):
            copy.start()

    def last(self, begin, count):
        rows = pl.ds(begin, count)
        value = self.term[rows] + self.in_buf[0, self.half - 1, rows].astype(jnp.float32)
        return value + self.in_buf[1, self.half - 1, rows].astype(jnp.float32)

    def arrive_last(self):
        for copy in self.copies(self.half):
            copy.wait_recv()

    def finish(self):
        for step in range(max(1, self.half - 1), self.half + 1):
            for copy in self.copies(step):
                copy.wait_send()


def ring_sems(ranks):
    return [pltpu.SemaphoreType.DMA((2, ranks // 2)), pltpu.SemaphoreType.DMA((2, ranks // 2))]


def sum_bufs(local, ranks, width):
    return [
        pltpu.VMEM((2 * local, width), jnp.float32),
        pltpu.VMEM((2, 2, local, width), LOW),
        pltpu.VMEM((2, ranks // 2, local, width), LOW),
    ]


def turn(v):
    return pltpu.roll(v, v.shape[-1] // 2, v.ndim - 1)


def rows_scaled(v):
    inv = lax.rsqrt(jnp.mean(v * v, -1, keepdims=True) + EPS)
    return v * inv, inv


def rows_scaled_back(v, inv, grad):
    return inv * grad - v * (inv * inv * inv * jnp.mean(grad * v, -1, keepdims=True))


class Spread:
    def __init__(self, rows, block, ranks, own, cols, sems):
        self.rows, self.block, self.ranks, self.own, self.cols = rows, block, ranks, own, cols
        self.send, self.recv, self.hop_send, self.hop_recv, self.here = sems
        self.seq, self.dp = lax.axis_index("seq"), lax.axis_index("dp")
        y, core = lax.div(self.dp, 2), lax.rem(self.dp, 2)
        self.beside, self.sibling = (1 - y) * 2 + core, y * 2 + 1 - core

    def at(self, dp):
        return pl.ds(pl.multiple_of(dp * self.own, self.own), self.own)

    def exchange(self):
        for step in range(1, self.ranks):
            peer = lax.rem(self.seq + step, self.ranks)
            yield push(
                self.rows.at[peer, :, self.cols],
                self.block.at[self.seq, self.at(self.dp), self.cols],
                self.send.at[step],
                self.recv.at[step],
                (peer, self.dp),
            )

    def keep(self):
        return pltpu.make_async_copy(
            self.rows.at[self.seq, :, self.cols],
            self.block.at[self.seq, self.at(self.dp), self.cols],
            self.here,
        )

    def hop(self, number):
        dp = self.beside if number == 2 else self.dp
        part = self.block.at[:, self.at(dp), self.cols]
        to = self.beside if number == 0 else self.sibling
        return push(part, part, self.hop_send.at[number], self.hop_recv.at[number], (self.seq, to))

    def start(self):
        self.keep().start()
        for copy in self.exchange():
            copy.start()

    def arrive(self):
        self.keep().wait()
        for copy in self.exchange():
            copy.wait_recv()

    def finish(self):
        for copy in self.exchange():
            copy.wait_send()
        for number in range(3):
            self.hop(number).wait_send()


def spread_sems(ranks):
    return [
        pltpu.SemaphoreType.DMA((ranks,)),
        pltpu.SemaphoreType.DMA((ranks,)),
        pltpu.SemaphoreType.DMA((3,)),
        pltpu.SemaphoreType.DMA((3,)),
        pltpu.SemaphoreType.DMA,
    ]


class WholeGather:
    def __init__(self, block, ranks, own, sems):
        self.block, self.ranks, self.half, self.own = block, ranks, ranks // 2, own
        self.send, self.recv, self.y_send, self.y_recv, self.core_send, self.core_recv = sems
        self.seq, self.dp = lax.axis_index("seq"), lax.axis_index("dp")
        self.right, self.left = neighbours(ranks)
        self.place = ring_place(self.seq, ranks)
        y, core = lax.div(self.dp, 2), lax.rem(self.dp, 2)
        self.beside, self.sibling = (1 - y) * 2 + core, y * 2 + 1 - core

    def at(self, rel, dp, begin, count):
        seq = ring_seq(lax.rem(self.place + rel + self.ranks, self.ranks), self.ranks)
        return self.block.at[seq, pl.ds(pl.multiple_of(dp * self.own + begin, count), count)]

    def copies(self, step):
        last = step == self.half
        rows = self.own // 2 if last else self.own
        skip = self.own // 2 if last else 0
        given = []
        for way, rel, begin, device in ((0, 1 - step, 0, self.right), (1, step - 1, skip, self.left)):
            part = self.at(rel, self.dp, begin, rows)
            given.append(push(part, part, self.send.at[way, step - 1], self.recv.at[way, step - 1], device))
        return given

    def start(self, step):
        for copy in self.copies(step):
            copy.start()

    def hops(self, step):
        for at, rel in enumerate(ring_order(self.ranks)):
            if min(rel, self.ranks - rel) == step:
                part = self.at(rel, self.dp, 0, self.own)
                yield push(part, part, self.y_send.at[at], self.y_recv.at[at], (self.seq, self.beside))
                yield push(part, part, self.core_send.at[at], self.core_recv.at[at], (self.seq, self.sibling))

    def arrive(self, step):
        for copy in self.copies(step):
            copy.wait_recv()

    def forward(self, step):
        for copy in self.hops(step):
            copy.start()

    def cross(self):
        part = self.block.at[:, pl.ds(pl.multiple_of(self.beside * self.own, self.own), self.own)]
        at = self.ranks
        return push(part, part, self.core_send.at[at], self.core_recv.at[at], (self.seq, self.sibling))

    def complete(self):
        for step in range(self.half + 1):
            for copy in self.hops(step):
                copy.wait_recv()
        self.cross().start()
        self.cross().wait_recv()

    def finish(self):
        for step in range(1, self.half + 1):
            for copy in self.copies(step):
                copy.wait_send()
        for step in range(self.half + 1):
            for copy in self.hops(step):
                copy.wait_send()
        self.cross().wait_send()


def whole_sems(ranks):
    return (
        ring_sems(ranks)
        + [pltpu.SemaphoreType.DMA((ranks,))] * 2
        + [pltpu.SemaphoreType.DMA((ranks + 1,))] * 2
    )


class Reduce:
    def __init__(self, grads, from_core, from_y, total, own, first, count, cols, sems):
        self.grads, self.from_core, self.from_y, self.total = grads, from_core, from_y, total
        self.own, self.begin, self.count, self.cols = own, first, count, cols
        self.send, self.recv = sems
        self.seq, dp = lax.axis_index("seq"), lax.axis_index("dp")
        self.y, self.core = lax.div(dp, 2), lax.rem(dp, 2)
        self.beside, self.sibling = (1 - self.y) * 2 + self.core, self.y * 2 + 1 - self.core

    def at(self, y, core):
        return pl.ds(pl.multiple_of((y * 2 + core) * self.own, self.own), self.own)

    def hop(self, number):
        some, cols = pl.ds(self.begin, self.count), self.cols
        if number == 2:
            src, dst, to = self.from_core.at[0, some, :, cols], self.from_y.at[some, :, cols], self.beside
        else:
            rows = self.at(1 - self.y if number == 0 else self.y, 1 - self.core)
            src, dst, to = self.grads.at[some, rows, cols], self.from_core.at[number, some, :, cols], self.sibling
        return push(src, dst, self.send.at[number], self.recv.at[number], (self.seq, to))

    def first(self):
        self.hop(0).start()
        self.hop(1).start()

    def second(self):
        self.hop(0).wait_recv()
        rows = self.at(1 - self.y, self.core)

        def some(at, _):
            value = self.grads[at, rows, self.cols].astype(jnp.float32)
            value = value + self.from_core[0, at, :, self.cols].astype(jnp.float32)
            self.from_core[0, at, :, self.cols] = value.astype(LOW)
            return 0

        lax.fori_loop(self.begin, self.begin + self.count, some, 0)
        self.hop(2).start()

    def third(self):
        self.hop(1).wait_recv()
        self.hop(2).wait_recv()
        rows = self.at(self.y, self.core)

        def some(at, _):
            value = self.grads[at, rows, self.cols].astype(jnp.float32)
            value = value + self.from_core[1, at, :, self.cols].astype(jnp.float32)
            value = value + self.from_y[at, :, self.cols].astype(jnp.float32)
            self.total[at, :, self.cols] = value.astype(LOW)
            return 0

        lax.fori_loop(self.begin, self.begin + self.count, some, 0)

    def finish(self):
        for number in range(3):
            self.hop(number).wait_send()


def reduce_sems():
    return [pltpu.SemaphoreType.DMA((3,)), pltpu.SemaphoreType.DMA((3,))]


def reduce_bufs(ranks, own, cols):
    return [pltpu.VMEM((2, ranks, own, cols), LOW), pltpu.VMEM((ranks, own, cols), LOW)]


class Deliver:
    def __init__(self, rows, out, cols, ranks, sems):
        self.rows, self.out, self.cols, self.ranks = rows, out, cols, ranks
        self.send, self.recv, self.here = sems
        self.seq, self.dp = lax.axis_index("seq"), lax.axis_index("dp")

    def exchange(self):
        for step in range(1, self.ranks):
            peer = lax.rem(self.seq + step, self.ranks)
            yield push(
                self.rows.at[peer, :, self.cols],
                self.out.at[self.seq, :, self.cols],
                self.send.at[step],
                self.recv.at[step],
                (peer, self.dp),
            )

    def keep(self):
        return pltpu.make_async_copy(
            self.rows.at[self.seq, :, self.cols], self.out.at[self.seq, :, self.cols], self.here
        )

    def start(self):
        self.keep().start()
        for copy in self.exchange():
            copy.start()

    def finish(self):
        self.keep().wait()
        for copy in self.exchange():
            copy.wait_recv()
        for copy in self.exchange():
            copy.wait_send()


def deliver_sems(ranks):
    return [pltpu.SemaphoreType.DMA((ranks,)), pltpu.SemaphoreType.DMA((ranks,)), pltpu.SemaphoreType.DMA]


def enter_kernel(
    ranks, order, starts, tokens, freqs, attn_gain, mlp_gain, w_query, w_key, w_value, w_output, w_gate, w_up, w_down,
    first_in, qkv, attn_block, mlp_rows, x_all, out_block, cosv, sinv, pos, begins, pos_row,
    held, normal, kept, block, a_rows, m_rows, gate, up, down, whole, *sems,
):
    local, width = tokens.shape
    own = w_query.shape[0]
    size = freqs.shape[1]
    cols = qkv.shape[1]
    half = ranks // 2
    local_sems = sems[7]
    seq, dp = lax.axis_index("seq"), lax.axis_index("dp")
    right, left = neighbours(ranks)
    attn = Spread(a_rows, block, ranks, own, pl.ds(0, a_rows.shape[2]), sems[2:7])
    peers = [(lax.rem(seq + step, ranks), dp) for step in range(1, ranks)]
    peers += [(seq, attn.beside), (seq, attn.sibling)]
    knock(peers)
    loads = [
        move(src, dst, local_sems.at[at])
        for at, (src, dst) in enumerate(((w_gate, gate), (w_up, up), (w_down, down)))
    ]
    row = functools.partial(block_row, local=local, ranks=ranks)
    held[pl.ds(row(0), local)] = tokens[...]

    def column(row):
        same = lax.broadcasted_iota(jnp.int32, (own, own), 0) == lax.broadcasted_iota(jnp.int32, (own, own), 1)
        return jnp.sum(jnp.where(same, row, 0.0), 1, keepdims=True)

    def lay(target, first, weight, gain):
        each = weight.shape[1] // ranks
        for rank in range(ranks):
            part = weight[:, rank * each : (rank + 1) * each]
            if gain is not None:
                part = (part.astype(jnp.float32) * gain).astype(LOW)
            target[rank, :, first : first + each] = part
        return first + each

    gain = column(attn_gain[...])
    at = 0
    for weight in (w_query, w_key, w_value):
        at = lay(a_rows, at, weight, gain)
    whole[seq, pl.ds(pl.multiple_of(dp * own, own), own)] = w_output[...]
    answered(peers)
    ring = RingGather(held, local, ranks, sems[0], sems[1], right, left, row)
    outs = WholeGather(whole, ranks, own, sems[8:14])
    ring.start(1)
    attn.start()
    outs.start(1)
    outs.forward(0)
    stores = []

    def scale_rows(step):
        for rel in rels_of(step, ranks):

            def some(at, _):
                rows = pl.ds(pl.multiple_of(row(rel) + at * 32, 32), 32)
                normal[rows] = rows_scaled(held[rows].astype(jnp.float32))[0].astype(LOW)
                return 0

            lax.fori_loop(0, local // 32, some, 0)

    def project(step):
        rels = rels_of(step, ranks)
        value = dot_nn(block_rows(normal, rels, local, ranks), block[...].reshape(width, cols))
        for at, rel in enumerate(rels):
            kept[pl.ds(row(rel), local)] = value[at * local : (at + 1) * local]

    for load in loads:
        load.wait()
    gain = column(mlp_gain[...])
    each = gate.shape[1] // ranks
    lay(m_rows, 0, gate, gain)
    lay(m_rows, each, up, gain)
    lay(m_rows, 2 * each, down, None)
    stores.append(move(m_rows, mlp_rows, local_sems.at[len(stores)]))
    scale_rows(0)
    def both(step):
        ring.arrive(step)
        if step < half:
            ring.start(step + 1)
        outs.arrive(step)
        if step < half:
            outs.start(step + 1)
        outs.forward(step)
        scale_rows(step)

    both(1)
    attn.arrive()
    attn.hop(0).start()
    attn.hop(1).start()
    spans = order.shape[0]
    span = local * ranks // spans
    for at in range(ranks):
        rows = pl.ds(at * local, local)
        ids = at * local + lax.broadcasted_iota(jnp.int32, (1, local), 1)
        where = jnp.zeros_like(ids)
        for slot in range(spans):
            inside = (ids >= slot * span) & (ids < (slot + 1) * span)
            where = where + jnp.where(inside, ids + (order[slot] - slot) * span, 0)
        first = jnp.zeros_like(ids)
        for doc in range(starts.shape[1]):
            first = jnp.maximum(first, jnp.where(starts[0, doc] <= where, starts[0, doc], 0))
        pos_row[:, rows] = where
        across = jnp.broadcast_to(where, (local, local)).T
        pos[rows] = across[:, :1]
        begins[rows] = jnp.broadcast_to(first, (local, local)).T[:, :1]
        angle = across[:, :1].astype(jnp.float32) * freqs[...]
        lane = lax.broadcasted_iota(jnp.int32, (local, size), 1)
        cosv[rows] = jnp.cos(angle)
        sine = jnp.sin(angle)
        sinv[rows] = jnp.where(lane < size // 2, -sine, sine)
    both(2)
    attn.hop(0).wait_recv()
    attn.hop(2).start()
    for step in range(3, half):
        both(step)
    attn.hop(1).wait_recv()
    attn.hop(2).wait_recv()
    stores.append(move(block, attn_block, local_sems.at[len(stores)]))
    for step in range(half):
        project(step)
    both(half)
    stores.append(move(held, x_all, local_sems.at[len(stores)]))
    stores.append(move(normal, first_in, local_sems.at[len(stores)]))
    project(half)
    stores.append(move(kept, qkv, local_sems.at[len(stores)]))
    outs.complete()
    stores.append(move(whole, out_block, local_sems.at[len(stores)]))
    ring.finish()
    outs.finish()
    attn.finish()
    for store in stores:
        store.wait()


def attend_kernel(
    ranks, kv_heads, out_grad, qkv, cosv, sinv, pos, begins, pos_row, query_gain, key_gain, mlp_rows, x_all, out_block,
    q_low, k_low, v_low, resid, out_low, second, dy_all, prob, mlp_block,
    dys, probs, xs, whole, sums, outs, *sems,
):
    local, width = out_grad.shape
    rows = local * ranks
    size = cosv.shape[1]
    heads = q_low.shape[0]
    share = heads // kv_heads
    half = ranks // 2
    scale = 1.0 / math.sqrt(size)
    o_cols = heads * size
    deep = whole.shape[1]
    right, left = neighbours(ranks)
    seq, dp = lax.axis_index("seq"), lax.axis_index("dp")
    own = mlp_rows.shape[1]
    third = mlp_rows.shape[2] // 3
    mlp = [
        Spread(mlp_rows, mlp_block, ranks, own, pl.ds(at * third, third), sems[4 + 5 * at : 9 + 5 * at])
        for at in range(3)
    ]
    local_sems = sems[19]
    peers = [(lax.rem(seq + step, ranks), dp) for step in range(1, ranks)]
    peers += [(seq, mlp[0].beside), (seq, mlp[0].sibling)]
    knock(peers)
    loads = [move(x_all, xs, local_sems.at[0]), move(out_block, whole, local_sems.at[1])]
    row = functools.partial(block_row, local=local, ranks=ranks)
    dys[pl.ds(row(0), local)] = out_grad[...]
    answered(peers)
    ring = RingGather(dys, local, ranks, sems[0], sems[1], right, left, row)
    for piece in mlp:
        piece.start()
    ring.start(1)
    tile = rows // half
    stores = []

    def rotated(at, rows_at, gain):
        v = rows_scaled(qkv[rows_at, at * size : (at + 1) * size])[0] * gain[...]
        return (v * cosv[rows_at] + turn(v) * sinv[rows_at]).astype(LOW)

    for piece in range(half):
        rows_at = pl.ds(piece * tile, tile)
        for head in range(heads):
            q_low[head, rows_at] = rotated(head, rows_at, query_gain)
        for group in range(kv_heads):
            k_low[group, rows_at] = rotated(heads + group, rows_at, key_gain)
            at = (heads + kv_heads + group) * size
            v_low[group, rows_at] = qkv[rows_at, at : at + size].astype(LOW)

    def forward(piece):
        mlp[piece].arrive()
        mlp[piece].hop(0).start()
        mlp[piece].hop(1).start()

    for piece in range(half):
        rows_at = pl.ds(piece * tile, tile)
        seen = (pos_row[...] <= pos[rows_at]) & (pos_row[...] >= begins[rows_at])
        for head in range(heads):
            raw = dot_nt(q_low[head, rows_at], k_low[head // share]) * scale
            raw = jnp.where(seen, raw, NEG)
            weight = jnp.exp(raw - jnp.max(raw, -1, keepdims=True))
            weight = (weight * (1.0 / jnp.sum(weight, -1, keepdims=True))).astype(LOW)
            probs[head, rows_at] = weight
            value = dot_nn(weight, v_low[head // share])
            outs[rows_at, head * size : (head + 1) * size] = value.astype(LOW)
            stores.append(move(probs.at[head, rows_at], prob.at[head, rows_at], local_sems.at[2 + len(stores)]))
        if piece == 1:
            ring.arrive(1)
            ring.start(2)
        if piece >= 2:
            forward(piece - 2)
        if piece == half - 1:
            ring.arrive(2)
            ring.start(3)
    slots = {rel: at * rows for at, rel in enumerate(ring_order(ranks))}
    gather = RingGather(outs, rows, ranks, sems[2], sems[3], right, left, slots.get, True)
    gather.start(1)
    stores.append(move(outs.at[pl.ds(0, rows)], out_low, local_sems.at[2 + len(stores)]))
    for load in loads:
        load.wait()
    place = ring_place(seq, ranks)
    wide = 256

    def add(step):
        rels = rels_of(step, ranks)
        cols_of = [
            pl.ds(pl.multiple_of(ring_seq(lax.rem(place + rel, ranks), ranks) * o_cols, o_cols), o_cols)
            for rel in rels
        ]

        def some(at, _):
            cols = pl.ds(pl.multiple_of(lax.rem(at, ranks) * deep, deep), deep)
            begin = pl.multiple_of(lax.div(at, ranks) * wide, wide)
            rows_at = pl.ds(begin, wide)
            value = xs[rows_at, cols].astype(jnp.float32) if step == 0 else sums[rows_at, cols]
            for rel, own_cols in zip(rels, cols_of):
                part = outs[pl.ds(slots[rel] + begin, wide)]
                value = value + dot_nt(part, whole[lax.rem(at, ranks), :, own_cols])
            sums[rows_at, cols] = value
            return 0

        lax.fori_loop(0, ranks * rows // wide, some, 0)

    add(0)
    forward(2)
    for step in range(1, half + 1):
        gather.arrive(step)
        if step < half:
            gather.start(step + 1)
        if step == 1:
            for later in range(3, half):
                ring.arrive(later)
                ring.start(later + 1)
        add(step)
        if step < 4:
            mlp[step - 1].hop(0).wait_recv()
            mlp[step - 1].hop(2).start()

    def some(at, _):
        rows_at = pl.ds(pl.multiple_of(at * 32, 32), 32)
        xs[rows_at] = rows_scaled(sums[rows_at])[0].astype(LOW)
        return 0

    lax.fori_loop(0, rows // 32, some, 0)
    stores.append(move(xs, second, local_sems.at[2 + len(stores)]))
    resid[...] = sums[pl.ds(row(0), local)]
    ring.arrive(half)
    stores.append(move(dys, dy_all, local_sems.at[2 + len(stores)]))
    gather.finish()
    ring.finish()
    for piece in mlp:
        piece.hop(1).wait_recv()
        piece.hop(2).wait_recv()
        piece.finish()
    for store in stores:
        store.wait()


def mlp_kernel(
    ranks, out_grad, rest, second, dys, mlp_block, block_out, dresid, dresid_low, gain_grad, own_grads,
    grads, from_core, from_y, held, weights, hidden, dgu, resid, dy_all,
    term, out_buf, in_buf, y_out, y_in, here, *sems,
):
    local, width = out_grad.shape
    row = functools.partial(block_row, local=local, ranks=ranks)
    ff = hidden.shape[1]
    deep = weights.shape[1]
    half = ranks // 2
    right, left = neighbours(ranks)
    loads = [
        move(src, dst, here.at[at])
        for at, (src, dst) in enumerate(((mlp_block, weights), (dys, dy_all), (rest, resid), (second, held)))
    ]
    seq, dp = lax.axis_index("seq"), lax.axis_index("dp")
    own = own_grads.shape[1]
    pieces = [
        Reduce(
            grads, from_core, from_y, own_grads, own, at * ranks // 4, ranks // 4, pl.ds(0, 3 * ff),
            sems[4 + 2 * at : 6 + 2 * at],
        )
        for at in range(4)
    ]
    peers = [right, left, (seq, pieces[0].beside), (seq, pieces[0].sibling)]
    knock(peers)
    answered(peers)
    for at in (0, 1, 3):
        loads[at].wait()
    wide = 256

    def middle(begin, count, tall):
        def some(at, _):
            rows = pl.ds(pl.multiple_of(begin + lax.div(at, ff // wide) * tall, tall), tall)
            first = pl.multiple_of(lax.rem(at, ff // wide) * wide, wide)
            gate = dot_nn(held[rows], weights[:, :, pl.ds(first, wide)].reshape(width, wide))
            upper = dot_nn(held[rows], weights[:, :, pl.ds(ff + first, wide)].reshape(width, wide))
            dmid = dot_nn(dy_all[rows], weights[:, :, pl.ds(2 * ff + first, wide)].reshape(width, wide))
            sigma = 1.0 / (1.0 + jnp.exp(-gate))
            act = gate * sigma
            hidden[rows, pl.ds(first, wide)] = (act * upper).astype(LOW)
            slope = sigma * (1.0 + gate * (1.0 - sigma))
            dgu[rows, pl.ds(first, wide)] = (dmid * upper * slope).astype(LOW)
            dgu[rows, pl.ds(ff + first, wide)] = (dmid * act).astype(LOW)
            return 0

        lax.fori_loop(0, count // tall * (ff // wide), some, 0)

    middle(row(half), local, local)

    def back_part(rels):
        given, count = block_rows(dgu, rels, local, ranks), len(rels) * local

        def some(at, _):
            value = dot_nt(given, weights[at, :, : 2 * ff])
            term[:count, pl.ds(pl.multiple_of(at * deep, deep), deep)] = value
            return 0

        lax.fori_loop(0, ranks, some, 0)

    def out_part(rels):
        given, count = block_rows(hidden, rels, local, ranks), len(rels) * local

        def some(at, _):
            value = dot_nt(given, weights[at, :, 2 * ff :])
            term[:count, pl.ds(pl.multiple_of(at * deep, deep), deep)] = value
            return 0

        lax.fori_loop(0, ranks, some, 0)

    def weight_grads(first, count):
        def some(at, _):
            cols = pl.ds(pl.multiple_of(at * deep, deep), deep)
            grads[at, :, : 2 * ff] = dot_tn(held[:, cols], dgu[...]).astype(LOW)
            grads[at, :, 2 * ff :] = dot_tn(dy_all[:, cols], hidden[...]).astype(LOW)
            return 0

        lax.fori_loop(first, first + count, some, 0)

    back = RingSum(back_part, term, out_buf, in_buf, local, ranks, sems[0], sems[1], right, left)
    out = RingSum(out_part, term, y_out, y_in, local, ranks, sems[2], sems[3], right, left)
    for step in range(1, half + 1):
        back.compute(step)
        back.launch(step)
        out.compute(step)
        out.launch(step)
        if step == 1:
            middle(0, local * ranks, 2 * local)
        if step < 3:
            for piece in pieces[2 * step - 2 : 2 * step]:
                weight_grads(piece.begin, piece.count)
                piece.first()
        if 1 < step < 4:
            for piece in pieces[2 * step - 4 : 2 * step - 2]:
                piece.second()
        if step > 2:
            for piece in pieces[2 * step - 6 : 2 * step - 4]:
                piece.third()
    back.compute(half + 1)
    loads[2].wait()
    back.arrive_last()
    gain_grad[...] = jnp.zeros_like(gain_grad)

    def finish_back(at, _):
        begin = pl.multiple_of(at * 32, 32)
        rows = pl.ds(begin, 32)
        value = resid[rows]
        normal, inv = rows_scaled(value)
        grad = back.last(begin, 32)
        full = out_grad[rows].astype(jnp.float32) + rows_scaled_back(value, inv, grad)
        dresid[rows] = full
        dresid_low[rows] = full.astype(LOW)
        gain_grad[...] += jnp.sum(grad * normal, 0, keepdims=True)
        return 0

    lax.fori_loop(0, local // 32, finish_back, 0)
    out.compute(half + 1)
    out.arrive_last()

    def finish_out(at, _):
        begin = pl.multiple_of(at * 32, 32)
        rows = pl.ds(begin, 32)
        block_out[rows] = (resid[rows] + out.last(begin, 32)).astype(LOW)
        return 0

    lax.fori_loop(0, local // 32, finish_out, 0)
    back.finish()
    out.finish()
    for piece in pieces:
        piece.finish()


def back_kernel(
    ranks, kv_heads, tokens, dresid_low, query_gain, key_gain, mlp_gain_part, out_low_in, first_in_in, block_in,
    qkv_in, cos_in, sin_in, q_in, k_in, v_in, prob_in, dresid_in, mlp_own, out_block,
    tokens_grad, gains, mlp_sums, attn_sums,
    grads, from_core, from_y, own_grads, gain_grad, query_gain_grad, key_gain_grad,
    tiles, tiles_in, tile_sums, tile_sums_in, held, dout, dk, dv, dqkv,
    out_low, first_in, attn_block, qkv, cosv, sinv, q_low, k_low, v_low, prob, dresid, w_output,
    term, out_buf, in_buf, *sems,
):
    local, width = tokens.shape
    rows = local * ranks
    half = ranks // 2
    size = cosv.shape[1]
    heads = q_low.shape[0]
    share = heads // kv_heads
    scale = 1.0 / math.sqrt(size)
    cols = (heads + 2 * kv_heads) * size
    deep = attn_block.shape[1]
    o_cols = heads * size
    right, left = neighbours(ranks)
    seq, dp = lax.axis_index("seq"), lax.axis_index("dp")
    own = mlp_own.shape[1]
    copies = tiles.shape[1]
    all_cols = grads.shape[2]
    out_piece = Reduce(
        grads, from_core, from_y, own_grads, own, 0, ranks, pl.ds(cols, all_cols - cols), sems[4:6]
    )
    qkv_piece = Reduce(grads, from_core, from_y, own_grads, own, 0, ranks, pl.ds(0, cols), sems[6:8])
    mlp_way = Deliver(mlp_own, mlp_sums, pl.ds(0, mlp_own.shape[2]), ranks, sems[8:11])
    out_way = Deliver(own_grads, attn_sums, pl.ds(cols, all_cols - cols), ranks, sems[11:14])
    qkv_way = Deliver(own_grads, attn_sums, pl.ds(0, cols), ranks, sems[14:17])
    peers = [(lax.rem(seq + step, ranks), dp) for step in range(1, ranks)]
    peers += [(seq, lax.rem(dp + step, copies)) for step in range(1, copies)]
    knock(peers)
    local_sems = sems[21]
    loads = {}
    for at, (name, src, dst) in enumerate(
        (
            ("w_output", out_block.at[:, :, pl.ds(pl.multiple_of(seq * o_cols, o_cols), o_cols)], w_output),
            ("block", block_in, attn_block), ("out", out_low_in, out_low), ("v", v_in, v_low),
            ("prob", prob_in, prob), ("k", k_in, k_low), ("q", q_in, q_low), ("cos", cos_in, cosv),
            ("sin", sin_in, sinv), ("qkv", qkv_in, qkv), ("first", first_in_in, first_in),
            ("dresid", dresid_in, dresid),
        )
    ):
        loads[name] = move(src, dst, local_sems.at[at])
    row = functools.partial(block_row, local=local, ranks=ranks)
    held[pl.ds(row(0), local)] = dresid_low[...]
    answered(peers)
    ring = RingGather(held, local, ranks, sems[0], sems[1], right, left, row)
    ring.start(1)
    loads["w_output"].wait()
    loads["block"].wait()

    def project(step):
        rels = rels_of(step, ranks)
        value = dot_nn(block_rows(held, rels, local, ranks), w_output[...].reshape(width, o_cols)).astype(LOW)
        for at, rel in enumerate(rels):
            dout[pl.ds(row(rel), local)] = value[at * local : (at + 1) * local]

    project(0)
    for step in range(1, half + 1):
        ring.arrive(step)
        if step < half:
            ring.start(step + 1)
        if step == half - 1:
            mlp_way.start()
        project(step)
    loads["out"].wait()

    def out_grads(at, _):
        some_cols = pl.ds(pl.multiple_of(at * deep, deep), deep)
        grads[at, :, cols:] = dot_tn(held[:, some_cols], out_low[...]).astype(LOW)
        return 0

    lax.fori_loop(0, ranks, out_grads, 0)
    out_piece.first()
    for name in ("v", "prob", "k", "q", "cos", "sin", "qkv"):
        loads[name].wait()
    tile = rows // half
    query_gain_grad[...] = jnp.zeros_like(query_gain_grad)
    key_gain_grad[...] = jnp.zeros_like(key_gain_grad)

    def unrotated(grad, column, rows_at, gain, gain_grad_ref):
        grad = grad * cosv[rows_at] - turn(grad) * sinv[rows_at]
        value = qkv[rows_at, column * size : (column + 1) * size]
        normal, inv = rows_scaled(value)
        gain_grad_ref[...] += jnp.sum(grad * normal, 0, keepdims=True)
        back = rows_scaled_back(value, inv, grad * gain[...])
        dqkv[rows_at, column * size : (column + 1) * size] = back.astype(LOW)

    for head in range(heads):
        group = head // share

        def one(piece, _):
            rows_at = pl.ds(pl.multiple_of(piece * tile, tile), tile)
            weight = prob[head, rows_at]
            grad = dout[rows_at, head * size : (head + 1) * size]
            dprob = dot_nt(grad, v_low[group])
            full = weight.astype(jnp.float32)
            delta = jnp.sum(full * dprob, -1, keepdims=True)
            dscore = (full * (dprob - delta)).astype(LOW)
            dq = dot_nn(dscore, k_low[group]) * scale
            dk_add = dot_tn(dscore, q_low[head, rows_at]) * scale
            dv_add = dot_tn(weight, grad)
            dk[group] += dk_add
            dv[group] += dv_add
            unrotated(dq, head, rows_at, query_gain, query_gain_grad)
            return 0

        if head % share == 0:
            dk[group] = jnp.zeros_like(dk[group])
            dv[group] = jnp.zeros_like(dv[group])
        lax.fori_loop(0, half, one, 0)
        if head == 0:
            out_piece.second()
    for group in range(kv_heads):
        def one_key(piece, _):
            rows_at = pl.ds(pl.multiple_of(piece * tile, tile), tile)
            unrotated(dk[group, rows_at], heads + group, rows_at, key_gain, key_gain_grad)
            at = (heads + kv_heads + group) * size
            dqkv[rows_at, at : at + size] = dv[group, rows_at].astype(LOW)
            return 0

        lax.fori_loop(0, half, one_key, 0)

    def part(rels):
        given, count = block_rows(dqkv, rels, local, ranks), len(rels) * local

        def some(at, _):
            value = dot_nt(given, attn_block[at])
            term[:count, pl.ds(pl.multiple_of(at * deep, deep), deep)] = value
            return 0

        lax.fori_loop(0, ranks, some, 0)

    def qkv_grads(at, _):
        some_cols = pl.ds(pl.multiple_of(at * deep, deep), deep)
        grads[at, :, :cols] = dot_tn(first_in[:, some_cols], dqkv[...]).astype(LOW)
        return 0

    total = RingSum(part, term, out_buf, in_buf, local, ranks, sems[2], sems[3], right, left)
    for step in range(1, half + 1):
        total.compute(step)
        total.launch(step)
        if step == 1:
            loads["first"].wait()
            lax.fori_loop(0, ranks, qkv_grads, 0)
            qkv_piece.first()
            out_piece.third()
            out_way.start()
        if step == 2:
            qkv_piece.second()
        if step == half - 1:
            qkv_piece.third()
            qkv_way.start()
    total.compute(half + 1)
    loads["dresid"].wait()
    total.arrive_last()
    gain_grad[...] = jnp.zeros_like(gain_grad)

    def last(at, _):
        begin = pl.multiple_of(at * 32, 32)
        rows_at = pl.ds(begin, 32)
        value = tokens[rows_at].astype(jnp.float32)
        normal, inv = rows_scaled(value)
        grad = total.last(begin, 32)
        tokens_grad[rows_at] = dresid[rows_at] + rows_scaled_back(value, inv, grad)
        gain_grad[...] += jnp.sum(grad * normal, 0, keepdims=True)
        return 0

    lax.fori_loop(0, local // 32, last, 0)
    lane = lax.broadcasted_iota(jnp.int32, (1, size), 1)
    per_row = size // own
    for number in range(ranks * copies):
        at = number // per_row
        first = gain_grad[:, at * size : (at + 1) * size]
        second = mlp_gain_part[:, at * size : (at + 1) * size]
        shift = number % per_row * own
        first = pltpu.roll(first, (size - shift) % size, 1) if shift else first
        second = pltpu.roll(second, (size + own - shift) % size, 1) if shift != own else second
        tile_at = tiles.at[number // copies, number % copies]
        tile_at[0:1] = jnp.where(lane < own, first, second)
        tile_at[1:2] = query_gain_grad[...]
        tile_at[2:3] = key_gain_grad[...]
        tile_at[3:] = jnp.zeros((tiles.shape[2] - 3, size), jnp.float32)

    def to_ranks(step):
        peer = lax.rem(seq + step, ranks)
        return push(tiles.at[peer], tiles_in.at[seq], sems[17].at[step], sems[18].at[step], (peer, dp))

    def to_copies(step):
        peer = lax.rem(dp + step, copies)
        return push(
            tile_sums.at[peer], tile_sums_in.at[dp], sems[19].at[step], sems[20].at[step], (seq, peer)
        )

    for step in range(1, ranks):
        to_ranks(step).start()
    tiles_in[seq] = tiles[seq]
    for step in range(1, ranks):
        to_ranks(step).wait_recv()
    tile_sums[...] = jnp.sum(tiles_in[...], 0)
    for step in range(1, copies):
        to_copies(step).start()
    tile_sums_in[dp] = tile_sums[dp]
    for step in range(1, copies):
        to_copies(step).wait_recv()
    gains[...] = jnp.sum(tile_sums_in[...], 0)
    for step in range(1, ranks):
        to_ranks(step).wait_send()
    for step in range(1, copies):
        to_copies(step).wait_send()
    ring.finish()
    total.finish()
    out_piece.finish()
    qkv_piece.finish()
    mlp_way.finish()
    out_way.finish()
    qkv_way.finish()


def leave_kernel(attn_sums, mlp_sums, gains, attn_gain, mlp_gain, *outs):
    own = attn_gain.shape[1]
    same = lax.broadcasted_iota(jnp.int32, (own, own), 0) == lax.broadcasted_iota(jnp.int32, (own, own), 1)

    def column(row):
        return jnp.sum(jnp.where(same, row, 0.0), 1, keepdims=True)

    first, second = column(attn_gain[...]), column(mlp_gain[...])
    for sums, parts in ((attn_sums, zip(outs[:4], (first, first, first, None))), (mlp_sums, zip(outs[4:7], (second, second, None)))):
        at = 0
        for out, gain in parts:
            value = sums[0, :, at : at + out.shape[1]].astype(jnp.float32)
            out[...] = value if gain is None else value * gain
            at += out.shape[1]
    outs[7][...] = gains[0:1, :own] / attn_gain[...]
    outs[8][...] = gains[0:1, own : 2 * own] / mlp_gain[...]


VM = pl.BlockSpec(memory_space=pltpu.VMEM)
SM = pl.BlockSpec(memory_space=pltpu.SMEM)
ANY = pl.BlockSpec(memory_space=pl.ANY)


def call(kernel, number, ins, outs, scratch, operands):
    return pl.pallas_call(
        kernel,
        out_shape=[jax.ShapeDtypeStruct(shape, dtype) for shape, dtype, _ in outs],
        in_specs=ins,
        out_specs=[spec for _, _, spec in outs],
        scratch_shapes=scratch,
        compiler_params=pltpu.CompilerParams(
            collective_id=number, has_side_effects=True, vmem_limit_bytes=LIMIT
        ),
    )(*operands)


def columns_body(
    tokens,
    out_grad,
    span_order,
    doc_starts,
    w_query,
    w_key,
    w_value,
    w_output,
    attn_gain,
    query_gain,
    key_gain,
    w_gate,
    w_up,
    w_down,
    mlp_gain,
):
    ranks = lax.axis_size("seq")
    copies = lax.axis_size("dp")
    _, local, width = tokens.shape
    rows = local * ranks
    size = query_gain.shape[0]
    kv_heads = w_key.shape[1] // size // ranks
    heads = w_query.shape[1] // size // ranks
    q_cols, kv_cols = heads * size, kv_heads * size
    qkv_cols = q_cols + 2 * kv_cols
    a_cols = qkv_cols + q_cols
    ff = w_gate.shape[1] // ranks
    own = width // (ranks * copies)
    deep = own * copies
    half = ranks // 2
    f32, i32 = jnp.float32, jnp.int32
    exponents = np.arange(size) % (size // 2) * (-2.0 / size * math.log(1000000.0))
    freqs = jnp.asarray(np.exp(exponents)[None], f32)
    first_in, qkv, attn_block, mlp_rows, x_all, wo_all, cosv, sinv, pos, begins, pos_row = call(
        functools.partial(enter_kernel, ranks),
        1,
        [SM, SM] + [VM] * 8 + [ANY] * 3,
        [
            ((rows, width), LOW, ANY),
            ((rows, qkv_cols), f32, ANY),
            ((ranks, deep, qkv_cols), LOW, ANY),
            ((ranks, own, 3 * ff), LOW, ANY),
            ((rows, width), LOW, ANY),
            ((ranks, deep, q_cols * ranks), LOW, ANY),
            ((rows, size), f32, VM),
            ((rows, size), f32, VM),
            ((rows, 1), i32, VM),
            ((rows, 1), i32, VM),
            ((1, rows), i32, VM),
        ],
        [
            pltpu.VMEM((rows, width), LOW),
            pltpu.VMEM((rows, width), LOW),
            pltpu.VMEM((rows, qkv_cols), f32),
            pltpu.VMEM((ranks, deep, qkv_cols), LOW),
            pltpu.VMEM((ranks, own, qkv_cols), LOW),
            pltpu.VMEM((ranks, own, 3 * ff), LOW),
        ]
        + [pltpu.VMEM((own, ff * ranks), LOW)] * 3
        + [pltpu.VMEM((ranks, deep, q_cols * ranks), LOW)]
        + ring_sems(ranks)
        + spread_sems(ranks)
        + [pltpu.SemaphoreType.DMA((2 * half + 6,))]
        + whole_sems(ranks),
        (
            span_order, doc_starts, tokens[0], freqs, attn_gain[None], mlp_gain[None], w_query, w_key, w_value,
            w_output, w_gate, w_up, w_down,
        ),
    )
    q_gain, k_gain = query_gain[None], key_gain[None]
    q_low, k_low, v_low, resid, out_low, second, dy_all, prob, mlp_block = call(
        functools.partial(attend_kernel, ranks, kv_heads),
        2,
        [VM] * 9 + [ANY] * 3,
        [
            ((heads, rows, size), LOW, VM),
            ((kv_heads, rows, size), LOW, VM),
            ((kv_heads, rows, size), LOW, VM),
            ((local, width), f32, VM),
            ((rows, q_cols), LOW, ANY),
            ((rows, width), LOW, ANY),
            ((rows, width), LOW, ANY),
            ((heads, rows, rows), LOW, ANY),
            ((ranks, deep, 3 * ff), LOW, ANY),
        ],
        [
            pltpu.VMEM((rows, width), LOW),
            pltpu.VMEM((heads, rows, rows), LOW),
            pltpu.VMEM((rows, width), LOW),
            pltpu.VMEM((ranks, deep, q_cols * ranks), LOW),
            pltpu.VMEM((rows, width), f32),
            pltpu.VMEM((ranks * rows, q_cols), LOW),
        ]
        + ring_sems(ranks) * 2
        + spread_sems(ranks) * 3
        + [pltpu.SemaphoreType.DMA((heads * half + 5,))],
        (
            out_grad[0], qkv, cosv, sinv, pos, begins, pos_row, q_gain, k_gain, mlp_rows, x_all, wo_all,
        ),
    )
    block_out, dresid, dresid_low, dgm, mlp_own = call(
        functools.partial(mlp_kernel, ranks),
        3,
        [VM] + [ANY] * 4,
        [
            ((local, width), LOW, VM),
            ((local, width), f32, VM),
            ((local, width), LOW, VM),
            ((1, width), f32, VM),
            ((ranks, own, 3 * ff), LOW, VM),
        ],
        [pltpu.VMEM((ranks, deep, 3 * ff), LOW)]
        + reduce_bufs(ranks, own, 3 * ff)
        + [
            pltpu.VMEM((rows, width), LOW),
            pltpu.VMEM((ranks, deep, 3 * ff), LOW),
            pltpu.VMEM((rows, ff), LOW),
            pltpu.VMEM((rows, 2 * ff), LOW),
            pltpu.VMEM((local, width), f32),
            pltpu.VMEM((rows, width), LOW),
        ]
        + sum_bufs(local, ranks, width)
        + sum_bufs(local, ranks, width)[1:]
        + [pltpu.SemaphoreType.DMA((4,))]
        + ring_sems(ranks) * 2
        + reduce_sems() * 4,
        (out_grad[0], resid, second, dy_all, mlp_block),
    )
    tokens_grad, gains, mlp_sums, attn_sums = call(
        functools.partial(back_kernel, ranks, kv_heads),
        4,
        [VM] * 5 + [ANY] * 13,
        [
            ((local, width), f32, VM),
            ((8, size), f32, VM),
            ((ranks, own, 3 * ff), LOW, ANY),
            ((ranks, own, a_cols), LOW, VM),
        ],
        [pltpu.VMEM((ranks, deep, a_cols), LOW)]
        + reduce_bufs(ranks, own, a_cols)
        + [
            pltpu.VMEM((ranks, own, a_cols), LOW),
            pltpu.VMEM((1, width), f32),
            pltpu.VMEM((1, size), f32),
            pltpu.VMEM((1, size), f32),
            pltpu.VMEM((ranks, copies, 8, size), f32),
            pltpu.VMEM((ranks, copies, 8, size), f32),
            pltpu.VMEM((copies, 8, size), f32),
            pltpu.VMEM((copies, 8, size), f32),
            pltpu.VMEM((rows, width), LOW),
            pltpu.VMEM((rows, q_cols), LOW),
            pltpu.VMEM((kv_heads, rows, size), f32),
            pltpu.VMEM((kv_heads, rows, size), f32),
            pltpu.VMEM((rows, qkv_cols), LOW),
            pltpu.VMEM((rows, q_cols), LOW),
            pltpu.VMEM((rows, width), LOW),
            pltpu.VMEM((ranks, deep, qkv_cols), LOW),
            pltpu.VMEM((rows, qkv_cols), f32),
            pltpu.VMEM((rows, size), f32),
            pltpu.VMEM((rows, size), f32),
            pltpu.VMEM((heads, rows, size), LOW),
            pltpu.VMEM((kv_heads, rows, size), LOW),
            pltpu.VMEM((kv_heads, rows, size), LOW),
            pltpu.VMEM((heads, rows, rows), LOW),
            pltpu.VMEM((local, width), f32),
            pltpu.VMEM((ranks, deep, q_cols), LOW),
        ]
        + sum_bufs(local, ranks, width)
        + ring_sems(ranks) * 2
        + reduce_sems() * 2
        + deliver_sems(ranks) * 3
        + [pltpu.SemaphoreType.DMA((ranks,))] * 2
        + [pltpu.SemaphoreType.DMA((copies,))] * 2
        + [pltpu.SemaphoreType.DMA((12,))],
        (
            tokens[0], dresid_low, q_gain, k_gain, dgm, out_low, first_in, attn_block, qkv, cosv, sinv, q_low, k_low,
            v_low, prob, dresid, mlp_own, wo_all,
        ),
    )
    whole = pl.BlockSpec((1, own), lambda at: (0, 0))
    each = (q_cols, kv_cols, kv_cols, q_cols, ff, ff, ff)
    *grads, dga, dgm = pl.pallas_call(
        leave_kernel,
        grid=(ranks,),
        out_shape=[jax.ShapeDtypeStruct((own, cols * ranks), f32) for cols in each]
        + [jax.ShapeDtypeStruct((1, own), f32)] * 2,
        in_specs=[
            pl.BlockSpec((1, own, a_cols), lambda at: (at, 0, 0)),
            pl.BlockSpec((1, own, 3 * ff), lambda at: (at, 0, 0)),
            pl.BlockSpec((8, size), lambda at: (0, 0)),
            whole,
            whole,
        ],
        out_specs=[pl.BlockSpec((own, cols), lambda at: (0, at)) for cols in each] + [whole, whole],
    )(attn_sums, mlp_sums, gains, attn_gain[None], mlp_gain[None])
    return (
        block_out[None], tokens_grad[None], *grads[:4], dga[0], gains[1], gains[2], *grads[4:], dgm[0],
    )


def body(*args):
    tokens, w_key, query_gain = args[0], args[5], args[9]
    groups = w_key.shape[1] // query_gain.shape[0]
    ranks = lax.axis_size("seq")
    if tokens.shape[0] == 1 and ranks % 2 == 0 and groups % ranks == 0 and lax.axis_size("dp") == 4:
        return columns_body(*args)
    return gathered_body(*args)


def solution(mesh):
    return jax.shard_map(
        body,
        mesh=mesh,
        in_specs=(
            P("dp", "seq", None),
            P("dp", "seq", None),
            P(),
            P("dp", None),
            P(("seq", "dp"), None),
            P(("seq", "dp"), None),
            P(("seq", "dp"), None),
            P(("seq", "dp"), None),
            P(("seq", "dp")),
            P(),
            P(),
            P(("seq", "dp"), None),
            P(("seq", "dp"), None),
            P(("seq", "dp"), None),
            P(("seq", "dp")),
        ),
        out_specs=(
            P("dp", "seq", None),
            P("dp", "seq", None),
            P(("seq", "dp"), None),
            P(("seq", "dp"), None),
            P(("seq", "dp"), None),
            P(("seq", "dp"), None),
            P(("seq", "dp")),
            P(),
            P(),
            P(("seq", "dp"), None),
            P(("seq", "dp"), None),
            P(("seq", "dp"), None),
            P(("seq", "dp")),
        ),
        check_vma=False,
    )
```

```python
import functools
import math

import jax
import jax.numpy as jnp
import numpy as np
from jax import lax
from jax.experimental import pallas as pl
from jax.experimental.pallas import tpu as pltpu
from jax.sharding import PartitionSpec as P

EPS = 1e-06
NEG = -1e30


def normed(v, gain):
    scale_inv = lax.rsqrt(jnp.mean(v * v, -1, keepdims=True) + EPS)
    return (v * scale_inv * gain, scale_inv)


def norm_back(v, scale_inv, gain, grad):
    scaled = grad * gain
    inner = jnp.mean(scaled * v, -1, keepdims=True)
    dv = scale_inv * scaled - v * scale_inv * scale_inv * scale_inv * inner
    dgain = jnp.sum((grad * v * scale_inv).reshape(-1, v.shape[-1]), 0)
    return (dv, dgain)


def rotary(pos, width):
    half = width // 2
    freqs = jnp.exp(jnp.arange(half, dtype=jnp.float32) * (-2.0 / width * math.log(1000000.0)))
    angle = pos.astype(jnp.float32)[:, None] * freqs[None, :]
    return (jnp.cos(angle)[:, None, :], jnp.sin(angle)[:, None, :])


def rotate(v, cosv, sinv):
    half = v.shape[-1] // 2
    first, second = (v[..., :half], v[..., half:])
    return jnp.concatenate([first * cosv - second * sinv, second * cosv + first * sinv], -1)


def rotate_back(grad, cosv, sinv):
    half = grad.shape[-1] // 2
    first, second = (grad[..., :half], grad[..., half:])
    return jnp.concatenate([first * cosv + second * sinv, second * cosv - first * sinv], -1)


def place(order, begin, count, span):
    rows = begin + jnp.arange(count, dtype=jnp.int32)
    slots = rows // span
    picked = slots[:, None] == jnp.arange(order.shape[0], dtype=jnp.int32)[None, :]
    return jnp.sum(jnp.where(picked, order[None, :], 0), -1) * span + rows % span


def doc_of(starts, pos):
    return jnp.sum((starts[:, None, :] <= pos[None, :, None]).astype(jnp.int32), -1)


def gathered_body(
    tokens,
    out_grad,
    span_order,
    doc_starts,
    w_query,
    w_key,
    w_value,
    w_output,
    attn_gain,
    query_gain,
    key_gain,
    w_gate,
    w_up,
    w_down,
    mlp_gain,
):
    seqs, local, width = tokens.shape
    span = local // 2
    head_size = query_gain.shape[0]
    kv_heads = w_key.shape[1] // head_size
    heads = w_query.shape[1] // head_size
    share = heads // kv_heads
    kv_width = kv_heads * head_size
    ff_width = w_gate.shape[1]
    scale = 1.0 / math.sqrt(head_size)
    total_rows = seqs * local
    own_rows = width // lax.axis_size(("seq", "dp"))
    qpos = place(span_order, lax.axis_index("seq") * local, local, span)
    qdoc = doc_of(doc_starts, qpos)
    cosv, sinv = rotary(qpos, head_size)

    def gather_attn():
        return (
            lax.all_gather(w_query, ("seq", "dp"), axis=0, tiled=True),
            lax.all_gather(w_key, ("seq", "dp"), axis=0, tiled=True),
            lax.all_gather(w_value, ("seq", "dp"), axis=0, tiled=True),
            lax.all_gather(w_output, ("seq", "dp"), axis=0, tiled=True),
            lax.all_gather(
                attn_gain.astype(jnp.bfloat16), ("seq", "dp"), axis=0, tiled=True
            ).astype(attn_gain.dtype),
        )

    def gather_mlp():
        return (
            lax.all_gather(w_gate, ("seq", "dp"), axis=0, tiled=True),
            lax.all_gather(w_up, ("seq", "dp"), axis=0, tiled=True),
            lax.all_gather(w_down, ("seq", "dp"), axis=0, tiled=True),
            lax.all_gather(mlp_gain.astype(jnp.bfloat16), ("seq", "dp"), axis=0, tiled=True).astype(
                mlp_gain.dtype
            ),
        )

    x_rows = tokens.astype(jnp.float32).reshape(total_rows, width)
    wq_all, wk_all, wv_all, wo_all, ga_all = gather_attn()
    first_norm, first_inv = normed(x_rows, ga_all)
    first_in = first_norm.astype(jnp.bfloat16)
    q_raw = jnp.dot(first_in, wq_all, preferred_element_type=jnp.float32).reshape(
        seqs, local, heads, head_size
    )
    k_raw = jnp.dot(first_in, wk_all, preferred_element_type=jnp.float32).reshape(
        seqs, local, kv_heads, head_size
    )
    v_low = (
        jnp.dot(first_in, wv_all, preferred_element_type=jnp.float32)
        .astype(jnp.bfloat16)
        .reshape(seqs, local, kv_heads, head_size)
    )
    q_normed, q_inv = normed(q_raw, query_gain)
    k_normed, k_inv = normed(k_raw, key_gain)
    q_low = rotate(q_normed, cosv, sinv).astype(jnp.bfloat16)
    k_low = rotate(k_normed, cosv, sinv).astype(jnp.bfloat16)
    q_group = q_low.reshape(seqs, local, kv_heads, share, head_size)

    def scores(piece_key, start):
        count = piece_key.shape[1]
        kpos = place(span_order, start, count, span)
        kdoc = doc_of(doc_starts, kpos)
        visible = (qdoc[:, :, None] == kdoc[:, None, :]) & (
            kpos[None, None, :] <= qpos[None, :, None]
        )
        raw = (
            jnp.einsum("sqgjd,skgd->sgjqk", q_group, piece_key, preferred_element_type=jnp.float32)
            * scale
        )
        return (raw, visible[:, None, None])

    start_top = jnp.full((seqs, kv_heads, share, local), NEG, jnp.float32)
    piece = (
        lax.all_gather(k_low, "seq", axis=1, tiled=True),
        lax.all_gather(v_low, "seq", axis=1, tiled=True),
    )
    top = start_top
    raw, visible = scores(piece[0], jnp.int32(0))
    raw = jnp.where(visible, raw, NEG)
    new_top = jnp.maximum(top, jnp.max(raw, -1))
    weights = jnp.where(visible, jnp.exp(raw - new_top[..., None]), 0.0)
    total = jnp.sum(weights, -1)
    summed = jnp.einsum(
        "sgjqk,skgd->sgjqd",
        weights.astype(jnp.bfloat16),
        piece[1],
        preferred_element_type=jnp.float32,
    )
    top, total, summed = (new_top, total, summed)
    log_total = top + jnp.log(total)
    attn_vals = summed / total[..., None]
    out_low = (
        jnp.transpose(attn_vals, (0, 3, 1, 2, 4))
        .reshape(total_rows, heads * head_size)
        .astype(jnp.bfloat16)
    )
    resid = x_rows + jnp.einsum("nh,dh->nd", out_low, wo_all, preferred_element_type=jnp.float32)
    wg_all, wu_all, wd_all, gm_all = gather_mlp()
    second_norm, second_inv = normed(resid, gm_all)
    second_in = second_norm.astype(jnp.bfloat16)
    gate = jnp.dot(second_in, wg_all, preferred_element_type=jnp.float32)
    upper = jnp.dot(second_in, wu_all, preferred_element_type=jnp.float32)
    sigma = jax.nn.sigmoid(gate)
    act = gate * sigma
    hidden = (act * upper).astype(jnp.bfloat16)
    result = resid + jnp.einsum("nf,df->nd", hidden, wd_all, preferred_element_type=jnp.float32)
    block_out = result.astype(jnp.bfloat16).reshape(seqs, local, width)
    grad_low = out_grad.reshape(total_rows, width)
    wg_all, wu_all, wd_all, gm_all = gather_mlp()
    dmid = jnp.einsum("nd,df->nf", grad_low, wd_all, preferred_element_type=jnp.float32)
    dgate = (dmid * upper * sigma * (1.0 + gate * (1.0 - sigma))).astype(jnp.bfloat16)
    dupper = (dmid * act).astype(jnp.bfloat16)
    left = second_in
    outer = grad_low
    mlp_sums = lax.psum_scatter(
        jnp.concatenate(
            [
                jnp.einsum("nd,nf->df", left, dgate, preferred_element_type=jnp.float32),
                jnp.einsum("nd,nf->df", left, dupper, preferred_element_type=jnp.float32),
                jnp.einsum("nd,nf->df", outer, hidden, preferred_element_type=jnp.float32),
            ],
            1,
        ),
        ("seq", "dp"),
        scatter_dimension=0,
        tiled=True,
    )
    dsecond = jnp.einsum(
        "nf,df->nd", dgate, wg_all, preferred_element_type=jnp.float32
    ) + jnp.einsum("nf,df->nd", dupper, wu_all, preferred_element_type=jnp.float32)
    dresid_norm, dgm = norm_back(resid, second_inv, gm_all, dsecond)
    dresid = grad_low.astype(jnp.float32) + dresid_norm
    dresid_low = dresid.astype(jnp.bfloat16)
    wq_all, wk_all, wv_all, wo_all, ga_all = gather_attn()
    dout_low = jnp.einsum(
        "nd,dh->nh", dresid_low, wo_all, preferred_element_type=jnp.float32
    ).astype(jnp.bfloat16)
    dout_group = dout_low.reshape(seqs, local, kv_heads, share, head_size)
    delta = jnp.sum(jnp.transpose(dout_group.astype(jnp.float32), (0, 2, 3, 1, 4)) * attn_vals, -1)
    piece = (
        lax.all_gather(k_low, "seq", axis=1, tiled=True),
        lax.all_gather(v_low, "seq", axis=1, tiled=True),
    )
    count = piece[0].shape[1]
    raw, visible = scores(piece[0], jnp.int32(0))
    prob = jnp.where(visible, jnp.exp(raw - log_total[..., None]), 0.0)
    dprob = jnp.einsum(
        "sqgjd,skgd->sgjqk", dout_group, piece[1], preferred_element_type=jnp.float32
    )
    dscore = (prob * (dprob - delta[..., None])).astype(jnp.bfloat16)
    dq_sum = jnp.einsum("sgjqk,skgd->sqgjd", dscore, piece[0], preferred_element_type=jnp.float32)
    dk_part = (
        jnp.einsum("sgjqk,sqgjd->skgd", dscore, q_group, preferred_element_type=jnp.float32) * scale
    )
    dv_part = jnp.einsum(
        "sgjqk,sqgjd->skgd",
        prob.astype(jnp.bfloat16),
        dout_group,
        preferred_element_type=jnp.float32,
    )
    joined = jnp.concatenate(
        [dk_part.reshape(seqs, count, kv_width), dv_part.reshape(seqs, count, kv_width)], -1
    )
    buffer = joined
    dq_sum, buffer = (dq_sum, buffer)
    key_sums = lax.psum_scatter(
        buffer.astype(jnp.bfloat16), "seq", scatter_dimension=1, tiled=True
    ).astype(jnp.float32)
    dq_rot = (dq_sum * scale).reshape(seqs, local, heads, head_size)
    dq_raw, dgq = norm_back(q_raw, q_inv, query_gain, rotate_back(dq_rot, cosv, sinv))
    dk_rot = key_sums[..., :kv_width].reshape(seqs, local, kv_heads, head_size)
    dk_raw, dgk = norm_back(k_raw, k_inv, key_gain, rotate_back(dk_rot, cosv, sinv))
    dq_low = dq_raw.reshape(total_rows, heads * head_size).astype(jnp.bfloat16)
    dk_low = dk_raw.reshape(total_rows, kv_width).astype(jnp.bfloat16)
    dv_low = key_sums[..., kv_width:].reshape(total_rows, kv_width).astype(jnp.bfloat16)
    left = first_in
    outer = dresid_low
    attn_sums = lax.psum_scatter(
        jnp.concatenate(
            [
                jnp.einsum("nd,nh->dh", left, dq_low, preferred_element_type=jnp.float32),
                jnp.einsum("nd,nh->dh", left, dk_low, preferred_element_type=jnp.float32),
                jnp.einsum("nd,nh->dh", left, dv_low, preferred_element_type=jnp.float32),
                jnp.einsum("nd,nh->dh", outer, out_low, preferred_element_type=jnp.float32),
            ],
            1,
        ),
        ("seq", "dp"),
        scatter_dimension=0,
        tiled=True,
    )
    dfirst = jnp.einsum("nh,dh->nd", dq_low, wq_all, preferred_element_type=jnp.float32)
    dfirst = dfirst + jnp.einsum("nh,dh->nd", dk_low, wk_all, preferred_element_type=jnp.float32)
    dfirst = dfirst + jnp.einsum("nh,dh->nd", dv_low, wv_all, preferred_element_type=jnp.float32)
    dx_norm, dga = norm_back(x_rows, first_inv, ga_all, dfirst)
    tokens_grad = (dresid + dx_norm).reshape(seqs, local, width)
    dga_all, dgm_all, dgq_all, dgk_all = lax.psum((dga, dgm, dgq, dgk), ("seq", "dp"))
    offset = lax.axis_index(("seq", "dp")) * own_rows
    attn_gain_grad = lax.dynamic_slice_in_dim(dga_all, offset, own_rows, 0)
    mlp_gain_grad = lax.dynamic_slice_in_dim(dgm_all, offset, own_rows, 0)
    q_cols = heads * head_size
    w_query_grad = attn_sums[:, :q_cols]
    w_key_grad = attn_sums[:, q_cols : q_cols + kv_width]
    w_value_grad = attn_sums[:, q_cols + kv_width : q_cols + 2 * kv_width]
    w_output_grad = attn_sums[:, q_cols + 2 * kv_width :]
    w_gate_grad = mlp_sums[:, :ff_width]
    w_up_grad = mlp_sums[:, ff_width : 2 * ff_width]
    w_down_grad = mlp_sums[:, 2 * ff_width :]
    return (
        block_out,
        tokens_grad,
        w_query_grad,
        w_key_grad,
        w_value_grad,
        w_output_grad,
        attn_gain_grad,
        dgq_all,
        dgk_all,
        w_gate_grad,
        w_up_grad,
        w_down_grad,
        mlp_gain_grad,
    )


LOW = jnp.bfloat16
MESH = pl.DeviceIdType.MESH
LIMIT = 60 * 2**20


def ring_order(ranks):
    half = ranks // 2
    order = [0]
    for step in range(1, half):
        order += [step, ranks - step]
    return order + [half]


def ring_place(seq, ranks):
    z, x = lax.div(seq, 2), lax.rem(seq, 2)
    return z + x * (ranks - 1 - 2 * z)


def ring_seq(place, ranks):
    half = ranks // 2
    x, z = lax.div(place, half), lax.rem(place, half)
    return 2 * (z + x * (half - 1 - 2 * z)) + x


def neighbours(ranks):
    seq, dp = lax.axis_index("seq"), lax.axis_index("dp")
    at = ring_place(seq, ranks)
    right = ring_seq(lax.rem(at + 1, ranks), ranks)
    left = ring_seq(lax.rem(at + ranks - 1, ranks), ranks)
    return (right, dp), (left, dp)


def knock(devices):
    barrier = pltpu.get_barrier_semaphore()
    for device in devices:
        pl.semaphore_signal(barrier, inc=1, device_id=device, device_id_type=MESH)


def answered(devices):
    pl.semaphore_wait(pltpu.get_barrier_semaphore(), len(devices))


def move(src, dst, sem):
    copy = pltpu.make_async_copy(src, dst, sem)
    copy.start()
    return copy


def push(src, dst, send, recv, device):
    return pltpu.make_async_remote_copy(
        src_ref=src, dst_ref=dst, send_sem=send, recv_sem=recv, device_id=device, device_id_type=MESH
    )


def dot_nn(left, right):
    return jnp.dot(left, right, preferred_element_type=jnp.float32)


def dot_nt(left, right):
    return lax.dot_general(left, right, (((1,), (1,)), ((), ())), preferred_element_type=jnp.float32)


def dot_tn(left, right):
    return lax.dot_general(left, right, (((0,), (0,)), ((), ())), preferred_element_type=jnp.float32)


def block_row(rel, local, ranks):
    place = ring_place(lax.axis_index("seq"), ranks)
    return pl.multiple_of(ring_seq(lax.rem(place + rel, ranks), ranks) * local, local)


def block_rows(ref, rels, local, ranks):
    blocks = [ref[pl.ds(block_row(rel, local, ranks), local)] for rel in rels]
    return blocks[0] if len(blocks) == 1 else jnp.concatenate(blocks, 0)


def rels_of(step, ranks):
    return [rel for rel in ring_order(ranks) if min(rel, ranks - rel) == step]


class RingGather:
    def __init__(self, buf, local, ranks, send, recv, right, left, row, fixed=False):
        self.buf, self.local, self.half = buf, local, ranks // 2
        self.send, self.recv, self.right, self.left = send, recv, right, left
        self.ranks, self.row, self.fixed = ranks, row, fixed

    def copies(self, step):
        last = step == self.half
        rows = self.local // 2 if last else self.local
        skip = self.local // 2 if last else 0
        ranks, row = self.ranks, self.row
        behind, ahead = (ranks - step + 1) % ranks, step - 1
        if self.fixed:
            to_right, to_left = row(ranks - step), row(step)
        else:
            to_right, to_left = row(behind), row(ahead)
        pairs = ((behind, 0, to_right, self.right), (ahead, skip, to_left + skip, self.left))
        return [
            push(
                self.buf.at[pl.ds(self.row(src) + begin, rows)],
                self.buf.at[pl.ds(there, rows)],
                self.send.at[way, step - 1],
                self.recv.at[way, step - 1],
                device,
            )
            for way, (src, begin, there, device) in enumerate(pairs)
        ]

    def start(self, step):
        for copy in self.copies(step):
            copy.start()

    def arrive(self, step):
        for copy in self.copies(step):
            copy.wait_recv()

    def finish(self):
        for step in range(1, self.half + 1):
            for copy in self.copies(step):
                copy.wait_send()


class LineGather:
    def __init__(self, buf, local, ranks, send, recv, x_send, x_recv):
        self.buf, self.local, self.length = buf, local, ranks // 2
        self.send, self.recv, self.x_send, self.x_recv = send, recv, x_send, x_recv
        self.seq, self.dp = lax.axis_index("seq"), lax.axis_index("dp")
        self.z, self.x = lax.div(self.seq, 2), lax.rem(self.seq, 2)

    def block(self, z):
        return self.buf.at[pl.ds(pl.multiple_of((2 * z + self.x) * self.local, self.local), self.local)]

    def hop(self, way, step):
        block = self.block(self.z + (step - 1 if way else 1 - step))
        to = self.seq + (-2 if way else 2)
        return push(block, block, self.send.at[way, step - 1], self.recv.at[way, step - 1], (to, self.dp))

    def sends(self, way, step):
        if way:
            return (self.z > 0) & (self.z + step <= self.length)
        return (self.z < self.length - 1) & (self.z >= step - 1)

    def comes(self, way, step):
        return self.z + step < self.length if way else self.z >= step

    def across(self, way, step):
        block = self.block(self.z + (step if way else -step))
        at = step + way * (self.length - 1)
        return push(
            block, block, self.x_send.at[at], self.x_recv.at[at], (self.seq + 1 - 2 * self.x, self.dp)
        )

    def from_x(self, way, step):
        z = self.z + (step if way else -step)
        row = pl.multiple_of((2 * z + 1 - self.x) * self.local, self.local)
        block = self.buf.at[pl.ds(row, self.local)]
        at = step + way * (self.length - 1)
        return push(
            block, block, self.x_send.at[at], self.x_recv.at[at], (self.seq + 1 - 2 * self.x, self.dp)
        )

    def start(self, step):
        for way in range(2):
            pl.when(self.sends(way, step))(lambda way=way: self.hop(way, step).start())
        self.pass_on(step - 1)

    def pass_on(self, step):
        if step == 0:
            self.across(0, 0).start()
            return
        for way in range(2):
            pl.when(self.comes(way, step))(lambda way=way: self.across(way, step).start())

    def arrive(self, step):
        for way in range(2):
            pl.when(self.comes(way, step))(lambda way=way: self.incoming(way, step).wait_recv())

    def incoming(self, way, step):
        block = self.block(self.z + (step if way else -step))
        to = self.seq + 1 - 2 * self.x
        return push(block, block, self.send.at[way, step - 1], self.recv.at[way, step - 1], (to, self.dp))

    def run(self):
        for step in range(1, self.length):
            self.advance(step)

    def advance(self, step):
        self.arrive(step)
        if step < self.length - 1:
            self.start(step + 1)
        else:
            self.pass_on(step)

    def complete(self):
        self.from_x(0, 0).wait_recv()
        for step in range(1, self.length):
            for way in range(2):
                pl.when(self.comes(way, step))(lambda way=way: self.from_x(way, step).wait_recv())

    def finish(self):
        self.across(0, 0).wait_send()
        for step in range(1, self.length):
            for way in range(2):
                pl.when(self.sends(way, step))(lambda way=way: self.hop(way, step).wait_send())
                pl.when(self.comes(way, step))(lambda way=way: self.across(way, step).wait_send())


def line_sems(ranks):
    half = ranks // 2
    return [pltpu.SemaphoreType.DMA((2, half))] * 2 + [pltpu.SemaphoreType.DMA((2 * half,))] * 2


class RingSum:
    def __init__(self, part, term, out_buf, in_buf, local, ranks, send, recv, right, left):
        self.part, self.term, self.out_buf, self.in_buf = part, term, out_buf, in_buf
        self.local, self.ranks, self.half = local, ranks, ranks // 2
        self.send, self.recv, self.right, self.left = send, recv, right, left

    def copies(self, step):
        rows = self.local // 2 if step == 1 else self.local
        skip = self.local // 2 if step == 1 else 0
        return [
            push(
                self.out_buf.at[way, (step - 1) % 2, pl.ds(begin, rows)],
                self.in_buf.at[way, step - 1, pl.ds(begin, rows)],
                self.send.at[way, step - 1],
                self.recv.at[way, step - 1],
                device,
            )
            for way, begin, device in ((0, 0, self.right), (1, skip, self.left))
        ]

    def compute(self, step):
        if step == 1:
            self.part([self.half])
        elif step <= self.half:
            self.part(rels_of(self.half + 1 - step, self.ranks))
        else:
            self.part([0])

    def launch(self, step):
        local, skip = self.local, self.local // 2
        if step > 2:
            for copy in self.copies(step - 2):
                copy.wait_send()
        if step == 1:
            self.out_buf[0, 0, :skip] = self.term[:skip].astype(LOW)
            self.out_buf[1, 0, skip:] = self.term[skip:local].astype(LOW)
        else:
            for copy in self.copies(step - 1):
                copy.wait_recv()
            for way in range(2):
                for begin, with_sum in ((0, step > 2 or way == 0), (skip, step > 2 or way == 1)):
                    value = self.term[pl.ds(way * local + begin, skip)]
                    if with_sum:
                        value = value + self.in_buf[way, step - 2, pl.ds(begin, skip)].astype(jnp.float32)
                    self.out_buf[way, (step - 1) % 2, pl.ds(begin, skip)] = value.astype(LOW)
        for copy in self.copies(step):
            copy.start()

    def last(self, begin, count):
        rows = pl.ds(begin, count)
        value = self.term[rows] + self.in_buf[0, self.half - 1, rows].astype(jnp.float32)
        return value + self.in_buf[1, self.half - 1, rows].astype(jnp.float32)

    def arrive_last(self):
        for copy in self.copies(self.half):
            copy.wait_recv()

    def finish(self):
        for step in range(max(1, self.half - 1), self.half + 1):
            for copy in self.copies(step):
                copy.wait_send()


def ring_sems(ranks):
    return [pltpu.SemaphoreType.DMA((2, ranks // 2)), pltpu.SemaphoreType.DMA((2, ranks // 2))]


def sum_bufs(local, ranks, width):
    return [
        pltpu.VMEM((2 * local, width), jnp.float32),
        pltpu.VMEM((2, 2, local, width), LOW),
        pltpu.VMEM((2, ranks // 2, local, width), LOW),
    ]


def turn(v):
    return pltpu.roll(v, v.shape[-1] // 2, v.ndim - 1)


def rows_scaled(v):
    inv = lax.rsqrt(jnp.mean(v * v, -1, keepdims=True) + EPS)
    return v * inv, inv


def rows_scaled_back(v, inv, grad):
    return inv * grad - v * (inv * inv * inv * jnp.mean(grad * v, -1, keepdims=True))


class Spread:
    def __init__(self, rows, block, ranks, own, cols, sems):
        self.rows, self.block, self.ranks, self.own, self.cols = rows, block, ranks, own, cols
        self.send, self.recv, self.hop_send, self.hop_recv, self.here = sems
        self.seq, self.dp = lax.axis_index("seq"), lax.axis_index("dp")
        y, core = lax.div(self.dp, 2), lax.rem(self.dp, 2)
        self.beside, self.sibling = (1 - y) * 2 + core, y * 2 + 1 - core

    def at(self, dp):
        return pl.ds(pl.multiple_of(dp * self.own, self.own), self.own)

    def exchange(self):
        for step in range(1, self.ranks):
            peer = lax.rem(self.seq + step, self.ranks)
            yield push(
                self.rows.at[peer, :, self.cols],
                self.block.at[self.seq, self.at(self.dp), self.cols],
                self.send.at[step],
                self.recv.at[step],
                (peer, self.dp),
            )

    def keep(self):
        return pltpu.make_async_copy(
            self.rows.at[self.seq, :, self.cols],
            self.block.at[self.seq, self.at(self.dp), self.cols],
            self.here,
        )

    def hop(self, number):
        dp = self.beside if number == 2 else self.dp
        part = self.block.at[:, self.at(dp), self.cols]
        to = self.beside if number == 0 else self.sibling
        return push(part, part, self.hop_send.at[number], self.hop_recv.at[number], (self.seq, to))

    def start(self):
        self.keep().start()
        for copy in self.exchange():
            copy.start()

    def arrive(self):
        self.keep().wait()
        for copy in self.exchange():
            copy.wait_recv()

    def finish(self):
        for copy in self.exchange():
            copy.wait_send()
        for number in range(3):
            self.hop(number).wait_send()


def spread_sems(ranks):
    return [
        pltpu.SemaphoreType.DMA((ranks,)),
        pltpu.SemaphoreType.DMA((ranks,)),
        pltpu.SemaphoreType.DMA((3,)),
        pltpu.SemaphoreType.DMA((3,)),
        pltpu.SemaphoreType.DMA,
    ]


class WholeGather:
    def __init__(self, block, ranks, own, sems):
        self.block, self.ranks, self.half, self.own = block, ranks, ranks // 2, own
        self.send, self.recv, self.y_send, self.y_recv, self.core_send, self.core_recv = sems
        self.seq, self.dp = lax.axis_index("seq"), lax.axis_index("dp")
        self.right, self.left = neighbours(ranks)
        self.place = ring_place(self.seq, ranks)
        y, core = lax.div(self.dp, 2), lax.rem(self.dp, 2)
        self.beside, self.sibling = (1 - y) * 2 + core, y * 2 + 1 - core

    def at(self, rel, dp, begin, count):
        seq = ring_seq(lax.rem(self.place + rel + self.ranks, self.ranks), self.ranks)
        return self.block.at[seq, pl.ds(pl.multiple_of(dp * self.own + begin, count), count)]

    def copies(self, step):
        last = step == self.half
        rows = self.own // 2 if last else self.own
        skip = self.own // 2 if last else 0
        given = []
        for way, rel, begin, device in ((0, 1 - step, 0, self.right), (1, step - 1, skip, self.left)):
            part = self.at(rel, self.dp, begin, rows)
            given.append(push(part, part, self.send.at[way, step - 1], self.recv.at[way, step - 1], device))
        return given

    def start(self, step):
        for copy in self.copies(step):
            copy.start()

    def hops(self, step):
        for at, rel in enumerate(ring_order(self.ranks)):
            if min(rel, self.ranks - rel) == step:
                part = self.at(rel, self.dp, 0, self.own)
                yield push(part, part, self.y_send.at[at], self.y_recv.at[at], (self.seq, self.beside))
                yield push(part, part, self.core_send.at[at], self.core_recv.at[at], (self.seq, self.sibling))

    def arrive(self, step):
        for copy in self.copies(step):
            copy.wait_recv()

    def forward(self, step):
        for copy in self.hops(step):
            copy.start()

    def cross(self):
        part = self.block.at[:, pl.ds(pl.multiple_of(self.beside * self.own, self.own), self.own)]
        at = self.ranks
        return push(part, part, self.core_send.at[at], self.core_recv.at[at], (self.seq, self.sibling))

    def complete(self):
        for step in range(self.half + 1):
            for copy in self.hops(step):
                copy.wait_recv()
        self.cross().start()
        self.cross().wait_recv()

    def finish(self):
        for step in range(1, self.half + 1):
            for copy in self.copies(step):
                copy.wait_send()
        for step in range(self.half + 1):
            for copy in self.hops(step):
                copy.wait_send()
        self.cross().wait_send()


def whole_sems(ranks):
    return (
        ring_sems(ranks)
        + [pltpu.SemaphoreType.DMA((ranks,))] * 2
        + [pltpu.SemaphoreType.DMA((ranks + 1,))] * 2
    )


class Reduce:
    def __init__(self, grads, from_core, from_y, total, own, first, count, cols, sems):
        self.grads, self.from_core, self.from_y, self.total = grads, from_core, from_y, total
        self.own, self.begin, self.count, self.cols = own, first, count, cols
        self.send, self.recv = sems
        self.seq, dp = lax.axis_index("seq"), lax.axis_index("dp")
        self.y, self.core = lax.div(dp, 2), lax.rem(dp, 2)
        self.beside, self.sibling = (1 - self.y) * 2 + self.core, self.y * 2 + 1 - self.core

    def at(self, y, core):
        return pl.ds(pl.multiple_of((y * 2 + core) * self.own, self.own), self.own)

    def hop(self, number):
        some, cols = pl.ds(self.begin, self.count), self.cols
        if number == 2:
            src, dst, to = self.from_core.at[0, some, :, cols], self.from_y.at[some, :, cols], self.beside
        else:
            rows = self.at(1 - self.y if number == 0 else self.y, 1 - self.core)
            src, dst, to = self.grads.at[some, rows, cols], self.from_core.at[number, some, :, cols], self.sibling
        return push(src, dst, self.send.at[number], self.recv.at[number], (self.seq, to))

    def first(self):
        self.hop(0).start()
        self.hop(1).start()

    def second(self):
        self.hop(0).wait_recv()
        rows = self.at(1 - self.y, self.core)

        def some(at, _):
            value = self.grads[at, rows, self.cols].astype(jnp.float32)
            value = value + self.from_core[0, at, :, self.cols].astype(jnp.float32)
            self.from_core[0, at, :, self.cols] = value.astype(LOW)
            return 0

        lax.fori_loop(self.begin, self.begin + self.count, some, 0)
        self.hop(2).start()

    def third(self):
        self.hop(1).wait_recv()
        self.hop(2).wait_recv()
        rows = self.at(self.y, self.core)

        def some(at, _):
            value = self.grads[at, rows, self.cols].astype(jnp.float32)
            value = value + self.from_core[1, at, :, self.cols].astype(jnp.float32)
            value = value + self.from_y[at, :, self.cols].astype(jnp.float32)
            self.total[at, :, self.cols] = value.astype(LOW)
            return 0

        lax.fori_loop(self.begin, self.begin + self.count, some, 0)

    def finish(self):
        for number in range(3):
            self.hop(number).wait_send()


def reduce_sems():
    return [pltpu.SemaphoreType.DMA((3,)), pltpu.SemaphoreType.DMA((3,))]


def reduce_bufs(ranks, own, cols):
    return [pltpu.VMEM((2, ranks, own, cols), LOW), pltpu.VMEM((ranks, own, cols), LOW)]


class Deliver:
    def __init__(self, rows, out, cols, ranks, sems):
        self.rows, self.out, self.cols, self.ranks = rows, out, cols, ranks
        self.send, self.recv, self.here = sems
        self.seq, self.dp = lax.axis_index("seq"), lax.axis_index("dp")

    def exchange(self):
        for step in range(1, self.ranks):
            peer = lax.rem(self.seq + step, self.ranks)
            yield push(
                self.rows.at[peer, :, self.cols],
                self.out.at[self.seq, :, self.cols],
                self.send.at[step],
                self.recv.at[step],
                (peer, self.dp),
            )

    def keep(self):
        return pltpu.make_async_copy(
            self.rows.at[self.seq, :, self.cols], self.out.at[self.seq, :, self.cols], self.here
        )

    def start(self):
        self.keep().start()
        for copy in self.exchange():
            copy.start()

    def finish(self):
        self.keep().wait()
        for copy in self.exchange():
            copy.wait_recv()
        for copy in self.exchange():
            copy.wait_send()


def deliver_sems(ranks):
    return [pltpu.SemaphoreType.DMA((ranks,)), pltpu.SemaphoreType.DMA((ranks,)), pltpu.SemaphoreType.DMA]


def enter_kernel(
    ranks, order, starts, tokens, freqs, attn_gain, mlp_gain, w_query, w_key, w_value, w_output, w_gate, w_up, w_down,
    first_in, qkv, attn_block, mlp_rows, x_all, out_block, cosv, sinv, pos, begins, pos_row,
    held, normal, kept, block, a_rows, m_rows, gate, up, down, whole, *sems,
):
    local, width = tokens.shape
    own = w_query.shape[0]
    size = freqs.shape[1]
    cols = qkv.shape[1]
    half = ranks // 2
    local_sems = sems[7]
    seq, dp = lax.axis_index("seq"), lax.axis_index("dp")
    right, left = neighbours(ranks)
    attn = Spread(a_rows, block, ranks, own, pl.ds(0, a_rows.shape[2]), sems[2:7])
    peers = [(lax.rem(seq + step, ranks), dp) for step in range(1, ranks)]
    peers += [(seq, attn.beside), (seq, attn.sibling)]
    knock(peers)
    loads = [
        move(src, dst, local_sems.at[at])
        for at, (src, dst) in enumerate(((w_gate, gate), (w_up, up), (w_down, down)))
    ]
    row = functools.partial(block_row, local=local, ranks=ranks)
    held[pl.ds(row(0), local)] = tokens[...]

    def column(row):
        same = lax.broadcasted_iota(jnp.int32, (own, own), 0) == lax.broadcasted_iota(jnp.int32, (own, own), 1)
        return jnp.sum(jnp.where(same, row, 0.0), 1, keepdims=True)

    def lay(target, first, weight, gain):
        each = weight.shape[1] // ranks
        for rank in range(ranks):
            part = weight[:, rank * each : (rank + 1) * each]
            if gain is not None:
                part = (part.astype(jnp.float32) * gain).astype(LOW)
            target[rank, :, first : first + each] = part
        return first + each

    gain = column(attn_gain[...])
    at = 0
    for weight in (w_query, w_key, w_value):
        at = lay(a_rows, at, weight, gain)
    whole[seq, pl.ds(pl.multiple_of(dp * own, own), own)] = w_output[...]
    answered(peers)
    ring = RingGather(held, local, ranks, sems[0], sems[1], right, left, row)
    outs = WholeGather(whole, ranks, own, sems[8:14])
    ring.start(1)
    attn.start()
    outs.start(1)
    outs.forward(0)
    stores = []

    def scale_rows(step):
        for rel in rels_of(step, ranks):

            def some(at, _):
                rows = pl.ds(pl.multiple_of(row(rel) + at * 32, 32), 32)
                normal[rows] = rows_scaled(held[rows].astype(jnp.float32))[0].astype(LOW)
                return 0

            lax.fori_loop(0, local // 32, some, 0)
            block_at = pl.ds(row(rel), local)
            stores.append(move(normal.at[block_at], first_in.at[block_at], local_sems.at[len(stores)]))

    def project(step):
        rels = rels_of(step, ranks)
        value = dot_nn(block_rows(normal, rels, local, ranks), block[...].reshape(width, cols))
        for at, rel in enumerate(rels):
            block_at = pl.ds(row(rel), local)
            kept[block_at] = value[at * local : (at + 1) * local]
            stores.append(move(kept.at[block_at], qkv.at[block_at], local_sems.at[len(stores)]))

    for load in loads:
        load.wait()
    gain = column(mlp_gain[...])
    each = gate.shape[1] // ranks
    lay(m_rows, 0, gate, gain)
    lay(m_rows, each, up, gain)
    lay(m_rows, 2 * each, down, None)
    stores.append(move(m_rows, mlp_rows, local_sems.at[len(stores)]))
    scale_rows(0)
    def both(step):
        ring.arrive(step)
        if step < half:
            ring.start(step + 1)
        outs.arrive(step)
        if step < half:
            outs.start(step + 1)
        outs.forward(step)
        scale_rows(step)

    both(1)
    attn.arrive()
    attn.hop(0).start()
    attn.hop(1).start()
    spans = order.shape[0]
    span = local * ranks // spans
    for at in range(ranks):
        rows = pl.ds(at * local, local)
        ids = at * local + lax.broadcasted_iota(jnp.int32, (1, local), 1)
        where = jnp.zeros_like(ids)
        for slot in range(spans):
            inside = (ids >= slot * span) & (ids < (slot + 1) * span)
            where = where + jnp.where(inside, ids + (order[slot] - slot) * span, 0)
        first = jnp.zeros_like(ids)
        for doc in range(starts.shape[1]):
            first = jnp.maximum(first, jnp.where(starts[0, doc] <= where, starts[0, doc], 0))
        pos_row[:, rows] = where
        across = jnp.broadcast_to(where, (local, local)).T
        pos[rows] = across[:, :1]
        begins[rows] = jnp.broadcast_to(first, (local, local)).T[:, :1]
        angle = across[:, :1].astype(jnp.float32) * freqs[...]
        lane = lax.broadcasted_iota(jnp.int32, (local, size), 1)
        cosv[rows] = jnp.cos(angle)
        sine = jnp.sin(angle)
        sinv[rows] = jnp.where(lane < size // 2, -sine, sine)
    both(2)
    attn.hop(0).wait_recv()
    attn.hop(2).start()
    for step in range(3, half):
        both(step)
    attn.hop(1).wait_recv()
    attn.hop(2).wait_recv()
    stores.append(move(block, attn_block, local_sems.at[len(stores)]))
    for step in range(half):
        project(step)
    both(half)
    stores.append(move(held, x_all, local_sems.at[len(stores)]))
    project(half)
    outs.complete()
    stores.append(move(whole, out_block, local_sems.at[len(stores)]))
    ring.finish()
    outs.finish()
    attn.finish()
    for store in stores:
        store.wait()


def attend_kernel(
    ranks, kv_heads, out_grad, qkv, cosv, sinv, pos, begins, pos_row, query_gain, key_gain, mlp_rows, x_all, out_block,
    q_low, k_low, v_low, resid, out_low, second, dy_all, prob, mlp_block,
    dys, probs, xs, whole, sums, outs, *sems,
):
    local, width = out_grad.shape
    rows = local * ranks
    size = cosv.shape[1]
    heads = q_low.shape[0]
    share = heads // kv_heads
    half = ranks // 2
    scale = 1.0 / math.sqrt(size)
    o_cols = heads * size
    deep = whole.shape[1]
    right, left = neighbours(ranks)
    seq, dp = lax.axis_index("seq"), lax.axis_index("dp")
    own = mlp_rows.shape[1]
    third = mlp_rows.shape[2] // 3
    mlp = [
        Spread(mlp_rows, mlp_block, ranks, own, pl.ds(at * third, third), sems[4 + 5 * at : 9 + 5 * at])
        for at in range(3)
    ]
    local_sems = sems[19]
    peers = [(lax.rem(seq + step, ranks), dp) for step in range(1, ranks)]
    peers += [(seq, mlp[0].beside), (seq, mlp[0].sibling)]
    knock(peers)
    loads = [move(x_all, xs, local_sems.at[0]), move(out_block, whole, local_sems.at[1])]
    row = functools.partial(block_row, local=local, ranks=ranks)
    dys[pl.ds(row(0), local)] = out_grad[...]
    answered(peers)
    line = LineGather(dys, local, ranks, sems[0], sems[1], sems[20], sems[21])
    for piece in mlp:
        piece.start()
    line.start(1)
    tile = rows // half
    stores = []

    def rotated(at, rows_at, gain):
        v = rows_scaled(qkv[rows_at, at * size : (at + 1) * size])[0] * gain[...]
        return (v * cosv[rows_at] + turn(v) * sinv[rows_at]).astype(LOW)

    for piece in range(half):
        rows_at = pl.ds(piece * tile, tile)
        for head in range(heads):
            q_low[head, rows_at] = rotated(head, rows_at, query_gain)
        for group in range(kv_heads):
            k_low[group, rows_at] = rotated(heads + group, rows_at, key_gain)
            at = (heads + kv_heads + group) * size
            v_low[group, rows_at] = qkv[rows_at, at : at + size].astype(LOW)

    def forward(piece):
        mlp[piece].arrive()
        mlp[piece].hop(0).start()
        mlp[piece].hop(1).start()

    for piece in range(half):
        rows_at = pl.ds(piece * tile, tile)
        seen = (pos_row[...] <= pos[rows_at]) & (pos_row[...] >= begins[rows_at])
        for head in range(heads):
            raw = dot_nt(q_low[head, rows_at], k_low[head // share]) * scale
            raw = jnp.where(seen, raw, NEG)
            weight = jnp.exp(raw - jnp.max(raw, -1, keepdims=True))
            weight = (weight * (1.0 / jnp.sum(weight, -1, keepdims=True))).astype(LOW)
            probs[head, rows_at] = weight
            value = dot_nn(weight, v_low[head // share])
            outs[rows_at, head * size : (head + 1) * size] = value.astype(LOW)
            stores.append(move(probs.at[head, rows_at], prob.at[head, rows_at], local_sems.at[2 + len(stores)]))
        if piece == 1:
            line.advance(1)
        if piece >= 2:
            forward(piece - 2)
        if piece == half - 1:
            line.advance(2)
    slots = {rel: at * rows for at, rel in enumerate(ring_order(ranks))}
    gather = RingGather(outs, rows, ranks, sems[2], sems[3], right, left, slots.get, True)
    gather.start(1)
    stores.append(move(outs.at[pl.ds(0, rows)], out_low, local_sems.at[2 + len(stores)]))
    for load in loads:
        load.wait()
    place = ring_place(seq, ranks)
    wide = 512

    def add(rels, first):
        cols_of = [
            pl.ds(pl.multiple_of(ring_seq(lax.rem(place + rel, ranks), ranks) * o_cols, o_cols), o_cols)
            for rel in rels
        ]

        def some(at, _):
            block = lax.rem(at, ranks)
            cols = pl.ds(pl.multiple_of(block * deep, deep), deep)
            begin = pl.multiple_of(lax.div(at, ranks) * wide, wide)
            rows_at = pl.ds(begin, wide)
            parts = [outs[pl.ds(slots[rel] + begin, wide)] for rel in rels]
            weights = [whole[block, :, own_cols] for own_cols in cols_of]
            value = dot_nt(jnp.concatenate(parts, 1), jnp.concatenate(weights, 1))
            sums[rows_at, cols] = value + (xs[rows_at, cols].astype(jnp.float32) if first else sums[rows_at, cols])
            return 0

        lax.fori_loop(0, ranks * rows // wide, some, 0)

    forward(2)
    order = ring_order(ranks)
    near = ranks // 2 + 1
    for step in range(1, half + 1):
        gather.arrive(step)
        if step < half:
            gather.start(step + 1)
        if step == 1:
            for later in range(3, half):
                line.advance(later)
        if step == half // 2:
            add(order[:near], True)
        if step < 4:
            mlp[step - 1].hop(0).wait_recv()
            mlp[step - 1].hop(2).start()
    add(order[near:], False)

    def some(at, _):
        rows_at = pl.ds(pl.multiple_of(at * 32, 32), 32)
        xs[rows_at] = rows_scaled(sums[rows_at])[0].astype(LOW)
        return 0

    lax.fori_loop(0, rows // 32, some, 0)
    stores.append(move(xs, second, local_sems.at[2 + len(stores)]))
    resid[...] = sums[pl.ds(row(0), local)]
    line.complete()
    stores.append(move(dys, dy_all, local_sems.at[2 + len(stores)]))
    gather.finish()
    line.finish()
    for piece in mlp:
        piece.hop(1).wait_recv()
        piece.hop(2).wait_recv()
        piece.finish()
    for store in stores:
        store.wait()


def mlp_kernel(
    ranks, out_grad, rest, second, dys, mlp_block, block_out, dresid, dresid_low, gain_grad, own_grads,
    grads, from_core, from_y, held, weights, hidden, dgu, resid, dy_all,
    term, out_buf, in_buf, y_out, y_in, here, *sems,
):
    local, width = out_grad.shape
    row = functools.partial(block_row, local=local, ranks=ranks)
    ff = hidden.shape[1]
    deep = weights.shape[1]
    half = ranks // 2
    right, left = neighbours(ranks)
    loads = [
        move(src, dst, here.at[at])
        for at, (src, dst) in enumerate(((mlp_block, weights), (dys, dy_all), (rest, resid), (second, held)))
    ]
    seq, dp = lax.axis_index("seq"), lax.axis_index("dp")
    own = own_grads.shape[1]
    pieces = [
        Reduce(
            grads, from_core, from_y, own_grads, own, at * ranks // 4, ranks // 4, pl.ds(0, 3 * ff),
            sems[4 + 2 * at : 6 + 2 * at],
        )
        for at in range(4)
    ]
    peers = [right, left, (seq, pieces[0].beside), (seq, pieces[0].sibling)]
    knock(peers)
    answered(peers)
    for at in (0, 1, 3):
        loads[at].wait()
    wide = 256

    def middle(begin, count, tall):
        def some(at, _):
            rows = pl.ds(pl.multiple_of(begin + lax.div(at, ff // wide) * tall, tall), tall)
            first = pl.multiple_of(lax.rem(at, ff // wide) * wide, wide)
            gate = dot_nn(held[rows], weights[:, :, pl.ds(first, wide)].reshape(width, wide))
            upper = dot_nn(held[rows], weights[:, :, pl.ds(ff + first, wide)].reshape(width, wide))
            dmid = dot_nn(dy_all[rows], weights[:, :, pl.ds(2 * ff + first, wide)].reshape(width, wide))
            sigma = 1.0 / (1.0 + jnp.exp(-gate))
            act = gate * sigma
            hidden[rows, pl.ds(first, wide)] = (act * upper).astype(LOW)
            slope = sigma * (1.0 + gate * (1.0 - sigma))
            dgu[rows, pl.ds(first, wide)] = (dmid * upper * slope).astype(LOW)
            dgu[rows, pl.ds(ff + first, wide)] = (dmid * act).astype(LOW)
            return 0

        lax.fori_loop(0, count // tall * (ff // wide), some, 0)

    middle(row(half), local, local)

    def back_part(rels):
        given, count = block_rows(dgu, rels, local, ranks), len(rels) * local

        def some(at, _):
            value = dot_nt(given, weights[at, :, : 2 * ff])
            term[:count, pl.ds(pl.multiple_of(at * deep, deep), deep)] = value
            return 0

        lax.fori_loop(0, ranks, some, 0)

    def out_part(rels):
        given, count = block_rows(hidden, rels, local, ranks), len(rels) * local

        def some(at, _):
            value = dot_nt(given, weights[at, :, 2 * ff :])
            term[:count, pl.ds(pl.multiple_of(at * deep, deep), deep)] = value
            return 0

        lax.fori_loop(0, ranks, some, 0)

    def weight_grads(first, count):
        def some(at, _):
            cols = pl.ds(pl.multiple_of(at * deep, deep), deep)
            grads[at, :, : 2 * ff] = dot_tn(held[:, cols], dgu[...]).astype(LOW)
            grads[at, :, 2 * ff :] = dot_tn(dy_all[:, cols], hidden[...]).astype(LOW)
            return 0

        lax.fori_loop(first, first + count, some, 0)

    back = RingSum(back_part, term, out_buf, in_buf, local, ranks, sems[0], sems[1], right, left)
    out = RingSum(out_part, term, y_out, y_in, local, ranks, sems[2], sems[3], right, left)
    for step in range(1, half + 1):
        back.compute(step)
        back.launch(step)
        out.compute(step)
        out.launch(step)
        if step == 1:
            middle(0, local * ranks, 2 * local)
        if step < 3:
            for piece in pieces[2 * step - 2 : 2 * step]:
                weight_grads(piece.begin, piece.count)
                piece.first()
        if 1 < step < 4:
            for piece in pieces[2 * step - 4 : 2 * step - 2]:
                piece.second()
        if step > 2:
            for piece in pieces[2 * step - 6 : 2 * step - 4]:
                piece.third()
    back.compute(half + 1)
    loads[2].wait()
    back.arrive_last()
    gain_grad[...] = jnp.zeros_like(gain_grad)

    def finish_back(at, _):
        begin = pl.multiple_of(at * 32, 32)
        rows = pl.ds(begin, 32)
        value = resid[rows]
        normal, inv = rows_scaled(value)
        grad = back.last(begin, 32)
        full = out_grad[rows].astype(jnp.float32) + rows_scaled_back(value, inv, grad)
        dresid[rows] = full
        dresid_low[rows] = full.astype(LOW)
        gain_grad[...] += jnp.sum(grad * normal, 0, keepdims=True)
        return 0

    lax.fori_loop(0, local // 32, finish_back, 0)
    out.compute(half + 1)
    out.arrive_last()

    def finish_out(at, _):
        begin = pl.multiple_of(at * 32, 32)
        rows = pl.ds(begin, 32)
        block_out[rows] = (resid[rows] + out.last(begin, 32)).astype(LOW)
        return 0

    lax.fori_loop(0, local // 32, finish_out, 0)
    back.finish()
    out.finish()
    for piece in pieces:
        piece.finish()


def back_kernel(
    ranks, kv_heads, tokens, dresid_low, query_gain, key_gain, mlp_gain_part, out_low_in, first_in_in, block_in,
    qkv_in, cos_in, sin_in, q_in, k_in, v_in, prob_in, dresid_in, mlp_own, out_block,
    tokens_grad, gains, mlp_sums, attn_sums,
    grads, from_core, from_y, own_grads, gain_grad, query_gain_grad, key_gain_grad,
    tiles, tiles_in, tile_sums, tile_sums_in, held, dout, dk, dv, dqkv,
    out_low, first_in, attn_block, qkv, cosv, sinv, q_low, k_low, v_low, prob, dresid, w_output,
    term, out_buf, in_buf, *sems,
):
    local, width = tokens.shape
    rows = local * ranks
    half = ranks // 2
    size = cosv.shape[1]
    heads = q_low.shape[0]
    share = heads // kv_heads
    scale = 1.0 / math.sqrt(size)
    cols = (heads + 2 * kv_heads) * size
    deep = attn_block.shape[1]
    o_cols = heads * size
    right, left = neighbours(ranks)
    seq, dp = lax.axis_index("seq"), lax.axis_index("dp")
    own = mlp_own.shape[1]
    copies = tiles.shape[1]
    all_cols = grads.shape[2]
    out_piece = Reduce(
        grads, from_core, from_y, own_grads, own, 0, ranks, pl.ds(cols, all_cols - cols), sems[4:6]
    )
    qkv_piece = Reduce(grads, from_core, from_y, own_grads, own, 0, ranks, pl.ds(0, cols), sems[6:8])
    third = mlp_own.shape[2] // 3
    mlp_ways = [
        Deliver(mlp_own, mlp_sums, pl.ds(at * third, third), ranks, [*sems[8:11], *sems[22:28]][3 * at : 3 * at + 3])
        for at in range(3)
    ]
    out_way = Deliver(own_grads, attn_sums, pl.ds(cols, all_cols - cols), ranks, sems[11:14])
    qkv_way = Deliver(own_grads, attn_sums, pl.ds(0, cols), ranks, sems[14:17])
    peers = [(lax.rem(seq + step, ranks), dp) for step in range(1, ranks)]
    peers += [(seq, lax.rem(dp + step, copies)) for step in range(1, copies)]
    knock(peers)
    local_sems = sems[21]
    loads = {}
    for at, (name, src, dst) in enumerate(
        (
            ("w_output", out_block.at[:, :, pl.ds(pl.multiple_of(seq * o_cols, o_cols), o_cols)], w_output),
            ("block", block_in, attn_block), ("out", out_low_in, out_low), ("v", v_in, v_low),
            ("prob", prob_in, prob), ("k", k_in, k_low), ("q", q_in, q_low), ("cos", cos_in, cosv),
            ("sin", sin_in, sinv), ("qkv", qkv_in, qkv), ("first", first_in_in, first_in),
            ("dresid", dresid_in, dresid),
        )
    ):
        loads[name] = move(src, dst, local_sems.at[at])
    row = functools.partial(block_row, local=local, ranks=ranks)
    held[pl.ds(row(0), local)] = dresid_low[...]
    answered(peers)
    line = LineGather(held, local, ranks, sems[0], sems[1], sems[28], sems[29])
    line.start(1)
    mlp_ways[0].start()
    line.run()
    loads["w_output"].wait()
    loads["block"].wait()
    for way in mlp_ways[1:]:
        way.start()
    line.complete()
    for at in range(0, rows, 2 * local):
        some = pl.ds(at, 2 * local)
        dout[some] = dot_nn(held[some], w_output[...].reshape(width, o_cols)).astype(LOW)
    loads["out"].wait()

    def out_grads(at, _):
        some_cols = pl.ds(pl.multiple_of(at * deep, deep), deep)
        grads[at, :, cols:] = dot_tn(held[:, some_cols], out_low[...]).astype(LOW)
        return 0

    lax.fori_loop(0, ranks, out_grads, 0)
    out_piece.first()
    for name in ("v", "prob", "k", "q", "cos", "sin", "qkv"):
        loads[name].wait()
    tile = rows // half
    query_gain_grad[...] = jnp.zeros_like(query_gain_grad)
    key_gain_grad[...] = jnp.zeros_like(key_gain_grad)

    def unrotated(grad, column, rows_at, gain, gain_grad_ref):
        grad = grad * cosv[rows_at] - turn(grad) * sinv[rows_at]
        value = qkv[rows_at, column * size : (column + 1) * size]
        normal, inv = rows_scaled(value)
        gain_grad_ref[...] += jnp.sum(grad * normal, 0, keepdims=True)
        back = rows_scaled_back(value, inv, grad * gain[...])
        dqkv[rows_at, column * size : (column + 1) * size] = back.astype(LOW)

    for head in range(heads):
        group = head // share

        def one(piece, _):
            rows_at = pl.ds(pl.multiple_of(piece * tile, tile), tile)
            weight = prob[head, rows_at]
            grad = dout[rows_at, head * size : (head + 1) * size]
            dprob = dot_nt(grad, v_low[group])
            full = weight.astype(jnp.float32)
            delta = jnp.sum(full * dprob, -1, keepdims=True)
            dscore = (full * (dprob - delta)).astype(LOW)
            dq = dot_nn(dscore, k_low[group]) * scale
            dk_add = dot_tn(dscore, q_low[head, rows_at]) * scale
            dv_add = dot_tn(weight, grad)
            dk[group] += dk_add
            dv[group] += dv_add
            unrotated(dq, head, rows_at, query_gain, query_gain_grad)
            return 0

        if head % share == 0:
            dk[group] = jnp.zeros_like(dk[group])
            dv[group] = jnp.zeros_like(dv[group])
        lax.fori_loop(0, half, one, 0)
        if head == 0:
            out_piece.second()
    for group in range(kv_heads):
        def one_key(piece, _):
            rows_at = pl.ds(pl.multiple_of(piece * tile, tile), tile)
            unrotated(dk[group, rows_at], heads + group, rows_at, key_gain, key_gain_grad)
            at = (heads + kv_heads + group) * size
            dqkv[rows_at, at : at + size] = dv[group, rows_at].astype(LOW)
            return 0

        lax.fori_loop(0, half, one_key, 0)

    def part(rels):
        given, count = block_rows(dqkv, rels, local, ranks), len(rels) * local

        def some(at, _):
            value = dot_nt(given, attn_block[at])
            term[:count, pl.ds(pl.multiple_of(at * deep, deep), deep)] = value
            return 0

        lax.fori_loop(0, ranks, some, 0)

    def qkv_grads(at, _):
        some_cols = pl.ds(pl.multiple_of(at * deep, deep), deep)
        grads[at, :, :cols] = dot_tn(first_in[:, some_cols], dqkv[...]).astype(LOW)
        return 0

    total = RingSum(part, term, out_buf, in_buf, local, ranks, sems[2], sems[3], right, left)
    for step in range(1, half + 1):
        total.compute(step)
        total.launch(step)
        if step == 1:
            loads["first"].wait()
            lax.fori_loop(0, ranks, qkv_grads, 0)
            qkv_piece.first()
            out_piece.third()
            out_way.start()
        if step == 2:
            qkv_piece.second()
        if step == half - 1:
            qkv_piece.third()
            qkv_way.start()
    total.compute(half + 1)
    loads["dresid"].wait()
    total.arrive_last()
    gain_grad[...] = jnp.zeros_like(gain_grad)

    def last(at, _):
        begin = pl.multiple_of(at * 32, 32)
        rows_at = pl.ds(begin, 32)
        value = tokens[rows_at].astype(jnp.float32)
        normal, inv = rows_scaled(value)
        grad = total.last(begin, 32)
        tokens_grad[rows_at] = dresid[rows_at] + rows_scaled_back(value, inv, grad)
        gain_grad[...] += jnp.sum(grad * normal, 0, keepdims=True)
        return 0

    lax.fori_loop(0, local // 32, last, 0)
    lane = lax.broadcasted_iota(jnp.int32, (1, size), 1)
    per_row = size // own
    for number in range(ranks * copies):
        at = number // per_row
        first = gain_grad[:, at * size : (at + 1) * size]
        second = mlp_gain_part[:, at * size : (at + 1) * size]
        shift = number % per_row * own
        first = pltpu.roll(first, (size - shift) % size, 1) if shift else first
        second = pltpu.roll(second, (size + own - shift) % size, 1) if shift != own else second
        tile_at = tiles.at[number // copies, number % copies]
        tile_at[0:1] = jnp.where(lane < own, first, second)
        tile_at[1:2] = query_gain_grad[...]
        tile_at[2:3] = key_gain_grad[...]
        tile_at[3:] = jnp.zeros((tiles.shape[2] - 3, size), jnp.float32)

    def to_ranks(step):
        peer = lax.rem(seq + step, ranks)
        return push(tiles.at[peer], tiles_in.at[seq], sems[17].at[step], sems[18].at[step], (peer, dp))

    def to_copies(step):
        peer = lax.rem(dp + step, copies)
        return push(
            tile_sums.at[peer], tile_sums_in.at[dp], sems[19].at[step], sems[20].at[step], (seq, peer)
        )

    for step in range(1, ranks):
        to_ranks(step).start()
    tiles_in[seq] = tiles[seq]
    for step in range(1, ranks):
        to_ranks(step).wait_recv()
    tile_sums[...] = jnp.sum(tiles_in[...], 0)
    for step in range(1, copies):
        to_copies(step).start()
    tile_sums_in[dp] = tile_sums[dp]
    for step in range(1, copies):
        to_copies(step).wait_recv()
    gains[...] = jnp.sum(tile_sums_in[...], 0)
    for step in range(1, ranks):
        to_ranks(step).wait_send()
    for step in range(1, copies):
        to_copies(step).wait_send()
    line.finish()
    total.finish()
    out_piece.finish()
    qkv_piece.finish()
    for way in mlp_ways:
        way.finish()
    out_way.finish()
    qkv_way.finish()


def leave_kernel(attn_sums, mlp_sums, gains, attn_gain, mlp_gain, *outs):
    own = attn_gain.shape[1]
    same = lax.broadcasted_iota(jnp.int32, (own, own), 0) == lax.broadcasted_iota(jnp.int32, (own, own), 1)

    def column(row):
        return jnp.sum(jnp.where(same, row, 0.0), 1, keepdims=True)

    first, second = column(attn_gain[...]), column(mlp_gain[...])
    for sums, parts in ((attn_sums, zip(outs[:4], (first, first, first, None))), (mlp_sums, zip(outs[4:7], (second, second, None)))):
        at = 0
        for out, gain in parts:
            value = sums[0, :, at : at + out.shape[1]].astype(jnp.float32)
            out[...] = value if gain is None else value * gain
            at += out.shape[1]
    outs[7][...] = gains[0:1, :own] / attn_gain[...]
    outs[8][...] = gains[0:1, own : 2 * own] / mlp_gain[...]


VM = pl.BlockSpec(memory_space=pltpu.VMEM)
SM = pl.BlockSpec(memory_space=pltpu.SMEM)
ANY = pl.BlockSpec(memory_space=pl.ANY)


def call(kernel, number, ins, outs, scratch, operands):
    return pl.pallas_call(
        kernel,
        out_shape=[jax.ShapeDtypeStruct(shape, dtype) for shape, dtype, _ in outs],
        in_specs=ins,
        out_specs=[spec for _, _, spec in outs],
        scratch_shapes=scratch,
        compiler_params=pltpu.CompilerParams(
            collective_id=number, has_side_effects=True, vmem_limit_bytes=LIMIT
        ),
    )(*operands)


def columns_body(
    tokens,
    out_grad,
    span_order,
    doc_starts,
    w_query,
    w_key,
    w_value,
    w_output,
    attn_gain,
    query_gain,
    key_gain,
    w_gate,
    w_up,
    w_down,
    mlp_gain,
):
    ranks = lax.axis_size("seq")
    copies = lax.axis_size("dp")
    _, local, width = tokens.shape
    rows = local * ranks
    size = query_gain.shape[0]
    kv_heads = w_key.shape[1] // size // ranks
    heads = w_query.shape[1] // size // ranks
    q_cols, kv_cols = heads * size, kv_heads * size
    qkv_cols = q_cols + 2 * kv_cols
    a_cols = qkv_cols + q_cols
    ff = w_gate.shape[1] // ranks
    own = width // (ranks * copies)
    deep = own * copies
    half = ranks // 2
    f32, i32 = jnp.float32, jnp.int32
    exponents = np.arange(size) % (size // 2) * (-2.0 / size * math.log(1000000.0))
    freqs = jnp.asarray(np.exp(exponents)[None], f32)
    first_in, qkv, attn_block, mlp_rows, x_all, wo_all, cosv, sinv, pos, begins, pos_row = call(
        functools.partial(enter_kernel, ranks),
        1,
        [SM, SM] + [VM] * 8 + [ANY] * 3,
        [
            ((rows, width), LOW, ANY),
            ((rows, qkv_cols), f32, ANY),
            ((ranks, deep, qkv_cols), LOW, ANY),
            ((ranks, own, 3 * ff), LOW, ANY),
            ((rows, width), LOW, ANY),
            ((ranks, deep, q_cols * ranks), LOW, ANY),
            ((rows, size), f32, VM),
            ((rows, size), f32, VM),
            ((rows, 1), i32, VM),
            ((rows, 1), i32, VM),
            ((1, rows), i32, VM),
        ],
        [
            pltpu.VMEM((rows, width), LOW),
            pltpu.VMEM((rows, width), LOW),
            pltpu.VMEM((rows, qkv_cols), f32),
            pltpu.VMEM((ranks, deep, qkv_cols), LOW),
            pltpu.VMEM((ranks, own, qkv_cols), LOW),
            pltpu.VMEM((ranks, own, 3 * ff), LOW),
        ]
        + [pltpu.VMEM((own, ff * ranks), LOW)] * 3
        + [pltpu.VMEM((ranks, deep, q_cols * ranks), LOW)]
        + ring_sems(ranks)
        + spread_sems(ranks)
        + [pltpu.SemaphoreType.DMA((2 * ranks + 4,))]
        + whole_sems(ranks),
        (
            span_order, doc_starts, tokens[0], freqs, attn_gain[None], mlp_gain[None], w_query, w_key, w_value,
            w_output, w_gate, w_up, w_down,
        ),
    )
    q_gain, k_gain = query_gain[None], key_gain[None]
    q_low, k_low, v_low, resid, out_low, second, dy_all, prob, mlp_block = call(
        functools.partial(attend_kernel, ranks, kv_heads),
        2,
        [VM] * 9 + [ANY] * 3,
        [
            ((heads, rows, size), LOW, VM),
            ((kv_heads, rows, size), LOW, VM),
            ((kv_heads, rows, size), LOW, VM),
            ((local, width), f32, VM),
            ((rows, q_cols), LOW, ANY),
            ((rows, width), LOW, ANY),
            ((rows, width), LOW, ANY),
            ((heads, rows, rows), LOW, ANY),
            ((ranks, deep, 3 * ff), LOW, ANY),
        ],
        [
            pltpu.VMEM((rows, width), LOW),
            pltpu.VMEM((heads, rows, rows), LOW),
            pltpu.VMEM((rows, width), LOW),
            pltpu.VMEM((ranks, deep, q_cols * ranks), LOW),
            pltpu.VMEM((rows, width), f32),
            pltpu.VMEM((ranks * rows, q_cols), LOW),
        ]
        + ring_sems(ranks) * 2
        + spread_sems(ranks) * 3
        + [pltpu.SemaphoreType.DMA((heads * half + 5,))]
        + line_sems(ranks)[2:],
        (
            out_grad[0], qkv, cosv, sinv, pos, begins, pos_row, q_gain, k_gain, mlp_rows, x_all, wo_all,
        ),
    )
    block_out, dresid, dresid_low, dgm, mlp_own = call(
        functools.partial(mlp_kernel, ranks),
        3,
        [VM] + [ANY] * 4,
        [
            ((local, width), LOW, VM),
            ((local, width), f32, VM),
            ((local, width), LOW, VM),
            ((1, width), f32, VM),
            ((ranks, own, 3 * ff), LOW, VM),
        ],
        [pltpu.VMEM((ranks, deep, 3 * ff), LOW)]
        + reduce_bufs(ranks, own, 3 * ff)
        + [
            pltpu.VMEM((rows, width), LOW),
            pltpu.VMEM((ranks, deep, 3 * ff), LOW),
            pltpu.VMEM((rows, ff), LOW),
            pltpu.VMEM((rows, 2 * ff), LOW),
            pltpu.VMEM((local, width), f32),
            pltpu.VMEM((rows, width), LOW),
        ]
        + sum_bufs(local, ranks, width)
        + sum_bufs(local, ranks, width)[1:]
        + [pltpu.SemaphoreType.DMA((4,))]
        + ring_sems(ranks) * 2
        + reduce_sems() * 4,
        (out_grad[0], resid, second, dy_all, mlp_block),
    )
    tokens_grad, gains, mlp_sums, attn_sums = call(
        functools.partial(back_kernel, ranks, kv_heads),
        4,
        [VM] * 5 + [ANY] * 13,
        [
            ((local, width), f32, VM),
            ((8, size), f32, VM),
            ((ranks, own, 3 * ff), LOW, ANY),
            ((ranks, own, a_cols), LOW, VM),
        ],
        [pltpu.VMEM((ranks, deep, a_cols), LOW)]
        + reduce_bufs(ranks, own, a_cols)
        + [
            pltpu.VMEM((ranks, own, a_cols), LOW),
            pltpu.VMEM((1, width), f32),
            pltpu.VMEM((1, size), f32),
            pltpu.VMEM((1, size), f32),
            pltpu.VMEM((ranks, copies, 8, size), f32),
            pltpu.VMEM((ranks, copies, 8, size), f32),
            pltpu.VMEM((copies, 8, size), f32),
            pltpu.VMEM((copies, 8, size), f32),
            pltpu.VMEM((rows, width), LOW),
            pltpu.VMEM((rows, q_cols), LOW),
            pltpu.VMEM((kv_heads, rows, size), f32),
            pltpu.VMEM((kv_heads, rows, size), f32),
            pltpu.VMEM((rows, qkv_cols), LOW),
            pltpu.VMEM((rows, q_cols), LOW),
            pltpu.VMEM((rows, width), LOW),
            pltpu.VMEM((ranks, deep, qkv_cols), LOW),
            pltpu.VMEM((rows, qkv_cols), f32),
            pltpu.VMEM((rows, size), f32),
            pltpu.VMEM((rows, size), f32),
            pltpu.VMEM((heads, rows, size), LOW),
            pltpu.VMEM((kv_heads, rows, size), LOW),
            pltpu.VMEM((kv_heads, rows, size), LOW),
            pltpu.VMEM((heads, rows, rows), LOW),
            pltpu.VMEM((local, width), f32),
            pltpu.VMEM((ranks, deep, q_cols), LOW),
        ]
        + sum_bufs(local, ranks, width)
        + ring_sems(ranks) * 2
        + reduce_sems() * 2
        + deliver_sems(ranks) * 3
        + [pltpu.SemaphoreType.DMA((ranks,))] * 2
        + [pltpu.SemaphoreType.DMA((copies,))] * 2
        + [pltpu.SemaphoreType.DMA((12,))]
        + deliver_sems(ranks) * 2
        + line_sems(ranks)[2:],
        (
            tokens[0], dresid_low, q_gain, k_gain, dgm, out_low, first_in, attn_block, qkv, cosv, sinv, q_low, k_low,
            v_low, prob, dresid, mlp_own, wo_all,
        ),
    )
    whole = pl.BlockSpec((1, own), lambda at: (0, 0))
    each = (q_cols, kv_cols, kv_cols, q_cols, ff, ff, ff)
    *grads, dga, dgm = pl.pallas_call(
        leave_kernel,
        grid=(ranks,),
        out_shape=[jax.ShapeDtypeStruct((own, cols * ranks), f32) for cols in each]
        + [jax.ShapeDtypeStruct((1, own), f32)] * 2,
        in_specs=[
            pl.BlockSpec((1, own, a_cols), lambda at: (at, 0, 0)),
            pl.BlockSpec((1, own, 3 * ff), lambda at: (at, 0, 0)),
            pl.BlockSpec((8, size), lambda at: (0, 0)),
            whole,
            whole,
        ],
        out_specs=[pl.BlockSpec((own, cols), lambda at: (0, at)) for cols in each] + [whole, whole],
    )(attn_sums, mlp_sums, gains, attn_gain[None], mlp_gain[None])
    return (
        block_out[None], tokens_grad[None], *grads[:4], dga[0], gains[1], gains[2], *grads[4:], dgm[0],
    )


def body(*args):
    tokens, w_key, query_gain = args[0], args[5], args[9]
    groups = w_key.shape[1] // query_gain.shape[0]
    ranks = lax.axis_size("seq")
    if tokens.shape[0] == 1 and ranks % 2 == 0 and groups % ranks == 0 and lax.axis_size("dp") == 4:
        return columns_body(*args)
    return gathered_body(*args)


def solution(mesh):
    return jax.shard_map(
        body,
        mesh=mesh,
        in_specs=(
            P("dp", "seq", None),
            P("dp", "seq", None),
            P(),
            P("dp", None),
            P(("seq", "dp"), None),
            P(("seq", "dp"), None),
            P(("seq", "dp"), None),
            P(("seq", "dp"), None),
            P(("seq", "dp")),
            P(),
            P(),
            P(("seq", "dp"), None),
            P(("seq", "dp"), None),
            P(("seq", "dp"), None),
            P(("seq", "dp")),
        ),
        out_specs=(
            P("dp", "seq", None),
            P("dp", "seq", None),
            P(("seq", "dp"), None),
            P(("seq", "dp"), None),
            P(("seq", "dp"), None),
            P(("seq", "dp"), None),
            P(("seq", "dp")),
            P(),
            P(),
            P(("seq", "dp"), None),
            P(("seq", "dp"), None),
            P(("seq", "dp"), None),
            P(("seq", "dp")),
        ),
        check_vma=False,
    )
```

```python
import functools
import math

import jax
import jax.numpy as jnp
import numpy as np
from jax import lax
from jax.experimental import pallas as pl
from jax.experimental.pallas import tpu as pltpu
from jax.sharding import PartitionSpec as P

EPS = 1e-06
NEG = -1e30


def normed(v, gain):
    scale_inv = lax.rsqrt(jnp.mean(v * v, -1, keepdims=True) + EPS)
    return (v * scale_inv * gain, scale_inv)


def norm_back(v, scale_inv, gain, grad):
    scaled = grad * gain
    inner = jnp.mean(scaled * v, -1, keepdims=True)
    dv = scale_inv * scaled - v * scale_inv * scale_inv * scale_inv * inner
    dgain = jnp.sum((grad * v * scale_inv).reshape(-1, v.shape[-1]), 0)
    return (dv, dgain)


def rotary(pos, width):
    half = width // 2
    freqs = jnp.exp(jnp.arange(half, dtype=jnp.float32) * (-2.0 / width * math.log(1000000.0)))
    angle = pos.astype(jnp.float32)[:, None] * freqs[None, :]
    return (jnp.cos(angle)[:, None, :], jnp.sin(angle)[:, None, :])


def rotate(v, cosv, sinv):
    half = v.shape[-1] // 2
    first, second = (v[..., :half], v[..., half:])
    return jnp.concatenate([first * cosv - second * sinv, second * cosv + first * sinv], -1)


def rotate_back(grad, cosv, sinv):
    half = grad.shape[-1] // 2
    first, second = (grad[..., :half], grad[..., half:])
    return jnp.concatenate([first * cosv + second * sinv, second * cosv - first * sinv], -1)


def place(order, begin, count, span):
    rows = begin + jnp.arange(count, dtype=jnp.int32)
    slots = rows // span
    picked = slots[:, None] == jnp.arange(order.shape[0], dtype=jnp.int32)[None, :]
    return jnp.sum(jnp.where(picked, order[None, :], 0), -1) * span + rows % span


def doc_of(starts, pos):
    return jnp.sum((starts[:, None, :] <= pos[None, :, None]).astype(jnp.int32), -1)


def gathered_body(
    tokens,
    out_grad,
    span_order,
    doc_starts,
    w_query,
    w_key,
    w_value,
    w_output,
    attn_gain,
    query_gain,
    key_gain,
    w_gate,
    w_up,
    w_down,
    mlp_gain,
):
    seqs, local, width = tokens.shape
    span = local // 2
    head_size = query_gain.shape[0]
    kv_heads = w_key.shape[1] // head_size
    heads = w_query.shape[1] // head_size
    share = heads // kv_heads
    kv_width = kv_heads * head_size
    ff_width = w_gate.shape[1]
    scale = 1.0 / math.sqrt(head_size)
    total_rows = seqs * local
    own_rows = width // lax.axis_size(("seq", "dp"))
    qpos = place(span_order, lax.axis_index("seq") * local, local, span)
    qdoc = doc_of(doc_starts, qpos)
    cosv, sinv = rotary(qpos, head_size)

    def gather_attn():
        return (
            lax.all_gather(w_query, ("seq", "dp"), axis=0, tiled=True),
            lax.all_gather(w_key, ("seq", "dp"), axis=0, tiled=True),
            lax.all_gather(w_value, ("seq", "dp"), axis=0, tiled=True),
            lax.all_gather(w_output, ("seq", "dp"), axis=0, tiled=True),
            lax.all_gather(
                attn_gain.astype(jnp.bfloat16), ("seq", "dp"), axis=0, tiled=True
            ).astype(attn_gain.dtype),
        )

    def gather_mlp():
        return (
            lax.all_gather(w_gate, ("seq", "dp"), axis=0, tiled=True),
            lax.all_gather(w_up, ("seq", "dp"), axis=0, tiled=True),
            lax.all_gather(w_down, ("seq", "dp"), axis=0, tiled=True),
            lax.all_gather(mlp_gain.astype(jnp.bfloat16), ("seq", "dp"), axis=0, tiled=True).astype(
                mlp_gain.dtype
            ),
        )

    x_rows = tokens.astype(jnp.float32).reshape(total_rows, width)
    wq_all, wk_all, wv_all, wo_all, ga_all = gather_attn()
    first_norm, first_inv = normed(x_rows, ga_all)
    first_in = first_norm.astype(jnp.bfloat16)
    q_raw = jnp.dot(first_in, wq_all, preferred_element_type=jnp.float32).reshape(
        seqs, local, heads, head_size
    )
    k_raw = jnp.dot(first_in, wk_all, preferred_element_type=jnp.float32).reshape(
        seqs, local, kv_heads, head_size
    )
    v_low = (
        jnp.dot(first_in, wv_all, preferred_element_type=jnp.float32)
        .astype(jnp.bfloat16)
        .reshape(seqs, local, kv_heads, head_size)
    )
    q_normed, q_inv = normed(q_raw, query_gain)
    k_normed, k_inv = normed(k_raw, key_gain)
    q_low = rotate(q_normed, cosv, sinv).astype(jnp.bfloat16)
    k_low = rotate(k_normed, cosv, sinv).astype(jnp.bfloat16)
    q_group = q_low.reshape(seqs, local, kv_heads, share, head_size)

    def scores(piece_key, start):
        count = piece_key.shape[1]
        kpos = place(span_order, start, count, span)
        kdoc = doc_of(doc_starts, kpos)
        visible = (qdoc[:, :, None] == kdoc[:, None, :]) & (
            kpos[None, None, :] <= qpos[None, :, None]
        )
        raw = (
            jnp.einsum("sqgjd,skgd->sgjqk", q_group, piece_key, preferred_element_type=jnp.float32)
            * scale
        )
        return (raw, visible[:, None, None])

    start_top = jnp.full((seqs, kv_heads, share, local), NEG, jnp.float32)
    piece = (
        lax.all_gather(k_low, "seq", axis=1, tiled=True),
        lax.all_gather(v_low, "seq", axis=1, tiled=True),
    )
    top = start_top
    raw, visible = scores(piece[0], jnp.int32(0))
    raw = jnp.where(visible, raw, NEG)
    new_top = jnp.maximum(top, jnp.max(raw, -1))
    weights = jnp.where(visible, jnp.exp(raw - new_top[..., None]), 0.0)
    total = jnp.sum(weights, -1)
    summed = jnp.einsum(
        "sgjqk,skgd->sgjqd",
        weights.astype(jnp.bfloat16),
        piece[1],
        preferred_element_type=jnp.float32,
    )
    top, total, summed = (new_top, total, summed)
    log_total = top + jnp.log(total)
    attn_vals = summed / total[..., None]
    out_low = (
        jnp.transpose(attn_vals, (0, 3, 1, 2, 4))
        .reshape(total_rows, heads * head_size)
        .astype(jnp.bfloat16)
    )
    resid = x_rows + jnp.einsum("nh,dh->nd", out_low, wo_all, preferred_element_type=jnp.float32)
    wg_all, wu_all, wd_all, gm_all = gather_mlp()
    second_norm, second_inv = normed(resid, gm_all)
    second_in = second_norm.astype(jnp.bfloat16)
    gate = jnp.dot(second_in, wg_all, preferred_element_type=jnp.float32)
    upper = jnp.dot(second_in, wu_all, preferred_element_type=jnp.float32)
    sigma = jax.nn.sigmoid(gate)
    act = gate * sigma
    hidden = (act * upper).astype(jnp.bfloat16)
    result = resid + jnp.einsum("nf,df->nd", hidden, wd_all, preferred_element_type=jnp.float32)
    block_out = result.astype(jnp.bfloat16).reshape(seqs, local, width)
    grad_low = out_grad.reshape(total_rows, width)
    wg_all, wu_all, wd_all, gm_all = gather_mlp()
    dmid = jnp.einsum("nd,df->nf", grad_low, wd_all, preferred_element_type=jnp.float32)
    dgate = (dmid * upper * sigma * (1.0 + gate * (1.0 - sigma))).astype(jnp.bfloat16)
    dupper = (dmid * act).astype(jnp.bfloat16)
    left = second_in
    outer = grad_low
    mlp_sums = lax.psum_scatter(
        jnp.concatenate(
            [
                jnp.einsum("nd,nf->df", left, dgate, preferred_element_type=jnp.float32),
                jnp.einsum("nd,nf->df", left, dupper, preferred_element_type=jnp.float32),
                jnp.einsum("nd,nf->df", outer, hidden, preferred_element_type=jnp.float32),
            ],
            1,
        ),
        ("seq", "dp"),
        scatter_dimension=0,
        tiled=True,
    )
    dsecond = jnp.einsum(
        "nf,df->nd", dgate, wg_all, preferred_element_type=jnp.float32
    ) + jnp.einsum("nf,df->nd", dupper, wu_all, preferred_element_type=jnp.float32)
    dresid_norm, dgm = norm_back(resid, second_inv, gm_all, dsecond)
    dresid = grad_low.astype(jnp.float32) + dresid_norm
    dresid_low = dresid.astype(jnp.bfloat16)
    wq_all, wk_all, wv_all, wo_all, ga_all = gather_attn()
    dout_low = jnp.einsum(
        "nd,dh->nh", dresid_low, wo_all, preferred_element_type=jnp.float32
    ).astype(jnp.bfloat16)
    dout_group = dout_low.reshape(seqs, local, kv_heads, share, head_size)
    delta = jnp.sum(jnp.transpose(dout_group.astype(jnp.float32), (0, 2, 3, 1, 4)) * attn_vals, -1)
    piece = (
        lax.all_gather(k_low, "seq", axis=1, tiled=True),
        lax.all_gather(v_low, "seq", axis=1, tiled=True),
    )
    count = piece[0].shape[1]
    raw, visible = scores(piece[0], jnp.int32(0))
    prob = jnp.where(visible, jnp.exp(raw - log_total[..., None]), 0.0)
    dprob = jnp.einsum(
        "sqgjd,skgd->sgjqk", dout_group, piece[1], preferred_element_type=jnp.float32
    )
    dscore = (prob * (dprob - delta[..., None])).astype(jnp.bfloat16)
    dq_sum = jnp.einsum("sgjqk,skgd->sqgjd", dscore, piece[0], preferred_element_type=jnp.float32)
    dk_part = (
        jnp.einsum("sgjqk,sqgjd->skgd", dscore, q_group, preferred_element_type=jnp.float32) * scale
    )
    dv_part = jnp.einsum(
        "sgjqk,sqgjd->skgd",
        prob.astype(jnp.bfloat16),
        dout_group,
        preferred_element_type=jnp.float32,
    )
    joined = jnp.concatenate(
        [dk_part.reshape(seqs, count, kv_width), dv_part.reshape(seqs, count, kv_width)], -1
    )
    buffer = joined
    dq_sum, buffer = (dq_sum, buffer)
    key_sums = lax.psum_scatter(
        buffer.astype(jnp.bfloat16), "seq", scatter_dimension=1, tiled=True
    ).astype(jnp.float32)
    dq_rot = (dq_sum * scale).reshape(seqs, local, heads, head_size)
    dq_raw, dgq = norm_back(q_raw, q_inv, query_gain, rotate_back(dq_rot, cosv, sinv))
    dk_rot = key_sums[..., :kv_width].reshape(seqs, local, kv_heads, head_size)
    dk_raw, dgk = norm_back(k_raw, k_inv, key_gain, rotate_back(dk_rot, cosv, sinv))
    dq_low = dq_raw.reshape(total_rows, heads * head_size).astype(jnp.bfloat16)
    dk_low = dk_raw.reshape(total_rows, kv_width).astype(jnp.bfloat16)
    dv_low = key_sums[..., kv_width:].reshape(total_rows, kv_width).astype(jnp.bfloat16)
    left = first_in
    outer = dresid_low
    attn_sums = lax.psum_scatter(
        jnp.concatenate(
            [
                jnp.einsum("nd,nh->dh", left, dq_low, preferred_element_type=jnp.float32),
                jnp.einsum("nd,nh->dh", left, dk_low, preferred_element_type=jnp.float32),
                jnp.einsum("nd,nh->dh", left, dv_low, preferred_element_type=jnp.float32),
                jnp.einsum("nd,nh->dh", outer, out_low, preferred_element_type=jnp.float32),
            ],
            1,
        ),
        ("seq", "dp"),
        scatter_dimension=0,
        tiled=True,
    )
    dfirst = jnp.einsum("nh,dh->nd", dq_low, wq_all, preferred_element_type=jnp.float32)
    dfirst = dfirst + jnp.einsum("nh,dh->nd", dk_low, wk_all, preferred_element_type=jnp.float32)
    dfirst = dfirst + jnp.einsum("nh,dh->nd", dv_low, wv_all, preferred_element_type=jnp.float32)
    dx_norm, dga = norm_back(x_rows, first_inv, ga_all, dfirst)
    tokens_grad = (dresid + dx_norm).reshape(seqs, local, width)
    dga_all, dgm_all, dgq_all, dgk_all = lax.psum((dga, dgm, dgq, dgk), ("seq", "dp"))
    offset = lax.axis_index(("seq", "dp")) * own_rows
    attn_gain_grad = lax.dynamic_slice_in_dim(dga_all, offset, own_rows, 0)
    mlp_gain_grad = lax.dynamic_slice_in_dim(dgm_all, offset, own_rows, 0)
    q_cols = heads * head_size
    w_query_grad = attn_sums[:, :q_cols]
    w_key_grad = attn_sums[:, q_cols : q_cols + kv_width]
    w_value_grad = attn_sums[:, q_cols + kv_width : q_cols + 2 * kv_width]
    w_output_grad = attn_sums[:, q_cols + 2 * kv_width :]
    w_gate_grad = mlp_sums[:, :ff_width]
    w_up_grad = mlp_sums[:, ff_width : 2 * ff_width]
    w_down_grad = mlp_sums[:, 2 * ff_width :]
    return (
        block_out,
        tokens_grad,
        w_query_grad,
        w_key_grad,
        w_value_grad,
        w_output_grad,
        attn_gain_grad,
        dgq_all,
        dgk_all,
        w_gate_grad,
        w_up_grad,
        w_down_grad,
        mlp_gain_grad,
    )


LOW = jnp.bfloat16
MESH = pl.DeviceIdType.MESH
LIMIT = 60 * 2**20


def ring_order(ranks):
    half = ranks // 2
    order = [0]
    for step in range(1, half):
        order += [step, ranks - step]
    return order + [half]


def ring_place(seq, ranks):
    z, x = lax.div(seq, 2), lax.rem(seq, 2)
    return z + x * (ranks - 1 - 2 * z)


def ring_seq(place, ranks):
    half = ranks // 2
    x, z = lax.div(place, half), lax.rem(place, half)
    return 2 * (z + x * (half - 1 - 2 * z)) + x


def neighbours(ranks):
    seq, dp = lax.axis_index("seq"), lax.axis_index("dp")
    at = ring_place(seq, ranks)
    right = ring_seq(lax.rem(at + 1, ranks), ranks)
    left = ring_seq(lax.rem(at + ranks - 1, ranks), ranks)
    return (right, dp), (left, dp)


def knock(devices):
    barrier = pltpu.get_barrier_semaphore()
    for device in devices:
        pl.semaphore_signal(barrier, inc=1, device_id=device, device_id_type=MESH)


def answered(devices):
    pl.semaphore_wait(pltpu.get_barrier_semaphore(), len(devices))


def move(src, dst, sem):
    copy = pltpu.make_async_copy(src, dst, sem)
    copy.start()
    return copy


def push(src, dst, send, recv, device):
    return pltpu.make_async_remote_copy(
        src_ref=src, dst_ref=dst, send_sem=send, recv_sem=recv, device_id=device, device_id_type=MESH
    )


def dot_nn(left, right):
    return jnp.dot(left, right, preferred_element_type=jnp.float32)


def dot_nt(left, right):
    return lax.dot_general(left, right, (((1,), (1,)), ((), ())), preferred_element_type=jnp.float32)


def dot_tn(left, right):
    return lax.dot_general(left, right, (((0,), (0,)), ((), ())), preferred_element_type=jnp.float32)


def block_row(rel, local, ranks):
    place = ring_place(lax.axis_index("seq"), ranks)
    return pl.multiple_of(ring_seq(lax.rem(place + rel, ranks), ranks) * local, local)


def block_rows(ref, rels, local, ranks):
    blocks = [ref[pl.ds(block_row(rel, local, ranks), local)] for rel in rels]
    return blocks[0] if len(blocks) == 1 else jnp.concatenate(blocks, 0)


def rels_of(step, ranks):
    return [rel for rel in ring_order(ranks) if min(rel, ranks - rel) == step]


class RingGather:
    def __init__(self, buf, local, ranks, send, recv, right, left, row, fixed=False):
        self.buf, self.local, self.half = buf, local, ranks // 2
        self.send, self.recv, self.right, self.left = send, recv, right, left
        self.ranks, self.row, self.fixed = ranks, row, fixed

    def copies(self, step):
        last = step == self.half
        rows = self.local // 2 if last else self.local
        skip = self.local // 2 if last else 0
        ranks, row = self.ranks, self.row
        behind, ahead = (ranks - step + 1) % ranks, step - 1
        if self.fixed:
            to_right, to_left = row(ranks - step), row(step)
        else:
            to_right, to_left = row(behind), row(ahead)
        pairs = ((behind, 0, to_right, self.right), (ahead, skip, to_left + skip, self.left))
        return [
            push(
                self.buf.at[pl.ds(self.row(src) + begin, rows)],
                self.buf.at[pl.ds(there, rows)],
                self.send.at[way, step - 1],
                self.recv.at[way, step - 1],
                device,
            )
            for way, (src, begin, there, device) in enumerate(pairs)
        ]

    def start(self, step):
        for copy in self.copies(step):
            copy.start()

    def arrive(self, step):
        for copy in self.copies(step):
            copy.wait_recv()

    def finish(self):
        for step in range(1, self.half + 1):
            for copy in self.copies(step):
                copy.wait_send()


class LineGather:
    def __init__(self, buf, local, ranks, send, recv, x_send, x_recv):
        self.buf, self.local, self.length = buf, local, ranks // 2
        self.send, self.recv, self.x_send, self.x_recv = send, recv, x_send, x_recv
        self.seq, self.dp = lax.axis_index("seq"), lax.axis_index("dp")
        self.z, self.x = lax.div(self.seq, 2), lax.rem(self.seq, 2)

    def block(self, z):
        return self.buf.at[pl.ds(pl.multiple_of((2 * z + self.x) * self.local, self.local), self.local)]

    def hop(self, way, step):
        block = self.block(self.z + (step - 1 if way else 1 - step))
        to = self.seq + (-2 if way else 2)
        return push(block, block, self.send.at[way, step - 1], self.recv.at[way, step - 1], (to, self.dp))

    def sends(self, way, step):
        if way:
            return (self.z > 0) & (self.z + step <= self.length)
        return (self.z < self.length - 1) & (self.z >= step - 1)

    def comes(self, way, step):
        return self.z + step < self.length if way else self.z >= step

    def across(self, way, step):
        block = self.block(self.z + (step if way else -step))
        at = step + way * (self.length - 1)
        return push(
            block, block, self.x_send.at[at], self.x_recv.at[at], (self.seq + 1 - 2 * self.x, self.dp)
        )

    def from_x(self, way, step):
        z = self.z + (step if way else -step)
        row = pl.multiple_of((2 * z + 1 - self.x) * self.local, self.local)
        block = self.buf.at[pl.ds(row, self.local)]
        at = step + way * (self.length - 1)
        return push(
            block, block, self.x_send.at[at], self.x_recv.at[at], (self.seq + 1 - 2 * self.x, self.dp)
        )

    def start(self, step):
        for way in range(2):
            pl.when(self.sends(way, step))(lambda way=way: self.hop(way, step).start())
        self.pass_on(step - 1)

    def pass_on(self, step):
        if step == 0:
            self.across(0, 0).start()
            return
        for way in range(2):
            pl.when(self.comes(way, step))(lambda way=way: self.across(way, step).start())

    def arrive(self, step):
        for way in range(2):
            pl.when(self.comes(way, step))(lambda way=way: self.incoming(way, step).wait_recv())

    def incoming(self, way, step):
        block = self.block(self.z + (step if way else -step))
        to = self.seq + 1 - 2 * self.x
        return push(block, block, self.send.at[way, step - 1], self.recv.at[way, step - 1], (to, self.dp))

    def run(self):
        for step in range(1, self.length):
            self.advance(step)

    def advance(self, step):
        self.arrive(step)
        if step < self.length - 1:
            self.start(step + 1)
        else:
            self.pass_on(step)

    def complete(self):
        self.from_x(0, 0).wait_recv()
        for step in range(1, self.length):
            for way in range(2):
                pl.when(self.comes(way, step))(lambda way=way: self.from_x(way, step).wait_recv())

    def finish(self):
        self.across(0, 0).wait_send()
        for step in range(1, self.length):
            for way in range(2):
                pl.when(self.sends(way, step))(lambda way=way: self.hop(way, step).wait_send())
                pl.when(self.comes(way, step))(lambda way=way: self.across(way, step).wait_send())


def line_sems(ranks):
    half = ranks // 2
    return [pltpu.SemaphoreType.DMA((2, half))] * 2 + [pltpu.SemaphoreType.DMA((2 * half,))] * 2


class RingSum:
    def __init__(self, part, term, out_buf, in_buf, local, ranks, send, recv, right, left):
        self.part, self.term, self.out_buf, self.in_buf = part, term, out_buf, in_buf
        self.local, self.ranks, self.half = local, ranks, ranks // 2
        self.send, self.recv, self.right, self.left = send, recv, right, left

    def copies(self, step):
        rows = self.local // 2 if step == 1 else self.local
        skip = self.local // 2 if step == 1 else 0
        return [
            push(
                self.out_buf.at[way, (step - 1) % 2, pl.ds(begin, rows)],
                self.in_buf.at[way, step - 1, pl.ds(begin, rows)],
                self.send.at[way, step - 1],
                self.recv.at[way, step - 1],
                device,
            )
            for way, begin, device in ((0, 0, self.right), (1, skip, self.left))
        ]

    def compute(self, step):
        if step == 1:
            self.part([self.half])
        elif step <= self.half:
            self.part(rels_of(self.half + 1 - step, self.ranks))
        else:
            self.part([0])

    def launch(self, step):
        local, skip = self.local, self.local // 2
        if step > 2:
            for copy in self.copies(step - 2):
                copy.wait_send()
        if step == 1:
            self.out_buf[0, 0, :skip] = self.term[:skip].astype(LOW)
            self.out_buf[1, 0, skip:] = self.term[skip:local].astype(LOW)
        else:
            for copy in self.copies(step - 1):
                copy.wait_recv()
            for way in range(2):
                for begin, with_sum in ((0, step > 2 or way == 0), (skip, step > 2 or way == 1)):
                    value = self.term[pl.ds(way * local + begin, skip)]
                    if with_sum:
                        value = value + self.in_buf[way, step - 2, pl.ds(begin, skip)].astype(jnp.float32)
                    self.out_buf[way, (step - 1) % 2, pl.ds(begin, skip)] = value.astype(LOW)
        for copy in self.copies(step):
            copy.start()

    def last(self, begin, count):
        rows = pl.ds(begin, count)
        value = self.term[rows] + self.in_buf[0, self.half - 1, rows].astype(jnp.float32)
        return value + self.in_buf[1, self.half - 1, rows].astype(jnp.float32)

    def arrive_last(self):
        for copy in self.copies(self.half):
            copy.wait_recv()

    def finish(self):
        for step in range(max(1, self.half - 1), self.half + 1):
            for copy in self.copies(step):
                copy.wait_send()


def ring_sems(ranks):
    return [pltpu.SemaphoreType.DMA((2, ranks // 2)), pltpu.SemaphoreType.DMA((2, ranks // 2))]


def sum_bufs(local, ranks, width):
    return [
        pltpu.VMEM((2 * local, width), jnp.float32),
        pltpu.VMEM((2, 2, local, width), LOW),
        pltpu.VMEM((2, ranks // 2, local, width), LOW),
    ]


def turn(v):
    return pltpu.roll(v, v.shape[-1] // 2, v.ndim - 1)


def rows_scaled(v):
    inv = lax.rsqrt(jnp.mean(v * v, -1, keepdims=True) + EPS)
    return v * inv, inv


def rows_scaled_back(v, inv, grad):
    return inv * grad - v * (inv * inv * inv * jnp.mean(grad * v, -1, keepdims=True))


class Spread:
    def __init__(self, rows, block, ranks, own, cols, sems):
        self.rows, self.block, self.ranks, self.own, self.cols = rows, block, ranks, own, cols
        self.send, self.recv, self.hop_send, self.hop_recv, self.here = sems
        self.seq, self.dp = lax.axis_index("seq"), lax.axis_index("dp")
        y, core = lax.div(self.dp, 2), lax.rem(self.dp, 2)
        self.beside, self.sibling = (1 - y) * 2 + core, y * 2 + 1 - core

    def at(self, dp):
        return pl.ds(pl.multiple_of(dp * self.own, self.own), self.own)

    def exchange(self):
        for step in range(1, self.ranks):
            peer = lax.rem(self.seq + step, self.ranks)
            yield push(
                self.rows.at[peer, :, self.cols],
                self.block.at[self.seq, self.at(self.dp), self.cols],
                self.send.at[step],
                self.recv.at[step],
                (peer, self.dp),
            )

    def keep(self):
        return pltpu.make_async_copy(
            self.rows.at[self.seq, :, self.cols],
            self.block.at[self.seq, self.at(self.dp), self.cols],
            self.here,
        )

    def hop(self, number):
        dp = self.beside if number == 2 else self.dp
        part = self.block.at[:, self.at(dp), self.cols]
        to = self.beside if number == 0 else self.sibling
        return push(part, part, self.hop_send.at[number], self.hop_recv.at[number], (self.seq, to))

    def start(self):
        self.keep().start()
        for copy in self.exchange():
            copy.start()

    def arrive(self):
        self.keep().wait()
        for copy in self.exchange():
            copy.wait_recv()

    def finish(self):
        for copy in self.exchange():
            copy.wait_send()
        for number in range(3):
            self.hop(number).wait_send()


def spread_sems(ranks):
    return [
        pltpu.SemaphoreType.DMA((ranks,)),
        pltpu.SemaphoreType.DMA((ranks,)),
        pltpu.SemaphoreType.DMA((3,)),
        pltpu.SemaphoreType.DMA((3,)),
        pltpu.SemaphoreType.DMA,
    ]


class Reduce:
    def __init__(self, grads, from_core, from_y, total, own, first, count, cols, sems):
        self.grads, self.from_core, self.from_y, self.total = grads, from_core, from_y, total
        self.own, self.begin, self.count, self.cols = own, first, count, cols
        self.send, self.recv = sems
        self.seq, dp = lax.axis_index("seq"), lax.axis_index("dp")
        self.y, self.core = lax.div(dp, 2), lax.rem(dp, 2)
        self.beside, self.sibling = (1 - self.y) * 2 + self.core, self.y * 2 + 1 - self.core

    def at(self, y, core):
        return pl.ds(pl.multiple_of((y * 2 + core) * self.own, self.own), self.own)

    def hop(self, number):
        some, cols = pl.ds(self.begin, self.count), self.cols
        if number == 2:
            src, dst, to = self.from_core.at[0, some, :, cols], self.from_y.at[some, :, cols], self.beside
        else:
            rows = self.at(1 - self.y if number == 0 else self.y, 1 - self.core)
            src, dst, to = self.grads.at[some, rows, cols], self.from_core.at[number, some, :, cols], self.sibling
        return push(src, dst, self.send.at[number], self.recv.at[number], (self.seq, to))

    def first(self):
        self.hop(0).start()
        self.hop(1).start()

    def second(self):
        self.hop(0).wait_recv()
        rows = self.at(1 - self.y, self.core)

        def some(at, _):
            value = self.grads[at, rows, self.cols].astype(jnp.float32)
            value = value + self.from_core[0, at, :, self.cols].astype(jnp.float32)
            self.from_core[0, at, :, self.cols] = value.astype(LOW)
            return 0

        lax.fori_loop(self.begin, self.begin + self.count, some, 0)
        self.hop(2).start()

    def third(self):
        self.hop(1).wait_recv()
        self.hop(2).wait_recv()
        rows = self.at(self.y, self.core)

        def some(at, _):
            value = self.grads[at, rows, self.cols].astype(jnp.float32)
            value = value + self.from_core[1, at, :, self.cols].astype(jnp.float32)
            value = value + self.from_y[at, :, self.cols].astype(jnp.float32)
            self.total[at, :, self.cols] = value.astype(LOW)
            return 0

        lax.fori_loop(self.begin, self.begin + self.count, some, 0)

    def finish(self):
        for number in range(3):
            self.hop(number).wait_send()


def reduce_sems():
    return [pltpu.SemaphoreType.DMA((3,)), pltpu.SemaphoreType.DMA((3,))]


def reduce_bufs(ranks, own, cols):
    return [pltpu.VMEM((2, ranks, own, cols), LOW), pltpu.VMEM((ranks, own, cols), LOW)]


class Deliver:
    def __init__(self, rows, out, cols, ranks, sems):
        self.rows, self.out, self.cols, self.ranks = rows, out, cols, ranks
        self.send, self.recv, self.here = sems
        self.seq, self.dp = lax.axis_index("seq"), lax.axis_index("dp")

    def exchange(self):
        for step in range(1, self.ranks):
            peer = lax.rem(self.seq + step, self.ranks)
            yield push(
                self.rows.at[peer, :, self.cols],
                self.out.at[self.seq, :, self.cols],
                self.send.at[step],
                self.recv.at[step],
                (peer, self.dp),
            )

    def keep(self):
        return pltpu.make_async_copy(
            self.rows.at[self.seq, :, self.cols], self.out.at[self.seq, :, self.cols], self.here
        )

    def start(self):
        self.keep().start()
        for copy in self.exchange():
            copy.start()

    def finish(self):
        self.keep().wait()
        for copy in self.exchange():
            copy.wait_recv()
        for copy in self.exchange():
            copy.wait_send()


def deliver_sems(ranks):
    return [pltpu.SemaphoreType.DMA((ranks,)), pltpu.SemaphoreType.DMA((ranks,)), pltpu.SemaphoreType.DMA]


def first_kernel(
    ranks, kv_heads, order, starts, tokens, out_grad, freqs, attn_gain, mlp_gain, query_gain, key_gain,
    w_query, w_key, w_value, w_output, w_gate, w_up, w_down,
    resid, second, cosv, sinv, q_low, k_low, v_low, out_low, first_in, qkv, attn_block, dy_all, prob, mlp_block,
    held, normal, kept, block, a_rows, m_rows, gate, up, down, dys, probs, pos, begins, pos_row,
    term, out_buf, in_buf, *sems,
):
    local, width = tokens.shape
    rows = local * ranks
    own = w_query.shape[0]
    size = freqs.shape[1]
    heads = q_low.shape[0]
    share = heads // kv_heads
    half = ranks // 2
    scale = 1.0 / math.sqrt(size)
    cols = (heads + 2 * kv_heads) * size
    deep = block.shape[1]
    row = functools.partial(block_row, local=local, ranks=ranks)
    seq, dp = lax.axis_index("seq"), lax.axis_index("dp")
    right, left = neighbours(ranks)
    attn = Spread(a_rows, block, ranks, own, pl.ds(0, a_rows.shape[2]), sems[8:13])
    third = m_rows.shape[2] // 3
    mlp = [
        Spread(m_rows, mlp_block, ranks, own, pl.ds(at * third, third), sems[13 + 5 * at : 18 + 5 * at])
        for at in range(3)
    ]
    local_sems = sems[28]
    peers = [(lax.rem(seq + step, ranks), dp) for step in range(1, ranks)]
    peers += [(seq, attn.beside), (seq, attn.sibling)]
    knock(peers)
    loads = [
        move(src, dst, local_sems.at[at])
        for at, (src, dst) in enumerate(((w_gate, gate), (w_up, up), (w_down, down)))
    ]
    held[pl.ds(row(0), local)] = tokens[...]
    dys[pl.ds(row(0), local)] = out_grad[...]

    def column(line):
        same = lax.broadcasted_iota(jnp.int32, (own, own), 0) == lax.broadcasted_iota(jnp.int32, (own, own), 1)
        return jnp.sum(jnp.where(same, line, 0.0), 1, keepdims=True)

    def lay(target, begin, weight, gain):
        each = weight.shape[1] // ranks
        for rank in range(ranks):
            part = weight[:, rank * each : (rank + 1) * each]
            if gain is not None:
                part = (part.astype(jnp.float32) * gain).astype(LOW)
            target[rank, :, begin : begin + each] = part
        return begin + each

    gain = column(attn_gain[...])
    at = 0
    for weight in (w_query, w_key, w_value):
        at = lay(a_rows, at, weight, gain)
    lay(a_rows, at, w_output, None)
    answered(peers)
    ring = RingGather(held, local, ranks, sems[0], sems[1], right, left, row)
    ring.start(1)
    attn.start()
    line = LineGather(dys, local, ranks, sems[4], sems[5], sems[6], sems[7])
    stores = []

    def store(src, dst):
        stores.append(move(src, dst, local_sems.at[len(loads) + len(stores)]))

    def scale_rows(step):
        for rel in rels_of(step, ranks):

            def some(at, _):
                rows_at = pl.ds(pl.multiple_of(row(rel) + at * 32, 32), 32)
                normal[rows_at] = rows_scaled(held[rows_at].astype(jnp.float32))[0].astype(LOW)
                return 0

            lax.fori_loop(0, local // 32, some, 0)

    for load in loads:
        load.wait()
    gain = column(mlp_gain[...])
    each = gate.shape[1] // ranks
    lay(m_rows, 0, gate, gain)
    lay(m_rows, each, up, gain)
    lay(m_rows, 2 * each, down, None)
    scale_rows(0)
    ring.arrive(1)
    ring.start(2)
    scale_rows(1)
    attn.arrive()
    attn.hop(0).start()
    attn.hop(1).start()
    spans = order.shape[0]
    span = rows // spans
    for at in range(ranks):
        rows_at = pl.ds(at * local, local)
        ids = at * local + lax.broadcasted_iota(jnp.int32, (1, local), 1)
        where = jnp.zeros_like(ids)
        for slot in range(spans):
            inside = (ids >= slot * span) & (ids < (slot + 1) * span)
            where = where + jnp.where(inside, ids + (order[slot] - slot) * span, 0)
        begin = jnp.zeros_like(ids)
        for doc in range(starts.shape[1]):
            begin = jnp.maximum(begin, jnp.where(starts[0, doc] <= where, starts[0, doc], 0))
        pos_row[:, rows_at] = where
        across = jnp.broadcast_to(where, (local, local)).T
        pos[rows_at] = across[:, :1]
        begins[rows_at] = jnp.broadcast_to(begin, (local, local)).T[:, :1]
        angle = across[:, :1].astype(jnp.float32) * freqs[...]
        lane = lax.broadcasted_iota(jnp.int32, (local, size), 1)
        cosv[rows_at] = jnp.cos(angle)
        sine = jnp.sin(angle)
        sinv[rows_at] = jnp.where(lane < size // 2, -sine, sine)
    for step in range(2, half):
        ring.arrive(step)
        ring.start(step + 1)
        scale_rows(step)
        if step == 2:
            attn.hop(0).wait_recv()
            attn.hop(2).start()
    for piece in mlp:
        piece.start()
    attn.hop(1).wait_recv()
    attn.hop(2).wait_recv()
    store(block, attn_block)

    def project(begin, count):
        rows_at = pl.ds(begin, count)
        kept[rows_at] = dot_nn(normal[rows_at], block[:, :, :cols].reshape(width, cols))

    ring.arrive(half)
    scale_rows(half)
    store(normal, first_in)
    tile = rows // half

    def rotated(at, rows_at, gain):
        v = rows_scaled(kept[rows_at, at * size : (at + 1) * size])[0] * gain[...]
        return (v * cosv[rows_at] + turn(v) * sinv[rows_at]).astype(LOW)

    for piece in range(half):
        rows_at = pl.ds(piece * tile, tile)
        project(piece * tile, tile)
        for head in range(heads):
            q_low[head, rows_at] = rotated(head, rows_at, query_gain)
        for group in range(kv_heads):
            k_low[group, rows_at] = rotated(heads + group, rows_at, key_gain)
            at = (heads + kv_heads + group) * size
            v_low[group, rows_at] = kept[rows_at, at : at + size].astype(LOW)
    store(kept, qkv)

    def forward(piece):
        mlp[piece].arrive()
        mlp[piece].hop(0).start()
        mlp[piece].hop(1).start()

    for piece in range(half):
        rows_at = pl.ds(piece * tile, tile)
        seen = (pos_row[...] <= pos[rows_at]) & (pos_row[...] >= begins[rows_at])
        for head in range(heads):
            raw = dot_nt(q_low[head, rows_at], k_low[head // share]) * scale
            raw = jnp.where(seen, raw, NEG)
            weight = jnp.exp(raw - jnp.max(raw, -1, keepdims=True))
            weight = (weight * (1.0 / jnp.sum(weight, -1, keepdims=True))).astype(LOW)
            probs[head, rows_at] = weight
            value = dot_nn(weight, v_low[head // share])
            out_low[rows_at, head * size : (head + 1) * size] = value.astype(LOW)
            store(probs.at[head, rows_at], prob.at[head, rows_at])
        if piece == half - 2:
            line.start(1)
            forward(0)
        if piece == half - 1:
            forward(1)

    def part(rels):
        def some(at, _):
            value = dot_nt(block_rows(out_low, rels, local, ranks), block[at, :, cols:])
            term[: len(rels) * local, pl.ds(pl.multiple_of(at * deep, deep), deep)] = value
            return 0

        lax.fori_loop(0, ranks, some, 0)

    total = RingSum(part, term, out_buf, in_buf, local, ranks, sems[2], sems[3], right, left)
    for step in range(1, half + 1):
        total.compute(step)
        total.launch(step)
        if step == 1:
            forward(2)
        if step < half:
            line.advance(step)
        if 1 < step:
            mlp[step - 2].hop(0).wait_recv()
            mlp[step - 2].hop(2).start()
    total.compute(half + 1)
    total.arrive_last()

    def some(at, _):
        begin = pl.multiple_of(at * 32, 32)
        rows_at = pl.ds(begin, 32)
        value = tokens[rows_at].astype(jnp.float32) + total.last(begin, 32)
        resid[rows_at] = value
        second[rows_at] = rows_scaled(value)[0].astype(LOW)
        return 0

    lax.fori_loop(0, local // 32, some, 0)
    line.complete()
    store(dys, dy_all)
    ring.finish()
    attn.finish()
    total.finish()
    line.finish()
    for piece in mlp:
        piece.hop(1).wait_recv()
        piece.hop(2).wait_recv()
        piece.finish()
    for given in stores:
        given.wait()


def mlp_kernel(
    ranks, second, out_grad, rest, dys, mlp_block, block_out, dresid, dresid_low, own_grads,
    grads, from_core, from_y, held, weights, hidden, dgu, resid, dy_all,
    term, out_buf, in_buf, y_out, y_in, here, *sems,
):
    local, width = second.shape
    row = functools.partial(block_row, local=local, ranks=ranks)
    ff = hidden.shape[1]
    deep = weights.shape[1]
    half = ranks // 2
    right, left = neighbours(ranks)
    loads = [
        move(src, dst, here.at[at])
        for at, (src, dst) in enumerate(((mlp_block, weights), (dys, dy_all), (rest, resid)))
    ]
    seq, dp = lax.axis_index("seq"), lax.axis_index("dp")
    own = own_grads.shape[1]
    pieces = [
        Reduce(
            grads, from_core, from_y, own_grads, own, at * ranks // 4, ranks // 4, pl.ds(0, 3 * ff),
            sems[6 + 2 * at : 8 + 2 * at],
        )
        for at in range(4)
    ]
    peers = [right, left, (seq, pieces[0].beside), (seq, pieces[0].sibling)]
    knock(peers)
    held[pl.ds(row(0), local)] = second[...]
    answered(peers)
    ring = RingGather(held, local, ranks, sems[0], sems[1], right, left, row)
    ring.start(1)
    loads[0].wait()
    loads[1].wait()
    wide = 256

    def middle(step):
        rels = rels_of(step, ranks)

        def some(at, _):
            first = pl.multiple_of(at * wide, wide)
            given, dy = block_rows(held, rels, local, ranks), block_rows(dy_all, rels, local, ranks)
            gate = dot_nn(given, weights[:, :, pl.ds(first, wide)].reshape(width, wide))
            upper = dot_nn(given, weights[:, :, pl.ds(ff + first, wide)].reshape(width, wide))
            dmid = dot_nn(dy, weights[:, :, pl.ds(2 * ff + first, wide)].reshape(width, wide))
            sigma = 1.0 / (1.0 + jnp.exp(-gate))
            act = gate * sigma
            value = (act * upper).astype(LOW)
            dgate = (dmid * upper * (sigma * (1.0 + gate * (1.0 - sigma)))).astype(LOW)
            dupper = (dmid * act).astype(LOW)
            for at, rel in enumerate(rels):
                rows, some_rows = pl.ds(row(rel), local), slice(at * local, (at + 1) * local)
                hidden[rows, pl.ds(first, wide)] = value[some_rows]
                dgu[rows, pl.ds(first, wide)] = dgate[some_rows]
                dgu[rows, pl.ds(ff + first, wide)] = dupper[some_rows]
            return 0

        lax.fori_loop(0, ff // wide, some, 0)

    middle(0)
    for step in range(1, half + 1):
        ring.arrive(step)
        if step < half:
            ring.start(step + 1)
        middle(step)

    def back_part(rels):
        def some(at, _):
            value = dot_nt(block_rows(dgu, rels, local, ranks), weights[at, :, : 2 * ff])
            term[: len(rels) * local, pl.ds(pl.multiple_of(at * deep, deep), deep)] = value
            return 0

        lax.fori_loop(0, ranks, some, 0)

    def out_part(rels):
        def some(at, _):
            value = dot_nt(block_rows(hidden, rels, local, ranks), weights[at, :, 2 * ff :])
            term[: len(rels) * local, pl.ds(pl.multiple_of(at * deep, deep), deep)] = value
            return 0

        lax.fori_loop(0, ranks, some, 0)

    def weight_grads(first, count):
        def some(at, _):
            cols = pl.ds(pl.multiple_of(at * deep, deep), deep)
            grads[at, :, : 2 * ff] = dot_tn(held[:, cols], dgu[...]).astype(LOW)
            grads[at, :, 2 * ff :] = dot_tn(dy_all[:, cols], hidden[...]).astype(LOW)
            return 0

        lax.fori_loop(first, first + count, some, 0)

    back = RingSum(back_part, term, out_buf, in_buf, local, ranks, sems[2], sems[3], right, left)
    out = RingSum(out_part, term, y_out, y_in, local, ranks, sems[4], sems[5], right, left)
    for step in range(1, half + 1):
        back.compute(step)
        back.launch(step)
        out.compute(step)
        out.launch(step)
        if step < 3:
            for piece in pieces[2 * step - 2 : 2 * step]:
                weight_grads(piece.begin, piece.count)
                piece.first()
        if 1 < step < 4:
            for piece in pieces[2 * step - 4 : 2 * step - 2]:
                piece.second()
        if step > 2:
            for piece in pieces[2 * step - 6 : 2 * step - 4]:
                piece.third()
    back.compute(half + 1)
    loads[2].wait()
    back.arrive_last()

    def finish_back(at, _):
        begin = pl.multiple_of(at * 32, 32)
        rows = pl.ds(begin, 32)
        value = resid[rows]
        inv = rows_scaled(value)[1]
        grad = back.last(begin, 32)
        full = out_grad[rows].astype(jnp.float32) + rows_scaled_back(value, inv, grad)
        dresid[rows] = full
        dresid_low[rows] = full.astype(LOW)
        return 0

    lax.fori_loop(0, local // 32, finish_back, 0)
    out.compute(half + 1)
    out.arrive_last()

    def finish_out(at, _):
        begin = pl.multiple_of(at * 32, 32)
        rows = pl.ds(begin, 32)
        block_out[rows] = (resid[rows] + out.last(begin, 32)).astype(LOW)
        return 0

    lax.fori_loop(0, local // 32, finish_out, 0)
    ring.finish()
    back.finish()
    out.finish()
    for piece in pieces:
        piece.finish()


def back_kernel(
    ranks, kv_heads, tokens, dresid_low, query_gain, key_gain, out_low_in, first_in_in, block_in,
    qkv_in, cos_in, sin_in, q_in, k_in, v_in, prob_in, dresid_in, mlp_own,
    tokens_grad, gains, mlp_sums, attn_sums,
    grads, from_core, from_y, own_grads, query_gain_grad, key_gain_grad,
    tile, tiles_in, tile_sum, tile_sums_in, held, dout, dk, dv, dqkv,
    out_low, first_in, attn_block, qkv, cosv, sinv, q_low, k_low, v_low, prob, dresid, term, out_buf, in_buf, *sems,
):
    local, width = tokens.shape
    rows = local * ranks
    half = ranks // 2
    size = cosv.shape[1]
    heads = q_low.shape[0]
    share = heads // kv_heads
    scale = 1.0 / math.sqrt(size)
    cols = (heads + 2 * kv_heads) * size
    deep = attn_block.shape[1]
    o_cols = heads * size
    right, left = neighbours(ranks)
    seq, dp = lax.axis_index("seq"), lax.axis_index("dp")
    own = mlp_own.shape[1]
    copies = lax.axis_size("dp")
    row = functools.partial(block_row, local=local, ranks=ranks)
    all_cols = grads.shape[2]
    out_piece = Reduce(
        grads, from_core, from_y, own_grads, own, 0, ranks, pl.ds(cols, all_cols - cols), sems[4:6]
    )
    qkv_piece = Reduce(grads, from_core, from_y, own_grads, own, 0, ranks, pl.ds(0, cols), sems[6:8])
    third = mlp_own.shape[2] // 3
    mlp_ways = [
        Deliver(mlp_own, mlp_sums, pl.ds(at * third, third), ranks, [*sems[8:11], *sems[22:28]][3 * at : 3 * at + 3])
        for at in range(3)
    ]
    out_way = Deliver(own_grads, attn_sums, pl.ds(cols, all_cols - cols), ranks, sems[11:14])
    qkv_way = Deliver(own_grads, attn_sums, pl.ds(0, cols), ranks, sems[14:17])
    peers = [(lax.rem(seq + step, ranks), dp) for step in range(1, ranks)]
    peers += [(seq, lax.rem(dp + step, copies)) for step in range(1, copies)]
    knock(peers)
    local_sems = sems[21]
    loads = {}
    for at, (name, src, dst) in enumerate(
        (
            ("block", block_in, attn_block), ("out", out_low_in, out_low), ("v", v_in, v_low),
            ("prob", prob_in, prob), ("k", k_in, k_low), ("q", q_in, q_low), ("cos", cos_in, cosv),
            ("sin", sin_in, sinv), ("qkv", qkv_in, qkv), ("first", first_in_in, first_in),
            ("dresid", dresid_in, dresid),
        )
    ):
        loads[name] = move(src, dst, local_sems.at[at])
    held[pl.ds(row(0), local)] = dresid_low[...]
    answered(peers)
    ring = RingGather(held, local, ranks, sems[0], sems[1], right, left, row)
    ring.start(1)
    loads["block"].wait()

    def project(step):
        rels = rels_of(step, ranks)
        weight = attn_block[:, :, cols:].reshape(width, o_cols)
        value = dot_nn(block_rows(held, rels, local, ranks), weight).astype(LOW)
        for at, rel in enumerate(rels):
            dout[pl.ds(row(rel), local)] = value[at * local : (at + 1) * local]

    project(0)
    for step in range(1, half + 1):
        ring.arrive(step)
        if step < half:
            ring.start(step + 1)
        if step == half - 1:
            for way in mlp_ways:
                way.start()
        project(step)
    loads["out"].wait()

    def out_grads(at, _):
        some_cols = pl.ds(pl.multiple_of(at * deep, deep), deep)
        grads[at, :, cols:] = dot_tn(held[:, some_cols], out_low[...]).astype(LOW)
        return 0

    lax.fori_loop(0, ranks, out_grads, 0)
    out_piece.first()
    for name in ("v", "prob", "k", "q", "cos", "sin", "qkv"):
        loads[name].wait()
    tall = rows // half
    query_gain_grad[...] = jnp.zeros_like(query_gain_grad)
    key_gain_grad[...] = jnp.zeros_like(key_gain_grad)

    def unrotated(grad, column, rows_at, gain, gain_grad_ref):
        grad = grad * cosv[rows_at] - turn(grad) * sinv[rows_at]
        value = qkv[rows_at, column * size : (column + 1) * size]
        normal, inv = rows_scaled(value)
        gain_grad_ref[...] += jnp.sum(grad * normal, 0, keepdims=True)
        back = rows_scaled_back(value, inv, grad * gain[...])
        dqkv[rows_at, column * size : (column + 1) * size] = back.astype(LOW)

    for head in range(heads):
        group = head // share

        def one(piece, _):
            rows_at = pl.ds(pl.multiple_of(piece * tall, tall), tall)
            weight = prob[head, rows_at]
            grad = dout[rows_at, head * size : (head + 1) * size]
            dprob = dot_nt(grad, v_low[group])
            full = weight.astype(jnp.float32)
            delta = jnp.sum(full * dprob, -1, keepdims=True)
            dscore = (full * (dprob - delta)).astype(LOW)
            dq = dot_nn(dscore, k_low[group]) * scale
            dk_add = dot_tn(dscore, q_low[head, rows_at]) * scale
            dv_add = dot_tn(weight, grad)
            dk[group] += dk_add
            dv[group] += dv_add
            unrotated(dq, head, rows_at, query_gain, query_gain_grad)
            return 0

        if head % share == 0:
            dk[group] = jnp.zeros_like(dk[group])
            dv[group] = jnp.zeros_like(dv[group])
        lax.fori_loop(0, half, one, 0)
        if head == 0:
            out_piece.second()
    for group in range(kv_heads):
        def one_key(piece, _):
            rows_at = pl.ds(pl.multiple_of(piece * tall, tall), tall)
            unrotated(dk[group, rows_at], heads + group, rows_at, key_gain, key_gain_grad)
            at = (heads + kv_heads + group) * size
            dqkv[rows_at, at : at + size] = dv[group, rows_at].astype(LOW)
            return 0

        lax.fori_loop(0, half, one_key, 0)

    def part(rels):
        def some(at, _):
            value = dot_nt(block_rows(dqkv, rels, local, ranks), attn_block[at, :, :cols])
            term[: len(rels) * local, pl.ds(pl.multiple_of(at * deep, deep), deep)] = value
            return 0

        lax.fori_loop(0, ranks, some, 0)

    def qkv_grads(at, _):
        some_cols = pl.ds(pl.multiple_of(at * deep, deep), deep)
        grads[at, :, :cols] = dot_tn(first_in[:, some_cols], dqkv[...]).astype(LOW)
        return 0

    def to_ranks(step):
        peer = lax.rem(seq + step, ranks)
        return push(tile, tiles_in.at[seq], sems[17].at[step], sems[18].at[step], (peer, dp))

    def to_copies(step):
        peer = lax.rem(dp + step, copies)
        return push(
            tile_sum, tile_sums_in.at[dp], sems[19].at[step], sems[20].at[step], (seq, peer)
        )

    tile[0:1] = query_gain_grad[...]
    tile[1:2] = key_gain_grad[...]
    tile[2:] = jnp.zeros((tile.shape[0] - 2, size), jnp.float32)
    for step in range(1, ranks):
        to_ranks(step).start()
    tiles_in[seq] = tile[...]
    total = RingSum(part, term, out_buf, in_buf, local, ranks, sems[2], sems[3], right, left)
    for step in range(1, half + 1):
        total.compute(step)
        total.launch(step)
        if step == 1:
            loads["first"].wait()
            lax.fori_loop(0, ranks, qkv_grads, 0)
            qkv_piece.first()
            out_piece.third()
            out_way.start()
        if step == 2:
            qkv_piece.second()
            for other in range(1, ranks):
                to_ranks(other).wait_recv()
            tile_sum[...] = jnp.sum(tiles_in[...], 0)
            for other in range(1, copies):
                to_copies(other).start()
            tile_sums_in[dp] = tile_sum[...]
        if step == half - 1:
            for other in range(1, copies):
                to_copies(other).wait_recv()
            gains[...] = jnp.sum(tile_sums_in[...], 0)
            qkv_piece.third()
            qkv_way.start()
    total.compute(half + 1)
    loads["dresid"].wait()
    total.arrive_last()

    def last(at, _):
        begin = pl.multiple_of(at * 32, 32)
        rows_at = pl.ds(begin, 32)
        value = tokens[rows_at].astype(jnp.float32)
        inv = rows_scaled(value)[1]
        grad = total.last(begin, 32)
        tokens_grad[rows_at] = dresid[rows_at] + rows_scaled_back(value, inv, grad)
        return 0

    lax.fori_loop(0, local // 32, last, 0)
    for step in range(1, ranks):
        to_ranks(step).wait_send()
    for step in range(1, copies):
        to_copies(step).wait_send()
    ring.finish()
    total.finish()
    out_piece.finish()
    qkv_piece.finish()
    for way in mlp_ways:
        way.finish()
    out_way.finish()
    qkv_way.finish()


def leave_kernel(
    attn_sums, mlp_sums, attn_gain, mlp_gain, w_query, w_key, w_value, w_gate, w_up,
    query_out, key_out, value_out, output_out, gate_out, up_out, down_out, attn_out, mlp_out,
):
    own = attn_gain.shape[1]
    same = lax.broadcasted_iota(jnp.int32, (own, own), 0) == lax.broadcasted_iota(jnp.int32, (own, own), 1)

    @pl.when(pl.program_id(0) == 0)
    def _():
        attn_out[...] = jnp.zeros_like(attn_out)
        mlp_out[...] = jnp.zeros_like(mlp_out)

    for sums, gain, gain_out, parts in (
        (attn_sums, attn_gain, attn_out, ((query_out, w_query), (key_out, w_key), (value_out, w_value), (output_out, None))),
        (mlp_sums, mlp_gain, mlp_out, ((gate_out, w_gate), (up_out, w_up), (down_out, None))),
    ):
        scale = jnp.sum(jnp.where(same, gain[...], 0.0), 1, keepdims=True)
        at = 0
        for out, weight in parts:
            value = sums[0, :, at : at + out.shape[1]].astype(jnp.float32)
            at += out.shape[1]
            if weight is None:
                out[...] = value
                continue
            out[...] = value * scale
            inner = jnp.sum(value * weight[...].astype(jnp.float32), 1, keepdims=True)
            gain_out[...] += jnp.sum(jnp.where(same, inner, 0.0), 0, keepdims=True)


VM = pl.BlockSpec(memory_space=pltpu.VMEM)
SM = pl.BlockSpec(memory_space=pltpu.SMEM)
ANY = pl.BlockSpec(memory_space=pl.ANY)


def call(kernel, number, ins, outs, scratch, operands):
    return pl.pallas_call(
        kernel,
        out_shape=[jax.ShapeDtypeStruct(shape, dtype) for shape, dtype, _ in outs],
        in_specs=ins,
        out_specs=[spec for _, _, spec in outs],
        scratch_shapes=scratch,
        compiler_params=pltpu.CompilerParams(
            collective_id=number, has_side_effects=True, vmem_limit_bytes=LIMIT
        ),
    )(*operands)


def columns_body(
    tokens,
    out_grad,
    span_order,
    doc_starts,
    w_query,
    w_key,
    w_value,
    w_output,
    attn_gain,
    query_gain,
    key_gain,
    w_gate,
    w_up,
    w_down,
    mlp_gain,
):
    ranks = lax.axis_size("seq")
    copies = lax.axis_size("dp")
    _, local, width = tokens.shape
    rows = local * ranks
    size = query_gain.shape[0]
    kv_heads = w_key.shape[1] // size // ranks
    heads = w_query.shape[1] // size // ranks
    q_cols, kv_cols = heads * size, kv_heads * size
    qkv_cols = q_cols + 2 * kv_cols
    a_cols = qkv_cols + q_cols
    ff = w_gate.shape[1] // ranks
    own = width // (ranks * copies)
    deep = own * copies
    half = ranks // 2
    f32, i32 = jnp.float32, jnp.int32
    exponents = np.arange(size) % (size // 2) * (-2.0 / size * math.log(1000000.0))
    freqs = jnp.asarray(np.exp(exponents)[None], f32)
    q_gain, k_gain = query_gain[None], key_gain[None]
    (
        resid, second, cosv, sinv, q_low, k_low, v_low, out_low, first_in, qkv, attn_block, dy_all, prob, mlp_block,
    ) = call(
        functools.partial(first_kernel, ranks, kv_heads),
        1,
        [SM, SM] + [VM] * 11 + [ANY] * 3,
        [
            ((local, width), f32, VM),
            ((local, width), LOW, VM),
            ((rows, size), f32, VM),
            ((rows, size), f32, VM),
            ((heads, rows, size), LOW, VM),
            ((kv_heads, rows, size), LOW, VM),
            ((kv_heads, rows, size), LOW, VM),
            ((rows, q_cols), LOW, VM),
            ((rows, width), LOW, ANY),
            ((rows, qkv_cols), f32, ANY),
            ((ranks, deep, a_cols), LOW, ANY),
            ((rows, width), LOW, ANY),
            ((heads, rows, rows), LOW, ANY),
            ((ranks, deep, 3 * ff), LOW, ANY),
        ],
        [
            pltpu.VMEM((rows, width), LOW),
            pltpu.VMEM((rows, width), LOW),
            pltpu.VMEM((rows, qkv_cols), f32),
            pltpu.VMEM((ranks, deep, a_cols), LOW),
            pltpu.VMEM((ranks, own, a_cols), LOW),
            pltpu.VMEM((ranks, own, 3 * ff), LOW),
        ]
        + [pltpu.VMEM((own, ff * ranks), LOW)] * 3
        + [
            pltpu.VMEM((rows, width), LOW),
            pltpu.VMEM((heads, rows, rows), LOW),
            pltpu.VMEM((rows, 1), i32),
            pltpu.VMEM((rows, 1), i32),
            pltpu.VMEM((1, rows), i32),
        ]
        + sum_bufs(local, ranks, width)
        + ring_sems(ranks) * 2
        + line_sems(ranks)
        + spread_sems(ranks) * 4
        + [pltpu.SemaphoreType.DMA((heads * half + 8,))],
        (
            span_order, doc_starts, tokens[0], out_grad[0], freqs, attn_gain[None], mlp_gain[None], q_gain, k_gain,
            w_query, w_key, w_value, w_output, w_gate, w_up, w_down,
        ),
    )
    block_out, dresid, dresid_low, mlp_own = call(
        functools.partial(mlp_kernel, ranks),
        2,
        [VM, VM, ANY, ANY, ANY],
        [
            ((local, width), LOW, VM),
            ((local, width), f32, VM),
            ((local, width), LOW, VM),
            ((ranks, own, 3 * ff), LOW, VM),
        ],
        [pltpu.VMEM((ranks, deep, 3 * ff), LOW)]
        + reduce_bufs(ranks, own, 3 * ff)
        + [
            pltpu.VMEM((rows, width), LOW),
            pltpu.VMEM((ranks, deep, 3 * ff), LOW),
            pltpu.VMEM((rows, ff), LOW),
            pltpu.VMEM((rows, 2 * ff), LOW),
            pltpu.VMEM((local, width), f32),
            pltpu.VMEM((rows, width), LOW),
        ]
        + sum_bufs(local, ranks, width)
        + sum_bufs(local, ranks, width)[1:]
        + [pltpu.SemaphoreType.DMA((3,))]
        + ring_sems(ranks) * 3
        + reduce_sems() * 4,
        (second, out_grad[0], resid, dy_all, mlp_block),
    )
    tokens_grad, gains, mlp_sums, attn_sums = call(
        functools.partial(back_kernel, ranks, kv_heads),
        3,
        [VM] * 4 + [ANY] * 12,
        [
            ((local, width), f32, VM),
            ((8, size), f32, VM),
            ((ranks, own, 3 * ff), LOW, ANY),
            ((ranks, own, a_cols), LOW, VM),
        ],
        [pltpu.VMEM((ranks, deep, a_cols), LOW)]
        + reduce_bufs(ranks, own, a_cols)
        + [
            pltpu.VMEM((ranks, own, a_cols), LOW),
            pltpu.VMEM((1, size), f32),
            pltpu.VMEM((1, size), f32),
            pltpu.VMEM((8, size), f32),
            pltpu.VMEM((ranks, 8, size), f32),
            pltpu.VMEM((8, size), f32),
            pltpu.VMEM((copies, 8, size), f32),
            pltpu.VMEM((rows, width), LOW),
            pltpu.VMEM((rows, q_cols), LOW),
            pltpu.VMEM((kv_heads, rows, size), f32),
            pltpu.VMEM((kv_heads, rows, size), f32),
            pltpu.VMEM((rows, qkv_cols), LOW),
            pltpu.VMEM((rows, q_cols), LOW),
            pltpu.VMEM((rows, width), LOW),
            pltpu.VMEM((ranks, deep, a_cols), LOW),
            pltpu.VMEM((rows, qkv_cols), f32),
            pltpu.VMEM((rows, size), f32),
            pltpu.VMEM((rows, size), f32),
            pltpu.VMEM((heads, rows, size), LOW),
            pltpu.VMEM((kv_heads, rows, size), LOW),
            pltpu.VMEM((kv_heads, rows, size), LOW),
            pltpu.VMEM((heads, rows, rows), LOW),
            pltpu.VMEM((local, width), f32),
        ]
        + sum_bufs(local, ranks, width)
        + ring_sems(ranks) * 2
        + reduce_sems() * 2
        + deliver_sems(ranks) * 3
        + [pltpu.SemaphoreType.DMA((ranks,))] * 2
        + [pltpu.SemaphoreType.DMA((copies,))] * 2
        + [pltpu.SemaphoreType.DMA((11,))]
        + deliver_sems(ranks) * 2,
        (
            tokens[0], dresid_low, q_gain, k_gain, out_low, first_in, attn_block, qkv, cosv, sinv, q_low, k_low,
            v_low, prob, dresid, mlp_own,
        ),
    )
    whole = pl.BlockSpec((1, own), lambda at: (0, 0))
    each = (q_cols, kv_cols, kv_cols, q_cols, ff, ff, ff)
    columns = [pl.BlockSpec((own, cols), lambda at: (0, at)) for cols in each]
    *grads, dga, dgm = pl.pallas_call(
        leave_kernel,
        grid=(ranks,),
        out_shape=[jax.ShapeDtypeStruct((own, cols * ranks), f32) for cols in each]
        + [jax.ShapeDtypeStruct((1, own), f32)] * 2,
        in_specs=[
            pl.BlockSpec((1, own, a_cols), lambda at: (at, 0, 0)),
            pl.BlockSpec((1, own, 3 * ff), lambda at: (at, 0, 0)),
            whole,
            whole,
            *columns[:3],
            *columns[4:6],
        ],
        out_specs=columns + [whole, whole],
    )(attn_sums, mlp_sums, attn_gain[None], mlp_gain[None], w_query, w_key, w_value, w_gate, w_up)
    return (
        block_out[None], tokens_grad[None], *grads[:4], dga[0], gains[0], gains[1], *grads[4:], dgm[0],
    )


def body(*args):
    tokens, w_key, query_gain = args[0], args[5], args[9]
    groups = w_key.shape[1] // query_gain.shape[0]
    ranks = lax.axis_size("seq")
    if tokens.shape[0] == 1 and ranks % 2 == 0 and groups % ranks == 0 and lax.axis_size("dp") == 4:
        return columns_body(*args)
    return gathered_body(*args)


def solution(mesh):
    return jax.shard_map(
        body,
        mesh=mesh,
        in_specs=(
            P("dp", "seq", None),
            P("dp", "seq", None),
            P(),
            P("dp", None),
            P(("seq", "dp"), None),
            P(("seq", "dp"), None),
            P(("seq", "dp"), None),
            P(("seq", "dp"), None),
            P(("seq", "dp")),
            P(),
            P(),
            P(("seq", "dp"), None),
            P(("seq", "dp"), None),
            P(("seq", "dp"), None),
            P(("seq", "dp")),
        ),
        out_specs=(
            P("dp", "seq", None),
            P("dp", "seq", None),
            P(("seq", "dp"), None),
            P(("seq", "dp"), None),
            P(("seq", "dp"), None),
            P(("seq", "dp"), None),
            P(("seq", "dp")),
            P(),
            P(),
            P(("seq", "dp"), None),
            P(("seq", "dp"), None),
            P(("seq", "dp"), None),
            P(("seq", "dp")),
        ),
        check_vma=False,
    )
```

```python
import functools
import math

import jax
import jax.numpy as jnp
import numpy as np
from jax import lax
from jax.experimental import pallas as pl
from jax.experimental.pallas import tpu as pltpu
from jax.sharding import PartitionSpec as P

EPS = 1e-06
NEG = -1e30


def normed(v, gain):
    scale_inv = lax.rsqrt(jnp.mean(v * v, -1, keepdims=True) + EPS)
    return (v * scale_inv * gain, scale_inv)


def norm_back(v, scale_inv, gain, grad):
    scaled = grad * gain
    inner = jnp.mean(scaled * v, -1, keepdims=True)
    dv = scale_inv * scaled - v * scale_inv * scale_inv * scale_inv * inner
    dgain = jnp.sum((grad * v * scale_inv).reshape(-1, v.shape[-1]), 0)
    return (dv, dgain)


def rotary(pos, width):
    half = width // 2
    freqs = jnp.exp(jnp.arange(half, dtype=jnp.float32) * (-2.0 / width * math.log(1000000.0)))
    angle = pos.astype(jnp.float32)[:, None] * freqs[None, :]
    return (jnp.cos(angle)[:, None, :], jnp.sin(angle)[:, None, :])


def rotate(v, cosv, sinv):
    half = v.shape[-1] // 2
    first, second = (v[..., :half], v[..., half:])
    return jnp.concatenate([first * cosv - second * sinv, second * cosv + first * sinv], -1)


def rotate_back(grad, cosv, sinv):
    half = grad.shape[-1] // 2
    first, second = (grad[..., :half], grad[..., half:])
    return jnp.concatenate([first * cosv + second * sinv, second * cosv - first * sinv], -1)


def place(order, begin, count, span):
    rows = begin + jnp.arange(count, dtype=jnp.int32)
    slots = rows // span
    picked = slots[:, None] == jnp.arange(order.shape[0], dtype=jnp.int32)[None, :]
    return jnp.sum(jnp.where(picked, order[None, :], 0), -1) * span + rows % span


def doc_of(starts, pos):
    return jnp.sum((starts[:, None, :] <= pos[None, :, None]).astype(jnp.int32), -1)


def gathered_body(
    tokens,
    out_grad,
    span_order,
    doc_starts,
    w_query,
    w_key,
    w_value,
    w_output,
    attn_gain,
    query_gain,
    key_gain,
    w_gate,
    w_up,
    w_down,
    mlp_gain,
):
    seqs, local, width = tokens.shape
    span = local // 2
    head_size = query_gain.shape[0]
    kv_heads = w_key.shape[1] // head_size
    heads = w_query.shape[1] // head_size
    share = heads // kv_heads
    kv_width = kv_heads * head_size
    ff_width = w_gate.shape[1]
    scale = 1.0 / math.sqrt(head_size)
    total_rows = seqs * local
    own_rows = width // lax.axis_size(("seq", "dp"))
    qpos = place(span_order, lax.axis_index("seq") * local, local, span)
    qdoc = doc_of(doc_starts, qpos)
    cosv, sinv = rotary(qpos, head_size)

    def gather_attn():
        return (
            lax.all_gather(w_query, ("seq", "dp"), axis=0, tiled=True),
            lax.all_gather(w_key, ("seq", "dp"), axis=0, tiled=True),
            lax.all_gather(w_value, ("seq", "dp"), axis=0, tiled=True),
            lax.all_gather(w_output, ("seq", "dp"), axis=0, tiled=True),
            lax.all_gather(
                attn_gain.astype(jnp.bfloat16), ("seq", "dp"), axis=0, tiled=True
            ).astype(attn_gain.dtype),
        )

    def gather_mlp():
        return (
            lax.all_gather(w_gate, ("seq", "dp"), axis=0, tiled=True),
            lax.all_gather(w_up, ("seq", "dp"), axis=0, tiled=True),
            lax.all_gather(w_down, ("seq", "dp"), axis=0, tiled=True),
            lax.all_gather(mlp_gain.astype(jnp.bfloat16), ("seq", "dp"), axis=0, tiled=True).astype(
                mlp_gain.dtype
            ),
        )

    x_rows = tokens.astype(jnp.float32).reshape(total_rows, width)
    wq_all, wk_all, wv_all, wo_all, ga_all = gather_attn()
    first_norm, first_inv = normed(x_rows, ga_all)
    first_in = first_norm.astype(jnp.bfloat16)
    q_raw = jnp.dot(first_in, wq_all, preferred_element_type=jnp.float32).reshape(
        seqs, local, heads, head_size
    )
    k_raw = jnp.dot(first_in, wk_all, preferred_element_type=jnp.float32).reshape(
        seqs, local, kv_heads, head_size
    )
    v_low = (
        jnp.dot(first_in, wv_all, preferred_element_type=jnp.float32)
        .astype(jnp.bfloat16)
        .reshape(seqs, local, kv_heads, head_size)
    )
    q_normed, q_inv = normed(q_raw, query_gain)
    k_normed, k_inv = normed(k_raw, key_gain)
    q_low = rotate(q_normed, cosv, sinv).astype(jnp.bfloat16)
    k_low = rotate(k_normed, cosv, sinv).astype(jnp.bfloat16)
    q_group = q_low.reshape(seqs, local, kv_heads, share, head_size)

    def scores(piece_key, start):
        count = piece_key.shape[1]
        kpos = place(span_order, start, count, span)
        kdoc = doc_of(doc_starts, kpos)
        visible = (qdoc[:, :, None] == kdoc[:, None, :]) & (
            kpos[None, None, :] <= qpos[None, :, None]
        )
        raw = (
            jnp.einsum("sqgjd,skgd->sgjqk", q_group, piece_key, preferred_element_type=jnp.float32)
            * scale
        )
        return (raw, visible[:, None, None])

    start_top = jnp.full((seqs, kv_heads, share, local), NEG, jnp.float32)
    piece = (
        lax.all_gather(k_low, "seq", axis=1, tiled=True),
        lax.all_gather(v_low, "seq", axis=1, tiled=True),
    )
    top = start_top
    raw, visible = scores(piece[0], jnp.int32(0))
    raw = jnp.where(visible, raw, NEG)
    new_top = jnp.maximum(top, jnp.max(raw, -1))
    weights = jnp.where(visible, jnp.exp(raw - new_top[..., None]), 0.0)
    total = jnp.sum(weights, -1)
    summed = jnp.einsum(
        "sgjqk,skgd->sgjqd",
        weights.astype(jnp.bfloat16),
        piece[1],
        preferred_element_type=jnp.float32,
    )
    top, total, summed = (new_top, total, summed)
    log_total = top + jnp.log(total)
    attn_vals = summed / total[..., None]
    out_low = (
        jnp.transpose(attn_vals, (0, 3, 1, 2, 4))
        .reshape(total_rows, heads * head_size)
        .astype(jnp.bfloat16)
    )
    resid = x_rows + jnp.einsum("nh,dh->nd", out_low, wo_all, preferred_element_type=jnp.float32)
    wg_all, wu_all, wd_all, gm_all = gather_mlp()
    second_norm, second_inv = normed(resid, gm_all)
    second_in = second_norm.astype(jnp.bfloat16)
    gate = jnp.dot(second_in, wg_all, preferred_element_type=jnp.float32)
    upper = jnp.dot(second_in, wu_all, preferred_element_type=jnp.float32)
    sigma = jax.nn.sigmoid(gate)
    act = gate * sigma
    hidden = (act * upper).astype(jnp.bfloat16)
    result = resid + jnp.einsum("nf,df->nd", hidden, wd_all, preferred_element_type=jnp.float32)
    block_out = result.astype(jnp.bfloat16).reshape(seqs, local, width)
    grad_low = out_grad.reshape(total_rows, width)
    wg_all, wu_all, wd_all, gm_all = gather_mlp()
    dmid = jnp.einsum("nd,df->nf", grad_low, wd_all, preferred_element_type=jnp.float32)
    dgate = (dmid * upper * sigma * (1.0 + gate * (1.0 - sigma))).astype(jnp.bfloat16)
    dupper = (dmid * act).astype(jnp.bfloat16)
    left = second_in
    outer = grad_low
    mlp_sums = lax.psum_scatter(
        jnp.concatenate(
            [
                jnp.einsum("nd,nf->df", left, dgate, preferred_element_type=jnp.float32),
                jnp.einsum("nd,nf->df", left, dupper, preferred_element_type=jnp.float32),
                jnp.einsum("nd,nf->df", outer, hidden, preferred_element_type=jnp.float32),
            ],
            1,
        ),
        ("seq", "dp"),
        scatter_dimension=0,
        tiled=True,
    )
    dsecond = jnp.einsum(
        "nf,df->nd", dgate, wg_all, preferred_element_type=jnp.float32
    ) + jnp.einsum("nf,df->nd", dupper, wu_all, preferred_element_type=jnp.float32)
    dresid_norm, dgm = norm_back(resid, second_inv, gm_all, dsecond)
    dresid = grad_low.astype(jnp.float32) + dresid_norm
    dresid_low = dresid.astype(jnp.bfloat16)
    wq_all, wk_all, wv_all, wo_all, ga_all = gather_attn()
    dout_low = jnp.einsum(
        "nd,dh->nh", dresid_low, wo_all, preferred_element_type=jnp.float32
    ).astype(jnp.bfloat16)
    dout_group = dout_low.reshape(seqs, local, kv_heads, share, head_size)
    delta = jnp.sum(jnp.transpose(dout_group.astype(jnp.float32), (0, 2, 3, 1, 4)) * attn_vals, -1)
    piece = (
        lax.all_gather(k_low, "seq", axis=1, tiled=True),
        lax.all_gather(v_low, "seq", axis=1, tiled=True),
    )
    count = piece[0].shape[1]
    raw, visible = scores(piece[0], jnp.int32(0))
    prob = jnp.where(visible, jnp.exp(raw - log_total[..., None]), 0.0)
    dprob = jnp.einsum(
        "sqgjd,skgd->sgjqk", dout_group, piece[1], preferred_element_type=jnp.float32
    )
    dscore = (prob * (dprob - delta[..., None])).astype(jnp.bfloat16)
    dq_sum = jnp.einsum("sgjqk,skgd->sqgjd", dscore, piece[0], preferred_element_type=jnp.float32)
    dk_part = (
        jnp.einsum("sgjqk,sqgjd->skgd", dscore, q_group, preferred_element_type=jnp.float32) * scale
    )
    dv_part = jnp.einsum(
        "sgjqk,sqgjd->skgd",
        prob.astype(jnp.bfloat16),
        dout_group,
        preferred_element_type=jnp.float32,
    )
    joined = jnp.concatenate(
        [dk_part.reshape(seqs, count, kv_width), dv_part.reshape(seqs, count, kv_width)], -1
    )
    buffer = joined
    dq_sum, buffer = (dq_sum, buffer)
    key_sums = lax.psum_scatter(
        buffer.astype(jnp.bfloat16), "seq", scatter_dimension=1, tiled=True
    ).astype(jnp.float32)
    dq_rot = (dq_sum * scale).reshape(seqs, local, heads, head_size)
    dq_raw, dgq = norm_back(q_raw, q_inv, query_gain, rotate_back(dq_rot, cosv, sinv))
    dk_rot = key_sums[..., :kv_width].reshape(seqs, local, kv_heads, head_size)
    dk_raw, dgk = norm_back(k_raw, k_inv, key_gain, rotate_back(dk_rot, cosv, sinv))
    dq_low = dq_raw.reshape(total_rows, heads * head_size).astype(jnp.bfloat16)
    dk_low = dk_raw.reshape(total_rows, kv_width).astype(jnp.bfloat16)
    dv_low = key_sums[..., kv_width:].reshape(total_rows, kv_width).astype(jnp.bfloat16)
    left = first_in
    outer = dresid_low
    attn_sums = lax.psum_scatter(
        jnp.concatenate(
            [
                jnp.einsum("nd,nh->dh", left, dq_low, preferred_element_type=jnp.float32),
                jnp.einsum("nd,nh->dh", left, dk_low, preferred_element_type=jnp.float32),
                jnp.einsum("nd,nh->dh", left, dv_low, preferred_element_type=jnp.float32),
                jnp.einsum("nd,nh->dh", outer, out_low, preferred_element_type=jnp.float32),
            ],
            1,
        ),
        ("seq", "dp"),
        scatter_dimension=0,
        tiled=True,
    )
    dfirst = jnp.einsum("nh,dh->nd", dq_low, wq_all, preferred_element_type=jnp.float32)
    dfirst = dfirst + jnp.einsum("nh,dh->nd", dk_low, wk_all, preferred_element_type=jnp.float32)
    dfirst = dfirst + jnp.einsum("nh,dh->nd", dv_low, wv_all, preferred_element_type=jnp.float32)
    dx_norm, dga = norm_back(x_rows, first_inv, ga_all, dfirst)
    tokens_grad = (dresid + dx_norm).reshape(seqs, local, width)
    dga_all, dgm_all, dgq_all, dgk_all = lax.psum((dga, dgm, dgq, dgk), ("seq", "dp"))
    offset = lax.axis_index(("seq", "dp")) * own_rows
    attn_gain_grad = lax.dynamic_slice_in_dim(dga_all, offset, own_rows, 0)
    mlp_gain_grad = lax.dynamic_slice_in_dim(dgm_all, offset, own_rows, 0)
    q_cols = heads * head_size
    w_query_grad = attn_sums[:, :q_cols]
    w_key_grad = attn_sums[:, q_cols : q_cols + kv_width]
    w_value_grad = attn_sums[:, q_cols + kv_width : q_cols + 2 * kv_width]
    w_output_grad = attn_sums[:, q_cols + 2 * kv_width :]
    w_gate_grad = mlp_sums[:, :ff_width]
    w_up_grad = mlp_sums[:, ff_width : 2 * ff_width]
    w_down_grad = mlp_sums[:, 2 * ff_width :]
    return (
        block_out,
        tokens_grad,
        w_query_grad,
        w_key_grad,
        w_value_grad,
        w_output_grad,
        attn_gain_grad,
        dgq_all,
        dgk_all,
        w_gate_grad,
        w_up_grad,
        w_down_grad,
        mlp_gain_grad,
    )


LOW = jnp.bfloat16
MESH = pl.DeviceIdType.MESH
LIMIT = 60 * 2**20


def ring_order(ranks):
    half = ranks // 2
    order = [0]
    for step in range(1, half):
        order += [step, ranks - step]
    return order + [half]


def ring_place(seq, ranks):
    z, x = lax.div(seq, 2), lax.rem(seq, 2)
    return z + x * (ranks - 1 - 2 * z)


def ring_seq(place, ranks):
    half = ranks // 2
    x, z = lax.div(place, half), lax.rem(place, half)
    return 2 * (z + x * (half - 1 - 2 * z)) + x


def neighbours(ranks):
    seq, dp = lax.axis_index("seq"), lax.axis_index("dp")
    at = ring_place(seq, ranks)
    right = ring_seq(lax.rem(at + 1, ranks), ranks)
    left = ring_seq(lax.rem(at + ranks - 1, ranks), ranks)
    return (right, dp), (left, dp)


def knock(devices):
    barrier = pltpu.get_barrier_semaphore()
    for device in devices:
        pl.semaphore_signal(barrier, inc=1, device_id=device, device_id_type=MESH)


def answered(devices):
    pl.semaphore_wait(pltpu.get_barrier_semaphore(), len(devices))


def move(src, dst, sem):
    copy = pltpu.make_async_copy(src, dst, sem)
    copy.start()
    return copy


def push(src, dst, send, recv, device):
    return pltpu.make_async_remote_copy(
        src_ref=src, dst_ref=dst, send_sem=send, recv_sem=recv, device_id=device, device_id_type=MESH
    )


def dot_nn(left, right):
    return jnp.dot(left, right, preferred_element_type=jnp.float32)


def dot_nt(left, right):
    return lax.dot_general(left, right, (((1,), (1,)), ((), ())), preferred_element_type=jnp.float32)


def dot_tn(left, right):
    return lax.dot_general(left, right, (((0,), (0,)), ((), ())), preferred_element_type=jnp.float32)


def block_row(rel, local, ranks):
    place = ring_place(lax.axis_index("seq"), ranks)
    return pl.multiple_of(ring_seq(lax.rem(place + rel, ranks), ranks) * local, local)


def block_rows(ref, rels, local, ranks):
    blocks = [ref[pl.ds(block_row(rel, local, ranks), local)] for rel in rels]
    return blocks[0] if len(blocks) == 1 else jnp.concatenate(blocks, 0)


def rels_of(step, ranks):
    return [rel for rel in ring_order(ranks) if min(rel, ranks - rel) == step]


class RingGather:
    def __init__(self, buf, local, ranks, send, recv, right, left, row):
        self.buf, self.sub, self.half = buf, local // 2, ranks // 2
        self.send, self.recv, self.right, self.left = send, recv, right, left
        self.ranks, self.row = ranks, row

    def copies(self, step, part):
        ways = ((0, (self.ranks - step + 1) % self.ranks, self.right), (1, step - 1, self.left))
        given = []
        for way, rel, device in ways:
            if step < self.half or way == part:
                block = self.buf.at[pl.ds(self.row(rel) + part * self.sub, self.sub)]
                at = 2 * (step - 1) + part
                given.append(push(block, block, self.send.at[way, at], self.recv.at[way, at], device))
        return given

    def start(self, step):
        for part in range(2):
            for copy in self.copies(step, part):
                copy.start()

    def advance(self, step):
        for part in range(2):
            for copy in self.copies(step, part):
                copy.wait_recv()
            if step < self.half:
                for copy in self.copies(step + 1, part):
                    copy.start()

    def finish(self):
        for step in range(1, self.half + 1):
            for part in range(2):
                for copy in self.copies(step, part):
                    copy.wait_send()


class LineGather:
    def __init__(self, buf, local, ranks, send, recv, x_send, x_recv):
        self.buf, self.local, self.length = buf, local, ranks // 2
        self.send, self.recv, self.x_send, self.x_recv = send, recv, x_send, x_recv
        self.seq, self.dp = lax.axis_index("seq"), lax.axis_index("dp")
        self.z, self.x = lax.div(self.seq, 2), lax.rem(self.seq, 2)

    def block(self, z):
        return self.buf.at[pl.ds(pl.multiple_of((2 * z + self.x) * self.local, self.local), self.local)]

    def hop(self, way, step):
        block = self.block(self.z + (step - 1 if way else 1 - step))
        to = self.seq + (-2 if way else 2)
        return push(block, block, self.send.at[way, step - 1], self.recv.at[way, step - 1], (to, self.dp))

    def sends(self, way, step):
        if way:
            return (self.z > 0) & (self.z + step <= self.length)
        return (self.z < self.length - 1) & (self.z >= step - 1)

    def comes(self, way, step):
        return self.z + step < self.length if way else self.z >= step

    def across(self, way, step):
        block = self.block(self.z + (step if way else -step))
        at = step + way * (self.length - 1)
        return push(
            block, block, self.x_send.at[at], self.x_recv.at[at], (self.seq + 1 - 2 * self.x, self.dp)
        )

    def from_x(self, way, step):
        z = self.z + (step if way else -step)
        row = pl.multiple_of((2 * z + 1 - self.x) * self.local, self.local)
        block = self.buf.at[pl.ds(row, self.local)]
        at = step + way * (self.length - 1)
        return push(
            block, block, self.x_send.at[at], self.x_recv.at[at], (self.seq + 1 - 2 * self.x, self.dp)
        )

    def start(self, step):
        for way in range(2):
            pl.when(self.sends(way, step))(lambda way=way: self.hop(way, step).start())
        self.pass_on(step - 1)

    def pass_on(self, step):
        if step == 0:
            self.across(0, 0).start()
            return
        for way in range(2):
            pl.when(self.comes(way, step))(lambda way=way: self.across(way, step).start())

    def arrive(self, step):
        for way in range(2):
            pl.when(self.comes(way, step))(lambda way=way: self.incoming(way, step).wait_recv())

    def incoming(self, way, step):
        block = self.block(self.z + (step if way else -step))
        to = self.seq + 1 - 2 * self.x
        return push(block, block, self.send.at[way, step - 1], self.recv.at[way, step - 1], (to, self.dp))

    def run(self):
        for step in range(1, self.length):
            self.advance(step)

    def advance(self, step):
        self.arrive(step)
        if step < self.length - 1:
            self.start(step + 1)
        else:
            self.pass_on(step)

    def complete(self):
        self.from_x(0, 0).wait_recv()
        for step in range(1, self.length):
            for way in range(2):
                pl.when(self.comes(way, step))(lambda way=way: self.from_x(way, step).wait_recv())

    def finish(self):
        self.across(0, 0).wait_send()
        for step in range(1, self.length):
            for way in range(2):
                pl.when(self.sends(way, step))(lambda way=way: self.hop(way, step).wait_send())
                pl.when(self.comes(way, step))(lambda way=way: self.across(way, step).wait_send())


def line_sems(ranks):
    half = ranks // 2
    return [pltpu.SemaphoreType.DMA((2, half))] * 2 + [pltpu.SemaphoreType.DMA((2 * half,))] * 2


class RingSum:
    def __init__(self, part, term, out_buf, in_buf, local, ranks, send, recv, right, left, stream=0, streams=1):
        self.part, self.term, self.out_buf, self.in_buf = part, term, out_buf, in_buf
        self.local, self.ranks, self.half = local, ranks, ranks // 2
        each = term.shape[1] // streams
        self.cols = pl.ds(stream * each, each)
        self.tiles = (stream * ranks // streams, (stream + 1) * ranks // streams)
        self.send, self.recv, self.right, self.left = send, recv, right, left

    def copies(self, step):
        rows = self.local // 2 if step == 1 else self.local
        skip = self.local // 2 if step == 1 else 0
        return [
            push(
                self.out_buf.at[way, (step - 1) % 2, pl.ds(begin, rows), self.cols],
                self.in_buf.at[way, step - 1, pl.ds(begin, rows), self.cols],
                self.send.at[way, step - 1],
                self.recv.at[way, step - 1],
                device,
            )
            for way, begin, device in ((0, 0, self.right), (1, skip, self.left))
        ]

    def compute(self, step):
        if step == 1:
            self.part([self.half], *self.tiles)
        elif step <= self.half:
            self.part(rels_of(self.half + 1 - step, self.ranks), *self.tiles)
        else:
            self.part([0], *self.tiles)

    def launch(self, step):
        local, skip = self.local, self.local // 2
        if step > 2:
            for copy in self.copies(step - 2):
                copy.wait_send()
        if step == 1:
            for way in range(2):
                rows = pl.ds(way * skip, skip)
                self.out_buf[way, 0, rows, self.cols] = self.term[rows, self.cols].astype(LOW)
        else:
            for copy in self.copies(step - 1):
                copy.wait_recv()
            for way in range(2):
                for begin, with_sum in ((0, step > 2 or way == 0), (skip, step > 2 or way == 1)):
                    value = self.term[pl.ds(way * local + begin, skip), self.cols]
                    if with_sum:
                        value = value + self.in_buf[way, step - 2, pl.ds(begin, skip), self.cols].astype(jnp.float32)
                    self.out_buf[way, (step - 1) % 2, pl.ds(begin, skip), self.cols] = value.astype(LOW)
        for copy in self.copies(step):
            copy.start()

    def last(self, begin, count):
        rows = pl.ds(begin, count)
        value = self.term[rows, self.cols] + self.in_buf[0, self.half - 1, rows, self.cols].astype(jnp.float32)
        return value + self.in_buf[1, self.half - 1, rows, self.cols].astype(jnp.float32)

    def arrive_last(self):
        for copy in self.copies(self.half):
            copy.wait_recv()

    def finish(self):
        for step in range(max(1, self.half - 1), self.half + 1):
            for copy in self.copies(step):
                copy.wait_send()


def two_sums(part, term, out_buf, in_buf, local, ranks, sems, right, left):
    return [
        RingSum(
            part, term, out_buf, in_buf, local, ranks, sems[2 * at], sems[2 * at + 1], right, left, at, 2
        )
        for at in range(2)
    ]


def ring_sems(ranks):
    return [pltpu.SemaphoreType.DMA((2, ranks)), pltpu.SemaphoreType.DMA((2, ranks))]


def sum_bufs(local, ranks, width):
    return [
        pltpu.VMEM((2 * local, width), jnp.float32),
        pltpu.VMEM((2, 2, local, width), LOW),
        pltpu.VMEM((2, ranks // 2, local, width), LOW),
    ]


def turn(v):
    return pltpu.roll(v, v.shape[-1] // 2, v.ndim - 1)


def rows_scaled(v):
    inv = lax.rsqrt(jnp.mean(v * v, -1, keepdims=True) + EPS)
    return v * inv, inv


def rows_scaled_back(v, inv, grad):
    return inv * grad - v * (inv * inv * inv * jnp.mean(grad * v, -1, keepdims=True))


class Spread:
    def __init__(self, rows, block, ranks, own, cols, sems):
        self.rows, self.block, self.ranks, self.own, self.cols = rows, block, ranks, own, cols
        self.send, self.recv, self.hop_send, self.hop_recv, self.here = sems
        self.seq, self.dp = lax.axis_index("seq"), lax.axis_index("dp")
        y, core = lax.div(self.dp, 2), lax.rem(self.dp, 2)
        self.beside, self.sibling = (1 - y) * 2 + core, y * 2 + 1 - core

    def at(self, dp):
        return pl.ds(pl.multiple_of(dp * self.own, self.own), self.own)

    def exchange(self):
        for step in range(1, self.ranks):
            peer = lax.rem(self.seq + step, self.ranks)
            yield push(
                self.rows.at[peer, :, self.cols],
                self.block.at[self.seq, self.at(self.dp), self.cols],
                self.send.at[step],
                self.recv.at[step],
                (peer, self.dp),
            )

    def keep(self):
        return pltpu.make_async_copy(
            self.rows.at[self.seq, :, self.cols],
            self.block.at[self.seq, self.at(self.dp), self.cols],
            self.here,
        )

    def hop(self, number):
        dp = self.beside if number == 2 else self.dp
        part = self.block.at[:, self.at(dp), self.cols]
        to = self.beside if number == 0 else self.sibling
        return push(part, part, self.hop_send.at[number], self.hop_recv.at[number], (self.seq, to))

    def start(self):
        self.keep().start()
        for copy in self.exchange():
            copy.start()

    def arrive(self):
        self.keep().wait()
        for copy in self.exchange():
            copy.wait_recv()

    def finish(self):
        for copy in self.exchange():
            copy.wait_send()
        for number in range(3):
            self.hop(number).wait_send()


def spread_sems(ranks):
    return [
        pltpu.SemaphoreType.DMA((ranks,)),
        pltpu.SemaphoreType.DMA((ranks,)),
        pltpu.SemaphoreType.DMA((3,)),
        pltpu.SemaphoreType.DMA((3,)),
        pltpu.SemaphoreType.DMA,
    ]


class Reduce:
    def __init__(self, grads, from_core, from_y, total, own, first, count, cols, sems):
        self.grads, self.from_core, self.from_y, self.total = grads, from_core, from_y, total
        self.own, self.begin, self.count, self.cols = own, first, count, cols
        self.send, self.recv = sems
        self.seq, dp = lax.axis_index("seq"), lax.axis_index("dp")
        self.y, self.core = lax.div(dp, 2), lax.rem(dp, 2)
        self.beside, self.sibling = (1 - self.y) * 2 + self.core, self.y * 2 + 1 - self.core

    def at(self, y, core):
        return pl.ds(pl.multiple_of((y * 2 + core) * self.own, self.own), self.own)

    def hop(self, number):
        some, cols = pl.ds(self.begin, self.count), self.cols
        if number == 2:
            src, dst, to = self.from_core.at[0, some, :, cols], self.from_y.at[some, :, cols], self.beside
        else:
            rows = self.at(1 - self.y if number == 0 else self.y, 1 - self.core)
            src, dst, to = self.grads.at[some, rows, cols], self.from_core.at[number, some, :, cols], self.sibling
        return push(src, dst, self.send.at[number], self.recv.at[number], (self.seq, to))

    def first(self):
        self.hop(0).start()
        self.hop(1).start()

    def second(self):
        self.hop(0).wait_recv()
        rows = self.at(1 - self.y, self.core)

        def some(at, _):
            value = self.grads[at, rows, self.cols].astype(jnp.float32)
            value = value + self.from_core[0, at, :, self.cols].astype(jnp.float32)
            self.from_core[0, at, :, self.cols] = value.astype(LOW)
            return 0

        lax.fori_loop(self.begin, self.begin + self.count, some, 0)
        self.hop(2).start()

    def third(self):
        self.hop(1).wait_recv()
        self.hop(2).wait_recv()
        rows = self.at(self.y, self.core)

        def some(at, _):
            value = self.grads[at, rows, self.cols].astype(jnp.float32)
            value = value + self.from_core[1, at, :, self.cols].astype(jnp.float32)
            value = value + self.from_y[at, :, self.cols].astype(jnp.float32)
            self.total[at, :, self.cols] = value.astype(LOW)
            return 0

        lax.fori_loop(self.begin, self.begin + self.count, some, 0)

    def finish(self):
        for number in range(3):
            self.hop(number).wait_send()


def reduce_sems():
    return [pltpu.SemaphoreType.DMA((3,)), pltpu.SemaphoreType.DMA((3,))]


def reduce_bufs(ranks, own, cols):
    return [pltpu.VMEM((2, ranks, own, cols), LOW), pltpu.VMEM((ranks, own, cols), LOW)]


class Deliver:
    def __init__(self, rows, out, cols, ranks, sems):
        self.rows, self.out, self.cols, self.ranks = rows, out, cols, ranks
        self.send, self.recv, self.here = sems
        self.seq, self.dp = lax.axis_index("seq"), lax.axis_index("dp")

    def exchange(self):
        for step in range(1, self.ranks):
            peer = lax.rem(self.seq + step, self.ranks)
            yield push(
                self.rows.at[peer, :, self.cols],
                self.out.at[self.seq, :, self.cols],
                self.send.at[step],
                self.recv.at[step],
                (peer, self.dp),
            )

    def keep(self):
        return pltpu.make_async_copy(
            self.rows.at[self.seq, :, self.cols], self.out.at[self.seq, :, self.cols], self.here
        )

    def start(self):
        self.keep().start()
        for copy in self.exchange():
            copy.start()

    def finish(self):
        self.keep().wait()
        for copy in self.exchange():
            copy.wait_recv()
        for copy in self.exchange():
            copy.wait_send()


def deliver_sems(ranks):
    return [pltpu.SemaphoreType.DMA((ranks,)), pltpu.SemaphoreType.DMA((ranks,)), pltpu.SemaphoreType.DMA]


def first_kernel(
    ranks, kv_heads, order, starts, tokens, out_grad, freqs, attn_gain, mlp_gain, query_gain, key_gain,
    w_query, w_key, w_value, w_output, w_gate, w_up, w_down,
    resid, second, cosv, sinv, q_low, k_low, v_low, out_low, first_in, qkv, attn_block, dy_all, prob, mlp_block,
    held, normal, kept, block, a_rows, m_rows, gate, up, down, dys, probs, pos, begins, pos_row,
    term, out_buf, in_buf, *sems,
):
    local, width = tokens.shape
    rows = local * ranks
    own = w_query.shape[0]
    size = freqs.shape[1]
    heads = q_low.shape[0]
    share = heads // kv_heads
    half = ranks // 2
    scale = 1.0 / math.sqrt(size)
    cols = (heads + 2 * kv_heads) * size
    deep = block.shape[1]
    row = functools.partial(block_row, local=local, ranks=ranks)
    seq, dp = lax.axis_index("seq"), lax.axis_index("dp")
    right, left = neighbours(ranks)
    attn = Spread(a_rows, block, ranks, own, pl.ds(0, a_rows.shape[2]), sems[8:13])
    third = m_rows.shape[2] // 3
    mlp = [
        Spread(m_rows, mlp_block, ranks, own, pl.ds(at * third, third), sems[13 + 5 * at : 18 + 5 * at])
        for at in range(3)
    ]
    local_sems = sems[28]
    peers = [(lax.rem(seq + step, ranks), dp) for step in range(1, ranks)]
    peers += [(seq, attn.beside), (seq, attn.sibling)]
    knock(peers)
    loads = [
        move(src, dst, local_sems.at[at])
        for at, (src, dst) in enumerate(((w_gate, gate), (w_up, up), (w_down, down)))
    ]
    held[pl.ds(row(0), local)] = tokens[...]
    dys[pl.ds(row(0), local)] = out_grad[...]

    def column(line):
        same = lax.broadcasted_iota(jnp.int32, (own, own), 0) == lax.broadcasted_iota(jnp.int32, (own, own), 1)
        return jnp.sum(jnp.where(same, line, 0.0), 1, keepdims=True)

    def lay(target, begin, weight, gain):
        each = weight.shape[1] // ranks
        for rank in range(ranks):
            part = weight[:, rank * each : (rank + 1) * each]
            if gain is not None:
                part = (part.astype(jnp.float32) * gain).astype(LOW)
            target[rank, :, begin : begin + each] = part
        return begin + each

    gain = column(attn_gain[...])
    at = 0
    for weight in (w_query, w_key, w_value):
        at = lay(a_rows, at, weight, gain)
    lay(a_rows, at, w_output, None)
    answered(peers)
    ring = RingGather(held, local, ranks, sems[0], sems[1], right, left, row)
    ring.start(1)
    attn.start()
    line = LineGather(dys, local, ranks, sems[4], sems[5], sems[6], sems[7])
    stores = []

    def store(src, dst):
        stores.append(move(src, dst, local_sems.at[len(loads) + len(stores)]))

    def scale_rows(step):
        for rel in rels_of(step, ranks):

            def some(at, _):
                rows_at = pl.ds(pl.multiple_of(row(rel) + at * 32, 32), 32)
                normal[rows_at] = rows_scaled(held[rows_at].astype(jnp.float32))[0].astype(LOW)
                return 0

            lax.fori_loop(0, local // 32, some, 0)

    for load in loads:
        load.wait()
    gain = column(mlp_gain[...])
    each = gate.shape[1] // ranks
    lay(m_rows, 0, gate, gain)
    lay(m_rows, each, up, gain)
    lay(m_rows, 2 * each, down, None)
    scale_rows(0)
    ring.advance(1)
    scale_rows(1)
    attn.arrive()
    attn.hop(0).start()
    attn.hop(1).start()
    spans = order.shape[0]
    span = rows // spans
    for at in range(ranks):
        rows_at = pl.ds(at * local, local)
        ids = at * local + lax.broadcasted_iota(jnp.int32, (1, local), 1)
        where = jnp.zeros_like(ids)
        for slot in range(spans):
            inside = (ids >= slot * span) & (ids < (slot + 1) * span)
            where = where + jnp.where(inside, ids + (order[slot] - slot) * span, 0)
        begin = jnp.zeros_like(ids)
        for doc in range(starts.shape[1]):
            begin = jnp.maximum(begin, jnp.where(starts[0, doc] <= where, starts[0, doc], 0))
        pos_row[:, rows_at] = where
        across = jnp.broadcast_to(where, (local, local)).T
        pos[rows_at] = across[:, :1]
        begins[rows_at] = jnp.broadcast_to(begin, (local, local)).T[:, :1]
        angle = across[:, :1].astype(jnp.float32) * freqs[...]
        lane = lax.broadcasted_iota(jnp.int32, (local, size), 1)
        cosv[rows_at] = jnp.cos(angle)
        sine = jnp.sin(angle)
        sinv[rows_at] = jnp.where(lane < size // 2, -sine, sine)
    for step in range(2, half):
        ring.advance(step)
        scale_rows(step)
        if step == 2:
            attn.hop(0).wait_recv()
            attn.hop(2).start()
    for piece in mlp:
        piece.start()
    attn.hop(1).wait_recv()
    attn.hop(2).wait_recv()
    store(block, attn_block)

    def project(begin, count):
        rows_at = pl.ds(begin, count)
        kept[rows_at] = dot_nn(normal[rows_at], block[:, :, :cols].reshape(width, cols))

    ring.advance(half)
    scale_rows(half)
    store(normal, first_in)
    tile = rows // half

    def rotated(at, rows_at, gain):
        v = rows_scaled(kept[rows_at, at * size : (at + 1) * size])[0] * gain[...]
        return (v * cosv[rows_at] + turn(v) * sinv[rows_at]).astype(LOW)

    for piece in range(half):
        rows_at = pl.ds(piece * tile, tile)
        project(piece * tile, tile)
        for head in range(heads):
            q_low[head, rows_at] = rotated(head, rows_at, query_gain)
        for group in range(kv_heads):
            k_low[group, rows_at] = rotated(heads + group, rows_at, key_gain)
            at = (heads + kv_heads + group) * size
            v_low[group, rows_at] = kept[rows_at, at : at + size].astype(LOW)
    store(kept, qkv)

    def forward(piece):
        mlp[piece].arrive()
        mlp[piece].hop(0).start()
        mlp[piece].hop(1).start()

    for piece in range(half):
        rows_at = pl.ds(piece * tile, tile)
        seen = (pos_row[...] <= pos[rows_at]) & (pos_row[...] >= begins[rows_at])
        for head in range(heads):
            raw = dot_nt(q_low[head, rows_at], k_low[head // share]) * scale
            raw = jnp.where(seen, raw, NEG)
            weight = jnp.exp(raw - jnp.max(raw, -1, keepdims=True))
            weight = (weight * (1.0 / jnp.sum(weight, -1, keepdims=True))).astype(LOW)
            probs[head, rows_at] = weight
            value = dot_nn(weight, v_low[head // share])
            out_low[rows_at, head * size : (head + 1) * size] = value.astype(LOW)
            store(probs.at[head, rows_at], prob.at[head, rows_at])
        if piece == half - 2:
            line.start(1)
            forward(0)
        if piece == half - 1:
            forward(1)

    def part(rels, begin, end):
        def some(at, _):
            value = dot_nt(block_rows(out_low, rels, local, ranks), block[at, :, cols:])
            term[: len(rels) * local, pl.ds(pl.multiple_of(at * deep, deep), deep)] = value
            return 0

        lax.fori_loop(begin, end, some, 0)

    totals = two_sums(part, term, out_buf, in_buf, local, ranks, [*sems[2:4], *sems[29:31]], right, left)
    for step in range(1, half + 1):
        for total in totals:
            total.compute(step)
            total.launch(step)
        if step == 1:
            forward(2)
        if step < half:
            line.advance(step)
        if 1 < step:
            mlp[step - 2].hop(0).wait_recv()
            mlp[step - 2].hop(2).start()
    for total in totals:
        total.compute(half + 1)
    for total in totals:
        total.arrive_last()

    def some(at, _):
        begin = pl.multiple_of(at * 32, 32)
        rows_at = pl.ds(begin, 32)
        value = jnp.concatenate([total.last(begin, 32) for total in totals], 1)
        value = tokens[rows_at].astype(jnp.float32) + value
        resid[rows_at] = value
        second[rows_at] = rows_scaled(value)[0].astype(LOW)
        return 0

    lax.fori_loop(0, local // 32, some, 0)
    line.complete()
    store(dys, dy_all)
    ring.finish()
    attn.finish()
    for total in totals:
        total.finish()
    line.finish()
    for piece in mlp:
        piece.hop(1).wait_recv()
        piece.hop(2).wait_recv()
        piece.finish()
    for given in stores:
        given.wait()


def mlp_kernel(
    ranks, second, out_grad, rest, dys, mlp_block, block_out, dresid, dresid_low, own_grads,
    grads, from_core, from_y, held, weights, hidden, dgu, resid, dy_all,
    term, out_buf, in_buf, y_out, y_in, here, *sems,
):
    local, width = second.shape
    row = functools.partial(block_row, local=local, ranks=ranks)
    ff = hidden.shape[1]
    deep = weights.shape[1]
    half = ranks // 2
    right, left = neighbours(ranks)
    loads = [
        move(src, dst, here.at[at])
        for at, (src, dst) in enumerate(((mlp_block, weights), (dys, dy_all), (rest, resid)))
    ]
    seq, dp = lax.axis_index("seq"), lax.axis_index("dp")
    own = own_grads.shape[1]
    pieces = [
        Reduce(
            grads, from_core, from_y, own_grads, own, at * ranks // 4, ranks // 4, pl.ds(0, 3 * ff),
            sems[6 + 2 * at : 8 + 2 * at],
        )
        for at in range(4)
    ]
    peers = [right, left, (seq, pieces[0].beside), (seq, pieces[0].sibling)]
    knock(peers)
    held[pl.ds(row(0), local)] = second[...]
    answered(peers)
    ring = RingGather(held, local, ranks, sems[0], sems[1], right, left, row)
    ring.start(1)
    loads[0].wait()
    loads[1].wait()
    wide = 256

    def middle(step):
        rels = rels_of(step, ranks)

        def some(at, _):
            first = pl.multiple_of(at * wide, wide)
            given, dy = block_rows(held, rels, local, ranks), block_rows(dy_all, rels, local, ranks)
            gate = dot_nn(given, weights[:, :, pl.ds(first, wide)].reshape(width, wide))
            upper = dot_nn(given, weights[:, :, pl.ds(ff + first, wide)].reshape(width, wide))
            dmid = dot_nn(dy, weights[:, :, pl.ds(2 * ff + first, wide)].reshape(width, wide))
            sigma = 1.0 / (1.0 + jnp.exp(-gate))
            act = gate * sigma
            value = (act * upper).astype(LOW)
            dgate = (dmid * upper * (sigma * (1.0 + gate * (1.0 - sigma)))).astype(LOW)
            dupper = (dmid * act).astype(LOW)
            for at, rel in enumerate(rels):
                rows, some_rows = pl.ds(row(rel), local), slice(at * local, (at + 1) * local)
                hidden[rows, pl.ds(first, wide)] = value[some_rows]
                dgu[rows, pl.ds(first, wide)] = dgate[some_rows]
                dgu[rows, pl.ds(ff + first, wide)] = dupper[some_rows]
            return 0

        lax.fori_loop(0, ff // wide, some, 0)

    middle(0)
    for step in range(1, half + 1):
        ring.advance(step)
        middle(step)

    def back_part(rels, begin, end):
        def some(at, _):
            value = dot_nt(block_rows(dgu, rels, local, ranks), weights[at, :, : 2 * ff])
            term[: len(rels) * local, pl.ds(pl.multiple_of(at * deep, deep), deep)] = value
            return 0

        lax.fori_loop(begin, end, some, 0)

    def out_part(rels, begin, end):
        def some(at, _):
            value = dot_nt(block_rows(hidden, rels, local, ranks), weights[at, :, 2 * ff :])
            term[: len(rels) * local, pl.ds(pl.multiple_of(at * deep, deep), deep)] = value
            return 0

        lax.fori_loop(begin, end, some, 0)

    def weight_grads(first, count):
        def some(at, _):
            cols = pl.ds(pl.multiple_of(at * deep, deep), deep)
            grads[at, :, : 2 * ff] = dot_tn(held[:, cols], dgu[...]).astype(LOW)
            grads[at, :, 2 * ff :] = dot_tn(dy_all[:, cols], hidden[...]).astype(LOW)
            return 0

        lax.fori_loop(first, first + count, some, 0)

    back = RingSum(back_part, term, out_buf, in_buf, local, ranks, sems[2], sems[3], right, left)
    out = RingSum(out_part, term, y_out, y_in, local, ranks, sems[4], sems[5], right, left)
    for step in range(1, half + 1):
        back.compute(step)
        back.launch(step)
        out.compute(step)
        out.launch(step)
        made, passed, summed = (((0, 1), (2,), (3,), ()), ((), (0, 1), (2,), (3,)), ((), (), (0, 1), (2,)))
        for piece in (pieces[at] for at in made[step - 1]):
            weight_grads(piece.begin, piece.count)
            piece.first()
        for at in passed[step - 1]:
            pieces[at].second()
        for at in summed[step - 1]:
            pieces[at].third()
    back.compute(half + 1)
    loads[2].wait()
    back.arrive_last()

    def finish_back(at, _):
        begin = pl.multiple_of(at * 32, 32)
        rows = pl.ds(begin, 32)
        value = resid[rows]
        inv = rows_scaled(value)[1]
        grad = back.last(begin, 32)
        full = out_grad[rows].astype(jnp.float32) + rows_scaled_back(value, inv, grad)
        dresid[rows] = full
        dresid_low[rows] = full.astype(LOW)
        return 0

    lax.fori_loop(0, local // 32, finish_back, 0)
    out.compute(half + 1)
    out.arrive_last()

    def finish_out(at, _):
        begin = pl.multiple_of(at * 32, 32)
        rows = pl.ds(begin, 32)
        block_out[rows] = (resid[rows] + out.last(begin, 32)).astype(LOW)
        return 0

    lax.fori_loop(0, local // 32, finish_out, 0)
    ring.finish()
    pieces[3].third()
    back.finish()
    out.finish()
    for piece in pieces:
        piece.finish()


def back_kernel(
    ranks, kv_heads, tokens, dresid_low, query_gain, key_gain, out_low_in, first_in_in, block_in,
    qkv_in, cos_in, sin_in, q_in, k_in, v_in, prob_in, dresid_in, mlp_own,
    tokens_grad, gains, mlp_sums, attn_sums,
    grads, from_core, from_y, own_grads, query_gain_grad, key_gain_grad,
    tile, tiles_in, tile_sum, tile_sums_in, held, dout, dk, dv, dqkv,
    out_low, first_in, attn_block, qkv, cosv, sinv, q_low, k_low, v_low, prob, dresid, term, out_buf, in_buf, *sems,
):
    local, width = tokens.shape
    rows = local * ranks
    half = ranks // 2
    size = cosv.shape[1]
    heads = q_low.shape[0]
    share = heads // kv_heads
    scale = 1.0 / math.sqrt(size)
    cols = (heads + 2 * kv_heads) * size
    deep = attn_block.shape[1]
    o_cols = heads * size
    right, left = neighbours(ranks)
    seq, dp = lax.axis_index("seq"), lax.axis_index("dp")
    own = mlp_own.shape[1]
    copies = lax.axis_size("dp")
    row = functools.partial(block_row, local=local, ranks=ranks)
    all_cols = grads.shape[2]
    out_piece = Reduce(
        grads, from_core, from_y, own_grads, own, 0, ranks, pl.ds(cols, all_cols - cols), sems[4:6]
    )
    qkv_piece = Reduce(grads, from_core, from_y, own_grads, own, 0, ranks, pl.ds(0, cols), sems[6:8])
    third = mlp_own.shape[2] // 3
    mlp_ways = [
        Deliver(mlp_own, mlp_sums, pl.ds(at * third, third), ranks, [*sems[8:11], *sems[22:28]][3 * at : 3 * at + 3])
        for at in range(3)
    ]
    out_way = Deliver(own_grads, attn_sums, pl.ds(cols, all_cols - cols), ranks, sems[11:14])
    qkv_way = Deliver(own_grads, attn_sums, pl.ds(0, cols), ranks, sems[14:17])
    peers = [(lax.rem(seq + step, ranks), dp) for step in range(1, ranks)]
    peers += [(seq, lax.rem(dp + step, copies)) for step in range(1, copies)]
    knock(peers)
    local_sems = sems[21]
    loads = {}
    for at, (name, src, dst) in enumerate(
        (
            ("block", block_in, attn_block), ("out", out_low_in, out_low), ("v", v_in, v_low),
            ("prob", prob_in, prob), ("k", k_in, k_low), ("q", q_in, q_low), ("cos", cos_in, cosv),
            ("sin", sin_in, sinv), ("qkv", qkv_in, qkv), ("first", first_in_in, first_in),
            ("dresid", dresid_in, dresid),
        )
    ):
        loads[name] = move(src, dst, local_sems.at[at])
    held[pl.ds(row(0), local)] = dresid_low[...]
    answered(peers)
    ring = RingGather(held, local, ranks, sems[0], sems[1], right, left, row)
    ring.start(1)
    loads["block"].wait()

    def project(step):
        rels = rels_of(step, ranks)
        weight = attn_block[:, :, cols:].reshape(width, o_cols)
        value = dot_nn(block_rows(held, rels, local, ranks), weight).astype(LOW)
        for at, rel in enumerate(rels):
            dout[pl.ds(row(rel), local)] = value[at * local : (at + 1) * local]

    project(0)
    for step in range(1, half + 1):
        ring.advance(step)
        if step == half - 1:
            for way in mlp_ways:
                way.start()
        project(step)
    loads["out"].wait()

    def out_grads(at, _):
        some_cols = pl.ds(pl.multiple_of(at * deep, deep), deep)
        grads[at, :, cols:] = dot_tn(held[:, some_cols], out_low[...]).astype(LOW)
        return 0

    lax.fori_loop(0, ranks, out_grads, 0)
    out_piece.first()
    for name in ("v", "prob", "k", "q", "cos", "sin", "qkv"):
        loads[name].wait()
    tall = rows // half
    query_gain_grad[...] = jnp.zeros_like(query_gain_grad)
    key_gain_grad[...] = jnp.zeros_like(key_gain_grad)

    def unrotated(grad, column, rows_at, gain, gain_grad_ref):
        grad = grad * cosv[rows_at] - turn(grad) * sinv[rows_at]
        value = qkv[rows_at, column * size : (column + 1) * size]
        normal, inv = rows_scaled(value)
        gain_grad_ref[...] += jnp.sum(grad * normal, 0, keepdims=True)
        back = rows_scaled_back(value, inv, grad * gain[...])
        dqkv[rows_at, column * size : (column + 1) * size] = back.astype(LOW)

    for head in range(heads):
        group = head // share

        def one(piece, _):
            rows_at = pl.ds(pl.multiple_of(piece * tall, tall), tall)
            weight = prob[head, rows_at]
            grad = dout[rows_at, head * size : (head + 1) * size]
            dprob = dot_nt(grad, v_low[group])
            full = weight.astype(jnp.float32)
            delta = jnp.sum(full * dprob, -1, keepdims=True)
            dscore = (full * (dprob - delta)).astype(LOW)
            dq = dot_nn(dscore, k_low[group]) * scale
            dk_add = dot_tn(dscore, q_low[head, rows_at]) * scale
            dv_add = dot_tn(weight, grad)
            dk[group] += dk_add
            dv[group] += dv_add
            unrotated(dq, head, rows_at, query_gain, query_gain_grad)
            return 0

        if head % share == 0:
            dk[group] = jnp.zeros_like(dk[group])
            dv[group] = jnp.zeros_like(dv[group])
        lax.fori_loop(0, half, one, 0)
        if head == 0:
            out_piece.second()
    for group in range(kv_heads):
        def one_key(piece, _):
            rows_at = pl.ds(pl.multiple_of(piece * tall, tall), tall)
            unrotated(dk[group, rows_at], heads + group, rows_at, key_gain, key_gain_grad)
            at = (heads + kv_heads + group) * size
            dqkv[rows_at, at : at + size] = dv[group, rows_at].astype(LOW)
            return 0

        lax.fori_loop(0, half, one_key, 0)

    def part(rels, begin, end):
        def some(at, _):
            value = dot_nt(block_rows(dqkv, rels, local, ranks), attn_block[at, :, :cols])
            term[: len(rels) * local, pl.ds(pl.multiple_of(at * deep, deep), deep)] = value
            return 0

        lax.fori_loop(begin, end, some, 0)

    def qkv_grads(at, _):
        some_cols = pl.ds(pl.multiple_of(at * deep, deep), deep)
        grads[at, :, :cols] = dot_tn(first_in[:, some_cols], dqkv[...]).astype(LOW)
        return 0

    def to_ranks(step):
        peer = lax.rem(seq + step, ranks)
        return push(tile, tiles_in.at[seq], sems[17].at[step], sems[18].at[step], (peer, dp))

    def to_copies(step):
        peer = lax.rem(dp + step, copies)
        return push(
            tile_sum, tile_sums_in.at[dp], sems[19].at[step], sems[20].at[step], (seq, peer)
        )

    tile[0:1] = query_gain_grad[...]
    tile[1:2] = key_gain_grad[...]
    tile[2:] = jnp.zeros((tile.shape[0] - 2, size), jnp.float32)
    for step in range(1, ranks):
        to_ranks(step).start()
    tiles_in[seq] = tile[...]
    totals = two_sums(part, term, out_buf, in_buf, local, ranks, [*sems[2:4], *sems[28:30]], right, left)
    for step in range(1, half + 1):
        for total in totals:
            total.compute(step)
            total.launch(step)
        if step == 1:
            loads["first"].wait()
            lax.fori_loop(0, ranks, qkv_grads, 0)
            qkv_piece.first()
            out_piece.third()
            out_way.start()
        if step == 2:
            qkv_piece.second()
            for other in range(1, ranks):
                to_ranks(other).wait_recv()
            tile_sum[...] = jnp.sum(tiles_in[...], 0)
            for other in range(1, copies):
                to_copies(other).start()
            tile_sums_in[dp] = tile_sum[...]
        if step == half - 1:
            for other in range(1, copies):
                to_copies(other).wait_recv()
            gains[...] = jnp.sum(tile_sums_in[...], 0)
            qkv_piece.third()
            qkv_way.start()
    for total in totals:
        total.compute(half + 1)
    loads["dresid"].wait()
    for total in totals:
        total.arrive_last()

    def last(at, _):
        begin = pl.multiple_of(at * 32, 32)
        rows_at = pl.ds(begin, 32)
        value = tokens[rows_at].astype(jnp.float32)
        inv = rows_scaled(value)[1]
        grad = jnp.concatenate([total.last(begin, 32) for total in totals], 1)
        tokens_grad[rows_at] = dresid[rows_at] + rows_scaled_back(value, inv, grad)
        return 0

    lax.fori_loop(0, local // 32, last, 0)
    for step in range(1, ranks):
        to_ranks(step).wait_send()
    for step in range(1, copies):
        to_copies(step).wait_send()
    ring.finish()
    for total in totals:
        total.finish()
    out_piece.finish()
    qkv_piece.finish()
    for way in mlp_ways:
        way.finish()
    out_way.finish()
    qkv_way.finish()


def leave_kernel(
    attn_sums, mlp_sums, attn_gain, mlp_gain, w_query, w_key, w_value, w_gate, w_up,
    query_out, key_out, value_out, output_out, gate_out, up_out, down_out, attn_out, mlp_out,
):
    own = attn_gain.shape[1]
    same = lax.broadcasted_iota(jnp.int32, (own, own), 0) == lax.broadcasted_iota(jnp.int32, (own, own), 1)

    @pl.when(pl.program_id(0) == 0)
    def _():
        attn_out[...] = jnp.zeros_like(attn_out)
        mlp_out[...] = jnp.zeros_like(mlp_out)

    for sums, gain, gain_out, parts in (
        (attn_sums, attn_gain, attn_out, ((query_out, w_query), (key_out, w_key), (value_out, w_value), (output_out, None))),
        (mlp_sums, mlp_gain, mlp_out, ((gate_out, w_gate), (up_out, w_up), (down_out, None))),
    ):
        scale = jnp.sum(jnp.where(same, gain[...], 0.0), 1, keepdims=True)
        at = 0
        for out, weight in parts:
            value = sums[0, :, at : at + out.shape[1]].astype(jnp.float32)
            at += out.shape[1]
            if weight is None:
                out[...] = value
                continue
            out[...] = value * scale
            inner = jnp.sum(value * weight[...].astype(jnp.float32), 1, keepdims=True)
            gain_out[...] += jnp.sum(jnp.where(same, inner, 0.0), 0, keepdims=True)


VM = pl.BlockSpec(memory_space=pltpu.VMEM)
SM = pl.BlockSpec(memory_space=pltpu.SMEM)
ANY = pl.BlockSpec(memory_space=pl.ANY)


def call(kernel, number, ins, outs, scratch, operands):
    return pl.pallas_call(
        kernel,
        out_shape=[jax.ShapeDtypeStruct(shape, dtype) for shape, dtype, _ in outs],
        in_specs=ins,
        out_specs=[spec for _, _, spec in outs],
        scratch_shapes=scratch,
        compiler_params=pltpu.CompilerParams(
            collective_id=number, has_side_effects=True, vmem_limit_bytes=LIMIT
        ),
    )(*operands)


def columns_body(
    tokens,
    out_grad,
    span_order,
    doc_starts,
    w_query,
    w_key,
    w_value,
    w_output,
    attn_gain,
    query_gain,
    key_gain,
    w_gate,
    w_up,
    w_down,
    mlp_gain,
):
    ranks = lax.axis_size("seq")
    copies = lax.axis_size("dp")
    _, local, width = tokens.shape
    rows = local * ranks
    size = query_gain.shape[0]
    kv_heads = w_key.shape[1] // size // ranks
    heads = w_query.shape[1] // size // ranks
    q_cols, kv_cols = heads * size, kv_heads * size
    qkv_cols = q_cols + 2 * kv_cols
    a_cols = qkv_cols + q_cols
    ff = w_gate.shape[1] // ranks
    own = width // (ranks * copies)
    deep = own * copies
    half = ranks // 2
    f32, i32 = jnp.float32, jnp.int32
    exponents = np.arange(size) % (size // 2) * (-2.0 / size * math.log(1000000.0))
    freqs = jnp.asarray(np.exp(exponents)[None], f32)
    q_gain, k_gain = query_gain[None], key_gain[None]
    (
        resid, second, cosv, sinv, q_low, k_low, v_low, out_low, first_in, qkv, attn_block, dy_all, prob, mlp_block,
    ) = call(
        functools.partial(first_kernel, ranks, kv_heads),
        1,
        [SM, SM] + [VM] * 11 + [ANY] * 3,
        [
            ((local, width), f32, VM),
            ((local, width), LOW, VM),
            ((rows, size), f32, VM),
            ((rows, size), f32, VM),
            ((heads, rows, size), LOW, VM),
            ((kv_heads, rows, size), LOW, VM),
            ((kv_heads, rows, size), LOW, VM),
            ((rows, q_cols), LOW, VM),
            ((rows, width), LOW, ANY),
            ((rows, qkv_cols), f32, ANY),
            ((ranks, deep, a_cols), LOW, ANY),
            ((rows, width), LOW, ANY),
            ((heads, rows, rows), LOW, ANY),
            ((ranks, deep, 3 * ff), LOW, ANY),
        ],
        [
            pltpu.VMEM((rows, width), LOW),
            pltpu.VMEM((rows, width), LOW),
            pltpu.VMEM((rows, qkv_cols), f32),
            pltpu.VMEM((ranks, deep, a_cols), LOW),
            pltpu.VMEM((ranks, own, a_cols), LOW),
            pltpu.VMEM((ranks, own, 3 * ff), LOW),
        ]
        + [pltpu.VMEM((own, ff * ranks), LOW)] * 3
        + [
            pltpu.VMEM((rows, width), LOW),
            pltpu.VMEM((heads, rows, rows), LOW),
            pltpu.VMEM((rows, 1), i32),
            pltpu.VMEM((rows, 1), i32),
            pltpu.VMEM((1, rows), i32),
        ]
        + sum_bufs(local, ranks, width)
        + ring_sems(ranks) * 2
        + line_sems(ranks)
        + spread_sems(ranks) * 4
        + [pltpu.SemaphoreType.DMA((heads * half + 8,))]
        + ring_sems(ranks),
        (
            span_order, doc_starts, tokens[0], out_grad[0], freqs, attn_gain[None], mlp_gain[None], q_gain, k_gain,
            w_query, w_key, w_value, w_output, w_gate, w_up, w_down,
        ),
    )
    block_out, dresid, dresid_low, mlp_own = call(
        functools.partial(mlp_kernel, ranks),
        2,
        [VM, VM, ANY, ANY, ANY],
        [
            ((local, width), LOW, VM),
            ((local, width), f32, VM),
            ((local, width), LOW, VM),
            ((ranks, own, 3 * ff), LOW, VM),
        ],
        [pltpu.VMEM((ranks, deep, 3 * ff), LOW)]
        + reduce_bufs(ranks, own, 3 * ff)
        + [
            pltpu.VMEM((rows, width), LOW),
            pltpu.VMEM((ranks, deep, 3 * ff), LOW),
            pltpu.VMEM((rows, ff), LOW),
            pltpu.VMEM((rows, 2 * ff), LOW),
            pltpu.VMEM((local, width), f32),
            pltpu.VMEM((rows, width), LOW),
        ]
        + sum_bufs(local, ranks, width)
        + sum_bufs(local, ranks, width)[1:]
        + [pltpu.SemaphoreType.DMA((3,))]
        + ring_sems(ranks) * 3
        + reduce_sems() * 4,
        (second, out_grad[0], resid, dy_all, mlp_block),
    )
    tokens_grad, gains, mlp_sums, attn_sums = call(
        functools.partial(back_kernel, ranks, kv_heads),
        3,
        [VM] * 4 + [ANY] * 12,
        [
            ((local, width), f32, VM),
            ((8, size), f32, VM),
            ((ranks, own, 3 * ff), LOW, ANY),
            ((ranks, own, a_cols), LOW, VM),
        ],
        [pltpu.VMEM((ranks, deep, a_cols), LOW)]
        + reduce_bufs(ranks, own, a_cols)
        + [
            pltpu.VMEM((ranks, own, a_cols), LOW),
            pltpu.VMEM((1, size), f32),
            pltpu.VMEM((1, size), f32),
            pltpu.VMEM((8, size), f32),
            pltpu.VMEM((ranks, 8, size), f32),
            pltpu.VMEM((8, size), f32),
            pltpu.VMEM((copies, 8, size), f32),
            pltpu.VMEM((rows, width), LOW),
            pltpu.VMEM((rows, q_cols), LOW),
            pltpu.VMEM((kv_heads, rows, size), f32),
            pltpu.VMEM((kv_heads, rows, size), f32),
            pltpu.VMEM((rows, qkv_cols), LOW),
            pltpu.VMEM((rows, q_cols), LOW),
            pltpu.VMEM((rows, width), LOW),
            pltpu.VMEM((ranks, deep, a_cols), LOW),
            pltpu.VMEM((rows, qkv_cols), f32),
            pltpu.VMEM((rows, size), f32),
            pltpu.VMEM((rows, size), f32),
            pltpu.VMEM((heads, rows, size), LOW),
            pltpu.VMEM((kv_heads, rows, size), LOW),
            pltpu.VMEM((kv_heads, rows, size), LOW),
            pltpu.VMEM((heads, rows, rows), LOW),
            pltpu.VMEM((local, width), f32),
        ]
        + sum_bufs(local, ranks, width)
        + ring_sems(ranks) * 2
        + reduce_sems() * 2
        + deliver_sems(ranks) * 3
        + [pltpu.SemaphoreType.DMA((ranks,))] * 2
        + [pltpu.SemaphoreType.DMA((copies,))] * 2
        + [pltpu.SemaphoreType.DMA((11,))]
        + deliver_sems(ranks) * 2
        + ring_sems(ranks),
        (
            tokens[0], dresid_low, q_gain, k_gain, out_low, first_in, attn_block, qkv, cosv, sinv, q_low, k_low,
            v_low, prob, dresid, mlp_own,
        ),
    )
    whole = pl.BlockSpec((1, own), lambda at: (0, 0))
    each = (q_cols, kv_cols, kv_cols, q_cols, ff, ff, ff)
    columns = [pl.BlockSpec((own, cols), lambda at: (0, at)) for cols in each]
    *grads, dga, dgm = pl.pallas_call(
        leave_kernel,
        grid=(ranks,),
        out_shape=[jax.ShapeDtypeStruct((own, cols * ranks), f32) for cols in each]
        + [jax.ShapeDtypeStruct((1, own), f32)] * 2,
        in_specs=[
            pl.BlockSpec((1, own, a_cols), lambda at: (at, 0, 0)),
            pl.BlockSpec((1, own, 3 * ff), lambda at: (at, 0, 0)),
            whole,
            whole,
            *columns[:3],
            *columns[4:6],
        ],
        out_specs=columns + [whole, whole],
    )(attn_sums, mlp_sums, attn_gain[None], mlp_gain[None], w_query, w_key, w_value, w_gate, w_up)
    return (
        block_out[None], tokens_grad[None], *grads[:4], dga[0], gains[0], gains[1], *grads[4:], dgm[0],
    )


def body(*args):
    tokens, w_key, query_gain = args[0], args[5], args[9]
    groups = w_key.shape[1] // query_gain.shape[0]
    ranks = lax.axis_size("seq")
    if tokens.shape[0] == 1 and ranks % 2 == 0 and groups % ranks == 0 and lax.axis_size("dp") == 4:
        return columns_body(*args)
    return gathered_body(*args)


def solution(mesh):
    return jax.shard_map(
        body,
        mesh=mesh,
        in_specs=(
            P("dp", "seq", None),
            P("dp", "seq", None),
            P(),
            P("dp", None),
            P(("seq", "dp"), None),
            P(("seq", "dp"), None),
            P(("seq", "dp"), None),
            P(("seq", "dp"), None),
            P(("seq", "dp")),
            P(),
            P(),
            P(("seq", "dp"), None),
            P(("seq", "dp"), None),
            P(("seq", "dp"), None),
            P(("seq", "dp")),
        ),
        out_specs=(
            P("dp", "seq", None),
            P("dp", "seq", None),
            P(("seq", "dp"), None),
            P(("seq", "dp"), None),
            P(("seq", "dp"), None),
            P(("seq", "dp"), None),
            P(("seq", "dp")),
            P(),
            P(),
            P(("seq", "dp"), None),
            P(("seq", "dp"), None),
            P(("seq", "dp"), None),
            P(("seq", "dp")),
        ),
        check_vma=False,
    )
```

```python
import functools
import math

import jax
import jax.numpy as jnp
import numpy as np
from jax import lax
from jax.experimental import pallas as pl
from jax.experimental.pallas import tpu as pltpu
from jax.sharding import PartitionSpec as P

EPS = 1e-06
NEG = -1e30


def normed(v, gain):
    scale_inv = lax.rsqrt(jnp.mean(v * v, -1, keepdims=True) + EPS)
    return (v * scale_inv * gain, scale_inv)


def norm_back(v, scale_inv, gain, grad):
    scaled = grad * gain
    inner = jnp.mean(scaled * v, -1, keepdims=True)
    dv = scale_inv * scaled - v * scale_inv * scale_inv * scale_inv * inner
    dgain = jnp.sum((grad * v * scale_inv).reshape(-1, v.shape[-1]), 0)
    return (dv, dgain)


def rotary(pos, width):
    half = width // 2
    freqs = jnp.exp(jnp.arange(half, dtype=jnp.float32) * (-2.0 / width * math.log(1000000.0)))
    angle = pos.astype(jnp.float32)[:, None] * freqs[None, :]
    return (jnp.cos(angle)[:, None, :], jnp.sin(angle)[:, None, :])


def rotate(v, cosv, sinv):
    half = v.shape[-1] // 2
    first, second = (v[..., :half], v[..., half:])
    return jnp.concatenate([first * cosv - second * sinv, second * cosv + first * sinv], -1)


def rotate_back(grad, cosv, sinv):
    half = grad.shape[-1] // 2
    first, second = (grad[..., :half], grad[..., half:])
    return jnp.concatenate([first * cosv + second * sinv, second * cosv - first * sinv], -1)


def place(order, begin, count, span):
    rows = begin + jnp.arange(count, dtype=jnp.int32)
    slots = rows // span
    picked = slots[:, None] == jnp.arange(order.shape[0], dtype=jnp.int32)[None, :]
    return jnp.sum(jnp.where(picked, order[None, :], 0), -1) * span + rows % span


def doc_of(starts, pos):
    return jnp.sum((starts[:, None, :] <= pos[None, :, None]).astype(jnp.int32), -1)


def gathered_body(
    tokens,
    out_grad,
    span_order,
    doc_starts,
    w_query,
    w_key,
    w_value,
    w_output,
    attn_gain,
    query_gain,
    key_gain,
    w_gate,
    w_up,
    w_down,
    mlp_gain,
):
    seqs, local, width = tokens.shape
    span = local // 2
    head_size = query_gain.shape[0]
    kv_heads = w_key.shape[1] // head_size
    heads = w_query.shape[1] // head_size
    share = heads // kv_heads
    kv_width = kv_heads * head_size
    ff_width = w_gate.shape[1]
    scale = 1.0 / math.sqrt(head_size)
    total_rows = seqs * local
    own_rows = width // lax.axis_size(("seq", "dp"))
    qpos = place(span_order, lax.axis_index("seq") * local, local, span)
    qdoc = doc_of(doc_starts, qpos)
    cosv, sinv = rotary(qpos, head_size)

    def gather_attn():
        return (
            lax.all_gather(w_query, ("seq", "dp"), axis=0, tiled=True),
            lax.all_gather(w_key, ("seq", "dp"), axis=0, tiled=True),
            lax.all_gather(w_value, ("seq", "dp"), axis=0, tiled=True),
            lax.all_gather(w_output, ("seq", "dp"), axis=0, tiled=True),
            lax.all_gather(
                attn_gain.astype(jnp.bfloat16), ("seq", "dp"), axis=0, tiled=True
            ).astype(attn_gain.dtype),
        )

    def gather_mlp():
        return (
            lax.all_gather(w_gate, ("seq", "dp"), axis=0, tiled=True),
            lax.all_gather(w_up, ("seq", "dp"), axis=0, tiled=True),
            lax.all_gather(w_down, ("seq", "dp"), axis=0, tiled=True),
            lax.all_gather(mlp_gain.astype(jnp.bfloat16), ("seq", "dp"), axis=0, tiled=True).astype(
                mlp_gain.dtype
            ),
        )

    x_rows = tokens.astype(jnp.float32).reshape(total_rows, width)
    wq_all, wk_all, wv_all, wo_all, ga_all = gather_attn()
    first_norm, first_inv = normed(x_rows, ga_all)
    first_in = first_norm.astype(jnp.bfloat16)
    q_raw = jnp.dot(first_in, wq_all, preferred_element_type=jnp.float32).reshape(
        seqs, local, heads, head_size
    )
    k_raw = jnp.dot(first_in, wk_all, preferred_element_type=jnp.float32).reshape(
        seqs, local, kv_heads, head_size
    )
    v_low = (
        jnp.dot(first_in, wv_all, preferred_element_type=jnp.float32)
        .astype(jnp.bfloat16)
        .reshape(seqs, local, kv_heads, head_size)
    )
    q_normed, q_inv = normed(q_raw, query_gain)
    k_normed, k_inv = normed(k_raw, key_gain)
    q_low = rotate(q_normed, cosv, sinv).astype(jnp.bfloat16)
    k_low = rotate(k_normed, cosv, sinv).astype(jnp.bfloat16)
    q_group = q_low.reshape(seqs, local, kv_heads, share, head_size)

    def scores(piece_key, start):
        count = piece_key.shape[1]
        kpos = place(span_order, start, count, span)
        kdoc = doc_of(doc_starts, kpos)
        visible = (qdoc[:, :, None] == kdoc[:, None, :]) & (
            kpos[None, None, :] <= qpos[None, :, None]
        )
        raw = (
            jnp.einsum("sqgjd,skgd->sgjqk", q_group, piece_key, preferred_element_type=jnp.float32)
            * scale
        )
        return (raw, visible[:, None, None])

    start_top = jnp.full((seqs, kv_heads, share, local), NEG, jnp.float32)
    piece = (
        lax.all_gather(k_low, "seq", axis=1, tiled=True),
        lax.all_gather(v_low, "seq", axis=1, tiled=True),
    )
    top = start_top
    raw, visible = scores(piece[0], jnp.int32(0))
    raw = jnp.where(visible, raw, NEG)
    new_top = jnp.maximum(top, jnp.max(raw, -1))
    weights = jnp.where(visible, jnp.exp(raw - new_top[..., None]), 0.0)
    total = jnp.sum(weights, -1)
    summed = jnp.einsum(
        "sgjqk,skgd->sgjqd",
        weights.astype(jnp.bfloat16),
        piece[1],
        preferred_element_type=jnp.float32,
    )
    top, total, summed = (new_top, total, summed)
    log_total = top + jnp.log(total)
    attn_vals = summed / total[..., None]
    out_low = (
        jnp.transpose(attn_vals, (0, 3, 1, 2, 4))
        .reshape(total_rows, heads * head_size)
        .astype(jnp.bfloat16)
    )
    resid = x_rows + jnp.einsum("nh,dh->nd", out_low, wo_all, preferred_element_type=jnp.float32)
    wg_all, wu_all, wd_all, gm_all = gather_mlp()
    second_norm, second_inv = normed(resid, gm_all)
    second_in = second_norm.astype(jnp.bfloat16)
    gate = jnp.dot(second_in, wg_all, preferred_element_type=jnp.float32)
    upper = jnp.dot(second_in, wu_all, preferred_element_type=jnp.float32)
    sigma = jax.nn.sigmoid(gate)
    act = gate * sigma
    hidden = (act * upper).astype(jnp.bfloat16)
    result = resid + jnp.einsum("nf,df->nd", hidden, wd_all, preferred_element_type=jnp.float32)
    block_out = result.astype(jnp.bfloat16).reshape(seqs, local, width)
    grad_low = out_grad.reshape(total_rows, width)
    wg_all, wu_all, wd_all, gm_all = gather_mlp()
    dmid = jnp.einsum("nd,df->nf", grad_low, wd_all, preferred_element_type=jnp.float32)
    dgate = (dmid * upper * sigma * (1.0 + gate * (1.0 - sigma))).astype(jnp.bfloat16)
    dupper = (dmid * act).astype(jnp.bfloat16)
    left = second_in
    outer = grad_low
    mlp_sums = lax.psum_scatter(
        jnp.concatenate(
            [
                jnp.einsum("nd,nf->df", left, dgate, preferred_element_type=jnp.float32),
                jnp.einsum("nd,nf->df", left, dupper, preferred_element_type=jnp.float32),
                jnp.einsum("nd,nf->df", outer, hidden, preferred_element_type=jnp.float32),
            ],
            1,
        ),
        ("seq", "dp"),
        scatter_dimension=0,
        tiled=True,
    )
    dsecond = jnp.einsum(
        "nf,df->nd", dgate, wg_all, preferred_element_type=jnp.float32
    ) + jnp.einsum("nf,df->nd", dupper, wu_all, preferred_element_type=jnp.float32)
    dresid_norm, dgm = norm_back(resid, second_inv, gm_all, dsecond)
    dresid = grad_low.astype(jnp.float32) + dresid_norm
    dresid_low = dresid.astype(jnp.bfloat16)
    wq_all, wk_all, wv_all, wo_all, ga_all = gather_attn()
    dout_low = jnp.einsum(
        "nd,dh->nh", dresid_low, wo_all, preferred_element_type=jnp.float32
    ).astype(jnp.bfloat16)
    dout_group = dout_low.reshape(seqs, local, kv_heads, share, head_size)
    delta = jnp.sum(jnp.transpose(dout_group.astype(jnp.float32), (0, 2, 3, 1, 4)) * attn_vals, -1)
    piece = (
        lax.all_gather(k_low, "seq", axis=1, tiled=True),
        lax.all_gather(v_low, "seq", axis=1, tiled=True),
    )
    count = piece[0].shape[1]
    raw, visible = scores(piece[0], jnp.int32(0))
    prob = jnp.where(visible, jnp.exp(raw - log_total[..., None]), 0.0)
    dprob = jnp.einsum(
        "sqgjd,skgd->sgjqk", dout_group, piece[1], preferred_element_type=jnp.float32
    )
    dscore = (prob * (dprob - delta[..., None])).astype(jnp.bfloat16)
    dq_sum = jnp.einsum("sgjqk,skgd->sqgjd", dscore, piece[0], preferred_element_type=jnp.float32)
    dk_part = (
        jnp.einsum("sgjqk,sqgjd->skgd", dscore, q_group, preferred_element_type=jnp.float32) * scale
    )
    dv_part = jnp.einsum(
        "sgjqk,sqgjd->skgd",
        prob.astype(jnp.bfloat16),
        dout_group,
        preferred_element_type=jnp.float32,
    )
    joined = jnp.concatenate(
        [dk_part.reshape(seqs, count, kv_width), dv_part.reshape(seqs, count, kv_width)], -1
    )
    buffer = joined
    dq_sum, buffer = (dq_sum, buffer)
    key_sums = lax.psum_scatter(
        buffer.astype(jnp.bfloat16), "seq", scatter_dimension=1, tiled=True
    ).astype(jnp.float32)
    dq_rot = (dq_sum * scale).reshape(seqs, local, heads, head_size)
    dq_raw, dgq = norm_back(q_raw, q_inv, query_gain, rotate_back(dq_rot, cosv, sinv))
    dk_rot = key_sums[..., :kv_width].reshape(seqs, local, kv_heads, head_size)
    dk_raw, dgk = norm_back(k_raw, k_inv, key_gain, rotate_back(dk_rot, cosv, sinv))
    dq_low = dq_raw.reshape(total_rows, heads * head_size).astype(jnp.bfloat16)
    dk_low = dk_raw.reshape(total_rows, kv_width).astype(jnp.bfloat16)
    dv_low = key_sums[..., kv_width:].reshape(total_rows, kv_width).astype(jnp.bfloat16)
    left = first_in
    outer = dresid_low
    attn_sums = lax.psum_scatter(
        jnp.concatenate(
            [
                jnp.einsum("nd,nh->dh", left, dq_low, preferred_element_type=jnp.float32),
                jnp.einsum("nd,nh->dh", left, dk_low, preferred_element_type=jnp.float32),
                jnp.einsum("nd,nh->dh", left, dv_low, preferred_element_type=jnp.float32),
                jnp.einsum("nd,nh->dh", outer, out_low, preferred_element_type=jnp.float32),
            ],
            1,
        ),
        ("seq", "dp"),
        scatter_dimension=0,
        tiled=True,
    )
    dfirst = jnp.einsum("nh,dh->nd", dq_low, wq_all, preferred_element_type=jnp.float32)
    dfirst = dfirst + jnp.einsum("nh,dh->nd", dk_low, wk_all, preferred_element_type=jnp.float32)
    dfirst = dfirst + jnp.einsum("nh,dh->nd", dv_low, wv_all, preferred_element_type=jnp.float32)
    dx_norm, dga = norm_back(x_rows, first_inv, ga_all, dfirst)
    tokens_grad = (dresid + dx_norm).reshape(seqs, local, width)
    dga_all, dgm_all, dgq_all, dgk_all = lax.psum((dga, dgm, dgq, dgk), ("seq", "dp"))
    offset = lax.axis_index(("seq", "dp")) * own_rows
    attn_gain_grad = lax.dynamic_slice_in_dim(dga_all, offset, own_rows, 0)
    mlp_gain_grad = lax.dynamic_slice_in_dim(dgm_all, offset, own_rows, 0)
    q_cols = heads * head_size
    w_query_grad = attn_sums[:, :q_cols]
    w_key_grad = attn_sums[:, q_cols : q_cols + kv_width]
    w_value_grad = attn_sums[:, q_cols + kv_width : q_cols + 2 * kv_width]
    w_output_grad = attn_sums[:, q_cols + 2 * kv_width :]
    w_gate_grad = mlp_sums[:, :ff_width]
    w_up_grad = mlp_sums[:, ff_width : 2 * ff_width]
    w_down_grad = mlp_sums[:, 2 * ff_width :]
    return (
        block_out,
        tokens_grad,
        w_query_grad,
        w_key_grad,
        w_value_grad,
        w_output_grad,
        attn_gain_grad,
        dgq_all,
        dgk_all,
        w_gate_grad,
        w_up_grad,
        w_down_grad,
        mlp_gain_grad,
    )


LOW = jnp.bfloat16
MESH = pl.DeviceIdType.MESH
LIMIT = 60 * 2**20


def ring_order(ranks):
    half = ranks // 2
    order = [0]
    for step in range(1, half):
        order += [step, ranks - step]
    return order + [half]


def ring_place(seq, ranks):
    z, x = lax.div(seq, 2), lax.rem(seq, 2)
    return z + x * (ranks - 1 - 2 * z)


def ring_seq(place, ranks):
    half = ranks // 2
    x, z = lax.div(place, half), lax.rem(place, half)
    return 2 * (z + x * (half - 1 - 2 * z)) + x


def neighbours(ranks):
    seq, dp = lax.axis_index("seq"), lax.axis_index("dp")
    at = ring_place(seq, ranks)
    right = ring_seq(lax.rem(at + 1, ranks), ranks)
    left = ring_seq(lax.rem(at + ranks - 1, ranks), ranks)
    return (right, dp), (left, dp)


def knock(devices):
    barrier = pltpu.get_barrier_semaphore()
    for device in devices:
        pl.semaphore_signal(barrier, inc=1, device_id=device, device_id_type=MESH)


def answered(devices):
    pl.semaphore_wait(pltpu.get_barrier_semaphore(), len(devices))


def move(src, dst, sem):
    copy = pltpu.make_async_copy(src, dst, sem)
    copy.start()
    return copy


def push(src, dst, send, recv, device):
    return pltpu.make_async_remote_copy(
        src_ref=src, dst_ref=dst, send_sem=send, recv_sem=recv, device_id=device, device_id_type=MESH
    )


def dot_nn(left, right):
    return jnp.dot(left, right, preferred_element_type=jnp.float32)


def dot_nt(left, right):
    return lax.dot_general(left, right, (((1,), (1,)), ((), ())), preferred_element_type=jnp.float32)


def dot_tn(left, right):
    return lax.dot_general(left, right, (((0,), (0,)), ((), ())), preferred_element_type=jnp.float32)


def block_row(rel, local, ranks):
    place = ring_place(lax.axis_index("seq"), ranks)
    return pl.multiple_of(ring_seq(lax.rem(place + rel, ranks), ranks) * local, local)


def block_rows(ref, rels, local, ranks):
    blocks = [ref[pl.ds(block_row(rel, local, ranks), local)] for rel in rels]
    return blocks[0] if len(blocks) == 1 else jnp.concatenate(blocks, 0)


def rels_of(step, ranks):
    return [rel for rel in ring_order(ranks) if min(rel, ranks - rel) == step]


class RingGather:
    def __init__(self, buf, local, ranks, send, recv, right, left, row):
        self.buf, self.sub, self.half = buf, local // 2, ranks // 2
        self.send, self.recv, self.right, self.left = send, recv, right, left
        self.ranks, self.row = ranks, row

    def copies(self, step, part):
        ways = ((0, (self.ranks - step + 1) % self.ranks, self.right), (1, step - 1, self.left))
        given = []
        for way, rel, device in ways:
            if step < self.half or way == part:
                block = self.buf.at[pl.ds(self.row(rel) + part * self.sub, self.sub)]
                at = 2 * (step - 1) + part
                given.append(push(block, block, self.send.at[way, at], self.recv.at[way, at], device))
        return given

    def start(self, step):
        for part in range(2):
            for copy in self.copies(step, part):
                copy.start()

    def advance(self, step):
        for part in range(2):
            for copy in self.copies(step, part):
                copy.wait_recv()
            if step < self.half:
                for copy in self.copies(step + 1, part):
                    copy.start()

    def finish(self):
        for step in range(1, self.half + 1):
            for part in range(2):
                for copy in self.copies(step, part):
                    copy.wait_send()


class LineGather:
    def __init__(self, buf, local, ranks, send, recv, x_send, x_recv):
        self.buf, self.local, self.length = buf, local, ranks // 2
        self.send, self.recv, self.x_send, self.x_recv = send, recv, x_send, x_recv
        self.seq, self.dp = lax.axis_index("seq"), lax.axis_index("dp")
        self.z, self.x = lax.div(self.seq, 2), lax.rem(self.seq, 2)

    def block(self, z):
        return self.buf.at[pl.ds(pl.multiple_of((2 * z + self.x) * self.local, self.local), self.local)]

    def hop(self, way, step):
        block = self.block(self.z + (step - 1 if way else 1 - step))
        to = self.seq + (-2 if way else 2)
        return push(block, block, self.send.at[way, step - 1], self.recv.at[way, step - 1], (to, self.dp))

    def sends(self, way, step):
        if way:
            return (self.z > 0) & (self.z + step <= self.length)
        return (self.z < self.length - 1) & (self.z >= step - 1)

    def comes(self, way, step):
        return self.z + step < self.length if way else self.z >= step

    def across(self, way, step):
        block = self.block(self.z + (step if way else -step))
        at = step + way * (self.length - 1)
        return push(
            block, block, self.x_send.at[at], self.x_recv.at[at], (self.seq + 1 - 2 * self.x, self.dp)
        )

    def from_x(self, way, step):
        z = self.z + (step if way else -step)
        row = pl.multiple_of((2 * z + 1 - self.x) * self.local, self.local)
        block = self.buf.at[pl.ds(row, self.local)]
        at = step + way * (self.length - 1)
        return push(
            block, block, self.x_send.at[at], self.x_recv.at[at], (self.seq + 1 - 2 * self.x, self.dp)
        )

    def start(self, step):
        for way in range(2):
            pl.when(self.sends(way, step))(lambda way=way: self.hop(way, step).start())
        self.pass_on(step - 1)

    def pass_on(self, step):
        if step == 0:
            self.across(0, 0).start()
            return
        for way in range(2):
            pl.when(self.comes(way, step))(lambda way=way: self.across(way, step).start())

    def arrive(self, step):
        for way in range(2):
            pl.when(self.comes(way, step))(lambda way=way: self.incoming(way, step).wait_recv())

    def incoming(self, way, step):
        block = self.block(self.z + (step if way else -step))
        to = self.seq + 1 - 2 * self.x
        return push(block, block, self.send.at[way, step - 1], self.recv.at[way, step - 1], (to, self.dp))

    def run(self):
        for step in range(1, self.length):
            self.advance(step)

    def advance(self, step):
        self.arrive(step)
        if step < self.length - 1:
            self.start(step + 1)
        else:
            self.pass_on(step)

    def complete(self):
        self.from_x(0, 0).wait_recv()
        for step in range(1, self.length):
            for way in range(2):
                pl.when(self.comes(way, step))(lambda way=way: self.from_x(way, step).wait_recv())

    def finish(self):
        self.across(0, 0).wait_send()
        for step in range(1, self.length):
            for way in range(2):
                pl.when(self.sends(way, step))(lambda way=way: self.hop(way, step).wait_send())
                pl.when(self.comes(way, step))(lambda way=way: self.across(way, step).wait_send())


def line_sems(ranks):
    half = ranks // 2
    return [pltpu.SemaphoreType.DMA((2, half))] * 2 + [pltpu.SemaphoreType.DMA((2 * half,))] * 2


class RingSum:
    def __init__(self, part, term, out_buf, in_buf, local, ranks, send, recv, right, left, stream=0, streams=1):
        self.part, self.term, self.out_buf, self.in_buf = part, term, out_buf, in_buf
        self.local, self.ranks, self.half = local, ranks, ranks // 2
        each = term.shape[1] // streams
        self.cols = pl.ds(stream * each, each)
        self.tiles = (stream * ranks // streams, (stream + 1) * ranks // streams)
        self.send, self.recv, self.right, self.left = send, recv, right, left

    def copies(self, step):
        rows = self.local // 2 if step == 1 else self.local
        skip = self.local // 2 if step == 1 else 0
        return [
            push(
                self.out_buf.at[way, (step - 1) % 2, pl.ds(begin, rows), self.cols],
                self.in_buf.at[way, step - 1, pl.ds(begin, rows), self.cols],
                self.send.at[way, step - 1],
                self.recv.at[way, step - 1],
                device,
            )
            for way, begin, device in ((0, 0, self.right), (1, skip, self.left))
        ]

    def compute(self, step):
        if step == 1:
            self.part([self.half], *self.tiles)
        elif step <= self.half:
            self.part(rels_of(self.half + 1 - step, self.ranks), *self.tiles)
        else:
            self.part([0], *self.tiles)

    def launch(self, step):
        local, skip = self.local, self.local // 2
        if step > 2:
            for copy in self.copies(step - 2):
                copy.wait_send()
        if step == 1:
            for way in range(2):
                rows = pl.ds(way * skip, skip)
                self.out_buf[way, 0, rows, self.cols] = self.term[rows, self.cols].astype(LOW)
        else:
            for copy in self.copies(step - 1):
                copy.wait_recv()
            for way in range(2):
                for begin, with_sum in ((0, step > 2 or way == 0), (skip, step > 2 or way == 1)):
                    value = self.term[pl.ds(way * local + begin, skip), self.cols]
                    if with_sum:
                        value = value + self.in_buf[way, step - 2, pl.ds(begin, skip), self.cols].astype(jnp.float32)
                    self.out_buf[way, (step - 1) % 2, pl.ds(begin, skip), self.cols] = value.astype(LOW)
        for copy in self.copies(step):
            copy.start()

    def last(self, begin, count):
        rows = pl.ds(begin, count)
        value = self.term[rows, self.cols] + self.in_buf[0, self.half - 1, rows, self.cols].astype(jnp.float32)
        return value + self.in_buf[1, self.half - 1, rows, self.cols].astype(jnp.float32)

    def arrive_last(self):
        for copy in self.copies(self.half):
            copy.wait_recv()

    def finish(self):
        for step in range(max(1, self.half - 1), self.half + 1):
            for copy in self.copies(step):
                copy.wait_send()


def two_sums(part, term, out_buf, in_buf, local, ranks, sems, right, left):
    return [
        RingSum(
            part, term, out_buf, in_buf, local, ranks, sems[2 * at], sems[2 * at + 1], right, left, at, 2
        )
        for at in range(2)
    ]


def ring_sems(ranks):
    return [pltpu.SemaphoreType.DMA((2, ranks)), pltpu.SemaphoreType.DMA((2, ranks))]


def sum_bufs(local, ranks, width):
    return [
        pltpu.VMEM((2 * local, width), jnp.float32),
        pltpu.VMEM((2, 2, local, width), LOW),
        pltpu.VMEM((2, ranks // 2, local, width), LOW),
    ]


def turn(v):
    return pltpu.roll(v, v.shape[-1] // 2, v.ndim - 1)


def rows_scaled(v):
    inv = lax.rsqrt(jnp.mean(v * v, -1, keepdims=True) + EPS)
    return v * inv, inv


def rows_scaled_back(v, inv, grad):
    return inv * grad - v * (inv * inv * inv * jnp.mean(grad * v, -1, keepdims=True))


class Spread:
    def __init__(self, rows, block, ranks, own, cols, sems):
        self.rows, self.block, self.ranks, self.own, self.cols = rows, block, ranks, own, cols
        self.send, self.recv, self.hop_send, self.hop_recv, self.here = sems
        self.seq, self.dp = lax.axis_index("seq"), lax.axis_index("dp")
        y, core = lax.div(self.dp, 2), lax.rem(self.dp, 2)
        self.beside, self.sibling = (1 - y) * 2 + core, y * 2 + 1 - core

    def at(self, dp):
        return pl.ds(pl.multiple_of(dp * self.own, self.own), self.own)

    def exchange(self):
        for step in range(1, self.ranks):
            peer = lax.rem(self.seq + step, self.ranks)
            yield push(
                self.rows.at[peer, :, self.cols],
                self.block.at[self.seq, self.at(self.dp), self.cols],
                self.send.at[step],
                self.recv.at[step],
                (peer, self.dp),
            )

    def keep(self):
        return pltpu.make_async_copy(
            self.rows.at[self.seq, :, self.cols],
            self.block.at[self.seq, self.at(self.dp), self.cols],
            self.here,
        )

    def hop(self, number):
        dp = self.beside if number == 2 else self.dp
        part = self.block.at[:, self.at(dp), self.cols]
        to = self.beside if number == 0 else self.sibling
        return push(part, part, self.hop_send.at[number], self.hop_recv.at[number], (self.seq, to))

    def start(self):
        self.keep().start()
        for copy in self.exchange():
            copy.start()

    def arrive(self):
        self.keep().wait()
        for copy in self.exchange():
            copy.wait_recv()

    def finish(self):
        for copy in self.exchange():
            copy.wait_send()
        for number in range(3):
            self.hop(number).wait_send()


def spread_sems(ranks):
    return [
        pltpu.SemaphoreType.DMA((ranks,)),
        pltpu.SemaphoreType.DMA((ranks,)),
        pltpu.SemaphoreType.DMA((3,)),
        pltpu.SemaphoreType.DMA((3,)),
        pltpu.SemaphoreType.DMA,
    ]


class WholeGather:
    def __init__(self, block, ranks, own, sems):
        self.block, self.ranks, self.half, self.own = block, ranks, ranks // 2, own
        self.send, self.recv, self.y_send, self.y_recv, self.core_send, self.core_recv = sems
        self.seq, self.dp = lax.axis_index("seq"), lax.axis_index("dp")
        self.right, self.left = neighbours(ranks)
        self.place = ring_place(self.seq, ranks)
        y, core = lax.div(self.dp, 2), lax.rem(self.dp, 2)
        self.beside, self.sibling = (1 - y) * 2 + core, y * 2 + 1 - core

    def at(self, rel, dp, begin, count):
        seq = ring_seq(lax.rem(self.place + rel + self.ranks, self.ranks), self.ranks)
        return self.block.at[seq, pl.ds(pl.multiple_of(dp * self.own + begin, count), count)]

    def copies(self, step):
        last = step == self.half
        rows = self.own // 2 if last else self.own
        skip = self.own // 2 if last else 0
        given = []
        for way, rel, begin, device in ((0, 1 - step, 0, self.right), (1, step - 1, skip, self.left)):
            part = self.at(rel, self.dp, begin, rows)
            given.append(push(part, part, self.send.at[way, step - 1], self.recv.at[way, step - 1], device))
        return given

    def start(self, step):
        for copy in self.copies(step):
            copy.start()

    def hops(self, step):
        for at, rel in enumerate(ring_order(self.ranks)):
            if min(rel, self.ranks - rel) == step:
                part = self.at(rel, self.dp, 0, self.own)
                yield push(part, part, self.y_send.at[at], self.y_recv.at[at], (self.seq, self.beside))
                yield push(part, part, self.core_send.at[at], self.core_recv.at[at], (self.seq, self.sibling))

    def arrive(self, step):
        for copy in self.copies(step):
            copy.wait_recv()

    def forward(self, step):
        for copy in self.hops(step):
            copy.start()

    def cross(self):
        part = self.block.at[:, pl.ds(pl.multiple_of(self.beside * self.own, self.own), self.own)]
        at = self.ranks
        return push(part, part, self.core_send.at[at], self.core_recv.at[at], (self.seq, self.sibling))

    def complete(self):
        for step in range(self.half + 1):
            for copy in self.hops(step):
                copy.wait_recv()
        self.cross().start()
        self.cross().wait_recv()

    def finish(self):
        for step in range(1, self.half + 1):
            for copy in self.copies(step):
                copy.wait_send()
        for step in range(self.half + 1):
            for copy in self.hops(step):
                copy.wait_send()
        self.cross().wait_send()


def whole_sems(ranks):
    return (
        ring_sems(ranks)
        + [pltpu.SemaphoreType.DMA((ranks,))] * 2
        + [pltpu.SemaphoreType.DMA((ranks + 1,))] * 2
    )


class Reduce:
    def __init__(self, grads, from_core, from_y, total, own, first, count, cols, sems):
        self.grads, self.from_core, self.from_y, self.total = grads, from_core, from_y, total
        self.own, self.begin, self.count, self.cols = own, first, count, cols
        self.send, self.recv = sems
        self.seq, dp = lax.axis_index("seq"), lax.axis_index("dp")
        self.y, self.core = lax.div(dp, 2), lax.rem(dp, 2)
        self.beside, self.sibling = (1 - self.y) * 2 + self.core, self.y * 2 + 1 - self.core

    def at(self, y, core):
        return pl.ds(pl.multiple_of((y * 2 + core) * self.own, self.own), self.own)

    def hop(self, number):
        some, cols = pl.ds(self.begin, self.count), self.cols
        if number == 2:
            src, dst, to = self.from_core.at[0, some, :, cols], self.from_y.at[some, :, cols], self.beside
        else:
            rows = self.at(1 - self.y if number == 0 else self.y, 1 - self.core)
            src, dst, to = self.grads.at[some, rows, cols], self.from_core.at[number, some, :, cols], self.sibling
        return push(src, dst, self.send.at[number], self.recv.at[number], (self.seq, to))

    def first(self):
        self.hop(0).start()
        self.hop(1).start()

    def second(self):
        self.hop(0).wait_recv()
        rows = self.at(1 - self.y, self.core)

        def some(at, _):
            value = self.grads[at, rows, self.cols].astype(jnp.float32)
            value = value + self.from_core[0, at, :, self.cols].astype(jnp.float32)
            self.from_core[0, at, :, self.cols] = value.astype(LOW)
            return 0

        lax.fori_loop(self.begin, self.begin + self.count, some, 0)
        self.hop(2).start()

    def third(self):
        self.hop(1).wait_recv()
        self.hop(2).wait_recv()
        rows = self.at(self.y, self.core)

        def some(at, _):
            value = self.grads[at, rows, self.cols].astype(jnp.float32)
            value = value + self.from_core[1, at, :, self.cols].astype(jnp.float32)
            value = value + self.from_y[at, :, self.cols].astype(jnp.float32)
            self.total[at, :, self.cols] = value.astype(LOW)
            return 0

        lax.fori_loop(self.begin, self.begin + self.count, some, 0)

    def finish(self):
        for number in range(3):
            self.hop(number).wait_send()


def reduce_sems():
    return [pltpu.SemaphoreType.DMA((3,)), pltpu.SemaphoreType.DMA((3,))]


def reduce_bufs(ranks, own, cols):
    return [pltpu.VMEM((2, ranks, own, cols), LOW), pltpu.VMEM((ranks, own, cols), LOW)]


class Deliver:
    def __init__(self, rows, out, cols, ranks, sems):
        self.rows, self.out, self.cols, self.ranks = rows, out, cols, ranks
        self.send, self.recv, self.here = sems
        self.seq, self.dp = lax.axis_index("seq"), lax.axis_index("dp")

    def exchange(self):
        for step in range(1, self.ranks):
            peer = lax.rem(self.seq + step, self.ranks)
            yield push(
                self.rows.at[peer, :, self.cols],
                self.out.at[self.seq, :, self.cols],
                self.send.at[step],
                self.recv.at[step],
                (peer, self.dp),
            )

    def keep(self):
        return pltpu.make_async_copy(
            self.rows.at[self.seq, :, self.cols], self.out.at[self.seq, :, self.cols], self.here
        )

    def start(self):
        self.keep().start()
        for copy in self.exchange():
            copy.start()

    def finish(self):
        self.keep().wait()
        for copy in self.exchange():
            copy.wait_recv()
        for copy in self.exchange():
            copy.wait_send()


def deliver_sems(ranks):
    return [pltpu.SemaphoreType.DMA((ranks,)), pltpu.SemaphoreType.DMA((ranks,)), pltpu.SemaphoreType.DMA]


def first_kernel(
    ranks, kv_heads, order, starts, tokens, out_grad, freqs, attn_gain, mlp_gain, query_gain, key_gain,
    w_query, w_key, w_value, w_output, w_gate, w_up, w_down,
    resid, second, cosv, sinv, q_low, k_low, v_low, own_out, first_in, qkv, attn_block, dy_all, prob, mlp_block, out_all,
    held, normal, kept, block, a_rows, m_rows, gate, up, down, dys, probs, pos, begins, pos_row,
    out_low, whole, *sems,
):
    local, width = tokens.shape
    rows = local * ranks
    own = w_query.shape[0]
    size = freqs.shape[1]
    heads = q_low.shape[0]
    share = heads // kv_heads
    half = ranks // 2
    scale = 1.0 / math.sqrt(size)
    cols = (heads + 2 * kv_heads) * size
    deep = block.shape[1]
    row = functools.partial(block_row, local=local, ranks=ranks)
    seq, dp = lax.axis_index("seq"), lax.axis_index("dp")
    right, left = neighbours(ranks)
    attn = Spread(a_rows, block, ranks, own, pl.ds(0, a_rows.shape[2]), sems[12:17])
    third = m_rows.shape[2] // 3
    mlp = [
        Spread(m_rows, mlp_block, ranks, own, pl.ds(at * third, third), sems[17 + 5 * at : 22 + 5 * at])
        for at in range(3)
    ]
    local_sems = sems[32]
    out_send, out_recv = sems[2:4]
    o_cols = heads * size
    peers = [(lax.rem(seq + step, ranks), dp) for step in range(1, ranks)]
    peers += [(seq, attn.beside), (seq, attn.sibling)]
    knock(peers)
    loads = [
        move(src, dst, local_sems.at[at])
        for at, (src, dst) in enumerate(((w_gate, gate), (w_up, up), (w_down, down)))
    ]
    held[pl.ds(row(0), local)] = tokens[...]
    dys[pl.ds(row(0), local)] = out_grad[...]

    def column(line):
        same = lax.broadcasted_iota(jnp.int32, (own, own), 0) == lax.broadcasted_iota(jnp.int32, (own, own), 1)
        return jnp.sum(jnp.where(same, line, 0.0), 1, keepdims=True)

    def lay(target, begin, weight, gain):
        each = weight.shape[1] // ranks
        for rank in range(ranks):
            part = weight[:, rank * each : (rank + 1) * each]
            if gain is not None:
                part = (part.astype(jnp.float32) * gain).astype(LOW)
            target[rank, :, begin : begin + each] = part
        return begin + each

    gain = column(attn_gain[...])
    at = 0
    for weight in (w_query, w_key, w_value):
        at = lay(a_rows, at, weight, gain)
    whole[seq, pl.ds(pl.multiple_of(dp * own, own), own)] = w_output[...]
    answered(peers)
    ring = RingGather(held, local, ranks, sems[0], sems[1], right, left, row)
    ring.start(1)
    attn.start()
    outs = WholeGather(whole, ranks, own, [*sems[8:12], *sems[33:35]])
    outs.forward(0)
    line = LineGather(dys, local, ranks, sems[4], sems[5], sems[6], sems[7])
    stores = []

    def store(src, dst):
        stores.append(move(src, dst, local_sems.at[len(loads) + len(stores)]))

    def scale_rows(step):
        for rel in rels_of(step, ranks):

            def some(at, _):
                rows_at = pl.ds(pl.multiple_of(row(rel) + at * 32, 32), 32)
                normal[rows_at] = rows_scaled(held[rows_at].astype(jnp.float32))[0].astype(LOW)
                return 0

            lax.fori_loop(0, local // 32, some, 0)

    for load in loads:
        load.wait()
    gain = column(mlp_gain[...])
    each = gate.shape[1] // ranks
    lay(m_rows, 0, gate, gain)
    lay(m_rows, each, up, gain)
    lay(m_rows, 2 * each, down, None)
    scale_rows(0)
    ring.advance(1)
    scale_rows(1)
    attn.arrive()
    attn.hop(0).start()
    attn.hop(1).start()
    spans = order.shape[0]
    span = rows // spans
    for at in range(ranks):
        rows_at = pl.ds(at * local, local)
        ids = at * local + lax.broadcasted_iota(jnp.int32, (1, local), 1)
        where = jnp.zeros_like(ids)
        for slot in range(spans):
            inside = (ids >= slot * span) & (ids < (slot + 1) * span)
            where = where + jnp.where(inside, ids + (order[slot] - slot) * span, 0)
        begin = jnp.zeros_like(ids)
        for doc in range(starts.shape[1]):
            begin = jnp.maximum(begin, jnp.where(starts[0, doc] <= where, starts[0, doc], 0))
        pos_row[:, rows_at] = where
        across = jnp.broadcast_to(where, (local, local)).T
        pos[rows_at] = across[:, :1]
        begins[rows_at] = jnp.broadcast_to(begin, (local, local)).T[:, :1]
        angle = across[:, :1].astype(jnp.float32) * freqs[...]
        lane = lax.broadcasted_iota(jnp.int32, (local, size), 1)
        cosv[rows_at] = jnp.cos(angle)
        sine = jnp.sin(angle)
        sinv[rows_at] = jnp.where(lane < size // 2, -sine, sine)
    for step in range(2, half):
        ring.advance(step)
        scale_rows(step)
        if step == 2:
            outs.start(1)
            attn.hop(0).wait_recv()
            attn.hop(2).start()

    def bring(step):
        outs.arrive(step)
        if step < half:
            outs.start(step + 1)
        outs.forward(step)

    bring(1)
    mlp[0].start()
    attn.hop(1).wait_recv()
    attn.hop(2).wait_recv()
    store(block, attn_block)

    def project(begin, count):
        rows_at = pl.ds(begin, count)
        kept[rows_at] = dot_nn(normal[rows_at], block[...].reshape(width, cols))

    ring.advance(half)
    bring(2)
    scale_rows(half)
    store(normal, first_in)
    tile = rows // half

    def rotated(at, rows_at, gain):
        v = rows_scaled(kept[rows_at, at * size : (at + 1) * size])[0] * gain[...]
        return (v * cosv[rows_at] + turn(v) * sinv[rows_at]).astype(LOW)

    for piece in range(half):
        rows_at = pl.ds(piece * tile, tile)
        project(piece * tile, tile)
        for head in range(heads):
            q_low[head, rows_at] = rotated(head, rows_at, query_gain)
        for group in range(kv_heads):
            k_low[group, rows_at] = rotated(heads + group, rows_at, key_gain)
            at = (heads + kv_heads + group) * size
            v_low[group, rows_at] = kept[rows_at, at : at + size].astype(LOW)
    store(kept, qkv)
    bring(3)
    mlp[1].start()

    def forward(piece):
        mlp[piece].arrive()
        mlp[piece].hop(0).start()
        mlp[piece].hop(1).start()

    for piece in range(half):
        rows_at = pl.ds(piece * tile, tile)
        seen = (pos_row[...] <= pos[rows_at]) & (pos_row[...] >= begins[rows_at])
        for head in range(heads):
            raw = dot_nt(q_low[head, rows_at], k_low[head // share]) * scale
            raw = jnp.where(seen, raw, NEG)
            weight = jnp.exp(raw - jnp.max(raw, -1, keepdims=True))
            weight = (weight * (1.0 / jnp.sum(weight, -1, keepdims=True))).astype(LOW)
            probs[head, rows_at] = weight
            value = dot_nn(weight, v_low[head // share])
            out_low[rows_at, head * size : (head + 1) * size] = value.astype(LOW)
            store(probs.at[head, rows_at], prob.at[head, rows_at])
        if piece == 0:
            bring(half)
        if piece == half - 2:
            forward(0)
    place = ring_place(seq, ranks)

    def exchange(rel):
        to = ring_seq(lax.rem(place + rel, ranks), ranks)
        return push(
            out_low.at[pl.ds(row(rel), local)],
            own_out.at[:, pl.ds(pl.multiple_of(seq * o_cols, o_cols), o_cols)],
            out_send.at[rel],
            out_recv.at[rel],
            (to, dp),
        )

    for rel in range(1, ranks):
        exchange(rel).start()
    own_out[:, pl.ds(pl.multiple_of(seq * o_cols, o_cols), o_cols)] = out_low[pl.ds(row(0), local)]
    line.start(1)
    mlp[2].start()
    forward(1)
    outs.complete()
    store(whole, out_all)
    for rel in range(1, ranks):
        exchange(rel).wait_recv()
    line.advance(1)

    def join(at, _):
        some = pl.ds(pl.multiple_of(at * deep, deep), deep)
        resid[:, some] = tokens[:, some].astype(jnp.float32) + dot_nt(own_out[...], whole[at])
        return 0

    lax.fori_loop(0, ranks, join, 0)

    def scale_second(at, _):
        rows_at = pl.ds(pl.multiple_of(at * 32, 32), 32)
        second[rows_at] = rows_scaled(resid[rows_at])[0].astype(LOW)
        return 0

    lax.fori_loop(0, local // 32, scale_second, 0)
    mlp[0].hop(0).wait_recv()
    mlp[0].hop(2).start()
    forward(2)
    for step in range(2, half):
        line.advance(step)
    for piece in mlp[1:]:
        piece.hop(0).wait_recv()
        piece.hop(2).start()
    line.complete()
    store(dys, dy_all)
    ring.finish()
    attn.finish()
    outs.finish()
    for rel in range(1, ranks):
        exchange(rel).wait_send()
    line.finish()
    for piece in mlp:
        piece.hop(1).wait_recv()
        piece.hop(2).wait_recv()
        piece.finish()
    for given in stores:
        given.wait()


def mlp_kernel(
    ranks, second, out_grad, rest, dys, mlp_block, block_out, dresid, dresid_low, own_grads,
    grads, from_core, from_y, held, weights, hidden, dgu, resid, dy_all,
    term, out_buf, in_buf, y_out, y_in, here, *sems,
):
    local, width = second.shape
    row = functools.partial(block_row, local=local, ranks=ranks)
    ff = hidden.shape[1]
    deep = weights.shape[1]
    half = ranks // 2
    right, left = neighbours(ranks)
    loads = [
        move(src, dst, here.at[at])
        for at, (src, dst) in enumerate(((mlp_block, weights), (dys, dy_all), (rest, resid)))
    ]
    seq, dp = lax.axis_index("seq"), lax.axis_index("dp")
    own = own_grads.shape[1]
    pieces = [
        Reduce(
            grads, from_core, from_y, own_grads, own, at * ranks // 4, ranks // 4, pl.ds(0, 3 * ff),
            sems[6 + 2 * at : 8 + 2 * at],
        )
        for at in range(4)
    ]
    peers = [right, left, (seq, pieces[0].beside), (seq, pieces[0].sibling)]
    knock(peers)
    held[pl.ds(row(0), local)] = second[...]
    answered(peers)
    ring = RingGather(held, local, ranks, sems[0], sems[1], right, left, row)
    ring.start(1)
    loads[0].wait()
    loads[1].wait()
    wide = 256

    def middle(step):
        rels = rels_of(step, ranks)

        def some(at, _):
            first = pl.multiple_of(at * wide, wide)
            given, dy = block_rows(held, rels, local, ranks), block_rows(dy_all, rels, local, ranks)
            gate = dot_nn(given, weights[:, :, pl.ds(first, wide)].reshape(width, wide))
            upper = dot_nn(given, weights[:, :, pl.ds(ff + first, wide)].reshape(width, wide))
            dmid = dot_nn(dy, weights[:, :, pl.ds(2 * ff + first, wide)].reshape(width, wide))
            sigma = 1.0 / (1.0 + jnp.exp(-gate))
            act = gate * sigma
            value = (act * upper).astype(LOW)
            dgate = (dmid * upper * (sigma * (1.0 + gate * (1.0 - sigma)))).astype(LOW)
            dupper = (dmid * act).astype(LOW)
            for at, rel in enumerate(rels):
                rows, some_rows = pl.ds(row(rel), local), slice(at * local, (at + 1) * local)
                hidden[rows, pl.ds(first, wide)] = value[some_rows]
                dgu[rows, pl.ds(first, wide)] = dgate[some_rows]
                dgu[rows, pl.ds(ff + first, wide)] = dupper[some_rows]
            return 0

        lax.fori_loop(0, ff // wide, some, 0)

    middle(0)
    for step in range(1, half + 1):
        ring.advance(step)
        middle(step)

    def back_part(rels, begin, end):
        def some(at, _):
            value = dot_nt(block_rows(dgu, rels, local, ranks), weights[at, :, : 2 * ff])
            term[: len(rels) * local, pl.ds(pl.multiple_of(at * deep, deep), deep)] = value
            return 0

        lax.fori_loop(begin, end, some, 0)

    def out_part(rels, begin, end):
        def some(at, _):
            value = dot_nt(block_rows(hidden, rels, local, ranks), weights[at, :, 2 * ff :])
            term[: len(rels) * local, pl.ds(pl.multiple_of(at * deep, deep), deep)] = value
            return 0

        lax.fori_loop(begin, end, some, 0)

    def weight_grads(first, count):
        def some(at, _):
            cols = pl.ds(pl.multiple_of(at * deep, deep), deep)
            grads[at, :, : 2 * ff] = dot_tn(held[:, cols], dgu[...]).astype(LOW)
            grads[at, :, 2 * ff :] = dot_tn(dy_all[:, cols], hidden[...]).astype(LOW)
            return 0

        lax.fori_loop(first, first + count, some, 0)

    back = RingSum(back_part, term, out_buf, in_buf, local, ranks, sems[2], sems[3], right, left)
    out = RingSum(out_part, term, y_out, y_in, local, ranks, sems[4], sems[5], right, left)
    for step in range(1, half + 1):
        back.compute(step)
        back.launch(step)
        out.compute(step)
        out.launch(step)
        made, passed, summed = (((0, 1), (2,), (3,), ()), ((), (0, 1), (2,), (3,)), ((), (), (0, 1), (2,)))
        for piece in (pieces[at] for at in made[step - 1]):
            weight_grads(piece.begin, piece.count)
            piece.first()
        for at in passed[step - 1]:
            pieces[at].second()
        for at in summed[step - 1]:
            pieces[at].third()
    back.compute(half + 1)
    loads[2].wait()
    back.arrive_last()

    def finish_back(at, _):
        begin = pl.multiple_of(at * 32, 32)
        rows = pl.ds(begin, 32)
        value = resid[rows]
        inv = rows_scaled(value)[1]
        grad = back.last(begin, 32)
        full = out_grad[rows].astype(jnp.float32) + rows_scaled_back(value, inv, grad)
        dresid[rows] = full
        dresid_low[rows] = full.astype(LOW)
        return 0

    lax.fori_loop(0, local // 32, finish_back, 0)
    out.compute(half + 1)
    out.arrive_last()

    def finish_out(at, _):
        begin = pl.multiple_of(at * 32, 32)
        rows = pl.ds(begin, 32)
        block_out[rows] = (resid[rows] + out.last(begin, 32)).astype(LOW)
        return 0

    lax.fori_loop(0, local // 32, finish_out, 0)
    ring.finish()
    pieces[3].third()
    back.finish()
    out.finish()
    for piece in pieces:
        piece.finish()


def back_kernel(
    ranks, kv_heads, tokens, dresid_low, query_gain, key_gain, own_out, first_in_in, block_in,
    qkv_in, cos_in, sin_in, q_in, k_in, v_in, prob_in, dresid_in, mlp_own, out_all,
    tokens_grad, gains, out_grad, mlp_sums, attn_sums,
    grads, from_core, from_y, own_grads, query_gain_grad, key_gain_grad,
    tile, tiles_in, tile_sum, tile_sums_in, dob, dout, dk, dv, dqkv,
    first_in, attn_block, qkv, cosv, sinv, q_low, k_low, v_low, prob, dresid, term, out_buf, in_buf,
    o_grads, o_core, o_y, o_own, o_term, o_out, o_in, *sems,
):
    local, width = tokens.shape
    rows = local * ranks
    half = ranks // 2
    size = cosv.shape[1]
    heads = q_low.shape[0]
    share = heads // kv_heads
    scale = 1.0 / math.sqrt(size)
    cols = (heads + 2 * kv_heads) * size
    deep = attn_block.shape[1]
    o_cols = heads * size
    right, left = neighbours(ranks)
    seq, dp = lax.axis_index("seq"), lax.axis_index("dp")
    own = mlp_own.shape[1]
    copies = lax.axis_size("dp")
    row = functools.partial(block_row, local=local, ranks=ranks)
    place = ring_place(seq, ranks)
    out_piece = Reduce(o_grads, o_core, o_y, o_own, own, 0, ranks, pl.ds(0, width), sems[4:6])
    qkv_piece = Reduce(grads, from_core, from_y, own_grads, own, 0, ranks, pl.ds(0, cols), sems[6:8])
    third = mlp_own.shape[2] // 3
    mlp_ways = [
        Deliver(mlp_own, mlp_sums, pl.ds(at * third, third), ranks, [*sems[8:11], *sems[22:28]][3 * at : 3 * at + 3])
        for at in range(3)
    ]
    dob_send, dob_recv = sems[0:2]
    qkv_way = Deliver(own_grads, attn_sums, pl.ds(0, cols), ranks, sems[14:17])
    peers = [(lax.rem(seq + step, ranks), dp) for step in range(1, ranks)]
    peers += [(seq, lax.rem(dp + step, copies)) for step in range(1, copies)]
    knock(peers)
    local_sems = sems[21]
    loads = {}
    for at, (name, src, dst) in enumerate(
        (
            ("out", out_all, o_grads), ("block", block_in, attn_block), ("v", v_in, v_low),
            ("prob", prob_in, prob), ("k", k_in, k_low), ("q", q_in, q_low), ("cos", cos_in, cosv),
            ("sin", sin_in, sinv), ("qkv", qkv_in, qkv), ("first", first_in_in, first_in),
            ("dresid", dresid_in, dresid),
        )
    ):
        loads[name] = move(src, dst, local_sems.at[at])
    answered(peers)
    loads["out"].wait()

    def columns_of(rank):
        return pl.ds(pl.multiple_of(rank * o_cols, o_cols), o_cols)

    def owner(rel):
        return ring_seq(lax.rem(place + rel, ranks), ranks)

    def exchange(rel):
        to = owner(rel)
        return push(
            dob.at[:, columns_of(to)], dout.at[pl.ds(row(0), local)], dob_send.at[rel], dob_recv.at[rel], (to, dp)
        )

    def project(rel):
        some = columns_of(owner(rel))
        dob[:, some] = dot_nn(dresid_low[...], o_grads[:, :, some].reshape(width, o_cols)).astype(LOW)

    for rel in (*ring_order(ranks)[1:][::-1], 0):
        project(rel)
        if rel:
            exchange(rel).start()
    dout[pl.ds(row(0), local)] = dob[:, columns_of(seq)]
    mlp_ways[0].start()

    def out_grads(at, _):
        some_cols = pl.ds(pl.multiple_of(at * deep, deep), deep)
        o_grads[at] = dot_tn(dresid_low[:, some_cols], own_out[...]).astype(LOW)
        return 0

    lax.fori_loop(0, ranks, out_grads, 0)
    out_piece.first()
    for rel in range(1, ranks):
        exchange(rel).wait_recv()
    for name in ("v", "prob", "k", "q", "cos", "sin", "qkv"):
        loads[name].wait()
    tall = rows // half
    query_gain_grad[...] = jnp.zeros_like(query_gain_grad)
    key_gain_grad[...] = jnp.zeros_like(key_gain_grad)

    def unrotated(grad, column, rows_at, gain, gain_grad_ref):
        grad = grad * cosv[rows_at] - turn(grad) * sinv[rows_at]
        value = qkv[rows_at, column * size : (column + 1) * size]
        normal, inv = rows_scaled(value)
        gain_grad_ref[...] += jnp.sum(grad * normal, 0, keepdims=True)
        back = rows_scaled_back(value, inv, grad * gain[...])
        dqkv[rows_at, column * size : (column + 1) * size] = back.astype(LOW)

    for head in range(heads):
        group = head // share

        def one(piece, _):
            rows_at = pl.ds(pl.multiple_of(piece * tall, tall), tall)
            weight = prob[head, rows_at]
            grad = dout[rows_at, head * size : (head + 1) * size]
            dprob = dot_nt(grad, v_low[group])
            full = weight.astype(jnp.float32)
            delta = jnp.sum(full * dprob, -1, keepdims=True)
            dscore = (full * (dprob - delta)).astype(LOW)
            dq = dot_nn(dscore, k_low[group]) * scale
            dk_add = dot_tn(dscore, q_low[head, rows_at]) * scale
            dv_add = dot_tn(weight, grad)
            dk[group] += dk_add
            dv[group] += dv_add
            unrotated(dq, head, rows_at, query_gain, query_gain_grad)
            return 0

        if head % share == 0:
            dk[group] = jnp.zeros_like(dk[group])
            dv[group] = jnp.zeros_like(dv[group])
        lax.fori_loop(0, half, one, 0)
        if head == 0:
            out_piece.second()
            mlp_ways[1].start()
    for group in range(kv_heads):
        def one_key(piece, _):
            rows_at = pl.ds(pl.multiple_of(piece * tall, tall), tall)
            unrotated(dk[group, rows_at], heads + group, rows_at, key_gain, key_gain_grad)
            at = (heads + kv_heads + group) * size
            dqkv[rows_at, at : at + size] = dv[group, rows_at].astype(LOW)
            return 0

        lax.fori_loop(0, half, one_key, 0)

    def part(rels, begin, end):
        def some(at, _):
            value = dot_nt(block_rows(dqkv, rels, local, ranks), attn_block[at])
            term[: len(rels) * local, pl.ds(pl.multiple_of(at * deep, deep), deep)] = value
            return 0

        lax.fori_loop(begin, end, some, 0)

    def qkv_grads(at, _):
        some_cols = pl.ds(pl.multiple_of(at * deep, deep), deep)
        grads[at] = dot_tn(first_in[:, some_cols], dqkv[...]).astype(LOW)
        return 0

    def to_ranks(step):
        peer = lax.rem(seq + step, ranks)
        return push(tile, tiles_in.at[seq], sems[17].at[step], sems[18].at[step], (peer, dp))

    def to_copies(step):
        peer = lax.rem(dp + step, copies)
        return push(
            tile_sum, tile_sums_in.at[dp], sems[19].at[step], sems[20].at[step], (seq, peer)
        )

    tile[0:1] = query_gain_grad[...]
    tile[1:2] = key_gain_grad[...]
    tile[2:] = jnp.zeros((tile.shape[0] - 2, size), jnp.float32)
    for step in range(1, ranks):
        to_ranks(step).start()
    tiles_in[seq] = tile[...]
    mlp_ways[2].start()
    loads["block"].wait()

    def out_part(rels, begin, end):
        for at, rel in enumerate(rels):
            o_term[at * own : (at + 1) * own] = o_own[owner(rel)].astype(jnp.float32)

    out_total = RingSum(out_part, o_term, o_out, o_in, own, ranks, sems[30], sems[31], right, left)
    totals = two_sums(part, term, out_buf, in_buf, local, ranks, [*sems[2:4], *sems[28:30]], right, left)
    for step in range(1, half + 1):
        for total in totals:
            total.compute(step)
            total.launch(step)
        if step == 1:
            loads["first"].wait()
            lax.fori_loop(0, ranks, qkv_grads, 0)
            qkv_piece.first()
        if step == 2:
            qkv_piece.second()
            for other in range(1, ranks):
                to_ranks(other).wait_recv()
            tile_sum[...] = jnp.sum(tiles_in[...], 0)
            for other in range(1, copies):
                to_copies(other).start()
            tile_sums_in[dp] = tile_sum[...]
        if step == half - 1:
            for other in range(1, copies):
                to_copies(other).wait_recv()
            gains[...] = jnp.sum(tile_sums_in[...], 0)
            qkv_piece.third()
            qkv_way.start()
    out_piece.third()
    for step in range(1, half + 1):
        out_total.compute(step)
        out_total.launch(step)
    for total in totals:
        total.compute(half + 1)
    loads["dresid"].wait()
    for total in totals:
        total.arrive_last()

    def last(at, _):
        begin = pl.multiple_of(at * 32, 32)
        rows_at = pl.ds(begin, 32)
        value = tokens[rows_at].astype(jnp.float32)
        inv = rows_scaled(value)[1]
        grad = jnp.concatenate([total.last(begin, 32) for total in totals], 1)
        tokens_grad[rows_at] = dresid[rows_at] + rows_scaled_back(value, inv, grad)
        return 0

    lax.fori_loop(0, local // 32, last, 0)
    out_total.compute(half + 1)
    out_total.arrive_last()
    out_grad[...] = out_total.last(0, own)
    for step in range(1, ranks):
        to_ranks(step).wait_send()
    for step in range(1, copies):
        to_copies(step).wait_send()
    out_total.finish()
    for rel in range(1, ranks):
        exchange(rel).wait_send()
    for total in totals:
        total.finish()
    out_piece.finish()
    qkv_piece.finish()
    for way in mlp_ways:
        way.finish()
    qkv_way.finish()


def leave_kernel(
    attn_sums, mlp_sums, attn_gain, mlp_gain, w_query, w_key, w_value, w_gate, w_up,
    query_out, key_out, value_out, gate_out, up_out, down_out, attn_out, mlp_out,
):
    own = attn_gain.shape[1]
    same = lax.broadcasted_iota(jnp.int32, (own, own), 0) == lax.broadcasted_iota(jnp.int32, (own, own), 1)

    @pl.when(pl.program_id(0) == 0)
    def _():
        attn_out[...] = jnp.zeros_like(attn_out)
        mlp_out[...] = jnp.zeros_like(mlp_out)

    for sums, gain, gain_out, parts in (
        (attn_sums, attn_gain, attn_out, ((query_out, w_query), (key_out, w_key), (value_out, w_value))),
        (mlp_sums, mlp_gain, mlp_out, ((gate_out, w_gate), (up_out, w_up), (down_out, None))),
    ):
        scale = jnp.sum(jnp.where(same, gain[...], 0.0), 1, keepdims=True)
        at = 0
        for out, weight in parts:
            value = sums[0, :, at : at + out.shape[1]].astype(jnp.float32)
            at += out.shape[1]
            if weight is None:
                out[...] = value
                continue
            out[...] = value * scale
            inner = jnp.sum(value * weight[...].astype(jnp.float32), 1, keepdims=True)
            gain_out[...] += jnp.sum(jnp.where(same, inner, 0.0), 0, keepdims=True)


VM = pl.BlockSpec(memory_space=pltpu.VMEM)
SM = pl.BlockSpec(memory_space=pltpu.SMEM)
ANY = pl.BlockSpec(memory_space=pl.ANY)


def call(kernel, number, ins, outs, scratch, operands):
    return pl.pallas_call(
        kernel,
        out_shape=[jax.ShapeDtypeStruct(shape, dtype) for shape, dtype, _ in outs],
        in_specs=ins,
        out_specs=[spec for _, _, spec in outs],
        scratch_shapes=scratch,
        compiler_params=pltpu.CompilerParams(
            collective_id=number, has_side_effects=True, vmem_limit_bytes=LIMIT
        ),
    )(*operands)


def columns_body(
    tokens,
    out_grad,
    span_order,
    doc_starts,
    w_query,
    w_key,
    w_value,
    w_output,
    attn_gain,
    query_gain,
    key_gain,
    w_gate,
    w_up,
    w_down,
    mlp_gain,
):
    ranks = lax.axis_size("seq")
    copies = lax.axis_size("dp")
    _, local, width = tokens.shape
    rows = local * ranks
    size = query_gain.shape[0]
    kv_heads = w_key.shape[1] // size // ranks
    heads = w_query.shape[1] // size // ranks
    q_cols, kv_cols = heads * size, kv_heads * size
    qkv_cols = q_cols + 2 * kv_cols
    ff = w_gate.shape[1] // ranks
    own = width // (ranks * copies)
    deep = own * copies
    half = ranks // 2
    f32, i32 = jnp.float32, jnp.int32
    exponents = np.arange(size) % (size // 2) * (-2.0 / size * math.log(1000000.0))
    freqs = jnp.asarray(np.exp(exponents)[None], f32)
    q_gain, k_gain = query_gain[None], key_gain[None]
    (
        resid, second, cosv, sinv, q_low, k_low, v_low, own_out, first_in, qkv, attn_block, dy_all, prob, mlp_block,
        out_all,
    ) = call(
        functools.partial(first_kernel, ranks, kv_heads),
        1,
        [SM, SM] + [VM] * 11 + [ANY] * 3,
        [
            ((local, width), f32, VM),
            ((local, width), LOW, VM),
            ((rows, size), f32, VM),
            ((rows, size), f32, VM),
            ((heads, rows, size), LOW, VM),
            ((kv_heads, rows, size), LOW, VM),
            ((kv_heads, rows, size), LOW, VM),
            ((local, q_cols * ranks), LOW, VM),
            ((rows, width), LOW, ANY),
            ((rows, qkv_cols), f32, ANY),
            ((ranks, deep, qkv_cols), LOW, ANY),
            ((rows, width), LOW, ANY),
            ((heads, rows, rows), LOW, ANY),
            ((ranks, deep, 3 * ff), LOW, ANY),
            ((ranks, deep, q_cols * ranks), LOW, ANY),
        ],
        [
            pltpu.VMEM((rows, width), LOW),
            pltpu.VMEM((rows, width), LOW),
            pltpu.VMEM((rows, qkv_cols), f32),
            pltpu.VMEM((ranks, deep, qkv_cols), LOW),
            pltpu.VMEM((ranks, own, qkv_cols), LOW),
            pltpu.VMEM((ranks, own, 3 * ff), LOW),
        ]
        + [pltpu.VMEM((own, ff * ranks), LOW)] * 3
        + [
            pltpu.VMEM((rows, width), LOW),
            pltpu.VMEM((heads, rows, rows), LOW),
            pltpu.VMEM((rows, 1), i32),
            pltpu.VMEM((rows, 1), i32),
            pltpu.VMEM((1, rows), i32),
            pltpu.VMEM((rows, q_cols), LOW),
            pltpu.VMEM((ranks, deep, q_cols * ranks), LOW),
        ]
        + ring_sems(ranks)
        + [pltpu.SemaphoreType.DMA((ranks,))] * 2
        + line_sems(ranks)
        + whole_sems(ranks)[:4]
        + spread_sems(ranks) * 4
        + [pltpu.SemaphoreType.DMA((heads * half + 8,))]
        + whole_sems(ranks)[4:],
        (
            span_order, doc_starts, tokens[0], out_grad[0], freqs, attn_gain[None], mlp_gain[None], q_gain, k_gain,
            w_query, w_key, w_value, w_output, w_gate, w_up, w_down,
        ),
    )
    block_out, dresid, dresid_low, mlp_own = call(
        functools.partial(mlp_kernel, ranks),
        2,
        [VM, VM, ANY, ANY, ANY],
        [
            ((local, width), LOW, VM),
            ((local, width), f32, VM),
            ((local, width), LOW, VM),
            ((ranks, own, 3 * ff), LOW, VM),
        ],
        [pltpu.VMEM((ranks, deep, 3 * ff), LOW)]
        + reduce_bufs(ranks, own, 3 * ff)
        + [
            pltpu.VMEM((rows, width), LOW),
            pltpu.VMEM((ranks, deep, 3 * ff), LOW),
            pltpu.VMEM((rows, ff), LOW),
            pltpu.VMEM((rows, 2 * ff), LOW),
            pltpu.VMEM((local, width), f32),
            pltpu.VMEM((rows, width), LOW),
        ]
        + sum_bufs(local, ranks, width)
        + sum_bufs(local, ranks, width)[1:]
        + [pltpu.SemaphoreType.DMA((3,))]
        + ring_sems(ranks) * 3
        + reduce_sems() * 4,
        (second, out_grad[0], resid, dy_all, mlp_block),
    )
    tokens_grad, gains, wo_grad, mlp_sums, attn_sums = call(
        functools.partial(back_kernel, ranks, kv_heads),
        3,
        [VM] * 5 + [ANY] * 12,
        [
            ((local, width), f32, VM),
            ((8, size), f32, VM),
            ((own, q_cols * ranks), f32, VM),
            ((ranks, own, 3 * ff), LOW, ANY),
            ((ranks, own, qkv_cols), LOW, VM),
        ],
        [pltpu.VMEM((ranks, deep, qkv_cols), LOW)]
        + reduce_bufs(ranks, own, qkv_cols)
        + [
            pltpu.VMEM((ranks, own, qkv_cols), LOW),
            pltpu.VMEM((1, size), f32),
            pltpu.VMEM((1, size), f32),
            pltpu.VMEM((8, size), f32),
            pltpu.VMEM((ranks, 8, size), f32),
            pltpu.VMEM((8, size), f32),
            pltpu.VMEM((copies, 8, size), f32),
            pltpu.VMEM((local, q_cols * ranks), LOW),
            pltpu.VMEM((rows, q_cols), LOW),
            pltpu.VMEM((kv_heads, rows, size), f32),
            pltpu.VMEM((kv_heads, rows, size), f32),
            pltpu.VMEM((rows, qkv_cols), LOW),
            pltpu.VMEM((rows, width), LOW),
            pltpu.VMEM((ranks, deep, qkv_cols), LOW),
            pltpu.VMEM((rows, qkv_cols), f32),
            pltpu.VMEM((rows, size), f32),
            pltpu.VMEM((rows, size), f32),
            pltpu.VMEM((heads, rows, size), LOW),
            pltpu.VMEM((kv_heads, rows, size), LOW),
            pltpu.VMEM((kv_heads, rows, size), LOW),
            pltpu.VMEM((heads, rows, rows), LOW),
            pltpu.VMEM((local, width), f32),
        ]
        + sum_bufs(local, ranks, width)
        + [pltpu.VMEM((ranks, deep, q_cols * ranks), LOW)]
        + reduce_bufs(ranks, own, q_cols * ranks)
        + [pltpu.VMEM((ranks, own, q_cols * ranks), LOW)]
        + sum_bufs(own, ranks, q_cols * ranks)
        + [pltpu.SemaphoreType.DMA((ranks,))] * 2
        + ring_sems(ranks)
        + reduce_sems() * 2
        + deliver_sems(ranks) * 3
        + [pltpu.SemaphoreType.DMA((ranks,))] * 2
        + [pltpu.SemaphoreType.DMA((copies,))] * 2
        + [pltpu.SemaphoreType.DMA((11,))]
        + deliver_sems(ranks) * 2
        + ring_sems(ranks) * 2,
        (
            tokens[0], dresid_low, q_gain, k_gain, own_out, first_in, attn_block, qkv, cosv, sinv, q_low, k_low,
            v_low, prob, dresid, mlp_own, out_all,
        ),
    )
    whole = pl.BlockSpec((1, own), lambda at: (0, 0))
    each = (q_cols, kv_cols, kv_cols, ff, ff, ff)
    columns = [pl.BlockSpec((own, cols), lambda at: (0, at)) for cols in each]
    *grads, dga, dgm = pl.pallas_call(
        leave_kernel,
        grid=(ranks,),
        out_shape=[jax.ShapeDtypeStruct((own, cols * ranks), f32) for cols in each]
        + [jax.ShapeDtypeStruct((1, own), f32)] * 2,
        in_specs=[
            pl.BlockSpec((1, own, qkv_cols), lambda at: (at, 0, 0)),
            pl.BlockSpec((1, own, 3 * ff), lambda at: (at, 0, 0)),
            whole,
            whole,
            *columns[:3],
            *columns[3:5],
        ],
        out_specs=columns + [whole, whole],
    )(attn_sums, mlp_sums, attn_gain[None], mlp_gain[None], w_query, w_key, w_value, w_gate, w_up)
    return (
        block_out[None], tokens_grad[None], *grads[:3], wo_grad, dga[0], gains[0], gains[1], *grads[3:], dgm[0],
    )


def body(*args):
    tokens, w_key, query_gain = args[0], args[5], args[9]
    groups = w_key.shape[1] // query_gain.shape[0]
    ranks = lax.axis_size("seq")
    if tokens.shape[0] == 1 and ranks % 2 == 0 and groups % ranks == 0 and lax.axis_size("dp") == 4:
        return columns_body(*args)
    return gathered_body(*args)


def solution(mesh):
    return jax.shard_map(
        body,
        mesh=mesh,
        in_specs=(
            P("dp", "seq", None),
            P("dp", "seq", None),
            P(),
            P("dp", None),
            P(("seq", "dp"), None),
            P(("seq", "dp"), None),
            P(("seq", "dp"), None),
            P(("seq", "dp"), None),
            P(("seq", "dp")),
            P(),
            P(),
            P(("seq", "dp"), None),
            P(("seq", "dp"), None),
            P(("seq", "dp"), None),
            P(("seq", "dp")),
        ),
        out_specs=(
            P("dp", "seq", None),
            P("dp", "seq", None),
            P(("seq", "dp"), None),
            P(("seq", "dp"), None),
            P(("seq", "dp"), None),
            P(("seq", "dp"), None),
            P(("seq", "dp")),
            P(),
            P(),
            P(("seq", "dp"), None),
            P(("seq", "dp"), None),
            P(("seq", "dp"), None),
            P(("seq", "dp")),
        ),
        check_vma=False,
    )
```

```python
import functools
import math

import jax
import jax.numpy as jnp
import numpy as np
from jax import lax
from jax.experimental import pallas as pl
from jax.experimental.pallas import tpu as pltpu
from jax.sharding import PartitionSpec as P

EPS = 1e-06
NEG = -1e30


def normed(v, gain):
    scale_inv = lax.rsqrt(jnp.mean(v * v, -1, keepdims=True) + EPS)
    return (v * scale_inv * gain, scale_inv)


def norm_back(v, scale_inv, gain, grad):
    scaled = grad * gain
    inner = jnp.mean(scaled * v, -1, keepdims=True)
    dv = scale_inv * scaled - v * scale_inv * scale_inv * scale_inv * inner
    dgain = jnp.sum((grad * v * scale_inv).reshape(-1, v.shape[-1]), 0)
    return (dv, dgain)


def rotary(pos, width):
    half = width // 2
    freqs = jnp.exp(jnp.arange(half, dtype=jnp.float32) * (-2.0 / width * math.log(1000000.0)))
    angle = pos.astype(jnp.float32)[:, None] * freqs[None, :]
    return (jnp.cos(angle)[:, None, :], jnp.sin(angle)[:, None, :])


def rotate(v, cosv, sinv):
    half = v.shape[-1] // 2
    first, second = (v[..., :half], v[..., half:])
    return jnp.concatenate([first * cosv - second * sinv, second * cosv + first * sinv], -1)


def rotate_back(grad, cosv, sinv):
    half = grad.shape[-1] // 2
    first, second = (grad[..., :half], grad[..., half:])
    return jnp.concatenate([first * cosv + second * sinv, second * cosv - first * sinv], -1)


def place(order, begin, count, span):
    rows = begin + jnp.arange(count, dtype=jnp.int32)
    slots = rows // span
    picked = slots[:, None] == jnp.arange(order.shape[0], dtype=jnp.int32)[None, :]
    return jnp.sum(jnp.where(picked, order[None, :], 0), -1) * span + rows % span


def doc_of(starts, pos):
    return jnp.sum((starts[:, None, :] <= pos[None, :, None]).astype(jnp.int32), -1)


def gathered_body(
    tokens,
    out_grad,
    span_order,
    doc_starts,
    w_query,
    w_key,
    w_value,
    w_output,
    attn_gain,
    query_gain,
    key_gain,
    w_gate,
    w_up,
    w_down,
    mlp_gain,
):
    seqs, local, width = tokens.shape
    span = local // 2
    head_size = query_gain.shape[0]
    kv_heads = w_key.shape[1] // head_size
    heads = w_query.shape[1] // head_size
    share = heads // kv_heads
    kv_width = kv_heads * head_size
    ff_width = w_gate.shape[1]
    scale = 1.0 / math.sqrt(head_size)
    total_rows = seqs * local
    own_rows = width // lax.axis_size(("seq", "dp"))
    qpos = place(span_order, lax.axis_index("seq") * local, local, span)
    qdoc = doc_of(doc_starts, qpos)
    cosv, sinv = rotary(qpos, head_size)

    def gather_attn():
        return (
            lax.all_gather(w_query, ("seq", "dp"), axis=0, tiled=True),
            lax.all_gather(w_key, ("seq", "dp"), axis=0, tiled=True),
            lax.all_gather(w_value, ("seq", "dp"), axis=0, tiled=True),
            lax.all_gather(w_output, ("seq", "dp"), axis=0, tiled=True),
            lax.all_gather(
                attn_gain.astype(jnp.bfloat16), ("seq", "dp"), axis=0, tiled=True
            ).astype(attn_gain.dtype),
        )

    def gather_mlp():
        return (
            lax.all_gather(w_gate, ("seq", "dp"), axis=0, tiled=True),
            lax.all_gather(w_up, ("seq", "dp"), axis=0, tiled=True),
            lax.all_gather(w_down, ("seq", "dp"), axis=0, tiled=True),
            lax.all_gather(mlp_gain.astype(jnp.bfloat16), ("seq", "dp"), axis=0, tiled=True).astype(
                mlp_gain.dtype
            ),
        )

    x_rows = tokens.astype(jnp.float32).reshape(total_rows, width)
    wq_all, wk_all, wv_all, wo_all, ga_all = gather_attn()
    first_norm, first_inv = normed(x_rows, ga_all)
    first_in = first_norm.astype(jnp.bfloat16)
    q_raw = jnp.dot(first_in, wq_all, preferred_element_type=jnp.float32).reshape(
        seqs, local, heads, head_size
    )
    k_raw = jnp.dot(first_in, wk_all, preferred_element_type=jnp.float32).reshape(
        seqs, local, kv_heads, head_size
    )
    v_low = (
        jnp.dot(first_in, wv_all, preferred_element_type=jnp.float32)
        .astype(jnp.bfloat16)
        .reshape(seqs, local, kv_heads, head_size)
    )
    q_normed, q_inv = normed(q_raw, query_gain)
    k_normed, k_inv = normed(k_raw, key_gain)
    q_low = rotate(q_normed, cosv, sinv).astype(jnp.bfloat16)
    k_low = rotate(k_normed, cosv, sinv).astype(jnp.bfloat16)
    q_group = q_low.reshape(seqs, local, kv_heads, share, head_size)

    def scores(piece_key, start):
        count = piece_key.shape[1]
        kpos = place(span_order, start, count, span)
        kdoc = doc_of(doc_starts, kpos)
        visible = (qdoc[:, :, None] == kdoc[:, None, :]) & (
            kpos[None, None, :] <= qpos[None, :, None]
        )
        raw = (
            jnp.einsum("sqgjd,skgd->sgjqk", q_group, piece_key, preferred_element_type=jnp.float32)
            * scale
        )
        return (raw, visible[:, None, None])

    start_top = jnp.full((seqs, kv_heads, share, local), NEG, jnp.float32)
    piece = (
        lax.all_gather(k_low, "seq", axis=1, tiled=True),
        lax.all_gather(v_low, "seq", axis=1, tiled=True),
    )
    top = start_top
    raw, visible = scores(piece[0], jnp.int32(0))
    raw = jnp.where(visible, raw, NEG)
    new_top = jnp.maximum(top, jnp.max(raw, -1))
    weights = jnp.where(visible, jnp.exp(raw - new_top[..., None]), 0.0)
    total = jnp.sum(weights, -1)
    summed = jnp.einsum(
        "sgjqk,skgd->sgjqd",
        weights.astype(jnp.bfloat16),
        piece[1],
        preferred_element_type=jnp.float32,
    )
    top, total, summed = (new_top, total, summed)
    log_total = top + jnp.log(total)
    attn_vals = summed / total[..., None]
    out_low = (
        jnp.transpose(attn_vals, (0, 3, 1, 2, 4))
        .reshape(total_rows, heads * head_size)
        .astype(jnp.bfloat16)
    )
    resid = x_rows + jnp.einsum("nh,dh->nd", out_low, wo_all, preferred_element_type=jnp.float32)
    wg_all, wu_all, wd_all, gm_all = gather_mlp()
    second_norm, second_inv = normed(resid, gm_all)
    second_in = second_norm.astype(jnp.bfloat16)
    gate = jnp.dot(second_in, wg_all, preferred_element_type=jnp.float32)
    upper = jnp.dot(second_in, wu_all, preferred_element_type=jnp.float32)
    sigma = jax.nn.sigmoid(gate)
    act = gate * sigma
    hidden = (act * upper).astype(jnp.bfloat16)
    result = resid + jnp.einsum("nf,df->nd", hidden, wd_all, preferred_element_type=jnp.float32)
    block_out = result.astype(jnp.bfloat16).reshape(seqs, local, width)
    grad_low = out_grad.reshape(total_rows, width)
    wg_all, wu_all, wd_all, gm_all = gather_mlp()
    dmid = jnp.einsum("nd,df->nf", grad_low, wd_all, preferred_element_type=jnp.float32)
    dgate = (dmid * upper * sigma * (1.0 + gate * (1.0 - sigma))).astype(jnp.bfloat16)
    dupper = (dmid * act).astype(jnp.bfloat16)
    left = second_in
    outer = grad_low
    mlp_sums = lax.psum_scatter(
        jnp.concatenate(
            [
                jnp.einsum("nd,nf->df", left, dgate, preferred_element_type=jnp.float32),
                jnp.einsum("nd,nf->df", left, dupper, preferred_element_type=jnp.float32),
                jnp.einsum("nd,nf->df", outer, hidden, preferred_element_type=jnp.float32),
            ],
            1,
        ),
        ("seq", "dp"),
        scatter_dimension=0,
        tiled=True,
    )
    dsecond = jnp.einsum(
        "nf,df->nd", dgate, wg_all, preferred_element_type=jnp.float32
    ) + jnp.einsum("nf,df->nd", dupper, wu_all, preferred_element_type=jnp.float32)
    dresid_norm, dgm = norm_back(resid, second_inv, gm_all, dsecond)
    dresid = grad_low.astype(jnp.float32) + dresid_norm
    dresid_low = dresid.astype(jnp.bfloat16)
    wq_all, wk_all, wv_all, wo_all, ga_all = gather_attn()
    dout_low = jnp.einsum(
        "nd,dh->nh", dresid_low, wo_all, preferred_element_type=jnp.float32
    ).astype(jnp.bfloat16)
    dout_group = dout_low.reshape(seqs, local, kv_heads, share, head_size)
    delta = jnp.sum(jnp.transpose(dout_group.astype(jnp.float32), (0, 2, 3, 1, 4)) * attn_vals, -1)
    piece = (
        lax.all_gather(k_low, "seq", axis=1, tiled=True),
        lax.all_gather(v_low, "seq", axis=1, tiled=True),
    )
    count = piece[0].shape[1]
    raw, visible = scores(piece[0], jnp.int32(0))
    prob = jnp.where(visible, jnp.exp(raw - log_total[..., None]), 0.0)
    dprob = jnp.einsum(
        "sqgjd,skgd->sgjqk", dout_group, piece[1], preferred_element_type=jnp.float32
    )
    dscore = (prob * (dprob - delta[..., None])).astype(jnp.bfloat16)
    dq_sum = jnp.einsum("sgjqk,skgd->sqgjd", dscore, piece[0], preferred_element_type=jnp.float32)
    dk_part = (
        jnp.einsum("sgjqk,sqgjd->skgd", dscore, q_group, preferred_element_type=jnp.float32) * scale
    )
    dv_part = jnp.einsum(
        "sgjqk,sqgjd->skgd",
        prob.astype(jnp.bfloat16),
        dout_group,
        preferred_element_type=jnp.float32,
    )
    joined = jnp.concatenate(
        [dk_part.reshape(seqs, count, kv_width), dv_part.reshape(seqs, count, kv_width)], -1
    )
    buffer = joined
    dq_sum, buffer = (dq_sum, buffer)
    key_sums = lax.psum_scatter(
        buffer.astype(jnp.bfloat16), "seq", scatter_dimension=1, tiled=True
    ).astype(jnp.float32)
    dq_rot = (dq_sum * scale).reshape(seqs, local, heads, head_size)
    dq_raw, dgq = norm_back(q_raw, q_inv, query_gain, rotate_back(dq_rot, cosv, sinv))
    dk_rot = key_sums[..., :kv_width].reshape(seqs, local, kv_heads, head_size)
    dk_raw, dgk = norm_back(k_raw, k_inv, key_gain, rotate_back(dk_rot, cosv, sinv))
    dq_low = dq_raw.reshape(total_rows, heads * head_size).astype(jnp.bfloat16)
    dk_low = dk_raw.reshape(total_rows, kv_width).astype(jnp.bfloat16)
    dv_low = key_sums[..., kv_width:].reshape(total_rows, kv_width).astype(jnp.bfloat16)
    left = first_in
    outer = dresid_low
    attn_sums = lax.psum_scatter(
        jnp.concatenate(
            [
                jnp.einsum("nd,nh->dh", left, dq_low, preferred_element_type=jnp.float32),
                jnp.einsum("nd,nh->dh", left, dk_low, preferred_element_type=jnp.float32),
                jnp.einsum("nd,nh->dh", left, dv_low, preferred_element_type=jnp.float32),
                jnp.einsum("nd,nh->dh", outer, out_low, preferred_element_type=jnp.float32),
            ],
            1,
        ),
        ("seq", "dp"),
        scatter_dimension=0,
        tiled=True,
    )
    dfirst = jnp.einsum("nh,dh->nd", dq_low, wq_all, preferred_element_type=jnp.float32)
    dfirst = dfirst + jnp.einsum("nh,dh->nd", dk_low, wk_all, preferred_element_type=jnp.float32)
    dfirst = dfirst + jnp.einsum("nh,dh->nd", dv_low, wv_all, preferred_element_type=jnp.float32)
    dx_norm, dga = norm_back(x_rows, first_inv, ga_all, dfirst)
    tokens_grad = (dresid + dx_norm).reshape(seqs, local, width)
    dga_all, dgm_all, dgq_all, dgk_all = lax.psum((dga, dgm, dgq, dgk), ("seq", "dp"))
    offset = lax.axis_index(("seq", "dp")) * own_rows
    attn_gain_grad = lax.dynamic_slice_in_dim(dga_all, offset, own_rows, 0)
    mlp_gain_grad = lax.dynamic_slice_in_dim(dgm_all, offset, own_rows, 0)
    q_cols = heads * head_size
    w_query_grad = attn_sums[:, :q_cols]
    w_key_grad = attn_sums[:, q_cols : q_cols + kv_width]
    w_value_grad = attn_sums[:, q_cols + kv_width : q_cols + 2 * kv_width]
    w_output_grad = attn_sums[:, q_cols + 2 * kv_width :]
    w_gate_grad = mlp_sums[:, :ff_width]
    w_up_grad = mlp_sums[:, ff_width : 2 * ff_width]
    w_down_grad = mlp_sums[:, 2 * ff_width :]
    return (
        block_out,
        tokens_grad,
        w_query_grad,
        w_key_grad,
        w_value_grad,
        w_output_grad,
        attn_gain_grad,
        dgq_all,
        dgk_all,
        w_gate_grad,
        w_up_grad,
        w_down_grad,
        mlp_gain_grad,
    )


LOW = jnp.bfloat16
MESH = pl.DeviceIdType.MESH
LIMIT = 60 * 2**20


def ring_order(ranks):
    half = ranks // 2
    order = [0]
    for step in range(1, half):
        order += [step, ranks - step]
    return order + [half]


def ring_place(seq, ranks):
    z, x = lax.div(seq, 2), lax.rem(seq, 2)
    return z + x * (ranks - 1 - 2 * z)


def ring_seq(place, ranks):
    half = ranks // 2
    x, z = lax.div(place, half), lax.rem(place, half)
    return 2 * (z + x * (half - 1 - 2 * z)) + x


def neighbours(ranks):
    seq, dp = lax.axis_index("seq"), lax.axis_index("dp")
    at = ring_place(seq, ranks)
    right = ring_seq(lax.rem(at + 1, ranks), ranks)
    left = ring_seq(lax.rem(at + ranks - 1, ranks), ranks)
    return (right, dp), (left, dp)


def knock(devices):
    barrier = pltpu.get_barrier_semaphore()
    for device in devices:
        pl.semaphore_signal(barrier, inc=1, device_id=device, device_id_type=MESH)


def answered(devices):
    pl.semaphore_wait(pltpu.get_barrier_semaphore(), len(devices))


def move(src, dst, sem):
    copy = pltpu.make_async_copy(src, dst, sem)
    copy.start()
    return copy


def push(src, dst, send, recv, device):
    return pltpu.make_async_remote_copy(
        src_ref=src, dst_ref=dst, send_sem=send, recv_sem=recv, device_id=device, device_id_type=MESH
    )


def dot_nn(left, right):
    return jnp.dot(left, right, preferred_element_type=jnp.float32)


def dot_nt(left, right):
    return lax.dot_general(left, right, (((1,), (1,)), ((), ())), preferred_element_type=jnp.float32)


def dot_tn(left, right):
    return lax.dot_general(left, right, (((0,), (0,)), ((), ())), preferred_element_type=jnp.float32)


def block_row(rel, local, ranks):
    place = ring_place(lax.axis_index("seq"), ranks)
    return pl.multiple_of(ring_seq(lax.rem(place + rel, ranks), ranks) * local, local)


def block_rows(ref, rels, local, ranks):
    blocks = [ref[pl.ds(block_row(rel, local, ranks), local)] for rel in rels]
    return blocks[0] if len(blocks) == 1 else jnp.concatenate(blocks, 0)


def rels_of(step, ranks):
    return [rel for rel in ring_order(ranks) if min(rel, ranks - rel) == step]


class RingGather:
    def __init__(self, buf, local, ranks, send, recv, right, left, row):
        self.buf, self.sub, self.half = buf, local // 2, ranks // 2
        self.send, self.recv, self.right, self.left = send, recv, right, left
        self.ranks, self.row = ranks, row

    def copies(self, step, part):
        ways = ((0, (self.ranks - step + 1) % self.ranks, self.right), (1, step - 1, self.left))
        given = []
        for way, rel, device in ways:
            if step < self.half or way == part:
                block = self.buf.at[pl.ds(self.row(rel) + part * self.sub, self.sub)]
                at = 2 * (step - 1) + part
                given.append(push(block, block, self.send.at[way, at], self.recv.at[way, at], device))
        return given

    def start(self, step):
        for part in range(2):
            for copy in self.copies(step, part):
                copy.start()

    def advance(self, step):
        for part in range(2):
            for copy in self.copies(step, part):
                copy.wait_recv()
            if step < self.half:
                for copy in self.copies(step + 1, part):
                    copy.start()

    def finish(self):
        for step in range(1, self.half + 1):
            for part in range(2):
                for copy in self.copies(step, part):
                    copy.wait_send()


class LineGather:
    def __init__(self, buf, local, ranks, send, recv, x_send, x_recv):
        self.buf, self.local, self.length = buf, local, ranks // 2
        self.send, self.recv, self.x_send, self.x_recv = send, recv, x_send, x_recv
        self.seq, self.dp = lax.axis_index("seq"), lax.axis_index("dp")
        self.z, self.x = lax.div(self.seq, 2), lax.rem(self.seq, 2)

    def block(self, z):
        return self.buf.at[pl.ds(pl.multiple_of((2 * z + self.x) * self.local, self.local), self.local)]

    def hop(self, way, step):
        block = self.block(self.z + (step - 1 if way else 1 - step))
        to = self.seq + (-2 if way else 2)
        return push(block, block, self.send.at[way, step - 1], self.recv.at[way, step - 1], (to, self.dp))

    def sends(self, way, step):
        if way:
            return (self.z > 0) & (self.z + step <= self.length)
        return (self.z < self.length - 1) & (self.z >= step - 1)

    def comes(self, way, step):
        return self.z + step < self.length if way else self.z >= step

    def across(self, way, step):
        block = self.block(self.z + (step if way else -step))
        at = step + way * (self.length - 1)
        return push(
            block, block, self.x_send.at[at], self.x_recv.at[at], (self.seq + 1 - 2 * self.x, self.dp)
        )

    def from_x(self, way, step):
        z = self.z + (step if way else -step)
        row = pl.multiple_of((2 * z + 1 - self.x) * self.local, self.local)
        block = self.buf.at[pl.ds(row, self.local)]
        at = step + way * (self.length - 1)
        return push(
            block, block, self.x_send.at[at], self.x_recv.at[at], (self.seq + 1 - 2 * self.x, self.dp)
        )

    def start(self, step):
        for way in range(2):
            pl.when(self.sends(way, step))(lambda way=way: self.hop(way, step).start())
        self.pass_on(step - 1)

    def pass_on(self, step):
        if step == 0:
            self.across(0, 0).start()
            return
        for way in range(2):
            pl.when(self.comes(way, step))(lambda way=way: self.across(way, step).start())

    def arrive(self, step):
        for way in range(2):
            pl.when(self.comes(way, step))(lambda way=way: self.incoming(way, step).wait_recv())

    def incoming(self, way, step):
        block = self.block(self.z + (step if way else -step))
        to = self.seq + 1 - 2 * self.x
        return push(block, block, self.send.at[way, step - 1], self.recv.at[way, step - 1], (to, self.dp))

    def run(self):
        for step in range(1, self.length):
            self.advance(step)

    def advance(self, step):
        self.arrive(step)
        if step < self.length - 1:
            self.start(step + 1)
        else:
            self.pass_on(step)

    def complete(self):
        self.from_x(0, 0).wait_recv()
        for step in range(1, self.length):
            for way in range(2):
                pl.when(self.comes(way, step))(lambda way=way: self.from_x(way, step).wait_recv())

    def finish(self):
        self.across(0, 0).wait_send()
        for step in range(1, self.length):
            for way in range(2):
                pl.when(self.sends(way, step))(lambda way=way: self.hop(way, step).wait_send())
                pl.when(self.comes(way, step))(lambda way=way: self.across(way, step).wait_send())


def line_sems(ranks):
    half = ranks // 2
    return [pltpu.SemaphoreType.DMA((2, half))] * 2 + [pltpu.SemaphoreType.DMA((2 * half,))] * 2


class RingSum:
    def __init__(self, part, term, out_buf, in_buf, local, ranks, send, recv, right, left, stream=0, streams=1):
        self.part, self.term, self.out_buf, self.in_buf = part, term, out_buf, in_buf
        self.local, self.ranks, self.half = local, ranks, ranks // 2
        each = term.shape[1] // streams
        self.cols = pl.ds(stream * each, each)
        self.tiles = (stream * ranks // streams, (stream + 1) * ranks // streams)
        self.send, self.recv, self.right, self.left = send, recv, right, left

    def copies(self, step):
        rows = self.local // 2 if step == 1 else self.local
        skip = self.local // 2 if step == 1 else 0
        return [
            push(
                self.out_buf.at[way, (step - 1) % 2, pl.ds(begin, rows), self.cols],
                self.in_buf.at[way, step - 1, pl.ds(begin, rows), self.cols],
                self.send.at[way, step - 1],
                self.recv.at[way, step - 1],
                device,
            )
            for way, begin, device in ((0, 0, self.right), (1, skip, self.left))
        ]

    def compute(self, step):
        if step == 1:
            self.part([self.half], *self.tiles)
        elif step <= self.half:
            self.part(rels_of(self.half + 1 - step, self.ranks), *self.tiles)
        else:
            self.part([0], *self.tiles)

    def launch(self, step):
        local, skip = self.local, self.local // 2
        if step > 2:
            for copy in self.copies(step - 2):
                copy.wait_send()
        if step == 1:
            for way in range(2):
                rows = pl.ds(way * skip, skip)
                self.out_buf[way, 0, rows, self.cols] = self.term[rows, self.cols].astype(LOW)
        else:
            for copy in self.copies(step - 1):
                copy.wait_recv()
            for way in range(2):
                for begin, with_sum in ((0, step > 2 or way == 0), (skip, step > 2 or way == 1)):
                    value = self.term[pl.ds(way * local + begin, skip), self.cols]
                    if with_sum:
                        value = value + self.in_buf[way, step - 2, pl.ds(begin, skip), self.cols].astype(jnp.float32)
                    self.out_buf[way, (step - 1) % 2, pl.ds(begin, skip), self.cols] = value.astype(LOW)
        for copy in self.copies(step):
            copy.start()

    def last(self, begin, count):
        rows = pl.ds(begin, count)
        value = self.term[rows, self.cols] + self.in_buf[0, self.half - 1, rows, self.cols].astype(jnp.float32)
        return value + self.in_buf[1, self.half - 1, rows, self.cols].astype(jnp.float32)

    def arrive_last(self):
        for copy in self.copies(self.half):
            copy.wait_recv()

    def finish(self):
        for step in range(max(1, self.half - 1), self.half + 1):
            for copy in self.copies(step):
                copy.wait_send()


def two_sums(part, term, out_buf, in_buf, local, ranks, sems, right, left):
    return [
        RingSum(
            part, term, out_buf, in_buf, local, ranks, sems[2 * at], sems[2 * at + 1], right, left, at, 2
        )
        for at in range(2)
    ]


def ring_sems(ranks):
    return [pltpu.SemaphoreType.DMA((2, ranks)), pltpu.SemaphoreType.DMA((2, ranks))]


def sum_bufs(local, ranks, width):
    return [
        pltpu.VMEM((2 * local, width), jnp.float32),
        pltpu.VMEM((2, 2, local, width), LOW),
        pltpu.VMEM((2, ranks // 2, local, width), LOW),
    ]


def turn(v):
    return pltpu.roll(v, v.shape[-1] // 2, v.ndim - 1)


def rows_scaled(v):
    inv = lax.rsqrt(jnp.mean(v * v, -1, keepdims=True) + EPS)
    return v * inv, inv


def rows_scaled_back(v, inv, grad):
    return inv * grad - v * (inv * inv * inv * jnp.mean(grad * v, -1, keepdims=True))


class Spread:
    def __init__(self, rows, block, ranks, own, cols, sems):
        self.rows, self.block, self.ranks, self.own, self.cols = rows, block, ranks, own, cols
        self.send, self.recv, self.hop_send, self.hop_recv, self.here = sems
        self.seq, self.dp = lax.axis_index("seq"), lax.axis_index("dp")
        y, core = lax.div(self.dp, 2), lax.rem(self.dp, 2)
        self.beside, self.sibling = (1 - y) * 2 + core, y * 2 + 1 - core

    def at(self, dp):
        return pl.ds(pl.multiple_of(dp * self.own, self.own), self.own)

    def exchange(self):
        for step in range(1, self.ranks):
            peer = lax.rem(self.seq + step, self.ranks)
            yield push(
                self.rows.at[peer, :, self.cols],
                self.block.at[self.seq, self.at(self.dp), self.cols],
                self.send.at[step],
                self.recv.at[step],
                (peer, self.dp),
            )

    def keep(self):
        return pltpu.make_async_copy(
            self.rows.at[self.seq, :, self.cols],
            self.block.at[self.seq, self.at(self.dp), self.cols],
            self.here,
        )

    def hop(self, number):
        dp = self.beside if number == 2 else self.dp
        part = self.block.at[:, self.at(dp), self.cols]
        to = self.beside if number == 0 else self.sibling
        return push(part, part, self.hop_send.at[number], self.hop_recv.at[number], (self.seq, to))

    def start(self):
        self.keep().start()
        for copy in self.exchange():
            copy.start()

    def arrive(self):
        self.keep().wait()
        for copy in self.exchange():
            copy.wait_recv()

    def finish(self):
        for copy in self.exchange():
            copy.wait_send()
        for number in range(3):
            self.hop(number).wait_send()


def spread_sems(ranks):
    return [
        pltpu.SemaphoreType.DMA((ranks,)),
        pltpu.SemaphoreType.DMA((ranks,)),
        pltpu.SemaphoreType.DMA((3,)),
        pltpu.SemaphoreType.DMA((3,)),
        pltpu.SemaphoreType.DMA,
    ]


class WholeGather:
    def __init__(self, block, ranks, own, sems):
        self.block, self.ranks, self.half, self.own = block, ranks, ranks // 2, own
        self.send, self.recv, self.y_send, self.y_recv, self.core_send, self.core_recv = sems
        self.seq, self.dp = lax.axis_index("seq"), lax.axis_index("dp")
        self.right, self.left = neighbours(ranks)
        self.place = ring_place(self.seq, ranks)
        y, core = lax.div(self.dp, 2), lax.rem(self.dp, 2)
        self.beside, self.sibling = (1 - y) * 2 + core, y * 2 + 1 - core

    def at(self, rel, dp, begin, count):
        seq = ring_seq(lax.rem(self.place + rel + self.ranks, self.ranks), self.ranks)
        return self.block.at[seq, pl.ds(pl.multiple_of(dp * self.own + begin, count), count)]

    def copies(self, step):
        last = step == self.half
        rows = self.own // 2 if last else self.own
        skip = self.own // 2 if last else 0
        given = []
        for way, rel, begin, device in ((0, 1 - step, 0, self.right), (1, step - 1, skip, self.left)):
            part = self.at(rel, self.dp, begin, rows)
            given.append(push(part, part, self.send.at[way, step - 1], self.recv.at[way, step - 1], device))
        return given

    def start(self, step):
        for copy in self.copies(step):
            copy.start()

    def hops(self, step):
        for at, rel in enumerate(ring_order(self.ranks)):
            if min(rel, self.ranks - rel) == step:
                part = self.at(rel, self.dp, 0, self.own)
                yield push(part, part, self.y_send.at[at], self.y_recv.at[at], (self.seq, self.beside))
                yield push(part, part, self.core_send.at[at], self.core_recv.at[at], (self.seq, self.sibling))

    def arrive(self, step):
        for copy in self.copies(step):
            copy.wait_recv()

    def forward(self, step):
        for copy in self.hops(step):
            copy.start()

    def cross(self):
        part = self.block.at[:, pl.ds(pl.multiple_of(self.beside * self.own, self.own), self.own)]
        at = self.ranks
        return push(part, part, self.core_send.at[at], self.core_recv.at[at], (self.seq, self.sibling))

    def complete(self):
        for step in range(self.half + 1):
            for copy in self.hops(step):
                copy.wait_recv()
        self.cross().start()
        self.cross().wait_recv()

    def finish(self):
        for step in range(1, self.half + 1):
            for copy in self.copies(step):
                copy.wait_send()
        for step in range(self.half + 1):
            for copy in self.hops(step):
                copy.wait_send()
        self.cross().wait_send()


def whole_sems(ranks):
    return (
        ring_sems(ranks)
        + [pltpu.SemaphoreType.DMA((ranks,))] * 2
        + [pltpu.SemaphoreType.DMA((ranks + 1,))] * 2
    )


class Reduce:
    def __init__(self, grads, from_core, from_y, total, own, first, count, cols, sems):
        self.grads, self.from_core, self.from_y, self.total = grads, from_core, from_y, total
        self.own, self.begin, self.count, self.cols = own, first, count, cols
        self.send, self.recv = sems
        self.seq, dp = lax.axis_index("seq"), lax.axis_index("dp")
        self.y, self.core = lax.div(dp, 2), lax.rem(dp, 2)
        self.beside, self.sibling = (1 - self.y) * 2 + self.core, self.y * 2 + 1 - self.core

    def at(self, y, core):
        return pl.ds(pl.multiple_of((y * 2 + core) * self.own, self.own), self.own)

    def hop(self, number):
        some, cols = pl.ds(self.begin, self.count), self.cols
        if number == 2:
            src, dst, to = self.from_core.at[0, some, :, cols], self.from_y.at[some, :, cols], self.beside
        else:
            rows = self.at(1 - self.y if number == 0 else self.y, 1 - self.core)
            src, dst, to = self.grads.at[some, rows, cols], self.from_core.at[number, some, :, cols], self.sibling
        return push(src, dst, self.send.at[number], self.recv.at[number], (self.seq, to))

    def first(self):
        self.hop(0).start()
        self.hop(1).start()

    def second(self):
        self.hop(0).wait_recv()
        rows = self.at(1 - self.y, self.core)

        def some(at, _):
            value = self.grads[at, rows, self.cols].astype(jnp.float32)
            value = value + self.from_core[0, at, :, self.cols].astype(jnp.float32)
            self.from_core[0, at, :, self.cols] = value.astype(LOW)
            return 0

        lax.fori_loop(self.begin, self.begin + self.count, some, 0)
        self.hop(2).start()

    def third(self):
        self.hop(1).wait_recv()
        self.hop(2).wait_recv()
        rows = self.at(self.y, self.core)

        def some(at, _):
            value = self.grads[at, rows, self.cols].astype(jnp.float32)
            value = value + self.from_core[1, at, :, self.cols].astype(jnp.float32)
            value = value + self.from_y[at, :, self.cols].astype(jnp.float32)
            self.total[at, :, self.cols] = value.astype(LOW)
            return 0

        lax.fori_loop(self.begin, self.begin + self.count, some, 0)

    def finish(self):
        for number in range(3):
            self.hop(number).wait_send()


def reduce_sems():
    return [pltpu.SemaphoreType.DMA((3,)), pltpu.SemaphoreType.DMA((3,))]


def reduce_bufs(ranks, own, cols):
    return [pltpu.VMEM((2, ranks, own, cols), LOW), pltpu.VMEM((ranks, own, cols), LOW)]


class Deliver:
    def __init__(self, rows, out, cols, ranks, sems):
        self.rows, self.out, self.cols, self.ranks = rows, out, cols, ranks
        self.send, self.recv, self.here = sems
        self.seq, self.dp = lax.axis_index("seq"), lax.axis_index("dp")

    def exchange(self):
        for step in range(1, self.ranks):
            peer = lax.rem(self.seq + step, self.ranks)
            yield push(
                self.rows.at[peer, :, self.cols],
                self.out.at[self.seq, :, self.cols],
                self.send.at[step],
                self.recv.at[step],
                (peer, self.dp),
            )

    def keep(self):
        return pltpu.make_async_copy(
            self.rows.at[self.seq, :, self.cols], self.out.at[self.seq, :, self.cols], self.here
        )

    def start(self):
        self.keep().start()
        for copy in self.exchange():
            copy.start()

    def finish(self):
        self.keep().wait()
        for copy in self.exchange():
            copy.wait_recv()
        for copy in self.exchange():
            copy.wait_send()


def deliver_sems(ranks):
    return [pltpu.SemaphoreType.DMA((ranks,)), pltpu.SemaphoreType.DMA((ranks,)), pltpu.SemaphoreType.DMA]


def first_kernel(
    ranks, kv_heads, order, starts, tokens, out_grad, freqs, attn_gain, mlp_gain, query_gain, key_gain,
    w_query, w_key, w_value, w_output, w_gate, w_up, w_down,
    resid, second, cosv, sinv, q_low, k_low, v_low, own_out, first_in, qkv, attn_block, dy_all, prob, mlp_block, out_all,
    held, normal, kept, block, a_rows, m_rows, gate, up, down, dys, probs, pos, begins, pos_row,
    out_low, whole, *sems,
):
    local, width = tokens.shape
    rows = local * ranks
    own = w_query.shape[0]
    size = freqs.shape[1]
    heads = q_low.shape[0]
    share = heads // kv_heads
    half = ranks // 2
    scale = 1.0 / math.sqrt(size)
    cols = (heads + 2 * kv_heads) * size
    deep = block.shape[1]
    row = functools.partial(block_row, local=local, ranks=ranks)
    seq, dp = lax.axis_index("seq"), lax.axis_index("dp")
    right, left = neighbours(ranks)
    attn = Spread(a_rows, block, ranks, own, pl.ds(0, a_rows.shape[2]), sems[12:17])
    third = m_rows.shape[2] // 3
    mlp = [
        Spread(m_rows, mlp_block, ranks, own, pl.ds(at * third, third), sems[17 + 5 * at : 22 + 5 * at])
        for at in range(3)
    ]
    local_sems = sems[32]
    out_send, out_recv = sems[2:4]
    o_cols = heads * size
    peers = [(lax.rem(seq + step, ranks), dp) for step in range(1, ranks)]
    peers += [(seq, attn.beside), (seq, attn.sibling)]
    knock(peers)
    loads = [
        move(src, dst, local_sems.at[at])
        for at, (src, dst) in enumerate(((w_gate, gate), (w_up, up), (w_down, down)))
    ]
    held[pl.ds(row(0), local)] = tokens[...]
    dys[pl.ds(row(0), local)] = out_grad[...]

    def column(line):
        same = lax.broadcasted_iota(jnp.int32, (own, own), 0) == lax.broadcasted_iota(jnp.int32, (own, own), 1)
        return jnp.sum(jnp.where(same, line, 0.0), 1, keepdims=True)

    def lay(target, begin, weight, gain):
        each = weight.shape[1] // ranks
        for rank in range(ranks):
            part = weight[:, rank * each : (rank + 1) * each]
            if gain is not None:
                part = (part.astype(jnp.float32) * gain).astype(LOW)
            target[rank, :, begin : begin + each] = part
        return begin + each

    gain = column(attn_gain[...])
    at = 0
    for weight in (w_query, w_key, w_value):
        at = lay(a_rows, at, weight, gain)
    whole[seq, pl.ds(pl.multiple_of(dp * own, own), own)] = w_output[...]
    answered(peers)
    ring = RingGather(held, local, ranks, sems[0], sems[1], right, left, row)
    ring.start(1)
    attn.start()
    outs = WholeGather(whole, ranks, own, [*sems[8:12], *sems[33:35]])
    outs.forward(0)
    line = LineGather(dys, local, ranks, sems[4], sems[5], sems[6], sems[7])
    stores = []

    def store(src, dst):
        stores.append(move(src, dst, local_sems.at[len(loads) + len(stores)]))

    def scale_rows(step):
        for rel in rels_of(step, ranks):

            def some(at, _):
                rows_at = pl.ds(pl.multiple_of(row(rel) + at * 32, 32), 32)
                normal[rows_at] = rows_scaled(held[rows_at].astype(jnp.float32))[0].astype(LOW)
                return 0

            lax.fori_loop(0, local // 32, some, 0)

    for load in loads:
        load.wait()
    gain = column(mlp_gain[...])
    each = gate.shape[1] // ranks
    lay(m_rows, 0, gate, gain)
    lay(m_rows, each, up, gain)
    lay(m_rows, 2 * each, down, None)
    scale_rows(0)
    ring.advance(1)
    scale_rows(1)
    attn.arrive()
    attn.hop(0).start()
    attn.hop(1).start()
    spans = order.shape[0]
    span = rows // spans
    for at in range(ranks):
        rows_at = pl.ds(at * local, local)
        ids = at * local + lax.broadcasted_iota(jnp.int32, (1, local), 1)
        where = jnp.zeros_like(ids)
        for slot in range(spans):
            inside = (ids >= slot * span) & (ids < (slot + 1) * span)
            where = where + jnp.where(inside, ids + (order[slot] - slot) * span, 0)
        begin = jnp.zeros_like(ids)
        for doc in range(starts.shape[1]):
            begin = jnp.maximum(begin, jnp.where(starts[0, doc] <= where, starts[0, doc], 0))
        pos_row[:, rows_at] = where
        across = jnp.broadcast_to(where, (local, local)).T
        pos[rows_at] = across[:, :1]
        begins[rows_at] = jnp.broadcast_to(begin, (local, local)).T[:, :1]
        angle = across[:, :1].astype(jnp.float32) * freqs[...]
        lane = lax.broadcasted_iota(jnp.int32, (local, size), 1)
        cosv[rows_at] = jnp.cos(angle)
        sine = jnp.sin(angle)
        sinv[rows_at] = jnp.where(lane < size // 2, -sine, sine)
    for step in range(2, half):
        ring.advance(step)
        scale_rows(step)
        if step == 2:
            outs.start(1)
            attn.hop(0).wait_recv()
            attn.hop(2).start()

    def bring(step):
        outs.arrive(step)
        if step < half:
            outs.start(step + 1)
        outs.forward(step)

    bring(1)
    mlp[0].start()
    attn.hop(1).wait_recv()
    attn.hop(2).wait_recv()
    store(block, attn_block)

    def project(begin, count):
        rows_at = pl.ds(begin, count)
        kept[rows_at] = dot_nn(normal[rows_at], block[...].reshape(width, cols))

    ring.advance(half)
    bring(2)
    scale_rows(half)
    store(normal, first_in)
    tile = rows // half

    def rotated(at, rows_at, gain):
        v = rows_scaled(kept[rows_at, at * size : (at + 1) * size])[0] * gain[...]
        return (v * cosv[rows_at] + turn(v) * sinv[rows_at]).astype(LOW)

    for piece in range(half):
        rows_at = pl.ds(piece * tile, tile)
        project(piece * tile, tile)
        for head in range(heads):
            q_low[head, rows_at] = rotated(head, rows_at, query_gain)
        for group in range(kv_heads):
            k_low[group, rows_at] = rotated(heads + group, rows_at, key_gain)
            at = (heads + kv_heads + group) * size
            v_low[group, rows_at] = kept[rows_at, at : at + size].astype(LOW)
    store(kept, qkv)
    bring(3)
    mlp[1].start()
    line.start(1)

    def forward(piece):
        mlp[piece].arrive()
        mlp[piece].hop(0).start()
        mlp[piece].hop(1).start()

    for piece in range(half):
        rows_at = pl.ds(piece * tile, tile)
        seen = (pos_row[...] <= pos[rows_at]) & (pos_row[...] >= begins[rows_at])
        for head in range(heads):
            raw = dot_nt(q_low[head, rows_at], k_low[head // share]) * scale
            raw = jnp.where(seen, raw, NEG)
            weight = jnp.exp(raw - jnp.max(raw, -1, keepdims=True))
            weight = (weight * (1.0 / jnp.sum(weight, -1, keepdims=True))).astype(LOW)
            probs[head, rows_at] = weight
            value = dot_nn(weight, v_low[head // share])
            out_low[rows_at, head * size : (head + 1) * size] = value.astype(LOW)
            store(probs.at[head, rows_at], prob.at[head, rows_at])
        if piece == 0:
            bring(half)
            mlp[2].start()
        if piece == half - 2:
            forward(0)
            line.advance(1)
    place = ring_place(seq, ranks)

    def exchange(rel):
        to = ring_seq(lax.rem(place + rel, ranks), ranks)
        return push(
            out_low.at[pl.ds(row(rel), local)],
            own_out.at[:, pl.ds(pl.multiple_of(seq * o_cols, o_cols), o_cols)],
            out_send.at[rel],
            out_recv.at[rel],
            (to, dp),
        )

    for rel in range(1, ranks):
        exchange(rel).start()
    own_out[:, pl.ds(pl.multiple_of(seq * o_cols, o_cols), o_cols)] = out_low[pl.ds(row(0), local)]
    forward(1)
    for step in range(2, half - 1):
        line.advance(step)
    outs.complete()
    store(whole, out_all)
    forward(2)
    line.advance(half - 1)
    mlp[0].hop(0).wait_recv()
    mlp[0].hop(2).start()
    for rel in range(1, ranks):
        exchange(rel).wait_recv()

    def join(at, _):
        some = pl.ds(pl.multiple_of(at * deep, deep), deep)
        resid[:, some] = tokens[:, some].astype(jnp.float32) + dot_nt(own_out[...], whole[at])
        return 0

    lax.fori_loop(0, ranks, join, 0)

    def scale_second(at, _):
        rows_at = pl.ds(pl.multiple_of(at * 32, 32), 32)
        second[rows_at] = rows_scaled(resid[rows_at])[0].astype(LOW)
        return 0

    lax.fori_loop(0, local // 32, scale_second, 0)
    for piece in mlp[1:]:
        piece.hop(0).wait_recv()
        piece.hop(2).start()
    line.complete()
    store(dys, dy_all)
    ring.finish()
    attn.finish()
    outs.finish()
    for rel in range(1, ranks):
        exchange(rel).wait_send()
    line.finish()
    for piece in mlp:
        piece.hop(1).wait_recv()
        piece.hop(2).wait_recv()
        piece.finish()
    for given in stores:
        given.wait()


def mlp_kernel(
    ranks, second, out_grad, rest, dys, mlp_block, block_out, dresid, dresid_low, own_grads,
    grads, from_core, from_y, held, weights, hidden, dgu, resid, dy_all,
    term, out_buf, in_buf, y_out, y_in, here, *sems,
):
    local, width = second.shape
    row = functools.partial(block_row, local=local, ranks=ranks)
    ff = hidden.shape[1]
    deep = weights.shape[1]
    half = ranks // 2
    right, left = neighbours(ranks)
    loads = [
        move(src, dst, here.at[at])
        for at, (src, dst) in enumerate(((mlp_block, weights), (dys, dy_all), (rest, resid)))
    ]
    seq, dp = lax.axis_index("seq"), lax.axis_index("dp")
    own = own_grads.shape[1]
    pieces = [
        Reduce(
            grads, from_core, from_y, own_grads, own, at * ranks // 4, ranks // 4, pl.ds(0, 3 * ff),
            sems[6 + 2 * at : 8 + 2 * at],
        )
        for at in range(4)
    ]
    peers = [right, left, (seq, pieces[0].beside), (seq, pieces[0].sibling)]
    knock(peers)
    held[pl.ds(row(0), local)] = second[...]
    answered(peers)
    ring = RingGather(held, local, ranks, sems[0], sems[1], right, left, row)
    ring.start(1)
    loads[0].wait()
    loads[1].wait()
    wide = 256

    def middle(step):
        rels = rels_of(step, ranks)

        def some(at, _):
            first = pl.multiple_of(at * wide, wide)
            given, dy = block_rows(held, rels, local, ranks), block_rows(dy_all, rels, local, ranks)
            gate = dot_nn(given, weights[:, :, pl.ds(first, wide)].reshape(width, wide))
            upper = dot_nn(given, weights[:, :, pl.ds(ff + first, wide)].reshape(width, wide))
            dmid = dot_nn(dy, weights[:, :, pl.ds(2 * ff + first, wide)].reshape(width, wide))
            sigma = 1.0 / (1.0 + jnp.exp(-gate))
            act = gate * sigma
            value = (act * upper).astype(LOW)
            dgate = (dmid * upper * (sigma * (1.0 + gate * (1.0 - sigma)))).astype(LOW)
            dupper = (dmid * act).astype(LOW)
            for at, rel in enumerate(rels):
                rows, some_rows = pl.ds(row(rel), local), slice(at * local, (at + 1) * local)
                hidden[rows, pl.ds(first, wide)] = value[some_rows]
                dgu[rows, pl.ds(first, wide)] = dgate[some_rows]
                dgu[rows, pl.ds(ff + first, wide)] = dupper[some_rows]
            return 0

        lax.fori_loop(0, ff // wide, some, 0)

    middle(0)
    for step in range(1, half + 1):
        ring.advance(step)
        middle(step)

    def back_part(rels, begin, end):
        def some(at, _):
            value = dot_nt(block_rows(dgu, rels, local, ranks), weights[at, :, : 2 * ff])
            term[: len(rels) * local, pl.ds(pl.multiple_of(at * deep, deep), deep)] = value
            return 0

        lax.fori_loop(begin, end, some, 0)

    def out_part(rels, begin, end):
        def some(at, _):
            value = dot_nt(block_rows(hidden, rels, local, ranks), weights[at, :, 2 * ff :])
            term[: len(rels) * local, pl.ds(pl.multiple_of(at * deep, deep), deep)] = value
            return 0

        lax.fori_loop(begin, end, some, 0)

    def weight_grads(first, count):
        def some(at, _):
            cols = pl.ds(pl.multiple_of(at * deep, deep), deep)
            grads[at, :, : 2 * ff] = dot_tn(held[:, cols], dgu[...]).astype(LOW)
            grads[at, :, 2 * ff :] = dot_tn(dy_all[:, cols], hidden[...]).astype(LOW)
            return 0

        lax.fori_loop(first, first + count, some, 0)

    back = RingSum(back_part, term, out_buf, in_buf, local, ranks, sems[2], sems[3], right, left)
    out = RingSum(out_part, term, y_out, y_in, local, ranks, sems[4], sems[5], right, left)
    for step in range(1, half + 1):
        back.compute(step)
        back.launch(step)
        out.compute(step)
        out.launch(step)
        made, passed, summed = (((0, 1), (2,), (3,), ()), ((), (0, 1), (2,), (3,)), ((), (), (0, 1), (2,)))
        for piece in (pieces[at] for at in made[step - 1]):
            weight_grads(piece.begin, piece.count)
            piece.first()
        for at in passed[step - 1]:
            pieces[at].second()
        for at in summed[step - 1]:
            pieces[at].third()
    back.compute(half + 1)
    loads[2].wait()
    back.arrive_last()

    def finish_back(at, _):
        begin = pl.multiple_of(at * 32, 32)
        rows = pl.ds(begin, 32)
        value = resid[rows]
        inv = rows_scaled(value)[1]
        grad = back.last(begin, 32)
        full = out_grad[rows].astype(jnp.float32) + rows_scaled_back(value, inv, grad)
        dresid[rows] = full
        dresid_low[rows] = full.astype(LOW)
        return 0

    lax.fori_loop(0, local // 32, finish_back, 0)
    out.compute(half + 1)
    out.arrive_last()

    def finish_out(at, _):
        begin = pl.multiple_of(at * 32, 32)
        rows = pl.ds(begin, 32)
        block_out[rows] = (resid[rows] + out.last(begin, 32)).astype(LOW)
        return 0

    lax.fori_loop(0, local // 32, finish_out, 0)
    ring.finish()
    pieces[3].third()
    back.finish()
    out.finish()
    for piece in pieces:
        piece.finish()


def back_kernel(
    ranks, kv_heads, tokens, dresid_low, query_gain, key_gain, own_out, first_in_in, block_in,
    qkv_in, cos_in, sin_in, q_in, k_in, v_in, prob_in, dresid_in, mlp_own, out_all,
    tokens_grad, gains, out_grad, mlp_sums, attn_sums,
    grads, from_core, from_y, own_grads, query_gain_grad, key_gain_grad,
    tile, tiles_in, tile_sum, tile_sums_in, dob, dout, dk, dv, dqkv,
    first_in, attn_block, qkv, cosv, sinv, q_low, k_low, v_low, prob, dresid, term, out_buf, in_buf,
    o_grads, o_core, o_y, o_own, o_term, o_out, o_in, *sems,
):
    local, width = tokens.shape
    rows = local * ranks
    half = ranks // 2
    size = cosv.shape[1]
    heads = q_low.shape[0]
    share = heads // kv_heads
    scale = 1.0 / math.sqrt(size)
    cols = (heads + 2 * kv_heads) * size
    deep = attn_block.shape[1]
    o_cols = heads * size
    right, left = neighbours(ranks)
    seq, dp = lax.axis_index("seq"), lax.axis_index("dp")
    own = mlp_own.shape[1]
    copies = lax.axis_size("dp")
    row = functools.partial(block_row, local=local, ranks=ranks)
    place = ring_place(seq, ranks)
    out_piece = Reduce(o_grads, o_core, o_y, o_own, own, 0, ranks, pl.ds(0, width), sems[4:6])
    qkv_piece = Reduce(grads, from_core, from_y, own_grads, own, 0, ranks, pl.ds(0, cols), sems[6:8])
    third = mlp_own.shape[2] // 3
    mlp_ways = [
        Deliver(mlp_own, mlp_sums, pl.ds(at * third, third), ranks, [*sems[8:11], *sems[22:28]][3 * at : 3 * at + 3])
        for at in range(3)
    ]
    dob_send, dob_recv = sems[0:2]
    qkv_way = Deliver(own_grads, attn_sums, pl.ds(0, cols), ranks, sems[14:17])
    peers = [(lax.rem(seq + step, ranks), dp) for step in range(1, ranks)]
    peers += [(seq, lax.rem(dp + step, copies)) for step in range(1, copies)]
    knock(peers)
    local_sems = sems[21]
    loads = {}
    for at, (name, src, dst) in enumerate(
        (
            ("out", out_all, o_grads), ("block", block_in, attn_block), ("v", v_in, v_low),
            ("prob", prob_in, prob), ("k", k_in, k_low), ("q", q_in, q_low), ("cos", cos_in, cosv),
            ("sin", sin_in, sinv), ("qkv", qkv_in, qkv), ("first", first_in_in, first_in),
            ("dresid", dresid_in, dresid),
        )
    ):
        loads[name] = move(src, dst, local_sems.at[at])
    answered(peers)
    loads["out"].wait()

    def columns_of(rank):
        return pl.ds(pl.multiple_of(rank * o_cols, o_cols), o_cols)

    def owner(rel):
        return ring_seq(lax.rem(place + rel, ranks), ranks)

    def exchange(rel):
        to = owner(rel)
        return push(
            dob.at[:, columns_of(to)], dout.at[pl.ds(row(0), local)], dob_send.at[rel], dob_recv.at[rel], (to, dp)
        )

    def project(rel):
        some = columns_of(owner(rel))
        dob[:, some] = dot_nn(dresid_low[...], o_grads[:, :, some].reshape(width, o_cols)).astype(LOW)

    for rel in (*ring_order(ranks)[1:][::-1], 0):
        project(rel)
        if rel:
            exchange(rel).start()
    dout[pl.ds(row(0), local)] = dob[:, columns_of(seq)]
    mlp_ways[0].start()

    def out_grads(at, _):
        some_cols = pl.ds(pl.multiple_of(at * deep, deep), deep)
        o_grads[at] = dot_tn(dresid_low[:, some_cols], own_out[...]).astype(LOW)
        return 0

    lax.fori_loop(0, ranks, out_grads, 0)
    out_piece.first()
    for rel in range(1, ranks):
        exchange(rel).wait_recv()
    for name in ("v", "prob", "k", "q", "cos", "sin", "qkv"):
        loads[name].wait()
    tall = rows // half
    query_gain_grad[...] = jnp.zeros_like(query_gain_grad)
    key_gain_grad[...] = jnp.zeros_like(key_gain_grad)

    def unrotated(grad, column, rows_at, gain, gain_grad_ref):
        grad = grad * cosv[rows_at] - turn(grad) * sinv[rows_at]
        value = qkv[rows_at, column * size : (column + 1) * size]
        normal, inv = rows_scaled(value)
        gain_grad_ref[...] += jnp.sum(grad * normal, 0, keepdims=True)
        back = rows_scaled_back(value, inv, grad * gain[...])
        dqkv[rows_at, column * size : (column + 1) * size] = back.astype(LOW)

    for head in range(heads):
        group = head // share

        def one(piece, _):
            rows_at = pl.ds(pl.multiple_of(piece * tall, tall), tall)
            weight = prob[head, rows_at]
            grad = dout[rows_at, head * size : (head + 1) * size]
            dprob = dot_nt(grad, v_low[group])
            full = weight.astype(jnp.float32)
            delta = jnp.sum(full * dprob, -1, keepdims=True)
            dscore = (full * (dprob - delta)).astype(LOW)
            dq = dot_nn(dscore, k_low[group]) * scale
            dk_add = dot_tn(dscore, q_low[head, rows_at]) * scale
            dv_add = dot_tn(weight, grad)
            dk[group] += dk_add
            dv[group] += dv_add
            unrotated(dq, head, rows_at, query_gain, query_gain_grad)
            return 0

        if head % share == 0:
            dk[group] = jnp.zeros_like(dk[group])
            dv[group] = jnp.zeros_like(dv[group])
        lax.fori_loop(0, half, one, 0)
        if head == 0:
            out_piece.second()
            mlp_ways[1].start()
    for group in range(kv_heads):
        def one_key(piece, _):
            rows_at = pl.ds(pl.multiple_of(piece * tall, tall), tall)
            unrotated(dk[group, rows_at], heads + group, rows_at, key_gain, key_gain_grad)
            at = (heads + kv_heads + group) * size
            dqkv[rows_at, at : at + size] = dv[group, rows_at].astype(LOW)
            return 0

        lax.fori_loop(0, half, one_key, 0)

    def part(rels, begin, end):
        def some(at, _):
            value = dot_nt(block_rows(dqkv, rels, local, ranks), attn_block[at])
            term[: len(rels) * local, pl.ds(pl.multiple_of(at * deep, deep), deep)] = value
            return 0

        lax.fori_loop(begin, end, some, 0)

    def qkv_grads(at, _):
        some_cols = pl.ds(pl.multiple_of(at * deep, deep), deep)
        grads[at] = dot_tn(first_in[:, some_cols], dqkv[...]).astype(LOW)
        return 0

    def to_ranks(step):
        peer = lax.rem(seq + step, ranks)
        return push(tile, tiles_in.at[seq], sems[17].at[step], sems[18].at[step], (peer, dp))

    def to_copies(step):
        peer = lax.rem(dp + step, copies)
        return push(
            tile_sum, tile_sums_in.at[dp], sems[19].at[step], sems[20].at[step], (seq, peer)
        )

    tile[0:1] = query_gain_grad[...]
    tile[1:2] = key_gain_grad[...]
    tile[2:] = jnp.zeros((tile.shape[0] - 2, size), jnp.float32)
    for step in range(1, ranks):
        to_ranks(step).start()
    tiles_in[seq] = tile[...]
    mlp_ways[2].start()
    loads["block"].wait()

    def out_part(rels, begin, end):
        for at, rel in enumerate(rels):
            o_term[at * own : (at + 1) * own] = o_own[owner(rel)].astype(jnp.float32)

    out_total = RingSum(out_part, o_term, o_out, o_in, own, ranks, sems[30], sems[31], right, left)
    totals = two_sums(part, term, out_buf, in_buf, local, ranks, [*sems[2:4], *sems[28:30]], right, left)
    for step in range(1, half + 1):
        for total in totals:
            total.compute(step)
            total.launch(step)
        if step == 1:
            loads["first"].wait()
            lax.fori_loop(0, ranks, qkv_grads, 0)
            qkv_piece.first()
        if step == 2:
            qkv_piece.second()
            for other in range(1, ranks):
                to_ranks(other).wait_recv()
            tile_sum[...] = jnp.sum(tiles_in[...], 0)
            for other in range(1, copies):
                to_copies(other).start()
            tile_sums_in[dp] = tile_sum[...]
        if step == half - 1:
            for other in range(1, copies):
                to_copies(other).wait_recv()
            gains[...] = jnp.sum(tile_sums_in[...], 0)
            qkv_piece.third()
            qkv_way.start()
    out_piece.third()
    for step in range(1, half + 1):
        out_total.compute(step)
        out_total.launch(step)
    for total in totals:
        total.compute(half + 1)
    loads["dresid"].wait()
    for total in totals:
        total.arrive_last()

    def last(at, _):
        begin = pl.multiple_of(at * 32, 32)
        rows_at = pl.ds(begin, 32)
        value = tokens[rows_at].astype(jnp.float32)
        inv = rows_scaled(value)[1]
        grad = jnp.concatenate([total.last(begin, 32) for total in totals], 1)
        tokens_grad[rows_at] = dresid[rows_at] + rows_scaled_back(value, inv, grad)
        return 0

    lax.fori_loop(0, local // 32, last, 0)
    out_total.compute(half + 1)
    out_total.arrive_last()
    out_grad[...] = out_total.last(0, own)
    for step in range(1, ranks):
        to_ranks(step).wait_send()
    for step in range(1, copies):
        to_copies(step).wait_send()
    out_total.finish()
    for rel in range(1, ranks):
        exchange(rel).wait_send()
    for total in totals:
        total.finish()
    out_piece.finish()
    qkv_piece.finish()
    for way in mlp_ways:
        way.finish()
    qkv_way.finish()


def leave_kernel(
    attn_sums, mlp_sums, attn_gain, mlp_gain, w_query, w_key, w_value, w_gate, w_up,
    query_out, key_out, value_out, gate_out, up_out, down_out, attn_out, mlp_out,
):
    own = attn_gain.shape[1]
    same = lax.broadcasted_iota(jnp.int32, (own, own), 0) == lax.broadcasted_iota(jnp.int32, (own, own), 1)

    @pl.when(pl.program_id(0) == 0)
    def _():
        attn_out[...] = jnp.zeros_like(attn_out)
        mlp_out[...] = jnp.zeros_like(mlp_out)

    for sums, gain, gain_out, parts in (
        (attn_sums, attn_gain, attn_out, ((query_out, w_query), (key_out, w_key), (value_out, w_value))),
        (mlp_sums, mlp_gain, mlp_out, ((gate_out, w_gate), (up_out, w_up), (down_out, None))),
    ):
        scale = jnp.sum(jnp.where(same, gain[...], 0.0), 1, keepdims=True)
        at = 0
        for out, weight in parts:
            value = sums[0, :, at : at + out.shape[1]].astype(jnp.float32)
            at += out.shape[1]
            if weight is None:
                out[...] = value
                continue
            out[...] = value * scale
            inner = jnp.sum(value * weight[...].astype(jnp.float32), 1, keepdims=True)
            gain_out[...] += jnp.sum(jnp.where(same, inner, 0.0), 0, keepdims=True)


VM = pl.BlockSpec(memory_space=pltpu.VMEM)
SM = pl.BlockSpec(memory_space=pltpu.SMEM)
ANY = pl.BlockSpec(memory_space=pl.ANY)


def call(kernel, number, ins, outs, scratch, operands):
    return pl.pallas_call(
        kernel,
        out_shape=[jax.ShapeDtypeStruct(shape, dtype) for shape, dtype, _ in outs],
        in_specs=ins,
        out_specs=[spec for _, _, spec in outs],
        scratch_shapes=scratch,
        compiler_params=pltpu.CompilerParams(
            collective_id=number, has_side_effects=True, vmem_limit_bytes=LIMIT
        ),
    )(*operands)


def columns_body(
    tokens,
    out_grad,
    span_order,
    doc_starts,
    w_query,
    w_key,
    w_value,
    w_output,
    attn_gain,
    query_gain,
    key_gain,
    w_gate,
    w_up,
    w_down,
    mlp_gain,
):
    ranks = lax.axis_size("seq")
    copies = lax.axis_size("dp")
    _, local, width = tokens.shape
    rows = local * ranks
    size = query_gain.shape[0]
    kv_heads = w_key.shape[1] // size // ranks
    heads = w_query.shape[1] // size // ranks
    q_cols, kv_cols = heads * size, kv_heads * size
    qkv_cols = q_cols + 2 * kv_cols
    ff = w_gate.shape[1] // ranks
    own = width // (ranks * copies)
    deep = own * copies
    half = ranks // 2
    f32, i32 = jnp.float32, jnp.int32
    exponents = np.arange(size) % (size // 2) * (-2.0 / size * math.log(1000000.0))
    freqs = jnp.asarray(np.exp(exponents)[None], f32)
    q_gain, k_gain = query_gain[None], key_gain[None]
    (
        resid, second, cosv, sinv, q_low, k_low, v_low, own_out, first_in, qkv, attn_block, dy_all, prob, mlp_block,
        out_all,
    ) = call(
        functools.partial(first_kernel, ranks, kv_heads),
        1,
        [SM, SM] + [VM] * 11 + [ANY] * 3,
        [
            ((local, width), f32, VM),
            ((local, width), LOW, VM),
            ((rows, size), f32, VM),
            ((rows, size), f32, VM),
            ((heads, rows, size), LOW, VM),
            ((kv_heads, rows, size), LOW, VM),
            ((kv_heads, rows, size), LOW, VM),
            ((local, q_cols * ranks), LOW, VM),
            ((rows, width), LOW, ANY),
            ((rows, qkv_cols), f32, ANY),
            ((ranks, deep, qkv_cols), LOW, ANY),
            ((rows, width), LOW, ANY),
            ((heads, rows, rows), LOW, ANY),
            ((ranks, deep, 3 * ff), LOW, ANY),
            ((ranks, deep, q_cols * ranks), LOW, ANY),
        ],
        [
            pltpu.VMEM((rows, width), LOW),
            pltpu.VMEM((rows, width), LOW),
            pltpu.VMEM((rows, qkv_cols), f32),
            pltpu.VMEM((ranks, deep, qkv_cols), LOW),
            pltpu.VMEM((ranks, own, qkv_cols), LOW),
            pltpu.VMEM((ranks, own, 3 * ff), LOW),
        ]
        + [pltpu.VMEM((own, ff * ranks), LOW)] * 3
        + [
            pltpu.VMEM((rows, width), LOW),
            pltpu.VMEM((heads, rows, rows), LOW),
            pltpu.VMEM((rows, 1), i32),
            pltpu.VMEM((rows, 1), i32),
            pltpu.VMEM((1, rows), i32),
            pltpu.VMEM((rows, q_cols), LOW),
            pltpu.VMEM((ranks, deep, q_cols * ranks), LOW),
        ]
        + ring_sems(ranks)
        + [pltpu.SemaphoreType.DMA((ranks,))] * 2
        + line_sems(ranks)
        + whole_sems(ranks)[:4]
        + spread_sems(ranks) * 4
        + [pltpu.SemaphoreType.DMA((heads * half + 8,))]
        + whole_sems(ranks)[4:],
        (
            span_order, doc_starts, tokens[0], out_grad[0], freqs, attn_gain[None], mlp_gain[None], q_gain, k_gain,
            w_query, w_key, w_value, w_output, w_gate, w_up, w_down,
        ),
    )
    block_out, dresid, dresid_low, mlp_own = call(
        functools.partial(mlp_kernel, ranks),
        2,
        [VM, VM, ANY, ANY, ANY],
        [
            ((local, width), LOW, VM),
            ((local, width), f32, VM),
            ((local, width), LOW, VM),
            ((ranks, own, 3 * ff), LOW, VM),
        ],
        [pltpu.VMEM((ranks, deep, 3 * ff), LOW)]
        + reduce_bufs(ranks, own, 3 * ff)
        + [
            pltpu.VMEM((rows, width), LOW),
            pltpu.VMEM((ranks, deep, 3 * ff), LOW),
            pltpu.VMEM((rows, ff), LOW),
            pltpu.VMEM((rows, 2 * ff), LOW),
            pltpu.VMEM((local, width), f32),
            pltpu.VMEM((rows, width), LOW),
        ]
        + sum_bufs(local, ranks, width)
        + sum_bufs(local, ranks, width)[1:]
        + [pltpu.SemaphoreType.DMA((3,))]
        + ring_sems(ranks) * 3
        + reduce_sems() * 4,
        (second, out_grad[0], resid, dy_all, mlp_block),
    )
    tokens_grad, gains, wo_grad, mlp_sums, attn_sums = call(
        functools.partial(back_kernel, ranks, kv_heads),
        3,
        [VM] * 5 + [ANY] * 12,
        [
            ((local, width), f32, VM),
            ((8, size), f32, VM),
            ((own, q_cols * ranks), f32, VM),
            ((ranks, own, 3 * ff), LOW, ANY),
            ((ranks, own, qkv_cols), LOW, VM),
        ],
        [pltpu.VMEM((ranks, deep, qkv_cols), LOW)]
        + reduce_bufs(ranks, own, qkv_cols)
        + [
            pltpu.VMEM((ranks, own, qkv_cols), LOW),
            pltpu.VMEM((1, size), f32),
            pltpu.VMEM((1, size), f32),
            pltpu.VMEM((8, size), f32),
            pltpu.VMEM((ranks, 8, size), f32),
            pltpu.VMEM((8, size), f32),
            pltpu.VMEM((copies, 8, size), f32),
            pltpu.VMEM((local, q_cols * ranks), LOW),
            pltpu.VMEM((rows, q_cols), LOW),
            pltpu.VMEM((kv_heads, rows, size), f32),
            pltpu.VMEM((kv_heads, rows, size), f32),
            pltpu.VMEM((rows, qkv_cols), LOW),
            pltpu.VMEM((rows, width), LOW),
            pltpu.VMEM((ranks, deep, qkv_cols), LOW),
            pltpu.VMEM((rows, qkv_cols), f32),
            pltpu.VMEM((rows, size), f32),
            pltpu.VMEM((rows, size), f32),
            pltpu.VMEM((heads, rows, size), LOW),
            pltpu.VMEM((kv_heads, rows, size), LOW),
            pltpu.VMEM((kv_heads, rows, size), LOW),
            pltpu.VMEM((heads, rows, rows), LOW),
            pltpu.VMEM((local, width), f32),
        ]
        + sum_bufs(local, ranks, width)
        + [pltpu.VMEM((ranks, deep, q_cols * ranks), LOW)]
        + reduce_bufs(ranks, own, q_cols * ranks)
        + [pltpu.VMEM((ranks, own, q_cols * ranks), LOW)]
        + sum_bufs(own, ranks, q_cols * ranks)
        + [pltpu.SemaphoreType.DMA((ranks,))] * 2
        + ring_sems(ranks)
        + reduce_sems() * 2
        + deliver_sems(ranks) * 3
        + [pltpu.SemaphoreType.DMA((ranks,))] * 2
        + [pltpu.SemaphoreType.DMA((copies,))] * 2
        + [pltpu.SemaphoreType.DMA((11,))]
        + deliver_sems(ranks) * 2
        + ring_sems(ranks) * 2,
        (
            tokens[0], dresid_low, q_gain, k_gain, own_out, first_in, attn_block, qkv, cosv, sinv, q_low, k_low,
            v_low, prob, dresid, mlp_own, out_all,
        ),
    )
    whole = pl.BlockSpec((1, own), lambda at: (0, 0))
    each = (q_cols, kv_cols, kv_cols, ff, ff, ff)
    columns = [pl.BlockSpec((own, cols), lambda at: (0, at)) for cols in each]
    *grads, dga, dgm = pl.pallas_call(
        leave_kernel,
        grid=(ranks,),
        out_shape=[jax.ShapeDtypeStruct((own, cols * ranks), f32) for cols in each]
        + [jax.ShapeDtypeStruct((1, own), f32)] * 2,
        in_specs=[
            pl.BlockSpec((1, own, qkv_cols), lambda at: (at, 0, 0)),
            pl.BlockSpec((1, own, 3 * ff), lambda at: (at, 0, 0)),
            whole,
            whole,
            *columns[:3],
            *columns[3:5],
        ],
        out_specs=columns + [whole, whole],
    )(attn_sums, mlp_sums, attn_gain[None], mlp_gain[None], w_query, w_key, w_value, w_gate, w_up)
    return (
        block_out[None], tokens_grad[None], *grads[:3], wo_grad, dga[0], gains[0], gains[1], *grads[3:], dgm[0],
    )


def body(*args):
    tokens, w_key, query_gain = args[0], args[5], args[9]
    groups = w_key.shape[1] // query_gain.shape[0]
    ranks = lax.axis_size("seq")
    if tokens.shape[0] == 1 and ranks % 2 == 0 and groups % ranks == 0 and lax.axis_size("dp") == 4:
        return columns_body(*args)
    return gathered_body(*args)


def solution(mesh):
    return jax.shard_map(
        body,
        mesh=mesh,
        in_specs=(
            P("dp", "seq", None),
            P("dp", "seq", None),
            P(),
            P("dp", None),
            P(("seq", "dp"), None),
            P(("seq", "dp"), None),
            P(("seq", "dp"), None),
            P(("seq", "dp"), None),
            P(("seq", "dp")),
            P(),
            P(),
            P(("seq", "dp"), None),
            P(("seq", "dp"), None),
            P(("seq", "dp"), None),
            P(("seq", "dp")),
        ),
        out_specs=(
            P("dp", "seq", None),
            P("dp", "seq", None),
            P(("seq", "dp"), None),
            P(("seq", "dp"), None),
            P(("seq", "dp"), None),
            P(("seq", "dp"), None),
            P(("seq", "dp")),
            P(),
            P(),
            P(("seq", "dp"), None),
            P(("seq", "dp"), None),
            P(("seq", "dp"), None),
            P(("seq", "dp")),
        ),
        check_vma=False,
    )
```

```python
import functools
import math

import jax
import jax.numpy as jnp
import numpy as np
from jax import lax
from jax.experimental import pallas as pl
from jax.experimental.pallas import tpu as pltpu
from jax.sharding import PartitionSpec as P

EPS = 1e-06
NEG = -1e30


def normed(v, gain):
    scale_inv = lax.rsqrt(jnp.mean(v * v, -1, keepdims=True) + EPS)
    return (v * scale_inv * gain, scale_inv)


def norm_back(v, scale_inv, gain, grad):
    scaled = grad * gain
    inner = jnp.mean(scaled * v, -1, keepdims=True)
    dv = scale_inv * scaled - v * scale_inv * scale_inv * scale_inv * inner
    dgain = jnp.sum((grad * v * scale_inv).reshape(-1, v.shape[-1]), 0)
    return (dv, dgain)


def rotary(pos, width):
    half = width // 2
    freqs = jnp.exp(jnp.arange(half, dtype=jnp.float32) * (-2.0 / width * math.log(1000000.0)))
    angle = pos.astype(jnp.float32)[:, None] * freqs[None, :]
    return (jnp.cos(angle)[:, None, :], jnp.sin(angle)[:, None, :])


def rotate(v, cosv, sinv):
    half = v.shape[-1] // 2
    first, second = (v[..., :half], v[..., half:])
    return jnp.concatenate([first * cosv - second * sinv, second * cosv + first * sinv], -1)


def rotate_back(grad, cosv, sinv):
    half = grad.shape[-1] // 2
    first, second = (grad[..., :half], grad[..., half:])
    return jnp.concatenate([first * cosv + second * sinv, second * cosv - first * sinv], -1)


def place(order, begin, count, span):
    rows = begin + jnp.arange(count, dtype=jnp.int32)
    slots = rows // span
    picked = slots[:, None] == jnp.arange(order.shape[0], dtype=jnp.int32)[None, :]
    return jnp.sum(jnp.where(picked, order[None, :], 0), -1) * span + rows % span


def doc_of(starts, pos):
    return jnp.sum((starts[:, None, :] <= pos[None, :, None]).astype(jnp.int32), -1)


def gathered_body(
    tokens,
    out_grad,
    span_order,
    doc_starts,
    w_query,
    w_key,
    w_value,
    w_output,
    attn_gain,
    query_gain,
    key_gain,
    w_gate,
    w_up,
    w_down,
    mlp_gain,
):
    seqs, local, width = tokens.shape
    span = local // 2
    head_size = query_gain.shape[0]
    kv_heads = w_key.shape[1] // head_size
    heads = w_query.shape[1] // head_size
    share = heads // kv_heads
    kv_width = kv_heads * head_size
    ff_width = w_gate.shape[1]
    scale = 1.0 / math.sqrt(head_size)
    total_rows = seqs * local
    own_rows = width // lax.axis_size(("seq", "dp"))
    qpos = place(span_order, lax.axis_index("seq") * local, local, span)
    qdoc = doc_of(doc_starts, qpos)
    cosv, sinv = rotary(qpos, head_size)

    def gather_attn():
        return (
            lax.all_gather(w_query, ("seq", "dp"), axis=0, tiled=True),
            lax.all_gather(w_key, ("seq", "dp"), axis=0, tiled=True),
            lax.all_gather(w_value, ("seq", "dp"), axis=0, tiled=True),
            lax.all_gather(w_output, ("seq", "dp"), axis=0, tiled=True),
            lax.all_gather(
                attn_gain.astype(jnp.bfloat16), ("seq", "dp"), axis=0, tiled=True
            ).astype(attn_gain.dtype),
        )

    def gather_mlp():
        return (
            lax.all_gather(w_gate, ("seq", "dp"), axis=0, tiled=True),
            lax.all_gather(w_up, ("seq", "dp"), axis=0, tiled=True),
            lax.all_gather(w_down, ("seq", "dp"), axis=0, tiled=True),
            lax.all_gather(mlp_gain.astype(jnp.bfloat16), ("seq", "dp"), axis=0, tiled=True).astype(
                mlp_gain.dtype
            ),
        )

    x_rows = tokens.astype(jnp.float32).reshape(total_rows, width)
    wq_all, wk_all, wv_all, wo_all, ga_all = gather_attn()
    first_norm, first_inv = normed(x_rows, ga_all)
    first_in = first_norm.astype(jnp.bfloat16)
    q_raw = jnp.dot(first_in, wq_all, preferred_element_type=jnp.float32).reshape(
        seqs, local, heads, head_size
    )
    k_raw = jnp.dot(first_in, wk_all, preferred_element_type=jnp.float32).reshape(
        seqs, local, kv_heads, head_size
    )
    v_low = (
        jnp.dot(first_in, wv_all, preferred_element_type=jnp.float32)
        .astype(jnp.bfloat16)
        .reshape(seqs, local, kv_heads, head_size)
    )
    q_normed, q_inv = normed(q_raw, query_gain)
    k_normed, k_inv = normed(k_raw, key_gain)
    q_low = rotate(q_normed, cosv, sinv).astype(jnp.bfloat16)
    k_low = rotate(k_normed, cosv, sinv).astype(jnp.bfloat16)
    q_group = q_low.reshape(seqs, local, kv_heads, share, head_size)

    def scores(piece_key, start):
        count = piece_key.shape[1]
        kpos = place(span_order, start, count, span)
        kdoc = doc_of(doc_starts, kpos)
        visible = (qdoc[:, :, None] == kdoc[:, None, :]) & (
            kpos[None, None, :] <= qpos[None, :, None]
        )
        raw = (
            jnp.einsum("sqgjd,skgd->sgjqk", q_group, piece_key, preferred_element_type=jnp.float32)
            * scale
        )
        return (raw, visible[:, None, None])

    start_top = jnp.full((seqs, kv_heads, share, local), NEG, jnp.float32)
    piece = (
        lax.all_gather(k_low, "seq", axis=1, tiled=True),
        lax.all_gather(v_low, "seq", axis=1, tiled=True),
    )
    top = start_top
    raw, visible = scores(piece[0], jnp.int32(0))
    raw = jnp.where(visible, raw, NEG)
    new_top = jnp.maximum(top, jnp.max(raw, -1))
    weights = jnp.where(visible, jnp.exp(raw - new_top[..., None]), 0.0)
    total = jnp.sum(weights, -1)
    summed = jnp.einsum(
        "sgjqk,skgd->sgjqd",
        weights.astype(jnp.bfloat16),
        piece[1],
        preferred_element_type=jnp.float32,
    )
    top, total, summed = (new_top, total, summed)
    log_total = top + jnp.log(total)
    attn_vals = summed / total[..., None]
    out_low = (
        jnp.transpose(attn_vals, (0, 3, 1, 2, 4))
        .reshape(total_rows, heads * head_size)
        .astype(jnp.bfloat16)
    )
    resid = x_rows + jnp.einsum("nh,dh->nd", out_low, wo_all, preferred_element_type=jnp.float32)
    wg_all, wu_all, wd_all, gm_all = gather_mlp()
    second_norm, second_inv = normed(resid, gm_all)
    second_in = second_norm.astype(jnp.bfloat16)
    gate = jnp.dot(second_in, wg_all, preferred_element_type=jnp.float32)
    upper = jnp.dot(second_in, wu_all, preferred_element_type=jnp.float32)
    sigma = jax.nn.sigmoid(gate)
    act = gate * sigma
    hidden = (act * upper).astype(jnp.bfloat16)
    result = resid + jnp.einsum("nf,df->nd", hidden, wd_all, preferred_element_type=jnp.float32)
    block_out = result.astype(jnp.bfloat16).reshape(seqs, local, width)
    grad_low = out_grad.reshape(total_rows, width)
    wg_all, wu_all, wd_all, gm_all = gather_mlp()
    dmid = jnp.einsum("nd,df->nf", grad_low, wd_all, preferred_element_type=jnp.float32)
    dgate = (dmid * upper * sigma * (1.0 + gate * (1.0 - sigma))).astype(jnp.bfloat16)
    dupper = (dmid * act).astype(jnp.bfloat16)
    left = second_in
    outer = grad_low
    mlp_sums = lax.psum_scatter(
        jnp.concatenate(
            [
                jnp.einsum("nd,nf->df", left, dgate, preferred_element_type=jnp.float32),
                jnp.einsum("nd,nf->df", left, dupper, preferred_element_type=jnp.float32),
                jnp.einsum("nd,nf->df", outer, hidden, preferred_element_type=jnp.float32),
            ],
            1,
        ),
        ("seq", "dp"),
        scatter_dimension=0,
        tiled=True,
    )
    dsecond = jnp.einsum(
        "nf,df->nd", dgate, wg_all, preferred_element_type=jnp.float32
    ) + jnp.einsum("nf,df->nd", dupper, wu_all, preferred_element_type=jnp.float32)
    dresid_norm, dgm = norm_back(resid, second_inv, gm_all, dsecond)
    dresid = grad_low.astype(jnp.float32) + dresid_norm
    dresid_low = dresid.astype(jnp.bfloat16)
    wq_all, wk_all, wv_all, wo_all, ga_all = gather_attn()
    dout_low = jnp.einsum(
        "nd,dh->nh", dresid_low, wo_all, preferred_element_type=jnp.float32
    ).astype(jnp.bfloat16)
    dout_group = dout_low.reshape(seqs, local, kv_heads, share, head_size)
    delta = jnp.sum(jnp.transpose(dout_group.astype(jnp.float32), (0, 2, 3, 1, 4)) * attn_vals, -1)
    piece = (
        lax.all_gather(k_low, "seq", axis=1, tiled=True),
        lax.all_gather(v_low, "seq", axis=1, tiled=True),
    )
    count = piece[0].shape[1]
    raw, visible = scores(piece[0], jnp.int32(0))
    prob = jnp.where(visible, jnp.exp(raw - log_total[..., None]), 0.0)
    dprob = jnp.einsum(
        "sqgjd,skgd->sgjqk", dout_group, piece[1], preferred_element_type=jnp.float32
    )
    dscore = (prob * (dprob - delta[..., None])).astype(jnp.bfloat16)
    dq_sum = jnp.einsum("sgjqk,skgd->sqgjd", dscore, piece[0], preferred_element_type=jnp.float32)
    dk_part = (
        jnp.einsum("sgjqk,sqgjd->skgd", dscore, q_group, preferred_element_type=jnp.float32) * scale
    )
    dv_part = jnp.einsum(
        "sgjqk,sqgjd->skgd",
        prob.astype(jnp.bfloat16),
        dout_group,
        preferred_element_type=jnp.float32,
    )
    joined = jnp.concatenate(
        [dk_part.reshape(seqs, count, kv_width), dv_part.reshape(seqs, count, kv_width)], -1
    )
    buffer = joined
    dq_sum, buffer = (dq_sum, buffer)
    key_sums = lax.psum_scatter(
        buffer.astype(jnp.bfloat16), "seq", scatter_dimension=1, tiled=True
    ).astype(jnp.float32)
    dq_rot = (dq_sum * scale).reshape(seqs, local, heads, head_size)
    dq_raw, dgq = norm_back(q_raw, q_inv, query_gain, rotate_back(dq_rot, cosv, sinv))
    dk_rot = key_sums[..., :kv_width].reshape(seqs, local, kv_heads, head_size)
    dk_raw, dgk = norm_back(k_raw, k_inv, key_gain, rotate_back(dk_rot, cosv, sinv))
    dq_low = dq_raw.reshape(total_rows, heads * head_size).astype(jnp.bfloat16)
    dk_low = dk_raw.reshape(total_rows, kv_width).astype(jnp.bfloat16)
    dv_low = key_sums[..., kv_width:].reshape(total_rows, kv_width).astype(jnp.bfloat16)
    left = first_in
    outer = dresid_low
    attn_sums = lax.psum_scatter(
        jnp.concatenate(
            [
                jnp.einsum("nd,nh->dh", left, dq_low, preferred_element_type=jnp.float32),
                jnp.einsum("nd,nh->dh", left, dk_low, preferred_element_type=jnp.float32),
                jnp.einsum("nd,nh->dh", left, dv_low, preferred_element_type=jnp.float32),
                jnp.einsum("nd,nh->dh", outer, out_low, preferred_element_type=jnp.float32),
            ],
            1,
        ),
        ("seq", "dp"),
        scatter_dimension=0,
        tiled=True,
    )
    dfirst = jnp.einsum("nh,dh->nd", dq_low, wq_all, preferred_element_type=jnp.float32)
    dfirst = dfirst + jnp.einsum("nh,dh->nd", dk_low, wk_all, preferred_element_type=jnp.float32)
    dfirst = dfirst + jnp.einsum("nh,dh->nd", dv_low, wv_all, preferred_element_type=jnp.float32)
    dx_norm, dga = norm_back(x_rows, first_inv, ga_all, dfirst)
    tokens_grad = (dresid + dx_norm).reshape(seqs, local, width)
    dga_all, dgm_all, dgq_all, dgk_all = lax.psum((dga, dgm, dgq, dgk), ("seq", "dp"))
    offset = lax.axis_index(("seq", "dp")) * own_rows
    attn_gain_grad = lax.dynamic_slice_in_dim(dga_all, offset, own_rows, 0)
    mlp_gain_grad = lax.dynamic_slice_in_dim(dgm_all, offset, own_rows, 0)
    q_cols = heads * head_size
    w_query_grad = attn_sums[:, :q_cols]
    w_key_grad = attn_sums[:, q_cols : q_cols + kv_width]
    w_value_grad = attn_sums[:, q_cols + kv_width : q_cols + 2 * kv_width]
    w_output_grad = attn_sums[:, q_cols + 2 * kv_width :]
    w_gate_grad = mlp_sums[:, :ff_width]
    w_up_grad = mlp_sums[:, ff_width : 2 * ff_width]
    w_down_grad = mlp_sums[:, 2 * ff_width :]
    return (
        block_out,
        tokens_grad,
        w_query_grad,
        w_key_grad,
        w_value_grad,
        w_output_grad,
        attn_gain_grad,
        dgq_all,
        dgk_all,
        w_gate_grad,
        w_up_grad,
        w_down_grad,
        mlp_gain_grad,
    )


LOW = jnp.bfloat16
MESH = pl.DeviceIdType.MESH
LIMIT = 60 * 2**20


def ring_order(ranks):
    half = ranks // 2
    order = [0]
    for step in range(1, half):
        order += [step, ranks - step]
    return order + [half]


def ring_place(seq, ranks):
    z, x = lax.div(seq, 2), lax.rem(seq, 2)
    return z + x * (ranks - 1 - 2 * z)


def ring_seq(place, ranks):
    half = ranks // 2
    x, z = lax.div(place, half), lax.rem(place, half)
    return 2 * (z + x * (half - 1 - 2 * z)) + x


def neighbours(ranks):
    seq, dp = lax.axis_index("seq"), lax.axis_index("dp")
    at = ring_place(seq, ranks)
    right = ring_seq(lax.rem(at + 1, ranks), ranks)
    left = ring_seq(lax.rem(at + ranks - 1, ranks), ranks)
    return (right, dp), (left, dp)


def knock(devices):
    barrier = pltpu.get_barrier_semaphore()
    for device in devices:
        pl.semaphore_signal(barrier, inc=1, device_id=device, device_id_type=MESH)


def answered(devices):
    pl.semaphore_wait(pltpu.get_barrier_semaphore(), len(devices))


def move(src, dst, sem):
    copy = pltpu.make_async_copy(src, dst, sem)
    copy.start()
    return copy


def push(src, dst, send, recv, device):
    return pltpu.make_async_remote_copy(
        src_ref=src, dst_ref=dst, send_sem=send, recv_sem=recv, device_id=device, device_id_type=MESH
    )


def dot_nn(left, right):
    return jnp.dot(left, right, preferred_element_type=jnp.float32)


def dot_nt(left, right):
    return lax.dot_general(left, right, (((1,), (1,)), ((), ())), preferred_element_type=jnp.float32)


def dot_tn(left, right):
    return lax.dot_general(left, right, (((0,), (0,)), ((), ())), preferred_element_type=jnp.float32)


def block_row(rel, local, ranks):
    place = ring_place(lax.axis_index("seq"), ranks)
    return pl.multiple_of(ring_seq(lax.rem(place + rel, ranks), ranks) * local, local)


def block_rows(ref, rels, local, ranks):
    blocks = [ref[pl.ds(block_row(rel, local, ranks), local)] for rel in rels]
    return blocks[0] if len(blocks) == 1 else jnp.concatenate(blocks, 0)


def rels_of(step, ranks):
    return [rel for rel in ring_order(ranks) if min(rel, ranks - rel) == step]


class RingGather:
    def __init__(self, buf, local, ranks, send, recv, right, left, row):
        self.buf, self.sub, self.half = buf, local // 2, ranks // 2
        self.send, self.recv, self.right, self.left = send, recv, right, left
        self.ranks, self.row = ranks, row

    def copies(self, step, part):
        ways = ((0, (self.ranks - step + 1) % self.ranks, self.right), (1, step - 1, self.left))
        given = []
        for way, rel, device in ways:
            if step < self.half or way == part:
                block = self.buf.at[pl.ds(self.row(rel) + part * self.sub, self.sub)]
                at = 2 * (step - 1) + part
                given.append(push(block, block, self.send.at[way, at], self.recv.at[way, at], device))
        return given

    def start(self, step):
        for part in range(2):
            for copy in self.copies(step, part):
                copy.start()

    def advance(self, step):
        for part in range(2):
            for copy in self.copies(step, part):
                copy.wait_recv()
            if step < self.half:
                for copy in self.copies(step + 1, part):
                    copy.start()

    def finish(self):
        for step in range(1, self.half + 1):
            for part in range(2):
                for copy in self.copies(step, part):
                    copy.wait_send()


class LineGather:
    def __init__(self, buf, local, ranks, send, recv, x_send, x_recv):
        self.buf, self.local, self.length = buf, local, ranks // 2
        self.send, self.recv, self.x_send, self.x_recv = send, recv, x_send, x_recv
        self.seq, self.dp = lax.axis_index("seq"), lax.axis_index("dp")
        self.z, self.x = lax.div(self.seq, 2), lax.rem(self.seq, 2)

    def block(self, z):
        return self.buf.at[pl.ds(pl.multiple_of((2 * z + self.x) * self.local, self.local), self.local)]

    def hop(self, way, step):
        block = self.block(self.z + (step - 1 if way else 1 - step))
        to = self.seq + (-2 if way else 2)
        return push(block, block, self.send.at[way, step - 1], self.recv.at[way, step - 1], (to, self.dp))

    def sends(self, way, step):
        if way:
            return (self.z > 0) & (self.z + step <= self.length)
        return (self.z < self.length - 1) & (self.z >= step - 1)

    def comes(self, way, step):
        return self.z + step < self.length if way else self.z >= step

    def across(self, way, step):
        block = self.block(self.z + (step if way else -step))
        at = step + way * (self.length - 1)
        return push(
            block, block, self.x_send.at[at], self.x_recv.at[at], (self.seq + 1 - 2 * self.x, self.dp)
        )

    def from_x(self, way, step):
        z = self.z + (step if way else -step)
        row = pl.multiple_of((2 * z + 1 - self.x) * self.local, self.local)
        block = self.buf.at[pl.ds(row, self.local)]
        at = step + way * (self.length - 1)
        return push(
            block, block, self.x_send.at[at], self.x_recv.at[at], (self.seq + 1 - 2 * self.x, self.dp)
        )

    def start(self, step):
        for way in range(2):
            pl.when(self.sends(way, step))(lambda way=way: self.hop(way, step).start())
        self.pass_on(step - 1)

    def pass_on(self, step):
        if step == 0:
            self.across(0, 0).start()
            return
        for way in range(2):
            pl.when(self.comes(way, step))(lambda way=way: self.across(way, step).start())

    def arrive(self, step):
        for way in range(2):
            pl.when(self.comes(way, step))(lambda way=way: self.incoming(way, step).wait_recv())

    def incoming(self, way, step):
        block = self.block(self.z + (step if way else -step))
        to = self.seq + 1 - 2 * self.x
        return push(block, block, self.send.at[way, step - 1], self.recv.at[way, step - 1], (to, self.dp))

    def run(self):
        for step in range(1, self.length):
            self.advance(step)

    def advance(self, step):
        self.arrive(step)
        if step < self.length - 1:
            self.start(step + 1)
        else:
            self.pass_on(step)

    def complete(self):
        self.from_x(0, 0).wait_recv()
        for step in range(1, self.length):
            for way in range(2):
                pl.when(self.comes(way, step))(lambda way=way: self.from_x(way, step).wait_recv())

    def finish(self):
        self.across(0, 0).wait_send()
        for step in range(1, self.length):
            for way in range(2):
                pl.when(self.sends(way, step))(lambda way=way: self.hop(way, step).wait_send())
                pl.when(self.comes(way, step))(lambda way=way: self.across(way, step).wait_send())


def line_sems(ranks):
    half = ranks // 2
    return [pltpu.SemaphoreType.DMA((2, half))] * 2 + [pltpu.SemaphoreType.DMA((2 * half,))] * 2


class RingSum:
    def __init__(self, part, term, out_buf, in_buf, local, ranks, send, recv, right, left, stream=0, streams=1):
        self.part, self.term, self.out_buf, self.in_buf = part, term, out_buf, in_buf
        self.local, self.ranks, self.half = local, ranks, ranks // 2
        each = term.shape[1] // streams
        self.cols = pl.ds(stream * each, each)
        self.tiles = (stream * ranks // streams, (stream + 1) * ranks // streams)
        self.send, self.recv, self.right, self.left = send, recv, right, left

    def copies(self, step):
        rows = self.local // 2 if step == 1 else self.local
        skip = self.local // 2 if step == 1 else 0
        return [
            push(
                self.out_buf.at[way, (step - 1) % 2, pl.ds(begin, rows), self.cols],
                self.in_buf.at[way, step - 1, pl.ds(begin, rows), self.cols],
                self.send.at[way, step - 1],
                self.recv.at[way, step - 1],
                device,
            )
            for way, begin, device in ((0, 0, self.right), (1, skip, self.left))
        ]

    def compute(self, step):
        if step == 1:
            self.part([self.half], *self.tiles)
        elif step <= self.half:
            self.part(rels_of(self.half + 1 - step, self.ranks), *self.tiles)
        else:
            self.part([0], *self.tiles)

    def launch(self, step):
        local, skip = self.local, self.local // 2
        if step > 2:
            for copy in self.copies(step - 2):
                copy.wait_send()
        if step == 1:
            for way in range(2):
                rows = pl.ds(way * skip, skip)
                self.out_buf[way, 0, rows, self.cols] = self.term[rows, self.cols].astype(LOW)
        else:
            for copy in self.copies(step - 1):
                copy.wait_recv()
            for way in range(2):
                for begin, with_sum in ((0, step > 2 or way == 0), (skip, step > 2 or way == 1)):
                    value = self.term[pl.ds(way * local + begin, skip), self.cols]
                    if with_sum:
                        value = value + self.in_buf[way, step - 2, pl.ds(begin, skip), self.cols].astype(jnp.float32)
                    self.out_buf[way, (step - 1) % 2, pl.ds(begin, skip), self.cols] = value.astype(LOW)
        for copy in self.copies(step):
            copy.start()

    def last(self, begin, count):
        rows = pl.ds(begin, count)
        value = self.term[rows, self.cols] + self.in_buf[0, self.half - 1, rows, self.cols].astype(jnp.float32)
        return value + self.in_buf[1, self.half - 1, rows, self.cols].astype(jnp.float32)

    def arrive_last(self):
        for copy in self.copies(self.half):
            copy.wait_recv()

    def finish(self):
        for step in range(max(1, self.half - 1), self.half + 1):
            for copy in self.copies(step):
                copy.wait_send()


def two_sums(part, term, out_buf, in_buf, local, ranks, sems, right, left):
    return [
        RingSum(
            part, term, out_buf, in_buf, local, ranks, sems[2 * at], sems[2 * at + 1], right, left, at, 2
        )
        for at in range(2)
    ]


def ring_sems(ranks):
    return [pltpu.SemaphoreType.DMA((2, ranks)), pltpu.SemaphoreType.DMA((2, ranks))]


def sum_bufs(local, ranks, width):
    return [
        pltpu.VMEM((2 * local, width), jnp.float32),
        pltpu.VMEM((2, 2, local, width), LOW),
        pltpu.VMEM((2, ranks // 2, local, width), LOW),
    ]


def turn(v):
    return pltpu.roll(v, v.shape[-1] // 2, v.ndim - 1)


def rows_scaled(v):
    inv = lax.rsqrt(jnp.mean(v * v, -1, keepdims=True) + EPS)
    return v * inv, inv


def rows_scaled_back(v, inv, grad):
    return inv * grad - v * (inv * inv * inv * jnp.mean(grad * v, -1, keepdims=True))


class Spread:
    def __init__(self, rows, block, ranks, own, cols, sems):
        self.rows, self.block, self.ranks, self.own, self.cols = rows, block, ranks, own, cols
        self.send, self.recv, self.hop_send, self.hop_recv, self.here = sems
        self.seq, self.dp = lax.axis_index("seq"), lax.axis_index("dp")
        y, core = lax.div(self.dp, 2), lax.rem(self.dp, 2)
        self.beside, self.sibling = (1 - y) * 2 + core, y * 2 + 1 - core

    def at(self, dp):
        return pl.ds(pl.multiple_of(dp * self.own, self.own), self.own)

    def exchange(self):
        for step in range(1, self.ranks):
            peer = lax.rem(self.seq + step, self.ranks)
            yield push(
                self.rows.at[peer, :, self.cols],
                self.block.at[self.seq, self.at(self.dp), self.cols],
                self.send.at[step],
                self.recv.at[step],
                (peer, self.dp),
            )

    def keep(self):
        return pltpu.make_async_copy(
            self.rows.at[self.seq, :, self.cols],
            self.block.at[self.seq, self.at(self.dp), self.cols],
            self.here,
        )

    def hop(self, number):
        dp = self.beside if number == 2 else self.dp
        part = self.block.at[:, self.at(dp), self.cols]
        to = self.beside if number == 0 else self.sibling
        return push(part, part, self.hop_send.at[number], self.hop_recv.at[number], (self.seq, to))

    def start(self):
        self.keep().start()
        for copy in self.exchange():
            copy.start()

    def arrive(self):
        self.keep().wait()
        for copy in self.exchange():
            copy.wait_recv()

    def finish(self):
        for copy in self.exchange():
            copy.wait_send()
        for number in range(3):
            self.hop(number).wait_send()


def spread_sems(ranks):
    return [
        pltpu.SemaphoreType.DMA((ranks,)),
        pltpu.SemaphoreType.DMA((ranks,)),
        pltpu.SemaphoreType.DMA((3,)),
        pltpu.SemaphoreType.DMA((3,)),
        pltpu.SemaphoreType.DMA,
    ]


class WholeGather:
    def __init__(self, block, ranks, own, sems):
        self.block, self.ranks, self.half, self.own = block, ranks, ranks // 2, own
        self.send, self.recv, self.y_send, self.y_recv, self.core_send, self.core_recv = sems
        self.seq, self.dp = lax.axis_index("seq"), lax.axis_index("dp")
        self.right, self.left = neighbours(ranks)
        self.place = ring_place(self.seq, ranks)
        y, core = lax.div(self.dp, 2), lax.rem(self.dp, 2)
        self.beside, self.sibling = (1 - y) * 2 + core, y * 2 + 1 - core

    def at(self, rel, dp, begin, count):
        seq = ring_seq(lax.rem(self.place + rel + self.ranks, self.ranks), self.ranks)
        return self.block.at[seq, pl.ds(pl.multiple_of(dp * self.own + begin, count), count)]

    def copies(self, step):
        last = step == self.half
        rows = self.own // 2 if last else self.own
        skip = self.own // 2 if last else 0
        given = []
        for way, rel, begin, device in ((0, 1 - step, 0, self.right), (1, step - 1, skip, self.left)):
            part = self.at(rel, self.dp, begin, rows)
            given.append(push(part, part, self.send.at[way, step - 1], self.recv.at[way, step - 1], device))
        return given

    def start(self, step):
        for copy in self.copies(step):
            copy.start()

    def hops(self, step):
        for at, rel in enumerate(ring_order(self.ranks)):
            if min(rel, self.ranks - rel) == step:
                part = self.at(rel, self.dp, 0, self.own)
                yield push(part, part, self.y_send.at[at], self.y_recv.at[at], (self.seq, self.beside))
                yield push(part, part, self.core_send.at[at], self.core_recv.at[at], (self.seq, self.sibling))

    def arrive(self, step):
        for copy in self.copies(step):
            copy.wait_recv()

    def forward(self, step):
        for copy in self.hops(step):
            copy.start()

    def cross(self):
        part = self.block.at[:, pl.ds(pl.multiple_of(self.beside * self.own, self.own), self.own)]
        at = self.ranks
        return push(part, part, self.core_send.at[at], self.core_recv.at[at], (self.seq, self.sibling))

    def complete(self):
        for step in range(self.half + 1):
            for copy in self.hops(step):
                copy.wait_recv()
        self.cross().start()
        self.cross().wait_recv()

    def finish(self):
        for step in range(1, self.half + 1):
            for copy in self.copies(step):
                copy.wait_send()
        for step in range(self.half + 1):
            for copy in self.hops(step):
                copy.wait_send()
        self.cross().wait_send()


def whole_sems(ranks):
    return (
        ring_sems(ranks)
        + [pltpu.SemaphoreType.DMA((ranks,))] * 2
        + [pltpu.SemaphoreType.DMA((ranks + 1,))] * 2
    )


class Reduce:
    def __init__(self, grads, from_core, from_y, total, own, first, count, cols, sems):
        self.grads, self.from_core, self.from_y, self.total = grads, from_core, from_y, total
        self.own, self.begin, self.count, self.cols = own, first, count, cols
        self.send, self.recv = sems
        self.seq, dp = lax.axis_index("seq"), lax.axis_index("dp")
        self.y, self.core = lax.div(dp, 2), lax.rem(dp, 2)
        self.beside, self.sibling = (1 - self.y) * 2 + self.core, self.y * 2 + 1 - self.core

    def at(self, y, core):
        return pl.ds(pl.multiple_of((y * 2 + core) * self.own, self.own), self.own)

    def hop(self, number):
        some, cols = pl.ds(self.begin, self.count), self.cols
        if number == 2:
            src, dst, to = self.from_core.at[0, some, :, cols], self.from_y.at[some, :, cols], self.beside
        else:
            rows = self.at(1 - self.y if number == 0 else self.y, 1 - self.core)
            src, dst, to = self.grads.at[some, rows, cols], self.from_core.at[number, some, :, cols], self.sibling
        return push(src, dst, self.send.at[number], self.recv.at[number], (self.seq, to))

    def first(self):
        self.hop(0).start()
        self.hop(1).start()

    def second(self):
        self.hop(0).wait_recv()
        rows = self.at(1 - self.y, self.core)

        def some(at, _):
            value = self.grads[at, rows, self.cols].astype(jnp.float32)
            value = value + self.from_core[0, at, :, self.cols].astype(jnp.float32)
            self.from_core[0, at, :, self.cols] = value.astype(LOW)
            return 0

        lax.fori_loop(self.begin, self.begin + self.count, some, 0)
        self.hop(2).start()

    def third(self):
        self.hop(1).wait_recv()
        self.hop(2).wait_recv()
        rows = self.at(self.y, self.core)

        def some(at, _):
            value = self.grads[at, rows, self.cols].astype(jnp.float32)
            value = value + self.from_core[1, at, :, self.cols].astype(jnp.float32)
            value = value + self.from_y[at, :, self.cols].astype(jnp.float32)
            self.total[at, :, self.cols] = value.astype(LOW)
            return 0

        lax.fori_loop(self.begin, self.begin + self.count, some, 0)

    def finish(self):
        for number in range(3):
            self.hop(number).wait_send()


def reduce_sems():
    return [pltpu.SemaphoreType.DMA((3,)), pltpu.SemaphoreType.DMA((3,))]


def reduce_bufs(ranks, own, cols):
    return [pltpu.VMEM((2, ranks, own, cols), LOW), pltpu.VMEM((ranks, own, cols), LOW)]


class Deliver:
    def __init__(self, rows, out, cols, ranks, sems):
        self.rows, self.out, self.cols, self.ranks = rows, out, cols, ranks
        self.send, self.recv, self.here = sems
        self.seq, self.dp = lax.axis_index("seq"), lax.axis_index("dp")

    def exchange(self):
        for step in range(1, self.ranks):
            peer = lax.rem(self.seq + step, self.ranks)
            yield push(
                self.rows.at[peer, :, self.cols],
                self.out.at[self.seq, :, self.cols],
                self.send.at[step],
                self.recv.at[step],
                (peer, self.dp),
            )

    def keep(self):
        return pltpu.make_async_copy(
            self.rows.at[self.seq, :, self.cols], self.out.at[self.seq, :, self.cols], self.here
        )

    def start(self):
        self.keep().start()
        for copy in self.exchange():
            copy.start()

    def finish(self):
        self.keep().wait()
        for copy in self.exchange():
            copy.wait_recv()
        for copy in self.exchange():
            copy.wait_send()


def deliver_sems(ranks):
    return [pltpu.SemaphoreType.DMA((ranks,)), pltpu.SemaphoreType.DMA((ranks,)), pltpu.SemaphoreType.DMA]


def first_kernel(
    ranks, kv_heads, order, starts, tokens, out_grad, freqs, attn_gain, mlp_gain, query_gain, key_gain,
    w_query, w_key, w_value, w_output, w_gate, w_up, w_down,
    resid, second, cosv, sinv, q_low, k_low, v_low, own_out, first_in, qkv, attn_block, dy_all, prob, mlp_block, out_all,
    held, normal, kept, block, a_rows, m_rows, gate, up, down, dys, probs, pos, begins, pos_row,
    out_low, whole, *sems,
):
    local, width = tokens.shape
    rows = local * ranks
    own = w_query.shape[0]
    size = freqs.shape[1]
    heads = q_low.shape[0]
    share = heads // kv_heads
    half = ranks // 2
    scale = 1.0 / math.sqrt(size)
    cols = (heads + 2 * kv_heads) * size
    deep = block.shape[1]
    row = functools.partial(block_row, local=local, ranks=ranks)
    seq, dp = lax.axis_index("seq"), lax.axis_index("dp")
    right, left = neighbours(ranks)
    attn = Spread(a_rows, block, ranks, own, pl.ds(0, a_rows.shape[2]), sems[12:17])
    third = m_rows.shape[2] // 3
    mlp = [
        Spread(m_rows, mlp_block, ranks, own, pl.ds(at * third, third), sems[17 + 5 * at : 22 + 5 * at])
        for at in range(3)
    ]
    local_sems = sems[32]
    out_send, out_recv = sems[2:4]
    o_cols = heads * size
    peers = [(lax.rem(seq + step, ranks), dp) for step in range(1, ranks)]
    peers += [(seq, attn.beside), (seq, attn.sibling)]
    knock(peers)
    loads = [
        move(src, dst, local_sems.at[at])
        for at, (src, dst) in enumerate(((w_gate, gate), (w_up, up), (w_down, down)))
    ]
    held[pl.ds(row(0), local)] = tokens[...]
    dys[pl.ds(row(0), local)] = out_grad[...]

    def column(line):
        same = lax.broadcasted_iota(jnp.int32, (own, own), 0) == lax.broadcasted_iota(jnp.int32, (own, own), 1)
        return jnp.sum(jnp.where(same, line, 0.0), 1, keepdims=True)

    def lay(target, begin, weight, gain):
        each = weight.shape[1] // ranks
        for rank in range(ranks):
            part = weight[:, rank * each : (rank + 1) * each]
            if gain is not None:
                part = (part.astype(jnp.float32) * gain).astype(LOW)
            target[rank, :, begin : begin + each] = part
        return begin + each

    gain = column(attn_gain[...])
    at = 0
    for weight in (w_query, w_key, w_value):
        at = lay(a_rows, at, weight, gain)
    whole[seq, pl.ds(pl.multiple_of(dp * own, own), own)] = w_output[...]
    answered(peers)
    ring = RingGather(held, local, ranks, sems[0], sems[1], right, left, row)
    ring.start(1)
    attn.start()
    outs = WholeGather(whole, ranks, own, [*sems[8:12], *sems[33:35]])
    outs.forward(0)
    line = LineGather(dys, local, ranks, sems[4], sems[5], sems[6], sems[7])
    stores = []

    def store(src, dst):
        stores.append(move(src, dst, local_sems.at[len(loads) + len(stores)]))

    def scale_rows(step):
        for rel in rels_of(step, ranks):

            def some(at, _):
                rows_at = pl.ds(pl.multiple_of(row(rel) + at * 32, 32), 32)
                normal[rows_at] = rows_scaled(held[rows_at].astype(jnp.float32))[0].astype(LOW)
                return 0

            lax.fori_loop(0, local // 32, some, 0)

    for load in loads:
        load.wait()
    gain = column(mlp_gain[...])
    each = gate.shape[1] // ranks
    lay(m_rows, 0, gate, gain)
    lay(m_rows, each, up, gain)
    lay(m_rows, 2 * each, down, None)
    scale_rows(0)
    ring.advance(1)
    scale_rows(1)
    attn.arrive()
    attn.hop(0).start()
    attn.hop(1).start()
    spans = order.shape[0]
    span = rows // spans
    for at in range(ranks):
        rows_at = pl.ds(at * local, local)
        ids = at * local + lax.broadcasted_iota(jnp.int32, (1, local), 1)
        where = jnp.zeros_like(ids)
        for slot in range(spans):
            inside = (ids >= slot * span) & (ids < (slot + 1) * span)
            where = where + jnp.where(inside, ids + (order[slot] - slot) * span, 0)
        begin = jnp.zeros_like(ids)
        for doc in range(starts.shape[1]):
            begin = jnp.maximum(begin, jnp.where(starts[0, doc] <= where, starts[0, doc], 0))
        pos_row[:, rows_at] = where
        across = jnp.broadcast_to(where, (local, local)).T
        pos[rows_at] = across[:, :1]
        begins[rows_at] = jnp.broadcast_to(begin, (local, local)).T[:, :1]
        angle = across[:, :1].astype(jnp.float32) * freqs[...]
        lane = lax.broadcasted_iota(jnp.int32, (local, size), 1)
        cosv[rows_at] = jnp.cos(angle)
        sine = jnp.sin(angle)
        sinv[rows_at] = jnp.where(lane < size // 2, -sine, sine)
    for step in range(2, half):
        ring.advance(step)
        scale_rows(step)
        if step == 2:
            outs.start(1)
            attn.hop(0).wait_recv()
            attn.hop(2).start()

    def bring(step):
        outs.arrive(step)
        if step < half:
            outs.start(step + 1)
        outs.forward(step)

    bring(1)
    line.start(1)
    attn.hop(1).wait_recv()
    attn.hop(2).wait_recv()
    store(block, attn_block)

    def project(begin, count):
        rows_at = pl.ds(begin, count)
        kept[rows_at] = dot_nn(normal[rows_at], block[...].reshape(width, cols))

    ring.advance(half)
    bring(2)
    mlp[0].start()
    scale_rows(half)
    store(normal, first_in)
    tile = rows // half

    def rotated(at, rows_at, gain):
        v = rows_scaled(kept[rows_at, at * size : (at + 1) * size])[0] * gain[...]
        return (v * cosv[rows_at] + turn(v) * sinv[rows_at]).astype(LOW)

    for piece in range(half):
        rows_at = pl.ds(piece * tile, tile)
        project(piece * tile, tile)
        for head in range(heads):
            q_low[head, rows_at] = rotated(head, rows_at, query_gain)
        for group in range(kv_heads):
            k_low[group, rows_at] = rotated(heads + group, rows_at, key_gain)
            at = (heads + kv_heads + group) * size
            v_low[group, rows_at] = kept[rows_at, at : at + size].astype(LOW)
    store(kept, qkv)
    bring(3)
    line.advance(1)
    mlp[1].start()

    def forward(piece):
        mlp[piece].arrive()
        mlp[piece].hop(0).start()
        mlp[piece].hop(1).start()

    for piece in range(half):
        rows_at = pl.ds(piece * tile, tile)
        seen = (pos_row[...] <= pos[rows_at]) & (pos_row[...] >= begins[rows_at])
        for head in range(heads):
            raw = dot_nt(q_low[head, rows_at], k_low[head // share]) * scale
            raw = jnp.where(seen, raw, NEG)
            weight = jnp.exp(raw - jnp.max(raw, -1, keepdims=True))
            weight = (weight * (1.0 / jnp.sum(weight, -1, keepdims=True))).astype(LOW)
            probs[head, rows_at] = weight
            value = dot_nn(weight, v_low[head // share])
            out_low[rows_at, head * size : (head + 1) * size] = value.astype(LOW)
            store(probs.at[head, rows_at], prob.at[head, rows_at])
        if piece == 0:
            bring(half)
            mlp[2].start()
        if piece == 1:
            forward(0)
        if piece == half - 1:
            line.advance(2)
    place = ring_place(seq, ranks)

    def exchange(rel):
        to = ring_seq(lax.rem(place + rel, ranks), ranks)
        return push(
            out_low.at[pl.ds(row(rel), local)],
            own_out.at[:, pl.ds(pl.multiple_of(seq * o_cols, o_cols), o_cols)],
            out_send.at[rel],
            out_recv.at[rel],
            (to, dp),
        )

    for rel in range(1, ranks):
        exchange(rel).start()
    own_out[:, pl.ds(pl.multiple_of(seq * o_cols, o_cols), o_cols)] = out_low[pl.ds(row(0), local)]
    forward(1)
    for step in range(3, half):
        line.advance(step)
    outs.complete()
    store(whole, out_all)
    forward(2)
    mlp[0].hop(0).wait_recv()
    mlp[0].hop(2).start()
    for rel in range(1, ranks):
        exchange(rel).wait_recv()

    def join(at, _):
        some = pl.ds(pl.multiple_of(at * deep, deep), deep)
        resid[:, some] = tokens[:, some].astype(jnp.float32) + dot_nt(own_out[...], whole[at])
        return 0

    lax.fori_loop(0, ranks, join, 0)

    def scale_second(at, _):
        rows_at = pl.ds(pl.multiple_of(at * 32, 32), 32)
        second[rows_at] = rows_scaled(resid[rows_at])[0].astype(LOW)
        return 0

    lax.fori_loop(0, local // 32, scale_second, 0)
    for piece in mlp[1:]:
        piece.hop(0).wait_recv()
        piece.hop(2).start()
    line.complete()
    store(dys, dy_all)
    ring.finish()
    attn.finish()
    outs.finish()
    for rel in range(1, ranks):
        exchange(rel).wait_send()
    line.finish()
    for piece in mlp:
        piece.hop(1).wait_recv()
        piece.hop(2).wait_recv()
        piece.finish()
    for given in stores:
        given.wait()


def mlp_kernel(
    ranks, second, out_grad, rest, dys, mlp_block, block_out, dresid, dresid_low, own_grads,
    grads, from_core, from_y, held, weights, hidden, dgu, resid, dy_all,
    term, out_buf, in_buf, y_out, y_in, here, *sems,
):
    local, width = second.shape
    row = functools.partial(block_row, local=local, ranks=ranks)
    ff = hidden.shape[1]
    deep = weights.shape[1]
    half = ranks // 2
    right, left = neighbours(ranks)
    loads = [
        move(src, dst, here.at[at])
        for at, (src, dst) in enumerate(((mlp_block, weights), (dys, dy_all), (rest, resid)))
    ]
    seq, dp = lax.axis_index("seq"), lax.axis_index("dp")
    own = own_grads.shape[1]
    pieces = [
        Reduce(
            grads, from_core, from_y, own_grads, own, at * ranks // 4, ranks // 4, pl.ds(0, 3 * ff),
            sems[6 + 2 * at : 8 + 2 * at],
        )
        for at in range(4)
    ]
    peers = [right, left, (seq, pieces[0].beside), (seq, pieces[0].sibling)]
    knock(peers)
    held[pl.ds(row(0), local)] = second[...]
    answered(peers)
    ring = RingGather(held, local, ranks, sems[0], sems[1], right, left, row)
    ring.start(1)
    loads[0].wait()
    loads[1].wait()
    wide = 256

    def middle(step):
        rels = rels_of(step, ranks)

        def some(at, _):
            first = pl.multiple_of(at * wide, wide)
            given, dy = block_rows(held, rels, local, ranks), block_rows(dy_all, rels, local, ranks)
            gate = dot_nn(given, weights[:, :, pl.ds(first, wide)].reshape(width, wide))
            upper = dot_nn(given, weights[:, :, pl.ds(ff + first, wide)].reshape(width, wide))
            dmid = dot_nn(dy, weights[:, :, pl.ds(2 * ff + first, wide)].reshape(width, wide))
            sigma = 1.0 / (1.0 + jnp.exp(-gate))
            act = gate * sigma
            value = (act * upper).astype(LOW)
            dgate = (dmid * upper * (sigma * (1.0 + gate * (1.0 - sigma)))).astype(LOW)
            dupper = (dmid * act).astype(LOW)
            for at, rel in enumerate(rels):
                rows, some_rows = pl.ds(row(rel), local), slice(at * local, (at + 1) * local)
                hidden[rows, pl.ds(first, wide)] = value[some_rows]
                dgu[rows, pl.ds(first, wide)] = dgate[some_rows]
                dgu[rows, pl.ds(ff + first, wide)] = dupper[some_rows]
            return 0

        lax.fori_loop(0, ff // wide, some, 0)

    middle(0)
    for step in range(1, half + 1):
        ring.advance(step)
        middle(step)

    def back_part(rels, begin, end):
        def some(at, _):
            value = dot_nt(block_rows(dgu, rels, local, ranks), weights[at, :, : 2 * ff])
            term[: len(rels) * local, pl.ds(pl.multiple_of(at * deep, deep), deep)] = value
            return 0

        lax.fori_loop(begin, end, some, 0)

    def out_part(rels, begin, end):
        def some(at, _):
            value = dot_nt(block_rows(hidden, rels, local, ranks), weights[at, :, 2 * ff :])
            term[: len(rels) * local, pl.ds(pl.multiple_of(at * deep, deep), deep)] = value
            return 0

        lax.fori_loop(begin, end, some, 0)

    def weight_grads(first, count):
        def some(at, _):
            cols = pl.ds(pl.multiple_of(at * deep, deep), deep)
            grads[at, :, : 2 * ff] = dot_tn(held[:, cols], dgu[...]).astype(LOW)
            grads[at, :, 2 * ff :] = dot_tn(dy_all[:, cols], hidden[...]).astype(LOW)
            return 0

        lax.fori_loop(first, first + count, some, 0)

    back = RingSum(back_part, term, out_buf, in_buf, local, ranks, sems[2], sems[3], right, left)
    out = RingSum(out_part, term, y_out, y_in, local, ranks, sems[4], sems[5], right, left)
    for step in range(1, half + 1):
        back.compute(step)
        back.launch(step)
        out.compute(step)
        out.launch(step)
        made, passed, summed = (((0, 1), (2,), (3,), ()), ((), (0, 1), (2,), (3,)), ((), (), (0, 1), (2,)))
        for piece in (pieces[at] for at in made[step - 1]):
            weight_grads(piece.begin, piece.count)
            piece.first()
        for at in passed[step - 1]:
            pieces[at].second()
        for at in summed[step - 1]:
            pieces[at].third()
    back.compute(half + 1)
    loads[2].wait()
    back.arrive_last()

    def finish_back(at, _):
        begin = pl.multiple_of(at * 32, 32)
        rows = pl.ds(begin, 32)
        value = resid[rows]
        inv = rows_scaled(value)[1]
        grad = back.last(begin, 32)
        full = out_grad[rows].astype(jnp.float32) + rows_scaled_back(value, inv, grad)
        dresid[rows] = full
        dresid_low[rows] = full.astype(LOW)
        return 0

    lax.fori_loop(0, local // 32, finish_back, 0)
    out.compute(half + 1)
    out.arrive_last()

    def finish_out(at, _):
        begin = pl.multiple_of(at * 32, 32)
        rows = pl.ds(begin, 32)
        block_out[rows] = (resid[rows] + out.last(begin, 32)).astype(LOW)
        return 0

    lax.fori_loop(0, local // 32, finish_out, 0)
    ring.finish()
    pieces[3].third()
    back.finish()
    out.finish()
    for piece in pieces:
        piece.finish()


def back_kernel(
    ranks, kv_heads, tokens, dresid_low, query_gain, key_gain, own_out, first_in_in, block_in,
    qkv_in, cos_in, sin_in, q_in, k_in, v_in, prob_in, dresid_in, mlp_own, out_all,
    tokens_grad, gains, out_grad, mlp_sums, attn_sums,
    grads, from_core, from_y, own_grads, query_gain_grad, key_gain_grad,
    tile, tiles_in, tile_sum, tile_sums_in, dob, dout, dk, dv, dqkv,
    first_in, attn_block, qkv, cosv, sinv, q_low, k_low, v_low, prob, dresid, term, out_buf, in_buf,
    o_grads, o_core, o_y, o_own, o_term, o_out, o_in, *sems,
):
    local, width = tokens.shape
    rows = local * ranks
    half = ranks // 2
    size = cosv.shape[1]
    heads = q_low.shape[0]
    share = heads // kv_heads
    scale = 1.0 / math.sqrt(size)
    cols = (heads + 2 * kv_heads) * size
    deep = attn_block.shape[1]
    o_cols = heads * size
    right, left = neighbours(ranks)
    seq, dp = lax.axis_index("seq"), lax.axis_index("dp")
    own = mlp_own.shape[1]
    copies = lax.axis_size("dp")
    row = functools.partial(block_row, local=local, ranks=ranks)
    place = ring_place(seq, ranks)
    out_piece = Reduce(o_grads, o_core, o_y, o_own, own, 0, ranks, pl.ds(0, width), sems[4:6])
    qkv_piece = Reduce(grads, from_core, from_y, own_grads, own, 0, ranks, pl.ds(0, cols), sems[6:8])
    third = mlp_own.shape[2] // 3
    mlp_ways = [
        Deliver(mlp_own, mlp_sums, pl.ds(at * third, third), ranks, [*sems[8:11], *sems[22:28]][3 * at : 3 * at + 3])
        for at in range(3)
    ]
    dob_send, dob_recv = sems[0:2]
    qkv_way = Deliver(own_grads, attn_sums, pl.ds(0, cols), ranks, sems[14:17])
    peers = [(lax.rem(seq + step, ranks), dp) for step in range(1, ranks)]
    peers += [(seq, lax.rem(dp + step, copies)) for step in range(1, copies)]
    knock(peers)
    local_sems = sems[21]
    loads = {}
    for at, (name, src, dst) in enumerate(
        (
            ("out", out_all, o_grads), ("block", block_in, attn_block), ("v", v_in, v_low),
            ("prob", prob_in, prob), ("k", k_in, k_low), ("q", q_in, q_low), ("cos", cos_in, cosv),
            ("sin", sin_in, sinv), ("qkv", qkv_in, qkv), ("first", first_in_in, first_in),
            ("dresid", dresid_in, dresid),
        )
    ):
        loads[name] = move(src, dst, local_sems.at[at])
    answered(peers)
    loads["out"].wait()

    def columns_of(rank):
        return pl.ds(pl.multiple_of(rank * o_cols, o_cols), o_cols)

    def owner(rel):
        return ring_seq(lax.rem(place + rel, ranks), ranks)

    def exchange(rel):
        to = owner(rel)
        return push(
            dob.at[:, columns_of(to)], dout.at[pl.ds(row(0), local)], dob_send.at[rel], dob_recv.at[rel], (to, dp)
        )

    def project(rel):
        some = columns_of(owner(rel))
        dob[:, some] = dot_nn(dresid_low[...], o_grads[:, :, some].reshape(width, o_cols)).astype(LOW)

    for rel in (*ring_order(ranks)[1:][::-1], 0):
        project(rel)
        if rel:
            exchange(rel).start()
    dout[pl.ds(row(0), local)] = dob[:, columns_of(seq)]
    mlp_ways[0].start()

    def out_grads(at, _):
        some_cols = pl.ds(pl.multiple_of(at * deep, deep), deep)
        o_grads[at] = dot_tn(dresid_low[:, some_cols], own_out[...]).astype(LOW)
        return 0

    lax.fori_loop(0, ranks, out_grads, 0)
    out_piece.first()
    for rel in range(1, ranks):
        exchange(rel).wait_recv()
    for name in ("v", "prob", "k", "q", "cos", "sin", "qkv"):
        loads[name].wait()
    tall = rows // half
    query_gain_grad[...] = jnp.zeros_like(query_gain_grad)
    key_gain_grad[...] = jnp.zeros_like(key_gain_grad)

    def unrotated(grad, column, rows_at, gain, gain_grad_ref):
        grad = grad * cosv[rows_at] - turn(grad) * sinv[rows_at]
        value = qkv[rows_at, column * size : (column + 1) * size]
        normal, inv = rows_scaled(value)
        gain_grad_ref[...] += jnp.sum(grad * normal, 0, keepdims=True)
        back = rows_scaled_back(value, inv, grad * gain[...])
        dqkv[rows_at, column * size : (column + 1) * size] = back.astype(LOW)

    for head in range(heads):
        group = head // share

        def one(piece, _):
            rows_at = pl.ds(pl.multiple_of(piece * tall, tall), tall)
            weight = prob[head, rows_at]
            grad = dout[rows_at, head * size : (head + 1) * size]
            dprob = dot_nt(grad, v_low[group])
            full = weight.astype(jnp.float32)
            delta = jnp.sum(full * dprob, -1, keepdims=True)
            dscore = (full * (dprob - delta)).astype(LOW)
            dq = dot_nn(dscore, k_low[group]) * scale
            dk_add = dot_tn(dscore, q_low[head, rows_at]) * scale
            dv_add = dot_tn(weight, grad)
            dk[group] += dk_add
            dv[group] += dv_add
            unrotated(dq, head, rows_at, query_gain, query_gain_grad)
            return 0

        if head % share == 0:
            dk[group] = jnp.zeros_like(dk[group])
            dv[group] = jnp.zeros_like(dv[group])
        lax.fori_loop(0, half, one, 0)
        if head == 0:
            out_piece.second()
            mlp_ways[1].start()
    for group in range(kv_heads):
        def one_key(piece, _):
            rows_at = pl.ds(pl.multiple_of(piece * tall, tall), tall)
            unrotated(dk[group, rows_at], heads + group, rows_at, key_gain, key_gain_grad)
            at = (heads + kv_heads + group) * size
            dqkv[rows_at, at : at + size] = dv[group, rows_at].astype(LOW)
            return 0

        lax.fori_loop(0, half, one_key, 0)

    def part(rels, begin, end):
        def some(at, _):
            value = dot_nt(block_rows(dqkv, rels, local, ranks), attn_block[at])
            term[: len(rels) * local, pl.ds(pl.multiple_of(at * deep, deep), deep)] = value
            return 0

        lax.fori_loop(begin, end, some, 0)

    def qkv_grads(at, _):
        some_cols = pl.ds(pl.multiple_of(at * deep, deep), deep)
        grads[at] = dot_tn(first_in[:, some_cols], dqkv[...]).astype(LOW)
        return 0

    def to_ranks(step):
        peer = lax.rem(seq + step, ranks)
        return push(tile, tiles_in.at[seq], sems[17].at[step], sems[18].at[step], (peer, dp))

    def to_copies(step):
        peer = lax.rem(dp + step, copies)
        return push(
            tile_sum, tile_sums_in.at[dp], sems[19].at[step], sems[20].at[step], (seq, peer)
        )

    tile[0:1] = query_gain_grad[...]
    tile[1:2] = key_gain_grad[...]
    tile[2:] = jnp.zeros((tile.shape[0] - 2, size), jnp.float32)
    for step in range(1, ranks):
        to_ranks(step).start()
    tiles_in[seq] = tile[...]
    mlp_ways[2].start()
    loads["block"].wait()

    def out_part(rels, begin, end):
        for at, rel in enumerate(rels):
            o_term[at * own : (at + 1) * own] = o_own[owner(rel)].astype(jnp.float32)

    out_total = RingSum(out_part, o_term, o_out, o_in, own, ranks, sems[30], sems[31], right, left)
    totals = two_sums(part, term, out_buf, in_buf, local, ranks, [*sems[2:4], *sems[28:30]], right, left)
    for step in range(1, half + 1):
        for total in totals:
            total.compute(step)
            total.launch(step)
        if step == 1:
            loads["first"].wait()
            lax.fori_loop(0, ranks, qkv_grads, 0)
            qkv_piece.first()
        if step == 2:
            qkv_piece.second()
            for other in range(1, ranks):
                to_ranks(other).wait_recv()
            tile_sum[...] = jnp.sum(tiles_in[...], 0)
            for other in range(1, copies):
                to_copies(other).start()
            tile_sums_in[dp] = tile_sum[...]
        if step == half - 1:
            for other in range(1, copies):
                to_copies(other).wait_recv()
            gains[...] = jnp.sum(tile_sums_in[...], 0)
            qkv_piece.third()
            qkv_way.start()
    out_piece.third()
    for step in range(1, half + 1):
        out_total.compute(step)
        out_total.launch(step)
    for total in totals:
        total.compute(half + 1)
    loads["dresid"].wait()
    for total in totals:
        total.arrive_last()

    def last(at, _):
        begin = pl.multiple_of(at * 32, 32)
        rows_at = pl.ds(begin, 32)
        value = tokens[rows_at].astype(jnp.float32)
        inv = rows_scaled(value)[1]
        grad = jnp.concatenate([total.last(begin, 32) for total in totals], 1)
        tokens_grad[rows_at] = dresid[rows_at] + rows_scaled_back(value, inv, grad)
        return 0

    lax.fori_loop(0, local // 32, last, 0)
    out_total.compute(half + 1)
    out_total.arrive_last()
    out_grad[...] = out_total.last(0, own)
    for step in range(1, ranks):
        to_ranks(step).wait_send()
    for step in range(1, copies):
        to_copies(step).wait_send()
    out_total.finish()
    for rel in range(1, ranks):
        exchange(rel).wait_send()
    for total in totals:
        total.finish()
    out_piece.finish()
    qkv_piece.finish()
    for way in mlp_ways:
        way.finish()
    qkv_way.finish()


def leave_kernel(
    attn_sums, mlp_sums, attn_gain, mlp_gain, w_query, w_key, w_value, w_gate, w_up,
    query_out, key_out, value_out, gate_out, up_out, down_out, attn_out, mlp_out,
):
    own = attn_gain.shape[1]
    same = lax.broadcasted_iota(jnp.int32, (own, own), 0) == lax.broadcasted_iota(jnp.int32, (own, own), 1)

    @pl.when(pl.program_id(0) == 0)
    def _():
        attn_out[...] = jnp.zeros_like(attn_out)
        mlp_out[...] = jnp.zeros_like(mlp_out)

    for sums, gain, gain_out, parts in (
        (attn_sums, attn_gain, attn_out, ((query_out, w_query), (key_out, w_key), (value_out, w_value))),
        (mlp_sums, mlp_gain, mlp_out, ((gate_out, w_gate), (up_out, w_up), (down_out, None))),
    ):
        scale = jnp.sum(jnp.where(same, gain[...], 0.0), 1, keepdims=True)
        at = 0
        for out, weight in parts:
            value = sums[0, :, at : at + out.shape[1]].astype(jnp.float32)
            at += out.shape[1]
            if weight is None:
                out[...] = value
                continue
            out[...] = value * scale
            inner = jnp.sum(value * weight[...].astype(jnp.float32), 1, keepdims=True)
            gain_out[...] += jnp.sum(jnp.where(same, inner, 0.0), 0, keepdims=True)


VM = pl.BlockSpec(memory_space=pltpu.VMEM)
SM = pl.BlockSpec(memory_space=pltpu.SMEM)
ANY = pl.BlockSpec(memory_space=pl.ANY)


def call(kernel, number, ins, outs, scratch, operands):
    return pl.pallas_call(
        kernel,
        out_shape=[jax.ShapeDtypeStruct(shape, dtype) for shape, dtype, _ in outs],
        in_specs=ins,
        out_specs=[spec for _, _, spec in outs],
        scratch_shapes=scratch,
        compiler_params=pltpu.CompilerParams(
            collective_id=number, has_side_effects=True, vmem_limit_bytes=LIMIT
        ),
    )(*operands)


def columns_body(
    tokens,
    out_grad,
    span_order,
    doc_starts,
    w_query,
    w_key,
    w_value,
    w_output,
    attn_gain,
    query_gain,
    key_gain,
    w_gate,
    w_up,
    w_down,
    mlp_gain,
):
    ranks = lax.axis_size("seq")
    copies = lax.axis_size("dp")
    _, local, width = tokens.shape
    rows = local * ranks
    size = query_gain.shape[0]
    kv_heads = w_key.shape[1] // size // ranks
    heads = w_query.shape[1] // size // ranks
    q_cols, kv_cols = heads * size, kv_heads * size
    qkv_cols = q_cols + 2 * kv_cols
    ff = w_gate.shape[1] // ranks
    own = width // (ranks * copies)
    deep = own * copies
    half = ranks // 2
    f32, i32 = jnp.float32, jnp.int32
    exponents = np.arange(size) % (size // 2) * (-2.0 / size * math.log(1000000.0))
    freqs = jnp.asarray(np.exp(exponents)[None], f32)
    q_gain, k_gain = query_gain[None], key_gain[None]
    (
        resid, second, cosv, sinv, q_low, k_low, v_low, own_out, first_in, qkv, attn_block, dy_all, prob, mlp_block,
        out_all,
    ) = call(
        functools.partial(first_kernel, ranks, kv_heads),
        1,
        [SM, SM] + [VM] * 11 + [ANY] * 3,
        [
            ((local, width), f32, VM),
            ((local, width), LOW, VM),
            ((rows, size), f32, VM),
            ((rows, size), f32, VM),
            ((heads, rows, size), LOW, VM),
            ((kv_heads, rows, size), LOW, VM),
            ((kv_heads, rows, size), LOW, VM),
            ((local, q_cols * ranks), LOW, VM),
            ((rows, width), LOW, ANY),
            ((rows, qkv_cols), f32, ANY),
            ((ranks, deep, qkv_cols), LOW, ANY),
            ((rows, width), LOW, ANY),
            ((heads, rows, rows), LOW, ANY),
            ((ranks, deep, 3 * ff), LOW, ANY),
            ((ranks, deep, q_cols * ranks), LOW, ANY),
        ],
        [
            pltpu.VMEM((rows, width), LOW),
            pltpu.VMEM((rows, width), LOW),
            pltpu.VMEM((rows, qkv_cols), f32),
            pltpu.VMEM((ranks, deep, qkv_cols), LOW),
            pltpu.VMEM((ranks, own, qkv_cols), LOW),
            pltpu.VMEM((ranks, own, 3 * ff), LOW),
        ]
        + [pltpu.VMEM((own, ff * ranks), LOW)] * 3
        + [
            pltpu.VMEM((rows, width), LOW),
            pltpu.VMEM((heads, rows, rows), LOW),
            pltpu.VMEM((rows, 1), i32),
            pltpu.VMEM((rows, 1), i32),
            pltpu.VMEM((1, rows), i32),
            pltpu.VMEM((rows, q_cols), LOW),
            pltpu.VMEM((ranks, deep, q_cols * ranks), LOW),
        ]
        + ring_sems(ranks)
        + [pltpu.SemaphoreType.DMA((ranks,))] * 2
        + line_sems(ranks)
        + whole_sems(ranks)[:4]
        + spread_sems(ranks) * 4
        + [pltpu.SemaphoreType.DMA((heads * half + 8,))]
        + whole_sems(ranks)[4:],
        (
            span_order, doc_starts, tokens[0], out_grad[0], freqs, attn_gain[None], mlp_gain[None], q_gain, k_gain,
            w_query, w_key, w_value, w_output, w_gate, w_up, w_down,
        ),
    )
    block_out, dresid, dresid_low, mlp_own = call(
        functools.partial(mlp_kernel, ranks),
        2,
        [VM, VM, ANY, ANY, ANY],
        [
            ((local, width), LOW, VM),
            ((local, width), f32, VM),
            ((local, width), LOW, VM),
            ((ranks, own, 3 * ff), LOW, VM),
        ],
        [pltpu.VMEM((ranks, deep, 3 * ff), LOW)]
        + reduce_bufs(ranks, own, 3 * ff)
        + [
            pltpu.VMEM((rows, width), LOW),
            pltpu.VMEM((ranks, deep, 3 * ff), LOW),
            pltpu.VMEM((rows, ff), LOW),
            pltpu.VMEM((rows, 2 * ff), LOW),
            pltpu.VMEM((local, width), f32),
            pltpu.VMEM((rows, width), LOW),
        ]
        + sum_bufs(local, ranks, width)
        + sum_bufs(local, ranks, width)[1:]
        + [pltpu.SemaphoreType.DMA((3,))]
        + ring_sems(ranks) * 3
        + reduce_sems() * 4,
        (second, out_grad[0], resid, dy_all, mlp_block),
    )
    tokens_grad, gains, wo_grad, mlp_sums, attn_sums = call(
        functools.partial(back_kernel, ranks, kv_heads),
        3,
        [VM] * 5 + [ANY] * 12,
        [
            ((local, width), f32, VM),
            ((8, size), f32, VM),
            ((own, q_cols * ranks), f32, VM),
            ((ranks, own, 3 * ff), LOW, ANY),
            ((ranks, own, qkv_cols), LOW, VM),
        ],
        [pltpu.VMEM((ranks, deep, qkv_cols), LOW)]
        + reduce_bufs(ranks, own, qkv_cols)
        + [
            pltpu.VMEM((ranks, own, qkv_cols), LOW),
            pltpu.VMEM((1, size), f32),
            pltpu.VMEM((1, size), f32),
            pltpu.VMEM((8, size), f32),
            pltpu.VMEM((ranks, 8, size), f32),
            pltpu.VMEM((8, size), f32),
            pltpu.VMEM((copies, 8, size), f32),
            pltpu.VMEM((local, q_cols * ranks), LOW),
            pltpu.VMEM((rows, q_cols), LOW),
            pltpu.VMEM((kv_heads, rows, size), f32),
            pltpu.VMEM((kv_heads, rows, size), f32),
            pltpu.VMEM((rows, qkv_cols), LOW),
            pltpu.VMEM((rows, width), LOW),
            pltpu.VMEM((ranks, deep, qkv_cols), LOW),
            pltpu.VMEM((rows, qkv_cols), f32),
            pltpu.VMEM((rows, size), f32),
            pltpu.VMEM((rows, size), f32),
            pltpu.VMEM((heads, rows, size), LOW),
            pltpu.VMEM((kv_heads, rows, size), LOW),
            pltpu.VMEM((kv_heads, rows, size), LOW),
            pltpu.VMEM((heads, rows, rows), LOW),
            pltpu.VMEM((local, width), f32),
        ]
        + sum_bufs(local, ranks, width)
        + [pltpu.VMEM((ranks, deep, q_cols * ranks), LOW)]
        + reduce_bufs(ranks, own, q_cols * ranks)
        + [pltpu.VMEM((ranks, own, q_cols * ranks), LOW)]
        + sum_bufs(own, ranks, q_cols * ranks)
        + [pltpu.SemaphoreType.DMA((ranks,))] * 2
        + ring_sems(ranks)
        + reduce_sems() * 2
        + deliver_sems(ranks) * 3
        + [pltpu.SemaphoreType.DMA((ranks,))] * 2
        + [pltpu.SemaphoreType.DMA((copies,))] * 2
        + [pltpu.SemaphoreType.DMA((11,))]
        + deliver_sems(ranks) * 2
        + ring_sems(ranks) * 2,
        (
            tokens[0], dresid_low, q_gain, k_gain, own_out, first_in, attn_block, qkv, cosv, sinv, q_low, k_low,
            v_low, prob, dresid, mlp_own, out_all,
        ),
    )
    whole = pl.BlockSpec((1, own), lambda at: (0, 0))
    each = (q_cols, kv_cols, kv_cols, ff, ff, ff)
    columns = [pl.BlockSpec((own, cols), lambda at: (0, at)) for cols in each]
    *grads, dga, dgm = pl.pallas_call(
        leave_kernel,
        grid=(ranks,),
        out_shape=[jax.ShapeDtypeStruct((own, cols * ranks), f32) for cols in each]
        + [jax.ShapeDtypeStruct((1, own), f32)] * 2,
        in_specs=[
            pl.BlockSpec((1, own, qkv_cols), lambda at: (at, 0, 0)),
            pl.BlockSpec((1, own, 3 * ff), lambda at: (at, 0, 0)),
            whole,
            whole,
            *columns[:3],
            *columns[3:5],
        ],
        out_specs=columns + [whole, whole],
    )(attn_sums, mlp_sums, attn_gain[None], mlp_gain[None], w_query, w_key, w_value, w_gate, w_up)
    return (
        block_out[None], tokens_grad[None], *grads[:3], wo_grad, dga[0], gains[0], gains[1], *grads[3:], dgm[0],
    )


def body(*args):
    tokens, w_key, query_gain = args[0], args[5], args[9]
    groups = w_key.shape[1] // query_gain.shape[0]
    ranks = lax.axis_size("seq")
    if tokens.shape[0] == 1 and ranks % 2 == 0 and groups % ranks == 0 and lax.axis_size("dp") == 4:
        return columns_body(*args)
    return gathered_body(*args)


def solution(mesh):
    return jax.shard_map(
        body,
        mesh=mesh,
        in_specs=(
            P("dp", "seq", None),
            P("dp", "seq", None),
            P(),
            P("dp", None),
            P(("seq", "dp"), None),
            P(("seq", "dp"), None),
            P(("seq", "dp"), None),
            P(("seq", "dp"), None),
            P(("seq", "dp")),
            P(),
            P(),
            P(("seq", "dp"), None),
            P(("seq", "dp"), None),
            P(("seq", "dp"), None),
            P(("seq", "dp")),
        ),
        out_specs=(
            P("dp", "seq", None),
            P("dp", "seq", None),
            P(("seq", "dp"), None),
            P(("seq", "dp"), None),
            P(("seq", "dp"), None),
            P(("seq", "dp"), None),
            P(("seq", "dp")),
            P(),
            P(),
            P(("seq", "dp"), None),
            P(("seq", "dp"), None),
            P(("seq", "dp"), None),
            P(("seq", "dp")),
        ),
        check_vma=False,
    )
```

```python
import functools
import math

import jax
import jax.numpy as jnp
import numpy as np
from jax import lax
from jax.experimental import pallas as pl
from jax.experimental.pallas import tpu as pltpu
from jax.sharding import PartitionSpec as P

EPS = 1e-06
NEG = -1e30


def normed(v, gain):
    scale_inv = lax.rsqrt(jnp.mean(v * v, -1, keepdims=True) + EPS)
    return (v * scale_inv * gain, scale_inv)


def norm_back(v, scale_inv, gain, grad):
    scaled = grad * gain
    inner = jnp.mean(scaled * v, -1, keepdims=True)
    dv = scale_inv * scaled - v * scale_inv * scale_inv * scale_inv * inner
    dgain = jnp.sum((grad * v * scale_inv).reshape(-1, v.shape[-1]), 0)
    return (dv, dgain)


def rotary(pos, width):
    half = width // 2
    freqs = jnp.exp(jnp.arange(half, dtype=jnp.float32) * (-2.0 / width * math.log(1000000.0)))
    angle = pos.astype(jnp.float32)[:, None] * freqs[None, :]
    return (jnp.cos(angle)[:, None, :], jnp.sin(angle)[:, None, :])


def rotate(v, cosv, sinv):
    half = v.shape[-1] // 2
    first, second = (v[..., :half], v[..., half:])
    return jnp.concatenate([first * cosv - second * sinv, second * cosv + first * sinv], -1)


def rotate_back(grad, cosv, sinv):
    half = grad.shape[-1] // 2
    first, second = (grad[..., :half], grad[..., half:])
    return jnp.concatenate([first * cosv + second * sinv, second * cosv - first * sinv], -1)


def place(order, begin, count, span):
    rows = begin + jnp.arange(count, dtype=jnp.int32)
    slots = rows // span
    picked = slots[:, None] == jnp.arange(order.shape[0], dtype=jnp.int32)[None, :]
    return jnp.sum(jnp.where(picked, order[None, :], 0), -1) * span + rows % span


def doc_of(starts, pos):
    return jnp.sum((starts[:, None, :] <= pos[None, :, None]).astype(jnp.int32), -1)


def gathered_body(
    tokens,
    out_grad,
    span_order,
    doc_starts,
    w_query,
    w_key,
    w_value,
    w_output,
    attn_gain,
    query_gain,
    key_gain,
    w_gate,
    w_up,
    w_down,
    mlp_gain,
):
    seqs, local, width = tokens.shape
    span = local // 2
    head_size = query_gain.shape[0]
    kv_heads = w_key.shape[1] // head_size
    heads = w_query.shape[1] // head_size
    share = heads // kv_heads
    kv_width = kv_heads * head_size
    ff_width = w_gate.shape[1]
    scale = 1.0 / math.sqrt(head_size)
    total_rows = seqs * local
    own_rows = width // lax.axis_size(("seq", "dp"))
    qpos = place(span_order, lax.axis_index("seq") * local, local, span)
    qdoc = doc_of(doc_starts, qpos)
    cosv, sinv = rotary(qpos, head_size)

    def gather_attn():
        return (
            lax.all_gather(w_query, ("seq", "dp"), axis=0, tiled=True),
            lax.all_gather(w_key, ("seq", "dp"), axis=0, tiled=True),
            lax.all_gather(w_value, ("seq", "dp"), axis=0, tiled=True),
            lax.all_gather(w_output, ("seq", "dp"), axis=0, tiled=True),
            lax.all_gather(
                attn_gain.astype(jnp.bfloat16), ("seq", "dp"), axis=0, tiled=True
            ).astype(attn_gain.dtype),
        )

    def gather_mlp():
        return (
            lax.all_gather(w_gate, ("seq", "dp"), axis=0, tiled=True),
            lax.all_gather(w_up, ("seq", "dp"), axis=0, tiled=True),
            lax.all_gather(w_down, ("seq", "dp"), axis=0, tiled=True),
            lax.all_gather(mlp_gain.astype(jnp.bfloat16), ("seq", "dp"), axis=0, tiled=True).astype(
                mlp_gain.dtype
            ),
        )

    x_rows = tokens.astype(jnp.float32).reshape(total_rows, width)
    wq_all, wk_all, wv_all, wo_all, ga_all = gather_attn()
    first_norm, first_inv = normed(x_rows, ga_all)
    first_in = first_norm.astype(jnp.bfloat16)
    q_raw = jnp.dot(first_in, wq_all, preferred_element_type=jnp.float32).reshape(
        seqs, local, heads, head_size
    )
    k_raw = jnp.dot(first_in, wk_all, preferred_element_type=jnp.float32).reshape(
        seqs, local, kv_heads, head_size
    )
    v_low = (
        jnp.dot(first_in, wv_all, preferred_element_type=jnp.float32)
        .astype(jnp.bfloat16)
        .reshape(seqs, local, kv_heads, head_size)
    )
    q_normed, q_inv = normed(q_raw, query_gain)
    k_normed, k_inv = normed(k_raw, key_gain)
    q_low = rotate(q_normed, cosv, sinv).astype(jnp.bfloat16)
    k_low = rotate(k_normed, cosv, sinv).astype(jnp.bfloat16)
    q_group = q_low.reshape(seqs, local, kv_heads, share, head_size)

    def scores(piece_key, start):
        count = piece_key.shape[1]
        kpos = place(span_order, start, count, span)
        kdoc = doc_of(doc_starts, kpos)
        visible = (qdoc[:, :, None] == kdoc[:, None, :]) & (
            kpos[None, None, :] <= qpos[None, :, None]
        )
        raw = (
            jnp.einsum("sqgjd,skgd->sgjqk", q_group, piece_key, preferred_element_type=jnp.float32)
            * scale
        )
        return (raw, visible[:, None, None])

    start_top = jnp.full((seqs, kv_heads, share, local), NEG, jnp.float32)
    piece = (
        lax.all_gather(k_low, "seq", axis=1, tiled=True),
        lax.all_gather(v_low, "seq", axis=1, tiled=True),
    )
    top = start_top
    raw, visible = scores(piece[0], jnp.int32(0))
    raw = jnp.where(visible, raw, NEG)
    new_top = jnp.maximum(top, jnp.max(raw, -1))
    weights = jnp.where(visible, jnp.exp(raw - new_top[..., None]), 0.0)
    total = jnp.sum(weights, -1)
    summed = jnp.einsum(
        "sgjqk,skgd->sgjqd",
        weights.astype(jnp.bfloat16),
        piece[1],
        preferred_element_type=jnp.float32,
    )
    top, total, summed = (new_top, total, summed)
    log_total = top + jnp.log(total)
    attn_vals = summed / total[..., None]
    out_low = (
        jnp.transpose(attn_vals, (0, 3, 1, 2, 4))
        .reshape(total_rows, heads * head_size)
        .astype(jnp.bfloat16)
    )
    resid = x_rows + jnp.einsum("nh,dh->nd", out_low, wo_all, preferred_element_type=jnp.float32)
    wg_all, wu_all, wd_all, gm_all = gather_mlp()
    second_norm, second_inv = normed(resid, gm_all)
    second_in = second_norm.astype(jnp.bfloat16)
    gate = jnp.dot(second_in, wg_all, preferred_element_type=jnp.float32)
    upper = jnp.dot(second_in, wu_all, preferred_element_type=jnp.float32)
    sigma = jax.nn.sigmoid(gate)
    act = gate * sigma
    hidden = (act * upper).astype(jnp.bfloat16)
    result = resid + jnp.einsum("nf,df->nd", hidden, wd_all, preferred_element_type=jnp.float32)
    block_out = result.astype(jnp.bfloat16).reshape(seqs, local, width)
    grad_low = out_grad.reshape(total_rows, width)
    wg_all, wu_all, wd_all, gm_all = gather_mlp()
    dmid = jnp.einsum("nd,df->nf", grad_low, wd_all, preferred_element_type=jnp.float32)
    dgate = (dmid * upper * sigma * (1.0 + gate * (1.0 - sigma))).astype(jnp.bfloat16)
    dupper = (dmid * act).astype(jnp.bfloat16)
    left = second_in
    outer = grad_low
    mlp_sums = lax.psum_scatter(
        jnp.concatenate(
            [
                jnp.einsum("nd,nf->df", left, dgate, preferred_element_type=jnp.float32),
                jnp.einsum("nd,nf->df", left, dupper, preferred_element_type=jnp.float32),
                jnp.einsum("nd,nf->df", outer, hidden, preferred_element_type=jnp.float32),
            ],
            1,
        ),
        ("seq", "dp"),
        scatter_dimension=0,
        tiled=True,
    )
    dsecond = jnp.einsum(
        "nf,df->nd", dgate, wg_all, preferred_element_type=jnp.float32
    ) + jnp.einsum("nf,df->nd", dupper, wu_all, preferred_element_type=jnp.float32)
    dresid_norm, dgm = norm_back(resid, second_inv, gm_all, dsecond)
    dresid = grad_low.astype(jnp.float32) + dresid_norm
    dresid_low = dresid.astype(jnp.bfloat16)
    wq_all, wk_all, wv_all, wo_all, ga_all = gather_attn()
    dout_low = jnp.einsum(
        "nd,dh->nh", dresid_low, wo_all, preferred_element_type=jnp.float32
    ).astype(jnp.bfloat16)
    dout_group = dout_low.reshape(seqs, local, kv_heads, share, head_size)
    delta = jnp.sum(jnp.transpose(dout_group.astype(jnp.float32), (0, 2, 3, 1, 4)) * attn_vals, -1)
    piece = (
        lax.all_gather(k_low, "seq", axis=1, tiled=True),
        lax.all_gather(v_low, "seq", axis=1, tiled=True),
    )
    count = piece[0].shape[1]
    raw, visible = scores(piece[0], jnp.int32(0))
    prob = jnp.where(visible, jnp.exp(raw - log_total[..., None]), 0.0)
    dprob = jnp.einsum(
        "sqgjd,skgd->sgjqk", dout_group, piece[1], preferred_element_type=jnp.float32
    )
    dscore = (prob * (dprob - delta[..., None])).astype(jnp.bfloat16)
    dq_sum = jnp.einsum("sgjqk,skgd->sqgjd", dscore, piece[0], preferred_element_type=jnp.float32)
    dk_part = (
        jnp.einsum("sgjqk,sqgjd->skgd", dscore, q_group, preferred_element_type=jnp.float32) * scale
    )
    dv_part = jnp.einsum(
        "sgjqk,sqgjd->skgd",
        prob.astype(jnp.bfloat16),
        dout_group,
        preferred_element_type=jnp.float32,
    )
    joined = jnp.concatenate(
        [dk_part.reshape(seqs, count, kv_width), dv_part.reshape(seqs, count, kv_width)], -1
    )
    buffer = joined
    dq_sum, buffer = (dq_sum, buffer)
    key_sums = lax.psum_scatter(
        buffer.astype(jnp.bfloat16), "seq", scatter_dimension=1, tiled=True
    ).astype(jnp.float32)
    dq_rot = (dq_sum * scale).reshape(seqs, local, heads, head_size)
    dq_raw, dgq = norm_back(q_raw, q_inv, query_gain, rotate_back(dq_rot, cosv, sinv))
    dk_rot = key_sums[..., :kv_width].reshape(seqs, local, kv_heads, head_size)
    dk_raw, dgk = norm_back(k_raw, k_inv, key_gain, rotate_back(dk_rot, cosv, sinv))
    dq_low = dq_raw.reshape(total_rows, heads * head_size).astype(jnp.bfloat16)
    dk_low = dk_raw.reshape(total_rows, kv_width).astype(jnp.bfloat16)
    dv_low = key_sums[..., kv_width:].reshape(total_rows, kv_width).astype(jnp.bfloat16)
    left = first_in
    outer = dresid_low
    attn_sums = lax.psum_scatter(
        jnp.concatenate(
            [
                jnp.einsum("nd,nh->dh", left, dq_low, preferred_element_type=jnp.float32),
                jnp.einsum("nd,nh->dh", left, dk_low, preferred_element_type=jnp.float32),
                jnp.einsum("nd,nh->dh", left, dv_low, preferred_element_type=jnp.float32),
                jnp.einsum("nd,nh->dh", outer, out_low, preferred_element_type=jnp.float32),
            ],
            1,
        ),
        ("seq", "dp"),
        scatter_dimension=0,
        tiled=True,
    )
    dfirst = jnp.einsum("nh,dh->nd", dq_low, wq_all, preferred_element_type=jnp.float32)
    dfirst = dfirst + jnp.einsum("nh,dh->nd", dk_low, wk_all, preferred_element_type=jnp.float32)
    dfirst = dfirst + jnp.einsum("nh,dh->nd", dv_low, wv_all, preferred_element_type=jnp.float32)
    dx_norm, dga = norm_back(x_rows, first_inv, ga_all, dfirst)
    tokens_grad = (dresid + dx_norm).reshape(seqs, local, width)
    dga_all, dgm_all, dgq_all, dgk_all = lax.psum((dga, dgm, dgq, dgk), ("seq", "dp"))
    offset = lax.axis_index(("seq", "dp")) * own_rows
    attn_gain_grad = lax.dynamic_slice_in_dim(dga_all, offset, own_rows, 0)
    mlp_gain_grad = lax.dynamic_slice_in_dim(dgm_all, offset, own_rows, 0)
    q_cols = heads * head_size
    w_query_grad = attn_sums[:, :q_cols]
    w_key_grad = attn_sums[:, q_cols : q_cols + kv_width]
    w_value_grad = attn_sums[:, q_cols + kv_width : q_cols + 2 * kv_width]
    w_output_grad = attn_sums[:, q_cols + 2 * kv_width :]
    w_gate_grad = mlp_sums[:, :ff_width]
    w_up_grad = mlp_sums[:, ff_width : 2 * ff_width]
    w_down_grad = mlp_sums[:, 2 * ff_width :]
    return (
        block_out,
        tokens_grad,
        w_query_grad,
        w_key_grad,
        w_value_grad,
        w_output_grad,
        attn_gain_grad,
        dgq_all,
        dgk_all,
        w_gate_grad,
        w_up_grad,
        w_down_grad,
        mlp_gain_grad,
    )


LOW = jnp.bfloat16
MESH = pl.DeviceIdType.MESH
LIMIT = 60 * 2**20


def ring_order(ranks):
    half = ranks // 2
    order = [0]
    for step in range(1, half):
        order += [step, ranks - step]
    return order + [half]


def ring_place(seq, ranks):
    z, x = lax.div(seq, 2), lax.rem(seq, 2)
    return z + x * (ranks - 1 - 2 * z)


def ring_seq(place, ranks):
    half = ranks // 2
    x, z = lax.div(place, half), lax.rem(place, half)
    return 2 * (z + x * (half - 1 - 2 * z)) + x


def neighbours(ranks):
    seq, dp = lax.axis_index("seq"), lax.axis_index("dp")
    at = ring_place(seq, ranks)
    right = ring_seq(lax.rem(at + 1, ranks), ranks)
    left = ring_seq(lax.rem(at + ranks - 1, ranks), ranks)
    return (right, dp), (left, dp)


def knock(devices):
    barrier = pltpu.get_barrier_semaphore()
    for device in devices:
        pl.semaphore_signal(barrier, inc=1, device_id=device, device_id_type=MESH)


def answered(devices):
    pl.semaphore_wait(pltpu.get_barrier_semaphore(), len(devices))


def move(src, dst, sem):
    copy = pltpu.make_async_copy(src, dst, sem)
    copy.start()
    return copy


def push(src, dst, send, recv, device):
    return pltpu.make_async_remote_copy(
        src_ref=src, dst_ref=dst, send_sem=send, recv_sem=recv, device_id=device, device_id_type=MESH
    )


def dot_nn(left, right):
    return jnp.dot(left, right, preferred_element_type=jnp.float32)


def dot_nt(left, right):
    return lax.dot_general(left, right, (((1,), (1,)), ((), ())), preferred_element_type=jnp.float32)


def dot_tn(left, right):
    return lax.dot_general(left, right, (((0,), (0,)), ((), ())), preferred_element_type=jnp.float32)


def block_row(rel, local, ranks):
    place = ring_place(lax.axis_index("seq"), ranks)
    return pl.multiple_of(ring_seq(lax.rem(place + rel, ranks), ranks) * local, local)


def block_rows(ref, rels, local, ranks):
    blocks = [ref[pl.ds(block_row(rel, local, ranks), local)] for rel in rels]
    return blocks[0] if len(blocks) == 1 else jnp.concatenate(blocks, 0)


def rels_of(step, ranks):
    return [rel for rel in ring_order(ranks) if min(rel, ranks - rel) == step]


class RingGather:
    def __init__(self, buf, local, ranks, send, recv, right, left, row):
        self.buf, self.sub, self.half = buf, local // 2, ranks // 2
        self.send, self.recv, self.right, self.left = send, recv, right, left
        self.ranks, self.row = ranks, row

    def copies(self, step, part):
        ways = ((0, (self.ranks - step + 1) % self.ranks, self.right), (1, step - 1, self.left))
        given = []
        for way, rel, device in ways:
            if step < self.half or way == part:
                block = self.buf.at[pl.ds(self.row(rel) + part * self.sub, self.sub)]
                at = 2 * (step - 1) + part
                given.append(push(block, block, self.send.at[way, at], self.recv.at[way, at], device))
        return given

    def start(self, step):
        for part in range(2):
            for copy in self.copies(step, part):
                copy.start()

    def advance(self, step):
        for part in range(2):
            for copy in self.copies(step, part):
                copy.wait_recv()
            if step < self.half:
                for copy in self.copies(step + 1, part):
                    copy.start()

    def finish(self):
        for step in range(1, self.half + 1):
            for part in range(2):
                for copy in self.copies(step, part):
                    copy.wait_send()


class LineGather:
    def __init__(self, buf, local, ranks, send, recv, x_send, x_recv):
        self.buf, self.local, self.length = buf, local, ranks // 2
        self.send, self.recv, self.x_send, self.x_recv = send, recv, x_send, x_recv
        self.seq, self.dp = lax.axis_index("seq"), lax.axis_index("dp")
        self.z, self.x = lax.div(self.seq, 2), lax.rem(self.seq, 2)

    def block(self, z):
        return self.buf.at[pl.ds(pl.multiple_of((2 * z + self.x) * self.local, self.local), self.local)]

    def hop(self, way, step):
        block = self.block(self.z + (step - 1 if way else 1 - step))
        to = self.seq + (-2 if way else 2)
        return push(block, block, self.send.at[way, step - 1], self.recv.at[way, step - 1], (to, self.dp))

    def sends(self, way, step):
        if way:
            return (self.z > 0) & (self.z + step <= self.length)
        return (self.z < self.length - 1) & (self.z >= step - 1)

    def comes(self, way, step):
        return self.z + step < self.length if way else self.z >= step

    def across(self, way, step):
        block = self.block(self.z + (step if way else -step))
        at = step + way * (self.length - 1)
        return push(
            block, block, self.x_send.at[at], self.x_recv.at[at], (self.seq + 1 - 2 * self.x, self.dp)
        )

    def from_x(self, way, step):
        z = self.z + (step if way else -step)
        row = pl.multiple_of((2 * z + 1 - self.x) * self.local, self.local)
        block = self.buf.at[pl.ds(row, self.local)]
        at = step + way * (self.length - 1)
        return push(
            block, block, self.x_send.at[at], self.x_recv.at[at], (self.seq + 1 - 2 * self.x, self.dp)
        )

    def start(self, step):
        for way in range(2):
            pl.when(self.sends(way, step))(lambda way=way: self.hop(way, step).start())
        self.pass_on(step - 1)

    def pass_on(self, step):
        if step == 0:
            self.across(0, 0).start()
            return
        for way in range(2):
            pl.when(self.comes(way, step))(lambda way=way: self.across(way, step).start())

    def arrive(self, step):
        for way in range(2):
            pl.when(self.comes(way, step))(lambda way=way: self.incoming(way, step).wait_recv())

    def incoming(self, way, step):
        block = self.block(self.z + (step if way else -step))
        to = self.seq + 1 - 2 * self.x
        return push(block, block, self.send.at[way, step - 1], self.recv.at[way, step - 1], (to, self.dp))

    def run(self):
        for step in range(1, self.length):
            self.advance(step)

    def advance(self, step):
        self.arrive(step)
        if step < self.length - 1:
            self.start(step + 1)
        else:
            self.pass_on(step)

    def complete(self):
        self.from_x(0, 0).wait_recv()
        for step in range(1, self.length):
            for way in range(2):
                pl.when(self.comes(way, step))(lambda way=way: self.from_x(way, step).wait_recv())

    def finish(self):
        self.across(0, 0).wait_send()
        for step in range(1, self.length):
            for way in range(2):
                pl.when(self.sends(way, step))(lambda way=way: self.hop(way, step).wait_send())
                pl.when(self.comes(way, step))(lambda way=way: self.across(way, step).wait_send())


def line_sems(ranks):
    half = ranks // 2
    return [pltpu.SemaphoreType.DMA((2, half))] * 2 + [pltpu.SemaphoreType.DMA((2 * half,))] * 2


class RingSum:
    def __init__(self, part, term, out_buf, in_buf, local, ranks, send, recv, right, left, stream=0, streams=1):
        self.part, self.term, self.out_buf, self.in_buf = part, term, out_buf, in_buf
        self.local, self.ranks, self.half = local, ranks, ranks // 2
        each = term.shape[1] // streams
        self.cols = pl.ds(stream * each, each)
        self.tiles = (stream * ranks // streams, (stream + 1) * ranks // streams)
        self.send, self.recv, self.right, self.left = send, recv, right, left

    def copies(self, step):
        rows = self.local // 2 if step == 1 else self.local
        skip = self.local // 2 if step == 1 else 0
        return [
            push(
                self.out_buf.at[way, (step - 1) % 2, pl.ds(begin, rows), self.cols],
                self.in_buf.at[way, step - 1, pl.ds(begin, rows), self.cols],
                self.send.at[way, step - 1],
                self.recv.at[way, step - 1],
                device,
            )
            for way, begin, device in ((0, 0, self.right), (1, skip, self.left))
        ]

    def compute(self, step):
        if step == 1:
            self.part([self.half], *self.tiles)
        elif step <= self.half:
            self.part(rels_of(self.half + 1 - step, self.ranks), *self.tiles)
        else:
            self.part([0], *self.tiles)

    def launch(self, step):
        local, skip = self.local, self.local // 2
        if step > 2:
            for copy in self.copies(step - 2):
                copy.wait_send()
        if step == 1:
            for way in range(2):
                rows = pl.ds(way * skip, skip)
                self.out_buf[way, 0, rows, self.cols] = self.term[rows, self.cols].astype(LOW)
        else:
            for copy in self.copies(step - 1):
                copy.wait_recv()
            for way in range(2):
                for begin, with_sum in ((0, step > 2 or way == 0), (skip, step > 2 or way == 1)):
                    value = self.term[pl.ds(way * local + begin, skip), self.cols]
                    if with_sum:
                        value = value + self.in_buf[way, step - 2, pl.ds(begin, skip), self.cols].astype(jnp.float32)
                    self.out_buf[way, (step - 1) % 2, pl.ds(begin, skip), self.cols] = value.astype(LOW)
        for copy in self.copies(step):
            copy.start()

    def last(self, begin, count):
        rows = pl.ds(begin, count)
        value = self.term[rows, self.cols] + self.in_buf[0, self.half - 1, rows, self.cols].astype(jnp.float32)
        return value + self.in_buf[1, self.half - 1, rows, self.cols].astype(jnp.float32)

    def arrive_last(self):
        for copy in self.copies(self.half):
            copy.wait_recv()

    def finish(self):
        for step in range(max(1, self.half - 1), self.half + 1):
            for copy in self.copies(step):
                copy.wait_send()


def two_sums(part, term, out_buf, in_buf, local, ranks, sems, right, left):
    return [
        RingSum(
            part, term, out_buf, in_buf, local, ranks, sems[2 * at], sems[2 * at + 1], right, left, at, 2
        )
        for at in range(2)
    ]


def ring_sems(ranks):
    return [pltpu.SemaphoreType.DMA((2, ranks)), pltpu.SemaphoreType.DMA((2, ranks))]


def sum_bufs(local, ranks, width):
    return [
        pltpu.VMEM((2 * local, width), jnp.float32),
        pltpu.VMEM((2, 2, local, width), LOW),
        pltpu.VMEM((2, ranks // 2, local, width), LOW),
    ]


def turn(v):
    return pltpu.roll(v, v.shape[-1] // 2, v.ndim - 1)


def rows_scaled(v):
    inv = lax.rsqrt(jnp.mean(v * v, -1, keepdims=True) + EPS)
    return v * inv, inv


def rows_scaled_back(v, inv, grad):
    return inv * grad - v * (inv * inv * inv * jnp.mean(grad * v, -1, keepdims=True))


class Spread:
    def __init__(self, rows, block, ranks, own, cols, sems):
        self.rows, self.block, self.ranks, self.own, self.cols = rows, block, ranks, own, cols
        self.send, self.recv, self.hop_send, self.hop_recv, self.here = sems
        self.seq, self.dp = lax.axis_index("seq"), lax.axis_index("dp")
        y, core = lax.div(self.dp, 2), lax.rem(self.dp, 2)
        self.beside, self.sibling = (1 - y) * 2 + core, y * 2 + 1 - core

    def at(self, dp):
        return pl.ds(pl.multiple_of(dp * self.own, self.own), self.own)

    def exchange(self):
        for step in range(1, self.ranks):
            peer = lax.rem(self.seq + step, self.ranks)
            yield push(
                self.rows.at[peer, :, self.cols],
                self.block.at[self.seq, self.at(self.dp), self.cols],
                self.send.at[step],
                self.recv.at[step],
                (peer, self.dp),
            )

    def keep(self):
        return pltpu.make_async_copy(
            self.rows.at[self.seq, :, self.cols],
            self.block.at[self.seq, self.at(self.dp), self.cols],
            self.here,
        )

    def hop(self, number):
        dp = self.beside if number == 2 else self.dp
        part = self.block.at[:, self.at(dp), self.cols]
        to = self.beside if number == 0 else self.sibling
        return push(part, part, self.hop_send.at[number], self.hop_recv.at[number], (self.seq, to))

    def start(self):
        self.keep().start()
        for copy in self.exchange():
            copy.start()

    def arrive(self):
        self.keep().wait()
        for copy in self.exchange():
            copy.wait_recv()

    def finish(self):
        for copy in self.exchange():
            copy.wait_send()
        for number in range(3):
            self.hop(number).wait_send()


def spread_sems(ranks):
    return [
        pltpu.SemaphoreType.DMA((ranks,)),
        pltpu.SemaphoreType.DMA((ranks,)),
        pltpu.SemaphoreType.DMA((3,)),
        pltpu.SemaphoreType.DMA((3,)),
        pltpu.SemaphoreType.DMA,
    ]


class WholeGather:
    def __init__(self, block, ranks, own, sems):
        self.block, self.ranks, self.half, self.own = block, ranks, ranks // 2, own
        self.send, self.recv, self.y_send, self.y_recv, self.core_send, self.core_recv = sems
        self.seq, self.dp = lax.axis_index("seq"), lax.axis_index("dp")
        self.right, self.left = neighbours(ranks)
        self.place = ring_place(self.seq, ranks)
        y, core = lax.div(self.dp, 2), lax.rem(self.dp, 2)
        self.beside, self.sibling = (1 - y) * 2 + core, y * 2 + 1 - core

    def at(self, rel, dp, begin, count):
        seq = ring_seq(lax.rem(self.place + rel + self.ranks, self.ranks), self.ranks)
        return self.block.at[seq, pl.ds(pl.multiple_of(dp * self.own + begin, count), count)]

    def copies(self, step):
        last = step == self.half
        rows = self.own // 2 if last else self.own
        skip = self.own // 2 if last else 0
        given = []
        for way, rel, begin, device in ((0, 1 - step, 0, self.right), (1, step - 1, skip, self.left)):
            part = self.at(rel, self.dp, begin, rows)
            given.append(push(part, part, self.send.at[way, step - 1], self.recv.at[way, step - 1], device))
        return given

    def start(self, step):
        for copy in self.copies(step):
            copy.start()

    def hops(self, step):
        for at, rel in enumerate(ring_order(self.ranks)):
            if min(rel, self.ranks - rel) == step:
                part = self.at(rel, self.dp, 0, self.own)
                yield push(part, part, self.y_send.at[at], self.y_recv.at[at], (self.seq, self.beside))
                yield push(part, part, self.core_send.at[at], self.core_recv.at[at], (self.seq, self.sibling))

    def arrive(self, step):
        for copy in self.copies(step):
            copy.wait_recv()

    def forward(self, step):
        for copy in self.hops(step):
            copy.start()

    def cross(self):
        part = self.block.at[:, pl.ds(pl.multiple_of(self.beside * self.own, self.own), self.own)]
        at = self.ranks
        return push(part, part, self.core_send.at[at], self.core_recv.at[at], (self.seq, self.sibling))

    def complete(self):
        for step in range(self.half + 1):
            for copy in self.hops(step):
                copy.wait_recv()
        self.cross().start()
        self.cross().wait_recv()

    def finish(self):
        for step in range(1, self.half + 1):
            for copy in self.copies(step):
                copy.wait_send()
        for step in range(self.half + 1):
            for copy in self.hops(step):
                copy.wait_send()
        self.cross().wait_send()


def whole_sems(ranks):
    return (
        ring_sems(ranks)
        + [pltpu.SemaphoreType.DMA((ranks,))] * 2
        + [pltpu.SemaphoreType.DMA((ranks + 1,))] * 2
    )


class Reduce:
    def __init__(self, grads, from_core, from_y, total, own, first, count, cols, sems):
        self.grads, self.from_core, self.from_y, self.total = grads, from_core, from_y, total
        self.own, self.begin, self.count, self.cols = own, first, count, cols
        self.send, self.recv = sems
        self.seq, dp = lax.axis_index("seq"), lax.axis_index("dp")
        self.y, self.core = lax.div(dp, 2), lax.rem(dp, 2)
        self.beside, self.sibling = (1 - self.y) * 2 + self.core, self.y * 2 + 1 - self.core

    def at(self, y, core):
        return pl.ds(pl.multiple_of((y * 2 + core) * self.own, self.own), self.own)

    def hop(self, number):
        some, cols = pl.ds(self.begin, self.count), self.cols
        if number == 2:
            src, dst, to = self.from_core.at[0, some, :, cols], self.from_y.at[some, :, cols], self.beside
        else:
            rows = self.at(1 - self.y if number == 0 else self.y, 1 - self.core)
            src, dst, to = self.grads.at[some, rows, cols], self.from_core.at[number, some, :, cols], self.sibling
        return push(src, dst, self.send.at[number], self.recv.at[number], (self.seq, to))

    def first(self):
        self.hop(0).start()
        self.hop(1).start()

    def second(self):
        self.hop(0).wait_recv()
        rows = self.at(1 - self.y, self.core)

        def some(at, _):
            value = self.grads[at, rows, self.cols].astype(jnp.float32)
            value = value + self.from_core[0, at, :, self.cols].astype(jnp.float32)
            self.from_core[0, at, :, self.cols] = value.astype(LOW)
            return 0

        lax.fori_loop(self.begin, self.begin + self.count, some, 0)
        self.hop(2).start()

    def third(self):
        self.hop(1).wait_recv()
        self.hop(2).wait_recv()
        rows = self.at(self.y, self.core)

        def some(at, _):
            value = self.grads[at, rows, self.cols].astype(jnp.float32)
            value = value + self.from_core[1, at, :, self.cols].astype(jnp.float32)
            value = value + self.from_y[at, :, self.cols].astype(jnp.float32)
            self.total[at, :, self.cols] = value.astype(LOW)
            return 0

        lax.fori_loop(self.begin, self.begin + self.count, some, 0)

    def finish(self):
        for number in range(3):
            self.hop(number).wait_send()


def reduce_sems():
    return [pltpu.SemaphoreType.DMA((3,)), pltpu.SemaphoreType.DMA((3,))]


def reduce_bufs(ranks, own, cols):
    return [pltpu.VMEM((2, ranks, own, cols), LOW), pltpu.VMEM((ranks, own, cols), LOW)]


class Deliver:
    def __init__(self, rows, out, cols, ranks, sems):
        self.rows, self.out, self.cols, self.ranks = rows, out, cols, ranks
        self.send, self.recv, self.here = sems
        self.seq, self.dp = lax.axis_index("seq"), lax.axis_index("dp")

    def exchange(self):
        for step in range(1, self.ranks):
            peer = lax.rem(self.seq + step, self.ranks)
            yield push(
                self.rows.at[peer, :, self.cols],
                self.out.at[self.seq, :, self.cols],
                self.send.at[step],
                self.recv.at[step],
                (peer, self.dp),
            )

    def keep(self):
        return pltpu.make_async_copy(
            self.rows.at[self.seq, :, self.cols], self.out.at[self.seq, :, self.cols], self.here
        )

    def start(self):
        self.keep().start()
        for copy in self.exchange():
            copy.start()

    def finish(self):
        self.keep().wait()
        for copy in self.exchange():
            copy.wait_recv()
        for copy in self.exchange():
            copy.wait_send()


def deliver_sems(ranks):
    return [pltpu.SemaphoreType.DMA((ranks,)), pltpu.SemaphoreType.DMA((ranks,)), pltpu.SemaphoreType.DMA]


def first_kernel(
    ranks, kv_heads, order, starts, tokens, out_grad, freqs, attn_gain, mlp_gain, query_gain, key_gain,
    w_query, w_key, w_value, w_output, w_gate, w_up, w_down,
    resid, second, cosv, sinv, q_low, k_low, v_low, own_out, first_in, qkv, attn_block, dy_all, prob, mlp_block, out_all,
    held, normal, kept, block, a_rows, m_rows, gate, up, down, dys, probs, pos, begins, pos_row,
    out_low, whole, *sems,
):
    local, width = tokens.shape
    rows = local * ranks
    own = w_query.shape[0]
    size = freqs.shape[1]
    heads = q_low.shape[0]
    share = heads // kv_heads
    half = ranks // 2
    scale = 1.0 / math.sqrt(size)
    cols = (heads + 2 * kv_heads) * size
    deep = block.shape[1]
    row = functools.partial(block_row, local=local, ranks=ranks)
    seq, dp = lax.axis_index("seq"), lax.axis_index("dp")
    right, left = neighbours(ranks)
    attn = Spread(a_rows, block, ranks, own, pl.ds(0, a_rows.shape[2]), sems[12:17])
    third = m_rows.shape[2] // 3
    mlp = [
        Spread(m_rows, mlp_block, ranks, own, pl.ds(at * third, third), sems[17 + 5 * at : 22 + 5 * at])
        for at in range(3)
    ]
    local_sems = sems[32]
    out_send, out_recv = sems[2:4]
    o_cols = heads * size
    peers = [(lax.rem(seq + step, ranks), dp) for step in range(1, ranks)]
    peers += [(seq, attn.beside), (seq, attn.sibling)]
    knock(peers)
    loads = [
        move(src, dst, local_sems.at[at])
        for at, (src, dst) in enumerate(((w_gate, gate), (w_up, up), (w_down, down)))
    ]
    held[pl.ds(row(0), local)] = tokens[...]
    dys[pl.ds(row(0), local)] = out_grad[...]

    def column(line):
        same = lax.broadcasted_iota(jnp.int32, (own, own), 0) == lax.broadcasted_iota(jnp.int32, (own, own), 1)
        return jnp.sum(jnp.where(same, line, 0.0), 1, keepdims=True)

    def lay(target, begin, weight, gain):
        each = weight.shape[1] // ranks
        for rank in range(ranks):
            part = weight[:, rank * each : (rank + 1) * each]
            if gain is not None:
                part = (part.astype(jnp.float32) * gain).astype(LOW)
            target[rank, :, begin : begin + each] = part
        return begin + each

    gain = column(attn_gain[...])
    at = 0
    for weight in (w_query, w_key, w_value):
        at = lay(a_rows, at, weight, gain)
    whole[seq, pl.ds(pl.multiple_of(dp * own, own), own)] = w_output[...]
    answered(peers)
    ring = RingGather(held, local, ranks, sems[0], sems[1], right, left, row)
    ring.start(1)
    attn.start()
    outs = WholeGather(whole, ranks, own, [*sems[8:12], *sems[33:35]])
    outs.forward(0)
    line = LineGather(dys, local, ranks, sems[4], sems[5], sems[6], sems[7])
    stores = []

    def store(src, dst):
        stores.append(move(src, dst, local_sems.at[len(loads) + len(stores)]))

    def scale_rows(step):
        for rel in rels_of(step, ranks):

            def some(at, _):
                rows_at = pl.ds(pl.multiple_of(row(rel) + at * 32, 32), 32)
                normal[rows_at] = rows_scaled(held[rows_at].astype(jnp.float32))[0].astype(LOW)
                return 0

            lax.fori_loop(0, local // 32, some, 0)

    for load in loads:
        load.wait()
    gain = column(mlp_gain[...])
    each = gate.shape[1] // ranks
    lay(m_rows, 0, gate, gain)
    lay(m_rows, each, up, gain)
    lay(m_rows, 2 * each, down, None)
    scale_rows(0)
    def bring(step):
        outs.arrive(step)
        if step < half:
            outs.start(step + 1)
        outs.forward(step)

    def forward(piece):
        mlp[piece].arrive()
        mlp[piece].hop(0).start()
        mlp[piece].hop(1).start()

    def hop_over(piece):
        mlp[piece].hop(0).wait_recv()
        mlp[piece].hop(2).start()

    def pass_on(step):
        ring.advance(step)
        scale_rows(step)

    pass_on(1)
    line.start(1)
    pass_on(2)
    outs.start(1)
    attn.arrive()
    attn.hop(0).start()
    attn.hop(1).start()
    attn.hop(0).wait_recv()
    attn.hop(2).start()
    for step in range(3, half):
        pass_on(step)
    bring(1)
    pass_on(half)
    mlp[0].start()
    spans = order.shape[0]
    span = rows // spans
    for at in range(ranks):
        rows_at = pl.ds(at * local, local)
        ids = at * local + lax.broadcasted_iota(jnp.int32, (1, local), 1)
        where = jnp.zeros_like(ids)
        for slot in range(spans):
            inside = (ids >= slot * span) & (ids < (slot + 1) * span)
            where = where + jnp.where(inside, ids + (order[slot] - slot) * span, 0)
        begin = jnp.zeros_like(ids)
        for doc in range(starts.shape[1]):
            begin = jnp.maximum(begin, jnp.where(starts[0, doc] <= where, starts[0, doc], 0))
        pos_row[:, rows_at] = where
        across = jnp.broadcast_to(where, (local, local)).T
        pos[rows_at] = across[:, :1]
        begins[rows_at] = jnp.broadcast_to(begin, (local, local)).T[:, :1]
        angle = across[:, :1].astype(jnp.float32) * freqs[...]
        lane = lax.broadcasted_iota(jnp.int32, (local, size), 1)
        cosv[rows_at] = jnp.cos(angle)
        sine = jnp.sin(angle)
        sinv[rows_at] = jnp.where(lane < size // 2, -sine, sine)
    bring(2)
    line.advance(1)
    attn.hop(1).wait_recv()
    attn.hop(2).wait_recv()
    store(block, attn_block)

    def project(begin, count):
        rows_at = pl.ds(begin, count)
        kept[rows_at] = dot_nn(normal[rows_at], block[...].reshape(width, cols))

    store(normal, first_in)
    tile = rows // half

    def rotated(at, rows_at, gain):
        v = rows_scaled(kept[rows_at, at * size : (at + 1) * size])[0] * gain[...]
        return (v * cosv[rows_at] + turn(v) * sinv[rows_at]).astype(LOW)

    for piece in range(half):
        rows_at = pl.ds(piece * tile, tile)
        project(piece * tile, tile)
        for head in range(heads):
            q_low[head, rows_at] = rotated(head, rows_at, query_gain)
        for group in range(kv_heads):
            k_low[group, rows_at] = rotated(heads + group, rows_at, key_gain)
            at = (heads + kv_heads + group) * size
            v_low[group, rows_at] = kept[rows_at, at : at + size].astype(LOW)
    store(kept, qkv)
    forward(0)

    for piece in range(half):
        rows_at = pl.ds(piece * tile, tile)
        seen = (pos_row[...] <= pos[rows_at]) & (pos_row[...] >= begins[rows_at])
        for head in range(heads):
            raw = dot_nt(q_low[head, rows_at], k_low[head // share]) * scale
            raw = jnp.where(seen, raw, NEG)
            weight = jnp.exp(raw - jnp.max(raw, -1, keepdims=True))
            weight = (weight * (1.0 / jnp.sum(weight, -1, keepdims=True))).astype(LOW)
            probs[head, rows_at] = weight
            value = dot_nn(weight, v_low[head // share])
            out_low[rows_at, head * size : (head + 1) * size] = value.astype(LOW)
            store(probs.at[head, rows_at], prob.at[head, rows_at])
        if piece == 0:
            bring(3)
        if piece == 1:
            mlp[1].start()
            line.advance(2)
            bring(half)
    mlp[2].start()
    hop_over(0)
    forward(1)
    forward(2)
    place = ring_place(seq, ranks)

    def exchange(rel):
        to = ring_seq(lax.rem(place + rel, ranks), ranks)
        return push(
            out_low.at[pl.ds(row(rel), local)],
            own_out.at[:, pl.ds(pl.multiple_of(seq * o_cols, o_cols), o_cols)],
            out_send.at[rel],
            out_recv.at[rel],
            (to, dp),
        )

    for rel in range(1, ranks):
        exchange(rel).start()
    own_out[:, pl.ds(pl.multiple_of(seq * o_cols, o_cols), o_cols)] = out_low[pl.ds(row(0), local)]
    outs.complete()
    store(whole, out_all)
    hop_over(1)
    for step in range(3, half):
        line.advance(step)
    for rel in range(1, ranks):
        exchange(rel).wait_recv()

    def join(at, _):
        some = pl.ds(pl.multiple_of(at * deep, deep), deep)
        resid[:, some] = tokens[:, some].astype(jnp.float32) + dot_nt(own_out[...], whole[at])
        return 0

    lax.fori_loop(0, ranks, join, 0)

    def scale_second(at, _):
        rows_at = pl.ds(pl.multiple_of(at * 32, 32), 32)
        second[rows_at] = rows_scaled(resid[rows_at])[0].astype(LOW)
        return 0

    lax.fori_loop(0, local // 32, scale_second, 0)
    hop_over(2)
    line.complete()
    store(dys, dy_all)
    ring.finish()
    attn.finish()
    outs.finish()
    for rel in range(1, ranks):
        exchange(rel).wait_send()
    line.finish()
    for piece in mlp:
        piece.hop(1).wait_recv()
        piece.hop(2).wait_recv()
        piece.finish()
    for given in stores:
        given.wait()


def mlp_kernel(
    ranks, second, out_grad, rest, dys, mlp_block, block_out, dresid, dresid_low, own_grads,
    grads, from_core, from_y, held, weights, hidden, dgu, resid, dy_all,
    term, out_buf, in_buf, y_out, y_in, here, *sems,
):
    local, width = second.shape
    row = functools.partial(block_row, local=local, ranks=ranks)
    ff = hidden.shape[1]
    deep = weights.shape[1]
    half = ranks // 2
    right, left = neighbours(ranks)
    loads = [
        move(src, dst, here.at[at])
        for at, (src, dst) in enumerate(((mlp_block, weights), (dys, dy_all), (rest, resid)))
    ]
    seq, dp = lax.axis_index("seq"), lax.axis_index("dp")
    own = own_grads.shape[1]
    pieces = [
        Reduce(
            grads, from_core, from_y, own_grads, own, at * ranks // 4, ranks // 4, pl.ds(0, 3 * ff),
            sems[6 + 2 * at : 8 + 2 * at],
        )
        for at in range(4)
    ]
    peers = [right, left, (seq, pieces[0].beside), (seq, pieces[0].sibling)]
    knock(peers)
    held[pl.ds(row(0), local)] = second[...]
    answered(peers)
    ring = RingGather(held, local, ranks, sems[0], sems[1], right, left, row)
    ring.start(1)
    loads[0].wait()
    loads[1].wait()
    wide = 256

    def middle(step):
        rels = rels_of(step, ranks)

        def some(at, _):
            first = pl.multiple_of(at * wide, wide)
            given, dy = block_rows(held, rels, local, ranks), block_rows(dy_all, rels, local, ranks)
            gate = dot_nn(given, weights[:, :, pl.ds(first, wide)].reshape(width, wide))
            upper = dot_nn(given, weights[:, :, pl.ds(ff + first, wide)].reshape(width, wide))
            dmid = dot_nn(dy, weights[:, :, pl.ds(2 * ff + first, wide)].reshape(width, wide))
            sigma = 1.0 / (1.0 + jnp.exp(-gate))
            act = gate * sigma
            value = (act * upper).astype(LOW)
            dgate = (dmid * upper * (sigma * (1.0 + gate * (1.0 - sigma)))).astype(LOW)
            dupper = (dmid * act).astype(LOW)
            for at, rel in enumerate(rels):
                rows, some_rows = pl.ds(row(rel), local), slice(at * local, (at + 1) * local)
                hidden[rows, pl.ds(first, wide)] = value[some_rows]
                dgu[rows, pl.ds(first, wide)] = dgate[some_rows]
                dgu[rows, pl.ds(ff + first, wide)] = dupper[some_rows]
            return 0

        lax.fori_loop(0, ff // wide, some, 0)

    middle(0)
    for step in range(1, half + 1):
        ring.advance(step)
        middle(step)

    def back_part(rels, begin, end):
        def some(at, _):
            value = dot_nt(block_rows(dgu, rels, local, ranks), weights[at, :, : 2 * ff])
            term[: len(rels) * local, pl.ds(pl.multiple_of(at * deep, deep), deep)] = value
            return 0

        lax.fori_loop(begin, end, some, 0)

    def out_part(rels, begin, end):
        def some(at, _):
            value = dot_nt(block_rows(hidden, rels, local, ranks), weights[at, :, 2 * ff :])
            term[: len(rels) * local, pl.ds(pl.multiple_of(at * deep, deep), deep)] = value
            return 0

        lax.fori_loop(begin, end, some, 0)

    def weight_grads(first, count):
        def some(at, _):
            cols = pl.ds(pl.multiple_of(at * deep, deep), deep)
            grads[at, :, : 2 * ff] = dot_tn(held[:, cols], dgu[...]).astype(LOW)
            grads[at, :, 2 * ff :] = dot_tn(dy_all[:, cols], hidden[...]).astype(LOW)
            return 0

        lax.fori_loop(first, first + count, some, 0)

    back = RingSum(back_part, term, out_buf, in_buf, local, ranks, sems[2], sems[3], right, left)
    out = RingSum(out_part, term, y_out, y_in, local, ranks, sems[4], sems[5], right, left)
    for step in range(1, half + 1):
        back.compute(step)
        back.launch(step)
        out.compute(step)
        out.launch(step)
        made, passed, summed = (((0, 1), (2,), (3,), ()), ((), (0, 1), (2,), (3,)), ((), (), (0, 1), (2,)))
        for piece in (pieces[at] for at in made[step - 1]):
            weight_grads(piece.begin, piece.count)
            piece.first()
        for at in passed[step - 1]:
            pieces[at].second()
        for at in summed[step - 1]:
            pieces[at].third()
    back.compute(half + 1)
    loads[2].wait()
    back.arrive_last()

    def finish_back(at, _):
        begin = pl.multiple_of(at * 32, 32)
        rows = pl.ds(begin, 32)
        value = resid[rows]
        inv = rows_scaled(value)[1]
        grad = back.last(begin, 32)
        full = out_grad[rows].astype(jnp.float32) + rows_scaled_back(value, inv, grad)
        dresid[rows] = full
        dresid_low[rows] = full.astype(LOW)
        return 0

    lax.fori_loop(0, local // 32, finish_back, 0)
    out.compute(half + 1)
    out.arrive_last()

    def finish_out(at, _):
        begin = pl.multiple_of(at * 32, 32)
        rows = pl.ds(begin, 32)
        block_out[rows] = (resid[rows] + out.last(begin, 32)).astype(LOW)
        return 0

    lax.fori_loop(0, local // 32, finish_out, 0)
    ring.finish()
    pieces[3].third()
    back.finish()
    out.finish()
    for piece in pieces:
        piece.finish()


def back_kernel(
    ranks, kv_heads, tokens, dresid_low, query_gain, key_gain, own_out, first_in_in, block_in,
    qkv_in, cos_in, sin_in, q_in, k_in, v_in, prob_in, dresid_in, mlp_own, out_all,
    tokens_grad, gains, out_grad, mlp_sums, attn_sums,
    grads, from_core, from_y, own_grads, query_gain_grad, key_gain_grad,
    tile, tiles_in, tile_sum, tile_sums_in, dob, dout, dk, dv, dqkv,
    first_in, attn_block, qkv, cosv, sinv, q_low, k_low, v_low, prob, dresid, term, out_buf, in_buf,
    o_grads, o_core, o_y, o_own, o_term, o_out, o_in, *sems,
):
    local, width = tokens.shape
    rows = local * ranks
    half = ranks // 2
    size = cosv.shape[1]
    heads = q_low.shape[0]
    share = heads // kv_heads
    scale = 1.0 / math.sqrt(size)
    cols = (heads + 2 * kv_heads) * size
    deep = attn_block.shape[1]
    o_cols = heads * size
    right, left = neighbours(ranks)
    seq, dp = lax.axis_index("seq"), lax.axis_index("dp")
    own = mlp_own.shape[1]
    copies = lax.axis_size("dp")
    row = functools.partial(block_row, local=local, ranks=ranks)
    place = ring_place(seq, ranks)
    out_piece = Reduce(o_grads, o_core, o_y, o_own, own, 0, ranks, pl.ds(0, width), sems[4:6])
    qkv_piece = Reduce(grads, from_core, from_y, own_grads, own, 0, ranks, pl.ds(0, cols), sems[6:8])
    third = mlp_own.shape[2] // 3
    mlp_ways = [
        Deliver(mlp_own, mlp_sums, pl.ds(at * third, third), ranks, [*sems[8:11], *sems[22:28]][3 * at : 3 * at + 3])
        for at in range(3)
    ]
    dob_send, dob_recv = sems[0:2]
    qkv_way = Deliver(own_grads, attn_sums, pl.ds(0, cols), ranks, sems[14:17])
    peers = [(lax.rem(seq + step, ranks), dp) for step in range(1, ranks)]
    peers += [(seq, lax.rem(dp + step, copies)) for step in range(1, copies)]
    knock(peers)
    local_sems = sems[21]
    loads = {}
    for at, (name, src, dst) in enumerate(
        (
            ("out", out_all, o_grads), ("block", block_in, attn_block), ("v", v_in, v_low),
            ("prob", prob_in, prob), ("k", k_in, k_low), ("q", q_in, q_low), ("cos", cos_in, cosv),
            ("sin", sin_in, sinv), ("qkv", qkv_in, qkv), ("first", first_in_in, first_in),
            ("dresid", dresid_in, dresid),
        )
    ):
        loads[name] = move(src, dst, local_sems.at[at])
    answered(peers)
    loads["out"].wait()

    def columns_of(rank):
        return pl.ds(pl.multiple_of(rank * o_cols, o_cols), o_cols)

    def owner(rel):
        return ring_seq(lax.rem(place + rel, ranks), ranks)

    def exchange(rel):
        to = owner(rel)
        return push(
            dob.at[:, columns_of(to)], dout.at[pl.ds(row(0), local)], dob_send.at[rel], dob_recv.at[rel], (to, dp)
        )

    def project(rel):
        some = columns_of(owner(rel))
        dob[:, some] = dot_nn(dresid_low[...], o_grads[:, :, some].reshape(width, o_cols)).astype(LOW)

    for rel in (*ring_order(ranks)[1:][::-1], 0):
        project(rel)
        if rel:
            exchange(rel).start()
    dout[pl.ds(row(0), local)] = dob[:, columns_of(seq)]
    mlp_ways[0].start()

    def out_grads(at, _):
        some_cols = pl.ds(pl.multiple_of(at * deep, deep), deep)
        o_grads[at] = dot_tn(dresid_low[:, some_cols], own_out[...]).astype(LOW)
        return 0

    lax.fori_loop(0, ranks, out_grads, 0)
    out_piece.first()
    for rel in range(1, ranks):
        exchange(rel).wait_recv()
    for name in ("v", "prob", "k", "q", "cos", "sin", "qkv"):
        loads[name].wait()
    tall = rows // half
    query_gain_grad[...] = jnp.zeros_like(query_gain_grad)
    key_gain_grad[...] = jnp.zeros_like(key_gain_grad)

    def unrotated(grad, column, rows_at, gain, gain_grad_ref):
        grad = grad * cosv[rows_at] - turn(grad) * sinv[rows_at]
        value = qkv[rows_at, column * size : (column + 1) * size]
        normal, inv = rows_scaled(value)
        gain_grad_ref[...] += jnp.sum(grad * normal, 0, keepdims=True)
        back = rows_scaled_back(value, inv, grad * gain[...])
        dqkv[rows_at, column * size : (column + 1) * size] = back.astype(LOW)

    for head in range(heads):
        group = head // share

        def one(piece, _):
            rows_at = pl.ds(pl.multiple_of(piece * tall, tall), tall)
            weight = prob[head, rows_at]
            grad = dout[rows_at, head * size : (head + 1) * size]
            dprob = dot_nt(grad, v_low[group])
            full = weight.astype(jnp.float32)
            delta = jnp.sum(full * dprob, -1, keepdims=True)
            dscore = (full * (dprob - delta)).astype(LOW)
            dq = dot_nn(dscore, k_low[group]) * scale
            dk_add = dot_tn(dscore, q_low[head, rows_at]) * scale
            dv_add = dot_tn(weight, grad)
            dk[group] += dk_add
            dv[group] += dv_add
            unrotated(dq, head, rows_at, query_gain, query_gain_grad)
            return 0

        if head % share == 0:
            dk[group] = jnp.zeros_like(dk[group])
            dv[group] = jnp.zeros_like(dv[group])
        lax.fori_loop(0, half, one, 0)
        if head == 0:
            out_piece.second()
            mlp_ways[1].start()
    for group in range(kv_heads):
        def one_key(piece, _):
            rows_at = pl.ds(pl.multiple_of(piece * tall, tall), tall)
            unrotated(dk[group, rows_at], heads + group, rows_at, key_gain, key_gain_grad)
            at = (heads + kv_heads + group) * size
            dqkv[rows_at, at : at + size] = dv[group, rows_at].astype(LOW)
            return 0

        lax.fori_loop(0, half, one_key, 0)

    def part(rels, begin, end):
        def some(at, _):
            value = dot_nt(block_rows(dqkv, rels, local, ranks), attn_block[at])
            term[: len(rels) * local, pl.ds(pl.multiple_of(at * deep, deep), deep)] = value
            return 0

        lax.fori_loop(begin, end, some, 0)

    def qkv_grads(at, _):
        some_cols = pl.ds(pl.multiple_of(at * deep, deep), deep)
        grads[at] = dot_tn(first_in[:, some_cols], dqkv[...]).astype(LOW)
        return 0

    def to_ranks(step):
        peer = lax.rem(seq + step, ranks)
        return push(tile, tiles_in.at[seq], sems[17].at[step], sems[18].at[step], (peer, dp))

    def to_copies(step):
        peer = lax.rem(dp + step, copies)
        return push(
            tile_sum, tile_sums_in.at[dp], sems[19].at[step], sems[20].at[step], (seq, peer)
        )

    tile[0:1] = query_gain_grad[...]
    tile[1:2] = key_gain_grad[...]
    tile[2:] = jnp.zeros((tile.shape[0] - 2, size), jnp.float32)
    for step in range(1, ranks):
        to_ranks(step).start()
    tiles_in[seq] = tile[...]
    mlp_ways[2].start()
    loads["block"].wait()

    def out_part(rels, begin, end):
        for at, rel in enumerate(rels):
            o_term[at * own : (at + 1) * own] = o_own[owner(rel)].astype(jnp.float32)

    out_total = RingSum(out_part, o_term, o_out, o_in, own, ranks, sems[30], sems[31], right, left)
    totals = two_sums(part, term, out_buf, in_buf, local, ranks, [*sems[2:4], *sems[28:30]], right, left)
    for step in range(1, half + 1):
        for total in totals:
            total.compute(step)
            total.launch(step)
        if step == 1:
            loads["first"].wait()
            lax.fori_loop(0, ranks, qkv_grads, 0)
            qkv_piece.first()
        if step == 2:
            qkv_piece.second()
            for other in range(1, ranks):
                to_ranks(other).wait_recv()
            tile_sum[...] = jnp.sum(tiles_in[...], 0)
            for other in range(1, copies):
                to_copies(other).start()
            tile_sums_in[dp] = tile_sum[...]
        if step == half - 1:
            for other in range(1, copies):
                to_copies(other).wait_recv()
            gains[...] = jnp.sum(tile_sums_in[...], 0)
            qkv_piece.third()
            qkv_way.start()
    out_piece.third()
    for step in range(1, half + 1):
        out_total.compute(step)
        out_total.launch(step)
    for total in totals:
        total.compute(half + 1)
    loads["dresid"].wait()
    for total in totals:
        total.arrive_last()

    def last(at, _):
        begin = pl.multiple_of(at * 32, 32)
        rows_at = pl.ds(begin, 32)
        value = tokens[rows_at].astype(jnp.float32)
        inv = rows_scaled(value)[1]
        grad = jnp.concatenate([total.last(begin, 32) for total in totals], 1)
        tokens_grad[rows_at] = dresid[rows_at] + rows_scaled_back(value, inv, grad)
        return 0

    lax.fori_loop(0, local // 32, last, 0)
    out_total.compute(half + 1)
    out_total.arrive_last()
    out_grad[...] = out_total.last(0, own)
    for step in range(1, ranks):
        to_ranks(step).wait_send()
    for step in range(1, copies):
        to_copies(step).wait_send()
    out_total.finish()
    for rel in range(1, ranks):
        exchange(rel).wait_send()
    for total in totals:
        total.finish()
    out_piece.finish()
    qkv_piece.finish()
    for way in mlp_ways:
        way.finish()
    qkv_way.finish()


def leave_kernel(
    attn_sums, mlp_sums, attn_gain, mlp_gain, w_query, w_key, w_value, w_gate, w_up,
    query_out, key_out, value_out, gate_out, up_out, down_out, attn_out, mlp_out,
):
    own = attn_gain.shape[1]
    same = lax.broadcasted_iota(jnp.int32, (own, own), 0) == lax.broadcasted_iota(jnp.int32, (own, own), 1)

    @pl.when(pl.program_id(0) == 0)
    def _():
        attn_out[...] = jnp.zeros_like(attn_out)
        mlp_out[...] = jnp.zeros_like(mlp_out)

    for sums, gain, gain_out, parts in (
        (attn_sums, attn_gain, attn_out, ((query_out, w_query), (key_out, w_key), (value_out, w_value))),
        (mlp_sums, mlp_gain, mlp_out, ((gate_out, w_gate), (up_out, w_up), (down_out, None))),
    ):
        scale = jnp.sum(jnp.where(same, gain[...], 0.0), 1, keepdims=True)
        at = 0
        for out, weight in parts:
            value = sums[0, :, at : at + out.shape[1]].astype(jnp.float32)
            at += out.shape[1]
            if weight is None:
                out[...] = value
                continue
            out[...] = value * scale
            inner = jnp.sum(value * weight[...].astype(jnp.float32), 1, keepdims=True)
            gain_out[...] += jnp.sum(jnp.where(same, inner, 0.0), 0, keepdims=True)


VM = pl.BlockSpec(memory_space=pltpu.VMEM)
SM = pl.BlockSpec(memory_space=pltpu.SMEM)
ANY = pl.BlockSpec(memory_space=pl.ANY)


def call(kernel, number, ins, outs, scratch, operands):
    return pl.pallas_call(
        kernel,
        out_shape=[jax.ShapeDtypeStruct(shape, dtype) for shape, dtype, _ in outs],
        in_specs=ins,
        out_specs=[spec for _, _, spec in outs],
        scratch_shapes=scratch,
        compiler_params=pltpu.CompilerParams(
            collective_id=number, has_side_effects=True, vmem_limit_bytes=LIMIT
        ),
    )(*operands)


def columns_body(
    tokens,
    out_grad,
    span_order,
    doc_starts,
    w_query,
    w_key,
    w_value,
    w_output,
    attn_gain,
    query_gain,
    key_gain,
    w_gate,
    w_up,
    w_down,
    mlp_gain,
):
    ranks = lax.axis_size("seq")
    copies = lax.axis_size("dp")
    _, local, width = tokens.shape
    rows = local * ranks
    size = query_gain.shape[0]
    kv_heads = w_key.shape[1] // size // ranks
    heads = w_query.shape[1] // size // ranks
    q_cols, kv_cols = heads * size, kv_heads * size
    qkv_cols = q_cols + 2 * kv_cols
    ff = w_gate.shape[1] // ranks
    own = width // (ranks * copies)
    deep = own * copies
    half = ranks // 2
    f32, i32 = jnp.float32, jnp.int32
    exponents = np.arange(size) % (size // 2) * (-2.0 / size * math.log(1000000.0))
    freqs = jnp.asarray(np.exp(exponents)[None], f32)
    q_gain, k_gain = query_gain[None], key_gain[None]
    (
        resid, second, cosv, sinv, q_low, k_low, v_low, own_out, first_in, qkv, attn_block, dy_all, prob, mlp_block,
        out_all,
    ) = call(
        functools.partial(first_kernel, ranks, kv_heads),
        1,
        [SM, SM] + [VM] * 11 + [ANY] * 3,
        [
            ((local, width), f32, VM),
            ((local, width), LOW, VM),
            ((rows, size), f32, VM),
            ((rows, size), f32, VM),
            ((heads, rows, size), LOW, VM),
            ((kv_heads, rows, size), LOW, VM),
            ((kv_heads, rows, size), LOW, VM),
            ((local, q_cols * ranks), LOW, VM),
            ((rows, width), LOW, ANY),
            ((rows, qkv_cols), f32, ANY),
            ((ranks, deep, qkv_cols), LOW, ANY),
            ((rows, width), LOW, ANY),
            ((heads, rows, rows), LOW, ANY),
            ((ranks, deep, 3 * ff), LOW, ANY),
            ((ranks, deep, q_cols * ranks), LOW, ANY),
        ],
        [
            pltpu.VMEM((rows, width), LOW),
            pltpu.VMEM((rows, width), LOW),
            pltpu.VMEM((rows, qkv_cols), f32),
            pltpu.VMEM((ranks, deep, qkv_cols), LOW),
            pltpu.VMEM((ranks, own, qkv_cols), LOW),
            pltpu.VMEM((ranks, own, 3 * ff), LOW),
        ]
        + [pltpu.VMEM((own, ff * ranks), LOW)] * 3
        + [
            pltpu.VMEM((rows, width), LOW),
            pltpu.VMEM((heads, rows, rows), LOW),
            pltpu.VMEM((rows, 1), i32),
            pltpu.VMEM((rows, 1), i32),
            pltpu.VMEM((1, rows), i32),
            pltpu.VMEM((rows, q_cols), LOW),
            pltpu.VMEM((ranks, deep, q_cols * ranks), LOW),
        ]
        + ring_sems(ranks)
        + [pltpu.SemaphoreType.DMA((ranks,))] * 2
        + line_sems(ranks)
        + whole_sems(ranks)[:4]
        + spread_sems(ranks) * 4
        + [pltpu.SemaphoreType.DMA((heads * half + 8,))]
        + whole_sems(ranks)[4:],
        (
            span_order, doc_starts, tokens[0], out_grad[0], freqs, attn_gain[None], mlp_gain[None], q_gain, k_gain,
            w_query, w_key, w_value, w_output, w_gate, w_up, w_down,
        ),
    )
    block_out, dresid, dresid_low, mlp_own = call(
        functools.partial(mlp_kernel, ranks),
        2,
        [VM, VM, ANY, ANY, ANY],
        [
            ((local, width), LOW, VM),
            ((local, width), f32, VM),
            ((local, width), LOW, VM),
            ((ranks, own, 3 * ff), LOW, VM),
        ],
        [pltpu.VMEM((ranks, deep, 3 * ff), LOW)]
        + reduce_bufs(ranks, own, 3 * ff)
        + [
            pltpu.VMEM((rows, width), LOW),
            pltpu.VMEM((ranks, deep, 3 * ff), LOW),
            pltpu.VMEM((rows, ff), LOW),
            pltpu.VMEM((rows, 2 * ff), LOW),
            pltpu.VMEM((local, width), f32),
            pltpu.VMEM((rows, width), LOW),
        ]
        + sum_bufs(local, ranks, width)
        + sum_bufs(local, ranks, width)[1:]
        + [pltpu.SemaphoreType.DMA((3,))]
        + ring_sems(ranks) * 3
        + reduce_sems() * 4,
        (second, out_grad[0], resid, dy_all, mlp_block),
    )
    tokens_grad, gains, wo_grad, mlp_sums, attn_sums = call(
        functools.partial(back_kernel, ranks, kv_heads),
        3,
        [VM] * 5 + [ANY] * 12,
        [
            ((local, width), f32, VM),
            ((8, size), f32, VM),
            ((own, q_cols * ranks), f32, VM),
            ((ranks, own, 3 * ff), LOW, ANY),
            ((ranks, own, qkv_cols), LOW, VM),
        ],
        [pltpu.VMEM((ranks, deep, qkv_cols), LOW)]
        + reduce_bufs(ranks, own, qkv_cols)
        + [
            pltpu.VMEM((ranks, own, qkv_cols), LOW),
            pltpu.VMEM((1, size), f32),
            pltpu.VMEM((1, size), f32),
            pltpu.VMEM((8, size), f32),
            pltpu.VMEM((ranks, 8, size), f32),
            pltpu.VMEM((8, size), f32),
            pltpu.VMEM((copies, 8, size), f32),
            pltpu.VMEM((local, q_cols * ranks), LOW),
            pltpu.VMEM((rows, q_cols), LOW),
            pltpu.VMEM((kv_heads, rows, size), f32),
            pltpu.VMEM((kv_heads, rows, size), f32),
            pltpu.VMEM((rows, qkv_cols), LOW),
            pltpu.VMEM((rows, width), LOW),
            pltpu.VMEM((ranks, deep, qkv_cols), LOW),
            pltpu.VMEM((rows, qkv_cols), f32),
            pltpu.VMEM((rows, size), f32),
            pltpu.VMEM((rows, size), f32),
            pltpu.VMEM((heads, rows, size), LOW),
            pltpu.VMEM((kv_heads, rows, size), LOW),
            pltpu.VMEM((kv_heads, rows, size), LOW),
            pltpu.VMEM((heads, rows, rows), LOW),
            pltpu.VMEM((local, width), f32),
        ]
        + sum_bufs(local, ranks, width)
        + [pltpu.VMEM((ranks, deep, q_cols * ranks), LOW)]
        + reduce_bufs(ranks, own, q_cols * ranks)
        + [pltpu.VMEM((ranks, own, q_cols * ranks), LOW)]
        + sum_bufs(own, ranks, q_cols * ranks)
        + [pltpu.SemaphoreType.DMA((ranks,))] * 2
        + ring_sems(ranks)
        + reduce_sems() * 2
        + deliver_sems(ranks) * 3
        + [pltpu.SemaphoreType.DMA((ranks,))] * 2
        + [pltpu.SemaphoreType.DMA((copies,))] * 2
        + [pltpu.SemaphoreType.DMA((11,))]
        + deliver_sems(ranks) * 2
        + ring_sems(ranks) * 2,
        (
            tokens[0], dresid_low, q_gain, k_gain, own_out, first_in, attn_block, qkv, cosv, sinv, q_low, k_low,
            v_low, prob, dresid, mlp_own, out_all,
        ),
    )
    whole = pl.BlockSpec((1, own), lambda at: (0, 0))
    each = (q_cols, kv_cols, kv_cols, ff, ff, ff)
    columns = [pl.BlockSpec((own, cols), lambda at: (0, at)) for cols in each]
    *grads, dga, dgm = pl.pallas_call(
        leave_kernel,
        grid=(ranks,),
        out_shape=[jax.ShapeDtypeStruct((own, cols * ranks), f32) for cols in each]
        + [jax.ShapeDtypeStruct((1, own), f32)] * 2,
        in_specs=[
            pl.BlockSpec((1, own, qkv_cols), lambda at: (at, 0, 0)),
            pl.BlockSpec((1, own, 3 * ff), lambda at: (at, 0, 0)),
            whole,
            whole,
            *columns[:3],
            *columns[3:5],
        ],
        out_specs=columns + [whole, whole],
    )(attn_sums, mlp_sums, attn_gain[None], mlp_gain[None], w_query, w_key, w_value, w_gate, w_up)
    return (
        block_out[None], tokens_grad[None], *grads[:3], wo_grad, dga[0], gains[0], gains[1], *grads[3:], dgm[0],
    )


def body(*args):
    tokens, w_key, query_gain = args[0], args[5], args[9]
    groups = w_key.shape[1] // query_gain.shape[0]
    ranks = lax.axis_size("seq")
    if tokens.shape[0] == 1 and ranks % 2 == 0 and groups % ranks == 0 and lax.axis_size("dp") == 4:
        return columns_body(*args)
    return gathered_body(*args)


def solution(mesh):
    return jax.shard_map(
        body,
        mesh=mesh,
        in_specs=(
            P("dp", "seq", None),
            P("dp", "seq", None),
            P(),
            P("dp", None),
            P(("seq", "dp"), None),
            P(("seq", "dp"), None),
            P(("seq", "dp"), None),
            P(("seq", "dp"), None),
            P(("seq", "dp")),
            P(),
            P(),
            P(("seq", "dp"), None),
            P(("seq", "dp"), None),
            P(("seq", "dp"), None),
            P(("seq", "dp")),
        ),
        out_specs=(
            P("dp", "seq", None),
            P("dp", "seq", None),
            P(("seq", "dp"), None),
            P(("seq", "dp"), None),
            P(("seq", "dp"), None),
            P(("seq", "dp"), None),
            P(("seq", "dp")),
            P(),
            P(),
            P(("seq", "dp"), None),
            P(("seq", "dp"), None),
            P(("seq", "dp"), None),
            P(("seq", "dp")),
        ),
        check_vma=False,
    )
```

```python
import functools
import math

import jax
import jax.numpy as jnp
import numpy as np
from jax import lax
from jax.experimental import pallas as pl
from jax.experimental.pallas import tpu as pltpu
from jax.sharding import PartitionSpec as P

EPS = 1e-06
NEG = -1e30


def normed(v, gain):
    scale_inv = lax.rsqrt(jnp.mean(v * v, -1, keepdims=True) + EPS)
    return (v * scale_inv * gain, scale_inv)


def norm_back(v, scale_inv, gain, grad):
    scaled = grad * gain
    inner = jnp.mean(scaled * v, -1, keepdims=True)
    dv = scale_inv * scaled - v * scale_inv * scale_inv * scale_inv * inner
    dgain = jnp.sum((grad * v * scale_inv).reshape(-1, v.shape[-1]), 0)
    return (dv, dgain)


def rotary(pos, width):
    half = width // 2
    freqs = jnp.exp(jnp.arange(half, dtype=jnp.float32) * (-2.0 / width * math.log(1000000.0)))
    angle = pos.astype(jnp.float32)[:, None] * freqs[None, :]
    return (jnp.cos(angle)[:, None, :], jnp.sin(angle)[:, None, :])


def rotate(v, cosv, sinv):
    half = v.shape[-1] // 2
    first, second = (v[..., :half], v[..., half:])
    return jnp.concatenate([first * cosv - second * sinv, second * cosv + first * sinv], -1)


def rotate_back(grad, cosv, sinv):
    half = grad.shape[-1] // 2
    first, second = (grad[..., :half], grad[..., half:])
    return jnp.concatenate([first * cosv + second * sinv, second * cosv - first * sinv], -1)


def place(order, begin, count, span):
    rows = begin + jnp.arange(count, dtype=jnp.int32)
    slots = rows // span
    picked = slots[:, None] == jnp.arange(order.shape[0], dtype=jnp.int32)[None, :]
    return jnp.sum(jnp.where(picked, order[None, :], 0), -1) * span + rows % span


def doc_of(starts, pos):
    return jnp.sum((starts[:, None, :] <= pos[None, :, None]).astype(jnp.int32), -1)


def gathered_body(
    tokens,
    out_grad,
    span_order,
    doc_starts,
    w_query,
    w_key,
    w_value,
    w_output,
    attn_gain,
    query_gain,
    key_gain,
    w_gate,
    w_up,
    w_down,
    mlp_gain,
):
    seqs, local, width = tokens.shape
    span = local // 2
    head_size = query_gain.shape[0]
    kv_heads = w_key.shape[1] // head_size
    heads = w_query.shape[1] // head_size
    share = heads // kv_heads
    kv_width = kv_heads * head_size
    ff_width = w_gate.shape[1]
    scale = 1.0 / math.sqrt(head_size)
    total_rows = seqs * local
    own_rows = width // lax.axis_size(("seq", "dp"))
    qpos = place(span_order, lax.axis_index("seq") * local, local, span)
    qdoc = doc_of(doc_starts, qpos)
    cosv, sinv = rotary(qpos, head_size)

    def gather_attn():
        return (
            lax.all_gather(w_query, ("seq", "dp"), axis=0, tiled=True),
            lax.all_gather(w_key, ("seq", "dp"), axis=0, tiled=True),
            lax.all_gather(w_value, ("seq", "dp"), axis=0, tiled=True),
            lax.all_gather(w_output, ("seq", "dp"), axis=0, tiled=True),
            lax.all_gather(
                attn_gain.astype(jnp.bfloat16), ("seq", "dp"), axis=0, tiled=True
            ).astype(attn_gain.dtype),
        )

    def gather_mlp():
        return (
            lax.all_gather(w_gate, ("seq", "dp"), axis=0, tiled=True),
            lax.all_gather(w_up, ("seq", "dp"), axis=0, tiled=True),
            lax.all_gather(w_down, ("seq", "dp"), axis=0, tiled=True),
            lax.all_gather(mlp_gain.astype(jnp.bfloat16), ("seq", "dp"), axis=0, tiled=True).astype(
                mlp_gain.dtype
            ),
        )

    x_rows = tokens.astype(jnp.float32).reshape(total_rows, width)
    wq_all, wk_all, wv_all, wo_all, ga_all = gather_attn()
    first_norm, first_inv = normed(x_rows, ga_all)
    first_in = first_norm.astype(jnp.bfloat16)
    q_raw = jnp.dot(first_in, wq_all, preferred_element_type=jnp.float32).reshape(
        seqs, local, heads, head_size
    )
    k_raw = jnp.dot(first_in, wk_all, preferred_element_type=jnp.float32).reshape(
        seqs, local, kv_heads, head_size
    )
    v_low = (
        jnp.dot(first_in, wv_all, preferred_element_type=jnp.float32)
        .astype(jnp.bfloat16)
        .reshape(seqs, local, kv_heads, head_size)
    )
    q_normed, q_inv = normed(q_raw, query_gain)
    k_normed, k_inv = normed(k_raw, key_gain)
    q_low = rotate(q_normed, cosv, sinv).astype(jnp.bfloat16)
    k_low = rotate(k_normed, cosv, sinv).astype(jnp.bfloat16)
    q_group = q_low.reshape(seqs, local, kv_heads, share, head_size)

    def scores(piece_key, start):
        count = piece_key.shape[1]
        kpos = place(span_order, start, count, span)
        kdoc = doc_of(doc_starts, kpos)
        visible = (qdoc[:, :, None] == kdoc[:, None, :]) & (
            kpos[None, None, :] <= qpos[None, :, None]
        )
        raw = (
            jnp.einsum("sqgjd,skgd->sgjqk", q_group, piece_key, preferred_element_type=jnp.float32)
            * scale
        )
        return (raw, visible[:, None, None])

    start_top = jnp.full((seqs, kv_heads, share, local), NEG, jnp.float32)
    piece = (
        lax.all_gather(k_low, "seq", axis=1, tiled=True),
        lax.all_gather(v_low, "seq", axis=1, tiled=True),
    )
    top = start_top
    raw, visible = scores(piece[0], jnp.int32(0))
    raw = jnp.where(visible, raw, NEG)
    new_top = jnp.maximum(top, jnp.max(raw, -1))
    weights = jnp.where(visible, jnp.exp(raw - new_top[..., None]), 0.0)
    total = jnp.sum(weights, -1)
    summed = jnp.einsum(
        "sgjqk,skgd->sgjqd",
        weights.astype(jnp.bfloat16),
        piece[1],
        preferred_element_type=jnp.float32,
    )
    top, total, summed = (new_top, total, summed)
    log_total = top + jnp.log(total)
    attn_vals = summed / total[..., None]
    out_low = (
        jnp.transpose(attn_vals, (0, 3, 1, 2, 4))
        .reshape(total_rows, heads * head_size)
        .astype(jnp.bfloat16)
    )
    resid = x_rows + jnp.einsum("nh,dh->nd", out_low, wo_all, preferred_element_type=jnp.float32)
    wg_all, wu_all, wd_all, gm_all = gather_mlp()
    second_norm, second_inv = normed(resid, gm_all)
    second_in = second_norm.astype(jnp.bfloat16)
    gate = jnp.dot(second_in, wg_all, preferred_element_type=jnp.float32)
    upper = jnp.dot(second_in, wu_all, preferred_element_type=jnp.float32)
    sigma = jax.nn.sigmoid(gate)
    act = gate * sigma
    hidden = (act * upper).astype(jnp.bfloat16)
    result = resid + jnp.einsum("nf,df->nd", hidden, wd_all, preferred_element_type=jnp.float32)
    block_out = result.astype(jnp.bfloat16).reshape(seqs, local, width)
    grad_low = out_grad.reshape(total_rows, width)
    wg_all, wu_all, wd_all, gm_all = gather_mlp()
    dmid = jnp.einsum("nd,df->nf", grad_low, wd_all, preferred_element_type=jnp.float32)
    dgate = (dmid * upper * sigma * (1.0 + gate * (1.0 - sigma))).astype(jnp.bfloat16)
    dupper = (dmid * act).astype(jnp.bfloat16)
    left = second_in
    outer = grad_low
    mlp_sums = lax.psum_scatter(
        jnp.concatenate(
            [
                jnp.einsum("nd,nf->df", left, dgate, preferred_element_type=jnp.float32),
                jnp.einsum("nd,nf->df", left, dupper, preferred_element_type=jnp.float32),
                jnp.einsum("nd,nf->df", outer, hidden, preferred_element_type=jnp.float32),
            ],
            1,
        ),
        ("seq", "dp"),
        scatter_dimension=0,
        tiled=True,
    )
    dsecond = jnp.einsum(
        "nf,df->nd", dgate, wg_all, preferred_element_type=jnp.float32
    ) + jnp.einsum("nf,df->nd", dupper, wu_all, preferred_element_type=jnp.float32)
    dresid_norm, dgm = norm_back(resid, second_inv, gm_all, dsecond)
    dresid = grad_low.astype(jnp.float32) + dresid_norm
    dresid_low = dresid.astype(jnp.bfloat16)
    wq_all, wk_all, wv_all, wo_all, ga_all = gather_attn()
    dout_low = jnp.einsum(
        "nd,dh->nh", dresid_low, wo_all, preferred_element_type=jnp.float32
    ).astype(jnp.bfloat16)
    dout_group = dout_low.reshape(seqs, local, kv_heads, share, head_size)
    delta = jnp.sum(jnp.transpose(dout_group.astype(jnp.float32), (0, 2, 3, 1, 4)) * attn_vals, -1)
    piece = (
        lax.all_gather(k_low, "seq", axis=1, tiled=True),
        lax.all_gather(v_low, "seq", axis=1, tiled=True),
    )
    count = piece[0].shape[1]
    raw, visible = scores(piece[0], jnp.int32(0))
    prob = jnp.where(visible, jnp.exp(raw - log_total[..., None]), 0.0)
    dprob = jnp.einsum(
        "sqgjd,skgd->sgjqk", dout_group, piece[1], preferred_element_type=jnp.float32
    )
    dscore = (prob * (dprob - delta[..., None])).astype(jnp.bfloat16)
    dq_sum = jnp.einsum("sgjqk,skgd->sqgjd", dscore, piece[0], preferred_element_type=jnp.float32)
    dk_part = (
        jnp.einsum("sgjqk,sqgjd->skgd", dscore, q_group, preferred_element_type=jnp.float32) * scale
    )
    dv_part = jnp.einsum(
        "sgjqk,sqgjd->skgd",
        prob.astype(jnp.bfloat16),
        dout_group,
        preferred_element_type=jnp.float32,
    )
    joined = jnp.concatenate(
        [dk_part.reshape(seqs, count, kv_width), dv_part.reshape(seqs, count, kv_width)], -1
    )
    buffer = joined
    dq_sum, buffer = (dq_sum, buffer)
    key_sums = lax.psum_scatter(
        buffer.astype(jnp.bfloat16), "seq", scatter_dimension=1, tiled=True
    ).astype(jnp.float32)
    dq_rot = (dq_sum * scale).reshape(seqs, local, heads, head_size)
    dq_raw, dgq = norm_back(q_raw, q_inv, query_gain, rotate_back(dq_rot, cosv, sinv))
    dk_rot = key_sums[..., :kv_width].reshape(seqs, local, kv_heads, head_size)
    dk_raw, dgk = norm_back(k_raw, k_inv, key_gain, rotate_back(dk_rot, cosv, sinv))
    dq_low = dq_raw.reshape(total_rows, heads * head_size).astype(jnp.bfloat16)
    dk_low = dk_raw.reshape(total_rows, kv_width).astype(jnp.bfloat16)
    dv_low = key_sums[..., kv_width:].reshape(total_rows, kv_width).astype(jnp.bfloat16)
    left = first_in
    outer = dresid_low
    attn_sums = lax.psum_scatter(
        jnp.concatenate(
            [
                jnp.einsum("nd,nh->dh", left, dq_low, preferred_element_type=jnp.float32),
                jnp.einsum("nd,nh->dh", left, dk_low, preferred_element_type=jnp.float32),
                jnp.einsum("nd,nh->dh", left, dv_low, preferred_element_type=jnp.float32),
                jnp.einsum("nd,nh->dh", outer, out_low, preferred_element_type=jnp.float32),
            ],
            1,
        ),
        ("seq", "dp"),
        scatter_dimension=0,
        tiled=True,
    )
    dfirst = jnp.einsum("nh,dh->nd", dq_low, wq_all, preferred_element_type=jnp.float32)
    dfirst = dfirst + jnp.einsum("nh,dh->nd", dk_low, wk_all, preferred_element_type=jnp.float32)
    dfirst = dfirst + jnp.einsum("nh,dh->nd", dv_low, wv_all, preferred_element_type=jnp.float32)
    dx_norm, dga = norm_back(x_rows, first_inv, ga_all, dfirst)
    tokens_grad = (dresid + dx_norm).reshape(seqs, local, width)
    dga_all, dgm_all, dgq_all, dgk_all = lax.psum((dga, dgm, dgq, dgk), ("seq", "dp"))
    offset = lax.axis_index(("seq", "dp")) * own_rows
    attn_gain_grad = lax.dynamic_slice_in_dim(dga_all, offset, own_rows, 0)
    mlp_gain_grad = lax.dynamic_slice_in_dim(dgm_all, offset, own_rows, 0)
    q_cols = heads * head_size
    w_query_grad = attn_sums[:, :q_cols]
    w_key_grad = attn_sums[:, q_cols : q_cols + kv_width]
    w_value_grad = attn_sums[:, q_cols + kv_width : q_cols + 2 * kv_width]
    w_output_grad = attn_sums[:, q_cols + 2 * kv_width :]
    w_gate_grad = mlp_sums[:, :ff_width]
    w_up_grad = mlp_sums[:, ff_width : 2 * ff_width]
    w_down_grad = mlp_sums[:, 2 * ff_width :]
    return (
        block_out,
        tokens_grad,
        w_query_grad,
        w_key_grad,
        w_value_grad,
        w_output_grad,
        attn_gain_grad,
        dgq_all,
        dgk_all,
        w_gate_grad,
        w_up_grad,
        w_down_grad,
        mlp_gain_grad,
    )


LOW = jnp.bfloat16
MESH = pl.DeviceIdType.MESH
LIMIT = 60 * 2**20


def ring_order(ranks):
    half = ranks // 2
    order = [0]
    for step in range(1, half):
        order += [step, ranks - step]
    return order + [half]


def ring_place(seq, ranks):
    z, x = lax.div(seq, 2), lax.rem(seq, 2)
    return z + x * (ranks - 1 - 2 * z)


def ring_seq(place, ranks):
    half = ranks // 2
    x, z = lax.div(place, half), lax.rem(place, half)
    return 2 * (z + x * (half - 1 - 2 * z)) + x


def neighbours(ranks):
    seq, dp = lax.axis_index("seq"), lax.axis_index("dp")
    at = ring_place(seq, ranks)
    right = ring_seq(lax.rem(at + 1, ranks), ranks)
    left = ring_seq(lax.rem(at + ranks - 1, ranks), ranks)
    return (right, dp), (left, dp)


def knock(devices):
    barrier = pltpu.get_barrier_semaphore()
    for device in devices:
        pl.semaphore_signal(barrier, inc=1, device_id=device, device_id_type=MESH)


def answered(devices):
    pl.semaphore_wait(pltpu.get_barrier_semaphore(), len(devices))


def move(src, dst, sem):
    copy = pltpu.make_async_copy(src, dst, sem)
    copy.start()
    return copy


def push(src, dst, send, recv, device):
    return pltpu.make_async_remote_copy(
        src_ref=src, dst_ref=dst, send_sem=send, recv_sem=recv, device_id=device, device_id_type=MESH
    )


def dot_nn(left, right):
    return jnp.dot(left, right, preferred_element_type=jnp.float32)


def dot_nt(left, right):
    return lax.dot_general(left, right, (((1,), (1,)), ((), ())), preferred_element_type=jnp.float32)


def dot_tn(left, right):
    return lax.dot_general(left, right, (((0,), (0,)), ((), ())), preferred_element_type=jnp.float32)


def block_row(rel, local, ranks):
    place = ring_place(lax.axis_index("seq"), ranks)
    return pl.multiple_of(ring_seq(lax.rem(place + rel, ranks), ranks) * local, local)


def block_rows(ref, rels, local, ranks):
    blocks = [ref[pl.ds(block_row(rel, local, ranks), local)] for rel in rels]
    return blocks[0] if len(blocks) == 1 else jnp.concatenate(blocks, 0)


def rels_of(step, ranks):
    return [rel for rel in ring_order(ranks) if min(rel, ranks - rel) == step]


class RingGather:
    def __init__(self, buf, local, ranks, send, recv, right, left, row):
        self.buf, self.sub, self.half = buf, local // 2, ranks // 2
        self.send, self.recv, self.right, self.left = send, recv, right, left
        self.ranks, self.row = ranks, row

    def copies(self, step, part):
        ways = ((0, (self.ranks - step + 1) % self.ranks, self.right), (1, step - 1, self.left))
        given = []
        for way, rel, device in ways:
            if step < self.half or way == part:
                block = self.buf.at[pl.ds(self.row(rel) + part * self.sub, self.sub)]
                at = 2 * (step - 1) + part
                given.append(push(block, block, self.send.at[way, at], self.recv.at[way, at], device))
        return given

    def start(self, step):
        for part in range(2):
            for copy in self.copies(step, part):
                copy.start()

    def advance(self, step):
        for part in range(2):
            for copy in self.copies(step, part):
                copy.wait_recv()
            if step < self.half:
                for copy in self.copies(step + 1, part):
                    copy.start()

    def finish(self):
        for step in range(1, self.half + 1):
            for part in range(2):
                for copy in self.copies(step, part):
                    copy.wait_send()


class LineGather:
    def __init__(self, buf, local, ranks, send, recv, x_send, x_recv):
        self.buf, self.local, self.length = buf, local, ranks // 2
        self.send, self.recv, self.x_send, self.x_recv = send, recv, x_send, x_recv
        self.seq, self.dp = lax.axis_index("seq"), lax.axis_index("dp")
        self.z, self.x = lax.div(self.seq, 2), lax.rem(self.seq, 2)

    def block(self, z):
        return self.buf.at[pl.ds(pl.multiple_of((2 * z + self.x) * self.local, self.local), self.local)]

    def hop(self, way, step):
        block = self.block(self.z + (step - 1 if way else 1 - step))
        to = self.seq + (-2 if way else 2)
        return push(block, block, self.send.at[way, step - 1], self.recv.at[way, step - 1], (to, self.dp))

    def sends(self, way, step):
        if way:
            return (self.z > 0) & (self.z + step <= self.length)
        return (self.z < self.length - 1) & (self.z >= step - 1)

    def comes(self, way, step):
        return self.z + step < self.length if way else self.z >= step

    def across(self, way, step):
        block = self.block(self.z + (step if way else -step))
        at = step + way * (self.length - 1)
        return push(
            block, block, self.x_send.at[at], self.x_recv.at[at], (self.seq + 1 - 2 * self.x, self.dp)
        )

    def from_x(self, way, step):
        z = self.z + (step if way else -step)
        row = pl.multiple_of((2 * z + 1 - self.x) * self.local, self.local)
        block = self.buf.at[pl.ds(row, self.local)]
        at = step + way * (self.length - 1)
        return push(
            block, block, self.x_send.at[at], self.x_recv.at[at], (self.seq + 1 - 2 * self.x, self.dp)
        )

    def start(self, step):
        for way in range(2):
            pl.when(self.sends(way, step))(lambda way=way: self.hop(way, step).start())
        self.pass_on(step - 1)

    def pass_on(self, step):
        if step == 0:
            self.across(0, 0).start()
            return
        for way in range(2):
            pl.when(self.comes(way, step))(lambda way=way: self.across(way, step).start())

    def arrive(self, step):
        for way in range(2):
            pl.when(self.comes(way, step))(lambda way=way: self.incoming(way, step).wait_recv())

    def incoming(self, way, step):
        block = self.block(self.z + (step if way else -step))
        to = self.seq + 1 - 2 * self.x
        return push(block, block, self.send.at[way, step - 1], self.recv.at[way, step - 1], (to, self.dp))

    def run(self):
        for step in range(1, self.length):
            self.advance(step)

    def advance(self, step):
        self.arrive(step)
        if step < self.length - 1:
            self.start(step + 1)
        else:
            self.pass_on(step)

    def complete(self):
        self.from_x(0, 0).wait_recv()
        for step in range(1, self.length):
            for way in range(2):
                pl.when(self.comes(way, step))(lambda way=way: self.from_x(way, step).wait_recv())

    def finish(self):
        self.across(0, 0).wait_send()
        for step in range(1, self.length):
            for way in range(2):
                pl.when(self.sends(way, step))(lambda way=way: self.hop(way, step).wait_send())
                pl.when(self.comes(way, step))(lambda way=way: self.across(way, step).wait_send())


def line_sems(ranks):
    half = ranks // 2
    return [pltpu.SemaphoreType.DMA((2, half))] * 2 + [pltpu.SemaphoreType.DMA((2 * half,))] * 2


class RingSum:
    def __init__(self, part, term, out_buf, in_buf, local, ranks, send, recv, right, left, stream=0, streams=1):
        self.part, self.term, self.out_buf, self.in_buf = part, term, out_buf, in_buf
        self.local, self.ranks, self.half = local, ranks, ranks // 2
        each = term.shape[1] // streams
        self.cols = pl.ds(stream * each, each)
        self.tiles = (stream * ranks // streams, (stream + 1) * ranks // streams)
        self.send, self.recv, self.right, self.left = send, recv, right, left

    def copies(self, step):
        rows = self.local // 2 if step == 1 else self.local
        skip = self.local // 2 if step == 1 else 0
        return [
            push(
                self.out_buf.at[way, (step - 1) % 2, pl.ds(begin, rows), self.cols],
                self.in_buf.at[way, step - 1, pl.ds(begin, rows), self.cols],
                self.send.at[way, step - 1],
                self.recv.at[way, step - 1],
                device,
            )
            for way, begin, device in ((0, 0, self.right), (1, skip, self.left))
        ]

    def compute(self, step):
        if step == 1:
            self.part([self.half], *self.tiles)
        elif step <= self.half:
            self.part(rels_of(self.half + 1 - step, self.ranks), *self.tiles)
        else:
            self.part([0], *self.tiles)

    def launch(self, step):
        local, skip = self.local, self.local // 2
        if step > 2:
            for copy in self.copies(step - 2):
                copy.wait_send()
        if step == 1:
            for way in range(2):
                rows = pl.ds(way * skip, skip)
                self.out_buf[way, 0, rows, self.cols] = self.term[rows, self.cols].astype(LOW)
        else:
            for copy in self.copies(step - 1):
                copy.wait_recv()
            for way in range(2):
                for begin, with_sum in ((0, step > 2 or way == 0), (skip, step > 2 or way == 1)):
                    value = self.term[pl.ds(way * local + begin, skip), self.cols]
                    if with_sum:
                        value = value + self.in_buf[way, step - 2, pl.ds(begin, skip), self.cols].astype(jnp.float32)
                    self.out_buf[way, (step - 1) % 2, pl.ds(begin, skip), self.cols] = value.astype(LOW)
        for copy in self.copies(step):
            copy.start()

    def last(self, begin, count):
        rows = pl.ds(begin, count)
        value = self.term[rows, self.cols] + self.in_buf[0, self.half - 1, rows, self.cols].astype(jnp.float32)
        return value + self.in_buf[1, self.half - 1, rows, self.cols].astype(jnp.float32)

    def arrive_last(self):
        for copy in self.copies(self.half):
            copy.wait_recv()

    def finish(self):
        for step in range(max(1, self.half - 1), self.half + 1):
            for copy in self.copies(step):
                copy.wait_send()


def two_sums(part, term, out_buf, in_buf, local, ranks, sems, right, left):
    return [
        RingSum(
            part, term, out_buf, in_buf, local, ranks, sems[2 * at], sems[2 * at + 1], right, left, at, 2
        )
        for at in range(2)
    ]


def ring_sems(ranks):
    return [pltpu.SemaphoreType.DMA((2, ranks)), pltpu.SemaphoreType.DMA((2, ranks))]


def sum_bufs(local, ranks, width):
    return [
        pltpu.VMEM((2 * local, width), jnp.float32),
        pltpu.VMEM((2, 2, local, width), LOW),
        pltpu.VMEM((2, ranks // 2, local, width), LOW),
    ]


def turn(v):
    return pltpu.roll(v, v.shape[-1] // 2, v.ndim - 1)


def rows_scaled(v):
    inv = lax.rsqrt(jnp.mean(v * v, -1, keepdims=True) + EPS)
    return v * inv, inv


def rows_scaled_back(v, inv, grad):
    return inv * grad - v * (inv * inv * inv * jnp.mean(grad * v, -1, keepdims=True))


class Spread:
    def __init__(self, rows, block, ranks, own, cols, sems):
        self.rows, self.block, self.ranks, self.own, self.cols = rows, block, ranks, own, cols
        self.send, self.recv, self.hop_send, self.hop_recv, self.here = sems
        self.seq, self.dp = lax.axis_index("seq"), lax.axis_index("dp")
        y, core = lax.div(self.dp, 2), lax.rem(self.dp, 2)
        self.beside, self.sibling = (1 - y) * 2 + core, y * 2 + 1 - core

    def at(self, dp):
        return pl.ds(pl.multiple_of(dp * self.own, self.own), self.own)

    def exchange(self):
        for step in range(1, self.ranks):
            peer = lax.rem(self.seq + step, self.ranks)
            yield push(
                self.rows.at[peer, :, self.cols],
                self.block.at[self.seq, self.at(self.dp), self.cols],
                self.send.at[step],
                self.recv.at[step],
                (peer, self.dp),
            )

    def keep(self):
        return pltpu.make_async_copy(
            self.rows.at[self.seq, :, self.cols],
            self.block.at[self.seq, self.at(self.dp), self.cols],
            self.here,
        )

    def hop(self, number):
        dp = self.beside if number == 2 else self.dp
        part = self.block.at[:, self.at(dp), self.cols]
        to = self.beside if number == 0 else self.sibling
        return push(part, part, self.hop_send.at[number], self.hop_recv.at[number], (self.seq, to))

    def start(self):
        self.keep().start()
        for copy in self.exchange():
            copy.start()

    def arrive(self):
        self.keep().wait()
        for copy in self.exchange():
            copy.wait_recv()

    def finish(self):
        for copy in self.exchange():
            copy.wait_send()
        for number in range(3):
            self.hop(number).wait_send()


def spread_sems(ranks):
    return [
        pltpu.SemaphoreType.DMA((ranks,)),
        pltpu.SemaphoreType.DMA((ranks,)),
        pltpu.SemaphoreType.DMA((3,)),
        pltpu.SemaphoreType.DMA((3,)),
        pltpu.SemaphoreType.DMA,
    ]


class WholeGather:
    def __init__(self, block, ranks, own, sems):
        self.block, self.ranks, self.half, self.own = block, ranks, ranks // 2, own
        self.send, self.recv, self.y_send, self.y_recv, self.core_send, self.core_recv = sems
        self.seq, self.dp = lax.axis_index("seq"), lax.axis_index("dp")
        self.right, self.left = neighbours(ranks)
        self.place = ring_place(self.seq, ranks)
        y, core = lax.div(self.dp, 2), lax.rem(self.dp, 2)
        self.beside, self.sibling = (1 - y) * 2 + core, y * 2 + 1 - core

    def at(self, rel, dp, begin, count):
        seq = ring_seq(lax.rem(self.place + rel + self.ranks, self.ranks), self.ranks)
        return self.block.at[seq, pl.ds(pl.multiple_of(dp * self.own + begin, count), count)]

    def copies(self, step):
        last = step == self.half
        rows = self.own // 2 if last else self.own
        skip = self.own // 2 if last else 0
        given = []
        for way, rel, begin, device in ((0, 1 - step, 0, self.right), (1, step - 1, skip, self.left)):
            part = self.at(rel, self.dp, begin, rows)
            given.append(push(part, part, self.send.at[way, step - 1], self.recv.at[way, step - 1], device))
        return given

    def start(self, step):
        for copy in self.copies(step):
            copy.start()

    def hops(self, step):
        for at, rel in enumerate(ring_order(self.ranks)):
            if min(rel, self.ranks - rel) == step:
                part = self.at(rel, self.dp, 0, self.own)
                yield push(part, part, self.y_send.at[at], self.y_recv.at[at], (self.seq, self.beside))
                yield push(part, part, self.core_send.at[at], self.core_recv.at[at], (self.seq, self.sibling))

    def arrive(self, step):
        for copy in self.copies(step):
            copy.wait_recv()

    def forward(self, step):
        for copy in self.hops(step):
            copy.start()

    def cross(self):
        part = self.block.at[:, pl.ds(pl.multiple_of(self.beside * self.own, self.own), self.own)]
        at = self.ranks
        return push(part, part, self.core_send.at[at], self.core_recv.at[at], (self.seq, self.sibling))

    def complete(self):
        for step in range(self.half + 1):
            for copy in self.hops(step):
                copy.wait_recv()
        self.cross().start()
        self.cross().wait_recv()

    def finish(self):
        for step in range(1, self.half + 1):
            for copy in self.copies(step):
                copy.wait_send()
        for step in range(self.half + 1):
            for copy in self.hops(step):
                copy.wait_send()
        self.cross().wait_send()


def whole_sems(ranks):
    return (
        ring_sems(ranks)
        + [pltpu.SemaphoreType.DMA((ranks,))] * 2
        + [pltpu.SemaphoreType.DMA((ranks + 1,))] * 2
    )


class Reduce:
    def __init__(self, grads, from_core, from_y, total, own, first, count, cols, sems):
        self.grads, self.from_core, self.from_y, self.total = grads, from_core, from_y, total
        self.own, self.begin, self.count, self.cols = own, first, count, cols
        self.send, self.recv = sems
        self.seq, dp = lax.axis_index("seq"), lax.axis_index("dp")
        self.y, self.core = lax.div(dp, 2), lax.rem(dp, 2)
        self.beside, self.sibling = (1 - self.y) * 2 + self.core, self.y * 2 + 1 - self.core

    def at(self, y, core):
        return pl.ds(pl.multiple_of((y * 2 + core) * self.own, self.own), self.own)

    def hop(self, number):
        some, cols = pl.ds(self.begin, self.count), self.cols
        if number == 2:
            src, dst, to = self.from_core.at[0, some, :, cols], self.from_y.at[some, :, cols], self.beside
        else:
            rows = self.at(1 - self.y if number == 0 else self.y, 1 - self.core)
            src, dst, to = self.grads.at[some, rows, cols], self.from_core.at[number, some, :, cols], self.sibling
        return push(src, dst, self.send.at[number], self.recv.at[number], (self.seq, to))

    def first(self):
        self.hop(0).start()
        self.hop(1).start()

    def second(self):
        self.hop(0).wait_recv()
        rows = self.at(1 - self.y, self.core)

        def some(at, _):
            value = self.grads[at, rows, self.cols].astype(jnp.float32)
            value = value + self.from_core[0, at, :, self.cols].astype(jnp.float32)
            self.from_core[0, at, :, self.cols] = value.astype(LOW)
            return 0

        lax.fori_loop(self.begin, self.begin + self.count, some, 0)
        self.hop(2).start()

    def third(self):
        self.hop(1).wait_recv()
        self.hop(2).wait_recv()
        rows = self.at(self.y, self.core)

        def some(at, _):
            value = self.grads[at, rows, self.cols].astype(jnp.float32)
            value = value + self.from_core[1, at, :, self.cols].astype(jnp.float32)
            value = value + self.from_y[at, :, self.cols].astype(jnp.float32)
            self.total[at, :, self.cols] = value.astype(LOW)
            return 0

        lax.fori_loop(self.begin, self.begin + self.count, some, 0)

    def finish(self):
        for number in range(3):
            self.hop(number).wait_send()


def reduce_sems():
    return [pltpu.SemaphoreType.DMA((3,)), pltpu.SemaphoreType.DMA((3,))]


def reduce_bufs(ranks, own, cols):
    return [pltpu.VMEM((2, ranks, own, cols), LOW), pltpu.VMEM((ranks, own, cols), LOW)]


class Deliver:
    def __init__(self, rows, out, cols, ranks, sems):
        self.rows, self.out, self.cols, self.ranks = rows, out, cols, ranks
        self.send, self.recv, self.here = sems
        self.seq, self.dp = lax.axis_index("seq"), lax.axis_index("dp")

    def exchange(self):
        for step in range(1, self.ranks):
            peer = lax.rem(self.seq + step, self.ranks)
            yield push(
                self.rows.at[peer, :, self.cols],
                self.out.at[self.seq, :, self.cols],
                self.send.at[step],
                self.recv.at[step],
                (peer, self.dp),
            )

    def keep(self):
        return pltpu.make_async_copy(
            self.rows.at[self.seq, :, self.cols], self.out.at[self.seq, :, self.cols], self.here
        )

    def start(self):
        self.keep().start()
        for copy in self.exchange():
            copy.start()

    def finish(self):
        self.keep().wait()
        for copy in self.exchange():
            copy.wait_recv()
        for copy in self.exchange():
            copy.wait_send()


def deliver_sems(ranks):
    return [pltpu.SemaphoreType.DMA((ranks,)), pltpu.SemaphoreType.DMA((ranks,)), pltpu.SemaphoreType.DMA]


def first_kernel(
    ranks, kv_heads, order, starts, tokens, out_grad, freqs, attn_gain, mlp_gain, query_gain, key_gain,
    w_query, w_key, w_value, w_output, w_gate, w_up, w_down,
    resid, second, cosv, sinv, q_low, k_low, v_low, own_out, first_in, qkv, attn_block, dy_all, prob, mlp_block, out_all,
    held, normal, kept, block, a_rows, m_rows, gate, up, down, dys, probs, pos, begins, pos_row,
    out_low, whole, *sems,
):
    local, width = tokens.shape
    rows = local * ranks
    own = w_query.shape[0]
    size = freqs.shape[1]
    heads = q_low.shape[0]
    share = heads // kv_heads
    half = ranks // 2
    scale = 1.0 / math.sqrt(size)
    cols = (heads + 2 * kv_heads) * size
    deep = block.shape[1]
    row = functools.partial(block_row, local=local, ranks=ranks)
    seq, dp = lax.axis_index("seq"), lax.axis_index("dp")
    right, left = neighbours(ranks)
    attn = Spread(a_rows, block, ranks, own, pl.ds(0, a_rows.shape[2]), sems[12:17])
    third = m_rows.shape[2] // 3
    mlp = [
        Spread(m_rows, mlp_block, ranks, own, pl.ds(at * third, third), sems[17 + 5 * at : 22 + 5 * at])
        for at in range(3)
    ]
    local_sems = sems[32]
    out_send, out_recv = sems[2:4]
    o_cols = heads * size
    peers = [(lax.rem(seq + step, ranks), dp) for step in range(1, ranks)]
    peers += [(seq, attn.beside), (seq, attn.sibling)]
    knock(peers)
    loads = [
        move(src, dst, local_sems.at[at])
        for at, (src, dst) in enumerate(((w_gate, gate), (w_up, up), (w_down, down)))
    ]
    held[pl.ds(row(0), local)] = tokens[...]
    dys[pl.ds(row(0), local)] = out_grad[...]

    def column(line):
        same = lax.broadcasted_iota(jnp.int32, (own, own), 0) == lax.broadcasted_iota(jnp.int32, (own, own), 1)
        return jnp.sum(jnp.where(same, line, 0.0), 1, keepdims=True)

    def lay(target, begin, weight, gain):
        each = weight.shape[1] // ranks
        for rank in range(ranks):
            part = weight[:, rank * each : (rank + 1) * each]
            if gain is not None:
                part = (part.astype(jnp.float32) * gain).astype(LOW)
            target[rank, :, begin : begin + each] = part
        return begin + each

    gain = column(attn_gain[...])
    at = 0
    for weight in (w_query, w_key, w_value):
        at = lay(a_rows, at, weight, gain)
    whole[seq, pl.ds(pl.multiple_of(dp * own, own), own)] = w_output[...]
    answered(peers)
    ring = RingGather(held, local, ranks, sems[0], sems[1], right, left, row)
    ring.start(1)
    attn.start()
    outs = WholeGather(whole, ranks, own, [*sems[8:12], *sems[33:35]])
    outs.forward(0)
    line = LineGather(dys, local, ranks, sems[4], sems[5], sems[6], sems[7])
    stores = []

    def store(src, dst):
        stores.append(move(src, dst, local_sems.at[len(loads) + len(stores)]))

    def scale_rows(step):
        for rel in rels_of(step, ranks):

            def some(at, _):
                rows_at = pl.ds(pl.multiple_of(row(rel) + at * 32, 32), 32)
                normal[rows_at] = rows_scaled(held[rows_at].astype(jnp.float32))[0].astype(LOW)
                return 0

            lax.fori_loop(0, local // 32, some, 0)

    for load in loads:
        load.wait()
    gain = column(mlp_gain[...])
    each = gate.shape[1] // ranks
    lay(m_rows, 0, gate, gain)
    lay(m_rows, each, up, gain)
    lay(m_rows, 2 * each, down, None)
    scale_rows(0)
    def bring(step):
        outs.arrive(step)
        if step < half:
            outs.start(step + 1)
        outs.forward(step)

    def forward(piece):
        mlp[piece].arrive()
        mlp[piece].hop(0).start()
        mlp[piece].hop(1).start()

    def hop_over(piece):
        mlp[piece].hop(0).wait_recv()
        mlp[piece].hop(2).start()

    def pass_on(step):
        ring.advance(step)
        scale_rows(step)

    pass_on(1)
    line.start(1)
    pass_on(2)
    outs.start(1)
    attn.arrive()
    attn.hop(0).start()
    attn.hop(1).start()
    attn.hop(0).wait_recv()
    attn.hop(2).start()
    for step in range(3, half):
        pass_on(step)
    bring(1)
    pass_on(half)
    mlp[0].start()
    spans = order.shape[0]
    span = rows // spans
    for at in range(ranks):
        rows_at = pl.ds(at * local, local)
        ids = at * local + lax.broadcasted_iota(jnp.int32, (1, local), 1)
        where = jnp.zeros_like(ids)
        for slot in range(spans):
            inside = (ids >= slot * span) & (ids < (slot + 1) * span)
            where = where + jnp.where(inside, ids + (order[slot] - slot) * span, 0)
        begin = jnp.zeros_like(ids)
        for doc in range(starts.shape[1]):
            begin = jnp.maximum(begin, jnp.where(starts[0, doc] <= where, starts[0, doc], 0))
        pos_row[:, rows_at] = where
        across = jnp.broadcast_to(where, (local, local)).T
        pos[rows_at] = across[:, :1]
        begins[rows_at] = jnp.broadcast_to(begin, (local, local)).T[:, :1]
        angle = across[:, :1].astype(jnp.float32) * freqs[...]
        lane = lax.broadcasted_iota(jnp.int32, (local, size), 1)
        cosv[rows_at] = jnp.cos(angle)
        sine = jnp.sin(angle)
        sinv[rows_at] = jnp.where(lane < size // 2, -sine, sine)
    bring(2)
    line.advance(1)
    attn.hop(1).wait_recv()
    attn.hop(2).wait_recv()
    store(block, attn_block)

    def project(begin, count):
        rows_at = pl.ds(begin, count)
        kept[rows_at] = dot_nn(normal[rows_at], block[...].reshape(width, cols))

    store(normal, first_in)
    tile = rows // half

    def rotated(at, rows_at, gain):
        v = rows_scaled(kept[rows_at, at * size : (at + 1) * size])[0] * gain[...]
        return (v * cosv[rows_at] + turn(v) * sinv[rows_at]).astype(LOW)

    for piece in range(half):
        rows_at = pl.ds(piece * tile, tile)
        project(piece * tile, tile)
        for head in range(heads):
            q_low[head, rows_at] = rotated(head, rows_at, query_gain)
        for group in range(kv_heads):
            k_low[group, rows_at] = rotated(heads + group, rows_at, key_gain)
            at = (heads + kv_heads + group) * size
            v_low[group, rows_at] = kept[rows_at, at : at + size].astype(LOW)
    store(kept, qkv)
    forward(0)

    for piece in range(half):
        rows_at = pl.ds(piece * tile, tile)
        seen = (pos_row[...] <= pos[rows_at]) & (pos_row[...] >= begins[rows_at])
        for head in range(heads):
            raw = dot_nt(q_low[head, rows_at], k_low[head // share]) * scale
            raw = jnp.where(seen, raw, NEG)
            weight = jnp.exp(raw - jnp.max(raw, -1, keepdims=True))
            weight = (weight * (1.0 / jnp.sum(weight, -1, keepdims=True))).astype(LOW)
            probs[head, rows_at] = weight
            value = dot_nn(weight, v_low[head // share])
            out_low[rows_at, head * size : (head + 1) * size] = value.astype(LOW)
            store(probs.at[head, rows_at], prob.at[head, rows_at])
        if piece == 0:
            bring(3)
        if piece == 1:
            mlp[1].start()
            line.advance(2)
            bring(half)
    mlp[2].start()
    hop_over(0)
    forward(1)
    forward(2)
    place = ring_place(seq, ranks)

    def exchange(rel):
        to = ring_seq(lax.rem(place + rel, ranks), ranks)
        return push(
            out_low.at[pl.ds(row(rel), local)],
            own_out.at[:, pl.ds(pl.multiple_of(seq * o_cols, o_cols), o_cols)],
            out_send.at[rel],
            out_recv.at[rel],
            (to, dp),
        )

    for rel in range(1, ranks):
        exchange(rel).start()
    own_out[:, pl.ds(pl.multiple_of(seq * o_cols, o_cols), o_cols)] = out_low[pl.ds(row(0), local)]
    outs.complete()
    store(whole, out_all)
    hop_over(1)
    for step in range(3, half):
        line.advance(step)
    for rel in range(1, ranks):
        exchange(rel).wait_recv()

    def join(at, _):
        some = pl.ds(pl.multiple_of(at * deep, deep), deep)
        resid[:, some] = tokens[:, some].astype(jnp.float32) + dot_nt(own_out[...], whole[at])
        return 0

    lax.fori_loop(0, ranks, join, 0)

    def scale_second(at, _):
        rows_at = pl.ds(pl.multiple_of(at * 32, 32), 32)
        second[rows_at] = rows_scaled(resid[rows_at])[0].astype(LOW)
        return 0

    lax.fori_loop(0, local // 32, scale_second, 0)
    hop_over(2)
    line.complete()
    store(dys, dy_all)
    ring.finish()
    attn.finish()
    outs.finish()
    for rel in range(1, ranks):
        exchange(rel).wait_send()
    line.finish()
    for piece in mlp:
        piece.hop(1).wait_recv()
        piece.hop(2).wait_recv()
        piece.finish()
    for given in stores:
        given.wait()


def mlp_kernel(
    ranks, second, out_grad, rest, dys, mlp_block, block_out, dresid, dresid_low, own_grads,
    grads, from_core, from_y, held, weights, hidden, dgu, resid, dy_all,
    term, out_buf, in_buf, y_out, y_in, here, *sems,
):
    local, width = second.shape
    row = functools.partial(block_row, local=local, ranks=ranks)
    ff = hidden.shape[1]
    deep = weights.shape[1]
    half = ranks // 2
    right, left = neighbours(ranks)
    loads = [
        move(src, dst, here.at[at])
        for at, (src, dst) in enumerate(((mlp_block, weights), (dys, dy_all), (rest, resid)))
    ]
    seq, dp = lax.axis_index("seq"), lax.axis_index("dp")
    own = own_grads.shape[1]
    pieces = [
        Reduce(
            grads, from_core, from_y, own_grads, own, at * ranks // 4, ranks // 4, pl.ds(0, 3 * ff),
            sems[6 + 2 * at : 8 + 2 * at],
        )
        for at in range(4)
    ]
    peers = [right, left, (seq, pieces[0].beside), (seq, pieces[0].sibling)]
    knock(peers)
    held[pl.ds(row(0), local)] = second[...]
    answered(peers)
    ring = RingGather(held, local, ranks, sems[0], sems[1], right, left, row)
    ring.start(1)
    loads[0].wait()
    loads[1].wait()
    wide = 256

    def middle(step):
        rels = rels_of(step, ranks)

        def some(at, _):
            first = pl.multiple_of(at * wide, wide)
            given, dy = block_rows(held, rels, local, ranks), block_rows(dy_all, rels, local, ranks)
            gate = dot_nn(given, weights[:, :, pl.ds(first, wide)].reshape(width, wide))
            upper = dot_nn(given, weights[:, :, pl.ds(ff + first, wide)].reshape(width, wide))
            dmid = dot_nn(dy, weights[:, :, pl.ds(2 * ff + first, wide)].reshape(width, wide))
            sigma = 1.0 / (1.0 + jnp.exp(-gate))
            act = gate * sigma
            value = (act * upper).astype(LOW)
            dgate = (dmid * upper * (sigma * (1.0 + gate * (1.0 - sigma)))).astype(LOW)
            dupper = (dmid * act).astype(LOW)
            for at, rel in enumerate(rels):
                rows, some_rows = pl.ds(row(rel), local), slice(at * local, (at + 1) * local)
                hidden[rows, pl.ds(first, wide)] = value[some_rows]
                dgu[rows, pl.ds(first, wide)] = dgate[some_rows]
                dgu[rows, pl.ds(ff + first, wide)] = dupper[some_rows]
            return 0

        lax.fori_loop(0, ff // wide, some, 0)

    middle(0)
    for step in range(1, half + 1):
        ring.advance(step)
        middle(step)

    def back_part(rels, begin, end):
        def some(at, _):
            value = dot_nt(block_rows(dgu, rels, local, ranks), weights[at, :, : 2 * ff])
            term[: len(rels) * local, pl.ds(pl.multiple_of(at * deep, deep), deep)] = value
            return 0

        lax.fori_loop(begin, end, some, 0)

    def out_part(rels, begin, end):
        def some(at, _):
            value = dot_nt(block_rows(hidden, rels, local, ranks), weights[at, :, 2 * ff :])
            term[: len(rels) * local, pl.ds(pl.multiple_of(at * deep, deep), deep)] = value
            return 0

        lax.fori_loop(begin, end, some, 0)

    def weight_grads(first, count):
        def some(at, _):
            cols = pl.ds(pl.multiple_of(at * deep, deep), deep)
            grads[at, :, : 2 * ff] = dot_tn(held[:, cols], dgu[...]).astype(LOW)
            grads[at, :, 2 * ff :] = dot_tn(dy_all[:, cols], hidden[...]).astype(LOW)
            return 0

        lax.fori_loop(first, first + count, some, 0)

    back = RingSum(back_part, term, out_buf, in_buf, local, ranks, sems[2], sems[3], right, left)
    out = RingSum(out_part, term, y_out, y_in, local, ranks, sems[4], sems[5], right, left)
    for step in range(1, half + 1):
        back.compute(step)
        back.launch(step)
        out.compute(step)
        out.launch(step)
        made, passed, summed = (((), (0, 1), (2, 3), ()), ((), (), (0, 1), (2, 3)), ((), (), (), (0, 1)))
        for piece in (pieces[at] for at in made[step - 1]):
            weight_grads(piece.begin, piece.count)
            piece.first()
        for at in passed[step - 1]:
            pieces[at].second()
        for at in summed[step - 1]:
            pieces[at].third()
    back.compute(half + 1)
    loads[2].wait()
    back.arrive_last()

    def finish_back(at, _):
        begin = pl.multiple_of(at * 32, 32)
        rows = pl.ds(begin, 32)
        value = resid[rows]
        inv = rows_scaled(value)[1]
        grad = back.last(begin, 32)
        full = out_grad[rows].astype(jnp.float32) + rows_scaled_back(value, inv, grad)
        dresid[rows] = full
        dresid_low[rows] = full.astype(LOW)
        return 0

    lax.fori_loop(0, local // 32, finish_back, 0)
    out.compute(half + 1)
    out.arrive_last()

    def finish_out(at, _):
        begin = pl.multiple_of(at * 32, 32)
        rows = pl.ds(begin, 32)
        block_out[rows] = (resid[rows] + out.last(begin, 32)).astype(LOW)
        return 0

    lax.fori_loop(0, local // 32, finish_out, 0)
    ring.finish()
    for piece in pieces[2:]:
        piece.third()
    back.finish()
    out.finish()
    for piece in pieces:
        piece.finish()


def back_kernel(
    ranks, kv_heads, tokens, dresid_low, query_gain, key_gain, own_out, first_in_in, block_in,
    qkv_in, cos_in, sin_in, q_in, k_in, v_in, prob_in, dresid_in, mlp_own, out_all,
    tokens_grad, gains, out_grad, mlp_sums, attn_sums,
    grads, from_core, from_y, own_grads, query_gain_grad, key_gain_grad,
    tile, tiles_in, tile_sum, tile_sums_in, dob, dout, dk, dv, dqkv,
    first_in, attn_block, qkv, cosv, sinv, q_low, k_low, v_low, prob, dresid, term, out_buf, in_buf,
    o_grads, o_core, o_y, o_own, o_term, o_out, o_in, *sems,
):
    local, width = tokens.shape
    rows = local * ranks
    half = ranks // 2
    size = cosv.shape[1]
    heads = q_low.shape[0]
    share = heads // kv_heads
    scale = 1.0 / math.sqrt(size)
    cols = (heads + 2 * kv_heads) * size
    deep = attn_block.shape[1]
    o_cols = heads * size
    right, left = neighbours(ranks)
    seq, dp = lax.axis_index("seq"), lax.axis_index("dp")
    own = mlp_own.shape[1]
    copies = lax.axis_size("dp")
    row = functools.partial(block_row, local=local, ranks=ranks)
    place = ring_place(seq, ranks)
    out_piece = Reduce(o_grads, o_core, o_y, o_own, own, 0, ranks, pl.ds(0, width), sems[4:6])
    qkv_piece = Reduce(grads, from_core, from_y, own_grads, own, 0, ranks, pl.ds(0, cols), sems[6:8])
    third = mlp_own.shape[2] // 3
    mlp_ways = [
        Deliver(mlp_own, mlp_sums, pl.ds(at * third, third), ranks, [*sems[8:11], *sems[22:28]][3 * at : 3 * at + 3])
        for at in range(3)
    ]
    dob_send, dob_recv = sems[0:2]
    qkv_way = Deliver(own_grads, attn_sums, pl.ds(0, cols), ranks, sems[14:17])
    peers = [(lax.rem(seq + step, ranks), dp) for step in range(1, ranks)]
    peers += [(seq, lax.rem(dp + step, copies)) for step in range(1, copies)]
    knock(peers)
    local_sems = sems[21]
    loads = {}
    for at, (name, src, dst) in enumerate(
        (
            ("out", out_all, o_grads), ("block", block_in, attn_block), ("v", v_in, v_low),
            ("prob", prob_in, prob), ("k", k_in, k_low), ("q", q_in, q_low), ("cos", cos_in, cosv),
            ("sin", sin_in, sinv), ("qkv", qkv_in, qkv), ("first", first_in_in, first_in),
            ("dresid", dresid_in, dresid),
        )
    ):
        loads[name] = move(src, dst, local_sems.at[at])
    answered(peers)
    loads["out"].wait()

    def columns_of(rank):
        return pl.ds(pl.multiple_of(rank * o_cols, o_cols), o_cols)

    def owner(rel):
        return ring_seq(lax.rem(place + rel, ranks), ranks)

    def exchange(rel):
        to = owner(rel)
        return push(
            dob.at[:, columns_of(to)], dout.at[pl.ds(row(0), local)], dob_send.at[rel], dob_recv.at[rel], (to, dp)
        )

    def project(rel):
        some = columns_of(owner(rel))
        dob[:, some] = dot_nn(dresid_low[...], o_grads[:, :, some].reshape(width, o_cols)).astype(LOW)

    for rel in (*ring_order(ranks)[1:][::-1], 0):
        project(rel)
        if rel:
            exchange(rel).start()
    dout[pl.ds(row(0), local)] = dob[:, columns_of(seq)]

    def out_grads(at, _):
        some_cols = pl.ds(pl.multiple_of(at * deep, deep), deep)
        o_grads[at] = dot_tn(dresid_low[:, some_cols], own_out[...]).astype(LOW)
        return 0

    lax.fori_loop(0, ranks, out_grads, 0)
    mlp_ways[0].start()
    out_piece.first()
    out_piece.second()
    for rel in range(1, ranks):
        exchange(rel).wait_recv()
    for name in ("v", "prob", "k", "q", "cos", "sin", "qkv"):
        loads[name].wait()
    mlp_ways[1].start()
    tall = rows // half
    query_gain_grad[...] = jnp.zeros_like(query_gain_grad)
    key_gain_grad[...] = jnp.zeros_like(key_gain_grad)

    def unrotated(grad, column, rows_at, gain, gain_grad_ref):
        grad = grad * cosv[rows_at] - turn(grad) * sinv[rows_at]
        value = qkv[rows_at, column * size : (column + 1) * size]
        normal, inv = rows_scaled(value)
        gain_grad_ref[...] += jnp.sum(grad * normal, 0, keepdims=True)
        back = rows_scaled_back(value, inv, grad * gain[...])
        dqkv[rows_at, column * size : (column + 1) * size] = back.astype(LOW)

    for head in range(heads):
        group = head // share

        def one(piece, _):
            rows_at = pl.ds(pl.multiple_of(piece * tall, tall), tall)
            weight = prob[head, rows_at]
            grad = dout[rows_at, head * size : (head + 1) * size]
            dprob = dot_nt(grad, v_low[group])
            full = weight.astype(jnp.float32)
            delta = jnp.sum(full * dprob, -1, keepdims=True)
            dscore = (full * (dprob - delta)).astype(LOW)
            dq = dot_nn(dscore, k_low[group]) * scale
            dk_add = dot_tn(dscore, q_low[head, rows_at]) * scale
            dv_add = dot_tn(weight, grad)
            dk[group] += dk_add
            dv[group] += dv_add
            unrotated(dq, head, rows_at, query_gain, query_gain_grad)
            return 0

        if head % share == 0:
            dk[group] = jnp.zeros_like(dk[group])
            dv[group] = jnp.zeros_like(dv[group])
        lax.fori_loop(0, half, one, 0)
        if head == 0:
            mlp_ways[2].start()
    for group in range(kv_heads):
        def one_key(piece, _):
            rows_at = pl.ds(pl.multiple_of(piece * tall, tall), tall)
            unrotated(dk[group, rows_at], heads + group, rows_at, key_gain, key_gain_grad)
            at = (heads + kv_heads + group) * size
            dqkv[rows_at, at : at + size] = dv[group, rows_at].astype(LOW)
            return 0

        lax.fori_loop(0, half, one_key, 0)

    def part(rels, begin, end):
        def some(at, _):
            value = dot_nt(block_rows(dqkv, rels, local, ranks), attn_block[at])
            term[: len(rels) * local, pl.ds(pl.multiple_of(at * deep, deep), deep)] = value
            return 0

        lax.fori_loop(begin, end, some, 0)

    def qkv_grads(at, _):
        some_cols = pl.ds(pl.multiple_of(at * deep, deep), deep)
        grads[at] = dot_tn(first_in[:, some_cols], dqkv[...]).astype(LOW)
        return 0

    def to_ranks(step):
        peer = lax.rem(seq + step, ranks)
        return push(tile, tiles_in.at[seq], sems[17].at[step], sems[18].at[step], (peer, dp))

    def to_copies(step):
        peer = lax.rem(dp + step, copies)
        return push(
            tile_sum, tile_sums_in.at[dp], sems[19].at[step], sems[20].at[step], (seq, peer)
        )

    tile[0:1] = query_gain_grad[...]
    tile[1:2] = key_gain_grad[...]
    tile[2:] = jnp.zeros((tile.shape[0] - 2, size), jnp.float32)
    for step in range(1, ranks):
        to_ranks(step).start()
    tiles_in[seq] = tile[...]
    loads["block"].wait()

    def out_part(rels, begin, end):
        for at, rel in enumerate(rels):
            o_term[at * own : (at + 1) * own] = o_own[owner(rel)].astype(jnp.float32)

    out_total = RingSum(out_part, o_term, o_out, o_in, own, ranks, sems[30], sems[31], right, left)
    totals = two_sums(part, term, out_buf, in_buf, local, ranks, [*sems[2:4], *sems[28:30]], right, left)
    for step in range(1, half + 1):
        for total in totals:
            total.compute(step)
            total.launch(step)
        if step == 1:
            loads["first"].wait()
            lax.fori_loop(0, ranks, qkv_grads, 0)
            qkv_piece.first()
            qkv_piece.second()
        if step == 2:
            out_piece.third()
            for other in range(1, ranks):
                to_ranks(other).wait_recv()
            tile_sum[...] = jnp.sum(tiles_in[...], 0)
            for other in range(1, copies):
                to_copies(other).start()
            tile_sums_in[dp] = tile_sum[...]
        if step == half - 1:
            for other in range(1, copies):
                to_copies(other).wait_recv()
            gains[...] = jnp.sum(tile_sums_in[...], 0)
        if step > 1:
            out_total.compute(step - 1)
            out_total.launch(step - 1)
    out_total.compute(half)
    out_total.launch(half)
    qkv_piece.third()
    qkv_way.start()
    for total in totals:
        total.compute(half + 1)
    loads["dresid"].wait()
    for total in totals:
        total.arrive_last()

    def last(at, _):
        begin = pl.multiple_of(at * 32, 32)
        rows_at = pl.ds(begin, 32)
        value = tokens[rows_at].astype(jnp.float32)
        inv = rows_scaled(value)[1]
        grad = jnp.concatenate([total.last(begin, 32) for total in totals], 1)
        tokens_grad[rows_at] = dresid[rows_at] + rows_scaled_back(value, inv, grad)
        return 0

    lax.fori_loop(0, local // 32, last, 0)
    out_total.compute(half + 1)
    out_total.arrive_last()
    out_grad[...] = out_total.last(0, own)
    for step in range(1, ranks):
        to_ranks(step).wait_send()
    for step in range(1, copies):
        to_copies(step).wait_send()
    out_total.finish()
    for rel in range(1, ranks):
        exchange(rel).wait_send()
    for total in totals:
        total.finish()
    out_piece.finish()
    qkv_piece.finish()
    for way in mlp_ways:
        way.finish()
    qkv_way.finish()


def leave_kernel(
    attn_sums, mlp_sums, gains, attn_gain, mlp_gain, w_query, w_key, w_value, w_gate, w_up,
    query_out, key_out, value_out, gate_out, up_out, down_out, attn_out, mlp_out,
    head_query_out, head_key_out,
):
    own = attn_gain.shape[1]
    same = lax.broadcasted_iota(jnp.int32, (own, own), 0) == lax.broadcasted_iota(jnp.int32, (own, own), 1)

    @pl.when(pl.program_id(0) == 0)
    def _():
        attn_out[...] = jnp.zeros_like(attn_out)
        mlp_out[...] = jnp.zeros_like(mlp_out)
        head_query_out[...] = gains[0:1]
        head_key_out[...] = gains[1:2]

    for sums, gain, gain_out, parts in (
        (attn_sums, attn_gain, attn_out, ((query_out, w_query), (key_out, w_key), (value_out, w_value))),
        (mlp_sums, mlp_gain, mlp_out, ((gate_out, w_gate), (up_out, w_up), (down_out, None))),
    ):
        scale = jnp.sum(jnp.where(same, gain[...], 0.0), 1, keepdims=True)
        for rank in range(sums.shape[0]):
            at = 0
            for out, weight in parts:
                each = out.shape[1] // sums.shape[0]
                cols = slice(rank * each, (rank + 1) * each)
                value = sums[rank, :, at : at + each].astype(jnp.float32)
                at += each
                if weight is None:
                    out[:, cols] = value
                    continue
                out[:, cols] = value * scale
                inner = jnp.sum(value * weight[:, cols].astype(jnp.float32), 1, keepdims=True)
                gain_out[...] += jnp.sum(jnp.where(same, inner, 0.0), 0, keepdims=True)


VM = pl.BlockSpec(memory_space=pltpu.VMEM)
SM = pl.BlockSpec(memory_space=pltpu.SMEM)
ANY = pl.BlockSpec(memory_space=pl.ANY)


def call(kernel, number, ins, outs, scratch, operands):
    return pl.pallas_call(
        kernel,
        out_shape=[jax.ShapeDtypeStruct(shape, dtype) for shape, dtype, _ in outs],
        in_specs=ins,
        out_specs=[spec for _, _, spec in outs],
        scratch_shapes=scratch,
        compiler_params=pltpu.CompilerParams(
            collective_id=number, has_side_effects=True, vmem_limit_bytes=LIMIT
        ),
    )(*operands)


def columns_body(
    tokens,
    out_grad,
    span_order,
    doc_starts,
    w_query,
    w_key,
    w_value,
    w_output,
    attn_gain,
    query_gain,
    key_gain,
    w_gate,
    w_up,
    w_down,
    mlp_gain,
):
    ranks = lax.axis_size("seq")
    copies = lax.axis_size("dp")
    _, local, width = tokens.shape
    rows = local * ranks
    size = query_gain.shape[0]
    kv_heads = w_key.shape[1] // size // ranks
    heads = w_query.shape[1] // size // ranks
    q_cols, kv_cols = heads * size, kv_heads * size
    qkv_cols = q_cols + 2 * kv_cols
    ff = w_gate.shape[1] // ranks
    own = width // (ranks * copies)
    deep = own * copies
    half = ranks // 2
    f32, i32 = jnp.float32, jnp.int32
    exponents = np.arange(size) % (size // 2) * (-2.0 / size * math.log(1000000.0))
    freqs = jnp.asarray(np.exp(exponents)[None], f32)
    q_gain, k_gain = query_gain[None], key_gain[None]
    (
        resid, second, cosv, sinv, q_low, k_low, v_low, own_out, first_in, qkv, attn_block, dy_all, prob, mlp_block,
        out_all,
    ) = call(
        functools.partial(first_kernel, ranks, kv_heads),
        1,
        [SM, SM] + [VM] * 11 + [ANY] * 3,
        [
            ((local, width), f32, VM),
            ((local, width), LOW, VM),
            ((rows, size), f32, VM),
            ((rows, size), f32, VM),
            ((heads, rows, size), LOW, VM),
            ((kv_heads, rows, size), LOW, VM),
            ((kv_heads, rows, size), LOW, VM),
            ((local, q_cols * ranks), LOW, VM),
            ((rows, width), LOW, ANY),
            ((rows, qkv_cols), f32, ANY),
            ((ranks, deep, qkv_cols), LOW, ANY),
            ((rows, width), LOW, ANY),
            ((heads, rows, rows), LOW, ANY),
            ((ranks, deep, 3 * ff), LOW, ANY),
            ((ranks, deep, q_cols * ranks), LOW, ANY),
        ],
        [
            pltpu.VMEM((rows, width), LOW),
            pltpu.VMEM((rows, width), LOW),
            pltpu.VMEM((rows, qkv_cols), f32),
            pltpu.VMEM((ranks, deep, qkv_cols), LOW),
            pltpu.VMEM((ranks, own, qkv_cols), LOW),
            pltpu.VMEM((ranks, own, 3 * ff), LOW),
        ]
        + [pltpu.VMEM((own, ff * ranks), LOW)] * 3
        + [
            pltpu.VMEM((rows, width), LOW),
            pltpu.VMEM((heads, rows, rows), LOW),
            pltpu.VMEM((rows, 1), i32),
            pltpu.VMEM((rows, 1), i32),
            pltpu.VMEM((1, rows), i32),
            pltpu.VMEM((rows, q_cols), LOW),
            pltpu.VMEM((ranks, deep, q_cols * ranks), LOW),
        ]
        + ring_sems(ranks)
        + [pltpu.SemaphoreType.DMA((ranks,))] * 2
        + line_sems(ranks)
        + whole_sems(ranks)[:4]
        + spread_sems(ranks) * 4
        + [pltpu.SemaphoreType.DMA((heads * half + 8,))]
        + whole_sems(ranks)[4:],
        (
            span_order, doc_starts, tokens[0], out_grad[0], freqs, attn_gain[None], mlp_gain[None], q_gain, k_gain,
            w_query, w_key, w_value, w_output, w_gate, w_up, w_down,
        ),
    )
    block_out, dresid, dresid_low, mlp_own = call(
        functools.partial(mlp_kernel, ranks),
        2,
        [VM, VM, ANY, ANY, ANY],
        [
            ((local, width), LOW, VM),
            ((local, width), f32, VM),
            ((local, width), LOW, VM),
            ((ranks, own, 3 * ff), LOW, VM),
        ],
        [pltpu.VMEM((ranks, deep, 3 * ff), LOW)]
        + reduce_bufs(ranks, own, 3 * ff)
        + [
            pltpu.VMEM((rows, width), LOW),
            pltpu.VMEM((ranks, deep, 3 * ff), LOW),
            pltpu.VMEM((rows, ff), LOW),
            pltpu.VMEM((rows, 2 * ff), LOW),
            pltpu.VMEM((local, width), f32),
            pltpu.VMEM((rows, width), LOW),
        ]
        + sum_bufs(local, ranks, width)
        + sum_bufs(local, ranks, width)[1:]
        + [pltpu.SemaphoreType.DMA((3,))]
        + ring_sems(ranks) * 3
        + reduce_sems() * 4,
        (second, out_grad[0], resid, dy_all, mlp_block),
    )
    tokens_grad, gains, wo_grad, mlp_sums, attn_sums = call(
        functools.partial(back_kernel, ranks, kv_heads),
        3,
        [VM] * 5 + [ANY] * 12,
        [
            ((local, width), f32, VM),
            ((8, size), f32, VM),
            ((own, q_cols * ranks), f32, VM),
            ((ranks, own, 3 * ff), LOW, ANY),
            ((ranks, own, qkv_cols), LOW, VM),
        ],
        [pltpu.VMEM((ranks, deep, qkv_cols), LOW)]
        + reduce_bufs(ranks, own, qkv_cols)
        + [
            pltpu.VMEM((ranks, own, qkv_cols), LOW),
            pltpu.VMEM((1, size), f32),
            pltpu.VMEM((1, size), f32),
            pltpu.VMEM((8, size), f32),
            pltpu.VMEM((ranks, 8, size), f32),
            pltpu.VMEM((8, size), f32),
            pltpu.VMEM((copies, 8, size), f32),
            pltpu.VMEM((local, q_cols * ranks), LOW),
            pltpu.VMEM((rows, q_cols), LOW),
            pltpu.VMEM((kv_heads, rows, size), f32),
            pltpu.VMEM((kv_heads, rows, size), f32),
            pltpu.VMEM((rows, qkv_cols), LOW),
            pltpu.VMEM((rows, width), LOW),
            pltpu.VMEM((ranks, deep, qkv_cols), LOW),
            pltpu.VMEM((rows, qkv_cols), f32),
            pltpu.VMEM((rows, size), f32),
            pltpu.VMEM((rows, size), f32),
            pltpu.VMEM((heads, rows, size), LOW),
            pltpu.VMEM((kv_heads, rows, size), LOW),
            pltpu.VMEM((kv_heads, rows, size), LOW),
            pltpu.VMEM((heads, rows, rows), LOW),
            pltpu.VMEM((local, width), f32),
        ]
        + sum_bufs(local, ranks, width)
        + [pltpu.VMEM((ranks, deep, q_cols * ranks), LOW)]
        + reduce_bufs(ranks, own, q_cols * ranks)
        + [pltpu.VMEM((ranks, own, q_cols * ranks), LOW)]
        + sum_bufs(own, ranks, q_cols * ranks)
        + [pltpu.SemaphoreType.DMA((ranks,))] * 2
        + ring_sems(ranks)
        + reduce_sems() * 2
        + deliver_sems(ranks) * 3
        + [pltpu.SemaphoreType.DMA((ranks,))] * 2
        + [pltpu.SemaphoreType.DMA((copies,))] * 2
        + [pltpu.SemaphoreType.DMA((11,))]
        + deliver_sems(ranks) * 2
        + ring_sems(ranks) * 2,
        (
            tokens[0], dresid_low, q_gain, k_gain, own_out, first_in, attn_block, qkv, cosv, sinv, q_low, k_low,
            v_low, prob, dresid, mlp_own, out_all,
        ),
    )
    whole = pl.BlockSpec((1, own), lambda at: (0, 0))
    each = (q_cols, kv_cols, kv_cols, ff, ff, ff)
    many = 2
    columns = [pl.BlockSpec((own, many * cols), lambda at: (0, at)) for cols in each]
    head = pl.BlockSpec((1, size), lambda at: (0, 0))
    *grads, dga, dgm, dgq, dgk = pl.pallas_call(
        leave_kernel,
        grid=(ranks // many,),
        out_shape=[jax.ShapeDtypeStruct((own, cols * ranks), f32) for cols in each]
        + [jax.ShapeDtypeStruct((1, own), f32)] * 2
        + [jax.ShapeDtypeStruct((1, size), f32)] * 2,
        in_specs=[
            pl.BlockSpec((many, own, qkv_cols), lambda at: (at, 0, 0)),
            pl.BlockSpec((many, own, 3 * ff), lambda at: (at, 0, 0)),
            pl.BlockSpec((8, size), lambda at: (0, 0)),
            whole,
            whole,
            *columns[:3],
            *columns[3:5],
        ],
        out_specs=columns + [whole, whole, head, head],
    )(attn_sums, mlp_sums, gains, attn_gain[None], mlp_gain[None], w_query, w_key, w_value, w_gate, w_up)
    return (
        block_out[None], tokens_grad[None], *grads[:3], wo_grad, dga[0], dgq[0], dgk[0], *grads[3:], dgm[0],
    )


def body(*args):
    tokens, w_key, query_gain = args[0], args[5], args[9]
    groups = w_key.shape[1] // query_gain.shape[0]
    ranks = lax.axis_size("seq")
    if tokens.shape[0] == 1 and ranks % 2 == 0 and groups % ranks == 0 and lax.axis_size("dp") == 4:
        return columns_body(*args)
    return gathered_body(*args)


def solution(mesh):
    return jax.shard_map(
        body,
        mesh=mesh,
        in_specs=(
            P("dp", "seq", None),
            P("dp", "seq", None),
            P(),
            P("dp", None),
            P(("seq", "dp"), None),
            P(("seq", "dp"), None),
            P(("seq", "dp"), None),
            P(("seq", "dp"), None),
            P(("seq", "dp")),
            P(),
            P(),
            P(("seq", "dp"), None),
            P(("seq", "dp"), None),
            P(("seq", "dp"), None),
            P(("seq", "dp")),
        ),
        out_specs=(
            P("dp", "seq", None),
            P("dp", "seq", None),
            P(("seq", "dp"), None),
            P(("seq", "dp"), None),
            P(("seq", "dp"), None),
            P(("seq", "dp"), None),
            P(("seq", "dp")),
            P(),
            P(),
            P(("seq", "dp"), None),
            P(("seq", "dp"), None),
            P(("seq", "dp"), None),
            P(("seq", "dp")),
        ),
        check_vma=False,
    )
```

```python
import functools
import math

import jax
import jax.numpy as jnp
import numpy as np
from jax import lax
from jax.experimental import pallas as pl
from jax.experimental.pallas import tpu as pltpu
from jax.sharding import PartitionSpec as P

EPS = 1e-06
NEG = -1e30


def normed(v, gain):
    scale_inv = lax.rsqrt(jnp.mean(v * v, -1, keepdims=True) + EPS)
    return (v * scale_inv * gain, scale_inv)


def norm_back(v, scale_inv, gain, grad):
    scaled = grad * gain
    inner = jnp.mean(scaled * v, -1, keepdims=True)
    dv = scale_inv * scaled - v * scale_inv * scale_inv * scale_inv * inner
    dgain = jnp.sum((grad * v * scale_inv).reshape(-1, v.shape[-1]), 0)
    return (dv, dgain)


def rotary(pos, width):
    half = width // 2
    freqs = jnp.exp(jnp.arange(half, dtype=jnp.float32) * (-2.0 / width * math.log(1000000.0)))
    angle = pos.astype(jnp.float32)[:, None] * freqs[None, :]
    return (jnp.cos(angle)[:, None, :], jnp.sin(angle)[:, None, :])


def rotate(v, cosv, sinv):
    half = v.shape[-1] // 2
    first, second = (v[..., :half], v[..., half:])
    return jnp.concatenate([first * cosv - second * sinv, second * cosv + first * sinv], -1)


def rotate_back(grad, cosv, sinv):
    half = grad.shape[-1] // 2
    first, second = (grad[..., :half], grad[..., half:])
    return jnp.concatenate([first * cosv + second * sinv, second * cosv - first * sinv], -1)


def place(order, begin, count, span):
    rows = begin + jnp.arange(count, dtype=jnp.int32)
    slots = rows // span
    picked = slots[:, None] == jnp.arange(order.shape[0], dtype=jnp.int32)[None, :]
    return jnp.sum(jnp.where(picked, order[None, :], 0), -1) * span + rows % span


def doc_of(starts, pos):
    return jnp.sum((starts[:, None, :] <= pos[None, :, None]).astype(jnp.int32), -1)


def gathered_body(
    tokens,
    out_grad,
    span_order,
    doc_starts,
    w_query,
    w_key,
    w_value,
    w_output,
    attn_gain,
    query_gain,
    key_gain,
    w_gate,
    w_up,
    w_down,
    mlp_gain,
):
    seqs, local, width = tokens.shape
    span = local // 2
    head_size = query_gain.shape[0]
    kv_heads = w_key.shape[1] // head_size
    heads = w_query.shape[1] // head_size
    share = heads // kv_heads
    kv_width = kv_heads * head_size
    ff_width = w_gate.shape[1]
    scale = 1.0 / math.sqrt(head_size)
    total_rows = seqs * local
    own_rows = width // lax.axis_size(("seq", "dp"))
    qpos = place(span_order, lax.axis_index("seq") * local, local, span)
    qdoc = doc_of(doc_starts, qpos)
    cosv, sinv = rotary(qpos, head_size)

    def gather_attn():
        return (
            lax.all_gather(w_query, ("seq", "dp"), axis=0, tiled=True),
            lax.all_gather(w_key, ("seq", "dp"), axis=0, tiled=True),
            lax.all_gather(w_value, ("seq", "dp"), axis=0, tiled=True),
            lax.all_gather(w_output, ("seq", "dp"), axis=0, tiled=True),
            lax.all_gather(
                attn_gain.astype(jnp.bfloat16), ("seq", "dp"), axis=0, tiled=True
            ).astype(attn_gain.dtype),
        )

    def gather_mlp():
        return (
            lax.all_gather(w_gate, ("seq", "dp"), axis=0, tiled=True),
            lax.all_gather(w_up, ("seq", "dp"), axis=0, tiled=True),
            lax.all_gather(w_down, ("seq", "dp"), axis=0, tiled=True),
            lax.all_gather(mlp_gain.astype(jnp.bfloat16), ("seq", "dp"), axis=0, tiled=True).astype(
                mlp_gain.dtype
            ),
        )

    x_rows = tokens.astype(jnp.float32).reshape(total_rows, width)
    wq_all, wk_all, wv_all, wo_all, ga_all = gather_attn()
    first_norm, first_inv = normed(x_rows, ga_all)
    first_in = first_norm.astype(jnp.bfloat16)
    q_raw = jnp.dot(first_in, wq_all, preferred_element_type=jnp.float32).reshape(
        seqs, local, heads, head_size
    )
    k_raw = jnp.dot(first_in, wk_all, preferred_element_type=jnp.float32).reshape(
        seqs, local, kv_heads, head_size
    )
    v_low = (
        jnp.dot(first_in, wv_all, preferred_element_type=jnp.float32)
        .astype(jnp.bfloat16)
        .reshape(seqs, local, kv_heads, head_size)
    )
    q_normed, q_inv = normed(q_raw, query_gain)
    k_normed, k_inv = normed(k_raw, key_gain)
    q_low = rotate(q_normed, cosv, sinv).astype(jnp.bfloat16)
    k_low = rotate(k_normed, cosv, sinv).astype(jnp.bfloat16)
    q_group = q_low.reshape(seqs, local, kv_heads, share, head_size)

    def scores(piece_key, start):
        count = piece_key.shape[1]
        kpos = place(span_order, start, count, span)
        kdoc = doc_of(doc_starts, kpos)
        visible = (qdoc[:, :, None] == kdoc[:, None, :]) & (
            kpos[None, None, :] <= qpos[None, :, None]
        )
        raw = (
            jnp.einsum("sqgjd,skgd->sgjqk", q_group, piece_key, preferred_element_type=jnp.float32)
            * scale
        )
        return (raw, visible[:, None, None])

    start_top = jnp.full((seqs, kv_heads, share, local), NEG, jnp.float32)
    piece = (
        lax.all_gather(k_low, "seq", axis=1, tiled=True),
        lax.all_gather(v_low, "seq", axis=1, tiled=True),
    )
    top = start_top
    raw, visible = scores(piece[0], jnp.int32(0))
    raw = jnp.where(visible, raw, NEG)
    new_top = jnp.maximum(top, jnp.max(raw, -1))
    weights = jnp.where(visible, jnp.exp(raw - new_top[..., None]), 0.0)
    total = jnp.sum(weights, -1)
    summed = jnp.einsum(
        "sgjqk,skgd->sgjqd",
        weights.astype(jnp.bfloat16),
        piece[1],
        preferred_element_type=jnp.float32,
    )
    top, total, summed = (new_top, total, summed)
    log_total = top + jnp.log(total)
    attn_vals = summed / total[..., None]
    out_low = (
        jnp.transpose(attn_vals, (0, 3, 1, 2, 4))
        .reshape(total_rows, heads * head_size)
        .astype(jnp.bfloat16)
    )
    resid = x_rows + jnp.einsum("nh,dh->nd", out_low, wo_all, preferred_element_type=jnp.float32)
    wg_all, wu_all, wd_all, gm_all = gather_mlp()
    second_norm, second_inv = normed(resid, gm_all)
    second_in = second_norm.astype(jnp.bfloat16)
    gate = jnp.dot(second_in, wg_all, preferred_element_type=jnp.float32)
    upper = jnp.dot(second_in, wu_all, preferred_element_type=jnp.float32)
    sigma = jax.nn.sigmoid(gate)
    act = gate * sigma
    hidden = (act * upper).astype(jnp.bfloat16)
    result = resid + jnp.einsum("nf,df->nd", hidden, wd_all, preferred_element_type=jnp.float32)
    block_out = result.astype(jnp.bfloat16).reshape(seqs, local, width)
    grad_low = out_grad.reshape(total_rows, width)
    wg_all, wu_all, wd_all, gm_all = gather_mlp()
    dmid = jnp.einsum("nd,df->nf", grad_low, wd_all, preferred_element_type=jnp.float32)
    dgate = (dmid * upper * sigma * (1.0 + gate * (1.0 - sigma))).astype(jnp.bfloat16)
    dupper = (dmid * act).astype(jnp.bfloat16)
    left = second_in
    outer = grad_low
    mlp_sums = lax.psum_scatter(
        jnp.concatenate(
            [
                jnp.einsum("nd,nf->df", left, dgate, preferred_element_type=jnp.float32),
                jnp.einsum("nd,nf->df", left, dupper, preferred_element_type=jnp.float32),
                jnp.einsum("nd,nf->df", outer, hidden, preferred_element_type=jnp.float32),
            ],
            1,
        ),
        ("seq", "dp"),
        scatter_dimension=0,
        tiled=True,
    )
    dsecond = jnp.einsum(
        "nf,df->nd", dgate, wg_all, preferred_element_type=jnp.float32
    ) + jnp.einsum("nf,df->nd", dupper, wu_all, preferred_element_type=jnp.float32)
    dresid_norm, dgm = norm_back(resid, second_inv, gm_all, dsecond)
    dresid = grad_low.astype(jnp.float32) + dresid_norm
    dresid_low = dresid.astype(jnp.bfloat16)
    wq_all, wk_all, wv_all, wo_all, ga_all = gather_attn()
    dout_low = jnp.einsum(
        "nd,dh->nh", dresid_low, wo_all, preferred_element_type=jnp.float32
    ).astype(jnp.bfloat16)
    dout_group = dout_low.reshape(seqs, local, kv_heads, share, head_size)
    delta = jnp.sum(jnp.transpose(dout_group.astype(jnp.float32), (0, 2, 3, 1, 4)) * attn_vals, -1)
    piece = (
        lax.all_gather(k_low, "seq", axis=1, tiled=True),
        lax.all_gather(v_low, "seq", axis=1, tiled=True),
    )
    count = piece[0].shape[1]
    raw, visible = scores(piece[0], jnp.int32(0))
    prob = jnp.where(visible, jnp.exp(raw - log_total[..., None]), 0.0)
    dprob = jnp.einsum(
        "sqgjd,skgd->sgjqk", dout_group, piece[1], preferred_element_type=jnp.float32
    )
    dscore = (prob * (dprob - delta[..., None])).astype(jnp.bfloat16)
    dq_sum = jnp.einsum("sgjqk,skgd->sqgjd", dscore, piece[0], preferred_element_type=jnp.float32)
    dk_part = (
        jnp.einsum("sgjqk,sqgjd->skgd", dscore, q_group, preferred_element_type=jnp.float32) * scale
    )
    dv_part = jnp.einsum(
        "sgjqk,sqgjd->skgd",
        prob.astype(jnp.bfloat16),
        dout_group,
        preferred_element_type=jnp.float32,
    )
    joined = jnp.concatenate(
        [dk_part.reshape(seqs, count, kv_width), dv_part.reshape(seqs, count, kv_width)], -1
    )
    buffer = joined
    dq_sum, buffer = (dq_sum, buffer)
    key_sums = lax.psum_scatter(
        buffer.astype(jnp.bfloat16), "seq", scatter_dimension=1, tiled=True
    ).astype(jnp.float32)
    dq_rot = (dq_sum * scale).reshape(seqs, local, heads, head_size)
    dq_raw, dgq = norm_back(q_raw, q_inv, query_gain, rotate_back(dq_rot, cosv, sinv))
    dk_rot = key_sums[..., :kv_width].reshape(seqs, local, kv_heads, head_size)
    dk_raw, dgk = norm_back(k_raw, k_inv, key_gain, rotate_back(dk_rot, cosv, sinv))
    dq_low = dq_raw.reshape(total_rows, heads * head_size).astype(jnp.bfloat16)
    dk_low = dk_raw.reshape(total_rows, kv_width).astype(jnp.bfloat16)
    dv_low = key_sums[..., kv_width:].reshape(total_rows, kv_width).astype(jnp.bfloat16)
    left = first_in
    outer = dresid_low
    attn_sums = lax.psum_scatter(
        jnp.concatenate(
            [
                jnp.einsum("nd,nh->dh", left, dq_low, preferred_element_type=jnp.float32),
                jnp.einsum("nd,nh->dh", left, dk_low, preferred_element_type=jnp.float32),
                jnp.einsum("nd,nh->dh", left, dv_low, preferred_element_type=jnp.float32),
                jnp.einsum("nd,nh->dh", outer, out_low, preferred_element_type=jnp.float32),
            ],
            1,
        ),
        ("seq", "dp"),
        scatter_dimension=0,
        tiled=True,
    )
    dfirst = jnp.einsum("nh,dh->nd", dq_low, wq_all, preferred_element_type=jnp.float32)
    dfirst = dfirst + jnp.einsum("nh,dh->nd", dk_low, wk_all, preferred_element_type=jnp.float32)
    dfirst = dfirst + jnp.einsum("nh,dh->nd", dv_low, wv_all, preferred_element_type=jnp.float32)
    dx_norm, dga = norm_back(x_rows, first_inv, ga_all, dfirst)
    tokens_grad = (dresid + dx_norm).reshape(seqs, local, width)
    dga_all, dgm_all, dgq_all, dgk_all = lax.psum((dga, dgm, dgq, dgk), ("seq", "dp"))
    offset = lax.axis_index(("seq", "dp")) * own_rows
    attn_gain_grad = lax.dynamic_slice_in_dim(dga_all, offset, own_rows, 0)
    mlp_gain_grad = lax.dynamic_slice_in_dim(dgm_all, offset, own_rows, 0)
    q_cols = heads * head_size
    w_query_grad = attn_sums[:, :q_cols]
    w_key_grad = attn_sums[:, q_cols : q_cols + kv_width]
    w_value_grad = attn_sums[:, q_cols + kv_width : q_cols + 2 * kv_width]
    w_output_grad = attn_sums[:, q_cols + 2 * kv_width :]
    w_gate_grad = mlp_sums[:, :ff_width]
    w_up_grad = mlp_sums[:, ff_width : 2 * ff_width]
    w_down_grad = mlp_sums[:, 2 * ff_width :]
    return (
        block_out,
        tokens_grad,
        w_query_grad,
        w_key_grad,
        w_value_grad,
        w_output_grad,
        attn_gain_grad,
        dgq_all,
        dgk_all,
        w_gate_grad,
        w_up_grad,
        w_down_grad,
        mlp_gain_grad,
    )


LOW = jnp.bfloat16
MESH = pl.DeviceIdType.MESH
LIMIT = 60 * 2**20


def ring_order(ranks):
    half = ranks // 2
    order = [0]
    for step in range(1, half):
        order += [step, ranks - step]
    return order + [half]


def ring_place(seq, ranks):
    z, x = lax.div(seq, 2), lax.rem(seq, 2)
    return z + x * (ranks - 1 - 2 * z)


def ring_seq(place, ranks):
    half = ranks // 2
    x, z = lax.div(place, half), lax.rem(place, half)
    return 2 * (z + x * (half - 1 - 2 * z)) + x


def neighbours(ranks):
    seq, dp = lax.axis_index("seq"), lax.axis_index("dp")
    at = ring_place(seq, ranks)
    right = ring_seq(lax.rem(at + 1, ranks), ranks)
    left = ring_seq(lax.rem(at + ranks - 1, ranks), ranks)
    return (right, dp), (left, dp)


def knock(devices):
    barrier = pltpu.get_barrier_semaphore()
    for device in devices:
        pl.semaphore_signal(barrier, inc=1, device_id=device, device_id_type=MESH)


def answered(devices):
    pl.semaphore_wait(pltpu.get_barrier_semaphore(), len(devices))


def move(src, dst, sem):
    copy = pltpu.make_async_copy(src, dst, sem)
    copy.start()
    return copy


def push(src, dst, send, recv, device):
    return pltpu.make_async_remote_copy(
        src_ref=src, dst_ref=dst, send_sem=send, recv_sem=recv, device_id=device, device_id_type=MESH
    )


def dot_nn(left, right):
    return jnp.dot(left, right, preferred_element_type=jnp.float32)


def dot_nt(left, right):
    return lax.dot_general(left, right, (((1,), (1,)), ((), ())), preferred_element_type=jnp.float32)


def dot_tn(left, right):
    return lax.dot_general(left, right, (((0,), (0,)), ((), ())), preferred_element_type=jnp.float32)


def block_row(rel, local, ranks):
    place = ring_place(lax.axis_index("seq"), ranks)
    return pl.multiple_of(ring_seq(lax.rem(place + rel, ranks), ranks) * local, local)


def block_rows(ref, rels, local, ranks):
    blocks = [ref[pl.ds(block_row(rel, local, ranks), local)] for rel in rels]
    return blocks[0] if len(blocks) == 1 else jnp.concatenate(blocks, 0)


def rels_of(step, ranks):
    return [rel for rel in ring_order(ranks) if min(rel, ranks - rel) == step]


class RingGather:
    def __init__(self, buf, local, ranks, send, recv, right, left, row):
        self.buf, self.sub, self.half = buf, local // 2, ranks // 2
        self.send, self.recv, self.right, self.left = send, recv, right, left
        self.ranks, self.row = ranks, row

    def copies(self, step, part):
        ways = ((0, (self.ranks - step + 1) % self.ranks, self.right), (1, step - 1, self.left))
        given = []
        for way, rel, device in ways:
            if step < self.half or way == part:
                block = self.buf.at[pl.ds(self.row(rel) + part * self.sub, self.sub)]
                at = 2 * (step - 1) + part
                given.append(push(block, block, self.send.at[way, at], self.recv.at[way, at], device))
        return given

    def start(self, step):
        for part in range(2):
            for copy in self.copies(step, part):
                copy.start()

    def advance(self, step):
        for part in range(2):
            for copy in self.copies(step, part):
                copy.wait_recv()
            if step < self.half:
                for copy in self.copies(step + 1, part):
                    copy.start()

    def finish(self):
        for step in range(1, self.half + 1):
            for part in range(2):
                for copy in self.copies(step, part):
                    copy.wait_send()


class LineGather:
    def __init__(self, buf, local, ranks, send, recv, x_send, x_recv):
        self.buf, self.local, self.length = buf, local, ranks // 2
        self.send, self.recv, self.x_send, self.x_recv = send, recv, x_send, x_recv
        self.seq, self.dp = lax.axis_index("seq"), lax.axis_index("dp")
        self.z, self.x = lax.div(self.seq, 2), lax.rem(self.seq, 2)

    def block(self, z):
        return self.buf.at[pl.ds(pl.multiple_of((2 * z + self.x) * self.local, self.local), self.local)]

    def hop(self, way, step):
        block = self.block(self.z + (step - 1 if way else 1 - step))
        to = self.seq + (-2 if way else 2)
        return push(block, block, self.send.at[way, step - 1], self.recv.at[way, step - 1], (to, self.dp))

    def sends(self, way, step):
        if way:
            return (self.z > 0) & (self.z + step <= self.length)
        return (self.z < self.length - 1) & (self.z >= step - 1)

    def comes(self, way, step):
        return self.z + step < self.length if way else self.z >= step

    def across(self, way, step):
        block = self.block(self.z + (step if way else -step))
        at = step + way * (self.length - 1)
        return push(
            block, block, self.x_send.at[at], self.x_recv.at[at], (self.seq + 1 - 2 * self.x, self.dp)
        )

    def from_x(self, way, step):
        z = self.z + (step if way else -step)
        row = pl.multiple_of((2 * z + 1 - self.x) * self.local, self.local)
        block = self.buf.at[pl.ds(row, self.local)]
        at = step + way * (self.length - 1)
        return push(
            block, block, self.x_send.at[at], self.x_recv.at[at], (self.seq + 1 - 2 * self.x, self.dp)
        )

    def start(self, step):
        for way in range(2):
            pl.when(self.sends(way, step))(lambda way=way: self.hop(way, step).start())
        self.pass_on(step - 1)

    def pass_on(self, step):
        if step == 0:
            self.across(0, 0).start()
            return
        for way in range(2):
            pl.when(self.comes(way, step))(lambda way=way: self.across(way, step).start())

    def arrive(self, step):
        for way in range(2):
            pl.when(self.comes(way, step))(lambda way=way: self.incoming(way, step).wait_recv())

    def incoming(self, way, step):
        block = self.block(self.z + (step if way else -step))
        to = self.seq + 1 - 2 * self.x
        return push(block, block, self.send.at[way, step - 1], self.recv.at[way, step - 1], (to, self.dp))

    def run(self):
        for step in range(1, self.length):
            self.advance(step)

    def advance(self, step):
        self.arrive(step)
        if step < self.length - 1:
            self.start(step + 1)
        else:
            self.pass_on(step)

    def complete(self):
        self.from_x(0, 0).wait_recv()
        for step in range(1, self.length):
            for way in range(2):
                pl.when(self.comes(way, step))(lambda way=way: self.from_x(way, step).wait_recv())

    def finish(self):
        self.across(0, 0).wait_send()
        for step in range(1, self.length):
            for way in range(2):
                pl.when(self.sends(way, step))(lambda way=way: self.hop(way, step).wait_send())
                pl.when(self.comes(way, step))(lambda way=way: self.across(way, step).wait_send())


def line_sems(ranks):
    half = ranks // 2
    return [pltpu.SemaphoreType.DMA((2, half))] * 2 + [pltpu.SemaphoreType.DMA((2 * half,))] * 2


class RingSum:
    def __init__(self, part, term, out_buf, in_buf, local, ranks, send, recv, right, left, stream=0, streams=1):
        self.part, self.term, self.out_buf, self.in_buf = part, term, out_buf, in_buf
        self.local, self.ranks, self.half = local, ranks, ranks // 2
        each = term.shape[1] // streams
        self.cols = pl.ds(stream * each, each)
        self.tiles = (stream * ranks // streams, (stream + 1) * ranks // streams)
        self.send, self.recv, self.right, self.left = send, recv, right, left

    def copies(self, step):
        rows = self.local // 2 if step == 1 else self.local
        skip = self.local // 2 if step == 1 else 0
        return [
            push(
                self.out_buf.at[way, (step - 1) % 2, pl.ds(begin, rows), self.cols],
                self.in_buf.at[way, step - 1, pl.ds(begin, rows), self.cols],
                self.send.at[way, step - 1],
                self.recv.at[way, step - 1],
                device,
            )
            for way, begin, device in ((0, 0, self.right), (1, skip, self.left))
        ]

    def compute(self, step):
        if step == 1:
            self.part([self.half], *self.tiles)
        elif step <= self.half:
            self.part(rels_of(self.half + 1 - step, self.ranks), *self.tiles)
        else:
            self.part([0], *self.tiles)

    def launch(self, step):
        local, skip = self.local, self.local // 2
        if step > 2:
            for copy in self.copies(step - 2):
                copy.wait_send()
        if step == 1:
            for way in range(2):
                rows = pl.ds(way * skip, skip)
                self.out_buf[way, 0, rows, self.cols] = self.term[rows, self.cols].astype(LOW)
        else:
            for copy in self.copies(step - 1):
                copy.wait_recv()
            for way in range(2):
                for begin, with_sum in ((0, step > 2 or way == 0), (skip, step > 2 or way == 1)):
                    value = self.term[pl.ds(way * local + begin, skip), self.cols]
                    if with_sum:
                        value = value + self.in_buf[way, step - 2, pl.ds(begin, skip), self.cols].astype(jnp.float32)
                    self.out_buf[way, (step - 1) % 2, pl.ds(begin, skip), self.cols] = value.astype(LOW)
        for copy in self.copies(step):
            copy.start()

    def last(self, begin, count):
        rows = pl.ds(begin, count)
        value = self.term[rows, self.cols] + self.in_buf[0, self.half - 1, rows, self.cols].astype(jnp.float32)
        return value + self.in_buf[1, self.half - 1, rows, self.cols].astype(jnp.float32)

    def arrive_last(self):
        for copy in self.copies(self.half):
            copy.wait_recv()

    def finish(self):
        for step in range(max(1, self.half - 1), self.half + 1):
            for copy in self.copies(step):
                copy.wait_send()


def two_sums(part, term, out_buf, in_buf, local, ranks, sems, right, left):
    return [
        RingSum(
            part, term, out_buf, in_buf, local, ranks, sems[2 * at], sems[2 * at + 1], right, left, at, 2
        )
        for at in range(2)
    ]


def ring_sems(ranks):
    return [pltpu.SemaphoreType.DMA((2, ranks)), pltpu.SemaphoreType.DMA((2, ranks))]


def sum_bufs(local, ranks, width):
    return [
        pltpu.VMEM((2 * local, width), jnp.float32),
        pltpu.VMEM((2, 2, local, width), LOW),
        pltpu.VMEM((2, ranks // 2, local, width), LOW),
    ]


def turn(v):
    return pltpu.roll(v, v.shape[-1] // 2, v.ndim - 1)


def rows_scaled(v):
    inv = lax.rsqrt(jnp.mean(v * v, -1, keepdims=True) + EPS)
    return v * inv, inv


def rows_scaled_back(v, inv, grad):
    return inv * grad - v * (inv * inv * inv * jnp.mean(grad * v, -1, keepdims=True))


class Spread:
    def __init__(self, rows, block, ranks, own, cols, sems):
        self.rows, self.block, self.ranks, self.own, self.cols = rows, block, ranks, own, cols
        self.send, self.recv, self.hop_send, self.hop_recv, self.here = sems
        self.seq, self.dp = lax.axis_index("seq"), lax.axis_index("dp")
        y, core = lax.div(self.dp, 2), lax.rem(self.dp, 2)
        self.beside, self.sibling = (1 - y) * 2 + core, y * 2 + 1 - core

    def at(self, dp):
        return pl.ds(pl.multiple_of(dp * self.own, self.own), self.own)

    def exchange(self):
        for step in range(1, self.ranks):
            peer = lax.rem(self.seq + step, self.ranks)
            yield push(
                self.rows.at[peer, :, self.cols],
                self.block.at[self.seq, self.at(self.dp), self.cols],
                self.send.at[step],
                self.recv.at[step],
                (peer, self.dp),
            )

    def keep(self):
        return pltpu.make_async_copy(
            self.rows.at[self.seq, :, self.cols],
            self.block.at[self.seq, self.at(self.dp), self.cols],
            self.here,
        )

    def hop(self, number):
        dp = self.beside if number == 2 else self.dp
        part = self.block.at[:, self.at(dp), self.cols]
        to = self.beside if number == 0 else self.sibling
        return push(part, part, self.hop_send.at[number], self.hop_recv.at[number], (self.seq, to))

    def start(self):
        self.keep().start()
        for copy in self.exchange():
            copy.start()

    def arrive(self):
        self.keep().wait()
        for copy in self.exchange():
            copy.wait_recv()

    def finish(self):
        for copy in self.exchange():
            copy.wait_send()
        for number in range(3):
            self.hop(number).wait_send()


def spread_sems(ranks):
    return [
        pltpu.SemaphoreType.DMA((ranks,)),
        pltpu.SemaphoreType.DMA((ranks,)),
        pltpu.SemaphoreType.DMA((3,)),
        pltpu.SemaphoreType.DMA((3,)),
        pltpu.SemaphoreType.DMA,
    ]


class WholeGather:
    def __init__(self, block, ranks, own, sems):
        self.block, self.ranks, self.half, self.own = block, ranks, ranks // 2, own
        self.send, self.recv, self.y_send, self.y_recv, self.core_send, self.core_recv = sems
        self.seq, self.dp = lax.axis_index("seq"), lax.axis_index("dp")
        self.right, self.left = neighbours(ranks)
        self.place = ring_place(self.seq, ranks)
        y, core = lax.div(self.dp, 2), lax.rem(self.dp, 2)
        self.beside, self.sibling = (1 - y) * 2 + core, y * 2 + 1 - core

    def at(self, rel, dp, begin, count):
        seq = ring_seq(lax.rem(self.place + rel + self.ranks, self.ranks), self.ranks)
        return self.block.at[seq, pl.ds(pl.multiple_of(dp * self.own + begin, count), count)]

    def copies(self, step):
        last = step == self.half
        rows = self.own // 2 if last else self.own
        skip = self.own // 2 if last else 0
        given = []
        for way, rel, begin, device in ((0, 1 - step, 0, self.right), (1, step - 1, skip, self.left)):
            part = self.at(rel, self.dp, begin, rows)
            given.append(push(part, part, self.send.at[way, step - 1], self.recv.at[way, step - 1], device))
        return given

    def start(self, step):
        for copy in self.copies(step):
            copy.start()

    def hops(self, step):
        for at, rel in enumerate(ring_order(self.ranks)):
            if min(rel, self.ranks - rel) == step:
                part = self.at(rel, self.dp, 0, self.own)
                yield push(part, part, self.y_send.at[at], self.y_recv.at[at], (self.seq, self.beside))
                yield push(part, part, self.core_send.at[at], self.core_recv.at[at], (self.seq, self.sibling))

    def arrive(self, step):
        for copy in self.copies(step):
            copy.wait_recv()

    def forward(self, step):
        for copy in self.hops(step):
            copy.start()

    def cross(self):
        part = self.block.at[:, pl.ds(pl.multiple_of(self.beside * self.own, self.own), self.own)]
        at = self.ranks
        return push(part, part, self.core_send.at[at], self.core_recv.at[at], (self.seq, self.sibling))

    def complete(self):
        for step in range(self.half + 1):
            for copy in self.hops(step):
                copy.wait_recv()
        self.cross().start()
        self.cross().wait_recv()

    def finish(self):
        for step in range(1, self.half + 1):
            for copy in self.copies(step):
                copy.wait_send()
        for step in range(self.half + 1):
            for copy in self.hops(step):
                copy.wait_send()
        self.cross().wait_send()


def whole_sems(ranks):
    return (
        ring_sems(ranks)
        + [pltpu.SemaphoreType.DMA((ranks,))] * 2
        + [pltpu.SemaphoreType.DMA((ranks + 1,))] * 2
    )


class Reduce:
    def __init__(self, grads, from_core, from_y, total, own, first, count, cols, sems):
        self.grads, self.from_core, self.from_y, self.total = grads, from_core, from_y, total
        self.own, self.begin, self.count, self.cols = own, first, count, cols
        self.send, self.recv = sems
        self.seq, dp = lax.axis_index("seq"), lax.axis_index("dp")
        self.y, self.core = lax.div(dp, 2), lax.rem(dp, 2)
        self.beside, self.sibling = (1 - self.y) * 2 + self.core, self.y * 2 + 1 - self.core

    def at(self, y, core):
        return pl.ds(pl.multiple_of((y * 2 + core) * self.own, self.own), self.own)

    def hop(self, number):
        some, cols = pl.ds(self.begin, self.count), self.cols
        if number == 2:
            src, dst, to = self.from_core.at[0, some, :, cols], self.from_y.at[some, :, cols], self.beside
        else:
            rows = self.at(1 - self.y if number == 0 else self.y, 1 - self.core)
            src, dst, to = self.grads.at[some, rows, cols], self.from_core.at[number, some, :, cols], self.sibling
        return push(src, dst, self.send.at[number], self.recv.at[number], (self.seq, to))

    def first(self):
        self.hop(0).start()
        self.hop(1).start()

    def second(self):
        self.hop(0).wait_recv()
        rows = self.at(1 - self.y, self.core)

        def some(at, _):
            value = self.grads[at, rows, self.cols].astype(jnp.float32)
            value = value + self.from_core[0, at, :, self.cols].astype(jnp.float32)
            self.from_core[0, at, :, self.cols] = value.astype(LOW)
            return 0

        lax.fori_loop(self.begin, self.begin + self.count, some, 0)
        self.hop(2).start()

    def third(self):
        self.hop(1).wait_recv()
        self.hop(2).wait_recv()
        rows = self.at(self.y, self.core)

        def some(at, _):
            value = self.grads[at, rows, self.cols].astype(jnp.float32)
            value = value + self.from_core[1, at, :, self.cols].astype(jnp.float32)
            value = value + self.from_y[at, :, self.cols].astype(jnp.float32)
            self.total[at, :, self.cols] = value.astype(LOW)
            return 0

        lax.fori_loop(self.begin, self.begin + self.count, some, 0)

    def finish(self):
        for number in range(3):
            self.hop(number).wait_send()


def reduce_sems():
    return [pltpu.SemaphoreType.DMA((3,)), pltpu.SemaphoreType.DMA((3,))]


def reduce_bufs(ranks, own, cols):
    return [pltpu.VMEM((2, ranks, own, cols), LOW), pltpu.VMEM((ranks, own, cols), LOW)]


class Deliver:
    def __init__(self, rows, out, cols, ranks, sems):
        self.rows, self.out, self.cols, self.ranks = rows, out, cols, ranks
        self.send, self.recv, self.here = sems
        self.seq, self.dp = lax.axis_index("seq"), lax.axis_index("dp")

    def exchange(self):
        for step in range(1, self.ranks):
            peer = lax.rem(self.seq + step, self.ranks)
            yield push(
                self.rows.at[peer, :, self.cols],
                self.out.at[self.seq, :, self.cols],
                self.send.at[step],
                self.recv.at[step],
                (peer, self.dp),
            )

    def keep(self):
        return pltpu.make_async_copy(
            self.rows.at[self.seq, :, self.cols], self.out.at[self.seq, :, self.cols], self.here
        )

    def start(self):
        self.keep().start()
        for copy in self.exchange():
            copy.start()

    def finish(self):
        self.keep().wait()
        for copy in self.exchange():
            copy.wait_recv()
        for copy in self.exchange():
            copy.wait_send()


def deliver_sems(ranks):
    return [pltpu.SemaphoreType.DMA((ranks,)), pltpu.SemaphoreType.DMA((ranks,)), pltpu.SemaphoreType.DMA]


def first_kernel(
    ranks, kv_heads, order, starts, tokens, out_grad, freqs, attn_gain, mlp_gain, query_gain, key_gain,
    w_query, w_key, w_value, w_output, w_gate, w_up, w_down,
    resid, second, cosv, sinv, q_low, k_low, v_low, own_out, first_in, qkv, attn_block, dy_all, prob, mlp_block, out_all,
    held, normal, kept, block, a_rows, m_rows, gate, up, down, dys, probs, pos, begins, pos_row,
    out_low, whole, *sems,
):
    local, width = tokens.shape
    rows = local * ranks
    own = w_query.shape[0]
    size = freqs.shape[1]
    heads = q_low.shape[0]
    share = heads // kv_heads
    half = ranks // 2
    scale = 1.0 / math.sqrt(size)
    cols = (heads + 2 * kv_heads) * size
    deep = block.shape[1]
    row = functools.partial(block_row, local=local, ranks=ranks)
    seq, dp = lax.axis_index("seq"), lax.axis_index("dp")
    right, left = neighbours(ranks)
    attn = Spread(a_rows, block, ranks, own, pl.ds(0, a_rows.shape[2]), sems[12:17])
    third = m_rows.shape[2] // 3
    mlp = [
        Spread(m_rows, mlp_block, ranks, own, pl.ds(at * third, third), sems[17 + 5 * at : 22 + 5 * at])
        for at in range(3)
    ]
    local_sems = sems[32]
    out_send, out_recv = sems[2:4]
    o_cols = heads * size
    peers = [(lax.rem(seq + step, ranks), dp) for step in range(1, ranks)]
    peers += [(seq, attn.beside), (seq, attn.sibling)]
    knock(peers)
    loads = [
        move(src, dst, local_sems.at[at])
        for at, (src, dst) in enumerate(((w_gate, gate), (w_up, up), (w_down, down)))
    ]
    held[pl.ds(row(0), local)] = tokens[...]
    dys[pl.ds(row(0), local)] = out_grad[...]

    def column(line):
        same = lax.broadcasted_iota(jnp.int32, (own, own), 0) == lax.broadcasted_iota(jnp.int32, (own, own), 1)
        return jnp.sum(jnp.where(same, line, 0.0), 1, keepdims=True)

    def lay(target, begin, weight, gain):
        each = weight.shape[1] // ranks
        for rank in range(ranks):
            part = weight[:, rank * each : (rank + 1) * each]
            if gain is not None:
                part = (part.astype(jnp.float32) * gain).astype(LOW)
            target[rank, :, begin : begin + each] = part
        return begin + each

    gain = column(attn_gain[...])
    at = 0
    for weight in (w_query, w_key, w_value):
        at = lay(a_rows, at, weight, gain)
    whole[seq, pl.ds(pl.multiple_of(dp * own, own), own)] = w_output[...]
    answered(peers)
    ring = RingGather(held, local, ranks, sems[0], sems[1], right, left, row)
    ring.start(1)
    attn.start()
    outs = WholeGather(whole, ranks, own, [*sems[8:12], *sems[33:35]])
    outs.forward(0)
    line = LineGather(dys, local, ranks, sems[4], sems[5], sems[6], sems[7])
    stores = []

    def store(src, dst):
        stores.append(move(src, dst, local_sems.at[len(loads) + len(stores)]))

    def scale_rows(step):
        for rel in rels_of(step, ranks):

            def some(at, _):
                rows_at = pl.ds(pl.multiple_of(row(rel) + at * 32, 32), 32)
                normal[rows_at] = rows_scaled(held[rows_at].astype(jnp.float32))[0].astype(LOW)
                return 0

            lax.fori_loop(0, local // 32, some, 0)

    for load in loads:
        load.wait()
    gain = column(mlp_gain[...])
    each = gate.shape[1] // ranks
    lay(m_rows, 0, gate, gain)
    lay(m_rows, each, up, gain)
    lay(m_rows, 2 * each, down, None)
    scale_rows(0)
    def bring(step):
        outs.arrive(step)
        if step < half:
            outs.start(step + 1)
        outs.forward(step)

    def forward(piece):
        mlp[piece].arrive()
        mlp[piece].hop(0).start()
        mlp[piece].hop(1).start()

    def hop_over(piece):
        mlp[piece].hop(0).wait_recv()
        mlp[piece].hop(2).start()

    def pass_on(step):
        ring.advance(step)
        scale_rows(step)

    pass_on(1)
    line.start(1)
    pass_on(2)
    outs.start(1)
    attn.arrive()
    attn.hop(0).start()
    attn.hop(1).start()
    attn.hop(0).wait_recv()
    attn.hop(2).start()
    for step in range(3, half):
        pass_on(step)
    bring(1)
    pass_on(half)
    mlp[0].start()
    spans = order.shape[0]
    span = rows // spans
    for at in range(ranks):
        rows_at = pl.ds(at * local, local)
        ids = at * local + lax.broadcasted_iota(jnp.int32, (1, local), 1)
        where = jnp.zeros_like(ids)
        for slot in range(spans):
            inside = (ids >= slot * span) & (ids < (slot + 1) * span)
            where = where + jnp.where(inside, ids + (order[slot] - slot) * span, 0)
        begin = jnp.zeros_like(ids)
        for doc in range(starts.shape[1]):
            begin = jnp.maximum(begin, jnp.where(starts[0, doc] <= where, starts[0, doc], 0))
        pos_row[:, rows_at] = where
        across = jnp.broadcast_to(where, (local, local)).T
        pos[rows_at] = across[:, :1]
        begins[rows_at] = jnp.broadcast_to(begin, (local, local)).T[:, :1]
        angle = across[:, :1].astype(jnp.float32) * freqs[...]
        lane = lax.broadcasted_iota(jnp.int32, (local, size), 1)
        cosv[rows_at] = jnp.cos(angle)
        sine = jnp.sin(angle)
        sinv[rows_at] = jnp.where(lane < size // 2, -sine, sine)
    bring(2)
    line.advance(1)
    attn.hop(1).wait_recv()
    attn.hop(2).wait_recv()
    store(block, attn_block)

    def project(begin, count):
        rows_at = pl.ds(begin, count)
        kept[rows_at] = dot_nn(normal[rows_at], block[...].reshape(width, cols))

    store(normal, first_in)
    tile = rows // half

    def rotated(at, rows_at, gain):
        v = rows_scaled(kept[rows_at, at * size : (at + 1) * size])[0] * gain[...]
        return (v * cosv[rows_at] + turn(v) * sinv[rows_at]).astype(LOW)

    for piece in range(half):
        rows_at = pl.ds(piece * tile, tile)
        project(piece * tile, tile)
        for head in range(heads):
            q_low[head, rows_at] = rotated(head, rows_at, query_gain)
        for group in range(kv_heads):
            k_low[group, rows_at] = rotated(heads + group, rows_at, key_gain)
            at = (heads + kv_heads + group) * size
            v_low[group, rows_at] = kept[rows_at, at : at + size].astype(LOW)
    store(kept, qkv)
    forward(0)

    for piece in range(half):
        rows_at = pl.ds(piece * tile, tile)
        seen = (pos_row[...] <= pos[rows_at]) & (pos_row[...] >= begins[rows_at])
        for head in range(heads):
            raw = dot_nt(q_low[head, rows_at], k_low[head // share]) * scale
            raw = jnp.where(seen, raw, NEG)
            weight = jnp.exp(raw - jnp.max(raw, -1, keepdims=True))
            weight = (weight * (1.0 / jnp.sum(weight, -1, keepdims=True))).astype(LOW)
            probs[head, rows_at] = weight
            value = dot_nn(weight, v_low[head // share])
            out_low[rows_at, head * size : (head + 1) * size] = value.astype(LOW)
            store(probs.at[head, rows_at], prob.at[head, rows_at])
        if piece == 0:
            bring(3)
        if piece == 1:
            mlp[1].start()
            line.advance(2)
            bring(half)
    mlp[2].start()
    hop_over(0)
    forward(1)
    forward(2)
    place = ring_place(seq, ranks)

    def exchange(rel):
        to = ring_seq(lax.rem(place + rel, ranks), ranks)
        return push(
            out_low.at[pl.ds(row(rel), local)],
            own_out.at[:, pl.ds(pl.multiple_of(seq * o_cols, o_cols), o_cols)],
            out_send.at[rel],
            out_recv.at[rel],
            (to, dp),
        )

    for rel in range(1, ranks):
        exchange(rel).start()
    own_out[:, pl.ds(pl.multiple_of(seq * o_cols, o_cols), o_cols)] = out_low[pl.ds(row(0), local)]
    outs.complete()
    store(whole, out_all)
    hop_over(1)
    for step in range(3, half):
        line.advance(step)
    for rel in range(1, ranks):
        exchange(rel).wait_recv()

    def join(at, _):
        some = pl.ds(pl.multiple_of(at * deep, deep), deep)
        resid[:, some] = tokens[:, some].astype(jnp.float32) + dot_nt(own_out[...], whole[at])
        return 0

    lax.fori_loop(0, ranks, join, 0)

    def scale_second(at, _):
        rows_at = pl.ds(pl.multiple_of(at * 32, 32), 32)
        second[rows_at] = rows_scaled(resid[rows_at])[0].astype(LOW)
        return 0

    lax.fori_loop(0, local // 32, scale_second, 0)
    hop_over(2)
    line.complete()
    store(dys, dy_all)
    ring.finish()
    attn.finish()
    outs.finish()
    for rel in range(1, ranks):
        exchange(rel).wait_send()
    line.finish()
    for piece in mlp:
        piece.hop(1).wait_recv()
        piece.hop(2).wait_recv()
        piece.finish()
    for given in stores:
        given.wait()


def mlp_kernel(
    ranks, second, out_grad, rest, dys, mlp_block, block_out, dresid, dresid_low, own_grads,
    grads, from_core, from_y, held, weights, hidden, dgu, resid, dy_all,
    term, out_buf, in_buf, y_out, y_in, here, *sems,
):
    local, width = second.shape
    row = functools.partial(block_row, local=local, ranks=ranks)
    ff = hidden.shape[1]
    deep = weights.shape[1]
    half = ranks // 2
    right, left = neighbours(ranks)
    loads = [
        move(src, dst, here.at[at])
        for at, (src, dst) in enumerate(((mlp_block, weights), (dys, dy_all), (rest, resid)))
    ]
    seq, dp = lax.axis_index("seq"), lax.axis_index("dp")
    own = own_grads.shape[1]
    pieces = [
        Reduce(
            grads, from_core, from_y, own_grads, own, at * ranks // 4, ranks // 4, pl.ds(0, 3 * ff),
            sems[6 + 2 * at : 8 + 2 * at],
        )
        for at in range(4)
    ]
    peers = [right, left, (seq, pieces[0].beside), (seq, pieces[0].sibling)]
    knock(peers)
    held[pl.ds(row(0), local)] = second[...]
    answered(peers)
    ring = RingGather(held, local, ranks, sems[0], sems[1], right, left, row)
    ring.start(1)
    loads[0].wait()
    loads[1].wait()
    wide = 256

    def middle(step):
        rels = rels_of(step, ranks)

        def some(at, _):
            first = pl.multiple_of(at * wide, wide)
            given, dy = block_rows(held, rels, local, ranks), block_rows(dy_all, rels, local, ranks)
            gate = dot_nn(given, weights[:, :, pl.ds(first, wide)].reshape(width, wide))
            upper = dot_nn(given, weights[:, :, pl.ds(ff + first, wide)].reshape(width, wide))
            dmid = dot_nn(dy, weights[:, :, pl.ds(2 * ff + first, wide)].reshape(width, wide))
            sigma = 1.0 / (1.0 + jnp.exp(-gate))
            act = gate * sigma
            value = (act * upper).astype(LOW)
            dgate = (dmid * upper * (sigma * (1.0 + gate * (1.0 - sigma)))).astype(LOW)
            dupper = (dmid * act).astype(LOW)
            for at, rel in enumerate(rels):
                rows, some_rows = pl.ds(row(rel), local), slice(at * local, (at + 1) * local)
                hidden[rows, pl.ds(first, wide)] = value[some_rows]
                dgu[rows, pl.ds(first, wide)] = dgate[some_rows]
                dgu[rows, pl.ds(ff + first, wide)] = dupper[some_rows]
            return 0

        lax.fori_loop(0, ff // wide, some, 0)

    middle(0)
    for step in range(1, half + 1):
        ring.advance(step)
        middle(step)

    def back_part(rels, begin, end):
        def some(at, _):
            value = dot_nt(block_rows(dgu, rels, local, ranks), weights[at, :, : 2 * ff])
            term[: len(rels) * local, pl.ds(pl.multiple_of(at * deep, deep), deep)] = value
            return 0

        lax.fori_loop(begin, end, some, 0)

    def out_part(rels, begin, end):
        def some(at, _):
            value = dot_nt(block_rows(hidden, rels, local, ranks), weights[at, :, 2 * ff :])
            term[: len(rels) * local, pl.ds(pl.multiple_of(at * deep, deep), deep)] = value
            return 0

        lax.fori_loop(begin, end, some, 0)

    def weight_grads(first, count):
        def some(at, _):
            cols = pl.ds(pl.multiple_of(at * deep, deep), deep)
            grads[at, :, : 2 * ff] = dot_tn(held[:, cols], dgu[...]).astype(LOW)
            grads[at, :, 2 * ff :] = dot_tn(dy_all[:, cols], hidden[...]).astype(LOW)
            return 0

        lax.fori_loop(first, first + count, some, 0)

    back = RingSum(back_part, term, out_buf, in_buf, local, ranks, sems[2], sems[3], right, left)
    out = RingSum(out_part, term, y_out, y_in, local, ranks, sems[4], sems[5], right, left)
    for step in range(1, half + 1):
        back.compute(step)
        back.launch(step)
        out.compute(step)
        out.launch(step)
        made, passed, summed = (((0, 1), (2, 3), (), ()), ((), (0, 1), (2, 3), ()), ((), (), (0, 1), (2, 3)))
        for piece in (pieces[at] for at in made[step - 1]):
            weight_grads(piece.begin, piece.count)
            piece.first()
        for at in passed[step - 1]:
            pieces[at].second()
        for at in summed[step - 1]:
            pieces[at].third()
    back.compute(half + 1)
    loads[2].wait()
    back.arrive_last()

    def finish_back(at, _):
        begin = pl.multiple_of(at * 32, 32)
        rows = pl.ds(begin, 32)
        value = resid[rows]
        inv = rows_scaled(value)[1]
        grad = back.last(begin, 32)
        full = out_grad[rows].astype(jnp.float32) + rows_scaled_back(value, inv, grad)
        dresid[rows] = full
        dresid_low[rows] = full.astype(LOW)
        return 0

    lax.fori_loop(0, local // 32, finish_back, 0)
    out.compute(half + 1)
    out.arrive_last()

    def finish_out(at, _):
        begin = pl.multiple_of(at * 32, 32)
        rows = pl.ds(begin, 32)
        block_out[rows] = (resid[rows] + out.last(begin, 32)).astype(LOW)
        return 0

    lax.fori_loop(0, local // 32, finish_out, 0)
    ring.finish()
    back.finish()
    out.finish()
    for piece in pieces:
        piece.finish()


def back_kernel(
    ranks, kv_heads, tokens, dresid_low, query_gain, key_gain, own_out, first_in_in, block_in,
    qkv_in, cos_in, sin_in, q_in, k_in, v_in, prob_in, dresid_in, mlp_own, out_all,
    tokens_grad, gains, out_grad, mlp_sums, attn_sums,
    grads, from_core, from_y, own_grads, query_gain_grad, key_gain_grad,
    tile, tiles_in, tile_sum, tile_sums_in, dob, dout, dk, dv, dqkv,
    first_in, attn_block, qkv, cosv, sinv, q_low, k_low, v_low, prob, dresid, term, out_buf, in_buf,
    o_grads, o_core, o_y, o_own, o_term, o_out, o_in, *sems,
):
    local, width = tokens.shape
    rows = local * ranks
    half = ranks // 2
    size = cosv.shape[1]
    heads = q_low.shape[0]
    share = heads // kv_heads
    scale = 1.0 / math.sqrt(size)
    cols = (heads + 2 * kv_heads) * size
    deep = attn_block.shape[1]
    o_cols = heads * size
    right, left = neighbours(ranks)
    seq, dp = lax.axis_index("seq"), lax.axis_index("dp")
    own = mlp_own.shape[1]
    copies = lax.axis_size("dp")
    row = functools.partial(block_row, local=local, ranks=ranks)
    place = ring_place(seq, ranks)
    out_piece = Reduce(o_grads, o_core, o_y, o_own, own, 0, ranks, pl.ds(0, width), sems[4:6])
    qkv_piece = Reduce(grads, from_core, from_y, own_grads, own, 0, ranks, pl.ds(0, cols), sems[6:8])
    third = mlp_own.shape[2] // 3
    mlp_ways = [
        Deliver(mlp_own, mlp_sums, pl.ds(at * third, third), ranks, [*sems[8:11], *sems[22:28]][3 * at : 3 * at + 3])
        for at in range(3)
    ]
    dob_send, dob_recv = sems[0:2]
    qkv_way = Deliver(own_grads, attn_sums, pl.ds(0, cols), ranks, sems[14:17])
    peers = [(lax.rem(seq + step, ranks), dp) for step in range(1, ranks)]
    peers += [(seq, lax.rem(dp + step, copies)) for step in range(1, copies)]
    knock(peers)
    local_sems = sems[21]
    loads = {}
    for at, (name, src, dst) in enumerate(
        (
            ("out", out_all, o_grads), ("block", block_in, attn_block), ("v", v_in, v_low),
            ("prob", prob_in, prob), ("k", k_in, k_low), ("q", q_in, q_low), ("cos", cos_in, cosv),
            ("sin", sin_in, sinv), ("qkv", qkv_in, qkv), ("first", first_in_in, first_in),
            ("dresid", dresid_in, dresid),
        )
    ):
        loads[name] = move(src, dst, local_sems.at[at])
    answered(peers)
    loads["out"].wait()

    def columns_of(rank):
        return pl.ds(pl.multiple_of(rank * o_cols, o_cols), o_cols)

    def owner(rel):
        return ring_seq(lax.rem(place + rel, ranks), ranks)

    def exchange(rel):
        to = owner(rel)
        return push(
            dob.at[:, columns_of(to)], dout.at[pl.ds(row(0), local)], dob_send.at[rel], dob_recv.at[rel], (to, dp)
        )

    def project(rel):
        some = columns_of(owner(rel))
        dob[:, some] = dot_nn(dresid_low[...], o_grads[:, :, some].reshape(width, o_cols)).astype(LOW)

    for rel in (*ring_order(ranks)[1:][::-1], 0):
        project(rel)
        if rel:
            exchange(rel).start()
    dout[pl.ds(row(0), local)] = dob[:, columns_of(seq)]

    def out_grads(at, _):
        some_cols = pl.ds(pl.multiple_of(at * deep, deep), deep)
        o_grads[at] = dot_tn(dresid_low[:, some_cols], own_out[...]).astype(LOW)
        return 0

    lax.fori_loop(0, ranks, out_grads, 0)
    mlp_ways[0].start()
    out_piece.first()
    out_piece.second()
    for rel in range(1, ranks):
        exchange(rel).wait_recv()
    for name in ("v", "prob", "k", "q", "cos", "sin", "qkv"):
        loads[name].wait()
    mlp_ways[1].start()
    tall = rows // half
    query_gain_grad[...] = jnp.zeros_like(query_gain_grad)
    key_gain_grad[...] = jnp.zeros_like(key_gain_grad)

    def unrotated(grad, column, rows_at, gain, gain_grad_ref):
        grad = grad * cosv[rows_at] - turn(grad) * sinv[rows_at]
        value = qkv[rows_at, column * size : (column + 1) * size]
        normal, inv = rows_scaled(value)
        gain_grad_ref[...] += jnp.sum(grad * normal, 0, keepdims=True)
        back = rows_scaled_back(value, inv, grad * gain[...])
        dqkv[rows_at, column * size : (column + 1) * size] = back.astype(LOW)

    for head in range(heads):
        group = head // share

        def one(piece, _):
            rows_at = pl.ds(pl.multiple_of(piece * tall, tall), tall)
            weight = prob[head, rows_at]
            grad = dout[rows_at, head * size : (head + 1) * size]
            dprob = dot_nt(grad, v_low[group])
            full = weight.astype(jnp.float32)
            delta = jnp.sum(full * dprob, -1, keepdims=True)
            dscore = (full * (dprob - delta)).astype(LOW)
            dq = dot_nn(dscore, k_low[group]) * scale
            dk_add = dot_tn(dscore, q_low[head, rows_at]) * scale
            dv_add = dot_tn(weight, grad)
            dk[group] += dk_add
            dv[group] += dv_add
            unrotated(dq, head, rows_at, query_gain, query_gain_grad)
            return 0

        if head % share == 0:
            dk[group] = jnp.zeros_like(dk[group])
            dv[group] = jnp.zeros_like(dv[group])
        lax.fori_loop(0, half, one, 0)
        if head == 0:
            mlp_ways[2].start()
    for group in range(kv_heads):
        def one_key(piece, _):
            rows_at = pl.ds(pl.multiple_of(piece * tall, tall), tall)
            unrotated(dk[group, rows_at], heads + group, rows_at, key_gain, key_gain_grad)
            at = (heads + kv_heads + group) * size
            dqkv[rows_at, at : at + size] = dv[group, rows_at].astype(LOW)
            return 0

        lax.fori_loop(0, half, one_key, 0)

    def part(rels, begin, end):
        def some(at, _):
            value = dot_nt(block_rows(dqkv, rels, local, ranks), attn_block[at])
            term[: len(rels) * local, pl.ds(pl.multiple_of(at * deep, deep), deep)] = value
            return 0

        lax.fori_loop(begin, end, some, 0)

    def qkv_grads(at, _):
        some_cols = pl.ds(pl.multiple_of(at * deep, deep), deep)
        grads[at] = dot_tn(first_in[:, some_cols], dqkv[...]).astype(LOW)
        return 0

    def to_ranks(step):
        peer = lax.rem(seq + step, ranks)
        return push(tile, tiles_in.at[seq], sems[17].at[step], sems[18].at[step], (peer, dp))

    def to_copies(step):
        peer = lax.rem(dp + step, copies)
        return push(
            tile_sum, tile_sums_in.at[dp], sems[19].at[step], sems[20].at[step], (seq, peer)
        )

    tile[0:1] = query_gain_grad[...]
    tile[1:2] = key_gain_grad[...]
    tile[2:] = jnp.zeros((tile.shape[0] - 2, size), jnp.float32)
    for step in range(1, ranks):
        to_ranks(step).start()
    tiles_in[seq] = tile[...]
    loads["block"].wait()

    def out_part(rels, begin, end):
        for at, rel in enumerate(rels):
            o_term[at * own : (at + 1) * own] = o_own[owner(rel)].astype(jnp.float32)

    out_total = RingSum(out_part, o_term, o_out, o_in, own, ranks, sems[30], sems[31], right, left)
    totals = two_sums(part, term, out_buf, in_buf, local, ranks, [*sems[2:4], *sems[28:30]], right, left)
    for step in range(1, half + 1):
        for total in totals:
            total.compute(step)
            total.launch(step)
        if step == 1:
            loads["first"].wait()
            lax.fori_loop(0, ranks, qkv_grads, 0)
            qkv_piece.first()
            qkv_piece.second()
        if step == 2:
            out_piece.third()
            for other in range(1, ranks):
                to_ranks(other).wait_recv()
            tile_sum[...] = jnp.sum(tiles_in[...], 0)
            for other in range(1, copies):
                to_copies(other).start()
            tile_sums_in[dp] = tile_sum[...]
        if step == half - 1:
            for other in range(1, copies):
                to_copies(other).wait_recv()
            gains[...] = jnp.sum(tile_sums_in[...], 0)
        if step > 1:
            out_total.compute(step - 1)
            out_total.launch(step - 1)
    out_total.compute(half)
    out_total.launch(half)
    qkv_piece.third()
    qkv_way.start()
    for total in totals:
        total.compute(half + 1)
    loads["dresid"].wait()
    for total in totals:
        total.arrive_last()

    def last(at, _):
        begin = pl.multiple_of(at * 32, 32)
        rows_at = pl.ds(begin, 32)
        value = tokens[rows_at].astype(jnp.float32)
        inv = rows_scaled(value)[1]
        grad = jnp.concatenate([total.last(begin, 32) for total in totals], 1)
        tokens_grad[rows_at] = dresid[rows_at] + rows_scaled_back(value, inv, grad)
        return 0

    lax.fori_loop(0, local // 32, last, 0)
    out_total.compute(half + 1)
    out_total.arrive_last()
    out_grad[...] = out_total.last(0, own)
    for step in range(1, ranks):
        to_ranks(step).wait_send()
    for step in range(1, copies):
        to_copies(step).wait_send()
    out_total.finish()
    for rel in range(1, ranks):
        exchange(rel).wait_send()
    for total in totals:
        total.finish()
    out_piece.finish()
    qkv_piece.finish()
    for way in mlp_ways:
        way.finish()
    qkv_way.finish()


def leave_kernel(
    attn_sums, mlp_sums, gains, attn_gain, mlp_gain, w_query, w_key, w_value, w_gate, w_up,
    query_out, key_out, value_out, gate_out, up_out, down_out, attn_out, mlp_out,
    head_query_out, head_key_out,
):
    own = attn_gain.shape[1]
    same = lax.broadcasted_iota(jnp.int32, (own, own), 0) == lax.broadcasted_iota(jnp.int32, (own, own), 1)

    @pl.when(pl.program_id(0) == 0)
    def _():
        attn_out[...] = jnp.zeros_like(attn_out)
        mlp_out[...] = jnp.zeros_like(mlp_out)
        head_query_out[...] = gains[0:1]
        head_key_out[...] = gains[1:2]

    for sums, gain, gain_out, parts in (
        (attn_sums, attn_gain, attn_out, ((query_out, w_query), (key_out, w_key), (value_out, w_value))),
        (mlp_sums, mlp_gain, mlp_out, ((gate_out, w_gate), (up_out, w_up), (down_out, None))),
    ):
        scale = jnp.sum(jnp.where(same, gain[...], 0.0), 1, keepdims=True)
        for rank in range(sums.shape[0]):
            at = 0
            for out, weight in parts:
                each = out.shape[1] // sums.shape[0]
                cols = slice(rank * each, (rank + 1) * each)
                value = sums[rank, :, at : at + each].astype(jnp.float32)
                at += each
                if weight is None:
                    out[:, cols] = value
                    continue
                out[:, cols] = value * scale
                inner = jnp.sum(value * weight[:, cols].astype(jnp.float32), 1, keepdims=True)
                gain_out[...] += jnp.sum(jnp.where(same, inner, 0.0), 0, keepdims=True)


VM = pl.BlockSpec(memory_space=pltpu.VMEM)
SM = pl.BlockSpec(memory_space=pltpu.SMEM)
ANY = pl.BlockSpec(memory_space=pl.ANY)


def call(kernel, number, ins, outs, scratch, operands):
    return pl.pallas_call(
        kernel,
        out_shape=[jax.ShapeDtypeStruct(shape, dtype) for shape, dtype, _ in outs],
        in_specs=ins,
        out_specs=[spec for _, _, spec in outs],
        scratch_shapes=scratch,
        compiler_params=pltpu.CompilerParams(
            collective_id=number, has_side_effects=True, vmem_limit_bytes=LIMIT
        ),
    )(*operands)


def columns_body(
    tokens,
    out_grad,
    span_order,
    doc_starts,
    w_query,
    w_key,
    w_value,
    w_output,
    attn_gain,
    query_gain,
    key_gain,
    w_gate,
    w_up,
    w_down,
    mlp_gain,
):
    ranks = lax.axis_size("seq")
    copies = lax.axis_size("dp")
    _, local, width = tokens.shape
    rows = local * ranks
    size = query_gain.shape[0]
    kv_heads = w_key.shape[1] // size // ranks
    heads = w_query.shape[1] // size // ranks
    q_cols, kv_cols = heads * size, kv_heads * size
    qkv_cols = q_cols + 2 * kv_cols
    ff = w_gate.shape[1] // ranks
    own = width // (ranks * copies)
    deep = own * copies
    half = ranks // 2
    f32, i32 = jnp.float32, jnp.int32
    exponents = np.arange(size) % (size // 2) * (-2.0 / size * math.log(1000000.0))
    freqs = jnp.asarray(np.exp(exponents)[None], f32)
    q_gain, k_gain = query_gain[None], key_gain[None]
    (
        resid, second, cosv, sinv, q_low, k_low, v_low, own_out, first_in, qkv, attn_block, dy_all, prob, mlp_block,
        out_all,
    ) = call(
        functools.partial(first_kernel, ranks, kv_heads),
        1,
        [SM, SM] + [VM] * 11 + [ANY] * 3,
        [
            ((local, width), f32, VM),
            ((local, width), LOW, VM),
            ((rows, size), f32, VM),
            ((rows, size), f32, VM),
            ((heads, rows, size), LOW, VM),
            ((kv_heads, rows, size), LOW, VM),
            ((kv_heads, rows, size), LOW, VM),
            ((local, q_cols * ranks), LOW, VM),
            ((rows, width), LOW, ANY),
            ((rows, qkv_cols), f32, ANY),
            ((ranks, deep, qkv_cols), LOW, ANY),
            ((rows, width), LOW, ANY),
            ((heads, rows, rows), LOW, ANY),
            ((ranks, deep, 3 * ff), LOW, ANY),
            ((ranks, deep, q_cols * ranks), LOW, ANY),
        ],
        [
            pltpu.VMEM((rows, width), LOW),
            pltpu.VMEM((rows, width), LOW),
            pltpu.VMEM((rows, qkv_cols), f32),
            pltpu.VMEM((ranks, deep, qkv_cols), LOW),
            pltpu.VMEM((ranks, own, qkv_cols), LOW),
            pltpu.VMEM((ranks, own, 3 * ff), LOW),
        ]
        + [pltpu.VMEM((own, ff * ranks), LOW)] * 3
        + [
            pltpu.VMEM((rows, width), LOW),
            pltpu.VMEM((heads, rows, rows), LOW),
            pltpu.VMEM((rows, 1), i32),
            pltpu.VMEM((rows, 1), i32),
            pltpu.VMEM((1, rows), i32),
            pltpu.VMEM((rows, q_cols), LOW),
            pltpu.VMEM((ranks, deep, q_cols * ranks), LOW),
        ]
        + ring_sems(ranks)
        + [pltpu.SemaphoreType.DMA((ranks,))] * 2
        + line_sems(ranks)
        + whole_sems(ranks)[:4]
        + spread_sems(ranks) * 4
        + [pltpu.SemaphoreType.DMA((heads * half + 8,))]
        + whole_sems(ranks)[4:],
        (
            span_order, doc_starts, tokens[0], out_grad[0], freqs, attn_gain[None], mlp_gain[None], q_gain, k_gain,
            w_query, w_key, w_value, w_output, w_gate, w_up, w_down,
        ),
    )
    block_out, dresid, dresid_low, mlp_own = call(
        functools.partial(mlp_kernel, ranks),
        2,
        [VM, VM, ANY, ANY, ANY],
        [
            ((local, width), LOW, VM),
            ((local, width), f32, VM),
            ((local, width), LOW, VM),
            ((ranks, own, 3 * ff), LOW, VM),
        ],
        [pltpu.VMEM((ranks, deep, 3 * ff), LOW)]
        + reduce_bufs(ranks, own, 3 * ff)
        + [
            pltpu.VMEM((rows, width), LOW),
            pltpu.VMEM((ranks, deep, 3 * ff), LOW),
            pltpu.VMEM((rows, ff), LOW),
            pltpu.VMEM((rows, 2 * ff), LOW),
            pltpu.VMEM((local, width), f32),
            pltpu.VMEM((rows, width), LOW),
        ]
        + sum_bufs(local, ranks, width)
        + sum_bufs(local, ranks, width)[1:]
        + [pltpu.SemaphoreType.DMA((3,))]
        + ring_sems(ranks) * 3
        + reduce_sems() * 4,
        (second, out_grad[0], resid, dy_all, mlp_block),
    )
    tokens_grad, gains, wo_grad, mlp_sums, attn_sums = call(
        functools.partial(back_kernel, ranks, kv_heads),
        3,
        [VM] * 5 + [ANY] * 12,
        [
            ((local, width), f32, VM),
            ((8, size), f32, VM),
            ((own, q_cols * ranks), f32, VM),
            ((ranks, own, 3 * ff), LOW, ANY),
            ((ranks, own, qkv_cols), LOW, VM),
        ],
        [pltpu.VMEM((ranks, deep, qkv_cols), LOW)]
        + reduce_bufs(ranks, own, qkv_cols)
        + [
            pltpu.VMEM((ranks, own, qkv_cols), LOW),
            pltpu.VMEM((1, size), f32),
            pltpu.VMEM((1, size), f32),
            pltpu.VMEM((8, size), f32),
            pltpu.VMEM((ranks, 8, size), f32),
            pltpu.VMEM((8, size), f32),
            pltpu.VMEM((copies, 8, size), f32),
            pltpu.VMEM((local, q_cols * ranks), LOW),
            pltpu.VMEM((rows, q_cols), LOW),
            pltpu.VMEM((kv_heads, rows, size), f32),
            pltpu.VMEM((kv_heads, rows, size), f32),
            pltpu.VMEM((rows, qkv_cols), LOW),
            pltpu.VMEM((rows, width), LOW),
            pltpu.VMEM((ranks, deep, qkv_cols), LOW),
            pltpu.VMEM((rows, qkv_cols), f32),
            pltpu.VMEM((rows, size), f32),
            pltpu.VMEM((rows, size), f32),
            pltpu.VMEM((heads, rows, size), LOW),
            pltpu.VMEM((kv_heads, rows, size), LOW),
            pltpu.VMEM((kv_heads, rows, size), LOW),
            pltpu.VMEM((heads, rows, rows), LOW),
            pltpu.VMEM((local, width), f32),
        ]
        + sum_bufs(local, ranks, width)
        + [pltpu.VMEM((ranks, deep, q_cols * ranks), LOW)]
        + reduce_bufs(ranks, own, q_cols * ranks)
        + [pltpu.VMEM((ranks, own, q_cols * ranks), LOW)]
        + sum_bufs(own, ranks, q_cols * ranks)
        + [pltpu.SemaphoreType.DMA((ranks,))] * 2
        + ring_sems(ranks)
        + reduce_sems() * 2
        + deliver_sems(ranks) * 3
        + [pltpu.SemaphoreType.DMA((ranks,))] * 2
        + [pltpu.SemaphoreType.DMA((copies,))] * 2
        + [pltpu.SemaphoreType.DMA((11,))]
        + deliver_sems(ranks) * 2
        + ring_sems(ranks) * 2,
        (
            tokens[0], dresid_low, q_gain, k_gain, own_out, first_in, attn_block, qkv, cosv, sinv, q_low, k_low,
            v_low, prob, dresid, mlp_own, out_all,
        ),
    )
    whole = pl.BlockSpec((1, own), lambda at: (0, 0))
    each = (q_cols, kv_cols, kv_cols, ff, ff, ff)
    many = 2
    columns = [pl.BlockSpec((own, many * cols), lambda at: (0, at)) for cols in each]
    head = pl.BlockSpec((1, size), lambda at: (0, 0))
    *grads, dga, dgm, dgq, dgk = pl.pallas_call(
        leave_kernel,
        grid=(ranks // many,),
        out_shape=[jax.ShapeDtypeStruct((own, cols * ranks), f32) for cols in each]
        + [jax.ShapeDtypeStruct((1, own), f32)] * 2
        + [jax.ShapeDtypeStruct((1, size), f32)] * 2,
        in_specs=[
            pl.BlockSpec((many, own, qkv_cols), lambda at: (at, 0, 0)),
            pl.BlockSpec((many, own, 3 * ff), lambda at: (at, 0, 0)),
            pl.BlockSpec((8, size), lambda at: (0, 0)),
            whole,
            whole,
            *columns[:3],
            *columns[3:5],
        ],
        out_specs=columns + [whole, whole, head, head],
    )(attn_sums, mlp_sums, gains, attn_gain[None], mlp_gain[None], w_query, w_key, w_value, w_gate, w_up)
    return (
        block_out[None], tokens_grad[None], *grads[:3], wo_grad, dga[0], dgq[0], dgk[0], *grads[3:], dgm[0],
    )


def body(*args):
    tokens, w_key, query_gain = args[0], args[5], args[9]
    groups = w_key.shape[1] // query_gain.shape[0]
    ranks = lax.axis_size("seq")
    if tokens.shape[0] == 1 and ranks % 2 == 0 and groups % ranks == 0 and lax.axis_size("dp") == 4:
        return columns_body(*args)
    return gathered_body(*args)


def solution(mesh):
    return jax.shard_map(
        body,
        mesh=mesh,
        in_specs=(
            P("dp", "seq", None),
            P("dp", "seq", None),
            P(),
            P("dp", None),
            P(("seq", "dp"), None),
            P(("seq", "dp"), None),
            P(("seq", "dp"), None),
            P(("seq", "dp"), None),
            P(("seq", "dp")),
            P(),
            P(),
            P(("seq", "dp"), None),
            P(("seq", "dp"), None),
            P(("seq", "dp"), None),
            P(("seq", "dp")),
        ),
        out_specs=(
            P("dp", "seq", None),
            P("dp", "seq", None),
            P(("seq", "dp"), None),
            P(("seq", "dp"), None),
            P(("seq", "dp"), None),
            P(("seq", "dp"), None),
            P(("seq", "dp")),
            P(),
            P(),
            P(("seq", "dp"), None),
            P(("seq", "dp"), None),
            P(("seq", "dp"), None),
            P(("seq", "dp")),
        ),
        check_vma=False,
    )
```

```python
import functools
import math

import jax
import jax.numpy as jnp
import numpy as np
from jax import lax
from jax.experimental import pallas as pl
from jax.experimental.pallas import tpu as pltpu
from jax.sharding import PartitionSpec as P

EPS = 1e-06
NEG = -1e30


def normed(v, gain):
    scale_inv = lax.rsqrt(jnp.mean(v * v, -1, keepdims=True) + EPS)
    return (v * scale_inv * gain, scale_inv)


def norm_back(v, scale_inv, gain, grad):
    scaled = grad * gain
    inner = jnp.mean(scaled * v, -1, keepdims=True)
    dv = scale_inv * scaled - v * scale_inv * scale_inv * scale_inv * inner
    dgain = jnp.sum((grad * v * scale_inv).reshape(-1, v.shape[-1]), 0)
    return (dv, dgain)


def rotary(pos, width):
    half = width // 2
    freqs = jnp.exp(jnp.arange(half, dtype=jnp.float32) * (-2.0 / width * math.log(1000000.0)))
    angle = pos.astype(jnp.float32)[:, None] * freqs[None, :]
    return (jnp.cos(angle)[:, None, :], jnp.sin(angle)[:, None, :])


def rotate(v, cosv, sinv):
    half = v.shape[-1] // 2
    first, second = (v[..., :half], v[..., half:])
    return jnp.concatenate([first * cosv - second * sinv, second * cosv + first * sinv], -1)


def rotate_back(grad, cosv, sinv):
    half = grad.shape[-1] // 2
    first, second = (grad[..., :half], grad[..., half:])
    return jnp.concatenate([first * cosv + second * sinv, second * cosv - first * sinv], -1)


def place(order, begin, count, span):
    rows = begin + jnp.arange(count, dtype=jnp.int32)
    slots = rows // span
    picked = slots[:, None] == jnp.arange(order.shape[0], dtype=jnp.int32)[None, :]
    return jnp.sum(jnp.where(picked, order[None, :], 0), -1) * span + rows % span


def doc_of(starts, pos):
    return jnp.sum((starts[:, None, :] <= pos[None, :, None]).astype(jnp.int32), -1)


def gathered_body(
    tokens,
    out_grad,
    span_order,
    doc_starts,
    w_query,
    w_key,
    w_value,
    w_output,
    attn_gain,
    query_gain,
    key_gain,
    w_gate,
    w_up,
    w_down,
    mlp_gain,
):
    seqs, local, width = tokens.shape
    span = local // 2
    head_size = query_gain.shape[0]
    kv_heads = w_key.shape[1] // head_size
    heads = w_query.shape[1] // head_size
    share = heads // kv_heads
    kv_width = kv_heads * head_size
    ff_width = w_gate.shape[1]
    scale = 1.0 / math.sqrt(head_size)
    total_rows = seqs * local
    own_rows = width // lax.axis_size(("seq", "dp"))
    qpos = place(span_order, lax.axis_index("seq") * local, local, span)
    qdoc = doc_of(doc_starts, qpos)
    cosv, sinv = rotary(qpos, head_size)

    def gather_attn():
        return (
            lax.all_gather(w_query, ("seq", "dp"), axis=0, tiled=True),
            lax.all_gather(w_key, ("seq", "dp"), axis=0, tiled=True),
            lax.all_gather(w_value, ("seq", "dp"), axis=0, tiled=True),
            lax.all_gather(w_output, ("seq", "dp"), axis=0, tiled=True),
            lax.all_gather(
                attn_gain.astype(jnp.bfloat16), ("seq", "dp"), axis=0, tiled=True
            ).astype(attn_gain.dtype),
        )

    def gather_mlp():
        return (
            lax.all_gather(w_gate, ("seq", "dp"), axis=0, tiled=True),
            lax.all_gather(w_up, ("seq", "dp"), axis=0, tiled=True),
            lax.all_gather(w_down, ("seq", "dp"), axis=0, tiled=True),
            lax.all_gather(mlp_gain.astype(jnp.bfloat16), ("seq", "dp"), axis=0, tiled=True).astype(
                mlp_gain.dtype
            ),
        )

    x_rows = tokens.astype(jnp.float32).reshape(total_rows, width)
    wq_all, wk_all, wv_all, wo_all, ga_all = gather_attn()
    first_norm, first_inv = normed(x_rows, ga_all)
    first_in = first_norm.astype(jnp.bfloat16)
    q_raw = jnp.dot(first_in, wq_all, preferred_element_type=jnp.float32).reshape(
        seqs, local, heads, head_size
    )
    k_raw = jnp.dot(first_in, wk_all, preferred_element_type=jnp.float32).reshape(
        seqs, local, kv_heads, head_size
    )
    v_low = (
        jnp.dot(first_in, wv_all, preferred_element_type=jnp.float32)
        .astype(jnp.bfloat16)
        .reshape(seqs, local, kv_heads, head_size)
    )
    q_normed, q_inv = normed(q_raw, query_gain)
    k_normed, k_inv = normed(k_raw, key_gain)
    q_low = rotate(q_normed, cosv, sinv).astype(jnp.bfloat16)
    k_low = rotate(k_normed, cosv, sinv).astype(jnp.bfloat16)
    q_group = q_low.reshape(seqs, local, kv_heads, share, head_size)

    def scores(piece_key, start):
        count = piece_key.shape[1]
        kpos = place(span_order, start, count, span)
        kdoc = doc_of(doc_starts, kpos)
        visible = (qdoc[:, :, None] == kdoc[:, None, :]) & (
            kpos[None, None, :] <= qpos[None, :, None]
        )
        raw = (
            jnp.einsum("sqgjd,skgd->sgjqk", q_group, piece_key, preferred_element_type=jnp.float32)
            * scale
        )
        return (raw, visible[:, None, None])

    start_top = jnp.full((seqs, kv_heads, share, local), NEG, jnp.float32)
    piece = (
        lax.all_gather(k_low, "seq", axis=1, tiled=True),
        lax.all_gather(v_low, "seq", axis=1, tiled=True),
    )
    top = start_top
    raw, visible = scores(piece[0], jnp.int32(0))
    raw = jnp.where(visible, raw, NEG)
    new_top = jnp.maximum(top, jnp.max(raw, -1))
    weights = jnp.where(visible, jnp.exp(raw - new_top[..., None]), 0.0)
    total = jnp.sum(weights, -1)
    summed = jnp.einsum(
        "sgjqk,skgd->sgjqd",
        weights.astype(jnp.bfloat16),
        piece[1],
        preferred_element_type=jnp.float32,
    )
    top, total, summed = (new_top, total, summed)
    log_total = top + jnp.log(total)
    attn_vals = summed / total[..., None]
    out_low = (
        jnp.transpose(attn_vals, (0, 3, 1, 2, 4))
        .reshape(total_rows, heads * head_size)
        .astype(jnp.bfloat16)
    )
    resid = x_rows + jnp.einsum("nh,dh->nd", out_low, wo_all, preferred_element_type=jnp.float32)
    wg_all, wu_all, wd_all, gm_all = gather_mlp()
    second_norm, second_inv = normed(resid, gm_all)
    second_in = second_norm.astype(jnp.bfloat16)
    gate = jnp.dot(second_in, wg_all, preferred_element_type=jnp.float32)
    upper = jnp.dot(second_in, wu_all, preferred_element_type=jnp.float32)
    sigma = jax.nn.sigmoid(gate)
    act = gate * sigma
    hidden = (act * upper).astype(jnp.bfloat16)
    result = resid + jnp.einsum("nf,df->nd", hidden, wd_all, preferred_element_type=jnp.float32)
    block_out = result.astype(jnp.bfloat16).reshape(seqs, local, width)
    grad_low = out_grad.reshape(total_rows, width)
    wg_all, wu_all, wd_all, gm_all = gather_mlp()
    dmid = jnp.einsum("nd,df->nf", grad_low, wd_all, preferred_element_type=jnp.float32)
    dgate = (dmid * upper * sigma * (1.0 + gate * (1.0 - sigma))).astype(jnp.bfloat16)
    dupper = (dmid * act).astype(jnp.bfloat16)
    left = second_in
    outer = grad_low
    mlp_sums = lax.psum_scatter(
        jnp.concatenate(
            [
                jnp.einsum("nd,nf->df", left, dgate, preferred_element_type=jnp.float32),
                jnp.einsum("nd,nf->df", left, dupper, preferred_element_type=jnp.float32),
                jnp.einsum("nd,nf->df", outer, hidden, preferred_element_type=jnp.float32),
            ],
            1,
        ),
        ("seq", "dp"),
        scatter_dimension=0,
        tiled=True,
    )
    dsecond = jnp.einsum(
        "nf,df->nd", dgate, wg_all, preferred_element_type=jnp.float32
    ) + jnp.einsum("nf,df->nd", dupper, wu_all, preferred_element_type=jnp.float32)
    dresid_norm, dgm = norm_back(resid, second_inv, gm_all, dsecond)
    dresid = grad_low.astype(jnp.float32) + dresid_norm
    dresid_low = dresid.astype(jnp.bfloat16)
    wq_all, wk_all, wv_all, wo_all, ga_all = gather_attn()
    dout_low = jnp.einsum(
        "nd,dh->nh", dresid_low, wo_all, preferred_element_type=jnp.float32
    ).astype(jnp.bfloat16)
    dout_group = dout_low.reshape(seqs, local, kv_heads, share, head_size)
    delta = jnp.sum(jnp.transpose(dout_group.astype(jnp.float32), (0, 2, 3, 1, 4)) * attn_vals, -1)
    piece = (
        lax.all_gather(k_low, "seq", axis=1, tiled=True),
        lax.all_gather(v_low, "seq", axis=1, tiled=True),
    )
    count = piece[0].shape[1]
    raw, visible = scores(piece[0], jnp.int32(0))
    prob = jnp.where(visible, jnp.exp(raw - log_total[..., None]), 0.0)
    dprob = jnp.einsum(
        "sqgjd,skgd->sgjqk", dout_group, piece[1], preferred_element_type=jnp.float32
    )
    dscore = (prob * (dprob - delta[..., None])).astype(jnp.bfloat16)
    dq_sum = jnp.einsum("sgjqk,skgd->sqgjd", dscore, piece[0], preferred_element_type=jnp.float32)
    dk_part = (
        jnp.einsum("sgjqk,sqgjd->skgd", dscore, q_group, preferred_element_type=jnp.float32) * scale
    )
    dv_part = jnp.einsum(
        "sgjqk,sqgjd->skgd",
        prob.astype(jnp.bfloat16),
        dout_group,
        preferred_element_type=jnp.float32,
    )
    joined = jnp.concatenate(
        [dk_part.reshape(seqs, count, kv_width), dv_part.reshape(seqs, count, kv_width)], -1
    )
    buffer = joined
    dq_sum, buffer = (dq_sum, buffer)
    key_sums = lax.psum_scatter(
        buffer.astype(jnp.bfloat16), "seq", scatter_dimension=1, tiled=True
    ).astype(jnp.float32)
    dq_rot = (dq_sum * scale).reshape(seqs, local, heads, head_size)
    dq_raw, dgq = norm_back(q_raw, q_inv, query_gain, rotate_back(dq_rot, cosv, sinv))
    dk_rot = key_sums[..., :kv_width].reshape(seqs, local, kv_heads, head_size)
    dk_raw, dgk = norm_back(k_raw, k_inv, key_gain, rotate_back(dk_rot, cosv, sinv))
    dq_low = dq_raw.reshape(total_rows, heads * head_size).astype(jnp.bfloat16)
    dk_low = dk_raw.reshape(total_rows, kv_width).astype(jnp.bfloat16)
    dv_low = key_sums[..., kv_width:].reshape(total_rows, kv_width).astype(jnp.bfloat16)
    left = first_in
    outer = dresid_low
    attn_sums = lax.psum_scatter(
        jnp.concatenate(
            [
                jnp.einsum("nd,nh->dh", left, dq_low, preferred_element_type=jnp.float32),
                jnp.einsum("nd,nh->dh", left, dk_low, preferred_element_type=jnp.float32),
                jnp.einsum("nd,nh->dh", left, dv_low, preferred_element_type=jnp.float32),
                jnp.einsum("nd,nh->dh", outer, out_low, preferred_element_type=jnp.float32),
            ],
            1,
        ),
        ("seq", "dp"),
        scatter_dimension=0,
        tiled=True,
    )
    dfirst = jnp.einsum("nh,dh->nd", dq_low, wq_all, preferred_element_type=jnp.float32)
    dfirst = dfirst + jnp.einsum("nh,dh->nd", dk_low, wk_all, preferred_element_type=jnp.float32)
    dfirst = dfirst + jnp.einsum("nh,dh->nd", dv_low, wv_all, preferred_element_type=jnp.float32)
    dx_norm, dga = norm_back(x_rows, first_inv, ga_all, dfirst)
    tokens_grad = (dresid + dx_norm).reshape(seqs, local, width)
    dga_all, dgm_all, dgq_all, dgk_all = lax.psum((dga, dgm, dgq, dgk), ("seq", "dp"))
    offset = lax.axis_index(("seq", "dp")) * own_rows
    attn_gain_grad = lax.dynamic_slice_in_dim(dga_all, offset, own_rows, 0)
    mlp_gain_grad = lax.dynamic_slice_in_dim(dgm_all, offset, own_rows, 0)
    q_cols = heads * head_size
    w_query_grad = attn_sums[:, :q_cols]
    w_key_grad = attn_sums[:, q_cols : q_cols + kv_width]
    w_value_grad = attn_sums[:, q_cols + kv_width : q_cols + 2 * kv_width]
    w_output_grad = attn_sums[:, q_cols + 2 * kv_width :]
    w_gate_grad = mlp_sums[:, :ff_width]
    w_up_grad = mlp_sums[:, ff_width : 2 * ff_width]
    w_down_grad = mlp_sums[:, 2 * ff_width :]
    return (
        block_out,
        tokens_grad,
        w_query_grad,
        w_key_grad,
        w_value_grad,
        w_output_grad,
        attn_gain_grad,
        dgq_all,
        dgk_all,
        w_gate_grad,
        w_up_grad,
        w_down_grad,
        mlp_gain_grad,
    )


LOW = jnp.bfloat16
MESH = pl.DeviceIdType.MESH
LIMIT = 60 * 2**20


def ring_order(ranks):
    half = ranks // 2
    order = [0]
    for step in range(1, half):
        order += [step, ranks - step]
    return order + [half]


def ring_place(seq, ranks):
    z, x = lax.div(seq, 2), lax.rem(seq, 2)
    return z + x * (ranks - 1 - 2 * z)


def ring_seq(place, ranks):
    half = ranks // 2
    x, z = lax.div(place, half), lax.rem(place, half)
    return 2 * (z + x * (half - 1 - 2 * z)) + x


def neighbours(ranks):
    seq, dp = lax.axis_index("seq"), lax.axis_index("dp")
    at = ring_place(seq, ranks)
    right = ring_seq(lax.rem(at + 1, ranks), ranks)
    left = ring_seq(lax.rem(at + ranks - 1, ranks), ranks)
    return (right, dp), (left, dp)


def knock(devices):
    barrier = pltpu.get_barrier_semaphore()
    for device in devices:
        pl.semaphore_signal(barrier, inc=1, device_id=device, device_id_type=MESH)


def answered(devices):
    pl.semaphore_wait(pltpu.get_barrier_semaphore(), len(devices))


def move(src, dst, sem):
    copy = pltpu.make_async_copy(src, dst, sem)
    copy.start()
    return copy


def push(src, dst, send, recv, device):
    return pltpu.make_async_remote_copy(
        src_ref=src, dst_ref=dst, send_sem=send, recv_sem=recv, device_id=device, device_id_type=MESH
    )


def dot_nn(left, right):
    return jnp.dot(left, right, preferred_element_type=jnp.float32)


def dot_nt(left, right):
    return lax.dot_general(left, right, (((1,), (1,)), ((), ())), preferred_element_type=jnp.float32)


def dot_tn(left, right):
    return lax.dot_general(left, right, (((0,), (0,)), ((), ())), preferred_element_type=jnp.float32)


def block_row(rel, local, ranks):
    place = ring_place(lax.axis_index("seq"), ranks)
    return pl.multiple_of(ring_seq(lax.rem(place + rel, ranks), ranks) * local, local)


def block_rows(ref, rels, local, ranks):
    blocks = [ref[pl.ds(block_row(rel, local, ranks), local)] for rel in rels]
    return blocks[0] if len(blocks) == 1 else jnp.concatenate(blocks, 0)


def rels_of(step, ranks):
    return [rel for rel in ring_order(ranks) if min(rel, ranks - rel) == step]


class RingGather:
    def __init__(self, buf, local, ranks, send, recv, right, left, row):
        self.buf, self.sub, self.half = buf, local // 2, ranks // 2
        self.send, self.recv, self.right, self.left = send, recv, right, left
        self.ranks, self.row = ranks, row

    def copies(self, step, part):
        ways = ((0, (self.ranks - step + 1) % self.ranks, self.right), (1, step - 1, self.left))
        given = []
        for way, rel, device in ways:
            if step < self.half or way == part:
                block = self.buf.at[pl.ds(self.row(rel) + part * self.sub, self.sub)]
                at = 2 * (step - 1) + part
                given.append(push(block, block, self.send.at[way, at], self.recv.at[way, at], device))
        return given

    def start(self, step):
        for part in range(2):
            for copy in self.copies(step, part):
                copy.start()

    def advance(self, step):
        for part in range(2):
            for copy in self.copies(step, part):
                copy.wait_recv()
            if step < self.half:
                for copy in self.copies(step + 1, part):
                    copy.start()

    def finish(self):
        for step in range(1, self.half + 1):
            for part in range(2):
                for copy in self.copies(step, part):
                    copy.wait_send()


class LineGather:
    def __init__(self, buf, local, ranks, send, recv, x_send, x_recv):
        self.buf, self.local, self.length = buf, local, ranks // 2
        self.send, self.recv, self.x_send, self.x_recv = send, recv, x_send, x_recv
        self.seq, self.dp = lax.axis_index("seq"), lax.axis_index("dp")
        self.z, self.x = lax.div(self.seq, 2), lax.rem(self.seq, 2)

    def block(self, z):
        return self.buf.at[pl.ds(pl.multiple_of((2 * z + self.x) * self.local, self.local), self.local)]

    def hop(self, way, step):
        block = self.block(self.z + (step - 1 if way else 1 - step))
        to = self.seq + (-2 if way else 2)
        return push(block, block, self.send.at[way, step - 1], self.recv.at[way, step - 1], (to, self.dp))

    def sends(self, way, step):
        if way:
            return (self.z > 0) & (self.z + step <= self.length)
        return (self.z < self.length - 1) & (self.z >= step - 1)

    def comes(self, way, step):
        return self.z + step < self.length if way else self.z >= step

    def across(self, way, step):
        block = self.block(self.z + (step if way else -step))
        at = step + way * (self.length - 1)
        return push(
            block, block, self.x_send.at[at], self.x_recv.at[at], (self.seq + 1 - 2 * self.x, self.dp)
        )

    def from_x(self, way, step):
        z = self.z + (step if way else -step)
        row = pl.multiple_of((2 * z + 1 - self.x) * self.local, self.local)
        block = self.buf.at[pl.ds(row, self.local)]
        at = step + way * (self.length - 1)
        return push(
            block, block, self.x_send.at[at], self.x_recv.at[at], (self.seq + 1 - 2 * self.x, self.dp)
        )

    def start(self, step):
        for way in range(2):
            pl.when(self.sends(way, step))(lambda way=way: self.hop(way, step).start())
        self.pass_on(step - 1)

    def pass_on(self, step):
        if step == 0:
            self.across(0, 0).start()
            return
        for way in range(2):
            pl.when(self.comes(way, step))(lambda way=way: self.across(way, step).start())

    def arrive(self, step):
        for way in range(2):
            pl.when(self.comes(way, step))(lambda way=way: self.incoming(way, step).wait_recv())

    def incoming(self, way, step):
        block = self.block(self.z + (step if way else -step))
        to = self.seq + 1 - 2 * self.x
        return push(block, block, self.send.at[way, step - 1], self.recv.at[way, step - 1], (to, self.dp))

    def run(self):
        for step in range(1, self.length):
            self.advance(step)

    def advance(self, step):
        self.arrive(step)
        if step < self.length - 1:
            self.start(step + 1)
        else:
            self.pass_on(step)

    def complete(self):
        self.from_x(0, 0).wait_recv()
        for step in range(1, self.length):
            for way in range(2):
                pl.when(self.comes(way, step))(lambda way=way: self.from_x(way, step).wait_recv())

    def finish(self):
        self.across(0, 0).wait_send()
        for step in range(1, self.length):
            for way in range(2):
                pl.when(self.sends(way, step))(lambda way=way: self.hop(way, step).wait_send())
                pl.when(self.comes(way, step))(lambda way=way: self.across(way, step).wait_send())


def line_sems(ranks):
    half = ranks // 2
    return [pltpu.SemaphoreType.DMA((2, half))] * 2 + [pltpu.SemaphoreType.DMA((2 * half,))] * 2


class RingSum:
    def __init__(self, part, term, out_buf, in_buf, local, ranks, send, recv, right, left, stream=0, streams=1):
        self.part, self.term, self.out_buf, self.in_buf = part, term, out_buf, in_buf
        self.local, self.ranks, self.half = local, ranks, ranks // 2
        each = term.shape[1] // streams
        self.cols = pl.ds(stream * each, each)
        self.tiles = (stream * ranks // streams, (stream + 1) * ranks // streams)
        self.send, self.recv, self.right, self.left = send, recv, right, left

    def copies(self, step):
        rows = self.local // 2 if step == 1 else self.local
        skip = self.local // 2 if step == 1 else 0
        return [
            push(
                self.out_buf.at[way, (step - 1) % 2, pl.ds(begin, rows), self.cols],
                self.in_buf.at[way, step - 1, pl.ds(begin, rows), self.cols],
                self.send.at[way, step - 1],
                self.recv.at[way, step - 1],
                device,
            )
            for way, begin, device in ((0, 0, self.right), (1, skip, self.left))
        ]

    def compute(self, step):
        if step == 1:
            self.part([self.half], *self.tiles)
        elif step <= self.half:
            self.part(rels_of(self.half + 1 - step, self.ranks), *self.tiles)
        else:
            self.part([0], *self.tiles)

    def launch(self, step):
        local, skip = self.local, self.local // 2
        if step > 2:
            for copy in self.copies(step - 2):
                copy.wait_send()
        if step == 1:
            for way in range(2):
                rows = pl.ds(way * skip, skip)
                self.out_buf[way, 0, rows, self.cols] = self.term[rows, self.cols].astype(LOW)
        else:
            for copy in self.copies(step - 1):
                copy.wait_recv()
            for way in range(2):
                for begin, with_sum in ((0, step > 2 or way == 0), (skip, step > 2 or way == 1)):
                    value = self.term[pl.ds(way * local + begin, skip), self.cols]
                    if with_sum:
                        value = value + self.in_buf[way, step - 2, pl.ds(begin, skip), self.cols].astype(jnp.float32)
                    self.out_buf[way, (step - 1) % 2, pl.ds(begin, skip), self.cols] = value.astype(LOW)
        for copy in self.copies(step):
            copy.start()

    def last(self, begin, count):
        rows = pl.ds(begin, count)
        value = self.term[rows, self.cols] + self.in_buf[0, self.half - 1, rows, self.cols].astype(jnp.float32)
        return value + self.in_buf[1, self.half - 1, rows, self.cols].astype(jnp.float32)

    def arrive_last(self):
        for copy in self.copies(self.half):
            copy.wait_recv()

    def finish(self):
        for step in range(max(1, self.half - 1), self.half + 1):
            for copy in self.copies(step):
                copy.wait_send()


def two_sums(part, term, out_buf, in_buf, local, ranks, sems, right, left):
    return [
        RingSum(
            part, term, out_buf, in_buf, local, ranks, sems[2 * at], sems[2 * at + 1], right, left, at, 2
        )
        for at in range(2)
    ]


def ring_sems(ranks):
    return [pltpu.SemaphoreType.DMA((2, ranks)), pltpu.SemaphoreType.DMA((2, ranks))]


def sum_bufs(local, ranks, width):
    return [
        pltpu.VMEM((2 * local, width), jnp.float32),
        pltpu.VMEM((2, 2, local, width), LOW),
        pltpu.VMEM((2, ranks // 2, local, width), LOW),
    ]


def turn(v):
    return pltpu.roll(v, v.shape[-1] // 2, v.ndim - 1)


def rows_scaled(v):
    inv = lax.rsqrt(jnp.mean(v * v, -1, keepdims=True) + EPS)
    return v * inv, inv


def rows_scaled_back(v, inv, grad):
    return inv * grad - v * (inv * inv * inv * jnp.mean(grad * v, -1, keepdims=True))


class Spread:
    def __init__(self, rows, block, ranks, own, cols, sems):
        self.rows, self.block, self.ranks, self.own, self.cols = rows, block, ranks, own, cols
        self.send, self.recv, self.hop_send, self.hop_recv, self.here = sems
        self.seq, self.dp = lax.axis_index("seq"), lax.axis_index("dp")
        y, core = lax.div(self.dp, 2), lax.rem(self.dp, 2)
        self.beside, self.sibling = (1 - y) * 2 + core, y * 2 + 1 - core

    def at(self, dp):
        return pl.ds(pl.multiple_of(dp * self.own, self.own), self.own)

    def exchange(self):
        for step in range(1, self.ranks):
            peer = lax.rem(self.seq + step, self.ranks)
            yield push(
                self.rows.at[peer, :, self.cols],
                self.block.at[self.seq, self.at(self.dp), self.cols],
                self.send.at[step],
                self.recv.at[step],
                (peer, self.dp),
            )

    def keep(self):
        return pltpu.make_async_copy(
            self.rows.at[self.seq, :, self.cols],
            self.block.at[self.seq, self.at(self.dp), self.cols],
            self.here,
        )

    def hop(self, number):
        dp = self.beside if number == 2 else self.dp
        part = self.block.at[:, self.at(dp), self.cols]
        to = self.beside if number == 0 else self.sibling
        return push(part, part, self.hop_send.at[number], self.hop_recv.at[number], (self.seq, to))

    def start(self):
        self.keep().start()
        for copy in self.exchange():
            copy.start()

    def arrive(self):
        self.keep().wait()
        for copy in self.exchange():
            copy.wait_recv()

    def finish(self):
        for copy in self.exchange():
            copy.wait_send()
        for number in range(3):
            self.hop(number).wait_send()


def spread_sems(ranks):
    return [
        pltpu.SemaphoreType.DMA((ranks,)),
        pltpu.SemaphoreType.DMA((ranks,)),
        pltpu.SemaphoreType.DMA((3,)),
        pltpu.SemaphoreType.DMA((3,)),
        pltpu.SemaphoreType.DMA,
    ]


class WholeGather:
    def __init__(self, block, ranks, own, sems):
        self.block, self.ranks, self.half, self.own = block, ranks, ranks // 2, own
        self.send, self.recv, self.y_send, self.y_recv, self.core_send, self.core_recv = sems
        self.seq, self.dp = lax.axis_index("seq"), lax.axis_index("dp")
        self.right, self.left = neighbours(ranks)
        self.place = ring_place(self.seq, ranks)
        y, core = lax.div(self.dp, 2), lax.rem(self.dp, 2)
        self.beside, self.sibling = (1 - y) * 2 + core, y * 2 + 1 - core

    def at(self, rel, dp, begin, count):
        seq = ring_seq(lax.rem(self.place + rel + self.ranks, self.ranks), self.ranks)
        return self.block.at[seq, pl.ds(pl.multiple_of(dp * self.own + begin, count), count)]

    def copies(self, step):
        last = step == self.half
        rows = self.own // 2 if last else self.own
        skip = self.own // 2 if last else 0
        given = []
        for way, rel, begin, device in ((0, 1 - step, 0, self.right), (1, step - 1, skip, self.left)):
            part = self.at(rel, self.dp, begin, rows)
            given.append(push(part, part, self.send.at[way, step - 1], self.recv.at[way, step - 1], device))
        return given

    def start(self, step):
        for copy in self.copies(step):
            copy.start()

    def hops(self, step):
        for at, rel in enumerate(ring_order(self.ranks)):
            if min(rel, self.ranks - rel) == step:
                part = self.at(rel, self.dp, 0, self.own)
                yield push(part, part, self.y_send.at[at], self.y_recv.at[at], (self.seq, self.beside))
                yield push(part, part, self.core_send.at[at], self.core_recv.at[at], (self.seq, self.sibling))

    def arrive(self, step):
        for copy in self.copies(step):
            copy.wait_recv()

    def forward(self, step):
        for copy in self.hops(step):
            copy.start()

    def cross(self):
        part = self.block.at[:, pl.ds(pl.multiple_of(self.beside * self.own, self.own), self.own)]
        at = self.ranks
        return push(part, part, self.core_send.at[at], self.core_recv.at[at], (self.seq, self.sibling))

    def complete(self):
        for step in range(self.half + 1):
            for copy in self.hops(step):
                copy.wait_recv()
        self.cross().start()
        self.cross().wait_recv()

    def finish(self):
        for step in range(1, self.half + 1):
            for copy in self.copies(step):
                copy.wait_send()
        for step in range(self.half + 1):
            for copy in self.hops(step):
                copy.wait_send()
        self.cross().wait_send()


def whole_sems(ranks):
    return (
        ring_sems(ranks)
        + [pltpu.SemaphoreType.DMA((ranks,))] * 2
        + [pltpu.SemaphoreType.DMA((ranks + 1,))] * 2
    )


class Reduce:
    def __init__(self, grads, from_core, from_y, total, own, first, count, cols, sems):
        self.grads, self.from_core, self.from_y, self.total = grads, from_core, from_y, total
        self.own, self.begin, self.count, self.cols = own, first, count, cols
        self.send, self.recv = sems
        self.seq, dp = lax.axis_index("seq"), lax.axis_index("dp")
        self.y, self.core = lax.div(dp, 2), lax.rem(dp, 2)
        self.beside, self.sibling = (1 - self.y) * 2 + self.core, self.y * 2 + 1 - self.core

    def at(self, y, core):
        return pl.ds(pl.multiple_of((y * 2 + core) * self.own, self.own), self.own)

    def hop(self, number):
        some, cols = pl.ds(self.begin, self.count), self.cols
        if number == 2:
            src, dst, to = self.from_core.at[0, some, :, cols], self.from_y.at[some, :, cols], self.beside
        else:
            rows = self.at(1 - self.y if number == 0 else self.y, 1 - self.core)
            src, dst, to = self.grads.at[some, rows, cols], self.from_core.at[number, some, :, cols], self.sibling
        return push(src, dst, self.send.at[number], self.recv.at[number], (self.seq, to))

    def first(self):
        self.hop(0).start()
        self.hop(1).start()

    def second(self):
        self.hop(0).wait_recv()
        rows = self.at(1 - self.y, self.core)

        def some(at, _):
            value = self.grads[at, rows, self.cols].astype(jnp.float32)
            value = value + self.from_core[0, at, :, self.cols].astype(jnp.float32)
            self.from_core[0, at, :, self.cols] = value.astype(LOW)
            return 0

        lax.fori_loop(self.begin, self.begin + self.count, some, 0)
        self.hop(2).start()

    def third(self):
        self.hop(1).wait_recv()
        self.hop(2).wait_recv()
        rows = self.at(self.y, self.core)

        def some(at, _):
            value = self.grads[at, rows, self.cols].astype(jnp.float32)
            value = value + self.from_core[1, at, :, self.cols].astype(jnp.float32)
            value = value + self.from_y[at, :, self.cols].astype(jnp.float32)
            self.total[at, :, self.cols] = value.astype(LOW)
            return 0

        lax.fori_loop(self.begin, self.begin + self.count, some, 0)

    def finish(self):
        for number in range(3):
            self.hop(number).wait_send()


def reduce_sems():
    return [pltpu.SemaphoreType.DMA((3,)), pltpu.SemaphoreType.DMA((3,))]


def reduce_bufs(ranks, own, cols):
    return [pltpu.VMEM((2, ranks, own, cols), LOW), pltpu.VMEM((ranks, own, cols), LOW)]


class Deliver:
    def __init__(self, rows, out, cols, ranks, sems):
        self.rows, self.out, self.cols, self.ranks = rows, out, cols, ranks
        self.send, self.recv, self.here = sems
        self.seq, self.dp = lax.axis_index("seq"), lax.axis_index("dp")

    def exchange(self):
        for step in range(1, self.ranks):
            peer = lax.rem(self.seq + step, self.ranks)
            yield push(
                self.rows.at[peer, :, self.cols],
                self.out.at[self.seq, :, self.cols],
                self.send.at[step],
                self.recv.at[step],
                (peer, self.dp),
            )

    def keep(self):
        return pltpu.make_async_copy(
            self.rows.at[self.seq, :, self.cols], self.out.at[self.seq, :, self.cols], self.here
        )

    def start(self):
        self.keep().start()
        for copy in self.exchange():
            copy.start()

    def finish(self):
        self.keep().wait()
        for copy in self.exchange():
            copy.wait_recv()
        for copy in self.exchange():
            copy.wait_send()


def deliver_sems(ranks):
    return [pltpu.SemaphoreType.DMA((ranks,)), pltpu.SemaphoreType.DMA((ranks,)), pltpu.SemaphoreType.DMA]


def first_kernel(
    ranks, kv_heads, order, starts, tokens, out_grad, freqs, attn_gain, mlp_gain, query_gain, key_gain,
    w_query, w_key, w_value, w_output, w_gate, w_up, w_down,
    resid, second, cosv, sinv, q_low, k_low, v_low, own_out, first_in, qkv, attn_block, dy_all, prob, mlp_block, out_all,
    held, normal, kept, block, a_rows, m_rows, gate, up, down, dys, probs, pos, begins, pos_row,
    out_low, whole, *sems,
):
    local, width = tokens.shape
    rows = local * ranks
    own = w_query.shape[0]
    size = freqs.shape[1]
    heads = q_low.shape[0]
    share = heads // kv_heads
    half = ranks // 2
    scale = 1.0 / math.sqrt(size)
    cols = (heads + 2 * kv_heads) * size
    deep = block.shape[1]
    row = functools.partial(block_row, local=local, ranks=ranks)
    seq, dp = lax.axis_index("seq"), lax.axis_index("dp")
    right, left = neighbours(ranks)
    attn = Spread(a_rows, block, ranks, own, pl.ds(0, a_rows.shape[2]), sems[12:17])
    third = m_rows.shape[2] // 3
    mlp = [
        Spread(m_rows, mlp_block, ranks, own, pl.ds(at * third, third), sems[17 + 5 * at : 22 + 5 * at])
        for at in range(3)
    ]
    local_sems = sems[32]
    out_send, out_recv = sems[2:4]
    o_cols = heads * size
    peers = [(lax.rem(seq + step, ranks), dp) for step in range(1, ranks)]
    peers += [(seq, attn.beside), (seq, attn.sibling)]
    knock(peers)
    loads = [
        move(src, dst, local_sems.at[at])
        for at, (src, dst) in enumerate(((w_gate, gate), (w_up, up), (w_down, down)))
    ]
    held[pl.ds(row(0), local)] = tokens[...]
    dys[pl.ds(row(0), local)] = out_grad[...]

    def column(line):
        same = lax.broadcasted_iota(jnp.int32, (own, own), 0) == lax.broadcasted_iota(jnp.int32, (own, own), 1)
        return jnp.sum(jnp.where(same, line, 0.0), 1, keepdims=True)

    def lay(target, begin, weight, gain):
        each = weight.shape[1] // ranks
        for rank in range(ranks):
            part = weight[:, rank * each : (rank + 1) * each]
            if gain is not None:
                part = (part.astype(jnp.float32) * gain).astype(LOW)
            target[rank, :, begin : begin + each] = part
        return begin + each

    gain = column(attn_gain[...])
    at = 0
    for weight in (w_query, w_key, w_value):
        at = lay(a_rows, at, weight, gain)
    whole[seq, pl.ds(pl.multiple_of(dp * own, own), own)] = w_output[...]
    answered(peers)
    ring = RingGather(held, local, ranks, sems[0], sems[1], right, left, row)
    ring.start(1)
    attn.start()
    outs = WholeGather(whole, ranks, own, [*sems[8:12], *sems[33:35]])
    outs.forward(0)
    line = LineGather(dys, local, ranks, sems[4], sems[5], sems[6], sems[7])
    stores = []

    def store(src, dst):
        stores.append(move(src, dst, local_sems.at[len(loads) + len(stores)]))

    def scale_rows(step):
        for rel in rels_of(step, ranks):

            def some(at, _):
                rows_at = pl.ds(pl.multiple_of(row(rel) + at * 32, 32), 32)
                normal[rows_at] = rows_scaled(held[rows_at].astype(jnp.float32))[0].astype(LOW)
                return 0

            lax.fori_loop(0, local // 32, some, 0)

    for load in loads:
        load.wait()
    gain = column(mlp_gain[...])
    each = gate.shape[1] // ranks
    lay(m_rows, 0, gate, gain)
    lay(m_rows, each, up, gain)
    lay(m_rows, 2 * each, down, None)
    scale_rows(0)
    def bring(step):
        outs.arrive(step)
        if step < half:
            outs.start(step + 1)
        outs.forward(step)

    def forward(piece):
        mlp[piece].arrive()
        mlp[piece].hop(0).start()
        mlp[piece].hop(1).start()

    def hop_over(piece):
        mlp[piece].hop(0).wait_recv()
        mlp[piece].hop(2).start()

    def pass_on(step):
        ring.advance(step)
        scale_rows(step)

    attn.arrive()
    attn.hop(0).start()
    attn.hop(1).start()
    outs.start(1)
    pass_on(1)
    line.start(1)
    pass_on(2)
    spans = order.shape[0]
    span = rows // spans
    for at in range(ranks):
        rows_at = pl.ds(at * local, local)
        ids = at * local + lax.broadcasted_iota(jnp.int32, (1, local), 1)
        where = jnp.zeros_like(ids)
        for slot in range(spans):
            inside = (ids >= slot * span) & (ids < (slot + 1) * span)
            where = where + jnp.where(inside, ids + (order[slot] - slot) * span, 0)
        begin = jnp.zeros_like(ids)
        for doc in range(starts.shape[1]):
            begin = jnp.maximum(begin, jnp.where(starts[0, doc] <= where, starts[0, doc], 0))
        pos_row[:, rows_at] = where
        across = jnp.broadcast_to(where, (local, local)).T
        pos[rows_at] = across[:, :1]
        begins[rows_at] = jnp.broadcast_to(begin, (local, local)).T[:, :1]
        angle = across[:, :1].astype(jnp.float32) * freqs[...]
        lane = lax.broadcasted_iota(jnp.int32, (local, size), 1)
        cosv[rows_at] = jnp.cos(angle)
        sine = jnp.sin(angle)
        sinv[rows_at] = jnp.where(lane < size // 2, -sine, sine)
    bring(1)
    for step in range(3, half):
        pass_on(step)
    bring(2)
    attn.hop(0).wait_recv()
    attn.hop(2).start()
    attn.hop(1).wait_recv()
    attn.hop(2).wait_recv()
    store(block, attn_block)
    pass_on(half)
    line.advance(1)
    mlp[0].start()

    def project(begin, count):
        rows_at = pl.ds(begin, count)
        kept[rows_at] = dot_nn(normal[rows_at], block[...].reshape(width, cols))

    store(normal, first_in)
    tile = rows // half

    def rotated(at, rows_at, gain):
        v = rows_scaled(kept[rows_at, at * size : (at + 1) * size])[0] * gain[...]
        return (v * cosv[rows_at] + turn(v) * sinv[rows_at]).astype(LOW)

    for piece in range(half):
        rows_at = pl.ds(piece * tile, tile)
        project(piece * tile, tile)
        for head in range(heads):
            q_low[head, rows_at] = rotated(head, rows_at, query_gain)
        for group in range(kv_heads):
            k_low[group, rows_at] = rotated(heads + group, rows_at, key_gain)
            at = (heads + kv_heads + group) * size
            v_low[group, rows_at] = kept[rows_at, at : at + size].astype(LOW)
    store(kept, qkv)

    done = 0
    for piece in range(half):
        rows_at = pl.ds(piece * tile, tile)
        seen = (pos_row[...] <= pos[rows_at]) & (pos_row[...] >= begins[rows_at])
        for head in range(heads):
            raw = dot_nt(q_low[head, rows_at], k_low[head // share]) * scale
            raw = jnp.where(seen, raw, NEG)
            weight = jnp.exp(raw - jnp.max(raw, -1, keepdims=True))
            weight = (weight * (1.0 / jnp.sum(weight, -1, keepdims=True))).astype(LOW)
            probs[head, rows_at] = weight
            value = dot_nn(weight, v_low[head // share])
            out_low[rows_at, head * size : (head + 1) * size] = value.astype(LOW)
            store(probs.at[head, rows_at], prob.at[head, rows_at])
            done += 1
            if done == 1:
                forward(0)
                line.advance(2)
                bring(3)
            if done == 2:
                mlp[1].start()
            if done == 5:
                bring(half)
            if done == 6:
                mlp[2].start()
                forward(1)
    outs.complete()
    store(whole, out_all)
    place = ring_place(seq, ranks)

    def exchange(rel):
        to = ring_seq(lax.rem(place + rel, ranks), ranks)
        return push(
            out_low.at[pl.ds(row(rel), local)],
            own_out.at[:, pl.ds(pl.multiple_of(seq * o_cols, o_cols), o_cols)],
            out_send.at[rel],
            out_recv.at[rel],
            (to, dp),
        )

    for rel in range(1, ranks):
        exchange(rel).start()
    own_out[:, pl.ds(pl.multiple_of(seq * o_cols, o_cols), o_cols)] = out_low[pl.ds(row(0), local)]
    hop_over(1)
    forward(2)
    for step in range(3, half):
        line.advance(step)

    def columns_of(rel):
        return pl.ds(pl.multiple_of(ring_seq(lax.rem(place + rel, ranks), ranks) * o_cols, o_cols), o_cols)

    def join(rels):
        def some(at, _):
            tile_cols = pl.ds(pl.multiple_of(at * deep, deep), deep)
            parts = jnp.concatenate([own_out[:, columns_of(rel)] for rel in rels], 1)
            weights = jnp.concatenate([whole[at, :, columns_of(rel)] for rel in rels], 1)
            before = tokens[:, tile_cols].astype(jnp.float32) if 0 in rels else resid[:, tile_cols]
            resid[:, tile_cols] = before + dot_nt(parts, weights)
            return 0

        lax.fori_loop(0, ranks, some, 0)

    near = ring_order(ranks)
    for at in range(0, ranks, 2):
        for rel in near[at : at + 2]:
            if rel:
                exchange(ranks - rel).wait_recv()
        join(near[at : at + 2])

    def scale_second(at, _):
        rows_at = pl.ds(pl.multiple_of(at * 32, 32), 32)
        second[rows_at] = rows_scaled(resid[rows_at])[0].astype(LOW)
        return 0

    lax.fori_loop(0, local // 32, scale_second, 0)
    hop_over(0)
    hop_over(2)
    line.complete()
    store(dys, dy_all)
    ring.finish()
    attn.finish()
    outs.finish()
    for rel in range(1, ranks):
        exchange(rel).wait_send()
    line.finish()
    for piece in mlp:
        piece.hop(1).wait_recv()
        piece.hop(2).wait_recv()
        piece.finish()
    for given in stores:
        given.wait()


def mlp_kernel(
    ranks, second, out_grad, rest, dys, mlp_block, block_out, dresid, dresid_low, own_grads,
    grads, from_core, from_y, held, weights, hidden, dgu, resid, dy_all,
    term, out_buf, in_buf, y_out, y_in, here, *sems,
):
    local, width = second.shape
    row = functools.partial(block_row, local=local, ranks=ranks)
    ff = hidden.shape[1]
    deep = weights.shape[1]
    half = ranks // 2
    right, left = neighbours(ranks)
    loads = [
        move(src, dst, here.at[at])
        for at, (src, dst) in enumerate(((mlp_block, weights), (dys, dy_all), (rest, resid)))
    ]
    seq, dp = lax.axis_index("seq"), lax.axis_index("dp")
    own = own_grads.shape[1]
    pieces = [
        Reduce(
            grads, from_core, from_y, own_grads, own, at * ranks // 4, ranks // 4, pl.ds(0, 3 * ff),
            sems[6 + 2 * at : 8 + 2 * at],
        )
        for at in range(4)
    ]
    peers = [right, left, (seq, pieces[0].beside), (seq, pieces[0].sibling)]
    knock(peers)
    held[pl.ds(row(0), local)] = second[...]
    answered(peers)
    ring = RingGather(held, local, ranks, sems[0], sems[1], right, left, row)
    ring.start(1)
    loads[0].wait()
    loads[1].wait()
    wide = 256

    def middle(step):
        rels = rels_of(step, ranks)

        def some(at, _):
            first = pl.multiple_of(at * wide, wide)
            given, dy = block_rows(held, rels, local, ranks), block_rows(dy_all, rels, local, ranks)
            gate = dot_nn(given, weights[:, :, pl.ds(first, wide)].reshape(width, wide))
            upper = dot_nn(given, weights[:, :, pl.ds(ff + first, wide)].reshape(width, wide))
            dmid = dot_nn(dy, weights[:, :, pl.ds(2 * ff + first, wide)].reshape(width, wide))
            sigma = 1.0 / (1.0 + jnp.exp(-gate))
            act = gate * sigma
            value = (act * upper).astype(LOW)
            dgate = (dmid * upper * (sigma * (1.0 + gate * (1.0 - sigma)))).astype(LOW)
            dupper = (dmid * act).astype(LOW)
            for at, rel in enumerate(rels):
                rows, some_rows = pl.ds(row(rel), local), slice(at * local, (at + 1) * local)
                hidden[rows, pl.ds(first, wide)] = value[some_rows]
                dgu[rows, pl.ds(first, wide)] = dgate[some_rows]
                dgu[rows, pl.ds(ff + first, wide)] = dupper[some_rows]
            return 0

        lax.fori_loop(0, ff // wide, some, 0)

    middle(0)
    for step in range(1, half + 1):
        ring.advance(step)
        middle(step)

    def back_part(rels, begin, end):
        def some(at, _):
            value = dot_nt(block_rows(dgu, rels, local, ranks), weights[at, :, : 2 * ff])
            term[: len(rels) * local, pl.ds(pl.multiple_of(at * deep, deep), deep)] = value
            return 0

        lax.fori_loop(begin, end, some, 0)

    def out_part(rels, begin, end):
        def some(at, _):
            value = dot_nt(block_rows(hidden, rels, local, ranks), weights[at, :, 2 * ff :])
            term[: len(rels) * local, pl.ds(pl.multiple_of(at * deep, deep), deep)] = value
            return 0

        lax.fori_loop(begin, end, some, 0)

    def weight_grads(first, count):
        def some(at, _):
            cols = pl.ds(pl.multiple_of(at * deep, deep), deep)
            grads[at, :, : 2 * ff] = dot_tn(held[:, cols], dgu[...]).astype(LOW)
            grads[at, :, 2 * ff :] = dot_tn(dy_all[:, cols], hidden[...]).astype(LOW)
            return 0

        lax.fori_loop(first, first + count, some, 0)

    back = RingSum(back_part, term, out_buf, in_buf, local, ranks, sems[2], sems[3], right, left)
    out = RingSum(out_part, term, y_out, y_in, local, ranks, sems[4], sems[5], right, left)
    for step in range(1, half + 1):
        back.compute(step)
        back.launch(step)
        out.compute(step)
        out.launch(step)
        made, passed, summed = (((0, 1), (2, 3), (), ()), ((), (0, 1), (2, 3), ()), ((), (), (0, 1), (2, 3)))
        for piece in (pieces[at] for at in made[step - 1]):
            weight_grads(piece.begin, piece.count)
            piece.first()
        for at in passed[step - 1]:
            pieces[at].second()
        for at in summed[step - 1]:
            pieces[at].third()
    back.compute(half + 1)
    loads[2].wait()
    back.arrive_last()

    def finish_back(at, _):
        begin = pl.multiple_of(at * 32, 32)
        rows = pl.ds(begin, 32)
        value = resid[rows]
        inv = rows_scaled(value)[1]
        grad = back.last(begin, 32)
        full = out_grad[rows].astype(jnp.float32) + rows_scaled_back(value, inv, grad)
        dresid[rows] = full
        dresid_low[rows] = full.astype(LOW)
        return 0

    lax.fori_loop(0, local // 32, finish_back, 0)
    out.compute(half + 1)
    out.arrive_last()

    def finish_out(at, _):
        begin = pl.multiple_of(at * 32, 32)
        rows = pl.ds(begin, 32)
        block_out[rows] = (resid[rows] + out.last(begin, 32)).astype(LOW)
        return 0

    lax.fori_loop(0, local // 32, finish_out, 0)
    ring.finish()
    back.finish()
    out.finish()
    for piece in pieces:
        piece.finish()


def back_kernel(
    ranks, kv_heads, tokens, dresid_low, query_gain, key_gain, own_out, first_in_in, block_in,
    qkv_in, cos_in, sin_in, q_in, k_in, v_in, prob_in, dresid_in, mlp_own, out_all,
    tokens_grad, gains, out_grad, mlp_sums, attn_sums,
    grads, from_core, from_y, own_grads, query_gain_grad, key_gain_grad,
    tile, tiles_in, tile_sum, tile_sums_in, dob, dout, dk, dv, dqkv,
    first_in, attn_block, qkv, cosv, sinv, q_low, k_low, v_low, prob, dresid, term, out_buf, in_buf,
    o_grads, o_core, o_y, o_own, o_term, o_out, o_in, *sems,
):
    local, width = tokens.shape
    rows = local * ranks
    half = ranks // 2
    size = cosv.shape[1]
    heads = q_low.shape[0]
    share = heads // kv_heads
    scale = 1.0 / math.sqrt(size)
    cols = (heads + 2 * kv_heads) * size
    deep = attn_block.shape[1]
    o_cols = heads * size
    right, left = neighbours(ranks)
    seq, dp = lax.axis_index("seq"), lax.axis_index("dp")
    own = mlp_own.shape[1]
    copies = lax.axis_size("dp")
    row = functools.partial(block_row, local=local, ranks=ranks)
    place = ring_place(seq, ranks)
    out_piece = Reduce(o_grads, o_core, o_y, o_own, own, 0, ranks, pl.ds(0, width), sems[4:6])
    qkv_piece = Reduce(grads, from_core, from_y, own_grads, own, 0, ranks, pl.ds(0, cols), sems[6:8])
    third = mlp_own.shape[2] // 3
    mlp_ways = [
        Deliver(mlp_own, mlp_sums, pl.ds(at * third, third), ranks, [*sems[8:11], *sems[22:28]][3 * at : 3 * at + 3])
        for at in range(3)
    ]
    dob_send, dob_recv = sems[0:2]
    qkv_way = Deliver(own_grads, attn_sums, pl.ds(0, cols), ranks, sems[14:17])
    peers = [(lax.rem(seq + step, ranks), dp) for step in range(1, ranks)]
    peers += [(seq, lax.rem(dp + step, copies)) for step in range(1, copies)]
    knock(peers)
    local_sems = sems[21]
    loads = {}
    for at, (name, src, dst) in enumerate(
        (
            ("out", out_all, o_grads), ("block", block_in, attn_block), ("v", v_in, v_low),
            ("prob", prob_in, prob), ("k", k_in, k_low), ("q", q_in, q_low), ("cos", cos_in, cosv),
            ("sin", sin_in, sinv), ("qkv", qkv_in, qkv), ("first", first_in_in, first_in),
            ("dresid", dresid_in, dresid),
        )
    ):
        loads[name] = move(src, dst, local_sems.at[at])
    answered(peers)
    loads["out"].wait()

    def columns_of(rank):
        return pl.ds(pl.multiple_of(rank * o_cols, o_cols), o_cols)

    def owner(rel):
        return ring_seq(lax.rem(place + rel, ranks), ranks)

    def exchange(rel):
        to = owner(rel)
        return push(
            dob.at[:, columns_of(to)], dout.at[pl.ds(row(0), local)], dob_send.at[rel], dob_recv.at[rel], (to, dp)
        )

    def project(rel):
        some = columns_of(owner(rel))
        dob[:, some] = dot_nn(dresid_low[...], o_grads[:, :, some].reshape(width, o_cols)).astype(LOW)

    for rel in (*ring_order(ranks)[1:][::-1], 0):
        project(rel)
        if rel:
            exchange(rel).start()
    dout[pl.ds(row(0), local)] = dob[:, columns_of(seq)]

    def out_grads(at, _):
        some_cols = pl.ds(pl.multiple_of(at * deep, deep), deep)
        o_grads[at] = dot_tn(dresid_low[:, some_cols], own_out[...]).astype(LOW)
        return 0

    lax.fori_loop(0, ranks, out_grads, 0)
    mlp_ways[0].start()
    out_piece.first()
    out_piece.second()
    for rel in range(1, ranks):
        exchange(rel).wait_recv()
    for name in ("v", "prob", "k", "q", "cos", "sin", "qkv"):
        loads[name].wait()
    mlp_ways[1].start()
    tall = rows // half
    query_gain_grad[...] = jnp.zeros_like(query_gain_grad)
    key_gain_grad[...] = jnp.zeros_like(key_gain_grad)

    def unrotated(grad, column, rows_at, gain, gain_grad_ref):
        grad = grad * cosv[rows_at] - turn(grad) * sinv[rows_at]
        value = qkv[rows_at, column * size : (column + 1) * size]
        normal, inv = rows_scaled(value)
        gain_grad_ref[...] += jnp.sum(grad * normal, 0, keepdims=True)
        back = rows_scaled_back(value, inv, grad * gain[...])
        dqkv[rows_at, column * size : (column + 1) * size] = back.astype(LOW)

    for head in range(heads):
        group = head // share

        def one(piece, _):
            rows_at = pl.ds(pl.multiple_of(piece * tall, tall), tall)
            weight = prob[head, rows_at]
            grad = dout[rows_at, head * size : (head + 1) * size]
            dprob = dot_nt(grad, v_low[group])
            full = weight.astype(jnp.float32)
            delta = jnp.sum(full * dprob, -1, keepdims=True)
            dscore = (full * (dprob - delta)).astype(LOW)
            dq = dot_nn(dscore, k_low[group]) * scale
            dk_add = dot_tn(dscore, q_low[head, rows_at]) * scale
            dv_add = dot_tn(weight, grad)
            dk[group] += dk_add
            dv[group] += dv_add
            unrotated(dq, head, rows_at, query_gain, query_gain_grad)
            return 0

        if head % share == 0:
            dk[group] = jnp.zeros_like(dk[group])
            dv[group] = jnp.zeros_like(dv[group])
        lax.fori_loop(0, half, one, 0)
        if head == 0:
            mlp_ways[2].start()
    for group in range(kv_heads):
        def one_key(piece, _):
            rows_at = pl.ds(pl.multiple_of(piece * tall, tall), tall)
            unrotated(dk[group, rows_at], heads + group, rows_at, key_gain, key_gain_grad)
            at = (heads + kv_heads + group) * size
            dqkv[rows_at, at : at + size] = dv[group, rows_at].astype(LOW)
            return 0

        lax.fori_loop(0, half, one_key, 0)

    def part(rels, begin, end):
        def some(at, _):
            value = dot_nt(block_rows(dqkv, rels, local, ranks), attn_block[at])
            term[: len(rels) * local, pl.ds(pl.multiple_of(at * deep, deep), deep)] = value
            return 0

        lax.fori_loop(begin, end, some, 0)

    def qkv_grads(at, _):
        some_cols = pl.ds(pl.multiple_of(at * deep, deep), deep)
        grads[at] = dot_tn(first_in[:, some_cols], dqkv[...]).astype(LOW)
        return 0

    def to_ranks(step):
        peer = lax.rem(seq + step, ranks)
        return push(tile, tiles_in.at[seq], sems[17].at[step], sems[18].at[step], (peer, dp))

    def to_copies(step):
        peer = lax.rem(dp + step, copies)
        return push(
            tile_sum, tile_sums_in.at[dp], sems[19].at[step], sems[20].at[step], (seq, peer)
        )

    tile[0:1] = query_gain_grad[...]
    tile[1:2] = key_gain_grad[...]
    tile[2:] = jnp.zeros((tile.shape[0] - 2, size), jnp.float32)
    for step in range(1, ranks):
        to_ranks(step).start()
    tiles_in[seq] = tile[...]
    loads["block"].wait()

    def out_part(rels, begin, end):
        for at, rel in enumerate(rels):
            o_term[at * own : (at + 1) * own] = o_own[owner(rel)].astype(jnp.float32)

    out_total = RingSum(out_part, o_term, o_out, o_in, own, ranks, sems[30], sems[31], right, left)
    totals = two_sums(part, term, out_buf, in_buf, local, ranks, [*sems[2:4], *sems[28:30]], right, left)
    for step in range(1, half + 1):
        for total in totals:
            total.compute(step)
            total.launch(step)
        if step == 1:
            loads["first"].wait()
            lax.fori_loop(0, ranks, qkv_grads, 0)
            qkv_piece.first()
            qkv_piece.second()
        if step == 2:
            out_piece.third()
            for other in range(1, ranks):
                to_ranks(other).wait_recv()
            tile_sum[...] = jnp.sum(tiles_in[...], 0)
            for other in range(1, copies):
                to_copies(other).start()
            tile_sums_in[dp] = tile_sum[...]
        if step == half - 1:
            for other in range(1, copies):
                to_copies(other).wait_recv()
            gains[...] = jnp.sum(tile_sums_in[...], 0)
        if step > 1:
            out_total.compute(step - 1)
            out_total.launch(step - 1)
    out_total.compute(half)
    out_total.launch(half)
    qkv_piece.third()
    qkv_way.start()
    for total in totals:
        total.compute(half + 1)
    loads["dresid"].wait()
    for total in totals:
        total.arrive_last()

    def last(at, _):
        begin = pl.multiple_of(at * 32, 32)
        rows_at = pl.ds(begin, 32)
        value = tokens[rows_at].astype(jnp.float32)
        inv = rows_scaled(value)[1]
        grad = jnp.concatenate([total.last(begin, 32) for total in totals], 1)
        tokens_grad[rows_at] = dresid[rows_at] + rows_scaled_back(value, inv, grad)
        return 0

    lax.fori_loop(0, local // 32, last, 0)
    out_total.compute(half + 1)
    out_total.arrive_last()
    out_grad[...] = out_total.last(0, own)
    for step in range(1, ranks):
        to_ranks(step).wait_send()
    for step in range(1, copies):
        to_copies(step).wait_send()
    out_total.finish()
    for rel in range(1, ranks):
        exchange(rel).wait_send()
    for total in totals:
        total.finish()
    out_piece.finish()
    qkv_piece.finish()
    for way in mlp_ways:
        way.finish()
    qkv_way.finish()


def leave_kernel(
    attn_sums, mlp_sums, gains, attn_gain, mlp_gain, w_query, w_key, w_value, w_gate, w_up,
    query_out, key_out, value_out, gate_out, up_out, down_out, attn_out, mlp_out,
    head_query_out, head_key_out,
):
    own = attn_gain.shape[1]
    same = lax.broadcasted_iota(jnp.int32, (own, own), 0) == lax.broadcasted_iota(jnp.int32, (own, own), 1)

    @pl.when(pl.program_id(0) == 0)
    def _():
        attn_out[...] = jnp.zeros_like(attn_out)
        mlp_out[...] = jnp.zeros_like(mlp_out)
        head_query_out[...] = gains[0:1]
        head_key_out[...] = gains[1:2]

    for sums, gain, gain_out, parts in (
        (attn_sums, attn_gain, attn_out, ((query_out, w_query), (key_out, w_key), (value_out, w_value))),
        (mlp_sums, mlp_gain, mlp_out, ((gate_out, w_gate), (up_out, w_up), (down_out, None))),
    ):
        scale = jnp.sum(jnp.where(same, gain[...], 0.0), 1, keepdims=True)
        for rank in range(sums.shape[0]):
            at = 0
            for out, weight in parts:
                each = out.shape[1] // sums.shape[0]
                cols = slice(rank * each, (rank + 1) * each)
                value = sums[rank, :, at : at + each].astype(jnp.float32)
                at += each
                if weight is None:
                    out[:, cols] = value
                    continue
                out[:, cols] = value * scale
                inner = jnp.sum(value * weight[:, cols].astype(jnp.float32), 1, keepdims=True)
                gain_out[...] += jnp.sum(jnp.where(same, inner, 0.0), 0, keepdims=True)


VM = pl.BlockSpec(memory_space=pltpu.VMEM)
SM = pl.BlockSpec(memory_space=pltpu.SMEM)
ANY = pl.BlockSpec(memory_space=pl.ANY)


def call(kernel, number, ins, outs, scratch, operands):
    return pl.pallas_call(
        kernel,
        out_shape=[jax.ShapeDtypeStruct(shape, dtype) for shape, dtype, _ in outs],
        in_specs=ins,
        out_specs=[spec for _, _, spec in outs],
        scratch_shapes=scratch,
        compiler_params=pltpu.CompilerParams(
            collective_id=number, has_side_effects=True, vmem_limit_bytes=LIMIT
        ),
    )(*operands)


def columns_body(
    tokens,
    out_grad,
    span_order,
    doc_starts,
    w_query,
    w_key,
    w_value,
    w_output,
    attn_gain,
    query_gain,
    key_gain,
    w_gate,
    w_up,
    w_down,
    mlp_gain,
):
    ranks = lax.axis_size("seq")
    copies = lax.axis_size("dp")
    _, local, width = tokens.shape
    rows = local * ranks
    size = query_gain.shape[0]
    kv_heads = w_key.shape[1] // size // ranks
    heads = w_query.shape[1] // size // ranks
    q_cols, kv_cols = heads * size, kv_heads * size
    qkv_cols = q_cols + 2 * kv_cols
    ff = w_gate.shape[1] // ranks
    own = width // (ranks * copies)
    deep = own * copies
    half = ranks // 2
    f32, i32 = jnp.float32, jnp.int32
    exponents = np.arange(size) % (size // 2) * (-2.0 / size * math.log(1000000.0))
    freqs = jnp.asarray(np.exp(exponents)[None], f32)
    q_gain, k_gain = query_gain[None], key_gain[None]
    (
        resid, second, cosv, sinv, q_low, k_low, v_low, own_out, first_in, qkv, attn_block, dy_all, prob, mlp_block,
        out_all,
    ) = call(
        functools.partial(first_kernel, ranks, kv_heads),
        1,
        [SM, SM] + [VM] * 11 + [ANY] * 3,
        [
            ((local, width), f32, VM),
            ((local, width), LOW, VM),
            ((rows, size), f32, VM),
            ((rows, size), f32, VM),
            ((heads, rows, size), LOW, VM),
            ((kv_heads, rows, size), LOW, VM),
            ((kv_heads, rows, size), LOW, VM),
            ((local, q_cols * ranks), LOW, VM),
            ((rows, width), LOW, ANY),
            ((rows, qkv_cols), f32, ANY),
            ((ranks, deep, qkv_cols), LOW, ANY),
            ((rows, width), LOW, ANY),
            ((heads, rows, rows), LOW, ANY),
            ((ranks, deep, 3 * ff), LOW, ANY),
            ((ranks, deep, q_cols * ranks), LOW, ANY),
        ],
        [
            pltpu.VMEM((rows, width), LOW),
            pltpu.VMEM((rows, width), LOW),
            pltpu.VMEM((rows, qkv_cols), f32),
            pltpu.VMEM((ranks, deep, qkv_cols), LOW),
            pltpu.VMEM((ranks, own, qkv_cols), LOW),
            pltpu.VMEM((ranks, own, 3 * ff), LOW),
        ]
        + [pltpu.VMEM((own, ff * ranks), LOW)] * 3
        + [
            pltpu.VMEM((rows, width), LOW),
            pltpu.VMEM((heads, rows, rows), LOW),
            pltpu.VMEM((rows, 1), i32),
            pltpu.VMEM((rows, 1), i32),
            pltpu.VMEM((1, rows), i32),
            pltpu.VMEM((rows, q_cols), LOW),
            pltpu.VMEM((ranks, deep, q_cols * ranks), LOW),
        ]
        + ring_sems(ranks)
        + [pltpu.SemaphoreType.DMA((ranks,))] * 2
        + line_sems(ranks)
        + whole_sems(ranks)[:4]
        + spread_sems(ranks) * 4
        + [pltpu.SemaphoreType.DMA((heads * half + 8,))]
        + whole_sems(ranks)[4:],
        (
            span_order, doc_starts, tokens[0], out_grad[0], freqs, attn_gain[None], mlp_gain[None], q_gain, k_gain,
            w_query, w_key, w_value, w_output, w_gate, w_up, w_down,
        ),
    )
    block_out, dresid, dresid_low, mlp_own = call(
        functools.partial(mlp_kernel, ranks),
        2,
        [VM, VM, ANY, ANY, ANY],
        [
            ((local, width), LOW, VM),
            ((local, width), f32, VM),
            ((local, width), LOW, VM),
            ((ranks, own, 3 * ff), LOW, VM),
        ],
        [pltpu.VMEM((ranks, deep, 3 * ff), LOW)]
        + reduce_bufs(ranks, own, 3 * ff)
        + [
            pltpu.VMEM((rows, width), LOW),
            pltpu.VMEM((ranks, deep, 3 * ff), LOW),
            pltpu.VMEM((rows, ff), LOW),
            pltpu.VMEM((rows, 2 * ff), LOW),
            pltpu.VMEM((local, width), f32),
            pltpu.VMEM((rows, width), LOW),
        ]
        + sum_bufs(local, ranks, width)
        + sum_bufs(local, ranks, width)[1:]
        + [pltpu.SemaphoreType.DMA((3,))]
        + ring_sems(ranks) * 3
        + reduce_sems() * 4,
        (second, out_grad[0], resid, dy_all, mlp_block),
    )
    tokens_grad, gains, wo_grad, mlp_sums, attn_sums = call(
        functools.partial(back_kernel, ranks, kv_heads),
        3,
        [VM] * 5 + [ANY] * 12,
        [
            ((local, width), f32, VM),
            ((8, size), f32, VM),
            ((own, q_cols * ranks), f32, VM),
            ((ranks, own, 3 * ff), LOW, ANY),
            ((ranks, own, qkv_cols), LOW, VM),
        ],
        [pltpu.VMEM((ranks, deep, qkv_cols), LOW)]
        + reduce_bufs(ranks, own, qkv_cols)
        + [
            pltpu.VMEM((ranks, own, qkv_cols), LOW),
            pltpu.VMEM((1, size), f32),
            pltpu.VMEM((1, size), f32),
            pltpu.VMEM((8, size), f32),
            pltpu.VMEM((ranks, 8, size), f32),
            pltpu.VMEM((8, size), f32),
            pltpu.VMEM((copies, 8, size), f32),
            pltpu.VMEM((local, q_cols * ranks), LOW),
            pltpu.VMEM((rows, q_cols), LOW),
            pltpu.VMEM((kv_heads, rows, size), f32),
            pltpu.VMEM((kv_heads, rows, size), f32),
            pltpu.VMEM((rows, qkv_cols), LOW),
            pltpu.VMEM((rows, width), LOW),
            pltpu.VMEM((ranks, deep, qkv_cols), LOW),
            pltpu.VMEM((rows, qkv_cols), f32),
            pltpu.VMEM((rows, size), f32),
            pltpu.VMEM((rows, size), f32),
            pltpu.VMEM((heads, rows, size), LOW),
            pltpu.VMEM((kv_heads, rows, size), LOW),
            pltpu.VMEM((kv_heads, rows, size), LOW),
            pltpu.VMEM((heads, rows, rows), LOW),
            pltpu.VMEM((local, width), f32),
        ]
        + sum_bufs(local, ranks, width)
        + [pltpu.VMEM((ranks, deep, q_cols * ranks), LOW)]
        + reduce_bufs(ranks, own, q_cols * ranks)
        + [pltpu.VMEM((ranks, own, q_cols * ranks), LOW)]
        + sum_bufs(own, ranks, q_cols * ranks)
        + [pltpu.SemaphoreType.DMA((ranks,))] * 2
        + ring_sems(ranks)
        + reduce_sems() * 2
        + deliver_sems(ranks) * 3
        + [pltpu.SemaphoreType.DMA((ranks,))] * 2
        + [pltpu.SemaphoreType.DMA((copies,))] * 2
        + [pltpu.SemaphoreType.DMA((11,))]
        + deliver_sems(ranks) * 2
        + ring_sems(ranks) * 2,
        (
            tokens[0], dresid_low, q_gain, k_gain, own_out, first_in, attn_block, qkv, cosv, sinv, q_low, k_low,
            v_low, prob, dresid, mlp_own, out_all,
        ),
    )
    whole = pl.BlockSpec((1, own), lambda at: (0, 0))
    each = (q_cols, kv_cols, kv_cols, ff, ff, ff)
    many = 2
    columns = [pl.BlockSpec((own, many * cols), lambda at: (0, at)) for cols in each]
    head = pl.BlockSpec((1, size), lambda at: (0, 0))
    *grads, dga, dgm, dgq, dgk = pl.pallas_call(
        leave_kernel,
        grid=(ranks // many,),
        out_shape=[jax.ShapeDtypeStruct((own, cols * ranks), f32) for cols in each]
        + [jax.ShapeDtypeStruct((1, own), f32)] * 2
        + [jax.ShapeDtypeStruct((1, size), f32)] * 2,
        in_specs=[
            pl.BlockSpec((many, own, qkv_cols), lambda at: (at, 0, 0)),
            pl.BlockSpec((many, own, 3 * ff), lambda at: (at, 0, 0)),
            pl.BlockSpec((8, size), lambda at: (0, 0)),
            whole,
            whole,
            *columns[:3],
            *columns[3:5],
        ],
        out_specs=columns + [whole, whole, head, head],
    )(attn_sums, mlp_sums, gains, attn_gain[None], mlp_gain[None], w_query, w_key, w_value, w_gate, w_up)
    return (
        block_out[None], tokens_grad[None], *grads[:3], wo_grad, dga[0], dgq[0], dgk[0], *grads[3:], dgm[0],
    )


def body(*args):
    tokens, w_key, query_gain = args[0], args[5], args[9]
    groups = w_key.shape[1] // query_gain.shape[0]
    ranks = lax.axis_size("seq")
    if tokens.shape[0] == 1 and ranks % 2 == 0 and groups % ranks == 0 and lax.axis_size("dp") == 4:
        return columns_body(*args)
    return gathered_body(*args)


def solution(mesh):
    return jax.shard_map(
        body,
        mesh=mesh,
        in_specs=(
            P("dp", "seq", None),
            P("dp", "seq", None),
            P(),
            P("dp", None),
            P(("seq", "dp"), None),
            P(("seq", "dp"), None),
            P(("seq", "dp"), None),
            P(("seq", "dp"), None),
            P(("seq", "dp")),
            P(),
            P(),
            P(("seq", "dp"), None),
            P(("seq", "dp"), None),
            P(("seq", "dp"), None),
            P(("seq", "dp")),
        ),
        out_specs=(
            P("dp", "seq", None),
            P("dp", "seq", None),
            P(("seq", "dp"), None),
            P(("seq", "dp"), None),
            P(("seq", "dp"), None),
            P(("seq", "dp"), None),
            P(("seq", "dp")),
            P(),
            P(),
            P(("seq", "dp"), None),
            P(("seq", "dp"), None),
            P(("seq", "dp"), None),
            P(("seq", "dp")),
        ),
        check_vma=False,
    )
```

```python
import functools
import math

import jax
import jax.numpy as jnp
import numpy as np
from jax import lax
from jax.experimental import pallas as pl
from jax.experimental.pallas import tpu as pltpu
from jax.sharding import PartitionSpec as P

EPS = 1e-06
NEG = -1e30


def normed(v, gain):
    scale_inv = lax.rsqrt(jnp.mean(v * v, -1, keepdims=True) + EPS)
    return (v * scale_inv * gain, scale_inv)


def norm_back(v, scale_inv, gain, grad):
    scaled = grad * gain
    inner = jnp.mean(scaled * v, -1, keepdims=True)
    dv = scale_inv * scaled - v * scale_inv * scale_inv * scale_inv * inner
    dgain = jnp.sum((grad * v * scale_inv).reshape(-1, v.shape[-1]), 0)
    return (dv, dgain)


def rotary(pos, width):
    half = width // 2
    freqs = jnp.exp(jnp.arange(half, dtype=jnp.float32) * (-2.0 / width * math.log(1000000.0)))
    angle = pos.astype(jnp.float32)[:, None] * freqs[None, :]
    return (jnp.cos(angle)[:, None, :], jnp.sin(angle)[:, None, :])


def rotate(v, cosv, sinv):
    half = v.shape[-1] // 2
    first, second = (v[..., :half], v[..., half:])
    return jnp.concatenate([first * cosv - second * sinv, second * cosv + first * sinv], -1)


def rotate_back(grad, cosv, sinv):
    half = grad.shape[-1] // 2
    first, second = (grad[..., :half], grad[..., half:])
    return jnp.concatenate([first * cosv + second * sinv, second * cosv - first * sinv], -1)


def place(order, begin, count, span):
    rows = begin + jnp.arange(count, dtype=jnp.int32)
    slots = rows // span
    picked = slots[:, None] == jnp.arange(order.shape[0], dtype=jnp.int32)[None, :]
    return jnp.sum(jnp.where(picked, order[None, :], 0), -1) * span + rows % span


def doc_of(starts, pos):
    return jnp.sum((starts[:, None, :] <= pos[None, :, None]).astype(jnp.int32), -1)


def gathered_body(
    tokens,
    out_grad,
    span_order,
    doc_starts,
    w_query,
    w_key,
    w_value,
    w_output,
    attn_gain,
    query_gain,
    key_gain,
    w_gate,
    w_up,
    w_down,
    mlp_gain,
):
    seqs, local, width = tokens.shape
    span = local // 2
    head_size = query_gain.shape[0]
    kv_heads = w_key.shape[1] // head_size
    heads = w_query.shape[1] // head_size
    share = heads // kv_heads
    kv_width = kv_heads * head_size
    ff_width = w_gate.shape[1]
    scale = 1.0 / math.sqrt(head_size)
    total_rows = seqs * local
    own_rows = width // lax.axis_size(("seq", "dp"))
    qpos = place(span_order, lax.axis_index("seq") * local, local, span)
    qdoc = doc_of(doc_starts, qpos)
    cosv, sinv = rotary(qpos, head_size)

    def gather_attn():
        return (
            lax.all_gather(w_query, ("seq", "dp"), axis=0, tiled=True),
            lax.all_gather(w_key, ("seq", "dp"), axis=0, tiled=True),
            lax.all_gather(w_value, ("seq", "dp"), axis=0, tiled=True),
            lax.all_gather(w_output, ("seq", "dp"), axis=0, tiled=True),
            lax.all_gather(
                attn_gain.astype(jnp.bfloat16), ("seq", "dp"), axis=0, tiled=True
            ).astype(attn_gain.dtype),
        )

    def gather_mlp():
        return (
            lax.all_gather(w_gate, ("seq", "dp"), axis=0, tiled=True),
            lax.all_gather(w_up, ("seq", "dp"), axis=0, tiled=True),
            lax.all_gather(w_down, ("seq", "dp"), axis=0, tiled=True),
            lax.all_gather(mlp_gain.astype(jnp.bfloat16), ("seq", "dp"), axis=0, tiled=True).astype(
                mlp_gain.dtype
            ),
        )

    x_rows = tokens.astype(jnp.float32).reshape(total_rows, width)
    wq_all, wk_all, wv_all, wo_all, ga_all = gather_attn()
    first_norm, first_inv = normed(x_rows, ga_all)
    first_in = first_norm.astype(jnp.bfloat16)
    q_raw = jnp.dot(first_in, wq_all, preferred_element_type=jnp.float32).reshape(
        seqs, local, heads, head_size
    )
    k_raw = jnp.dot(first_in, wk_all, preferred_element_type=jnp.float32).reshape(
        seqs, local, kv_heads, head_size
    )
    v_low = (
        jnp.dot(first_in, wv_all, preferred_element_type=jnp.float32)
        .astype(jnp.bfloat16)
        .reshape(seqs, local, kv_heads, head_size)
    )
    q_normed, q_inv = normed(q_raw, query_gain)
    k_normed, k_inv = normed(k_raw, key_gain)
    q_low = rotate(q_normed, cosv, sinv).astype(jnp.bfloat16)
    k_low = rotate(k_normed, cosv, sinv).astype(jnp.bfloat16)
    q_group = q_low.reshape(seqs, local, kv_heads, share, head_size)

    def scores(piece_key, start):
        count = piece_key.shape[1]
        kpos = place(span_order, start, count, span)
        kdoc = doc_of(doc_starts, kpos)
        visible = (qdoc[:, :, None] == kdoc[:, None, :]) & (
            kpos[None, None, :] <= qpos[None, :, None]
        )
        raw = (
            jnp.einsum("sqgjd,skgd->sgjqk", q_group, piece_key, preferred_element_type=jnp.float32)
            * scale
        )
        return (raw, visible[:, None, None])

    start_top = jnp.full((seqs, kv_heads, share, local), NEG, jnp.float32)
    piece = (
        lax.all_gather(k_low, "seq", axis=1, tiled=True),
        lax.all_gather(v_low, "seq", axis=1, tiled=True),
    )
    top = start_top
    raw, visible = scores(piece[0], jnp.int32(0))
    raw = jnp.where(visible, raw, NEG)
    new_top = jnp.maximum(top, jnp.max(raw, -1))
    weights = jnp.where(visible, jnp.exp(raw - new_top[..., None]), 0.0)
    total = jnp.sum(weights, -1)
    summed = jnp.einsum(
        "sgjqk,skgd->sgjqd",
        weights.astype(jnp.bfloat16),
        piece[1],
        preferred_element_type=jnp.float32,
    )
    top, total, summed = (new_top, total, summed)
    log_total = top + jnp.log(total)
    attn_vals = summed / total[..., None]
    out_low = (
        jnp.transpose(attn_vals, (0, 3, 1, 2, 4))
        .reshape(total_rows, heads * head_size)
        .astype(jnp.bfloat16)
    )
    resid = x_rows + jnp.einsum("nh,dh->nd", out_low, wo_all, preferred_element_type=jnp.float32)
    wg_all, wu_all, wd_all, gm_all = gather_mlp()
    second_norm, second_inv = normed(resid, gm_all)
    second_in = second_norm.astype(jnp.bfloat16)
    gate = jnp.dot(second_in, wg_all, preferred_element_type=jnp.float32)
    upper = jnp.dot(second_in, wu_all, preferred_element_type=jnp.float32)
    sigma = jax.nn.sigmoid(gate)
    act = gate * sigma
    hidden = (act * upper).astype(jnp.bfloat16)
    result = resid + jnp.einsum("nf,df->nd", hidden, wd_all, preferred_element_type=jnp.float32)
    block_out = result.astype(jnp.bfloat16).reshape(seqs, local, width)
    grad_low = out_grad.reshape(total_rows, width)
    wg_all, wu_all, wd_all, gm_all = gather_mlp()
    dmid = jnp.einsum("nd,df->nf", grad_low, wd_all, preferred_element_type=jnp.float32)
    dgate = (dmid * upper * sigma * (1.0 + gate * (1.0 - sigma))).astype(jnp.bfloat16)
    dupper = (dmid * act).astype(jnp.bfloat16)
    left = second_in
    outer = grad_low
    mlp_sums = lax.psum_scatter(
        jnp.concatenate(
            [
                jnp.einsum("nd,nf->df", left, dgate, preferred_element_type=jnp.float32),
                jnp.einsum("nd,nf->df", left, dupper, preferred_element_type=jnp.float32),
                jnp.einsum("nd,nf->df", outer, hidden, preferred_element_type=jnp.float32),
            ],
            1,
        ),
        ("seq", "dp"),
        scatter_dimension=0,
        tiled=True,
    )
    dsecond = jnp.einsum(
        "nf,df->nd", dgate, wg_all, preferred_element_type=jnp.float32
    ) + jnp.einsum("nf,df->nd", dupper, wu_all, preferred_element_type=jnp.float32)
    dresid_norm, dgm = norm_back(resid, second_inv, gm_all, dsecond)
    dresid = grad_low.astype(jnp.float32) + dresid_norm
    dresid_low = dresid.astype(jnp.bfloat16)
    wq_all, wk_all, wv_all, wo_all, ga_all = gather_attn()
    dout_low = jnp.einsum(
        "nd,dh->nh", dresid_low, wo_all, preferred_element_type=jnp.float32
    ).astype(jnp.bfloat16)
    dout_group = dout_low.reshape(seqs, local, kv_heads, share, head_size)
    delta = jnp.sum(jnp.transpose(dout_group.astype(jnp.float32), (0, 2, 3, 1, 4)) * attn_vals, -1)
    piece = (
        lax.all_gather(k_low, "seq", axis=1, tiled=True),
        lax.all_gather(v_low, "seq", axis=1, tiled=True),
    )
    count = piece[0].shape[1]
    raw, visible = scores(piece[0], jnp.int32(0))
    prob = jnp.where(visible, jnp.exp(raw - log_total[..., None]), 0.0)
    dprob = jnp.einsum(
        "sqgjd,skgd->sgjqk", dout_group, piece[1], preferred_element_type=jnp.float32
    )
    dscore = (prob * (dprob - delta[..., None])).astype(jnp.bfloat16)
    dq_sum = jnp.einsum("sgjqk,skgd->sqgjd", dscore, piece[0], preferred_element_type=jnp.float32)
    dk_part = (
        jnp.einsum("sgjqk,sqgjd->skgd", dscore, q_group, preferred_element_type=jnp.float32) * scale
    )
    dv_part = jnp.einsum(
        "sgjqk,sqgjd->skgd",
        prob.astype(jnp.bfloat16),
        dout_group,
        preferred_element_type=jnp.float32,
    )
    joined = jnp.concatenate(
        [dk_part.reshape(seqs, count, kv_width), dv_part.reshape(seqs, count, kv_width)], -1
    )
    buffer = joined
    dq_sum, buffer = (dq_sum, buffer)
    key_sums = lax.psum_scatter(
        buffer.astype(jnp.bfloat16), "seq", scatter_dimension=1, tiled=True
    ).astype(jnp.float32)
    dq_rot = (dq_sum * scale).reshape(seqs, local, heads, head_size)
    dq_raw, dgq = norm_back(q_raw, q_inv, query_gain, rotate_back(dq_rot, cosv, sinv))
    dk_rot = key_sums[..., :kv_width].reshape(seqs, local, kv_heads, head_size)
    dk_raw, dgk = norm_back(k_raw, k_inv, key_gain, rotate_back(dk_rot, cosv, sinv))
    dq_low = dq_raw.reshape(total_rows, heads * head_size).astype(jnp.bfloat16)
    dk_low = dk_raw.reshape(total_rows, kv_width).astype(jnp.bfloat16)
    dv_low = key_sums[..., kv_width:].reshape(total_rows, kv_width).astype(jnp.bfloat16)
    left = first_in
    outer = dresid_low
    attn_sums = lax.psum_scatter(
        jnp.concatenate(
            [
                jnp.einsum("nd,nh->dh", left, dq_low, preferred_element_type=jnp.float32),
                jnp.einsum("nd,nh->dh", left, dk_low, preferred_element_type=jnp.float32),
                jnp.einsum("nd,nh->dh", left, dv_low, preferred_element_type=jnp.float32),
                jnp.einsum("nd,nh->dh", outer, out_low, preferred_element_type=jnp.float32),
            ],
            1,
        ),
        ("seq", "dp"),
        scatter_dimension=0,
        tiled=True,
    )
    dfirst = jnp.einsum("nh,dh->nd", dq_low, wq_all, preferred_element_type=jnp.float32)
    dfirst = dfirst + jnp.einsum("nh,dh->nd", dk_low, wk_all, preferred_element_type=jnp.float32)
    dfirst = dfirst + jnp.einsum("nh,dh->nd", dv_low, wv_all, preferred_element_type=jnp.float32)
    dx_norm, dga = norm_back(x_rows, first_inv, ga_all, dfirst)
    tokens_grad = (dresid + dx_norm).reshape(seqs, local, width)
    dga_all, dgm_all, dgq_all, dgk_all = lax.psum((dga, dgm, dgq, dgk), ("seq", "dp"))
    offset = lax.axis_index(("seq", "dp")) * own_rows
    attn_gain_grad = lax.dynamic_slice_in_dim(dga_all, offset, own_rows, 0)
    mlp_gain_grad = lax.dynamic_slice_in_dim(dgm_all, offset, own_rows, 0)
    q_cols = heads * head_size
    w_query_grad = attn_sums[:, :q_cols]
    w_key_grad = attn_sums[:, q_cols : q_cols + kv_width]
    w_value_grad = attn_sums[:, q_cols + kv_width : q_cols + 2 * kv_width]
    w_output_grad = attn_sums[:, q_cols + 2 * kv_width :]
    w_gate_grad = mlp_sums[:, :ff_width]
    w_up_grad = mlp_sums[:, ff_width : 2 * ff_width]
    w_down_grad = mlp_sums[:, 2 * ff_width :]
    return (
        block_out,
        tokens_grad,
        w_query_grad,
        w_key_grad,
        w_value_grad,
        w_output_grad,
        attn_gain_grad,
        dgq_all,
        dgk_all,
        w_gate_grad,
        w_up_grad,
        w_down_grad,
        mlp_gain_grad,
    )


LOW = jnp.bfloat16
MESH = pl.DeviceIdType.MESH
LIMIT = 60 * 2**20


def ring_order(ranks):
    half = ranks // 2
    order = [0]
    for step in range(1, half):
        order += [step, ranks - step]
    return order + [half]


def ring_place(seq, ranks):
    z, x = lax.div(seq, 2), lax.rem(seq, 2)
    return z + x * (ranks - 1 - 2 * z)


def ring_seq(place, ranks):
    half = ranks // 2
    x, z = lax.div(place, half), lax.rem(place, half)
    return 2 * (z + x * (half - 1 - 2 * z)) + x


def neighbours(ranks):
    seq, dp = lax.axis_index("seq"), lax.axis_index("dp")
    at = ring_place(seq, ranks)
    right = ring_seq(lax.rem(at + 1, ranks), ranks)
    left = ring_seq(lax.rem(at + ranks - 1, ranks), ranks)
    return (right, dp), (left, dp)


def knock(devices):
    barrier = pltpu.get_barrier_semaphore()
    for device in devices:
        pl.semaphore_signal(barrier, inc=1, device_id=device, device_id_type=MESH)


def answered(devices):
    pl.semaphore_wait(pltpu.get_barrier_semaphore(), len(devices))


def move(src, dst, sem):
    copy = pltpu.make_async_copy(src, dst, sem)
    copy.start()
    return copy


def push(src, dst, send, recv, device):
    return pltpu.make_async_remote_copy(
        src_ref=src, dst_ref=dst, send_sem=send, recv_sem=recv, device_id=device, device_id_type=MESH
    )


def dot_nn(left, right):
    return jnp.dot(left, right, preferred_element_type=jnp.float32)


def dot_nt(left, right):
    return lax.dot_general(left, right, (((1,), (1,)), ((), ())), preferred_element_type=jnp.float32)


def dot_tn(left, right):
    return lax.dot_general(left, right, (((0,), (0,)), ((), ())), preferred_element_type=jnp.float32)


def block_row(rel, local, ranks):
    place = ring_place(lax.axis_index("seq"), ranks)
    return pl.multiple_of(ring_seq(lax.rem(place + rel, ranks), ranks) * local, local)


def block_rows(ref, rels, local, ranks):
    blocks = [ref[pl.ds(block_row(rel, local, ranks), local)] for rel in rels]
    return blocks[0] if len(blocks) == 1 else jnp.concatenate(blocks, 0)


def rels_of(step, ranks):
    return [rel for rel in ring_order(ranks) if min(rel, ranks - rel) == step]


class RingGather:
    def __init__(self, buf, local, ranks, send, recv, right, left, row):
        self.buf, self.sub, self.half = buf, local // 2, ranks // 2
        self.send, self.recv, self.right, self.left = send, recv, right, left
        self.ranks, self.row = ranks, row

    def copies(self, step, part):
        ways = ((0, (self.ranks - step + 1) % self.ranks, self.right), (1, step - 1, self.left))
        given = []
        for way, rel, device in ways:
            if step < self.half or way == part:
                block = self.buf.at[pl.ds(self.row(rel) + part * self.sub, self.sub)]
                at = 2 * (step - 1) + part
                given.append(push(block, block, self.send.at[way, at], self.recv.at[way, at], device))
        return given

    def start(self, step):
        for part in range(2):
            for copy in self.copies(step, part):
                copy.start()

    def advance(self, step):
        for part in range(2):
            for copy in self.copies(step, part):
                copy.wait_recv()
            if step < self.half:
                for copy in self.copies(step + 1, part):
                    copy.start()

    def finish(self):
        for step in range(1, self.half + 1):
            for part in range(2):
                for copy in self.copies(step, part):
                    copy.wait_send()


class LineGather:
    def __init__(self, buf, local, ranks, send, recv, x_send, x_recv):
        self.buf, self.local, self.length = buf, local, ranks // 2
        self.send, self.recv, self.x_send, self.x_recv = send, recv, x_send, x_recv
        self.seq, self.dp = lax.axis_index("seq"), lax.axis_index("dp")
        self.z, self.x = lax.div(self.seq, 2), lax.rem(self.seq, 2)

    def block(self, z):
        return self.buf.at[pl.ds(pl.multiple_of((2 * z + self.x) * self.local, self.local), self.local)]

    def hop(self, way, step):
        block = self.block(self.z + (step - 1 if way else 1 - step))
        to = self.seq + (-2 if way else 2)
        return push(block, block, self.send.at[way, step - 1], self.recv.at[way, step - 1], (to, self.dp))

    def sends(self, way, step):
        if way:
            return (self.z > 0) & (self.z + step <= self.length)
        return (self.z < self.length - 1) & (self.z >= step - 1)

    def comes(self, way, step):
        return self.z + step < self.length if way else self.z >= step

    def across(self, way, step):
        block = self.block(self.z + (step if way else -step))
        at = step + way * (self.length - 1)
        return push(
            block, block, self.x_send.at[at], self.x_recv.at[at], (self.seq + 1 - 2 * self.x, self.dp)
        )

    def from_x(self, way, step):
        z = self.z + (step if way else -step)
        row = pl.multiple_of((2 * z + 1 - self.x) * self.local, self.local)
        block = self.buf.at[pl.ds(row, self.local)]
        at = step + way * (self.length - 1)
        return push(
            block, block, self.x_send.at[at], self.x_recv.at[at], (self.seq + 1 - 2 * self.x, self.dp)
        )

    def start(self, step):
        for way in range(2):
            pl.when(self.sends(way, step))(lambda way=way: self.hop(way, step).start())
        self.pass_on(step - 1)

    def pass_on(self, step):
        if step == 0:
            self.across(0, 0).start()
            return
        for way in range(2):
            pl.when(self.comes(way, step))(lambda way=way: self.across(way, step).start())

    def arrive(self, step):
        for way in range(2):
            pl.when(self.comes(way, step))(lambda way=way: self.incoming(way, step).wait_recv())

    def incoming(self, way, step):
        block = self.block(self.z + (step if way else -step))
        to = self.seq + 1 - 2 * self.x
        return push(block, block, self.send.at[way, step - 1], self.recv.at[way, step - 1], (to, self.dp))

    def run(self):
        for step in range(1, self.length):
            self.advance(step)

    def advance(self, step):
        self.arrive(step)
        if step < self.length - 1:
            self.start(step + 1)
        else:
            self.pass_on(step)

    def complete(self):
        self.from_x(0, 0).wait_recv()
        for step in range(1, self.length):
            for way in range(2):
                pl.when(self.comes(way, step))(lambda way=way: self.from_x(way, step).wait_recv())

    def finish(self):
        self.across(0, 0).wait_send()
        for step in range(1, self.length):
            for way in range(2):
                pl.when(self.sends(way, step))(lambda way=way: self.hop(way, step).wait_send())
                pl.when(self.comes(way, step))(lambda way=way: self.across(way, step).wait_send())


def line_sems(ranks):
    half = ranks // 2
    return [pltpu.SemaphoreType.DMA((2, half))] * 2 + [pltpu.SemaphoreType.DMA((2 * half,))] * 2


class RingSum:
    def __init__(self, part, term, out_buf, in_buf, local, ranks, send, recv, right, left, stream=0, streams=1):
        self.part, self.term, self.out_buf, self.in_buf = part, term, out_buf, in_buf
        self.local, self.ranks, self.half = local, ranks, ranks // 2
        each = term.shape[1] // streams
        self.cols = pl.ds(stream * each, each)
        self.tiles = (stream * ranks // streams, (stream + 1) * ranks // streams)
        self.send, self.recv, self.right, self.left = send, recv, right, left

    def copies(self, step):
        rows = self.local // 2 if step == 1 else self.local
        skip = self.local // 2 if step == 1 else 0
        return [
            push(
                self.out_buf.at[way, (step - 1) % 2, pl.ds(begin, rows), self.cols],
                self.in_buf.at[way, step - 1, pl.ds(begin, rows), self.cols],
                self.send.at[way, step - 1],
                self.recv.at[way, step - 1],
                device,
            )
            for way, begin, device in ((0, 0, self.right), (1, skip, self.left))
        ]

    def compute(self, step):
        if step == 1:
            self.part([self.half], *self.tiles)
        elif step <= self.half:
            self.part(rels_of(self.half + 1 - step, self.ranks), *self.tiles)
        else:
            self.part([0], *self.tiles)

    def launch(self, step):
        local, skip = self.local, self.local // 2
        if step > 2:
            for copy in self.copies(step - 2):
                copy.wait_send()
        if step == 1:
            for way in range(2):
                rows = pl.ds(way * skip, skip)
                self.out_buf[way, 0, rows, self.cols] = self.term[rows, self.cols].astype(LOW)
        else:
            for copy in self.copies(step - 1):
                copy.wait_recv()
            for way in range(2):
                for begin, with_sum in ((0, step > 2 or way == 0), (skip, step > 2 or way == 1)):
                    value = self.term[pl.ds(way * local + begin, skip), self.cols]
                    if with_sum:
                        value = value + self.in_buf[way, step - 2, pl.ds(begin, skip), self.cols].astype(jnp.float32)
                    self.out_buf[way, (step - 1) % 2, pl.ds(begin, skip), self.cols] = value.astype(LOW)
        for copy in self.copies(step):
            copy.start()

    def last(self, begin, count):
        rows = pl.ds(begin, count)
        value = self.term[rows, self.cols] + self.in_buf[0, self.half - 1, rows, self.cols].astype(jnp.float32)
        return value + self.in_buf[1, self.half - 1, rows, self.cols].astype(jnp.float32)

    def arrive_last(self):
        for copy in self.copies(self.half):
            copy.wait_recv()

    def finish(self):
        for step in range(max(1, self.half - 1), self.half + 1):
            for copy in self.copies(step):
                copy.wait_send()


def two_sums(part, term, out_buf, in_buf, local, ranks, sems, right, left):
    return [
        RingSum(
            part, term, out_buf, in_buf, local, ranks, sems[2 * at], sems[2 * at + 1], right, left, at, 2
        )
        for at in range(2)
    ]


def ring_sems(ranks):
    return [pltpu.SemaphoreType.DMA((2, ranks)), pltpu.SemaphoreType.DMA((2, ranks))]


def sum_bufs(local, ranks, width):
    return [
        pltpu.VMEM((2 * local, width), jnp.float32),
        pltpu.VMEM((2, 2, local, width), LOW),
        pltpu.VMEM((2, ranks // 2, local, width), LOW),
    ]


def turn(v):
    return pltpu.roll(v, v.shape[-1] // 2, v.ndim - 1)


def rows_scaled(v):
    inv = lax.rsqrt(jnp.mean(v * v, -1, keepdims=True) + EPS)
    return v * inv, inv


def rows_scaled_back(v, inv, grad):
    return inv * grad - v * (inv * inv * inv * jnp.mean(grad * v, -1, keepdims=True))


class Spread:
    def __init__(self, rows, block, ranks, own, cols, sems):
        self.rows, self.block, self.ranks, self.own, self.cols = rows, block, ranks, own, cols
        self.send, self.recv, self.hop_send, self.hop_recv, self.here = sems
        self.seq, self.dp = lax.axis_index("seq"), lax.axis_index("dp")
        y, core = lax.div(self.dp, 2), lax.rem(self.dp, 2)
        self.beside, self.sibling = (1 - y) * 2 + core, y * 2 + 1 - core

    def at(self, dp):
        return pl.ds(pl.multiple_of(dp * self.own, self.own), self.own)

    def exchange(self):
        for step in range(1, self.ranks):
            peer = lax.rem(self.seq + step, self.ranks)
            yield push(
                self.rows.at[peer, :, self.cols],
                self.block.at[self.seq, self.at(self.dp), self.cols],
                self.send.at[step],
                self.recv.at[step],
                (peer, self.dp),
            )

    def keep(self):
        return pltpu.make_async_copy(
            self.rows.at[self.seq, :, self.cols],
            self.block.at[self.seq, self.at(self.dp), self.cols],
            self.here,
        )

    def hop(self, number):
        dp = self.beside if number == 2 else self.dp
        part = self.block.at[:, self.at(dp), self.cols]
        to = self.beside if number == 0 else self.sibling
        return push(part, part, self.hop_send.at[number], self.hop_recv.at[number], (self.seq, to))

    def start(self):
        self.keep().start()
        for copy in self.exchange():
            copy.start()

    def arrive(self):
        self.keep().wait()
        for copy in self.exchange():
            copy.wait_recv()

    def finish(self):
        for copy in self.exchange():
            copy.wait_send()
        for number in range(3):
            self.hop(number).wait_send()


def spread_sems(ranks):
    return [
        pltpu.SemaphoreType.DMA((ranks,)),
        pltpu.SemaphoreType.DMA((ranks,)),
        pltpu.SemaphoreType.DMA((3,)),
        pltpu.SemaphoreType.DMA((3,)),
        pltpu.SemaphoreType.DMA,
    ]


class WholeGather:
    def __init__(self, block, ranks, own, sems):
        self.block, self.ranks, self.half, self.own = block, ranks, ranks // 2, own
        self.send, self.recv, self.y_send, self.y_recv, self.core_send, self.core_recv = sems
        self.seq, self.dp = lax.axis_index("seq"), lax.axis_index("dp")
        self.right, self.left = neighbours(ranks)
        self.place = ring_place(self.seq, ranks)
        y, core = lax.div(self.dp, 2), lax.rem(self.dp, 2)
        self.beside, self.sibling = (1 - y) * 2 + core, y * 2 + 1 - core

    def at(self, rel, dp, begin, count):
        seq = ring_seq(lax.rem(self.place + rel + self.ranks, self.ranks), self.ranks)
        return self.block.at[seq, pl.ds(pl.multiple_of(dp * self.own + begin, count), count)]

    def copies(self, step):
        last = step == self.half
        rows = self.own // 2 if last else self.own
        skip = self.own // 2 if last else 0
        given = []
        for way, rel, begin, device in ((0, 1 - step, 0, self.right), (1, step - 1, skip, self.left)):
            part = self.at(rel, self.dp, begin, rows)
            given.append(push(part, part, self.send.at[way, step - 1], self.recv.at[way, step - 1], device))
        return given

    def start(self, step):
        for copy in self.copies(step):
            copy.start()

    def hops(self, step):
        for at, rel in enumerate(ring_order(self.ranks)):
            if min(rel, self.ranks - rel) == step:
                part = self.at(rel, self.dp, 0, self.own)
                yield push(part, part, self.y_send.at[at], self.y_recv.at[at], (self.seq, self.beside))
                yield push(part, part, self.core_send.at[at], self.core_recv.at[at], (self.seq, self.sibling))

    def arrive(self, step):
        for copy in self.copies(step):
            copy.wait_recv()

    def forward(self, step):
        for copy in self.hops(step):
            copy.start()

    def cross(self):
        part = self.block.at[:, pl.ds(pl.multiple_of(self.beside * self.own, self.own), self.own)]
        at = self.ranks
        return push(part, part, self.core_send.at[at], self.core_recv.at[at], (self.seq, self.sibling))

    def complete(self):
        for step in range(self.half + 1):
            for copy in self.hops(step):
                copy.wait_recv()
        self.cross().start()
        self.cross().wait_recv()

    def finish(self):
        for step in range(1, self.half + 1):
            for copy in self.copies(step):
                copy.wait_send()
        for step in range(self.half + 1):
            for copy in self.hops(step):
                copy.wait_send()
        self.cross().wait_send()


def whole_sems(ranks):
    return (
        ring_sems(ranks)
        + [pltpu.SemaphoreType.DMA((ranks,))] * 2
        + [pltpu.SemaphoreType.DMA((ranks + 1,))] * 2
    )


class Reduce:
    def __init__(self, grads, from_core, from_y, total, own, first, count, cols, sems):
        self.grads, self.from_core, self.from_y, self.total = grads, from_core, from_y, total
        self.own, self.begin, self.count, self.cols = own, first, count, cols
        self.send, self.recv = sems
        self.seq, dp = lax.axis_index("seq"), lax.axis_index("dp")
        self.y, self.core = lax.div(dp, 2), lax.rem(dp, 2)
        self.beside, self.sibling = (1 - self.y) * 2 + self.core, self.y * 2 + 1 - self.core

    def at(self, y, core):
        return pl.ds(pl.multiple_of((y * 2 + core) * self.own, self.own), self.own)

    def hop(self, number):
        some, cols = pl.ds(self.begin, self.count), self.cols
        if number == 2:
            src, dst, to = self.from_core.at[0, some, :, cols], self.from_y.at[some, :, cols], self.beside
        else:
            rows = self.at(1 - self.y if number == 0 else self.y, 1 - self.core)
            src, dst, to = self.grads.at[some, rows, cols], self.from_core.at[number, some, :, cols], self.sibling
        return push(src, dst, self.send.at[number], self.recv.at[number], (self.seq, to))

    def first(self):
        self.hop(0).start()
        self.hop(1).start()

    def second(self):
        self.hop(0).wait_recv()
        rows = self.at(1 - self.y, self.core)

        def some(at, _):
            value = self.grads[at, rows, self.cols].astype(jnp.float32)
            value = value + self.from_core[0, at, :, self.cols].astype(jnp.float32)
            self.from_core[0, at, :, self.cols] = value.astype(LOW)
            return 0

        lax.fori_loop(self.begin, self.begin + self.count, some, 0)
        self.hop(2).start()

    def third(self):
        self.hop(1).wait_recv()
        self.hop(2).wait_recv()
        rows = self.at(self.y, self.core)

        def some(at, _):
            value = self.grads[at, rows, self.cols].astype(jnp.float32)
            value = value + self.from_core[1, at, :, self.cols].astype(jnp.float32)
            value = value + self.from_y[at, :, self.cols].astype(jnp.float32)
            self.total[at, :, self.cols] = value.astype(LOW)
            return 0

        lax.fori_loop(self.begin, self.begin + self.count, some, 0)

    def finish(self):
        for number in range(3):
            self.hop(number).wait_send()


def reduce_sems():
    return [pltpu.SemaphoreType.DMA((3,)), pltpu.SemaphoreType.DMA((3,))]


def reduce_bufs(ranks, own, cols):
    return [pltpu.VMEM((2, ranks, own, cols), LOW), pltpu.VMEM((ranks, own, cols), LOW)]


class Deliver:
    def __init__(self, rows, out, cols, ranks, sems):
        self.rows, self.out, self.cols, self.ranks = rows, out, cols, ranks
        self.send, self.recv, self.here = sems
        self.seq, self.dp = lax.axis_index("seq"), lax.axis_index("dp")

    def exchange(self):
        for step in range(1, self.ranks):
            peer = lax.rem(self.seq + step, self.ranks)
            yield push(
                self.rows.at[peer, :, self.cols],
                self.out.at[self.seq, :, self.cols],
                self.send.at[step],
                self.recv.at[step],
                (peer, self.dp),
            )

    def keep(self):
        return pltpu.make_async_copy(
            self.rows.at[self.seq, :, self.cols], self.out.at[self.seq, :, self.cols], self.here
        )

    def start(self):
        self.keep().start()
        for copy in self.exchange():
            copy.start()

    def finish(self):
        self.keep().wait()
        for copy in self.exchange():
            copy.wait_recv()
        for copy in self.exchange():
            copy.wait_send()


def deliver_sems(ranks):
    return [pltpu.SemaphoreType.DMA((ranks,)), pltpu.SemaphoreType.DMA((ranks,)), pltpu.SemaphoreType.DMA]


def first_kernel(
    ranks, kv_heads, order, starts, tokens, out_grad, freqs, attn_gain, mlp_gain, query_gain, key_gain,
    w_query, w_key, w_value, w_output, w_gate, w_up, w_down,
    resid, second, cosv, sinv, q_low, k_low, v_low, own_out, first_in, qkv, attn_block, dy_all, prob, mlp_block, out_all,
    held, normal, kept, block, a_rows, m_rows, gate, up, down, dys, probs, pos, begins, pos_row,
    out_low, whole, *sems,
):
    local, width = tokens.shape
    rows = local * ranks
    own = w_query.shape[0]
    size = freqs.shape[1]
    heads = q_low.shape[0]
    share = heads // kv_heads
    half = ranks // 2
    scale = 1.0 / math.sqrt(size)
    cols = (heads + 2 * kv_heads) * size
    deep = block.shape[1]
    row = functools.partial(block_row, local=local, ranks=ranks)
    seq, dp = lax.axis_index("seq"), lax.axis_index("dp")
    right, left = neighbours(ranks)
    attn = Spread(a_rows, block, ranks, own, pl.ds(0, a_rows.shape[2]), sems[12:17])
    third = m_rows.shape[2] // 3
    cuts = ((0, third), (third, third), (2 * third, third // 2), (2 * third + third // 2, third // 2))
    mlp = [
        Spread(m_rows, mlp_block, ranks, own, pl.ds(*cut), sems[17 + 5 * at : 22 + 5 * at])
        for at, cut in enumerate(cuts)
    ]
    local_sems = sems[37]
    out_send, out_recv = sems[2:4]
    o_cols = heads * size
    peers = [(lax.rem(seq + step, ranks), dp) for step in range(1, ranks)]
    peers += [(seq, attn.beside), (seq, attn.sibling)]
    knock(peers)
    loads = [
        move(src, dst, local_sems.at[at])
        for at, (src, dst) in enumerate(((w_gate, gate), (w_up, up), (w_down, down)))
    ]
    held[pl.ds(row(0), local)] = tokens[...]
    dys[pl.ds(row(0), local)] = out_grad[...]

    def column(line):
        same = lax.broadcasted_iota(jnp.int32, (own, own), 0) == lax.broadcasted_iota(jnp.int32, (own, own), 1)
        return jnp.sum(jnp.where(same, line, 0.0), 1, keepdims=True)

    def lay(target, begin, weight, gain):
        each = weight.shape[1] // ranks
        for rank in range(ranks):
            part = weight[:, rank * each : (rank + 1) * each]
            if gain is not None:
                part = (part.astype(jnp.float32) * gain).astype(LOW)
            target[rank, :, begin : begin + each] = part
        return begin + each

    gain = column(attn_gain[...])
    at = 0
    for weight in (w_query, w_key, w_value):
        at = lay(a_rows, at, weight, gain)
    whole[seq, pl.ds(pl.multiple_of(dp * own, own), own)] = w_output[...]
    answered(peers)
    ring = RingGather(held, local, ranks, sems[0], sems[1], right, left, row)
    ring.start(1)
    attn.start()
    outs = WholeGather(whole, ranks, own, [*sems[8:12], *sems[38:40]])
    outs.forward(0)
    line = LineGather(dys, local, ranks, sems[4], sems[5], sems[6], sems[7])
    stores = []

    def store(src, dst):
        stores.append(move(src, dst, local_sems.at[len(loads) + len(stores)]))

    def scale_rows(step):
        for rel in rels_of(step, ranks):

            def some(at, _):
                rows_at = pl.ds(pl.multiple_of(row(rel) + at * 32, 32), 32)
                normal[rows_at] = rows_scaled(held[rows_at].astype(jnp.float32))[0].astype(LOW)
                return 0

            lax.fori_loop(0, local // 32, some, 0)

    for load in loads:
        load.wait()
    gain = column(mlp_gain[...])
    each = gate.shape[1] // ranks
    lay(m_rows, 0, gate, gain)
    lay(m_rows, each, up, gain)
    lay(m_rows, 2 * each, down, None)
    scale_rows(0)
    def bring(step):
        outs.arrive(step)
        if step < half:
            outs.start(step + 1)
        outs.forward(step)

    def forward(piece):
        mlp[piece].arrive()
        mlp[piece].hop(0).start()
        mlp[piece].hop(1).start()

    def hop_over(piece):
        mlp[piece].hop(0).wait_recv()
        mlp[piece].hop(2).start()

    def pass_on(step):
        ring.advance(step)
        scale_rows(step)

    pass_on(1)
    line.start(1)
    pass_on(2)
    outs.start(1)
    attn.arrive()
    attn.hop(0).start()
    attn.hop(1).start()
    attn.hop(0).wait_recv()
    attn.hop(2).start()
    for step in range(3, half):
        pass_on(step)
    bring(1)
    pass_on(half)
    mlp[0].start()
    spans = order.shape[0]
    span = rows // spans
    for at in range(ranks):
        rows_at = pl.ds(at * local, local)
        ids = at * local + lax.broadcasted_iota(jnp.int32, (1, local), 1)
        where = jnp.zeros_like(ids)
        for slot in range(spans):
            inside = (ids >= slot * span) & (ids < (slot + 1) * span)
            where = where + jnp.where(inside, ids + (order[slot] - slot) * span, 0)
        begin = jnp.zeros_like(ids)
        for doc in range(starts.shape[1]):
            begin = jnp.maximum(begin, jnp.where(starts[0, doc] <= where, starts[0, doc], 0))
        pos_row[:, rows_at] = where
        across = jnp.broadcast_to(where, (local, local)).T
        pos[rows_at] = across[:, :1]
        begins[rows_at] = jnp.broadcast_to(begin, (local, local)).T[:, :1]
        angle = across[:, :1].astype(jnp.float32) * freqs[...]
        lane = lax.broadcasted_iota(jnp.int32, (local, size), 1)
        cosv[rows_at] = jnp.cos(angle)
        sine = jnp.sin(angle)
        sinv[rows_at] = jnp.where(lane < size // 2, -sine, sine)
    bring(2)
    line.advance(1)
    attn.hop(1).wait_recv()
    attn.hop(2).wait_recv()
    store(block, attn_block)

    def project(begin, count):
        rows_at = pl.ds(begin, count)
        kept[rows_at] = dot_nn(normal[rows_at], block[...].reshape(width, cols))

    store(normal, first_in)
    tile = rows // half

    def rotated(at, rows_at, gain):
        v = rows_scaled(kept[rows_at, at * size : (at + 1) * size])[0] * gain[...]
        return (v * cosv[rows_at] + turn(v) * sinv[rows_at]).astype(LOW)

    for piece in range(half):
        rows_at = pl.ds(piece * tile, tile)
        project(piece * tile, tile)
        for head in range(heads):
            q_low[head, rows_at] = rotated(head, rows_at, query_gain)
        for group in range(kv_heads):
            k_low[group, rows_at] = rotated(heads + group, rows_at, key_gain)
            at = (heads + kv_heads + group) * size
            v_low[group, rows_at] = kept[rows_at, at : at + size].astype(LOW)
    store(kept, qkv)
    forward(0)

    for piece in range(half):
        rows_at = pl.ds(piece * tile, tile)
        seen = (pos_row[...] <= pos[rows_at]) & (pos_row[...] >= begins[rows_at])
        for head in range(heads):
            raw = dot_nt(q_low[head, rows_at], k_low[head // share]) * scale
            raw = jnp.where(seen, raw, NEG)
            weight = jnp.exp(raw - jnp.max(raw, -1, keepdims=True))
            weight = (weight * (1.0 / jnp.sum(weight, -1, keepdims=True))).astype(LOW)
            probs[head, rows_at] = weight
            value = dot_nn(weight, v_low[head // share])
            out_low[rows_at, head * size : (head + 1) * size] = value.astype(LOW)
            store(probs.at[head, rows_at], prob.at[head, rows_at])
        if piece == 0:
            bring(3)
        if piece == 1:
            mlp[1].start()
            line.advance(2)
            bring(half)
    mlp[2].start()
    mlp[3].start()
    hop_over(0)
    forward(1)
    forward(2)
    place = ring_place(seq, ranks)

    def exchange(rel):
        to = ring_seq(lax.rem(place + rel, ranks), ranks)
        return push(
            out_low.at[pl.ds(row(rel), local)],
            own_out.at[:, pl.ds(pl.multiple_of(seq * o_cols, o_cols), o_cols)],
            out_send.at[rel],
            out_recv.at[rel],
            (to, dp),
        )

    for rel in range(1, ranks):
        exchange(rel).start()
    own_out[:, pl.ds(pl.multiple_of(seq * o_cols, o_cols), o_cols)] = out_low[pl.ds(row(0), local)]
    forward(3)
    outs.complete()
    store(whole, out_all)
    hop_over(1)
    hop_over(2)
    for step in range(3, half):
        line.advance(step)

    def columns_of(rel):
        return pl.ds(pl.multiple_of(ring_seq(lax.rem(place + rel, ranks), ranks) * o_cols, o_cols), o_cols)

    def join(rels):
        def some(at, _):
            tile_cols = pl.ds(pl.multiple_of(at * deep, deep), deep)
            parts = jnp.concatenate([own_out[:, columns_of(rel)] for rel in rels], 1)
            weights = jnp.concatenate([whole[at, :, columns_of(rel)] for rel in rels], 1)
            before = tokens[:, tile_cols].astype(jnp.float32) if 0 in rels else resid[:, tile_cols]
            resid[:, tile_cols] = before + dot_nt(parts, weights)
            return 0

        lax.fori_loop(0, ranks, some, 0)

    near = ring_order(ranks)
    for at in range(0, ranks, 2):
        for rel in near[at : at + 2]:
            if rel:
                exchange(ranks - rel).wait_recv()
        join(near[at : at + 2])

    def scale_second(at, _):
        rows_at = pl.ds(pl.multiple_of(at * 32, 32), 32)
        second[rows_at] = rows_scaled(resid[rows_at])[0].astype(LOW)
        return 0

    lax.fori_loop(0, local // 32, scale_second, 0)
    hop_over(3)
    line.complete()
    store(dys, dy_all)
    ring.finish()
    attn.finish()
    outs.finish()
    for rel in range(1, ranks):
        exchange(rel).wait_send()
    line.finish()
    for piece in mlp:
        piece.hop(1).wait_recv()
        piece.hop(2).wait_recv()
        piece.finish()
    for given in stores:
        given.wait()


def mlp_kernel(
    ranks, second, out_grad, rest, dys, mlp_block, block_out, dresid, dresid_low, own_grads,
    grads, from_core, from_y, held, weights, hidden, dgu, resid, dy_all,
    term, out_buf, in_buf, y_out, y_in, here, *sems,
):
    local, width = second.shape
    row = functools.partial(block_row, local=local, ranks=ranks)
    ff = hidden.shape[1]
    deep = weights.shape[1]
    half = ranks // 2
    right, left = neighbours(ranks)
    loads = [
        move(src, dst, here.at[at])
        for at, (src, dst) in enumerate(((mlp_block, weights), (dys, dy_all), (rest, resid)))
    ]
    seq, dp = lax.axis_index("seq"), lax.axis_index("dp")
    own = own_grads.shape[1]
    pieces = [
        Reduce(
            grads, from_core, from_y, own_grads, own, at * ranks // 4, ranks // 4, pl.ds(0, 3 * ff),
            sems[6 + 2 * at : 8 + 2 * at],
        )
        for at in range(4)
    ]
    peers = [right, left, (seq, pieces[0].beside), (seq, pieces[0].sibling)]
    knock(peers)
    held[pl.ds(row(0), local)] = second[...]
    answered(peers)
    ring = RingGather(held, local, ranks, sems[0], sems[1], right, left, row)
    ring.start(1)
    loads[0].wait()
    loads[1].wait()
    wide = 256

    def middle(step):
        rels = rels_of(step, ranks)

        def some(at, _):
            first = pl.multiple_of(at * wide, wide)
            given, dy = block_rows(held, rels, local, ranks), block_rows(dy_all, rels, local, ranks)
            gate = dot_nn(given, weights[:, :, pl.ds(first, wide)].reshape(width, wide))
            upper = dot_nn(given, weights[:, :, pl.ds(ff + first, wide)].reshape(width, wide))
            dmid = dot_nn(dy, weights[:, :, pl.ds(2 * ff + first, wide)].reshape(width, wide))
            sigma = 1.0 / (1.0 + jnp.exp(-gate))
            act = gate * sigma
            value = (act * upper).astype(LOW)
            dgate = (dmid * upper * (sigma * (1.0 + gate * (1.0 - sigma)))).astype(LOW)
            dupper = (dmid * act).astype(LOW)
            for at, rel in enumerate(rels):
                rows, some_rows = pl.ds(row(rel), local), slice(at * local, (at + 1) * local)
                hidden[rows, pl.ds(first, wide)] = value[some_rows]
                dgu[rows, pl.ds(first, wide)] = dgate[some_rows]
                dgu[rows, pl.ds(ff + first, wide)] = dupper[some_rows]
            return 0

        lax.fori_loop(0, ff // wide, some, 0)

    middle(0)
    for step in range(1, half + 1):
        ring.advance(step)
        middle(step)

    def back_part(rels, begin, end):
        def some(at, _):
            value = dot_nt(block_rows(dgu, rels, local, ranks), weights[at, :, : 2 * ff])
            term[: len(rels) * local, pl.ds(pl.multiple_of(at * deep, deep), deep)] = value
            return 0

        lax.fori_loop(begin, end, some, 0)

    def out_part(rels, begin, end):
        def some(at, _):
            value = dot_nt(block_rows(hidden, rels, local, ranks), weights[at, :, 2 * ff :])
            term[: len(rels) * local, pl.ds(pl.multiple_of(at * deep, deep), deep)] = value
            return 0

        lax.fori_loop(begin, end, some, 0)

    def weight_grads(first, count):
        def some(at, _):
            cols = pl.ds(pl.multiple_of(at * deep, deep), deep)
            grads[at, :, : 2 * ff] = dot_tn(held[:, cols], dgu[...]).astype(LOW)
            grads[at, :, 2 * ff :] = dot_tn(dy_all[:, cols], hidden[...]).astype(LOW)
            return 0

        lax.fori_loop(first, first + count, some, 0)

    back = RingSum(back_part, term, out_buf, in_buf, local, ranks, sems[2], sems[3], right, left)
    out = RingSum(out_part, term, y_out, y_in, local, ranks, sems[4], sems[5], right, left)
    for step in range(1, half + 1):
        back.compute(step)
        back.launch(step)
        out.compute(step)
        out.launch(step)
        made, passed, summed = (((0, 1), (2, 3), (), ()), ((), (0, 1), (2, 3), ()), ((), (), (0, 1), (2, 3)))
        for piece in (pieces[at] for at in made[step - 1]):
            weight_grads(piece.begin, piece.count)
            piece.first()
        for at in passed[step - 1]:
            pieces[at].second()
        for at in summed[step - 1]:
            pieces[at].third()
    back.compute(half + 1)
    loads[2].wait()
    back.arrive_last()

    def finish_back(at, _):
        begin = pl.multiple_of(at * 32, 32)
        rows = pl.ds(begin, 32)
        value = resid[rows]
        inv = rows_scaled(value)[1]
        grad = back.last(begin, 32)
        full = out_grad[rows].astype(jnp.float32) + rows_scaled_back(value, inv, grad)
        dresid[rows] = full
        dresid_low[rows] = full.astype(LOW)
        return 0

    lax.fori_loop(0, local // 32, finish_back, 0)
    out.compute(half + 1)
    out.arrive_last()

    def finish_out(at, _):
        begin = pl.multiple_of(at * 32, 32)
        rows = pl.ds(begin, 32)
        block_out[rows] = (resid[rows] + out.last(begin, 32)).astype(LOW)
        return 0

    lax.fori_loop(0, local // 32, finish_out, 0)
    ring.finish()
    back.finish()
    out.finish()
    for piece in pieces:
        piece.finish()


def back_kernel(
    ranks, kv_heads, tokens, dresid_low, query_gain, key_gain, own_out, first_in_in, block_in,
    qkv_in, cos_in, sin_in, q_in, k_in, v_in, prob_in, dresid_in, mlp_own, out_all,
    tokens_grad, gains, out_grad, mlp_sums, attn_sums,
    grads, from_core, from_y, own_grads, query_gain_grad, key_gain_grad,
    tile, tiles_in, tile_sum, tile_sums_in, dob, dout, dk, dv, dqkv,
    first_in, attn_block, qkv, cosv, sinv, q_low, k_low, v_low, prob, dresid, term, out_buf, in_buf,
    o_grads, o_core, o_y, o_own, o_term, o_out, o_in, *sems,
):
    local, width = tokens.shape
    rows = local * ranks
    half = ranks // 2
    size = cosv.shape[1]
    heads = q_low.shape[0]
    share = heads // kv_heads
    scale = 1.0 / math.sqrt(size)
    cols = (heads + 2 * kv_heads) * size
    deep = attn_block.shape[1]
    o_cols = heads * size
    right, left = neighbours(ranks)
    seq, dp = lax.axis_index("seq"), lax.axis_index("dp")
    own = mlp_own.shape[1]
    copies = lax.axis_size("dp")
    row = functools.partial(block_row, local=local, ranks=ranks)
    place = ring_place(seq, ranks)
    out_piece = Reduce(o_grads, o_core, o_y, o_own, own, 0, ranks, pl.ds(0, width), sems[4:6])
    qkv_piece = Reduce(grads, from_core, from_y, own_grads, own, 0, ranks, pl.ds(0, cols), sems[6:8])
    third = mlp_own.shape[2] // 3
    mlp_ways = [
        Deliver(mlp_own, mlp_sums, pl.ds(at * third, third), ranks, [*sems[8:11], *sems[22:28]][3 * at : 3 * at + 3])
        for at in range(3)
    ]
    dob_send, dob_recv = sems[0:2]
    qkv_way = Deliver(own_grads, attn_sums, pl.ds(0, cols), ranks, sems[14:17])
    peers = [(lax.rem(seq + step, ranks), dp) for step in range(1, ranks)]
    peers += [(seq, lax.rem(dp + step, copies)) for step in range(1, copies)]
    knock(peers)
    local_sems = sems[21]
    loads = {}
    for at, (name, src, dst) in enumerate(
        (
            ("out", out_all, o_grads), ("block", block_in, attn_block), ("v", v_in, v_low),
            ("prob", prob_in, prob), ("k", k_in, k_low), ("q", q_in, q_low), ("cos", cos_in, cosv),
            ("sin", sin_in, sinv), ("qkv", qkv_in, qkv), ("first", first_in_in, first_in),
            ("dresid", dresid_in, dresid),
        )
    ):
        loads[name] = move(src, dst, local_sems.at[at])
    answered(peers)
    mlp_ways[0].start()
    loads["out"].wait()

    def columns_of(rank):
        return pl.ds(pl.multiple_of(rank * o_cols, o_cols), o_cols)

    def owner(rel):
        return ring_seq(lax.rem(place + rel, ranks), ranks)

    def exchange(rel):
        to = owner(rel)
        return push(
            dob.at[:, columns_of(to)], dout.at[pl.ds(row(0), local)], dob_send.at[rel], dob_recv.at[rel], (to, dp)
        )

    def project(rel):
        some = columns_of(owner(rel))
        dob[:, some] = dot_nn(dresid_low[...], o_grads[:, :, some].reshape(width, o_cols)).astype(LOW)

    for rel in (*ring_order(ranks)[1:][::-1], 0):
        project(rel)
        if rel:
            exchange(rel).start()
    dout[pl.ds(row(0), local)] = dob[:, columns_of(seq)]

    def out_grads(at, _):
        some_cols = pl.ds(pl.multiple_of(at * deep, deep), deep)
        o_grads[at] = dot_tn(dresid_low[:, some_cols], own_out[...]).astype(LOW)
        return 0

    lax.fori_loop(0, ranks, out_grads, 0)
    out_piece.first()
    out_piece.second()
    for rel in range(1, ranks):
        exchange(rel).wait_recv()
    for name in ("v", "prob", "k", "q", "cos", "sin", "qkv"):
        loads[name].wait()
    mlp_ways[1].start()
    tall = rows // half
    query_gain_grad[...] = jnp.zeros_like(query_gain_grad)
    key_gain_grad[...] = jnp.zeros_like(key_gain_grad)

    def unrotated(grad, column, rows_at, gain, gain_grad_ref):
        grad = grad * cosv[rows_at] - turn(grad) * sinv[rows_at]
        value = qkv[rows_at, column * size : (column + 1) * size]
        normal, inv = rows_scaled(value)
        gain_grad_ref[...] += jnp.sum(grad * normal, 0, keepdims=True)
        back = rows_scaled_back(value, inv, grad * gain[...])
        dqkv[rows_at, column * size : (column + 1) * size] = back.astype(LOW)

    for head in range(heads):
        group = head // share

        def one(piece, _):
            rows_at = pl.ds(pl.multiple_of(piece * tall, tall), tall)
            weight = prob[head, rows_at]
            grad = dout[rows_at, head * size : (head + 1) * size]
            dprob = dot_nt(grad, v_low[group])
            full = weight.astype(jnp.float32)
            delta = jnp.sum(full * dprob, -1, keepdims=True)
            dscore = (full * (dprob - delta)).astype(LOW)
            dq = dot_nn(dscore, k_low[group]) * scale
            dk_add = dot_tn(dscore, q_low[head, rows_at]) * scale
            dv_add = dot_tn(weight, grad)
            dk[group] += dk_add
            dv[group] += dv_add
            unrotated(dq, head, rows_at, query_gain, query_gain_grad)
            return 0

        if head % share == 0:
            dk[group] = jnp.zeros_like(dk[group])
            dv[group] = jnp.zeros_like(dv[group])
        lax.fori_loop(0, half, one, 0)
        if head == 0:
            mlp_ways[2].start()
    for group in range(kv_heads):
        def one_key(piece, _):
            rows_at = pl.ds(pl.multiple_of(piece * tall, tall), tall)
            unrotated(dk[group, rows_at], heads + group, rows_at, key_gain, key_gain_grad)
            at = (heads + kv_heads + group) * size
            dqkv[rows_at, at : at + size] = dv[group, rows_at].astype(LOW)
            return 0

        lax.fori_loop(0, half, one_key, 0)

    def part(rels, begin, end):
        def some(at, _):
            value = dot_nt(block_rows(dqkv, rels, local, ranks), attn_block[at])
            term[: len(rels) * local, pl.ds(pl.multiple_of(at * deep, deep), deep)] = value
            return 0

        lax.fori_loop(begin, end, some, 0)

    def qkv_grads(at, _):
        some_cols = pl.ds(pl.multiple_of(at * deep, deep), deep)
        grads[at] = dot_tn(first_in[:, some_cols], dqkv[...]).astype(LOW)
        return 0

    def to_ranks(step):
        peer = lax.rem(seq + step, ranks)
        return push(tile, tiles_in.at[seq], sems[17].at[step], sems[18].at[step], (peer, dp))

    def to_copies(step):
        peer = lax.rem(dp + step, copies)
        return push(
            tile_sum, tile_sums_in.at[dp], sems[19].at[step], sems[20].at[step], (seq, peer)
        )

    tile[0:1] = query_gain_grad[...]
    tile[1:2] = key_gain_grad[...]
    tile[2:] = jnp.zeros((tile.shape[0] - 2, size), jnp.float32)
    for step in range(1, ranks):
        to_ranks(step).start()
    tiles_in[seq] = tile[...]
    loads["block"].wait()

    def out_part(rels, begin, end):
        for at, rel in enumerate(rels):
            o_term[at * own : (at + 1) * own] = o_own[owner(rel)].astype(jnp.float32)

    out_total = RingSum(out_part, o_term, o_out, o_in, own, ranks, sems[30], sems[31], right, left)
    totals = two_sums(part, term, out_buf, in_buf, local, ranks, [*sems[2:4], *sems[28:30]], right, left)
    for step in range(1, half + 1):
        for total in totals:
            total.compute(step)
            total.launch(step)
        if step == 1:
            loads["first"].wait()
            lax.fori_loop(0, ranks, qkv_grads, 0)
            qkv_piece.first()
            qkv_piece.second()
        if step == 2:
            out_piece.third()
            for other in range(1, ranks):
                to_ranks(other).wait_recv()
            tile_sum[...] = jnp.sum(tiles_in[...], 0)
            for other in range(1, copies):
                to_copies(other).start()
            tile_sums_in[dp] = tile_sum[...]
        if step == half - 1:
            for other in range(1, copies):
                to_copies(other).wait_recv()
            gains[...] = jnp.sum(tile_sums_in[...], 0)
        if step > 1:
            out_total.compute(step - 1)
            out_total.launch(step - 1)
    out_total.compute(half)
    out_total.launch(half)
    qkv_piece.third()
    qkv_way.start()
    for total in totals:
        total.compute(half + 1)
    loads["dresid"].wait()
    for total in totals:
        total.arrive_last()

    def last(at, _):
        begin = pl.multiple_of(at * 32, 32)
        rows_at = pl.ds(begin, 32)
        value = tokens[rows_at].astype(jnp.float32)
        inv = rows_scaled(value)[1]
        grad = jnp.concatenate([total.last(begin, 32) for total in totals], 1)
        tokens_grad[rows_at] = dresid[rows_at] + rows_scaled_back(value, inv, grad)
        return 0

    lax.fori_loop(0, local // 32, last, 0)
    out_total.compute(half + 1)
    out_total.arrive_last()
    out_grad[...] = out_total.last(0, own)
    for step in range(1, ranks):
        to_ranks(step).wait_send()
    for step in range(1, copies):
        to_copies(step).wait_send()
    out_total.finish()
    for rel in range(1, ranks):
        exchange(rel).wait_send()
    for total in totals:
        total.finish()
    out_piece.finish()
    qkv_piece.finish()
    for way in mlp_ways:
        way.finish()
    qkv_way.finish()


def leave_kernel(
    attn_sums, mlp_sums, gains, attn_gain, mlp_gain, w_query, w_key, w_value, w_gate, w_up,
    query_out, key_out, value_out, gate_out, up_out, down_out, attn_out, mlp_out,
    head_query_out, head_key_out,
):
    own = attn_gain.shape[1]
    same = lax.broadcasted_iota(jnp.int32, (own, own), 0) == lax.broadcasted_iota(jnp.int32, (own, own), 1)

    @pl.when(pl.program_id(0) == 0)
    def _():
        attn_out[...] = jnp.zeros_like(attn_out)
        mlp_out[...] = jnp.zeros_like(mlp_out)
        head_query_out[...] = gains[0:1]
        head_key_out[...] = gains[1:2]

    for sums, gain, gain_out, parts in (
        (attn_sums, attn_gain, attn_out, ((query_out, w_query), (key_out, w_key), (value_out, w_value))),
        (mlp_sums, mlp_gain, mlp_out, ((gate_out, w_gate), (up_out, w_up), (down_out, None))),
    ):
        scale = jnp.sum(jnp.where(same, gain[...], 0.0), 1, keepdims=True)
        for rank in range(sums.shape[0]):
            at = 0
            for out, weight in parts:
                each = out.shape[1] // sums.shape[0]
                cols = slice(rank * each, (rank + 1) * each)
                value = sums[rank, :, at : at + each].astype(jnp.float32)
                at += each
                if weight is None:
                    out[:, cols] = value
                    continue
                out[:, cols] = value * scale
                inner = jnp.sum(value * weight[:, cols].astype(jnp.float32), 1, keepdims=True)
                gain_out[...] += jnp.sum(jnp.where(same, inner, 0.0), 0, keepdims=True)


VM = pl.BlockSpec(memory_space=pltpu.VMEM)
SM = pl.BlockSpec(memory_space=pltpu.SMEM)
ANY = pl.BlockSpec(memory_space=pl.ANY)


def call(kernel, number, ins, outs, scratch, operands):
    return pl.pallas_call(
        kernel,
        out_shape=[jax.ShapeDtypeStruct(shape, dtype) for shape, dtype, _ in outs],
        in_specs=ins,
        out_specs=[spec for _, _, spec in outs],
        scratch_shapes=scratch,
        compiler_params=pltpu.CompilerParams(
            collective_id=number, has_side_effects=True, vmem_limit_bytes=LIMIT
        ),
    )(*operands)


def columns_body(
    tokens,
    out_grad,
    span_order,
    doc_starts,
    w_query,
    w_key,
    w_value,
    w_output,
    attn_gain,
    query_gain,
    key_gain,
    w_gate,
    w_up,
    w_down,
    mlp_gain,
):
    ranks = lax.axis_size("seq")
    copies = lax.axis_size("dp")
    _, local, width = tokens.shape
    rows = local * ranks
    size = query_gain.shape[0]
    kv_heads = w_key.shape[1] // size // ranks
    heads = w_query.shape[1] // size // ranks
    q_cols, kv_cols = heads * size, kv_heads * size
    qkv_cols = q_cols + 2 * kv_cols
    ff = w_gate.shape[1] // ranks
    own = width // (ranks * copies)
    deep = own * copies
    half = ranks // 2
    f32, i32 = jnp.float32, jnp.int32
    exponents = np.arange(size) % (size // 2) * (-2.0 / size * math.log(1000000.0))
    freqs = jnp.asarray(np.exp(exponents)[None], f32)
    q_gain, k_gain = query_gain[None], key_gain[None]
    (
        resid, second, cosv, sinv, q_low, k_low, v_low, own_out, first_in, qkv, attn_block, dy_all, prob, mlp_block,
        out_all,
    ) = call(
        functools.partial(first_kernel, ranks, kv_heads),
        1,
        [SM, SM] + [VM] * 11 + [ANY] * 3,
        [
            ((local, width), f32, VM),
            ((local, width), LOW, VM),
            ((rows, size), f32, VM),
            ((rows, size), f32, VM),
            ((heads, rows, size), LOW, VM),
            ((kv_heads, rows, size), LOW, VM),
            ((kv_heads, rows, size), LOW, VM),
            ((local, q_cols * ranks), LOW, VM),
            ((rows, width), LOW, ANY),
            ((rows, qkv_cols), f32, ANY),
            ((ranks, deep, qkv_cols), LOW, ANY),
            ((rows, width), LOW, ANY),
            ((heads, rows, rows), LOW, ANY),
            ((ranks, deep, 3 * ff), LOW, ANY),
            ((ranks, deep, q_cols * ranks), LOW, ANY),
        ],
        [
            pltpu.VMEM((rows, width), LOW),
            pltpu.VMEM((rows, width), LOW),
            pltpu.VMEM((rows, qkv_cols), f32),
            pltpu.VMEM((ranks, deep, qkv_cols), LOW),
            pltpu.VMEM((ranks, own, qkv_cols), LOW),
            pltpu.VMEM((ranks, own, 3 * ff), LOW),
        ]
        + [pltpu.VMEM((own, ff * ranks), LOW)] * 3
        + [
            pltpu.VMEM((rows, width), LOW),
            pltpu.VMEM((heads, rows, rows), LOW),
            pltpu.VMEM((rows, 1), i32),
            pltpu.VMEM((rows, 1), i32),
            pltpu.VMEM((1, rows), i32),
            pltpu.VMEM((rows, q_cols), LOW),
            pltpu.VMEM((ranks, deep, q_cols * ranks), LOW),
        ]
        + ring_sems(ranks)
        + [pltpu.SemaphoreType.DMA((ranks,))] * 2
        + line_sems(ranks)
        + whole_sems(ranks)[:4]
        + spread_sems(ranks) * 5
        + [pltpu.SemaphoreType.DMA((heads * half + 8,))]
        + whole_sems(ranks)[4:],
        (
            span_order, doc_starts, tokens[0], out_grad[0], freqs, attn_gain[None], mlp_gain[None], q_gain, k_gain,
            w_query, w_key, w_value, w_output, w_gate, w_up, w_down,
        ),
    )
    block_out, dresid, dresid_low, mlp_own = call(
        functools.partial(mlp_kernel, ranks),
        2,
        [VM, VM, ANY, ANY, ANY],
        [
            ((local, width), LOW, VM),
            ((local, width), f32, VM),
            ((local, width), LOW, VM),
            ((ranks, own, 3 * ff), LOW, VM),
        ],
        [pltpu.VMEM((ranks, deep, 3 * ff), LOW)]
        + reduce_bufs(ranks, own, 3 * ff)
        + [
            pltpu.VMEM((rows, width), LOW),
            pltpu.VMEM((ranks, deep, 3 * ff), LOW),
            pltpu.VMEM((rows, ff), LOW),
            pltpu.VMEM((rows, 2 * ff), LOW),
            pltpu.VMEM((local, width), f32),
            pltpu.VMEM((rows, width), LOW),
        ]
        + sum_bufs(local, ranks, width)
        + sum_bufs(local, ranks, width)[1:]
        + [pltpu.SemaphoreType.DMA((3,))]
        + ring_sems(ranks) * 3
        + reduce_sems() * 4,
        (second, out_grad[0], resid, dy_all, mlp_block),
    )
    tokens_grad, gains, wo_grad, mlp_sums, attn_sums = call(
        functools.partial(back_kernel, ranks, kv_heads),
        3,
        [VM] * 5 + [ANY] * 12,
        [
            ((local, width), f32, VM),
            ((8, size), f32, VM),
            ((own, q_cols * ranks), f32, VM),
            ((ranks, own, 3 * ff), LOW, ANY),
            ((ranks, own, qkv_cols), LOW, VM),
        ],
        [pltpu.VMEM((ranks, deep, qkv_cols), LOW)]
        + reduce_bufs(ranks, own, qkv_cols)
        + [
            pltpu.VMEM((ranks, own, qkv_cols), LOW),
            pltpu.VMEM((1, size), f32),
            pltpu.VMEM((1, size), f32),
            pltpu.VMEM((8, size), f32),
            pltpu.VMEM((ranks, 8, size), f32),
            pltpu.VMEM((8, size), f32),
            pltpu.VMEM((copies, 8, size), f32),
            pltpu.VMEM((local, q_cols * ranks), LOW),
            pltpu.VMEM((rows, q_cols), LOW),
            pltpu.VMEM((kv_heads, rows, size), f32),
            pltpu.VMEM((kv_heads, rows, size), f32),
            pltpu.VMEM((rows, qkv_cols), LOW),
            pltpu.VMEM((rows, width), LOW),
            pltpu.VMEM((ranks, deep, qkv_cols), LOW),
            pltpu.VMEM((rows, qkv_cols), f32),
            pltpu.VMEM((rows, size), f32),
            pltpu.VMEM((rows, size), f32),
            pltpu.VMEM((heads, rows, size), LOW),
            pltpu.VMEM((kv_heads, rows, size), LOW),
            pltpu.VMEM((kv_heads, rows, size), LOW),
            pltpu.VMEM((heads, rows, rows), LOW),
            pltpu.VMEM((local, width), f32),
        ]
        + sum_bufs(local, ranks, width)
        + [pltpu.VMEM((ranks, deep, q_cols * ranks), LOW)]
        + reduce_bufs(ranks, own, q_cols * ranks)
        + [pltpu.VMEM((ranks, own, q_cols * ranks), LOW)]
        + sum_bufs(own, ranks, q_cols * ranks)
        + [pltpu.SemaphoreType.DMA((ranks,))] * 2
        + ring_sems(ranks)
        + reduce_sems() * 2
        + deliver_sems(ranks) * 3
        + [pltpu.SemaphoreType.DMA((ranks,))] * 2
        + [pltpu.SemaphoreType.DMA((copies,))] * 2
        + [pltpu.SemaphoreType.DMA((11,))]
        + deliver_sems(ranks) * 2
        + ring_sems(ranks) * 2,
        (
            tokens[0], dresid_low, q_gain, k_gain, own_out, first_in, attn_block, qkv, cosv, sinv, q_low, k_low,
            v_low, prob, dresid, mlp_own, out_all,
        ),
    )
    whole = pl.BlockSpec((1, own), lambda at: (0, 0))
    each = (q_cols, kv_cols, kv_cols, ff, ff, ff)
    many = 2
    columns = [pl.BlockSpec((own, many * cols), lambda at: (0, at)) for cols in each]
    head = pl.BlockSpec((1, size), lambda at: (0, 0))
    *grads, dga, dgm, dgq, dgk = pl.pallas_call(
        leave_kernel,
        grid=(ranks // many,),
        out_shape=[jax.ShapeDtypeStruct((own, cols * ranks), f32) for cols in each]
        + [jax.ShapeDtypeStruct((1, own), f32)] * 2
        + [jax.ShapeDtypeStruct((1, size), f32)] * 2,
        in_specs=[
            pl.BlockSpec((many, own, qkv_cols), lambda at: (at, 0, 0)),
            pl.BlockSpec((many, own, 3 * ff), lambda at: (at, 0, 0)),
            pl.BlockSpec((8, size), lambda at: (0, 0)),
            whole,
            whole,
            *columns[:3],
            *columns[3:5],
        ],
        out_specs=columns + [whole, whole, head, head],
    )(attn_sums, mlp_sums, gains, attn_gain[None], mlp_gain[None], w_query, w_key, w_value, w_gate, w_up)
    return (
        block_out[None], tokens_grad[None], *grads[:3], wo_grad, dga[0], dgq[0], dgk[0], *grads[3:], dgm[0],
    )


def body(*args):
    tokens, w_key, query_gain = args[0], args[5], args[9]
    groups = w_key.shape[1] // query_gain.shape[0]
    ranks = lax.axis_size("seq")
    if tokens.shape[0] == 1 and ranks % 2 == 0 and groups % ranks == 0 and lax.axis_size("dp") == 4:
        return columns_body(*args)
    return gathered_body(*args)


def solution(mesh):
    return jax.shard_map(
        body,
        mesh=mesh,
        in_specs=(
            P("dp", "seq", None),
            P("dp", "seq", None),
            P(),
            P("dp", None),
            P(("seq", "dp"), None),
            P(("seq", "dp"), None),
            P(("seq", "dp"), None),
            P(("seq", "dp"), None),
            P(("seq", "dp")),
            P(),
            P(),
            P(("seq", "dp"), None),
            P(("seq", "dp"), None),
            P(("seq", "dp"), None),
            P(("seq", "dp")),
        ),
        out_specs=(
            P("dp", "seq", None),
            P("dp", "seq", None),
            P(("seq", "dp"), None),
            P(("seq", "dp"), None),
            P(("seq", "dp"), None),
            P(("seq", "dp"), None),
            P(("seq", "dp")),
            P(),
            P(),
            P(("seq", "dp"), None),
            P(("seq", "dp"), None),
            P(("seq", "dp"), None),
            P(("seq", "dp")),
        ),
        check_vma=False,
    )
```

```python
import functools
import math

import jax
import jax.numpy as jnp
import numpy as np
from jax import lax
from jax.experimental import pallas as pl
from jax.experimental.pallas import tpu as pltpu
from jax.sharding import PartitionSpec as P

EPS = 1e-06
NEG = -1e30


def normed(v, gain):
    scale_inv = lax.rsqrt(jnp.mean(v * v, -1, keepdims=True) + EPS)
    return (v * scale_inv * gain, scale_inv)


def norm_back(v, scale_inv, gain, grad):
    scaled = grad * gain
    inner = jnp.mean(scaled * v, -1, keepdims=True)
    dv = scale_inv * scaled - v * scale_inv * scale_inv * scale_inv * inner
    dgain = jnp.sum((grad * v * scale_inv).reshape(-1, v.shape[-1]), 0)
    return (dv, dgain)


def rotary(pos, width):
    half = width // 2
    freqs = jnp.exp(jnp.arange(half, dtype=jnp.float32) * (-2.0 / width * math.log(1000000.0)))
    angle = pos.astype(jnp.float32)[:, None] * freqs[None, :]
    return (jnp.cos(angle)[:, None, :], jnp.sin(angle)[:, None, :])


def rotate(v, cosv, sinv):
    half = v.shape[-1] // 2
    first, second = (v[..., :half], v[..., half:])
    return jnp.concatenate([first * cosv - second * sinv, second * cosv + first * sinv], -1)


def rotate_back(grad, cosv, sinv):
    half = grad.shape[-1] // 2
    first, second = (grad[..., :half], grad[..., half:])
    return jnp.concatenate([first * cosv + second * sinv, second * cosv - first * sinv], -1)


def place(order, begin, count, span):
    rows = begin + jnp.arange(count, dtype=jnp.int32)
    slots = rows // span
    picked = slots[:, None] == jnp.arange(order.shape[0], dtype=jnp.int32)[None, :]
    return jnp.sum(jnp.where(picked, order[None, :], 0), -1) * span + rows % span


def doc_of(starts, pos):
    return jnp.sum((starts[:, None, :] <= pos[None, :, None]).astype(jnp.int32), -1)


def gathered_body(
    tokens,
    out_grad,
    span_order,
    doc_starts,
    w_query,
    w_key,
    w_value,
    w_output,
    attn_gain,
    query_gain,
    key_gain,
    w_gate,
    w_up,
    w_down,
    mlp_gain,
):
    seqs, local, width = tokens.shape
    span = local // 2
    head_size = query_gain.shape[0]
    kv_heads = w_key.shape[1] // head_size
    heads = w_query.shape[1] // head_size
    share = heads // kv_heads
    kv_width = kv_heads * head_size
    ff_width = w_gate.shape[1]
    scale = 1.0 / math.sqrt(head_size)
    total_rows = seqs * local
    own_rows = width // lax.axis_size(("seq", "dp"))
    qpos = place(span_order, lax.axis_index("seq") * local, local, span)
    qdoc = doc_of(doc_starts, qpos)
    cosv, sinv = rotary(qpos, head_size)

    def gather_attn():
        return (
            lax.all_gather(w_query, ("seq", "dp"), axis=0, tiled=True),
            lax.all_gather(w_key, ("seq", "dp"), axis=0, tiled=True),
            lax.all_gather(w_value, ("seq", "dp"), axis=0, tiled=True),
            lax.all_gather(w_output, ("seq", "dp"), axis=0, tiled=True),
            lax.all_gather(
                attn_gain.astype(jnp.bfloat16), ("seq", "dp"), axis=0, tiled=True
            ).astype(attn_gain.dtype),
        )

    def gather_mlp():
        return (
            lax.all_gather(w_gate, ("seq", "dp"), axis=0, tiled=True),
            lax.all_gather(w_up, ("seq", "dp"), axis=0, tiled=True),
            lax.all_gather(w_down, ("seq", "dp"), axis=0, tiled=True),
            lax.all_gather(mlp_gain.astype(jnp.bfloat16), ("seq", "dp"), axis=0, tiled=True).astype(
                mlp_gain.dtype
            ),
        )

    x_rows = tokens.astype(jnp.float32).reshape(total_rows, width)
    wq_all, wk_all, wv_all, wo_all, ga_all = gather_attn()
    first_norm, first_inv = normed(x_rows, ga_all)
    first_in = first_norm.astype(jnp.bfloat16)
    q_raw = jnp.dot(first_in, wq_all, preferred_element_type=jnp.float32).reshape(
        seqs, local, heads, head_size
    )
    k_raw = jnp.dot(first_in, wk_all, preferred_element_type=jnp.float32).reshape(
        seqs, local, kv_heads, head_size
    )
    v_low = (
        jnp.dot(first_in, wv_all, preferred_element_type=jnp.float32)
        .astype(jnp.bfloat16)
        .reshape(seqs, local, kv_heads, head_size)
    )
    q_normed, q_inv = normed(q_raw, query_gain)
    k_normed, k_inv = normed(k_raw, key_gain)
    q_low = rotate(q_normed, cosv, sinv).astype(jnp.bfloat16)
    k_low = rotate(k_normed, cosv, sinv).astype(jnp.bfloat16)
    q_group = q_low.reshape(seqs, local, kv_heads, share, head_size)

    def scores(piece_key, start):
        count = piece_key.shape[1]
        kpos = place(span_order, start, count, span)
        kdoc = doc_of(doc_starts, kpos)
        visible = (qdoc[:, :, None] == kdoc[:, None, :]) & (
            kpos[None, None, :] <= qpos[None, :, None]
        )
        raw = (
            jnp.einsum("sqgjd,skgd->sgjqk", q_group, piece_key, preferred_element_type=jnp.float32)
            * scale
        )
        return (raw, visible[:, None, None])

    start_top = jnp.full((seqs, kv_heads, share, local), NEG, jnp.float32)
    piece = (
        lax.all_gather(k_low, "seq", axis=1, tiled=True),
        lax.all_gather(v_low, "seq", axis=1, tiled=True),
    )
    top = start_top
    raw, visible = scores(piece[0], jnp.int32(0))
    raw = jnp.where(visible, raw, NEG)
    new_top = jnp.maximum(top, jnp.max(raw, -1))
    weights = jnp.where(visible, jnp.exp(raw - new_top[..., None]), 0.0)
    total = jnp.sum(weights, -1)
    summed = jnp.einsum(
        "sgjqk,skgd->sgjqd",
        weights.astype(jnp.bfloat16),
        piece[1],
        preferred_element_type=jnp.float32,
    )
    top, total, summed = (new_top, total, summed)
    log_total = top + jnp.log(total)
    attn_vals = summed / total[..., None]
    out_low = (
        jnp.transpose(attn_vals, (0, 3, 1, 2, 4))
        .reshape(total_rows, heads * head_size)
        .astype(jnp.bfloat16)
    )
    resid = x_rows + jnp.einsum("nh,dh->nd", out_low, wo_all, preferred_element_type=jnp.float32)
    wg_all, wu_all, wd_all, gm_all = gather_mlp()
    second_norm, second_inv = normed(resid, gm_all)
    second_in = second_norm.astype(jnp.bfloat16)
    gate = jnp.dot(second_in, wg_all, preferred_element_type=jnp.float32)
    upper = jnp.dot(second_in, wu_all, preferred_element_type=jnp.float32)
    sigma = jax.nn.sigmoid(gate)
    act = gate * sigma
    hidden = (act * upper).astype(jnp.bfloat16)
    result = resid + jnp.einsum("nf,df->nd", hidden, wd_all, preferred_element_type=jnp.float32)
    block_out = result.astype(jnp.bfloat16).reshape(seqs, local, width)
    grad_low = out_grad.reshape(total_rows, width)
    wg_all, wu_all, wd_all, gm_all = gather_mlp()
    dmid = jnp.einsum("nd,df->nf", grad_low, wd_all, preferred_element_type=jnp.float32)
    dgate = (dmid * upper * sigma * (1.0 + gate * (1.0 - sigma))).astype(jnp.bfloat16)
    dupper = (dmid * act).astype(jnp.bfloat16)
    left = second_in
    outer = grad_low
    mlp_sums = lax.psum_scatter(
        jnp.concatenate(
            [
                jnp.einsum("nd,nf->df", left, dgate, preferred_element_type=jnp.float32),
                jnp.einsum("nd,nf->df", left, dupper, preferred_element_type=jnp.float32),
                jnp.einsum("nd,nf->df", outer, hidden, preferred_element_type=jnp.float32),
            ],
            1,
        ),
        ("seq", "dp"),
        scatter_dimension=0,
        tiled=True,
    )
    dsecond = jnp.einsum(
        "nf,df->nd", dgate, wg_all, preferred_element_type=jnp.float32
    ) + jnp.einsum("nf,df->nd", dupper, wu_all, preferred_element_type=jnp.float32)
    dresid_norm, dgm = norm_back(resid, second_inv, gm_all, dsecond)
    dresid = grad_low.astype(jnp.float32) + dresid_norm
    dresid_low = dresid.astype(jnp.bfloat16)
    wq_all, wk_all, wv_all, wo_all, ga_all = gather_attn()
    dout_low = jnp.einsum(
        "nd,dh->nh", dresid_low, wo_all, preferred_element_type=jnp.float32
    ).astype(jnp.bfloat16)
    dout_group = dout_low.reshape(seqs, local, kv_heads, share, head_size)
    delta = jnp.sum(jnp.transpose(dout_group.astype(jnp.float32), (0, 2, 3, 1, 4)) * attn_vals, -1)
    piece = (
        lax.all_gather(k_low, "seq", axis=1, tiled=True),
        lax.all_gather(v_low, "seq", axis=1, tiled=True),
    )
    count = piece[0].shape[1]
    raw, visible = scores(piece[0], jnp.int32(0))
    prob = jnp.where(visible, jnp.exp(raw - log_total[..., None]), 0.0)
    dprob = jnp.einsum(
        "sqgjd,skgd->sgjqk", dout_group, piece[1], preferred_element_type=jnp.float32
    )
    dscore = (prob * (dprob - delta[..., None])).astype(jnp.bfloat16)
    dq_sum = jnp.einsum("sgjqk,skgd->sqgjd", dscore, piece[0], preferred_element_type=jnp.float32)
    dk_part = (
        jnp.einsum("sgjqk,sqgjd->skgd", dscore, q_group, preferred_element_type=jnp.float32) * scale
    )
    dv_part = jnp.einsum(
        "sgjqk,sqgjd->skgd",
        prob.astype(jnp.bfloat16),
        dout_group,
        preferred_element_type=jnp.float32,
    )
    joined = jnp.concatenate(
        [dk_part.reshape(seqs, count, kv_width), dv_part.reshape(seqs, count, kv_width)], -1
    )
    buffer = joined
    dq_sum, buffer = (dq_sum, buffer)
    key_sums = lax.psum_scatter(
        buffer.astype(jnp.bfloat16), "seq", scatter_dimension=1, tiled=True
    ).astype(jnp.float32)
    dq_rot = (dq_sum * scale).reshape(seqs, local, heads, head_size)
    dq_raw, dgq = norm_back(q_raw, q_inv, query_gain, rotate_back(dq_rot, cosv, sinv))
    dk_rot = key_sums[..., :kv_width].reshape(seqs, local, kv_heads, head_size)
    dk_raw, dgk = norm_back(k_raw, k_inv, key_gain, rotate_back(dk_rot, cosv, sinv))
    dq_low = dq_raw.reshape(total_rows, heads * head_size).astype(jnp.bfloat16)
    dk_low = dk_raw.reshape(total_rows, kv_width).astype(jnp.bfloat16)
    dv_low = key_sums[..., kv_width:].reshape(total_rows, kv_width).astype(jnp.bfloat16)
    left = first_in
    outer = dresid_low
    attn_sums = lax.psum_scatter(
        jnp.concatenate(
            [
                jnp.einsum("nd,nh->dh", left, dq_low, preferred_element_type=jnp.float32),
                jnp.einsum("nd,nh->dh", left, dk_low, preferred_element_type=jnp.float32),
                jnp.einsum("nd,nh->dh", left, dv_low, preferred_element_type=jnp.float32),
                jnp.einsum("nd,nh->dh", outer, out_low, preferred_element_type=jnp.float32),
            ],
            1,
        ),
        ("seq", "dp"),
        scatter_dimension=0,
        tiled=True,
    )
    dfirst = jnp.einsum("nh,dh->nd", dq_low, wq_all, preferred_element_type=jnp.float32)
    dfirst = dfirst + jnp.einsum("nh,dh->nd", dk_low, wk_all, preferred_element_type=jnp.float32)
    dfirst = dfirst + jnp.einsum("nh,dh->nd", dv_low, wv_all, preferred_element_type=jnp.float32)
    dx_norm, dga = norm_back(x_rows, first_inv, ga_all, dfirst)
    tokens_grad = (dresid + dx_norm).reshape(seqs, local, width)
    dga_all, dgm_all, dgq_all, dgk_all = lax.psum((dga, dgm, dgq, dgk), ("seq", "dp"))
    offset = lax.axis_index(("seq", "dp")) * own_rows
    attn_gain_grad = lax.dynamic_slice_in_dim(dga_all, offset, own_rows, 0)
    mlp_gain_grad = lax.dynamic_slice_in_dim(dgm_all, offset, own_rows, 0)
    q_cols = heads * head_size
    w_query_grad = attn_sums[:, :q_cols]
    w_key_grad = attn_sums[:, q_cols : q_cols + kv_width]
    w_value_grad = attn_sums[:, q_cols + kv_width : q_cols + 2 * kv_width]
    w_output_grad = attn_sums[:, q_cols + 2 * kv_width :]
    w_gate_grad = mlp_sums[:, :ff_width]
    w_up_grad = mlp_sums[:, ff_width : 2 * ff_width]
    w_down_grad = mlp_sums[:, 2 * ff_width :]
    return (
        block_out,
        tokens_grad,
        w_query_grad,
        w_key_grad,
        w_value_grad,
        w_output_grad,
        attn_gain_grad,
        dgq_all,
        dgk_all,
        w_gate_grad,
        w_up_grad,
        w_down_grad,
        mlp_gain_grad,
    )


LOW = jnp.bfloat16
MESH = pl.DeviceIdType.MESH
LIMIT = 60 * 2**20


def ring_order(ranks):
    half = ranks // 2
    order = [0]
    for step in range(1, half):
        order += [step, ranks - step]
    return order + [half]


def ring_place(seq, ranks):
    z, x = lax.div(seq, 2), lax.rem(seq, 2)
    return z + x * (ranks - 1 - 2 * z)


def ring_seq(place, ranks):
    half = ranks // 2
    x, z = lax.div(place, half), lax.rem(place, half)
    return 2 * (z + x * (half - 1 - 2 * z)) + x


def neighbours(ranks):
    seq, dp = lax.axis_index("seq"), lax.axis_index("dp")
    at = ring_place(seq, ranks)
    right = ring_seq(lax.rem(at + 1, ranks), ranks)
    left = ring_seq(lax.rem(at + ranks - 1, ranks), ranks)
    return (right, dp), (left, dp)


def knock(devices):
    barrier = pltpu.get_barrier_semaphore()
    for device in devices:
        pl.semaphore_signal(barrier, inc=1, device_id=device, device_id_type=MESH)


def answered(devices):
    pl.semaphore_wait(pltpu.get_barrier_semaphore(), len(devices))


def move(src, dst, sem):
    copy = pltpu.make_async_copy(src, dst, sem)
    copy.start()
    return copy


def push(src, dst, send, recv, device):
    return pltpu.make_async_remote_copy(
        src_ref=src, dst_ref=dst, send_sem=send, recv_sem=recv, device_id=device, device_id_type=MESH
    )


def dot_nn(left, right):
    return jnp.dot(left, right, preferred_element_type=jnp.float32)


def dot_nt(left, right):
    return lax.dot_general(left, right, (((1,), (1,)), ((), ())), preferred_element_type=jnp.float32)


def dot_tn(left, right):
    return lax.dot_general(left, right, (((0,), (0,)), ((), ())), preferred_element_type=jnp.float32)


def block_row(rel, local, ranks):
    place = ring_place(lax.axis_index("seq"), ranks)
    return pl.multiple_of(ring_seq(lax.rem(place + rel, ranks), ranks) * local, local)


def block_rows(ref, rels, local, ranks):
    blocks = [ref[pl.ds(block_row(rel, local, ranks), local)] for rel in rels]
    return blocks[0] if len(blocks) == 1 else jnp.concatenate(blocks, 0)


def rels_of(step, ranks):
    return [rel for rel in ring_order(ranks) if min(rel, ranks - rel) == step]


class RingGather:
    def __init__(self, buf, local, ranks, send, recv, right, left, row):
        self.buf, self.sub, self.half = buf, local // 2, ranks // 2
        self.send, self.recv, self.right, self.left = send, recv, right, left
        self.ranks, self.row = ranks, row

    def copies(self, step, part):
        ways = ((0, (self.ranks - step + 1) % self.ranks, self.right), (1, step - 1, self.left))
        given = []
        for way, rel, device in ways:
            if step < self.half or way == part:
                block = self.buf.at[pl.ds(self.row(rel) + part * self.sub, self.sub)]
                at = 2 * (step - 1) + part
                given.append(push(block, block, self.send.at[way, at], self.recv.at[way, at], device))
        return given

    def start(self, step):
        for part in range(2):
            for copy in self.copies(step, part):
                copy.start()

    def advance(self, step):
        for part in range(2):
            for copy in self.copies(step, part):
                copy.wait_recv()
            if step < self.half:
                for copy in self.copies(step + 1, part):
                    copy.start()

    def finish(self):
        for step in range(1, self.half + 1):
            for part in range(2):
                for copy in self.copies(step, part):
                    copy.wait_send()


class LineGather:
    def __init__(self, buf, local, ranks, send, recv, x_send, x_recv):
        self.buf, self.local, self.length = buf, local, ranks // 2
        self.send, self.recv, self.x_send, self.x_recv = send, recv, x_send, x_recv
        self.seq, self.dp = lax.axis_index("seq"), lax.axis_index("dp")
        self.z, self.x = lax.div(self.seq, 2), lax.rem(self.seq, 2)

    def block(self, z):
        return self.buf.at[pl.ds(pl.multiple_of((2 * z + self.x) * self.local, self.local), self.local)]

    def hop(self, way, step):
        block = self.block(self.z + (step - 1 if way else 1 - step))
        to = self.seq + (-2 if way else 2)
        return push(block, block, self.send.at[way, step - 1], self.recv.at[way, step - 1], (to, self.dp))

    def sends(self, way, step):
        if way:
            return (self.z > 0) & (self.z + step <= self.length)
        return (self.z < self.length - 1) & (self.z >= step - 1)

    def comes(self, way, step):
        return self.z + step < self.length if way else self.z >= step

    def across(self, way, step):
        block = self.block(self.z + (step if way else -step))
        at = step + way * (self.length - 1)
        return push(
            block, block, self.x_send.at[at], self.x_recv.at[at], (self.seq + 1 - 2 * self.x, self.dp)
        )

    def from_x(self, way, step):
        z = self.z + (step if way else -step)
        row = pl.multiple_of((2 * z + 1 - self.x) * self.local, self.local)
        block = self.buf.at[pl.ds(row, self.local)]
        at = step + way * (self.length - 1)
        return push(
            block, block, self.x_send.at[at], self.x_recv.at[at], (self.seq + 1 - 2 * self.x, self.dp)
        )

    def start(self, step):
        for way in range(2):
            pl.when(self.sends(way, step))(lambda way=way: self.hop(way, step).start())
        self.pass_on(step - 1)

    def pass_on(self, step):
        if step == 0:
            self.across(0, 0).start()
            return
        for way in range(2):
            pl.when(self.comes(way, step))(lambda way=way: self.across(way, step).start())

    def arrive(self, step):
        for way in range(2):
            pl.when(self.comes(way, step))(lambda way=way: self.incoming(way, step).wait_recv())

    def incoming(self, way, step):
        block = self.block(self.z + (step if way else -step))
        to = self.seq + 1 - 2 * self.x
        return push(block, block, self.send.at[way, step - 1], self.recv.at[way, step - 1], (to, self.dp))

    def run(self):
        for step in range(1, self.length):
            self.advance(step)

    def advance(self, step):
        self.arrive(step)
        if step < self.length - 1:
            self.start(step + 1)
        else:
            self.pass_on(step)

    def complete(self):
        self.from_x(0, 0).wait_recv()
        for step in range(1, self.length):
            for way in range(2):
                pl.when(self.comes(way, step))(lambda way=way: self.from_x(way, step).wait_recv())

    def finish(self):
        self.across(0, 0).wait_send()
        for step in range(1, self.length):
            for way in range(2):
                pl.when(self.sends(way, step))(lambda way=way: self.hop(way, step).wait_send())
                pl.when(self.comes(way, step))(lambda way=way: self.across(way, step).wait_send())


def line_sems(ranks):
    half = ranks // 2
    return [pltpu.SemaphoreType.DMA((2, half))] * 2 + [pltpu.SemaphoreType.DMA((2 * half,))] * 2


class RingSum:
    def __init__(self, part, term, out_buf, in_buf, local, ranks, send, recv, right, left, stream=0, streams=1):
        self.part, self.term, self.out_buf, self.in_buf = part, term, out_buf, in_buf
        self.local, self.ranks, self.half = local, ranks, ranks // 2
        each = term.shape[1] // streams
        self.cols = pl.ds(stream * each, each)
        self.tiles = (stream * ranks // streams, (stream + 1) * ranks // streams)
        self.send, self.recv, self.right, self.left = send, recv, right, left

    def copies(self, step):
        rows = self.local // 2 if step == 1 else self.local
        skip = self.local // 2 if step == 1 else 0
        return [
            push(
                self.out_buf.at[way, (step - 1) % 2, pl.ds(begin, rows), self.cols],
                self.in_buf.at[way, step - 1, pl.ds(begin, rows), self.cols],
                self.send.at[way, step - 1],
                self.recv.at[way, step - 1],
                device,
            )
            for way, begin, device in ((0, 0, self.right), (1, skip, self.left))
        ]

    def compute(self, step):
        if step == 1:
            self.part([self.half], *self.tiles)
        elif step <= self.half:
            self.part(rels_of(self.half + 1 - step, self.ranks), *self.tiles)
        else:
            self.part([0], *self.tiles)

    def launch(self, step):
        local, skip = self.local, self.local // 2
        if step > 2:
            for copy in self.copies(step - 2):
                copy.wait_send()
        if step == 1:
            for way in range(2):
                rows = pl.ds(way * skip, skip)
                self.out_buf[way, 0, rows, self.cols] = self.term[rows, self.cols].astype(LOW)
        else:
            for copy in self.copies(step - 1):
                copy.wait_recv()
            for way in range(2):
                for begin, with_sum in ((0, step > 2 or way == 0), (skip, step > 2 or way == 1)):
                    value = self.term[pl.ds(way * local + begin, skip), self.cols]
                    if with_sum:
                        value = value + self.in_buf[way, step - 2, pl.ds(begin, skip), self.cols].astype(jnp.float32)
                    self.out_buf[way, (step - 1) % 2, pl.ds(begin, skip), self.cols] = value.astype(LOW)
        for copy in self.copies(step):
            copy.start()

    def last(self, begin, count):
        rows = pl.ds(begin, count)
        value = self.term[rows, self.cols] + self.in_buf[0, self.half - 1, rows, self.cols].astype(jnp.float32)
        return value + self.in_buf[1, self.half - 1, rows, self.cols].astype(jnp.float32)

    def arrive_last(self):
        for copy in self.copies(self.half):
            copy.wait_recv()

    def finish(self):
        for step in range(max(1, self.half - 1), self.half + 1):
            for copy in self.copies(step):
                copy.wait_send()


def two_sums(part, term, out_buf, in_buf, local, ranks, sems, right, left):
    return [
        RingSum(
            part, term, out_buf, in_buf, local, ranks, sems[2 * at], sems[2 * at + 1], right, left, at, 2
        )
        for at in range(2)
    ]


def ring_sems(ranks):
    return [pltpu.SemaphoreType.DMA((2, ranks)), pltpu.SemaphoreType.DMA((2, ranks))]


def sum_bufs(local, ranks, width):
    return [
        pltpu.VMEM((2 * local, width), jnp.float32),
        pltpu.VMEM((2, 2, local, width), LOW),
        pltpu.VMEM((2, ranks // 2, local, width), LOW),
    ]


def turn(v):
    return pltpu.roll(v, v.shape[-1] // 2, v.ndim - 1)


def rows_scaled(v):
    inv = lax.rsqrt(jnp.mean(v * v, -1, keepdims=True) + EPS)
    return v * inv, inv


def rows_scaled_back(v, inv, grad):
    return inv * grad - v * (inv * inv * inv * jnp.mean(grad * v, -1, keepdims=True))


class Spread:
    def __init__(self, rows, block, ranks, own, cols, sems):
        self.rows, self.block, self.ranks, self.own, self.cols = rows, block, ranks, own, cols
        self.send, self.recv, self.hop_send, self.hop_recv, self.here = sems
        self.seq, self.dp = lax.axis_index("seq"), lax.axis_index("dp")
        y, core = lax.div(self.dp, 2), lax.rem(self.dp, 2)
        self.beside, self.sibling = (1 - y) * 2 + core, y * 2 + 1 - core

    def at(self, dp):
        return pl.ds(pl.multiple_of(dp * self.own, self.own), self.own)

    def exchange(self):
        for step in range(1, self.ranks):
            peer = lax.rem(self.seq + step, self.ranks)
            yield push(
                self.rows.at[peer, :, self.cols],
                self.block.at[self.seq, self.at(self.dp), self.cols],
                self.send.at[step],
                self.recv.at[step],
                (peer, self.dp),
            )

    def keep(self):
        return pltpu.make_async_copy(
            self.rows.at[self.seq, :, self.cols],
            self.block.at[self.seq, self.at(self.dp), self.cols],
            self.here,
        )

    def hop(self, number):
        dp = self.beside if number == 2 else self.dp
        part = self.block.at[:, self.at(dp), self.cols]
        to = self.beside if number == 0 else self.sibling
        return push(part, part, self.hop_send.at[number], self.hop_recv.at[number], (self.seq, to))

    def start(self):
        self.keep().start()
        for copy in self.exchange():
            copy.start()

    def arrive(self):
        self.keep().wait()
        for copy in self.exchange():
            copy.wait_recv()

    def finish(self):
        for copy in self.exchange():
            copy.wait_send()
        for number in range(3):
            self.hop(number).wait_send()


def spread_sems(ranks):
    return [
        pltpu.SemaphoreType.DMA((ranks,)),
        pltpu.SemaphoreType.DMA((ranks,)),
        pltpu.SemaphoreType.DMA((3,)),
        pltpu.SemaphoreType.DMA((3,)),
        pltpu.SemaphoreType.DMA,
    ]


class WholeGather:
    def __init__(self, block, ranks, own, sems):
        self.block, self.ranks, self.half, self.own = block, ranks, ranks // 2, own
        self.send, self.recv, self.y_send, self.y_recv, self.core_send, self.core_recv = sems
        self.seq, self.dp = lax.axis_index("seq"), lax.axis_index("dp")
        self.right, self.left = neighbours(ranks)
        self.place = ring_place(self.seq, ranks)
        y, core = lax.div(self.dp, 2), lax.rem(self.dp, 2)
        self.beside, self.sibling = (1 - y) * 2 + core, y * 2 + 1 - core

    def at(self, rel, dp, begin, count):
        seq = ring_seq(lax.rem(self.place + rel + self.ranks, self.ranks), self.ranks)
        return self.block.at[seq, pl.ds(pl.multiple_of(dp * self.own + begin, count), count)]

    def copies(self, step):
        last = step == self.half
        rows = self.own // 2 if last else self.own
        skip = self.own // 2 if last else 0
        given = []
        for way, rel, begin, device in ((0, 1 - step, 0, self.right), (1, step - 1, skip, self.left)):
            part = self.at(rel, self.dp, begin, rows)
            given.append(push(part, part, self.send.at[way, step - 1], self.recv.at[way, step - 1], device))
        return given

    def start(self, step):
        for copy in self.copies(step):
            copy.start()

    def hops(self, step):
        for at, rel in enumerate(ring_order(self.ranks)):
            if min(rel, self.ranks - rel) == step:
                part = self.at(rel, self.dp, 0, self.own)
                yield push(part, part, self.y_send.at[at], self.y_recv.at[at], (self.seq, self.beside))
                yield push(part, part, self.core_send.at[at], self.core_recv.at[at], (self.seq, self.sibling))

    def arrive(self, step):
        for copy in self.copies(step):
            copy.wait_recv()

    def forward(self, step):
        for copy in self.hops(step):
            copy.start()

    def cross(self):
        part = self.block.at[:, pl.ds(pl.multiple_of(self.beside * self.own, self.own), self.own)]
        at = self.ranks
        return push(part, part, self.core_send.at[at], self.core_recv.at[at], (self.seq, self.sibling))

    def complete(self):
        for step in range(self.half + 1):
            for copy in self.hops(step):
                copy.wait_recv()
        self.cross().start()
        self.cross().wait_recv()

    def finish(self):
        for step in range(1, self.half + 1):
            for copy in self.copies(step):
                copy.wait_send()
        for step in range(self.half + 1):
            for copy in self.hops(step):
                copy.wait_send()
        self.cross().wait_send()


def whole_sems(ranks):
    return (
        ring_sems(ranks)
        + [pltpu.SemaphoreType.DMA((ranks,))] * 2
        + [pltpu.SemaphoreType.DMA((ranks + 1,))] * 2
    )


class Reduce:
    def __init__(self, grads, from_core, from_y, total, own, first, count, cols, sems):
        self.grads, self.from_core, self.from_y, self.total = grads, from_core, from_y, total
        self.own, self.begin, self.count, self.cols = own, first, count, cols
        self.send, self.recv = sems
        self.seq, dp = lax.axis_index("seq"), lax.axis_index("dp")
        self.y, self.core = lax.div(dp, 2), lax.rem(dp, 2)
        self.beside, self.sibling = (1 - self.y) * 2 + self.core, self.y * 2 + 1 - self.core

    def at(self, y, core):
        return pl.ds(pl.multiple_of((y * 2 + core) * self.own, self.own), self.own)

    def hop(self, number):
        some, cols = pl.ds(self.begin, self.count), self.cols
        if number == 2:
            src, dst, to = self.from_core.at[0, some, :, cols], self.from_y.at[some, :, cols], self.beside
        else:
            rows = self.at(1 - self.y if number == 0 else self.y, 1 - self.core)
            src, dst, to = self.grads.at[some, rows, cols], self.from_core.at[number, some, :, cols], self.sibling
        return push(src, dst, self.send.at[number], self.recv.at[number], (self.seq, to))

    def first(self):
        self.hop(0).start()
        self.hop(1).start()

    def second(self):
        self.hop(0).wait_recv()
        rows = self.at(1 - self.y, self.core)

        def some(at, _):
            value = self.grads[at, rows, self.cols].astype(jnp.float32)
            value = value + self.from_core[0, at, :, self.cols].astype(jnp.float32)
            self.from_core[0, at, :, self.cols] = value.astype(LOW)
            return 0

        lax.fori_loop(self.begin, self.begin + self.count, some, 0)
        self.hop(2).start()

    def third(self):
        self.hop(1).wait_recv()
        self.hop(2).wait_recv()
        rows = self.at(self.y, self.core)

        def some(at, _):
            value = self.grads[at, rows, self.cols].astype(jnp.float32)
            value = value + self.from_core[1, at, :, self.cols].astype(jnp.float32)
            value = value + self.from_y[at, :, self.cols].astype(jnp.float32)
            self.total[at, :, self.cols] = value.astype(LOW)
            return 0

        lax.fori_loop(self.begin, self.begin + self.count, some, 0)

    def finish(self):
        for number in range(3):
            self.hop(number).wait_send()


def reduce_sems():
    return [pltpu.SemaphoreType.DMA((3,)), pltpu.SemaphoreType.DMA((3,))]


def reduce_bufs(ranks, own, cols):
    return [pltpu.VMEM((2, ranks, own, cols), LOW), pltpu.VMEM((ranks, own, cols), LOW)]


class Deliver:
    def __init__(self, rows, out, cols, ranks, sems):
        self.rows, self.out, self.cols, self.ranks = rows, out, cols, ranks
        self.send, self.recv, self.here = sems
        self.seq, self.dp = lax.axis_index("seq"), lax.axis_index("dp")

    def exchange(self):
        for step in range(1, self.ranks):
            peer = lax.rem(self.seq + step, self.ranks)
            yield push(
                self.rows.at[peer, :, self.cols],
                self.out.at[self.seq, :, self.cols],
                self.send.at[step],
                self.recv.at[step],
                (peer, self.dp),
            )

    def keep(self):
        return pltpu.make_async_copy(
            self.rows.at[self.seq, :, self.cols], self.out.at[self.seq, :, self.cols], self.here
        )

    def start(self):
        self.keep().start()
        for copy in self.exchange():
            copy.start()

    def finish(self):
        self.keep().wait()
        for copy in self.exchange():
            copy.wait_recv()
        for copy in self.exchange():
            copy.wait_send()


def deliver_sems(ranks):
    return [pltpu.SemaphoreType.DMA((ranks,)), pltpu.SemaphoreType.DMA((ranks,)), pltpu.SemaphoreType.DMA]


def first_kernel(
    ranks, kv_heads, order, starts, tokens, out_grad, freqs, attn_gain, mlp_gain, query_gain, key_gain,
    w_query, w_key, w_value, w_output, w_gate, w_up, w_down,
    resid, second, cosv, sinv, q_low, k_low, v_low, own_out, first_in, qkv, attn_block, dy_all, prob, mlp_block, out_all,
    held, normal, kept, block, a_rows, m_rows, gate, up, down, dys, probs, pos, begins, pos_row,
    out_low, whole, *sems,
):
    local, width = tokens.shape
    rows = local * ranks
    own = w_query.shape[0]
    size = freqs.shape[1]
    heads = q_low.shape[0]
    share = heads // kv_heads
    half = ranks // 2
    scale = 1.0 / math.sqrt(size)
    cols = (heads + 2 * kv_heads) * size
    deep = block.shape[1]
    row = functools.partial(block_row, local=local, ranks=ranks)
    seq, dp = lax.axis_index("seq"), lax.axis_index("dp")
    right, left = neighbours(ranks)
    attn = Spread(a_rows, block, ranks, own, pl.ds(0, a_rows.shape[2]), sems[12:17])
    third = m_rows.shape[2] // 3
    cuts = ((0, third), (third, third), (2 * third, third // 2), (2 * third + third // 2, third // 2))
    mlp = [
        Spread(m_rows, mlp_block, ranks, own, pl.ds(*cut), sems[17 + 5 * at : 22 + 5 * at])
        for at, cut in enumerate(cuts)
    ]
    local_sems = sems[37]
    out_send, out_recv = sems[2:4]
    o_cols = heads * size
    peers = [(lax.rem(seq + step, ranks), dp) for step in range(1, ranks)]
    peers += [(seq, attn.beside), (seq, attn.sibling)]
    knock(peers)
    loads = [
        move(src, dst, local_sems.at[at])
        for at, (src, dst) in enumerate(((w_gate, gate), (w_up, up), (w_down, down)))
    ]
    held[pl.ds(row(0), local)] = tokens[...]
    dys[pl.ds(row(0), local)] = out_grad[...]

    def column(line):
        same = lax.broadcasted_iota(jnp.int32, (own, own), 0) == lax.broadcasted_iota(jnp.int32, (own, own), 1)
        return jnp.sum(jnp.where(same, line, 0.0), 1, keepdims=True)

    def lay(target, begin, weight, gain):
        each = weight.shape[1] // ranks
        for rank in range(ranks):
            part = weight[:, rank * each : (rank + 1) * each]
            if gain is not None:
                part = (part.astype(jnp.float32) * gain).astype(LOW)
            target[rank, :, begin : begin + each] = part
        return begin + each

    gain = column(attn_gain[...])
    at = 0
    for weight in (w_query, w_key, w_value):
        at = lay(a_rows, at, weight, gain)
    whole[seq, pl.ds(pl.multiple_of(dp * own, own), own)] = w_output[...]
    answered(peers)
    ring = RingGather(held, local, ranks, sems[0], sems[1], right, left, row)
    ring.start(1)
    attn.start()
    outs = WholeGather(whole, ranks, own, [*sems[8:12], *sems[38:40]])
    outs.forward(0)
    line = LineGather(dys, local, ranks, sems[4], sems[5], sems[6], sems[7])
    stores = []

    def store(src, dst):
        stores.append(move(src, dst, local_sems.at[len(loads) + len(stores)]))

    def scale_rows(step):
        for rel in rels_of(step, ranks):

            def some(at, _):
                rows_at = pl.ds(pl.multiple_of(row(rel) + at * 32, 32), 32)
                normal[rows_at] = rows_scaled(held[rows_at].astype(jnp.float32))[0].astype(LOW)
                return 0

            lax.fori_loop(0, local // 32, some, 0)

    for load in loads:
        load.wait()
    gain = column(mlp_gain[...])
    each = gate.shape[1] // ranks
    lay(m_rows, 0, gate, gain)
    lay(m_rows, each, up, gain)
    lay(m_rows, 2 * each, down, None)
    scale_rows(0)
    def bring(step):
        outs.arrive(step)
        if step < half:
            outs.start(step + 1)
        outs.forward(step)

    def forward(piece):
        mlp[piece].arrive()
        mlp[piece].hop(0).start()
        mlp[piece].hop(1).start()

    def hop_over(piece):
        mlp[piece].hop(0).wait_recv()
        mlp[piece].hop(2).start()

    def pass_on(step):
        ring.advance(step)
        scale_rows(step)

    pass_on(1)
    line.start(1)
    pass_on(2)
    outs.start(1)
    attn.arrive()
    attn.hop(0).start()
    attn.hop(1).start()
    attn.hop(0).wait_recv()
    attn.hop(2).start()
    for step in range(3, half):
        pass_on(step)
    bring(1)
    pass_on(half)
    mlp[0].start()
    spans = order.shape[0]
    span = rows // spans
    for at in range(ranks):
        rows_at = pl.ds(at * local, local)
        ids = at * local + lax.broadcasted_iota(jnp.int32, (1, local), 1)
        where = jnp.zeros_like(ids)
        for slot in range(spans):
            inside = (ids >= slot * span) & (ids < (slot + 1) * span)
            where = where + jnp.where(inside, ids + (order[slot] - slot) * span, 0)
        begin = jnp.zeros_like(ids)
        for doc in range(starts.shape[1]):
            begin = jnp.maximum(begin, jnp.where(starts[0, doc] <= where, starts[0, doc], 0))
        pos_row[:, rows_at] = where
        across = jnp.broadcast_to(where, (local, local)).T
        pos[rows_at] = across[:, :1]
        begins[rows_at] = jnp.broadcast_to(begin, (local, local)).T[:, :1]
        angle = across[:, :1].astype(jnp.float32) * freqs[...]
        lane = lax.broadcasted_iota(jnp.int32, (local, size), 1)
        cosv[rows_at] = jnp.cos(angle)
        sine = jnp.sin(angle)
        sinv[rows_at] = jnp.where(lane < size // 2, -sine, sine)
    bring(2)
    line.advance(1)
    attn.hop(1).wait_recv()
    attn.hop(2).wait_recv()
    store(block, attn_block)

    def project(begin, count):
        rows_at = pl.ds(begin, count)
        kept[rows_at] = dot_nn(normal[rows_at], block[...].reshape(width, cols))

    store(normal, first_in)
    tile = rows // half

    def rotated(at, rows_at, gain):
        v = rows_scaled(kept[rows_at, at * size : (at + 1) * size])[0] * gain[...]
        return (v * cosv[rows_at] + turn(v) * sinv[rows_at]).astype(LOW)

    for piece in range(half):
        rows_at = pl.ds(piece * tile, tile)
        project(piece * tile, tile)
        for head in range(heads):
            q_low[head, rows_at] = rotated(head, rows_at, query_gain)
        for group in range(kv_heads):
            k_low[group, rows_at] = rotated(heads + group, rows_at, key_gain)
            at = (heads + kv_heads + group) * size
            v_low[group, rows_at] = kept[rows_at, at : at + size].astype(LOW)
    store(kept, qkv)
    forward(0)

    for piece in range(half):
        rows_at = pl.ds(piece * tile, tile)
        seen = (pos_row[...] <= pos[rows_at]) & (pos_row[...] >= begins[rows_at])
        for head in range(heads):
            raw = dot_nt(q_low[head, rows_at], k_low[head // share]) * scale
            raw = jnp.where(seen, raw, NEG)
            weight = jnp.exp(raw - jnp.max(raw, -1, keepdims=True))
            weight = (weight * (1.0 / jnp.sum(weight, -1, keepdims=True))).astype(LOW)
            probs[head, rows_at] = weight
            value = dot_nn(weight, v_low[head // share])
            out_low[rows_at, head * size : (head + 1) * size] = value.astype(LOW)
            store(probs.at[head, rows_at], prob.at[head, rows_at])
        if piece == 0:
            bring(3)
        if piece == 1:
            mlp[1].start()
            line.advance(2)
            bring(half)
    mlp[2].start()
    mlp[3].start()
    hop_over(0)
    forward(1)
    forward(2)
    place = ring_place(seq, ranks)

    def exchange(rel):
        to = ring_seq(lax.rem(place + rel, ranks), ranks)
        return push(
            out_low.at[pl.ds(row(rel), local)],
            own_out.at[:, pl.ds(pl.multiple_of(seq * o_cols, o_cols), o_cols)],
            out_send.at[rel],
            out_recv.at[rel],
            (to, dp),
        )

    for rel in range(1, ranks):
        exchange(rel).start()
    own_out[:, pl.ds(pl.multiple_of(seq * o_cols, o_cols), o_cols)] = out_low[pl.ds(row(0), local)]
    forward(3)
    outs.complete()
    store(whole, out_all)
    hop_over(1)
    hop_over(2)
    for step in range(3, half):
        line.advance(step)

    for rel in range(1, ranks):
        exchange(rel).wait_recv()

    def join(at, _):
        some = pl.ds(pl.multiple_of(at * deep, deep), deep)
        resid[:, some] = tokens[:, some].astype(jnp.float32) + dot_nt(own_out[...], whole[at])
        return 0

    lax.fori_loop(0, ranks, join, 0)

    def scale_second(at, _):
        rows_at = pl.ds(pl.multiple_of(at * 32, 32), 32)
        second[rows_at] = rows_scaled(resid[rows_at])[0].astype(LOW)
        return 0

    lax.fori_loop(0, local // 32, scale_second, 0)
    hop_over(3)
    line.complete()
    store(dys, dy_all)
    ring.finish()
    attn.finish()
    outs.finish()
    for rel in range(1, ranks):
        exchange(rel).wait_send()
    line.finish()
    for piece in mlp:
        piece.hop(1).wait_recv()
        piece.hop(2).wait_recv()
        piece.finish()
    for given in stores:
        given.wait()


def mlp_kernel(
    ranks, second, out_grad, rest, dys, mlp_block, block_out, dresid, dresid_low, own_grads,
    grads, from_core, from_y, held, weights, hidden, dgu, resid, dy_all,
    term, out_buf, in_buf, y_out, y_in, here, *sems,
):
    local, width = second.shape
    row = functools.partial(block_row, local=local, ranks=ranks)
    ff = hidden.shape[1]
    deep = weights.shape[1]
    half = ranks // 2
    right, left = neighbours(ranks)
    loads = [
        move(src, dst, here.at[at])
        for at, (src, dst) in enumerate(((mlp_block, weights), (dys, dy_all), (rest, resid)))
    ]
    seq, dp = lax.axis_index("seq"), lax.axis_index("dp")
    own = own_grads.shape[1]
    pieces = [
        Reduce(
            grads, from_core, from_y, own_grads, own, at * ranks // 4, ranks // 4, pl.ds(0, 3 * ff),
            sems[6 + 2 * at : 8 + 2 * at],
        )
        for at in range(4)
    ]
    peers = [right, left, (seq, pieces[0].beside), (seq, pieces[0].sibling)]
    knock(peers)
    held[pl.ds(row(0), local)] = second[...]
    answered(peers)
    ring = RingGather(held, local, ranks, sems[0], sems[1], right, left, row)
    ring.start(1)
    loads[0].wait()
    loads[1].wait()
    wide = 256

    def middle(step):
        rels = rels_of(step, ranks)

        def some(at, _):
            first = pl.multiple_of(at * wide, wide)
            given, dy = block_rows(held, rels, local, ranks), block_rows(dy_all, rels, local, ranks)
            gate = dot_nn(given, weights[:, :, pl.ds(first, wide)].reshape(width, wide))
            upper = dot_nn(given, weights[:, :, pl.ds(ff + first, wide)].reshape(width, wide))
            dmid = dot_nn(dy, weights[:, :, pl.ds(2 * ff + first, wide)].reshape(width, wide))
            sigma = 1.0 / (1.0 + jnp.exp(-gate))
            act = gate * sigma
            value = (act * upper).astype(LOW)
            dgate = (dmid * upper * (sigma * (1.0 + gate * (1.0 - sigma)))).astype(LOW)
            dupper = (dmid * act).astype(LOW)
            for at, rel in enumerate(rels):
                rows, some_rows = pl.ds(row(rel), local), slice(at * local, (at + 1) * local)
                hidden[rows, pl.ds(first, wide)] = value[some_rows]
                dgu[rows, pl.ds(first, wide)] = dgate[some_rows]
                dgu[rows, pl.ds(ff + first, wide)] = dupper[some_rows]
            return 0

        lax.fori_loop(0, ff // wide, some, 0)

    middle(0)
    for step in range(1, half + 1):
        ring.advance(step)
        middle(step)

    def back_part(rels, begin, end):
        def some(at, _):
            value = dot_nt(block_rows(dgu, rels, local, ranks), weights[at, :, : 2 * ff])
            term[: len(rels) * local, pl.ds(pl.multiple_of(at * deep, deep), deep)] = value
            return 0

        lax.fori_loop(begin, end, some, 0)

    def out_part(rels, begin, end):
        def some(at, _):
            value = dot_nt(block_rows(hidden, rels, local, ranks), weights[at, :, 2 * ff :])
            term[: len(rels) * local, pl.ds(pl.multiple_of(at * deep, deep), deep)] = value
            return 0

        lax.fori_loop(begin, end, some, 0)

    def weight_grads(first, count):
        def some(at, _):
            cols = pl.ds(pl.multiple_of(at * deep, deep), deep)
            grads[at, :, : 2 * ff] = dot_tn(held[:, cols], dgu[...]).astype(LOW)
            grads[at, :, 2 * ff :] = dot_tn(dy_all[:, cols], hidden[...]).astype(LOW)
            return 0

        lax.fori_loop(first, first + count, some, 0)

    back = RingSum(back_part, term, out_buf, in_buf, local, ranks, sems[2], sems[3], right, left)
    out = RingSum(out_part, term, y_out, y_in, local, ranks, sems[4], sems[5], right, left)
    for step in range(1, half + 1):
        back.compute(step)
        back.launch(step)
        out.compute(step)
        out.launch(step)
        made, passed, summed = (((0, 1), (2, 3), (), ()), ((), (0, 1), (2, 3), ()), ((), (), (0, 1), (2, 3)))
        for piece in (pieces[at] for at in made[step - 1]):
            weight_grads(piece.begin, piece.count)
            piece.first()
        for at in passed[step - 1]:
            pieces[at].second()
        for at in summed[step - 1]:
            pieces[at].third()
    back.compute(half + 1)
    loads[2].wait()
    back.arrive_last()

    def finish_back(at, _):
        begin = pl.multiple_of(at * 32, 32)
        rows = pl.ds(begin, 32)
        value = resid[rows]
        inv = rows_scaled(value)[1]
        grad = back.last(begin, 32)
        full = out_grad[rows].astype(jnp.float32) + rows_scaled_back(value, inv, grad)
        dresid[rows] = full
        dresid_low[rows] = full.astype(LOW)
        return 0

    lax.fori_loop(0, local // 32, finish_back, 0)
    out.compute(half + 1)
    out.arrive_last()

    def finish_out(at, _):
        begin = pl.multiple_of(at * 32, 32)
        rows = pl.ds(begin, 32)
        block_out[rows] = (resid[rows] + out.last(begin, 32)).astype(LOW)
        return 0

    lax.fori_loop(0, local // 32, finish_out, 0)
    ring.finish()
    back.finish()
    out.finish()
    for piece in pieces:
        piece.finish()


def back_kernel(
    ranks, kv_heads, tokens, dresid_low, query_gain, key_gain, own_out, first_in_in, block_in,
    qkv_in, cos_in, sin_in, q_in, k_in, v_in, prob_in, dresid_in, mlp_own, out_all,
    tokens_grad, gains, out_grad, mlp_sums, attn_sums,
    grads, from_core, from_y, own_grads, query_gain_grad, key_gain_grad,
    tile, tiles_in, tile_sum, tile_sums_in, dob, dout, dk, dv, dqkv,
    first_in, attn_block, qkv, cosv, sinv, q_low, k_low, v_low, prob, dresid, term, out_buf, in_buf,
    o_grads, o_core, o_y, o_own, o_term, o_out, o_in, *sems,
):
    local, width = tokens.shape
    rows = local * ranks
    half = ranks // 2
    size = cosv.shape[1]
    heads = q_low.shape[0]
    share = heads // kv_heads
    scale = 1.0 / math.sqrt(size)
    cols = (heads + 2 * kv_heads) * size
    deep = attn_block.shape[1]
    o_cols = heads * size
    right, left = neighbours(ranks)
    seq, dp = lax.axis_index("seq"), lax.axis_index("dp")
    own = mlp_own.shape[1]
    copies = lax.axis_size("dp")
    row = functools.partial(block_row, local=local, ranks=ranks)
    place = ring_place(seq, ranks)
    out_piece = Reduce(o_grads, o_core, o_y, o_own, own, 0, ranks, pl.ds(0, width), sems[4:6])
    qkv_piece = Reduce(grads, from_core, from_y, own_grads, own, 0, ranks, pl.ds(0, cols), sems[6:8])
    third = mlp_own.shape[2] // 3
    mlp_ways = [
        Deliver(mlp_own, mlp_sums, pl.ds(at * third, third), ranks, [*sems[8:11], *sems[22:28]][3 * at : 3 * at + 3])
        for at in range(3)
    ]
    dob_send, dob_recv = sems[0:2]
    qkv_way = Deliver(own_grads, attn_sums, pl.ds(0, cols), ranks, sems[14:17])
    peers = [(lax.rem(seq + step, ranks), dp) for step in range(1, ranks)]
    peers += [(seq, lax.rem(dp + step, copies)) for step in range(1, copies)]
    knock(peers)
    local_sems = sems[21]
    loads = {}
    for at, (name, src, dst) in enumerate(
        (
            ("out", out_all, o_grads), ("block", block_in, attn_block), ("v", v_in, v_low),
            ("prob", prob_in, prob), ("k", k_in, k_low), ("q", q_in, q_low), ("cos", cos_in, cosv),
            ("sin", sin_in, sinv), ("qkv", qkv_in, qkv), ("first", first_in_in, first_in),
            ("dresid", dresid_in, dresid),
        )
    ):
        loads[name] = move(src, dst, local_sems.at[at])
    answered(peers)
    mlp_ways[0].start()
    loads["out"].wait()

    def columns_of(rank):
        return pl.ds(pl.multiple_of(rank * o_cols, o_cols), o_cols)

    def owner(rel):
        return ring_seq(lax.rem(place + rel, ranks), ranks)

    def exchange(rel):
        to = owner(rel)
        return push(
            dob.at[:, columns_of(to)], dout.at[pl.ds(row(0), local)], dob_send.at[rel], dob_recv.at[rel], (to, dp)
        )

    def project(rel):
        some = columns_of(owner(rel))
        dob[:, some] = dot_nn(dresid_low[...], o_grads[:, :, some].reshape(width, o_cols)).astype(LOW)

    for rel in (*ring_order(ranks)[1:][::-1], 0):
        project(rel)
        if rel:
            exchange(rel).start()
    dout[pl.ds(row(0), local)] = dob[:, columns_of(seq)]

    def out_grads(at, _):
        some_cols = pl.ds(pl.multiple_of(at * deep, deep), deep)
        o_grads[at] = dot_tn(dresid_low[:, some_cols], own_out[...]).astype(LOW)
        return 0

    lax.fori_loop(0, ranks, out_grads, 0)
    out_piece.first()
    out_piece.second()
    for rel in range(1, ranks):
        exchange(rel).wait_recv()
    for name in ("v", "prob", "k", "q", "cos", "sin", "qkv"):
        loads[name].wait()
    mlp_ways[1].start()
    tall = rows // half
    query_gain_grad[...] = jnp.zeros_like(query_gain_grad)
    key_gain_grad[...] = jnp.zeros_like(key_gain_grad)

    def unrotated(grad, column, rows_at, gain, gain_grad_ref):
        grad = grad * cosv[rows_at] - turn(grad) * sinv[rows_at]
        value = qkv[rows_at, column * size : (column + 1) * size]
        normal, inv = rows_scaled(value)
        gain_grad_ref[...] += jnp.sum(grad * normal, 0, keepdims=True)
        back = rows_scaled_back(value, inv, grad * gain[...])
        dqkv[rows_at, column * size : (column + 1) * size] = back.astype(LOW)

    for head in range(heads):
        group = head // share

        def one(piece, _):
            rows_at = pl.ds(pl.multiple_of(piece * tall, tall), tall)
            weight = prob[head, rows_at]
            grad = dout[rows_at, head * size : (head + 1) * size]
            dprob = dot_nt(grad, v_low[group])
            full = weight.astype(jnp.float32)
            delta = jnp.sum(full * dprob, -1, keepdims=True)
            dscore = (full * (dprob - delta)).astype(LOW)
            dq = dot_nn(dscore, k_low[group]) * scale
            dk_add = dot_tn(dscore, q_low[head, rows_at]) * scale
            dv_add = dot_tn(weight, grad)
            dk[group] += dk_add
            dv[group] += dv_add
            unrotated(dq, head, rows_at, query_gain, query_gain_grad)
            return 0

        if head % share == 0:
            dk[group] = jnp.zeros_like(dk[group])
            dv[group] = jnp.zeros_like(dv[group])
        lax.fori_loop(0, half, one, 0)
        if head == 0:
            mlp_ways[2].start()
    for group in range(kv_heads):
        def one_key(piece, _):
            rows_at = pl.ds(pl.multiple_of(piece * tall, tall), tall)
            unrotated(dk[group, rows_at], heads + group, rows_at, key_gain, key_gain_grad)
            at = (heads + kv_heads + group) * size
            dqkv[rows_at, at : at + size] = dv[group, rows_at].astype(LOW)
            return 0

        lax.fori_loop(0, half, one_key, 0)

    def part(rels, begin, end):
        def some(at, _):
            value = dot_nt(block_rows(dqkv, rels, local, ranks), attn_block[at])
            term[: len(rels) * local, pl.ds(pl.multiple_of(at * deep, deep), deep)] = value
            return 0

        lax.fori_loop(begin, end, some, 0)

    def qkv_grads(at, _):
        some_cols = pl.ds(pl.multiple_of(at * deep, deep), deep)
        grads[at] = dot_tn(first_in[:, some_cols], dqkv[...]).astype(LOW)
        return 0

    def to_ranks(step):
        peer = lax.rem(seq + step, ranks)
        return push(tile, tiles_in.at[seq], sems[17].at[step], sems[18].at[step], (peer, dp))

    def to_copies(step):
        peer = lax.rem(dp + step, copies)
        return push(
            tile_sum, tile_sums_in.at[dp], sems[19].at[step], sems[20].at[step], (seq, peer)
        )

    tile[0:1] = query_gain_grad[...]
    tile[1:2] = key_gain_grad[...]
    tile[2:] = jnp.zeros((tile.shape[0] - 2, size), jnp.float32)
    for step in range(1, ranks):
        to_ranks(step).start()
    tiles_in[seq] = tile[...]
    loads["block"].wait()

    def out_part(rels, begin, end):
        for at, rel in enumerate(rels):
            o_term[at * own : (at + 1) * own] = o_own[owner(rel)].astype(jnp.float32)

    out_total = RingSum(out_part, o_term, o_out, o_in, own, ranks, sems[30], sems[31], right, left)
    totals = two_sums(part, term, out_buf, in_buf, local, ranks, [*sems[2:4], *sems[28:30]], right, left)
    for step in range(1, half + 1):
        for total in totals:
            total.compute(step)
            total.launch(step)
        if step == 1:
            loads["first"].wait()
            lax.fori_loop(0, ranks, qkv_grads, 0)
            qkv_piece.first()
            qkv_piece.second()
        if step == 2:
            out_piece.third()
            for other in range(1, ranks):
                to_ranks(other).wait_recv()
            tile_sum[...] = jnp.sum(tiles_in[...], 0)
            for other in range(1, copies):
                to_copies(other).start()
            tile_sums_in[dp] = tile_sum[...]
        if step == half - 1:
            for other in range(1, copies):
                to_copies(other).wait_recv()
            gains[...] = jnp.sum(tile_sums_in[...], 0)
        if step > 1:
            out_total.compute(step - 1)
            out_total.launch(step - 1)
    out_total.compute(half)
    out_total.launch(half)
    qkv_piece.third()
    qkv_way.start()
    for total in totals:
        total.compute(half + 1)
    loads["dresid"].wait()
    for total in totals:
        total.arrive_last()

    def last(at, _):
        begin = pl.multiple_of(at * 32, 32)
        rows_at = pl.ds(begin, 32)
        value = tokens[rows_at].astype(jnp.float32)
        inv = rows_scaled(value)[1]
        grad = jnp.concatenate([total.last(begin, 32) for total in totals], 1)
        tokens_grad[rows_at] = dresid[rows_at] + rows_scaled_back(value, inv, grad)
        return 0

    lax.fori_loop(0, local // 32, last, 0)
    out_total.compute(half + 1)
    out_total.arrive_last()
    out_grad[...] = out_total.last(0, own)
    for step in range(1, ranks):
        to_ranks(step).wait_send()
    for step in range(1, copies):
        to_copies(step).wait_send()
    out_total.finish()
    for rel in range(1, ranks):
        exchange(rel).wait_send()
    for total in totals:
        total.finish()
    out_piece.finish()
    qkv_piece.finish()
    for way in mlp_ways:
        way.finish()
    qkv_way.finish()


def leave_kernel(
    attn_sums, mlp_sums, gains, attn_gain, mlp_gain, w_query, w_key, w_value, w_gate, w_up,
    query_out, key_out, value_out, gate_out, up_out, down_out, attn_out, mlp_out,
    head_query_out, head_key_out,
):
    own = attn_gain.shape[1]
    same = lax.broadcasted_iota(jnp.int32, (own, own), 0) == lax.broadcasted_iota(jnp.int32, (own, own), 1)

    @pl.when(pl.program_id(0) == 0)
    def _():
        attn_out[...] = jnp.zeros_like(attn_out)
        mlp_out[...] = jnp.zeros_like(mlp_out)
        head_query_out[...] = gains[0:1]
        head_key_out[...] = gains[1:2]

    for sums, gain, gain_out, parts in (
        (attn_sums, attn_gain, attn_out, ((query_out, w_query), (key_out, w_key), (value_out, w_value))),
        (mlp_sums, mlp_gain, mlp_out, ((gate_out, w_gate), (up_out, w_up), (down_out, None))),
    ):
        scale = jnp.sum(jnp.where(same, gain[...], 0.0), 1, keepdims=True)
        for rank in range(sums.shape[0]):
            at = 0
            for out, weight in parts:
                each = out.shape[1] // sums.shape[0]
                cols = slice(rank * each, (rank + 1) * each)
                value = sums[rank, :, at : at + each].astype(jnp.float32)
                at += each
                if weight is None:
                    out[:, cols] = value
                    continue
                out[:, cols] = value * scale
                inner = jnp.sum(value * weight[:, cols].astype(jnp.float32), 1, keepdims=True)
                gain_out[...] += jnp.sum(jnp.where(same, inner, 0.0), 0, keepdims=True)


VM = pl.BlockSpec(memory_space=pltpu.VMEM)
SM = pl.BlockSpec(memory_space=pltpu.SMEM)
ANY = pl.BlockSpec(memory_space=pl.ANY)


def call(kernel, number, ins, outs, scratch, operands):
    return pl.pallas_call(
        kernel,
        out_shape=[jax.ShapeDtypeStruct(shape, dtype) for shape, dtype, _ in outs],
        in_specs=ins,
        out_specs=[spec for _, _, spec in outs],
        scratch_shapes=scratch,
        compiler_params=pltpu.CompilerParams(
            collective_id=number, has_side_effects=True, vmem_limit_bytes=LIMIT
        ),
    )(*operands)


def columns_body(
    tokens,
    out_grad,
    span_order,
    doc_starts,
    w_query,
    w_key,
    w_value,
    w_output,
    attn_gain,
    query_gain,
    key_gain,
    w_gate,
    w_up,
    w_down,
    mlp_gain,
):
    ranks = lax.axis_size("seq")
    copies = lax.axis_size("dp")
    _, local, width = tokens.shape
    rows = local * ranks
    size = query_gain.shape[0]
    kv_heads = w_key.shape[1] // size // ranks
    heads = w_query.shape[1] // size // ranks
    q_cols, kv_cols = heads * size, kv_heads * size
    qkv_cols = q_cols + 2 * kv_cols
    ff = w_gate.shape[1] // ranks
    own = width // (ranks * copies)
    deep = own * copies
    half = ranks // 2
    f32, i32 = jnp.float32, jnp.int32
    exponents = np.arange(size) % (size // 2) * (-2.0 / size * math.log(1000000.0))
    freqs = jnp.asarray(np.exp(exponents)[None], f32)
    q_gain, k_gain = query_gain[None], key_gain[None]
    (
        resid, second, cosv, sinv, q_low, k_low, v_low, own_out, first_in, qkv, attn_block, dy_all, prob, mlp_block,
        out_all,
    ) = call(
        functools.partial(first_kernel, ranks, kv_heads),
        1,
        [SM, SM] + [VM] * 11 + [ANY] * 3,
        [
            ((local, width), f32, VM),
            ((local, width), LOW, VM),
            ((rows, size), f32, VM),
            ((rows, size), f32, VM),
            ((heads, rows, size), LOW, VM),
            ((kv_heads, rows, size), LOW, VM),
            ((kv_heads, rows, size), LOW, VM),
            ((local, q_cols * ranks), LOW, VM),
            ((rows, width), LOW, ANY),
            ((rows, qkv_cols), f32, ANY),
            ((ranks, deep, qkv_cols), LOW, ANY),
            ((rows, width), LOW, ANY),
            ((heads, rows, rows), LOW, ANY),
            ((ranks, deep, 3 * ff), LOW, ANY),
            ((ranks, deep, q_cols * ranks), LOW, ANY),
        ],
        [
            pltpu.VMEM((rows, width), LOW),
            pltpu.VMEM((rows, width), LOW),
            pltpu.VMEM((rows, qkv_cols), f32),
            pltpu.VMEM((ranks, deep, qkv_cols), LOW),
            pltpu.VMEM((ranks, own, qkv_cols), LOW),
            pltpu.VMEM((ranks, own, 3 * ff), LOW),
        ]
        + [pltpu.VMEM((own, ff * ranks), LOW)] * 3
        + [
            pltpu.VMEM((rows, width), LOW),
            pltpu.VMEM((heads, rows, rows), LOW),
            pltpu.VMEM((rows, 1), i32),
            pltpu.VMEM((rows, 1), i32),
            pltpu.VMEM((1, rows), i32),
            pltpu.VMEM((rows, q_cols), LOW),
            pltpu.VMEM((ranks, deep, q_cols * ranks), LOW),
        ]
        + ring_sems(ranks)
        + [pltpu.SemaphoreType.DMA((ranks,))] * 2
        + line_sems(ranks)
        + whole_sems(ranks)[:4]
        + spread_sems(ranks) * 5
        + [pltpu.SemaphoreType.DMA((heads * half + 8,))]
        + whole_sems(ranks)[4:],
        (
            span_order, doc_starts, tokens[0], out_grad[0], freqs, attn_gain[None], mlp_gain[None], q_gain, k_gain,
            w_query, w_key, w_value, w_output, w_gate, w_up, w_down,
        ),
    )
    block_out, dresid, dresid_low, mlp_own = call(
        functools.partial(mlp_kernel, ranks),
        2,
        [VM, VM, ANY, ANY, ANY],
        [
            ((local, width), LOW, VM),
            ((local, width), f32, VM),
            ((local, width), LOW, VM),
            ((ranks, own, 3 * ff), LOW, VM),
        ],
        [pltpu.VMEM((ranks, deep, 3 * ff), LOW)]
        + reduce_bufs(ranks, own, 3 * ff)
        + [
            pltpu.VMEM((rows, width), LOW),
            pltpu.VMEM((ranks, deep, 3 * ff), LOW),
            pltpu.VMEM((rows, ff), LOW),
            pltpu.VMEM((rows, 2 * ff), LOW),
            pltpu.VMEM((local, width), f32),
            pltpu.VMEM((rows, width), LOW),
        ]
        + sum_bufs(local, ranks, width)
        + sum_bufs(local, ranks, width)[1:]
        + [pltpu.SemaphoreType.DMA((3,))]
        + ring_sems(ranks) * 3
        + reduce_sems() * 4,
        (second, out_grad[0], resid, dy_all, mlp_block),
    )
    tokens_grad, gains, wo_grad, mlp_sums, attn_sums = call(
        functools.partial(back_kernel, ranks, kv_heads),
        3,
        [VM] * 5 + [ANY] * 12,
        [
            ((local, width), f32, VM),
            ((8, size), f32, VM),
            ((own, q_cols * ranks), f32, VM),
            ((ranks, own, 3 * ff), LOW, ANY),
            ((ranks, own, qkv_cols), LOW, VM),
        ],
        [pltpu.VMEM((ranks, deep, qkv_cols), LOW)]
        + reduce_bufs(ranks, own, qkv_cols)
        + [
            pltpu.VMEM((ranks, own, qkv_cols), LOW),
            pltpu.VMEM((1, size), f32),
            pltpu.VMEM((1, size), f32),
            pltpu.VMEM((8, size), f32),
            pltpu.VMEM((ranks, 8, size), f32),
            pltpu.VMEM((8, size), f32),
            pltpu.VMEM((copies, 8, size), f32),
            pltpu.VMEM((local, q_cols * ranks), LOW),
            pltpu.VMEM((rows, q_cols), LOW),
            pltpu.VMEM((kv_heads, rows, size), f32),
            pltpu.VMEM((kv_heads, rows, size), f32),
            pltpu.VMEM((rows, qkv_cols), LOW),
            pltpu.VMEM((rows, width), LOW),
            pltpu.VMEM((ranks, deep, qkv_cols), LOW),
            pltpu.VMEM((rows, qkv_cols), f32),
            pltpu.VMEM((rows, size), f32),
            pltpu.VMEM((rows, size), f32),
            pltpu.VMEM((heads, rows, size), LOW),
            pltpu.VMEM((kv_heads, rows, size), LOW),
            pltpu.VMEM((kv_heads, rows, size), LOW),
            pltpu.VMEM((heads, rows, rows), LOW),
            pltpu.VMEM((local, width), f32),
        ]
        + sum_bufs(local, ranks, width)
        + [pltpu.VMEM((ranks, deep, q_cols * ranks), LOW)]
        + reduce_bufs(ranks, own, q_cols * ranks)
        + [pltpu.VMEM((ranks, own, q_cols * ranks), LOW)]
        + sum_bufs(own, ranks, q_cols * ranks)
        + [pltpu.SemaphoreType.DMA((ranks,))] * 2
        + ring_sems(ranks)
        + reduce_sems() * 2
        + deliver_sems(ranks) * 3
        + [pltpu.SemaphoreType.DMA((ranks,))] * 2
        + [pltpu.SemaphoreType.DMA((copies,))] * 2
        + [pltpu.SemaphoreType.DMA((11,))]
        + deliver_sems(ranks) * 2
        + ring_sems(ranks) * 2,
        (
            tokens[0], dresid_low, q_gain, k_gain, own_out, first_in, attn_block, qkv, cosv, sinv, q_low, k_low,
            v_low, prob, dresid, mlp_own, out_all,
        ),
    )
    whole = pl.BlockSpec((1, own), lambda at: (0, 0))
    each = (q_cols, kv_cols, kv_cols, ff, ff, ff)
    many = 2
    columns = [pl.BlockSpec((own, many * cols), lambda at: (0, at)) for cols in each]
    head = pl.BlockSpec((1, size), lambda at: (0, 0))
    *grads, dga, dgm, dgq, dgk = pl.pallas_call(
        leave_kernel,
        grid=(ranks // many,),
        out_shape=[jax.ShapeDtypeStruct((own, cols * ranks), f32) for cols in each]
        + [jax.ShapeDtypeStruct((1, own), f32)] * 2
        + [jax.ShapeDtypeStruct((1, size), f32)] * 2,
        in_specs=[
            pl.BlockSpec((many, own, qkv_cols), lambda at: (at, 0, 0)),
            pl.BlockSpec((many, own, 3 * ff), lambda at: (at, 0, 0)),
            pl.BlockSpec((8, size), lambda at: (0, 0)),
            whole,
            whole,
            *columns[:3],
            *columns[3:5],
        ],
        out_specs=columns + [whole, whole, head, head],
    )(attn_sums, mlp_sums, gains, attn_gain[None], mlp_gain[None], w_query, w_key, w_value, w_gate, w_up)
    return (
        block_out[None], tokens_grad[None], *grads[:3], wo_grad, dga[0], dgq[0], dgk[0], *grads[3:], dgm[0],
    )


def body(*args):
    tokens, w_key, query_gain = args[0], args[5], args[9]
    groups = w_key.shape[1] // query_gain.shape[0]
    ranks = lax.axis_size("seq")
    if tokens.shape[0] == 1 and ranks % 2 == 0 and groups % ranks == 0 and lax.axis_size("dp") == 4:
        return columns_body(*args)
    return gathered_body(*args)


def solution(mesh):
    return jax.shard_map(
        body,
        mesh=mesh,
        in_specs=(
            P("dp", "seq", None),
            P("dp", "seq", None),
            P(),
            P("dp", None),
            P(("seq", "dp"), None),
            P(("seq", "dp"), None),
            P(("seq", "dp"), None),
            P(("seq", "dp"), None),
            P(("seq", "dp")),
            P(),
            P(),
            P(("seq", "dp"), None),
            P(("seq", "dp"), None),
            P(("seq", "dp"), None),
            P(("seq", "dp")),
        ),
        out_specs=(
            P("dp", "seq", None),
            P("dp", "seq", None),
            P(("seq", "dp"), None),
            P(("seq", "dp"), None),
            P(("seq", "dp"), None),
            P(("seq", "dp"), None),
            P(("seq", "dp")),
            P(),
            P(),
            P(("seq", "dp"), None),
            P(("seq", "dp"), None),
            P(("seq", "dp"), None),
            P(("seq", "dp")),
        ),
        check_vma=False,
    )
```
